32 devices in a mesh: gx: 4 (over x, core), gy: 8 (over z, y).
Axes of the slice: x: 2, y: 2, z: 4, core: 2. Of those that a mesh axis runs over, the one named last changes fastest.
Arguments:
- velocity: float32 [2, 1, 2048, 2048], P(None, None, 'gy', 'gx'), may hold values from -6 to 6
- weights_x: float32 [4, 4096], replicated, may hold values from -0.25 to 0.75
- weights_y: float32 [4, 4096], replicated, may hold values from -0.25 to 0.75
- acoustic: bfloat16 [4, 1, 4096, 4096], P(None, None, 'gy', 'gx'), may hold values from -6 to 6
- wall_mask: int32 [1, 4096, 4096], P(None, 'gy', 'gx'), may hold values 0 or 1
Outputs:
- advanced: bfloat16 [4, 1, 4096, 4096], P(None, None, 'gy', 'gx')
The draws below stay inside these ranges and needn't reach their ends.
All inputs are finite; a program needn't handle non-finite values. No bound on the sum of `wall_mask` on one device may be relied on, other than what follows from the above.
Results may differ from the reference program's by a relative error of at most 0.002.
Values sent between devices are 32-bit elements; how exact they have to be, the bound alone decides.
No kernel may reach another device: no remote copies, remote signals or barrier semaphores. Data moves between devices by JAX's collectives and lax.ppermute only.
A program may use at most 128 MiB of HBM per device.

```python
import jax
import jax.numpy as jnp

NX = 2048
NY = 2048
PLANES = 1
AX = 4096
AY = 4096


def touch_ends(values, own_key, smallest, top_value):
    longest = values.shape.index(max(values.shape))
    spots = []
    for shift in (0, 1):
        where = [jax.random.randint(jax.random.fold_in(own_key, axis), (), 0, length) for axis, length in enumerate(values.shape)]
        where[longest] = (where[longest] + shift) % values.shape[longest]
        spots.append(tuple(where))
    return values.at[spots[0]].set(smallest).at[spots[1]].set(top_value)


def block_levels(key, dims, cuts, low, top_value):
    gain = 1.0
    for dim, parts in cuts:
        steps = jax.random.uniform(jax.random.fold_in(jax.random.fold_in(key, 6), dim), (parts,), jnp.float32, low / len(cuts), top_value / len(cuts))
        gain = gain * jnp.repeat(jnp.exp(steps), dims[dim] // parts).reshape((-1,) + (1,) * (len(dims) - 1 - dim))
    return gain


def noise(key, dims, scale, reach, pieces=(), kind=jnp.bfloat16):
    values = scale * jax.random.normal(key, dims, jnp.float32)
    if pieces:
        values = values * block_levels(key, dims, pieces, -0.22, 0.18)
    return jnp.clip(values, -reach, reach).astype(kind)


def setup_inputs(seed: int = 0) -> dict:
    key_of = jax.random.split(jax.random.key(seed), 6)
    return {
        "velocity": noise(key_of[0], (2, PLANES, NY, NX), 1.0, 6.0, ((2, 8), (3, 4)), jnp.float32),
        "weights_x": jnp.clip(jax.random.uniform(key_of[1], (4, AX), jnp.float32, -0.25, 0.75), -0.25, 0.75),
        "weights_y": jnp.clip(jax.random.uniform(key_of[2], (4, AY), jnp.float32, -0.25, 0.75), -0.25, 0.75),
        "acoustic": noise(key_of[3], (4, PLANES, AY, AX), 1.0, 6.0, ((2, 8), (3, 4))),
        "wall_mask": touch_ends((jax.random.randint(key_of[4], (PLANES, AY, AX), 0, 8) < 1).astype(jnp.int32), jax.random.fold_in(key_of[4], 1), 0, 1),
    }


stencil_weights = (0.75, -0.15, 1.0 / 60.0)
mean_flow = 0.3
time_step = 0.5


def signed_wave(length):
    counts = jnp.arange(length)
    return jnp.where(counts < length // 2, counts, counts - length)


def refine_last(samples, weights):
    coarse = samples.shape[-1]
    fine_index = jnp.arange(2 * coarse) // 2
    result = jnp.zeros(samples.shape[:-1] + (2 * coarse,), samples.dtype)
    for offset in range(4):
        tapped = jnp.take(samples, (fine_index - 1 + offset) % coarse, axis=-1)
        result = result + tapped * weights[offset]
    return result


def gradients(padded):
    height = padded.shape[-2] - 6
    breadth = padded.shape[-1] - 6
    rows_mid = padded[..., 3:3 + height, :]
    cols_mid = padded[..., :, 3:3 + breadth]
    along_x = jnp.zeros_like(padded[..., 3:3 + height, 3:3 + breadth])
    along_y = jnp.zeros_like(along_x)
    for index, weight in enumerate(stencil_weights):
        distance = index + 1
        along_x = along_x + weight * (rows_mid[..., 3 + distance:3 + distance + breadth] - rows_mid[..., 3 - distance:3 - distance + breadth])
        along_y = along_y + weight * (cols_mid[..., 3 + distance:3 + distance + height, :] - cols_mid[..., 3 - distance:3 - distance + height, :])
    return along_x, along_y


def tendency(padded, source):
    along_x, along_y = gradients(padded)
    diverge = along_x[1] + along_y[2]
    forcing = jnp.stack([-diverge, -along_x[3], -along_y[3], source - diverge])
    return forcing - mean_flow * along_x


def reference(velocity, weights_x, weights_y, acoustic, wall_mask):
    real_type = velocity.dtype
    acoustic = acoustic.astype(real_type)
    flow_x = velocity[0]
    flow_y = velocity[1]
    tensor = jnp.stack([flow_x * flow_x, flow_x * flow_y, flow_y * flow_y])
    spectra = jnp.fft.fft2(tensor, axes=(-2, -1))
    wave_x = signed_wave(NX).astype(real_type)[None, :]
    wave_y = signed_wave(NY).astype(real_type)[:, None]
    numerator = -(wave_x * wave_x * spectra[0] + 2.0 * wave_x * wave_y * spectra[1] + wave_y * wave_y * spectra[2])
    denominator = wave_x * wave_x + wave_y * wave_y
    positive = denominator > 0
    solved = jnp.where(positive, numerator / jnp.where(positive, denominator, 1.0), 0.0)
    pressure = jnp.real(jnp.fft.ifft2(solved, axes=(-2, -1))).astype(real_type)
    source = refine_last(pressure, weights_x)
    source = jnp.swapaxes(refine_last(jnp.swapaxes(source, -1, -2), weights_y), -1, -2)
    open_cells = (1 - wall_mask).astype(real_type)
    widths = ((0, 0), (0, 0), (3, 3), (3, 3))
    first_rate = tendency(jnp.pad(acoustic, widths), source)
    middle = open_cells * (acoustic + time_step * first_rate)
    second_rate = tendency(jnp.pad(middle, widths), source)
    return (open_cells * (acoustic + 0.5 * time_step * (first_rate + second_rate))).astype(jnp.bfloat16)
```

```python
import functools
import math

import jax
import jax.numpy as jnp
import ml_dtypes
import numpy as np
from jax import lax
from jax.experimental import pallas as pl
from jax.experimental.pallas import tpu as pltpu
from jax.sharding import PartitionSpec as P

stencil_weights = (0.75, -0.15, 1.0 / 60.0)
mean_flow = 0.3
time_step = 0.5

LANES = 128
RADIX = 8
HALO = 8
MARGIN = 16
TILE = 128
ROOT = math.sqrt(0.5)
BF16 = jnp.bfloat16
F32 = jnp.float32


def halves(table):
    high = table.astype(np.float32).astype(ml_dtypes.bfloat16)
    low = (table - high.astype(np.float64)).astype(np.float32).astype(ml_dtypes.bfloat16)
    return high, low


def packed_columns(cosine, sine):
    half = LANES // 2
    parts = []
    for first in range(0, cosine.shape[1], half):
        parts += [cosine[:, first : first + half], sine[:, first : first + half]]
    return np.concatenate(parts, axis=1)


@functools.lru_cache(maxsize=None)
def x_tables(length):
    base = length // RADIX
    m = np.arange(base)[:, None]
    q = np.arange(base)[None, :]
    angle = 2.0 * np.pi * ((m * q) % base) / base
    cosine, sine = np.cos(angle), np.sin(angle)
    full = np.concatenate([packed_columns(cosine, -sine), packed_columns(sine, cosine)], axis=0)
    half = base // 2
    zero_cos, zero_sin = cosine[:, :half].copy(), -sine[:, :half]
    zero_cos[:, 0] = 0.0
    zero_sin = zero_sin.copy()
    zero_sin[:, 0] = (-1.0) ** np.arange(base)
    zero = packed_columns(zero_cos, zero_sin)
    shifted = 2.0 * np.pi * ((m * (RADIX * q[:, :half] + RADIX // 2)) % length) / length
    middle = packed_columns(np.cos(shifted), -np.sin(shifted))
    turns = 2.0 * np.pi * np.arange(1, RADIX // 2)[:, None] * np.arange(base)[None, :] / length
    return full, zero, middle, np.cos(turns), np.sin(turns)


@functools.lru_cache(maxsize=None)
def y_tables(length):
    base = length // RADIX
    index = np.arange(base)
    angle = 2.0 * np.pi * ((index[:, None] * index[None, :]) % base) / base
    both = np.concatenate([np.cos(angle), np.sin(angle)], axis=0)
    turns = 2.0 * np.pi * np.arange(RADIX)[:, None] * index[None, :] / length
    sign = np.where(np.arange(LANES) < LANES // 2, 1.0, -1.0)
    cos_turn = np.broadcast_to(np.cos(turns)[:, :, None], (RADIX, base, LANES))
    sin_turn = np.sin(turns)[:, :, None] * sign
    return both, cos_turn.astype(np.float32), sin_turn.astype(np.float32)


@functools.lru_cache(maxsize=None)
def wave_table(length, count):
    slots = LANES // 4
    base = length // RADIX
    waves = []
    for residue in (1, 2, 3):
        waves.append(RADIX * np.arange(base) + residue)
    waves.append(RADIX * np.arange(base // 2))
    waves.append(RADIX * np.arange(base // 2) + RADIX // 2)
    waves = np.concatenate(waves)
    waves = np.where(waves == 0, length // 2, waves)
    waves = np.where(waves < length // 2, waves, waves - length).reshape(count, slots)
    return np.tile(waves, (1, 4)).astype(np.float32)


@functools.lru_cache(maxsize=None)
def band_table():
    band = np.zeros((4 * LANES, 2 * LANES))
    column = np.arange(2 * LANES)
    for index, weight in enumerate(stencil_weights):
        band[column + LANES + index + 1, column] = weight
        band[column + LANES - index - 1, column] = -weight
    return band


def split(values):
    high = values.astype(BF16)
    return high, (values - high.astype(F32)).astype(BF16)


def dot(left, right):
    return jnp.dot(left, right, preferred_element_type=F32)


def exact_dot(left, right):
    left_high, left_low = left
    right_high, right_low = right
    return dot(left_high, right_high) + (dot(left_low, right_high) + dot(left_high, right_low))


def lane_index(shape):
    return lax.broadcasted_iota(jnp.int32, shape, len(shape) - 1)


def spin(values, shift):
    return pltpu.roll(values, shift % values.shape[-1], values.ndim - 1)


def forward_x_kernel(lines, full_h, full_l, zero_h, zero_l, mid_h, mid_l, cos_ref, sin_ref, out, total):
    count, _, rows, local = lines.shape
    base = cos_ref.shape[1]
    per = local // base
    u = [lines[t // per, 0, :, (t % per) * base : (t % per + 1) * base] for t in range(RADIX)]
    v = [lines[t // per, 1, :, (t % per) * base : (t % per + 1) * base] for t in range(RADIX)]
    energy = sum(b * b for b in v)
    energy = jnp.sum(energy.reshape(rows // 8, 8, base), axis=0)
    total[...] = sum(energy[:, k : k + LANES] for k in range(0, base, LANES))
    fields = ([a * a - b * b for a, b in zip(u, v)], [2.0 * a * b for a, b in zip(u, v)])
    zeros, mids, reals, imags = [], [], [[], [], []], [[], [], []]
    for a in fields:
        s04, s26, s15, s37 = a[0] + a[4], a[2] + a[6], a[1] + a[5], a[3] + a[7]
        d04, d26, d15, d37 = a[0] - a[4], a[2] - a[6], a[1] - a[5], a[3] - a[7]
        zeros.append((s04 + s26) + (s15 + s37))
        mids.append((s04 + s26) - (s15 + s37))
        minus, plus = ROOT * (d15 - d37), ROOT * (d15 + d37)
        turned = (
            (d04 + minus, -d26 - plus),
            (s04 - s26, s37 - s15),
            (d04 - minus, d26 - plus),
        )
        for index, (real, imag) in enumerate(turned):
            c, s = cos_ref[index : index + 1, :], sin_ref[index : index + 1, :]
            reals[index].append(real * c + imag * s)
            imags[index].append(imag * c - real * s)
    stacked = jnp.concatenate(
        [
            jnp.concatenate([jnp.concatenate(reals[i], axis=0) for i in range(3)], axis=0),
            jnp.concatenate([jnp.concatenate(imags[i], axis=0) for i in range(3)], axis=0),
        ],
        axis=1,
    )
    full = exact_dot(split(stacked), (full_h[...], full_l[...]))
    zero = exact_dot(split(jnp.concatenate(zeros, axis=0)), (zero_h[...], zero_l[...]))
    mid = exact_dot(split(jnp.concatenate(mids, axis=0)), (mid_h[...], mid_l[...]))
    low = lane_index((rows, LANES)) % 64 < 32
    place = 0
    blocks = [full[2 * rows * i : 2 * rows * (i + 1)] for i in range(3)] + [zero, mid]
    for block in blocks:
        for first in range(0, block.shape[1], LANES):
            a = block[:rows, first : first + LANES]
            c = block[rows:, first : first + LANES]
            out[place] = jnp.where(low, a, spin(c, 32))
            out[place + 1] = jnp.where(low, spin(a, -32), c)
            place += 2


def eighths(x, turn):
    s04, s26, s15, s37 = x[0] + x[4], x[2] + x[6], x[1] + x[5], x[3] + x[7]
    d04, d26, d15, d37 = x[0] - x[4], x[2] - x[6], x[1] - x[5], x[3] - x[7]
    quarter = turn(s15 - s37)
    spun_26, spun_37 = turn(d26), turn(d37)
    one, three = d15 + spun_37, d15 - spun_37
    spun_one, spun_three = turn(one), turn(three)
    one = ROOT * (one + spun_one)
    three = ROOT * (spun_three - three)
    return [
        (s04 + s26) + (s15 + s37),
        (d04 + spun_26) + one,
        (s04 - s26) + quarter,
        (d04 - spun_26) + three,
        (s04 + s26) - (s15 + s37),
        (d04 + spun_26) - one,
        (s04 - s26) - quarter,
        (d04 - spun_26) - three,
    ]


def solve_y_kernel(count_x, lines, total, wave, both_h, both_l, cos_ref, sin_ref, out, held):
    count, rows, _ = lines.shape
    base = cos_ref.shape[1]
    length = count * rows
    block = count_x * rows
    per = base // rows
    lanes = lane_index((base, LANES))
    sign = jnp.where(lanes < 64, 1.0, -1.0).astype(F32)

    def minus_i(z):
        return spin(z, 64) * sign

    def plus_i(z):
        return spin(z, 64) * -sign

    fields = [
        jnp.concatenate([lines[t * per + k] for k in range(per)], axis=0) for t in range(RADIX)
    ]
    mixed = eighths(fields, minus_i)
    mixed = [mixed[0]] + [
        mixed[r] * cos_ref[r] + spin(mixed[r], 64) * sin_ref[r] for r in range(1, RADIX)
    ]
    tables = (both_h[...], both_l[...])
    product = exact_dot(tables, split(jnp.concatenate(mixed, axis=1)))
    kx = wave[0:1, :]
    is_first = lanes % 64 < 32
    q = lax.broadcasted_iota(jnp.int32, (base, LANES), 0)
    edge = jnp.float32(-(length // 2))
    solved = []
    for r in range(RADIX):
        at = slice(r * LANES, (r + 1) * LANES)
        spectrum = product[:base, at] + minus_i(product[base:, at])
        k = RADIX * q + r
        ky = jnp.where(k < length // 2, k, k - length).astype(F32)
        cross = jnp.where((kx == edge) == (ky == edge), kx * ky, 0.0)
        symbol = jnp.where(is_first, kx * kx, cross) / (kx * kx + ky * ky)
        terms = symbol * spectrum
        solved.append(terms + spin(terms, -32))
    product = exact_dot(tables, split(jnp.concatenate(solved, axis=1)))
    mixed = []
    for r in range(RADIX):
        at = slice(r * LANES, (r + 1) * LANES)
        value = product[:base, at] + plus_i(product[base:, at])
        if r:
            value = value * cos_ref[r] - spin(value, 64) * sin_ref[r]
        mixed.append(value)
    for t, values in enumerate(eighths(mixed, plus_i)):
        held[MARGIN + t * base : MARGIN + (t + 1) * base, :] = values
    held[0:MARGIN, :] = held[length : length + MARGIN, :]
    held[length + MARGIN : length + 2 * MARGIN, :] = held[MARGIN : 2 * MARGIN, :]
    spare = total[...] + spin(total[...], 32)
    kept = rows + 2 * MARGIN // count_x
    half = out.shape[1]
    rest = kept - half
    low = lane_index((8, LANES)) % 64 < 32
    for target in range(count):
        start = (target // count_x) * block + (target % count_x) * kept
        for row in range(0, half, 8):
            a = held[start + row : start + row + 8, :]
            if row < rest:
                b = spin(held[start + half + row : start + half + row + 8, :], 32)
            else:
                b = spare
            out[target, row : row + 8, :] = jnp.where(low, a, b)


def inverse_x_kernel(
    kept, scale, lines, full_h, full_l, zero_h, zero_l, mid_h, mid_l, cos_ref, sin_ref, out, held
):
    count, half, _ = lines.shape
    base = cos_ref.shape[1]
    length = RADIX * base
    rest = kept - half
    low = lane_index((half, LANES)) % 64 < 32
    groups, spare = [], None
    for first in range(0, count, 2):
        even, odd = lines[first], lines[first + 1]
        a = jnp.where(low, even, spin(odd, 32))
        b = jnp.where(low, spin(even, -32), odd)
        groups.append(jnp.concatenate([a, b[:rest]], axis=0))
        extra = b[rest : rest + 8]
        spare = extra if spare is None else spare + extra
    mean = jnp.sum(spare) * scale
    wide = 2 * base // LANES
    narrow = base // LANES
    stacked = jnp.concatenate(
        [jnp.concatenate(groups[i * wide : (i + 1) * wide], axis=1) for i in range(3)], axis=0
    )
    place = 3 * wide
    zeros = jnp.concatenate(groups[place : place + narrow], axis=1)
    mids = jnp.concatenate(groups[place + narrow : place + 2 * narrow], axis=1)
    full = exact_dot(split(stacked), (full_h[...], full_l[...]))
    zero = exact_dot(split(zeros), (zero_h[...], zero_l[...])) * scale
    mid = exact_dot(split(mids), (mid_h[...], mid_l[...])) * scale
    turned = []
    for i in range(3):
        real = full[i * kept : (i + 1) * kept, :base]
        imag = full[i * kept : (i + 1) * kept, base:]
        c = cos_ref[i : i + 1, :] * (2.0 * scale)
        s = sin_ref[i : i + 1, :] * (2.0 * scale)
        turned.append((real * c - imag * s, real * s + imag * c))
    for t in range(RADIX):
        value = zero + mid if t % 2 == 0 else zero - mid
        for i, (real, imag) in enumerate(turned):
            eighth = t * (i + 1) % RADIX
            c = (1.0, ROOT, 0.0, -ROOT, -1.0, -ROOT, 0.0, ROOT)[eighth]
            s = (0.0, ROOT, 1.0, ROOT, 0.0, -ROOT, -1.0, -ROOT)[eighth]
            if c:
                value = value + c * real
            if s:
                value = value - s * imag
        held[:, t * base : (t + 1) * base] = mean - value
    targets, _, width = out.shape
    local = width - LANES
    right = lane_index((kept, LANES)) < 64
    for target in range(targets):
        out[target, :, :local] = held[:, target * local : (target + 1) * local]
        after = (target + 1) * local % length
        before = (target * local - LANES) % length
        out[target, :, local:] = jnp.where(
            right, held[:, after : after + LANES], held[:, before : before + LANES]
        )


def windows(parts, first):
    tiles = parts[0].shape[-1] // LANES
    order = [(first + step) % tiles for step in (-1, 0, 1, 2)]
    if first == tiles - 1:
        order = order[:3]
    return tuple(
        jnp.concatenate([part[:, t * LANES : (t + 1) * LANES] for t in order], axis=1)
        for part in parts
    )


def slopes_x(parts, band_h, band_l, with_edge):
    tiles = parts[0].shape[-1] // LANES
    pieces = []
    for first in range(0, tiles - 1, 2):
        window = windows(parts, first)
        piece = dot(window[0], band_h[...]) + dot(window[0], band_l[...])
        if len(parts) > 1:
            piece = piece + dot(window[1], band_h[...])
        pieces.append(piece)
    if with_edge:
        window = windows(parts, tiles - 1)
        high, low = band_h[: 3 * LANES, :LANES], band_l[: 3 * LANES, :LANES]
        piece = dot(window[0], high) + dot(window[0], low)
        if len(parts) > 1:
            piece = piece + dot(window[1], high)
        pieces.append(piece)
    return jnp.concatenate(pieces, axis=1)


def slope_y(read):
    value = None
    for index, weight in enumerate(stencil_weights):
        term = weight * (read(index + 1) - read(-index - 1))
        value = term if value is None else value + term
    return value


def quiet_step_kernel(
    center, above, below, top, bottom, sides, open_ref, band_h, band_l, out, field, middle
):
    step = pl.program_id(0)
    last = pl.num_programs(0) - 1
    tile, width = center.shape[1], center.shape[2]
    full = field.shape[2]
    high = tile + 2 * HALO
    guard = HALO
    base = step * tile
    blank = jnp.zeros((guard, full), F32)
    for k in range(4):
        field[k, 0:guard, :] = blank
        field[k, guard + high :, :] = blank
        up = above[k].astype(F32)[above.shape[1] - HALO :, :]
        down = below[k].astype(F32)[:HALO, :]
        field[k, guard : guard + HALO, :width] = jnp.where(step == 0, top[k, :, :width], up)
        field[k, guard + HALO : guard + HALO + tile, :width] = center[k].astype(F32)
        field[k, guard + HALO + tile : guard + high, :width] = jnp.where(
            step == last, bottom[k, :, :width], down
        )
        field[k, guard : guard + high, width:] = sides[k, pl.ds(pl.multiple_of(base, 8), high), :]
    opened = open_ref[pl.ds(pl.multiple_of(base, 8), high), :]

    def rates(ref, at, count, lanes, x):
        def reader(k):
            return lambda d: ref[k, at + d : at + d + count, :lanes]
        along_b = slope_y(reader(2))
        along_p = slope_y(reader(3))
        diverge = x[1] + along_b
        return (
            diverge + mean_flow * x[0],
            x[3] + mean_flow * x[1],
            along_p + mean_flow * x[2],
            diverge + mean_flow * x[3],
        )

    values = [field[k, guard : guard + high, :] for k in range(4)]
    x = slopes_x((jnp.concatenate([v.astype(BF16) for v in values], axis=0),), band_h, band_l, True)
    x = [x[k * high : (k + 1) * high] for k in range(4)]
    drops = rates(field, guard, high, full, x)
    for k in range(4):
        middle[k, 0:guard, :] = blank
        middle[k, guard + high :, :] = blank
        middle[k, guard : guard + high, :] = opened * (values[k] - time_step * drops[k])
    at = guard + HALO
    inner = [middle[k, at : at + tile, :] for k in range(4)]
    x = slopes_x(split(jnp.concatenate(inner, axis=0)), band_h, band_l, False)
    x = [x[k * tile : (k + 1) * tile] for k in range(4)]
    drops = rates(middle, at, tile, width, x)
    shown = opened[HALO : HALO + tile, :width]
    for k in range(4):
        start = field[k, at : at + tile, :width]
        out[k] = 0.5 * (shown * start + inner[k][:, :width]) - 0.5 * time_step * shown * drops[k]


def source_kernel(lines, squares, rise_y, rise_x, quiet, open_ref, band_h, band_l, out, pressure, forced):
    step = pl.program_id(0)
    tile, width = quiet.shape[1], quiet.shape[2]
    high = tile + 2 * HALO
    reach = rise_y.shape[2]
    local = width // 2

    @pl.when(step == 0)
    def _():
        count, kept, _ = lines.shape
        for k in range(count):
            at = slice(k * kept, (k + 1) * kept)
            pressure[at, :] = lines[k] - squares[at, :] * squares[at, :]

    start = pl.multiple_of(step * (tile // 2) + MARGIN - HALO, 8)
    window = split(pressure[pl.ds(start, reach), :])
    tall = split(exact_dot(split(rise_y[0]), window))
    tiles = local // LANES + 1
    pieces = []
    for k in range(tiles):
        order = [(k + shift) % tiles for shift in (-1, 0, 1)]
        around = tuple(
            jnp.concatenate([part[:, t * LANES : (t + 1) * LANES] for t in order], axis=1)
            for part in tall
        )
        weights = split(rise_x[k] if k < tiles - 1 else rise_x[k][:, :LANES])
        pieces.append(exact_dot(around, weights))
    opened = open_ref[pl.ds(pl.multiple_of(step * tile, 8), high), :]
    source = time_step * opened * jnp.concatenate(pieces, axis=1)
    forced[...] = source
    inner = source[HALO : HALO + tile, :]
    x = slopes_x(split(inner), band_h, band_l, False)
    y = slope_y(lambda d: forced[HALO + d : HALO + d + tile, :width])
    shown = 0.5 * time_step * opened[HALO : HALO + tile, :width]
    x = shown * x
    out[0] = quiet[0].astype(out.dtype)
    out[1] = (quiet[1] - x).astype(out.dtype)
    out[2] = (quiet[2] - shown * y).astype(out.dtype)
    out[3] = (quiet[3] + inner[:, :width] - mean_flow * x).astype(out.dtype)


def call(kernel, operands, outs, scratch=(), grid=(), specs=None, out_specs=None, megabytes=48, flops=0, moved=0, name=None):
    def whole(array):
        zeros = (0,) * array.ndim
        return pl.BlockSpec(array.shape, lambda *_: zeros)

    chosen = specs or {}
    arguments = {}
    if grid:
        arguments["grid"] = grid
        arguments["in_specs"] = [chosen.get(i, whole(o)) for i, o in enumerate(operands)]
        arguments["out_specs"] = out_specs
    return pl.pallas_call(
        kernel,
        out_shape=outs,
        scratch_shapes=list(scratch),
        compiler_params=pltpu.CompilerParams(vmem_limit_bytes=megabytes << 20),
        cost_estimate=pl.CostEstimate(flops=flops, bytes_accessed=moved, transcendentals=0),
        name=name,
        **arguments,
    )(*operands)


def ring(array, axis, forward, wrap):
    size = lax.axis_size(axis)
    pairs = [(i, (i + 1) % size) for i in range(size if wrap else size - 1)]
    if not forward:
        pairs = [(j, i) for i, j in pairs]
    return lax.ppermute(array, axis, pairs)


def edged_columns(array, wrap):
    left = ring(array[..., -HALO:], "gx", True, wrap)
    right = ring(array[..., :HALO], "gx", False, wrap)
    blank = jnp.zeros(array.shape[:-1] + (LANES - 2 * HALO,), array.dtype)
    return jnp.concatenate([right, blank, left], axis=-1)


def edged_rows(array, sides, wrap):
    first = jnp.concatenate([array[..., :HALO, :], sides[..., :HALO, :]], axis=-1)
    last = jnp.concatenate([array[..., -HALO:, :], sides[..., -HALO:, :]], axis=-1)
    return ring(last, "gy", True, wrap), ring(first, "gy", False, wrap)


def pressure_lines(velocity):
    count_x, count_y = lax.axis_size("gx"), lax.axis_size("gy")
    count = count_x * count_y
    _, _, local_y, local_x = velocity.shape
    length_x, length_y = local_x * count_x, local_y * count_y
    rows = local_y // count_x
    sent = velocity.reshape(2, count_x, rows, local_x).swapaxes(0, 1)
    lines = lax.all_to_all(sent, "gx", 0, 0, tiled=True)
    full, zero, middle, cos_turn, sin_turn = x_tables(length_x)
    turns = (jnp.asarray(cos_turn, F32), jnp.asarray(sin_turn, F32))
    spectra, total = call(
        forward_x_kernel,
        (lines, *halves(full), *halves(zero), *halves(middle), *turns),
        (
            jax.ShapeDtypeStruct((count, rows, LANES), F32),
            jax.ShapeDtypeStruct((8, LANES), F32),
        ),
        flops=10**9,
        moved=4 << 20,
        name="forward_x",
    )
    spectra = lax.all_to_all(spectra, ("gy", "gx"), 0, 0, tiled=True)
    place = lax.axis_index("gy") * count_x + lax.axis_index("gx")
    waves = jnp.asarray(wave_table(length_x, count))
    wave = jnp.broadcast_to(lax.dynamic_slice(waves, (place, 0), (1, LANES)), (8, LANES))
    both, cos_rows, sin_rows = y_tables(length_y)
    kept = rows + 2 * MARGIN // count_x
    half = (kept // 2 + 8) // 8 * 8
    solved = call(
        functools.partial(solve_y_kernel, count_x),
        (spectra, total, wave, *halves(both), cos_rows, sin_rows),
        jax.ShapeDtypeStruct((count, half, LANES), F32),
        (pltpu.VMEM((length_y + 2 * MARGIN, LANES), F32),),
        flops=4 * 10**9,
        moved=6 << 20,
        name="solve_y",
    )
    solved = lax.all_to_all(solved, ("gy", "gx"), 0, 0, tiled=True)
    back = 2.0 * zero.T
    back[LANES // 2] *= 0.5
    scale = 1.0 / (length_x * length_y)
    pressed = call(
        functools.partial(inverse_x_kernel, kept, scale),
        (solved, *halves(full.T), *halves(back), *halves(2.0 * middle.T), *turns),
        jax.ShapeDtypeStruct((count_x, kept, local_x + LANES), F32),
        (pltpu.VMEM((kept, length_x), F32),),
        flops=10**9,
        moved=4 << 20,
        name="inverse_x",
    )
    return lax.all_to_all(pressed, "gx", 0, 0, tiled=True)


def refine_tables(weights_x, weights_y, tall, wide):
    columns = weights_x.shape[1]
    first = lax.axis_index("gx") * wide
    ends = jnp.concatenate([weights_x[:, -LANES:], weights_x, weights_x[:, :LANES]], axis=1)
    own = lax.dynamic_slice(ends, (0, first), (4, wide + 2 * LANES))
    half = LANES // 2
    edge = jnp.concatenate([own[:, wide + LANES : wide + LANES + half], own[:, half:LANES]], axis=1)
    edge = jnp.pad(edge, ((0, 0), (0, LANES)))
    own = own[:, LANES : wide + LANES]
    tiles = wide // (2 * LANES)
    weights = jnp.concatenate([own, edge], axis=1).reshape(4, tiles + 1, 1, 2 * LANES)
    fine = np.arange(2 * LANES)
    targets = np.tile(LANES + fine // 2 - 1, (tiles + 1, 1))
    targets[tiles] = np.where(fine < half, LANES + fine // 2 - 1, LANES + half + fine // 2 - 1)
    cells = np.arange(3 * LANES)[None, :, None]
    rise_x = sum(
        jnp.where(cells == targets[:, None, :] + t, weights[t], 0.0) for t in range(4)
    )
    high = TILE + 2 * HALO
    ends = jnp.concatenate([weights_y[:, -HALO:], weights_y, weights_y[:, :HALO]], axis=1)
    own = lax.dynamic_slice(ends, (0, lax.axis_index("gy") * tall), (4, tall + 2 * HALO))
    steps = tall // TILE
    own = jnp.stack([own[:, k * TILE : k * TILE + high] for k in range(steps)], axis=1)
    reach = TILE // 2 + 2 * HALO
    cells = np.arange(reach)[None, None, :]
    targets = (np.arange(high) // 2 + HALO // 2 - 1)[None, :, None]
    rise_y = sum(jnp.where(cells == targets + s, own[s][:, :, None], 0.0) for s in range(4))
    return rise_x, rise_y


def fast_shards(velocity, weights_x, weights_y, acoustic, wall_mask):
    lines = pressure_lines(velocity)
    acoustic = acoustic[:, 0]
    parts, tall, wide = acoustic.shape
    full, high, steps = wide + LANES, TILE + 2 * HALO, tall // TILE
    opened = 1.0 - wall_mask.astype(F32)
    fields = jnp.concatenate([acoustic.astype(F32), opened], axis=0)
    sides = edged_columns(fields, False)
    above, below = edged_rows(fields, sides, False)
    sides = jnp.concatenate([above[..., wide:], sides, below[..., wide:]], axis=1)
    open_all = jnp.concatenate([above[parts, :, :wide], opened[0], below[parts, :, :wide]], axis=0)
    open_all = jnp.concatenate([open_all, sides[parts]], axis=1)
    band = halves(band_table())
    small = 2 * HALO
    per = TILE // small
    block = (parts, TILE, wide)
    quiet = call(
        quiet_step_kernel,
        (acoustic, acoustic, acoustic, above[:parts], below[:parts], sides[:parts], open_all, *band),
        jax.ShapeDtypeStruct((parts, tall, wide), F32),
        (pltpu.VMEM((parts, high + 2 * HALO, full), F32),) * 2,
        grid=(steps,),
        specs={
            0: pl.BlockSpec(block, lambda i: (0, i, 0)),
            1: pl.BlockSpec((parts, small, wide), lambda i: (0, jnp.maximum(i * per - 1, 0), 0)),
            2: pl.BlockSpec(
                (parts, small, wide), lambda i: (0, jnp.minimum((i + 1) * per, steps * per - 1), 0)
            ),
        },
        out_specs=pl.BlockSpec(block, lambda i: (0, i, 0)),
        flops=12 * 10**9,
        moved=60 << 20,
        name="quiet_step",
    )
    flow = velocity[1, 0]
    beside = edged_columns(flow, True)
    over, under = edged_rows(flow, beside, True)
    flow = jnp.concatenate([over, jnp.concatenate([flow, beside], axis=1), under], axis=0)
    flow = jnp.pad(flow, ((MARGIN - HALO, MARGIN - HALO), (0, 0)))
    rise_x, rise_y = refine_tables(weights_x, weights_y, tall, wide)
    out = call(
        source_kernel,
        (lines, flow, rise_y, rise_x, quiet, open_all, *band),
        jax.ShapeDtypeStruct((parts, tall, wide), BF16),
        (pltpu.VMEM(flow.shape, F32), pltpu.VMEM((high, full), F32)),
        grid=(steps,),
        specs={
            2: pl.BlockSpec((1,) + rise_y.shape[1:], lambda i: (i, 0, 0)),
            4: pl.BlockSpec(block, lambda i: (0, i, 0)),
        },
        out_specs=pl.BlockSpec(block, lambda i: (0, i, 0)),
        flops=4 * 10**9,
        moved=16 << 20,
        name="source_step",
    )
    return out[:, None]


def fits(count_x, count_y, velocity, acoustic):
    _, planes, local_y, local_x = velocity
    _, _, tall, wide = acoustic
    length_x, length_y = local_x * count_x, local_y * count_y
    rows = local_y // count_x
    base_x, base_y = length_x // RADIX, length_y // RADIX
    return (
        planes == 1
        and length_x * 2 == count_x * count_y * LANES
        and base_x % (2 * LANES) == 0
        and local_x % base_x == 0
        and rows % 8 == 0
        and base_y % rows == 0
        and base_y % 8 == 0
        and MARGIN * 2 % (8 * count_x) == 0
        and tall == 2 * local_y
        and wide == 2 * local_x
        and tall % TILE == 0
        and wide % (2 * LANES) == 0
    )


def extended(array, sides, width):
    for axis, dim in sides:
        size, length = (lax.axis_size(axis), array.shape[dim])
        up = [(i, (i + 1) % size) for i in range(size - 1)]
        down = [(j, i) for i, j in up]
        last = lax.slice_in_dim(array, length - width, length, axis=dim)
        leading = lax.slice_in_dim(array, 0, width, axis=dim)
        before = lax.ppermute(last, axis, up)
        after = lax.ppermute(leading, axis, down)
        array = jnp.concatenate([before, array, after], axis=dim)
    return array


def gradients(padded):
    height = padded.shape[-2] - 6
    breadth = padded.shape[-1] - 6
    rows_mid = padded[..., 3 : 3 + height, :]
    cols_mid = padded[..., :, 3 : 3 + breadth]
    along_x = jnp.zeros_like(padded[..., 3 : 3 + height, 3 : 3 + breadth])
    along_y = jnp.zeros_like(along_x)
    for index, weight in enumerate(stencil_weights):
        distance = index + 1
        along_x = along_x + weight * (
            rows_mid[..., 3 + distance : 3 + distance + breadth]
            - rows_mid[..., 3 - distance : 3 - distance + breadth]
        )
        along_y = along_y + weight * (
            cols_mid[..., 3 + distance : 3 + distance + height, :]
            - cols_mid[..., 3 - distance : 3 - distance + height, :]
        )
    return (along_x, along_y)


def tendency(padded, source):
    along_x, along_y = gradients(padded)
    diverge = along_x[1] + along_y[2]
    forcing = jnp.stack([-diverge, -along_x[3], -along_y[3], source - diverge])
    return forcing - mean_flow * along_x


def spectral_index(flat, length):
    second = length // 16
    wave = flat // second + 16 * (flat % second)
    return jnp.where(wave < length // 2, wave, wave - length).astype(jnp.float32)


def twiddles(rows_count, cols_count, modulus, sign):
    products = jnp.arange(rows_count)[:, None] * jnp.arange(cols_count)[None, :] % modulus
    angles = 2.0 * math.pi / modulus * products.astype(jnp.float32)
    return (jnp.cos(angles), sign * jnp.sin(angles))


def mix_rows(real_part, imag_part, cosine, sine):
    exact = lax.Precision.HIGHEST
    cos_real = jnp.einsum("ka,...ab->...kb", cosine, real_part, precision=exact)
    cos_imag = jnp.einsum("ka,...ab->...kb", cosine, imag_part, precision=exact)
    sin_real = jnp.einsum("ka,...ab->...kb", sine, real_part, precision=exact)
    sin_imag = jnp.einsum("ka,...ab->...kb", sine, imag_part, precision=exact)
    return (cos_real - sin_imag, cos_imag + sin_real)


def mix_cols(real_part, imag_part, cosine, sine):
    exact = lax.Precision.HIGHEST
    cos_real = jnp.einsum("...kb,bc->...kc", real_part, cosine, precision=exact)
    cos_imag = jnp.einsum("...kb,bc->...kc", imag_part, cosine, precision=exact)
    sin_real = jnp.einsum("...kb,bc->...kc", real_part, sine, precision=exact)
    sin_imag = jnp.einsum("...kb,bc->...kc", imag_part, sine, precision=exact)
    return (cos_real - sin_imag, cos_imag + sin_real)


def rotate(real_part, imag_part, cosine, sine):
    return (real_part * cosine - imag_part * sine, real_part * sine + imag_part * cosine)


def discrete(real_part, imag_part, sign):
    length = real_part.shape[-1]
    second = length // 16
    initial = real_part.shape
    folded = initial[:-1] + (16, second)
    real_part = real_part.reshape(folded)
    imag_part = imag_part.reshape(folded)
    small_cos, small_sin = twiddles(16, 16, 16, sign)
    large_cos, large_sin = twiddles(second, second, second, sign)
    turn_cos, turn_sin = twiddles(16, second, length, sign)
    if sign < 0:
        real_part, imag_part = mix_rows(real_part, imag_part, small_cos, small_sin)
        real_part, imag_part = rotate(real_part, imag_part, turn_cos, turn_sin)
        real_part, imag_part = mix_cols(real_part, imag_part, large_cos, large_sin)
    else:
        real_part, imag_part = mix_cols(real_part, imag_part, large_cos, large_sin)
        real_part, imag_part = rotate(real_part, imag_part, turn_cos, turn_sin)
        real_part, imag_part = mix_rows(real_part, imag_part, small_cos, small_sin)
        real_part = real_part / length
        imag_part = imag_part / length
    return (real_part.reshape(initial), imag_part.reshape(initial))


def transform(stacked, sign, kind):
    if kind == "real_in":
        real_part = stacked
        imag_part = jnp.zeros_like(stacked)
    else:
        half = stacked.shape[0] // 2
        real_part = stacked[:half]
        imag_part = stacked[half:]
    real_out, imag_out = discrete(real_part, imag_part, sign)
    if kind == "real_out":
        return real_out
    return jnp.concatenate([real_out, imag_out], axis=0)


def project(stacked, wave_x, wave_y):
    coef_xx = wave_x * wave_x
    coef_xy = 2.0 * wave_x * wave_y
    coef_yy = wave_y * wave_y
    denominator = wave_x * wave_x + wave_y * wave_y
    positive = denominator > 0
    safe = jnp.where(positive, denominator, 1.0)

    def combine(parts):
        numerator = -(coef_xx * parts[0] + coef_xy * parts[1] + coef_yy * parts[2])
        return jnp.where(positive, numerator / safe, 0.0)

    return jnp.stack([combine(stacked[:3]), combine(stacked[3:])])


def refine(stacked, weights):
    result = jnp.zeros(stacked.shape[:-1] + (2 * stacked.shape[-1],), jnp.float32)
    for offset in range(4):
        result = (
            result
            + jnp.repeat(jnp.roll(stacked, 1 - offset, axis=-1), 2, axis=-1) * weights[offset]
        )
    return result


def lines_x(stacked, action):
    gathered = action(lax.all_to_all(stacked, "gx", split_axis=2, concat_axis=3, tiled=True))
    return lax.all_to_all(gathered, "gx", split_axis=3, concat_axis=2, tiled=True)


def lines_y(stacked, action):
    turned = jnp.swapaxes(stacked, 2, 3)
    gathered = action(lax.all_to_all(turned, "gy", split_axis=2, concat_axis=3, tiled=True))
    returned = lax.all_to_all(gathered, "gy", split_axis=3, concat_axis=2, tiled=True)
    return jnp.swapaxes(returned, 2, 3)


def expand(fields):
    return extended(fields, (("gx", 3), ("gy", 2)), 3)


def shards(velocity, weights_x, weights_y, acoustic, wall_mask):
    acoustic = acoustic.astype(jnp.float32)
    flow_x = velocity[0]
    flow_y = velocity[1]
    tensor = jnp.stack([flow_x * flow_x, flow_x * flow_y, flow_y * flow_y])
    count_gx = lax.axis_size("gx")
    count_gy = lax.axis_size("gy")
    place_x = lax.axis_index("gx")
    place_y = lax.axis_index("gy")
    local_y = tensor.shape[2]
    local_x = tensor.shape[3]
    length_x = local_x * count_gx
    length_y = local_y * count_gy

    def forward_real(portion):
        return transform(portion, -1, "real_in")

    def finish_x(portion):
        return refine(transform(portion, 1, "real_out"), weights_x)

    spectra = lines_x(tensor, forward_real)
    share_x = local_x // count_gy
    line_x = spectral_index(place_x * local_x + place_y * share_x + jnp.arange(share_x), length_x)[
        :, None
    ]
    line_y = spectral_index(jnp.arange(length_y), length_y)[None, :]

    def solve_y(portion):
        solved = project(transform(portion, -1, "complex"), line_x, line_y)
        return refine(transform(solved, 1, "complex"), weights_y)

    pressure = lines_y(spectra, solve_y)
    source = lines_x(pressure, finish_x)[0]
    open_cells = (1 - wall_mask).astype(jnp.float32)
    first_rate = tendency(expand(acoustic), source)
    middle = open_cells * (acoustic + time_step * first_rate)
    second_rate = tendency(expand(middle), source)
    return (open_cells * (acoustic + 0.5 * time_step * (first_rate + second_rate))).astype(
        jnp.bfloat16
    )


def solution(mesh):
    in_specs = (P(None, None, "gy", "gx"), P(), P(), P(None, None, "gy", "gx"), P(None, "gy", "gx"))
    out_specs = P(None, None, "gy", "gx")

    def chosen(velocity, weights_x, weights_y, acoustic, wall_mask):
        sizes = (mesh.shape["gx"], mesh.shape["gy"], velocity.shape, acoustic.shape)
        plan = fast_shards if fits(*sizes) else shards
        return plan(velocity, weights_x, weights_y, acoustic, wall_mask)

    return jax.shard_map(
        chosen, mesh=mesh, in_specs=in_specs, out_specs=out_specs, check_vma=False
    )
```

```python
import functools
import math

import jax
import jax.numpy as jnp
import ml_dtypes
import numpy as np
from jax import lax
from jax.experimental import pallas as pl
from jax.experimental.pallas import tpu as pltpu
from jax.sharding import PartitionSpec as P

stencil_weights = (0.75, -0.15, 1.0 / 60.0)
mean_flow = 0.3
time_step = 0.5
whole_weights = (45.0, -9.0, 1.0)

LANES = 128
RADIX = 8
HALO = 8
MARGIN = 16
TILE = 128
ROOT = math.sqrt(0.5)
BF16 = jnp.bfloat16
F32 = jnp.float32


def halves(table):
    high = table.astype(np.float32).astype(ml_dtypes.bfloat16)
    low = (table - high.astype(np.float64)).astype(np.float32).astype(ml_dtypes.bfloat16)
    return high, low


def packed_columns(cosine, sine):
    half = LANES // 2
    parts = []
    for first in range(0, cosine.shape[1], half):
        parts += [cosine[:, first : first + half], sine[:, first : first + half]]
    return np.concatenate(parts, axis=1)


@functools.lru_cache(maxsize=None)
def x_tables(length):
    base = length // RADIX
    m = np.arange(base)[:, None]
    q = np.arange(base)[None, :]
    angle = 2.0 * np.pi * ((m * q) % base) / base
    cosine, sine = np.cos(angle), np.sin(angle)
    full = np.concatenate([packed_columns(cosine, -sine), packed_columns(sine, cosine)], axis=0)
    half = base // 2
    zero_cos, zero_sin = cosine[:, :half].copy(), -sine[:, :half]
    zero_cos[:, 0] = 0.0
    zero_sin = zero_sin.copy()
    zero_sin[:, 0] = (-1.0) ** np.arange(base)
    zero = packed_columns(zero_cos, zero_sin)
    shifted = 2.0 * np.pi * ((m * (RADIX * q[:, :half] + RADIX // 2)) % length) / length
    middle = packed_columns(np.cos(shifted), -np.sin(shifted))
    turns = 2.0 * np.pi * np.arange(1, RADIX // 2)[:, None] * np.arange(base)[None, :] / length
    return full, zero, middle, np.cos(turns), np.sin(turns)


@functools.lru_cache(maxsize=None)
def y_tables(length):
    base = length // RADIX
    index = np.arange(base)
    angle = 2.0 * np.pi * ((index[:, None] * index[None, :]) % base) / base
    both = np.concatenate([np.cos(angle), np.sin(angle)], axis=0)
    turns = 2.0 * np.pi * np.arange(RADIX)[:, None] * index[None, :] / length
    sign = np.where(np.arange(LANES) < LANES // 2, 1.0, -1.0)
    cos_turn = np.broadcast_to(np.cos(turns)[:, :, None], (RADIX, base, LANES))
    sin_turn = np.sin(turns)[:, :, None] * sign
    return both, cos_turn.astype(np.float32), sin_turn.astype(np.float32)


@functools.lru_cache(maxsize=None)
def wave_table(length, count):
    slots = LANES // 4
    base = length // RADIX
    waves = []
    for residue in (1, 2, 3):
        waves.append(RADIX * np.arange(base) + residue)
    waves.append(RADIX * np.arange(base // 2))
    waves.append(RADIX * np.arange(base // 2) + RADIX // 2)
    waves = np.concatenate(waves)
    waves = np.where(waves == 0, length // 2, waves)
    waves = np.where(waves < length // 2, waves, waves - length).reshape(count, slots)
    return np.tile(waves, (1, 4)).astype(np.float32)


@functools.lru_cache(maxsize=None)
def band_table():
    band = np.zeros((4 * LANES, 2 * LANES))
    column = np.arange(2 * LANES)
    for index, weight in enumerate(whole_weights):
        band[column + LANES + index + 1, column] = weight
        band[column + LANES - index - 1, column] = -weight
    return band.astype(ml_dtypes.bfloat16)


def beside(*tables):
    high, low = halves(np.concatenate(tables, axis=1))
    return np.concatenate([high, low], axis=0)


def split(values):
    high = values.astype(BF16)
    return high, (values - high.astype(F32)).astype(BF16)


def dot(left, right):
    return jnp.dot(left, right, preferred_element_type=F32)


def exact_dot(left, right):
    left_high, left_low = left
    right_high, right_low = right
    return dot(left_high, right_high) + (dot(left_low, right_high) + dot(left_high, right_low))


def lane_index(shape):
    return lax.broadcasted_iota(jnp.int32, shape, len(shape) - 1)


def spin(values, shift):
    return pltpu.roll(values, shift % values.shape[-1], values.ndim - 1)


def lane_tile(values, index):
    return values[:, index * LANES : (index + 1) * LANES]


def x_parts(tables, base):
    wide = 2 * base
    full = (tables[:wide], tables[wide : 2 * wide])
    at = 2 * wide
    high, low = tables[at : at + base], tables[at + base : at + 2 * base]
    return full, (high[:, :base], low[:, :base]), (high[:, base:], low[:, base:])


def edges_kernel(velocity, left, right, left_wall, right_wall, sent, to_right, to_left):
    count, _, rows, width = sent.shape
    for e in range(count):
        for c in range(2):
            sent[e, c] = velocity[c, 0, e * rows : (e + 1) * rows, :]
    parts = left.shape[0]
    flow_rows = count * rows
    for k in range(parts + 1):
        at = slice(k * HALO, (k + 1) * HALO)
        if k < parts:
            first, last = left[k, 0].astype(F32), right[k, 0].astype(F32)
        else:
            first, last = 1.0 - left_wall[0].astype(F32), 1.0 - right_wall[0].astype(F32)
        to_left[at, :] = first.T[:HALO]
        to_right[at, :] = last.T[LANES - HALO :]
    at = slice((parts + 1) * HALO, (parts + 2) * HALO)
    blank = jnp.zeros((HALO, to_left.shape[1]), F32)
    to_left[at, :] = blank
    to_right[at, :] = blank
    to_left[at, :flow_rows] = velocity[1, 0, :, :LANES].T[:HALO]
    to_right[at, :flow_rows] = velocity[1, 0, :, width - LANES :].T[LANES - HALO :]


def sides_kernel(
    has, from_left, from_right, first_rows, last_rows, first_wall, last_wall, first_flow, last_flow, sides, flow_side, first, last
):
    parts, _, small, width = first_rows.shape
    flow_rows, local = flow_side.shape[0], first_flow.shape[-1]
    tall = sides.shape[1]
    gap = jnp.zeros((LANES - 2 * HALO, tall), F32)
    for k in range(parts + 1):
        at = slice(k * HALO, (k + 1) * HALO)
        tile = jnp.concatenate([from_right[at, :] * has[1], gap, from_left[at, :] * has[0]], axis=0).T
        sides[k] = tile
        if k < parts:
            top, low = first_rows[k, 0].astype(F32)[:HALO], last_rows[k, 0].astype(F32)[small - HALO :]
        else:
            top, low = 1.0 - first_wall[0].astype(F32), 1.0 - last_wall[0].astype(F32)
        first[at, :width] = top
        first[at, width:] = tile[:HALO]
        last[at, :width] = low
        last[at, width:] = tile[tall - HALO :]
    at = slice((parts + 1) * HALO, (parts + 2) * HALO)
    gap = gap[:, :flow_rows]
    tile = jnp.concatenate([from_right[at, :flow_rows], gap, from_left[at, :flow_rows]], axis=0).T
    flow_side[...] = tile
    blank = jnp.zeros((HALO, first.shape[1]), F32)
    first[at, :] = blank
    last[at, :] = blank
    first[at, :local] = first_flow[0, 0]
    last[at, :local] = last_flow[0, 0]
    first[at, local : local + LANES] = tile[:HALO]
    last[at, local : local + LANES] = tile[flow_rows - HALO :]


def forward_x_kernel(lines, tables, turns, out, total):
    count, _, rows, local = lines.shape
    base = turns.shape[1]
    per = local // base
    u = [lines[t // per, 0, :, (t % per) * base : (t % per + 1) * base] for t in range(RADIX)]
    v = [lines[t // per, 1, :, (t % per) * base : (t % per + 1) * base] for t in range(RADIX)]
    energy = sum(b * b for b in v)
    energy = jnp.sum(energy.reshape(rows // 8, 8, base), axis=0)
    total[...] = sum(energy[:, k : k + LANES] for k in range(0, base, LANES))
    fields = ([a * a - b * b for a, b in zip(u, v)], [2.0 * a * b for a, b in zip(u, v)])
    zeros, mids, reals, imags = [], [], [[], [], []], [[], [], []]
    for a in fields:
        s04, s26, s15, s37 = a[0] + a[4], a[2] + a[6], a[1] + a[5], a[3] + a[7]
        d04, d26, d15, d37 = a[0] - a[4], a[2] - a[6], a[1] - a[5], a[3] - a[7]
        zeros.append((s04 + s26) + (s15 + s37))
        mids.append((s04 + s26) - (s15 + s37))
        minus, plus = ROOT * (d15 - d37), ROOT * (d15 + d37)
        turned = (
            (d04 + minus, -d26 - plus),
            (s04 - s26, s37 - s15),
            (d04 - minus, d26 - plus),
        )
        for index, (real, imag) in enumerate(turned):
            c, s = turns[index : index + 1, :], turns[index + 3 : index + 4, :]
            reals[index].append(real * c + imag * s)
            imags[index].append(imag * c - real * s)
    stacked = jnp.concatenate(
        [
            jnp.concatenate([jnp.concatenate(reals[i], axis=0) for i in range(3)], axis=0),
            jnp.concatenate([jnp.concatenate(imags[i], axis=0) for i in range(3)], axis=0),
        ],
        axis=1,
    )
    full, zero, middle = x_parts(tables, base)
    full = exact_dot(split(stacked), full)
    zero = exact_dot(split(jnp.concatenate(zeros, axis=0)), zero)
    middle = exact_dot(split(jnp.concatenate(mids, axis=0)), middle)
    low = lane_index((rows, LANES)) % 64 < 32
    place = 0
    blocks = [full[2 * rows * i : 2 * rows * (i + 1)] for i in range(3)] + [zero, middle]
    for block in blocks:
        for first in range(0, block.shape[1], LANES):
            a = block[:rows, first : first + LANES]
            c = block[rows:, first : first + LANES]
            out[place] = jnp.where(low, a, spin(c, 32))
            out[place + 1] = jnp.where(low, spin(a, -32), c)
            place += 2


def eighths(x, turn):
    s04, s26, s15, s37 = x[0] + x[4], x[2] + x[6], x[1] + x[5], x[3] + x[7]
    d04, d26, d15, d37 = x[0] - x[4], x[2] - x[6], x[1] - x[5], x[3] - x[7]
    quarter = turn(s15 - s37)
    spun_26, spun_37 = turn(d26), turn(d37)
    one, three = d15 + spun_37, d15 - spun_37
    spun_one, spun_three = turn(one), turn(three)
    one = ROOT * (one + spun_one)
    three = ROOT * (spun_three - three)
    return [
        (s04 + s26) + (s15 + s37),
        (d04 + spun_26) + one,
        (s04 - s26) + quarter,
        (d04 - spun_26) + three,
        (s04 + s26) - (s15 + s37),
        (d04 + spun_26) - one,
        (s04 - s26) - quarter,
        (d04 - spun_26) - three,
    ]


def solve_y_kernel(count_x, lines, total, wave, both, turns, out, held):
    count, rows, _ = lines.shape
    base = turns.shape[1]
    length = count * rows
    block = count_x * rows
    per = base // rows
    lanes = lane_index((base, LANES))
    sign = jnp.where(lanes < 64, 1.0, -1.0).astype(F32)

    def minus_i(z):
        return spin(z, 64) * sign

    def plus_i(z):
        return spin(z, 64) * -sign

    fields = [
        jnp.concatenate([lines[t * per + k] for k in range(per)], axis=0) for t in range(RADIX)
    ]
    mixed = eighths(fields, minus_i)
    mixed = [mixed[0]] + [
        mixed[r] * turns[r] + spin(mixed[r], 64) * turns[RADIX + r] for r in range(1, RADIX)
    ]
    tables = (both[: 2 * base], both[2 * base :])
    product = exact_dot(tables, split(jnp.concatenate(mixed, axis=1)))
    kx = wave[0:1, :]
    is_first = lanes % 64 < 32
    q = lax.broadcasted_iota(jnp.int32, (base, LANES), 0)
    edge = jnp.float32(-(length // 2))
    solved = []
    for r in range(RADIX):
        at = slice(r * LANES, (r + 1) * LANES)
        spectrum = product[:base, at] + minus_i(product[base:, at])
        k = RADIX * q + r
        ky = jnp.where(k < length // 2, k, k - length).astype(F32)
        cross = jnp.where((kx == edge) == (ky == edge), kx * ky, 0.0)
        symbol = jnp.where(is_first, kx * kx, cross) / (kx * kx + ky * ky)
        terms = symbol * spectrum
        solved.append(terms + spin(terms, -32))
    product = exact_dot(tables, split(jnp.concatenate(solved, axis=1)))
    mixed = []
    for r in range(RADIX):
        at = slice(r * LANES, (r + 1) * LANES)
        value = product[:base, at] + plus_i(product[base:, at])
        if r:
            value = value * turns[r] - spin(value, 64) * turns[RADIX + r]
        mixed.append(value)
    for t, values in enumerate(eighths(mixed, plus_i)):
        held[MARGIN + t * base : MARGIN + (t + 1) * base, :] = values
    held[0:MARGIN, :] = held[length : length + MARGIN, :]
    held[length + MARGIN : length + 2 * MARGIN, :] = held[MARGIN : 2 * MARGIN, :]
    spare = total[...] + spin(total[...], 32)
    kept = rows + 2 * MARGIN // count_x
    half = out.shape[1]
    rest = kept - half
    low = lane_index((8, LANES)) % 64 < 32
    for target in range(count):
        start = (target // count_x) * block + (target % count_x) * kept
        for row in range(0, half, 8):
            a = held[start + row : start + row + 8, :]
            if row < rest:
                b = spin(held[start + half + row : start + half + row + 8, :], 32)
            else:
                b = spare
            out[target, row : row + 8, :] = jnp.where(low, a, b)


def inverse_x_kernel(
    kept, scale, lines, tables, turns, out, held
):
    count, half, _ = lines.shape
    base = turns.shape[1]
    length = RADIX * base
    rest = kept - half
    low = lane_index((half, LANES)) % 64 < 32
    groups, spare = [], None
    for first in range(0, count, 2):
        even, odd = lines[first], lines[first + 1]
        a = jnp.where(low, even, spin(odd, 32))
        b = jnp.where(low, spin(even, -32), odd)
        groups.append(jnp.concatenate([a, b[:rest]], axis=0))
        extra = b[rest : rest + 8]
        spare = extra if spare is None else spare + extra
    mean = jnp.sum(spare) * scale
    wide = 2 * base // LANES
    narrow = base // LANES
    stacked = jnp.concatenate(
        [jnp.concatenate(groups[i * wide : (i + 1) * wide], axis=1) for i in range(3)], axis=0
    )
    place = 3 * wide
    zeros = jnp.concatenate(groups[place : place + narrow], axis=1)
    mids = jnp.concatenate(groups[place + narrow : place + 2 * narrow], axis=1)
    full, zero, middle = x_parts(tables, base)
    full = exact_dot(split(stacked), full)
    zero = exact_dot(split(zeros), zero) * scale
    mid = exact_dot(split(mids), middle) * scale
    turned = []
    for i in range(3):
        real = full[i * kept : (i + 1) * kept, :base]
        imag = full[i * kept : (i + 1) * kept, base:]
        c = turns[i : i + 1, :] * (2.0 * scale)
        s = turns[i + 3 : i + 4, :] * (2.0 * scale)
        turned.append((real * c - imag * s, real * s + imag * c))
    for t in range(RADIX):
        value = zero + mid if t % 2 == 0 else zero - mid
        for i, (real, imag) in enumerate(turned):
            eighth = t * (i + 1) % RADIX
            c = (1.0, ROOT, 0.0, -ROOT, -1.0, -ROOT, 0.0, ROOT)[eighth]
            s = (0.0, ROOT, 1.0, ROOT, 0.0, -ROOT, -1.0, -ROOT)[eighth]
            if c:
                value = value + c * real
            if s:
                value = value - s * imag
        held[:, t * base : (t + 1) * base] = mean - value
    targets, _, width = out.shape
    local = width - LANES
    right = lane_index((kept, LANES)) < 64
    for target in range(targets):
        out[target, :, :local] = held[:, target * local : (target + 1) * local]
        after = (target + 1) * local % length
        before = (target * local - LANES) % length
        out[target, :, local:] = jnp.where(
            right, held[:, after : after + LANES], held[:, before : before + LANES]
        )


def slopes_x(parts, band, with_edge):
    tiles = parts[0].shape[-1] // LANES
    pieces = []
    for first in list(range(0, tiles - 1, 2)) + ([tiles - 1] if with_edge else []):
        steps = (-1, 0, 1, 2) if first < tiles - 1 else (-1, 0, 1)
        table = band[...] if first < tiles - 1 else band[: 3 * LANES, :LANES]
        order = [(first + step) % tiles for step in steps]
        piece = None
        for part in parts:
            term = dot(jnp.concatenate([lane_tile(part, t) for t in order], axis=1), table)
            piece = term if piece is None else piece + term
        pieces.append(piece)
    return jnp.concatenate(pieces, axis=1)


def slope_y(read):
    value = read(3) - read(-3)
    for index in (0, 1):
        value = value + whole_weights[index] * (read(index + 1) - read(-index - 1))
    return value


def edged(k, side, center, up, down, above, below, sides, has):
    step = pl.program_id(0)
    last = pl.num_programs(0) - 1
    tile, width = center.shape
    tall = sides.shape[1]
    base = pl.multiple_of(step * tile, 8)
    at = slice(k * HALO, (k + 1) * HALO)
    over = sides[side, pl.ds(pl.multiple_of(jnp.maximum(base - HALO, 0), 8), HALO), :]
    under = sides[side, pl.ds(pl.multiple_of(jnp.minimum(base + tile, tall - HALO), 8), HALO), :]
    over = jnp.concatenate([up, over], axis=1)
    under = jnp.concatenate([down, under], axis=1)
    over = jnp.where(step == 0, above[at, :] * has[2], over)
    under = jnp.where(step == last, below[at, :] * has[3], under)
    inner = jnp.concatenate([center, sides[side, pl.ds(base, tile), :]], axis=1)
    return jnp.concatenate([over, inner, under], axis=0)


def edged_open(k, side, wall, wall_up, wall_down, above, below, sides, has):
    open_cells = [1.0 - ref[0].astype(F32) for ref in (wall, wall_up, wall_down)]
    return edged(k, side, *open_cells, above, below, sides, has)


def quiet_step_kernel(
    has, center, up, down, wall, wall_up, wall_down, above, below, sides, band, out, field, middle
):
    parts, _, tile, width = center.shape
    full = field.shape[2]
    high = tile + 2 * HALO
    guard = HALO
    blank = jnp.zeros((guard, full), F32)
    opened = edged_open(parts, parts, wall, wall_up, wall_down, above, below, sides, has)
    values = []
    for k in range(parts):
        value = edged(
            k,
            k,
            center[k, 0].astype(F32),
            up[k, 0].astype(F32)[up.shape[2] - HALO :],
            down[k, 0].astype(F32)[:HALO],
            above,
            below,
            sides,
            has,
        )
        field[k, 0:guard, :] = blank
        field[k, guard : guard + high, :] = value
        field[k, guard + high :, :] = blank
        values.append(value)

    def drops(ref, at, count, lanes, x):
        along_b = slope_y(lambda d: ref[2, at + d : at + d + count, :lanes])
        along_p = slope_y(lambda d: ref[3, at + d : at + d + count, :lanes])
        diverge = x[1] + along_b
        return (
            diverge + mean_flow * x[0],
            x[3] + mean_flow * x[1],
            along_p + mean_flow * x[2],
            diverge + mean_flow * x[3],
        )

    x = slopes_x((jnp.concatenate([v.astype(BF16) for v in values], axis=0),), band, True)
    x = [x[k * high : (k + 1) * high] for k in range(parts)]
    dropped = drops(field, guard, high, full, x)
    for k in range(parts):
        middle[k, 0:guard, :] = blank
        middle[k, guard + high :, :] = blank
        middle[k, guard : guard + high, :] = opened * (values[k] - (time_step / 60.0) * dropped[k])
    at = guard + HALO
    inner = [middle[k, at : at + tile, :] for k in range(parts)]
    x = slopes_x(split(jnp.concatenate(inner, axis=0)), band, False)
    x = [x[k * tile : (k + 1) * tile] for k in range(parts)]
    dropped = drops(middle, at, tile, width, x)
    shown = opened[HALO : HALO + tile, :width]
    for k in range(parts):
        start = 0.5 * field[k, at : at + tile, :width] - (0.5 * time_step / 60.0) * dropped[k]
        out[k] = shown * start + 0.5 * inner[k][:, :width]


def source_kernel(
    has, lines, velocity, flow_side, wall, wall_up, wall_down, above, below, sides, rise_x, rise_y, quiet, band, out, raised, forced
):
    step = pl.program_id(0)
    parts, tile, width = quiet.shape
    high = tile + 2 * HALO
    tiles = forced.shape[0]

    @pl.when(step == 0)
    def _():
        at = slice((parts + 1) * HALO, (parts + 2) * HALO)
        flow = jnp.concatenate([velocity[0, 0], flow_side[...]], axis=1)
        size = flow.shape[1]
        flow = jnp.concatenate([above[at, :size], flow, below[at, :size]], axis=0)
        count = lines.shape[0]
        level = jnp.concatenate([lines[k] for k in range(count)], axis=0)
        level = level[MARGIN - HALO : MARGIN - HALO + flow.shape[0]] - flow * flow
        cells = size // LANES
        near = lane_index((flow.shape[0], LANES)) < 64
        for k in range(cells):
            after, before = lane_tile(level, (k + 1) % cells), lane_tile(level, (k - 1) % cells)
            around = jnp.concatenate([lane_tile(level, k), jnp.where(near, after, before)], axis=1)
            out_lanes = 2 * LANES if k < cells - 1 else LANES
            value = exact_dot(split(around), split(rise_x[k][:, :out_lanes]))
            raised[:, 2 * k * LANES : 2 * k * LANES + out_lanes] = value

    half = high // 2
    start = pl.multiple_of(step * (tile // 2), 8)
    window = raised[pl.ds(start, half + HALO), :]
    weights = rise_y[pl.ds(start, half), :]
    taps = [
        pltpu.roll(window, half + HALO - (HALO // 2 - 1 + s), 0)[:half] for s in range(4)
    ]
    opened = time_step * edged_open(parts, 0, wall, wall_up, wall_down, above, below, sides, has)
    for parity in range(2):
        value = sum(weights[:, 4 * parity + s : 4 * parity + s + 1] * taps[s] for s in range(4))
        for t in range(tiles):
            forced[t, pl.ds(parity, half, 2), :] = lane_tile(value, t)
    for t in range(tiles):
        forced[t] = forced[t] * lane_tile(opened, t)
    inner = jnp.concatenate([forced[t, HALO : HALO + tile, :] for t in range(tiles)], axis=1)
    shown = (0.5 / 60.0) * opened[HALO : HALO + tile, :width]
    x = shown * slopes_x(split(inner), band, False)
    y = jnp.concatenate(
        [
            slope_y(lambda d: forced[t, HALO + d : HALO + d + tile, :])
            for t in range(width // LANES)
        ],
        axis=1,
    )
    out[0, 0] = quiet[0].astype(out.dtype)
    out[1, 0] = (quiet[1] - x).astype(out.dtype)
    out[2, 0] = (quiet[2] - shown * y).astype(out.dtype)
    out[3, 0] = (quiet[3] + inner[:, :width] - mean_flow * x).astype(out.dtype)


def call(kernel, operands, outs, scratch=(), steps=0, specs=None, out_specs=None, megabytes=24, flops=0, moved=0, name=None):
    def whole(array):
        zeros = (0,) * len(array.shape)
        return pl.BlockSpec(array.shape, lambda *_: zeros)

    arguments = {}
    if steps:
        chosen = specs or {}
        arguments["grid"] = (steps,)
        arguments["in_specs"] = [chosen.get(i, whole(o)) for i, o in enumerate(operands)]
        arguments["out_specs"] = jax.tree.map(whole, outs) if out_specs is None else out_specs
    return pl.pallas_call(
        kernel,
        out_shape=outs,
        scratch_shapes=list(scratch),
        compiler_params=pltpu.CompilerParams(vmem_limit_bytes=megabytes << 20),
        cost_estimate=pl.CostEstimate(flops=flops, bytes_accessed=moved, transcendentals=0),
        name=name,
        **arguments,
    )(*operands)


def ring(array, axis, step):
    size = lax.axis_size(axis)
    return lax.ppermute(array, axis, [(i, (i + step) % size) for i in range(size)])


def shaped(*shape, kind=F32):
    return jax.ShapeDtypeStruct(shape, kind)


def pressure_lines(sent, count_y):
    count_x, _, rows, local_x = sent.shape
    count = count_x * count_y
    length_x, length_y = local_x * count_x, rows * count
    lines = lax.all_to_all(sent, "gx", 0, 0, tiled=True)
    full, zero, middle, cos_turn, sin_turn = x_tables(length_x)
    turns = np.zeros((8, cos_turn.shape[1]), np.float32)
    turns[0:3], turns[3:6] = cos_turn, sin_turn
    spectra, total = call(
        forward_x_kernel,
        (lines, np.concatenate([beside(full), beside(zero, middle)]), turns),
        (shaped(count, rows, LANES), shaped(8, LANES)),
        flops=10**9,
        moved=4 << 20,
        name="forward_x",
    )
    spectra = lax.all_to_all(spectra, ("gy", "gx"), 0, 0, tiled=True)
    place = lax.axis_index("gy") * count_x + lax.axis_index("gx")
    waves = jnp.asarray(wave_table(length_x, count))
    wave = lax.dynamic_slice(waves, (place, 0), (1, LANES))
    both, cos_rows, sin_rows = y_tables(length_y)
    kept = rows + 2 * MARGIN // count_x
    half = (kept // 2 + 8) // 8 * 8
    solved = call(
        functools.partial(solve_y_kernel, count_x),
        (spectra, total, wave, beside(both), np.concatenate([cos_rows, sin_rows], axis=0)),
        shaped(count, half, LANES),
        (pltpu.VMEM((length_y + 2 * MARGIN, LANES), F32),),
        flops=4 * 10**9,
        moved=6 << 20,
        name="solve_y",
    )
    solved = lax.all_to_all(solved, ("gy", "gx"), 0, 0, tiled=True)
    back = 2.0 * zero.T
    back[LANES // 2] *= 0.5
    tables = np.concatenate(
        [beside(full.T), beside(back, 2.0 * middle.T)]
    )
    pressed = call(
        functools.partial(inverse_x_kernel, kept, 1.0 / (length_x * length_y)),
        (solved, tables, turns),
        shaped(count_x, kept, local_x + LANES),
        (pltpu.VMEM((kept, length_x), F32),),
        flops=10**9,
        moved=4 << 20,
        name="inverse_x",
    )
    return lax.all_to_all(pressed, "gx", 0, 0, tiled=True)


def refine_tables(weights_x, weights_y, tall, wide):
    first = lax.axis_index("gx") * wide
    ends = jnp.concatenate([weights_x[:, -LANES:], weights_x, weights_x[:, :LANES]], axis=1)
    own = lax.dynamic_slice(ends, (0, first), (4, wide + 2 * LANES))
    half = LANES // 2
    edge = jnp.concatenate([own[:, wide + LANES : wide + LANES + half], own[:, half:LANES]], axis=1)
    edge = jnp.pad(edge, ((0, 0), (0, LANES)))
    tiles = wide // (2 * LANES)
    weights = jnp.concatenate([own[:, LANES : wide + LANES], edge], axis=1)
    weights = weights.reshape(4, tiles + 1, 1, 2 * LANES)
    fine = np.arange(2 * LANES)
    targets = np.tile(fine // 2 - 1, (tiles + 1, 1))
    targets[tiles] = np.where(fine < half, fine // 2 - 1, half + fine // 2 - 1)
    cells = lax.broadcasted_iota(jnp.int32, (tiles + 1, 2 * LANES, 2 * LANES), 1)
    targets = jnp.asarray(targets[:, None, :].astype(np.int32))
    rise_x = sum(
        jnp.where(cells == (targets + t) % (2 * LANES), weights[t], 0.0) for t in range(4)
    )
    ends = jnp.concatenate([weights_y[:, -HALO:], weights_y, weights_y[:, :HALO]], axis=1)
    own = lax.dynamic_slice(ends, (0, lax.axis_index("gy") * tall), (4, tall + 2 * HALO))
    rise_y = own.reshape(4, tall // 2 + HALO, 2).transpose(1, 2, 0).reshape(tall // 2 + HALO, 8)
    return rise_x, rise_y


def fast_shards(velocity, weights_x, weights_y, acoustic, wall_mask):
    parts, _, tall, wide = acoustic.shape
    _, _, local_y, local_x = velocity.shape
    count_x, count_y = lax.axis_size("gx"), lax.axis_size("gy")
    place_x, place_y = lax.axis_index("gx"), lax.axis_index("gy")
    full, high, steps = wide + LANES, TILE + 2 * HALO, tall // TILE
    strips = (parts + 2) * HALO
    small = 2 * HALO
    ends = ((0, 0, 0, 0), (0, 0, 0, wide // LANES - 1))
    has = jnp.stack([place_x > 0, place_x < count_x - 1, place_y > 0, place_y < count_y - 1])
    has = has.astype(F32)
    scalars = pl.BlockSpec(memory_space=pltpu.SMEM)

    def at(block, *index):
        return pl.BlockSpec(block, lambda i: index)

    sent, to_right, to_left = call(
        edges_kernel,
        (velocity, acoustic, acoustic, wall_mask, wall_mask),
        (
            shaped(count_x, 2, local_y // count_x, local_x),
            shaped(strips, tall),
            shaped(strips, tall),
        ),
        steps=1,
        specs={
            1: at((parts, 1, tall, LANES), 0, 0, 0, 0),
            2: at((parts, 1, tall, LANES), 0, 0, 0, wide // LANES - 1),
            3: at((1, tall, LANES), 0, 0, 0),
            4: at((1, tall, LANES), 0, 0, wide // LANES - 1),
        },
        moved=6 << 20,
        name="edges",
    )
    lines = pressure_lines(sent, count_y)
    from_left, from_right = ring(to_right, "gx", 1), ring(to_left, "gx", -1)
    sides, flow_side, first, last = call(
        sides_kernel,
        (has, from_left, from_right, acoustic, acoustic, wall_mask, wall_mask, velocity, velocity),
        (
            shaped(parts + 1, tall, LANES),
            shaped(local_y, LANES),
            shaped(strips, full),
            shaped(strips, full),
        ),
        steps=1,
        specs={
            0: scalars,
            3: at((parts, 1, small, wide), 0, 0, 0, 0),
            4: at((parts, 1, small, wide), 0, 0, tall // small - 1, 0),
            5: at((1, HALO, wide), 0, 0, 0),
            6: at((1, HALO, wide), 0, tall // HALO - 1, 0),
            7: at((1, 1, HALO, local_x), 1, 0, 0, 0),
            8: at((1, 1, HALO, local_x), 1, 0, local_y // HALO - 1, 0),
        },
        moved=6 << 20,
        name="sides",
    )
    above, below = ring(last, "gy", 1), ring(first, "gy", -1)
    band = band_table()
    per, rows = TILE // small, TILE // HALO
    walls = (
        pl.BlockSpec((1, TILE, wide), lambda i: (0, i, 0)),
        pl.BlockSpec((1, HALO, wide), lambda i: (0, jnp.maximum(i * rows - 1, 0), 0)),
        pl.BlockSpec((1, HALO, wide), lambda i: (0, jnp.minimum((i + 1) * rows, steps * rows - 1), 0)),
    )
    by_tile = pl.BlockSpec((parts, 1, TILE, wide), lambda i: (0, 0, i, 0))
    over = pl.BlockSpec((parts, 1, small, wide), lambda i: (0, 0, jnp.maximum(i * per - 1, 0), 0))
    under = pl.BlockSpec(
        (parts, 1, small, wide), lambda i: (0, 0, jnp.minimum((i + 1) * per, steps * per - 1), 0)
    )
    flat = pl.BlockSpec((parts, TILE, wide), lambda i: (0, i, 0))
    quiet = call(
        quiet_step_kernel,
        (has, acoustic, acoustic, acoustic, wall_mask, wall_mask, wall_mask, above, below, sides, band),
        shaped(parts, tall, wide),
        (pltpu.VMEM((parts, high + 2 * HALO, full), F32),) * 2,
        steps=steps,
        specs=dict(enumerate((scalars, by_tile, over, under) + walls)),
        out_specs=flat,
        megabytes=36,
        flops=9 * 10**9,
        moved=50 << 20,
        name="quiet_step",
    )
    rise_x, rise_y = refine_tables(weights_x, weights_y, tall, wide)
    operands = (has, lines, velocity, flow_side, wall_mask, wall_mask, wall_mask, above, below, sides, rise_x, rise_y, quiet, band)
    specs = {
        0: scalars,
        2: at((1, 1, local_y, local_x), 1, 0, 0, 0),
        9: at((1, tall, LANES), parts, 0, 0),
        12: flat,
    }
    specs.update({4 + i: spec for i, spec in enumerate(walls)})
    return call(
        source_kernel,
        operands,
        shaped(*acoustic.shape, kind=BF16),
        (pltpu.VMEM((local_y + 2 * HALO, full), F32), pltpu.VMEM((full // LANES, high, LANES), F32)),
        steps=steps,
        specs=specs,
        out_specs=by_tile,
        flops=4 * 10**9,
        moved=16 << 20,
        name="source_step",
    )


def fits(count_x, count_y, velocity, acoustic):
    _, planes, local_y, local_x = velocity
    _, _, tall, wide = acoustic
    length_x, length_y = local_x * count_x, local_y * count_y
    rows = local_y // count_x
    base_x, base_y = length_x // RADIX, length_y // RADIX
    return (
        planes == 1
        and length_x * 2 == count_x * count_y * LANES
        and base_x % (2 * LANES) == 0
        and local_x % base_x == 0
        and rows % 8 == 0
        and base_y % rows == 0
        and base_y % 8 == 0
        and MARGIN * 2 % (8 * count_x) == 0
        and tall == 2 * local_y
        and wide == 2 * local_x
        and tall % TILE == 0
        and wide % (2 * LANES) == 0
    )


def extended(array, sides, width):
    for axis, dim in sides:
        size, length = (lax.axis_size(axis), array.shape[dim])
        up = [(i, (i + 1) % size) for i in range(size - 1)]
        down = [(j, i) for i, j in up]
        last = lax.slice_in_dim(array, length - width, length, axis=dim)
        leading = lax.slice_in_dim(array, 0, width, axis=dim)
        before = lax.ppermute(last, axis, up)
        after = lax.ppermute(leading, axis, down)
        array = jnp.concatenate([before, array, after], axis=dim)
    return array


def gradients(padded):
    height = padded.shape[-2] - 6
    breadth = padded.shape[-1] - 6
    rows_mid = padded[..., 3 : 3 + height, :]
    cols_mid = padded[..., :, 3 : 3 + breadth]
    along_x = jnp.zeros_like(padded[..., 3 : 3 + height, 3 : 3 + breadth])
    along_y = jnp.zeros_like(along_x)
    for index, weight in enumerate(stencil_weights):
        distance = index + 1
        along_x = along_x + weight * (
            rows_mid[..., 3 + distance : 3 + distance + breadth]
            - rows_mid[..., 3 - distance : 3 - distance + breadth]
        )
        along_y = along_y + weight * (
            cols_mid[..., 3 + distance : 3 + distance + height, :]
            - cols_mid[..., 3 - distance : 3 - distance + height, :]
        )
    return (along_x, along_y)


def tendency(padded, source):
    along_x, along_y = gradients(padded)
    diverge = along_x[1] + along_y[2]
    forcing = jnp.stack([-diverge, -along_x[3], -along_y[3], source - diverge])
    return forcing - mean_flow * along_x


def spectral_index(flat, length):
    second = length // 16
    wave = flat // second + 16 * (flat % second)
    return jnp.where(wave < length // 2, wave, wave - length).astype(jnp.float32)


def twiddles(rows_count, cols_count, modulus, sign):
    products = jnp.arange(rows_count)[:, None] * jnp.arange(cols_count)[None, :] % modulus
    angles = 2.0 * math.pi / modulus * products.astype(jnp.float32)
    return (jnp.cos(angles), sign * jnp.sin(angles))


def mix_rows(real_part, imag_part, cosine, sine):
    exact = lax.Precision.HIGHEST
    cos_real = jnp.einsum("ka,...ab->...kb", cosine, real_part, precision=exact)
    cos_imag = jnp.einsum("ka,...ab->...kb", cosine, imag_part, precision=exact)
    sin_real = jnp.einsum("ka,...ab->...kb", sine, real_part, precision=exact)
    sin_imag = jnp.einsum("ka,...ab->...kb", sine, imag_part, precision=exact)
    return (cos_real - sin_imag, cos_imag + sin_real)


def mix_cols(real_part, imag_part, cosine, sine):
    exact = lax.Precision.HIGHEST
    cos_real = jnp.einsum("...kb,bc->...kc", real_part, cosine, precision=exact)
    cos_imag = jnp.einsum("...kb,bc->...kc", imag_part, cosine, precision=exact)
    sin_real = jnp.einsum("...kb,bc->...kc", real_part, sine, precision=exact)
    sin_imag = jnp.einsum("...kb,bc->...kc", imag_part, sine, precision=exact)
    return (cos_real - sin_imag, cos_imag + sin_real)


def rotate(real_part, imag_part, cosine, sine):
    return (real_part * cosine - imag_part * sine, real_part * sine + imag_part * cosine)


def discrete(real_part, imag_part, sign):
    length = real_part.shape[-1]
    second = length // 16
    initial = real_part.shape
    folded = initial[:-1] + (16, second)
    real_part = real_part.reshape(folded)
    imag_part = imag_part.reshape(folded)
    small_cos, small_sin = twiddles(16, 16, 16, sign)
    large_cos, large_sin = twiddles(second, second, second, sign)
    turn_cos, turn_sin = twiddles(16, second, length, sign)
    if sign < 0:
        real_part, imag_part = mix_rows(real_part, imag_part, small_cos, small_sin)
        real_part, imag_part = rotate(real_part, imag_part, turn_cos, turn_sin)
        real_part, imag_part = mix_cols(real_part, imag_part, large_cos, large_sin)
    else:
        real_part, imag_part = mix_cols(real_part, imag_part, large_cos, large_sin)
        real_part, imag_part = rotate(real_part, imag_part, turn_cos, turn_sin)
        real_part, imag_part = mix_rows(real_part, imag_part, small_cos, small_sin)
        real_part = real_part / length
        imag_part = imag_part / length
    return (real_part.reshape(initial), imag_part.reshape(initial))


def transform(stacked, sign, kind):
    if kind == "real_in":
        real_part = stacked
        imag_part = jnp.zeros_like(stacked)
    else:
        half = stacked.shape[0] // 2
        real_part = stacked[:half]
        imag_part = stacked[half:]
    real_out, imag_out = discrete(real_part, imag_part, sign)
    if kind == "real_out":
        return real_out
    return jnp.concatenate([real_out, imag_out], axis=0)


def project(stacked, wave_x, wave_y):
    coef_xx = wave_x * wave_x
    coef_xy = 2.0 * wave_x * wave_y
    coef_yy = wave_y * wave_y
    denominator = wave_x * wave_x + wave_y * wave_y
    positive = denominator > 0
    safe = jnp.where(positive, denominator, 1.0)

    def combine(parts):
        numerator = -(coef_xx * parts[0] + coef_xy * parts[1] + coef_yy * parts[2])
        return jnp.where(positive, numerator / safe, 0.0)

    return jnp.stack([combine(stacked[:3]), combine(stacked[3:])])


def refine(stacked, weights):
    result = jnp.zeros(stacked.shape[:-1] + (2 * stacked.shape[-1],), jnp.float32)
    for offset in range(4):
        result = (
            result
            + jnp.repeat(jnp.roll(stacked, 1 - offset, axis=-1), 2, axis=-1) * weights[offset]
        )
    return result


def lines_x(stacked, action):
    gathered = action(lax.all_to_all(stacked, "gx", split_axis=2, concat_axis=3, tiled=True))
    return lax.all_to_all(gathered, "gx", split_axis=3, concat_axis=2, tiled=True)


def lines_y(stacked, action):
    turned = jnp.swapaxes(stacked, 2, 3)
    gathered = action(lax.all_to_all(turned, "gy", split_axis=2, concat_axis=3, tiled=True))
    returned = lax.all_to_all(gathered, "gy", split_axis=3, concat_axis=2, tiled=True)
    return jnp.swapaxes(returned, 2, 3)


def expand(fields):
    return extended(fields, (("gx", 3), ("gy", 2)), 3)


def shards(velocity, weights_x, weights_y, acoustic, wall_mask):
    acoustic = acoustic.astype(jnp.float32)
    flow_x = velocity[0]
    flow_y = velocity[1]
    tensor = jnp.stack([flow_x * flow_x, flow_x * flow_y, flow_y * flow_y])
    count_gx = lax.axis_size("gx")
    count_gy = lax.axis_size("gy")
    place_x = lax.axis_index("gx")
    place_y = lax.axis_index("gy")
    local_y = tensor.shape[2]
    local_x = tensor.shape[3]
    length_x = local_x * count_gx
    length_y = local_y * count_gy

    def forward_real(portion):
        return transform(portion, -1, "real_in")

    def finish_x(portion):
        return refine(transform(portion, 1, "real_out"), weights_x)

    spectra = lines_x(tensor, forward_real)
    share_x = local_x // count_gy
    line_x = spectral_index(place_x * local_x + place_y * share_x + jnp.arange(share_x), length_x)[
        :, None
    ]
    line_y = spectral_index(jnp.arange(length_y), length_y)[None, :]

    def solve_y(portion):
        solved = project(transform(portion, -1, "complex"), line_x, line_y)
        return refine(transform(solved, 1, "complex"), weights_y)

    pressure = lines_y(spectra, solve_y)
    source = lines_x(pressure, finish_x)[0]
    open_cells = (1 - wall_mask).astype(jnp.float32)
    first_rate = tendency(expand(acoustic), source)
    middle = open_cells * (acoustic + time_step * first_rate)
    second_rate = tendency(expand(middle), source)
    return (open_cells * (acoustic + 0.5 * time_step * (first_rate + second_rate))).astype(
        jnp.bfloat16
    )


def solution(mesh):
    in_specs = (P(None, None, "gy", "gx"), P(), P(), P(None, None, "gy", "gx"), P(None, "gy", "gx"))
    out_specs = P(None, None, "gy", "gx")

    def chosen(velocity, weights_x, weights_y, acoustic, wall_mask):
        sizes = (mesh.shape["gx"], mesh.shape["gy"], velocity.shape, acoustic.shape)
        plan = fast_shards if fits(*sizes) else shards
        return plan(velocity, weights_x, weights_y, acoustic, wall_mask)

    return jax.shard_map(
        chosen, mesh=mesh, in_specs=in_specs, out_specs=out_specs, check_vma=False
    )
```

```python
import functools
import math

import jax
import jax.numpy as jnp
import ml_dtypes
import numpy as np
from jax import lax
from jax.experimental import pallas as pl
from jax.experimental.pallas import tpu as pltpu
from jax.sharding import PartitionSpec as P

stencil_weights = (0.75, -0.15, 1.0 / 60.0)
mean_flow = 0.3
time_step = 0.5
whole_weights = (45.0, -9.0, 1.0)

LANES = 128
RADIX = 8
HALO = 8
MARGIN = 16
TILE = 128
ROOT = math.sqrt(0.5)
BF16 = jnp.bfloat16
F32 = jnp.float32


def halves(table):
    high = table.astype(np.float32).astype(ml_dtypes.bfloat16)
    low = (table - high.astype(np.float64)).astype(np.float32).astype(ml_dtypes.bfloat16)
    return high, low


def packed_columns(cosine, sine):
    half = LANES // 2
    parts = []
    for first in range(0, cosine.shape[1], half):
        parts += [cosine[:, first : first + half], sine[:, first : first + half]]
    return np.concatenate(parts, axis=1)


@functools.lru_cache(maxsize=None)
def x_tables(length):
    base = length // RADIX
    m = np.arange(base)[:, None]
    q = np.arange(base)[None, :]
    angle = 2.0 * np.pi * ((m * q) % base) / base
    cosine, sine = np.cos(angle), np.sin(angle)
    full = np.concatenate([packed_columns(cosine, -sine), packed_columns(sine, cosine)], axis=0)
    half = base // 2
    zero_cos, zero_sin = cosine[:, :half].copy(), -sine[:, :half]
    zero_cos[:, 0] = 0.0
    zero_sin = zero_sin.copy()
    zero_sin[:, 0] = (-1.0) ** np.arange(base)
    zero = packed_columns(zero_cos, zero_sin)
    shifted = 2.0 * np.pi * ((m * (RADIX * q[:, :half] + RADIX // 2)) % length) / length
    middle = packed_columns(np.cos(shifted), -np.sin(shifted))
    turns = 2.0 * np.pi * np.arange(1, RADIX // 2)[:, None] * np.arange(base)[None, :] / length
    return full, zero, middle, np.cos(turns), np.sin(turns)


@functools.lru_cache(maxsize=None)
def y_tables(length):
    base = length // RADIX
    index = np.arange(base)
    angle = 2.0 * np.pi * ((index[:, None] * index[None, :]) % base) / base
    both = np.concatenate([np.cos(angle), np.sin(angle)], axis=0)
    turns = 2.0 * np.pi * np.arange(RADIX)[:, None] * index[None, :] / length
    return both, np.concatenate([np.cos(turns), np.sin(turns)], axis=0).T.astype(np.float32)


@functools.lru_cache(maxsize=None)
def wave_table(length, count):
    slots = LANES // 4
    base = length // RADIX
    waves = []
    for residue in (1, 2, 3):
        waves.append(RADIX * np.arange(base) + residue)
    waves.append(RADIX * np.arange(base // 2))
    waves.append(RADIX * np.arange(base // 2) + RADIX // 2)
    waves = np.concatenate(waves)
    waves = np.where(waves == 0, length // 2, waves)
    waves = np.where(waves < length // 2, waves, waves - length).reshape(count, slots)
    return np.tile(waves, (1, 4)).astype(np.float32)


@functools.lru_cache(maxsize=None)
def band_table():
    band = np.zeros((4 * LANES, 2 * LANES))
    column = np.arange(2 * LANES)
    for index, weight in enumerate(whole_weights):
        band[column + LANES + index + 1, column] = weight
        band[column + LANES - index - 1, column] = -weight
    return band.astype(ml_dtypes.bfloat16)


def beside(*tables):
    high, low = halves(np.concatenate(tables, axis=1))
    return np.concatenate([high, low], axis=0)


def split(values):
    high = values.astype(BF16)
    return high, (values - high.astype(F32)).astype(BF16)


def dot(left, right):
    return jnp.dot(left, right, preferred_element_type=F32)


def exact_dot(left, right):
    left_high, left_low = left
    right_high, right_low = right
    return dot(left_high, right_high) + (dot(left_low, right_high) + dot(left_high, right_low))


def lane_index(shape):
    return lax.broadcasted_iota(jnp.int32, shape, len(shape) - 1)


def spin(values, shift):
    return pltpu.roll(values, shift % values.shape[-1], values.ndim - 1)


def lane_tile(values, index):
    return values[:, index * LANES : (index + 1) * LANES]


def x_parts(tables, base):
    wide = 2 * base
    full = (tables[:wide], tables[wide : 2 * wide])
    at = 2 * wide
    high, low = tables[at : at + base], tables[at + base : at + 2 * base]
    return full, (high[:, :base], low[:, :base]), (high[:, base:], low[:, base:])


def edges_kernel(velocity, left, right, left_wall, right_wall, sent, to_right, to_left):
    count, _, rows, width = sent.shape
    for e in range(count):
        for c in range(2):
            sent[e, c] = velocity[c, 0, e * rows : (e + 1) * rows, :]
    parts = left.shape[0]
    flow_rows = count * rows
    for k in range(parts + 1):
        at = slice(k * HALO, (k + 1) * HALO)
        if k < parts:
            first, last = left[k, 0].astype(F32), right[k, 0].astype(F32)
        else:
            first, last = 1.0 - left_wall[0].astype(F32), 1.0 - right_wall[0].astype(F32)
        to_left[at, :] = first.T[:HALO]
        to_right[at, :] = last.T[LANES - HALO :]
    at = slice((parts + 1) * HALO, (parts + 2) * HALO)
    blank = jnp.zeros((HALO, to_left.shape[1]), F32)
    to_left[at, :] = blank
    to_right[at, :] = blank
    to_left[at, :flow_rows] = velocity[1, 0, :, :LANES].T[:HALO]
    to_right[at, :flow_rows] = velocity[1, 0, :, width - LANES :].T[LANES - HALO :]


def sides_kernel(
    has, from_left, from_right, first_rows, last_rows, first_wall, last_wall, first_flow, last_flow, sides, flow_side, first, last, mark
):
    parts, _, small, width = first_rows.shape
    flow_rows, local = flow_side.shape[0], first_flow.shape[-1]
    tall = sides.shape[1]
    gap = jnp.zeros((LANES - 2 * HALO, tall), F32)
    for k in range(parts + 1):
        at = slice(k * HALO, (k + 1) * HALO)
        tile = jnp.concatenate([from_right[at, :] * has[1], gap, from_left[at, :] * has[0]], axis=0).T
        sides[k] = tile
        if k < parts:
            top, low = first_rows[k, 0].astype(F32)[:HALO], last_rows[k, 0].astype(F32)[small - HALO :]
        else:
            top, low = 1.0 - first_wall[0].astype(F32), 1.0 - last_wall[0].astype(F32)
        first[at, :width] = top
        first[at, width:] = tile[:HALO]
        last[at, :width] = low
        last[at, width:] = tile[tall - HALO :]
    at = slice((parts + 1) * HALO, (parts + 2) * HALO)
    gap = gap[:, :flow_rows]
    tile = jnp.concatenate([from_right[at, :flow_rows], gap, from_left[at, :flow_rows]], axis=0).T
    flow_side[...] = tile
    blank = jnp.zeros((HALO, first.shape[1]), F32)
    first[at, :] = blank
    last[at, :] = blank
    first[at, :local] = first_flow[0, 0]
    last[at, :local] = last_flow[0, 0]
    first[at, local : local + LANES] = tile[:HALO]
    last[at, local : local + LANES] = tile[flow_rows - HALO :]
    mark[...] = jnp.zeros(mark.shape, F32)


def forward_x_kernel(lines, tables, turns, out, total):
    count, _, rows, local = lines.shape
    base = turns.shape[1]
    per = local // base
    u = [lines[t // per, 0, :, (t % per) * base : (t % per + 1) * base] for t in range(RADIX)]
    v = [lines[t // per, 1, :, (t % per) * base : (t % per + 1) * base] for t in range(RADIX)]
    energy = sum(b * b for b in v)
    energy = jnp.sum(energy.reshape(rows // 8, 8, base), axis=0)
    total[...] = sum(energy[:, k : k + LANES] for k in range(0, base, LANES))
    fields = ([a * a - b * b for a, b in zip(u, v)], [2.0 * a * b for a, b in zip(u, v)])
    zeros, mids, reals, imags = [], [], [[], [], []], [[], [], []]
    for a in fields:
        s04, s26, s15, s37 = a[0] + a[4], a[2] + a[6], a[1] + a[5], a[3] + a[7]
        d04, d26, d15, d37 = a[0] - a[4], a[2] - a[6], a[1] - a[5], a[3] - a[7]
        zeros.append((s04 + s26) + (s15 + s37))
        mids.append((s04 + s26) - (s15 + s37))
        minus, plus = ROOT * (d15 - d37), ROOT * (d15 + d37)
        turned = (
            (d04 + minus, -d26 - plus),
            (s04 - s26, s37 - s15),
            (d04 - minus, d26 - plus),
        )
        for index, (real, imag) in enumerate(turned):
            c, s = turns[index : index + 1, :], turns[index + 3 : index + 4, :]
            reals[index].append(real * c + imag * s)
            imags[index].append(imag * c - real * s)
    stacked = jnp.concatenate(
        [
            jnp.concatenate([jnp.concatenate(reals[i], axis=0) for i in range(3)], axis=0),
            jnp.concatenate([jnp.concatenate(imags[i], axis=0) for i in range(3)], axis=0),
        ],
        axis=1,
    )
    full, zero, middle = x_parts(tables, base)
    full = exact_dot(split(stacked), full)
    zero = exact_dot(split(jnp.concatenate(zeros, axis=0)), zero)
    middle = exact_dot(split(jnp.concatenate(mids, axis=0)), middle)
    low = lane_index((rows, LANES)) % 64 < 32
    place = 0
    blocks = [full[2 * rows * i : 2 * rows * (i + 1)] for i in range(3)] + [zero, middle]
    for block in blocks:
        for first in range(0, block.shape[1], LANES):
            a = block[:rows, first : first + LANES]
            c = block[rows:, first : first + LANES]
            out[place] = jnp.where(low, a, spin(c, 32))
            out[place + 1] = jnp.where(low, spin(a, -32), c)
            place += 2


def eighths(x, turn):
    s04, s26, s15, s37 = x[0] + x[4], x[2] + x[6], x[1] + x[5], x[3] + x[7]
    d04, d26, d15, d37 = x[0] - x[4], x[2] - x[6], x[1] - x[5], x[3] - x[7]
    quarter = turn(s15 - s37)
    spun_26, spun_37 = turn(d26), turn(d37)
    one, three = d15 + spun_37, d15 - spun_37
    spun_one, spun_three = turn(one), turn(three)
    one = ROOT * (one + spun_one)
    three = ROOT * (spun_three - three)
    return [
        (s04 + s26) + (s15 + s37),
        (d04 + spun_26) + one,
        (s04 - s26) + quarter,
        (d04 - spun_26) + three,
        (s04 + s26) - (s15 + s37),
        (d04 + spun_26) - one,
        (s04 - s26) - quarter,
        (d04 - spun_26) - three,
    ]


def solve_y_kernel(count_x, lines, total, wave, both, turns, out, held):
    count, rows, _ = lines.shape
    base = turns.shape[0]
    length = count * rows
    block = count_x * rows
    per = base // rows
    lanes = lane_index((base, LANES))
    sign = jnp.where(lanes < 64, 1.0, -1.0).astype(F32)

    def minus_i(z):
        return spin(z, 64) * sign

    def plus_i(z):
        return spin(z, 64) * -sign

    fields = [
        jnp.concatenate([lines[t * per + k] for k in range(per)], axis=0) for t in range(RADIX)
    ]
    mixed = eighths(fields, minus_i)
    table = turns[...]
    cosines = [table[:, r : r + 1] for r in range(RADIX)]
    sines = [table[:, RADIX + r : RADIX + r + 1] * sign for r in range(RADIX)]
    mixed = [mixed[0]] + [
        mixed[r] * cosines[r] + spin(mixed[r], 64) * sines[r] for r in range(1, RADIX)
    ]
    tables = (both[: 2 * base], both[2 * base :])
    product = exact_dot(tables, split(jnp.concatenate(mixed, axis=1)))
    kx = wave[0:1, :]
    is_first = lanes % 64 < 32
    q = lax.broadcasted_iota(jnp.int32, (base, LANES), 0)
    edge = jnp.float32(-(length // 2))
    solved = []
    for r in range(RADIX):
        at = slice(r * LANES, (r + 1) * LANES)
        spectrum = product[:base, at] + minus_i(product[base:, at])
        k = RADIX * q + r
        ky = jnp.where(k < length // 2, k, k - length).astype(F32)
        cross = jnp.where((kx == edge) == (ky == edge), kx * ky, 0.0)
        symbol = jnp.where(is_first, kx * kx, cross) / (kx * kx + ky * ky)
        terms = symbol * spectrum
        solved.append(terms + spin(terms, -32))
    product = exact_dot(tables, split(jnp.concatenate(solved, axis=1)))
    mixed = []
    for r in range(RADIX):
        at = slice(r * LANES, (r + 1) * LANES)
        value = product[:base, at] + plus_i(product[base:, at])
        if r:
            value = value * cosines[r] - spin(value, 64) * sines[r]
        mixed.append(value)
    for t, values in enumerate(eighths(mixed, plus_i)):
        held[MARGIN + t * base : MARGIN + (t + 1) * base, :] = values
    held[0:MARGIN, :] = held[length : length + MARGIN, :]
    held[length + MARGIN : length + 2 * MARGIN, :] = held[MARGIN : 2 * MARGIN, :]
    spare = total[...] + spin(total[...], 32)
    kept = rows + 2 * MARGIN // count_x
    half = out.shape[1]
    rest = kept - half
    low = lane_index((8, LANES)) % 64 < 32
    for target in range(count):
        start = (target // count_x) * block + (target % count_x) * kept
        for row in range(0, half, 8):
            a = held[start + row : start + row + 8, :]
            if row < rest:
                b = spin(held[start + half + row : start + half + row + 8, :], 32)
            else:
                b = spare
            out[target, row : row + 8, :] = jnp.where(low, a, b)


def inverse_x_kernel(
    kept, scale, lines, tables, turns, out, held
):
    count, half, _ = lines.shape
    base = turns.shape[1]
    length = RADIX * base
    rest = kept - half
    low = lane_index((half, LANES)) % 64 < 32
    groups, spare = [], None
    for first in range(0, count, 2):
        even, odd = lines[first], lines[first + 1]
        a = jnp.where(low, even, spin(odd, 32))
        b = jnp.where(low, spin(even, -32), odd)
        groups.append(jnp.concatenate([a, b[:rest]], axis=0))
        extra = b[rest : rest + 8]
        spare = extra if spare is None else spare + extra
    mean = jnp.sum(spare) * scale
    wide = 2 * base // LANES
    narrow = base // LANES
    stacked = jnp.concatenate(
        [jnp.concatenate(groups[i * wide : (i + 1) * wide], axis=1) for i in range(3)], axis=0
    )
    place = 3 * wide
    zeros = jnp.concatenate(groups[place : place + narrow], axis=1)
    mids = jnp.concatenate(groups[place + narrow : place + 2 * narrow], axis=1)
    full, zero, middle = x_parts(tables, base)
    full = exact_dot(split(stacked), full)
    zero = exact_dot(split(zeros), zero) * scale
    mid = exact_dot(split(mids), middle) * scale
    turned = []
    for i in range(3):
        real = full[i * kept : (i + 1) * kept, :base]
        imag = full[i * kept : (i + 1) * kept, base:]
        c = turns[i : i + 1, :] * (2.0 * scale)
        s = turns[i + 3 : i + 4, :] * (2.0 * scale)
        turned.append((real * c - imag * s, real * s + imag * c))
    for t in range(RADIX):
        value = zero + mid if t % 2 == 0 else zero - mid
        for i, (real, imag) in enumerate(turned):
            eighth = t * (i + 1) % RADIX
            c = (1.0, ROOT, 0.0, -ROOT, -1.0, -ROOT, 0.0, ROOT)[eighth]
            s = (0.0, ROOT, 1.0, ROOT, 0.0, -ROOT, -1.0, -ROOT)[eighth]
            if c:
                value = value + c * real
            if s:
                value = value - s * imag
        held[:, t * base : (t + 1) * base] = mean - value
    targets, _, width = out.shape
    local = width - LANES
    right = lane_index((kept, LANES)) < 64
    for target in range(targets):
        out[target, :, :local] = held[:, target * local : (target + 1) * local]
        after = (target + 1) * local % length
        before = (target * local - LANES) % length
        out[target, :, local:] = jnp.where(
            right, held[:, after : after + LANES], held[:, before : before + LANES]
        )


def slopes_x(parts, band, with_edge):
    tiles = parts[0].shape[-1] // LANES
    pieces = []
    for first in list(range(0, tiles - 1, 2)) + ([tiles - 1] if with_edge else []):
        steps = (-1, 0, 1, 2) if first < tiles - 1 else (-1, 0, 1)
        table = band[...] if first < tiles - 1 else band[: 3 * LANES, :LANES]
        order = [(first + step) % tiles for step in steps]
        piece = None
        for part in parts:
            term = dot(jnp.concatenate([lane_tile(part, t) for t in order], axis=1), table)
            piece = term if piece is None else piece + term
        pieces.append(piece)
    return jnp.concatenate(pieces, axis=1)


def slope_y(read):
    value = read(3) - read(-3)
    for index in (0, 1):
        value = value + whole_weights[index] * (read(index + 1) - read(-index - 1))
    return value


def edged(k, side, center, up, down, above, below, sides, has):
    step = pl.program_id(0)
    last = pl.num_programs(0) - 1
    tile, width = center.shape
    tall = sides.shape[1]
    base = pl.multiple_of(step * tile, 8)
    at = slice(k * HALO, (k + 1) * HALO)
    over = sides[side, pl.ds(pl.multiple_of(jnp.maximum(base - HALO, 0), 8), HALO), :]
    under = sides[side, pl.ds(pl.multiple_of(jnp.minimum(base + tile, tall - HALO), 8), HALO), :]
    over = jnp.concatenate([up, over], axis=1)
    under = jnp.concatenate([down, under], axis=1)
    over = jnp.where(step == 0, above[at, :] * has[2], over)
    under = jnp.where(step == last, below[at, :] * has[3], under)
    inner = jnp.concatenate([center, sides[side, pl.ds(base, tile), :]], axis=1)
    return jnp.concatenate([over, inner, under], axis=0)


def edged_open(k, side, wall, wall_up, wall_down, above, below, sides, has):
    open_cells = [1.0 - ref[0].astype(F32) for ref in (wall, wall_up, wall_down)]
    return edged(k, side, *open_cells, above, below, sides, has)


def quiet_step_kernel(
    has, center, up, down, wall, wall_up, wall_down, above, below, sides, band, out, mark, field, middle
):
    parts, _, tile, width = center.shape
    full = field.shape[2]
    high = tile + 2 * HALO
    guard = HALO
    blank = jnp.zeros((guard, full), F32)
    opened = edged_open(parts, parts, wall, wall_up, wall_down, above, below, sides, has)
    values = []
    for k in range(parts):
        value = edged(
            k,
            k,
            center[k, 0].astype(F32),
            up[k, 0].astype(F32)[up.shape[2] - HALO :],
            down[k, 0].astype(F32)[:HALO],
            above,
            below,
            sides,
            has,
        )
        field[k, 0:guard, :] = blank
        field[k, guard : guard + high, :] = value
        field[k, guard + high :, :] = blank
        values.append(value)

    def drops(ref, at, count, lanes, x):
        along_b = slope_y(lambda d: ref[2, at + d : at + d + count, :lanes])
        along_p = slope_y(lambda d: ref[3, at + d : at + d + count, :lanes])
        diverge = x[1] + along_b
        return (
            diverge + mean_flow * x[0],
            x[3] + mean_flow * x[1],
            along_p + mean_flow * x[2],
            diverge + mean_flow * x[3],
        )

    x = slopes_x((jnp.concatenate([v.astype(BF16) for v in values], axis=0),), band, True)
    x = [x[k * high : (k + 1) * high] for k in range(parts)]
    dropped = drops(field, guard, high, full, x)
    for k in range(parts):
        middle[k, 0:guard, :] = blank
        middle[k, guard + high :, :] = blank
        middle[k, guard : guard + high, :] = opened * (values[k] - (time_step / 60.0) * dropped[k])
    at = guard + HALO
    inner = [middle[k, at : at + tile, :] for k in range(parts)]
    x = slopes_x(split(jnp.concatenate(inner, axis=0)), band, False)
    x = [x[k * tile : (k + 1) * tile] for k in range(parts)]
    dropped = drops(middle, at, tile, width, x)
    shown = opened[HALO : HALO + tile, :width]
    for k in range(parts):
        start = 0.5 * field[k, at : at + tile, :width] - (0.5 * time_step / 60.0) * dropped[k]
        out[k] = shown * start + 0.5 * inner[k][:, :width]
    mark[...] = jnp.zeros(mark.shape, F32)


def source_kernel(
    has, lines, velocity, flow_side, wall, wall_up, wall_down, above, below, sides, rise_x, rise_y, quiet, band, out, raised, forced
):
    step = pl.program_id(0)
    parts, tile, width = quiet.shape
    high = tile + 2 * HALO
    tiles = forced.shape[0]

    @pl.when(step == 0)
    def _():
        at = slice((parts + 1) * HALO, (parts + 2) * HALO)
        flow = jnp.concatenate([velocity[0, 0], flow_side[...]], axis=1)
        size = flow.shape[1]
        flow = jnp.concatenate([above[at, :size], flow, below[at, :size]], axis=0)
        count = lines.shape[0]
        level = jnp.concatenate([lines[k] for k in range(count)], axis=0)
        level = level[MARGIN - HALO : MARGIN - HALO + flow.shape[0]] - flow * flow
        cells = size // LANES
        near = lane_index((flow.shape[0], LANES)) < 64
        for k in range(cells):
            after, before = lane_tile(level, (k + 1) % cells), lane_tile(level, (k - 1) % cells)
            around = jnp.concatenate([lane_tile(level, k), jnp.where(near, after, before)], axis=1)
            out_lanes = 2 * LANES if k < cells - 1 else LANES
            value = exact_dot(split(around), split(rise_x[k][:, :out_lanes]))
            raised[:, 2 * k * LANES : 2 * k * LANES + out_lanes] = value

    half = high // 2
    start = pl.multiple_of(step * (tile // 2), 8)
    window = raised[pl.ds(start, half + HALO), :]
    weights = rise_y[pl.ds(start, half), :]
    taps = [
        pltpu.roll(window, half + HALO - (HALO // 2 - 1 + s), 0)[:half] for s in range(4)
    ]
    opened = time_step * edged_open(parts, 0, wall, wall_up, wall_down, above, below, sides, has)
    for parity in range(2):
        value = sum(weights[:, 4 * parity + s : 4 * parity + s + 1] * taps[s] for s in range(4))
        for t in range(tiles):
            forced[t, pl.ds(parity, half, 2), :] = lane_tile(value, t)
    for t in range(tiles):
        forced[t] = forced[t] * lane_tile(opened, t)
    inner = jnp.concatenate([forced[t, HALO : HALO + tile, :] for t in range(tiles)], axis=1)
    shown = (0.5 / 60.0) * opened[HALO : HALO + tile, :width]
    x = shown * slopes_x(split(inner), band, False)
    y = jnp.concatenate(
        [
            slope_y(lambda d: forced[t, HALO + d : HALO + d + tile, :])
            for t in range(width // LANES)
        ],
        axis=1,
    )
    out[0, 0] = quiet[0].astype(out.dtype)
    out[1, 0] = (quiet[1] - x).astype(out.dtype)
    out[2, 0] = (quiet[2] - shown * y).astype(out.dtype)
    out[3, 0] = (quiet[3] + inner[:, :width] - mean_flow * x).astype(out.dtype)


def call(
    kernel, operands, outs, scratch=(), steps=0, specs=None, out_specs=None, after=(), megabytes=24, flops=0, moved=0, name=None
):
    count = len(operands)

    def body(*refs):
        kernel(*refs[:count], *refs[count + len(after) :])

    def whole(array):
        zeros = (0,) * len(array.shape)
        return pl.BlockSpec(array.shape, lambda *_: zeros)

    arguments = {}
    chosen = specs or {}
    if steps:
        arguments["grid"] = (steps,)
        in_specs = [chosen.get(i, whole(o)) for i, o in enumerate(operands)]
        arguments["out_specs"] = jax.tree.map(whole, outs) if out_specs is None else out_specs
    else:
        local = pl.BlockSpec(memory_space=pltpu.VMEM)
        in_specs = [chosen.get(i, local) for i in range(count)]
    return pl.pallas_call(
        body,
        out_shape=outs,
        in_specs=in_specs + [pl.BlockSpec(memory_space=pl.ANY)] * len(after),
        scratch_shapes=list(scratch),
        compiler_params=pltpu.CompilerParams(vmem_limit_bytes=megabytes << 20),
        cost_estimate=pl.CostEstimate(flops=flops, bytes_accessed=moved, transcendentals=0),
        name=name,
        **arguments,
    )(*operands, *after)


def ring(array, axis, step):
    size = lax.axis_size(axis)
    return lax.ppermute(array, axis, [(i, (i + step) % size) for i in range(size)])


def shaped(*shape, kind=F32):
    return jax.ShapeDtypeStruct(shape, kind)


def pressure_lines(sent, count_y, gathered, spread, stepped):
    count_x, _, rows, local_x = sent.shape
    count = count_x * count_y
    length_x, length_y = local_x * count_x, rows * count
    lines = lax.all_to_all(sent, "gx", 0, 0, tiled=True)
    full, zero, middle, cos_turn, sin_turn = x_tables(length_x)
    turns = np.zeros((8, cos_turn.shape[1]), np.float32)
    turns[0:3], turns[3:6] = cos_turn, sin_turn
    spectra, total = call(
        forward_x_kernel,
        (lines, np.concatenate([beside(full), beside(zero, middle)]), turns),
        (shaped(count, rows, LANES), shaped(8, LANES)),
        after=gathered,
        flops=10**9,
        moved=4 << 20,
        name="forward_x",
    )
    spectra = lax.all_to_all(spectra, ("gy", "gx"), 0, 0, tiled=True)
    place = lax.axis_index("gy") * count_x + lax.axis_index("gx")
    waves = jnp.asarray(wave_table(length_x, count))
    wave = lax.dynamic_slice(waves, (place, 0), (1, LANES))
    both, turns_y = y_tables(length_y)
    kept = rows + 2 * MARGIN // count_x
    half = (kept // 2 + 8) // 8 * 8
    solved = call(
        functools.partial(solve_y_kernel, count_x),
        (spectra, total, wave, beside(both), turns_y),
        shaped(count, half, LANES),
        (pltpu.VMEM((length_y + 2 * MARGIN, LANES), F32),),
        after=spread,
        flops=4 * 10**9,
        moved=6 << 20,
        name="solve_y",
    )
    solved = lax.all_to_all(solved, ("gy", "gx"), 0, 0, tiled=True)
    back = 2.0 * zero.T
    back[LANES // 2] *= 0.5
    tables = np.concatenate(
        [beside(full.T), beside(back, 2.0 * middle.T)]
    )
    pressed = call(
        functools.partial(inverse_x_kernel, kept, 1.0 / (length_x * length_y)),
        (solved, tables, turns),
        shaped(count_x, kept, local_x + LANES),
        (pltpu.VMEM((kept, length_x), F32),),
        after=stepped,
        flops=10**9,
        moved=4 << 20,
        name="inverse_x",
    )
    return lax.all_to_all(pressed, "gx", 0, 0, tiled=True)


def refine_tables(weights_x, weights_y, tall, wide):
    first = lax.axis_index("gx") * wide
    ends = jnp.concatenate([weights_x[:, -LANES:], weights_x, weights_x[:, :LANES]], axis=1)
    own = lax.dynamic_slice(ends, (0, first), (4, wide + 2 * LANES))
    half = LANES // 2
    edge = jnp.concatenate([own[:, wide + LANES : wide + LANES + half], own[:, half:LANES]], axis=1)
    edge = jnp.pad(edge, ((0, 0), (0, LANES)))
    tiles = wide // (2 * LANES)
    weights = jnp.concatenate([own[:, LANES : wide + LANES], edge], axis=1)
    weights = weights.reshape(4, tiles + 1, 1, 2 * LANES)
    fine = np.arange(2 * LANES)
    targets = np.tile(fine // 2 - 1, (tiles + 1, 1))
    targets[tiles] = np.where(fine < half, fine // 2 - 1, half + fine // 2 - 1)
    cells = lax.broadcasted_iota(jnp.int32, (tiles + 1, 2 * LANES, 2 * LANES), 1)
    targets = jnp.asarray(targets[:, None, :].astype(np.int32))
    rise_x = sum(
        jnp.where(cells == (targets + t) % (2 * LANES), weights[t], 0.0) for t in range(4)
    )
    ends = jnp.concatenate([weights_y[:, -HALO:], weights_y, weights_y[:, :HALO]], axis=1)
    own = lax.dynamic_slice(ends, (0, lax.axis_index("gy") * tall), (4, tall + 2 * HALO))
    rise_y = own.reshape(4, tall // 2 + HALO, 2).transpose(1, 2, 0).reshape(tall // 2 + HALO, 8)
    return rise_x, rise_y


def fast_shards(velocity, weights_x, weights_y, acoustic, wall_mask):
    parts, _, tall, wide = acoustic.shape
    _, _, local_y, local_x = velocity.shape
    count_x, count_y = lax.axis_size("gx"), lax.axis_size("gy")
    place_x, place_y = lax.axis_index("gx"), lax.axis_index("gy")
    full, high, steps = wide + LANES, TILE + 2 * HALO, tall // TILE
    strips = (parts + 2) * HALO
    small = 2 * HALO
    ends = ((0, 0, 0, 0), (0, 0, 0, wide // LANES - 1))
    has = jnp.stack([place_x > 0, place_x < count_x - 1, place_y > 0, place_y < count_y - 1])
    has = has.astype(F32)
    scalars = pl.BlockSpec(memory_space=pltpu.SMEM)

    def at(block, *index):
        return pl.BlockSpec(block, lambda i: index)

    sent, to_right, to_left = call(
        edges_kernel,
        (velocity, acoustic, acoustic, wall_mask, wall_mask),
        (
            shaped(count_x, 2, local_y // count_x, local_x),
            shaped(strips, tall),
            shaped(strips, tall),
        ),
        steps=1,
        specs={
            1: at((parts, 1, tall, LANES), 0, 0, 0, 0),
            2: at((parts, 1, tall, LANES), 0, 0, 0, wide // LANES - 1),
            3: at((1, tall, LANES), 0, 0, 0),
            4: at((1, tall, LANES), 0, 0, wide // LANES - 1),
        },
        moved=6 << 20,
        megabytes=56,
        name="edges",
    )
    from_left, from_right = ring(to_right, "gx", 1), ring(to_left, "gx", -1)
    sides, flow_side, first, last, beside_done = call(
        sides_kernel,
        (has, from_left, from_right, acoustic, acoustic, wall_mask, wall_mask, velocity, velocity),
        (
            shaped(parts + 1, tall, LANES),
            shaped(local_y, LANES),
            shaped(strips, full),
            shaped(strips, full),
            shaped(8, LANES),
        ),
        steps=1,
        specs={
            0: scalars,
            3: at((parts, 1, small, wide), 0, 0, 0, 0),
            4: at((parts, 1, small, wide), 0, 0, tall // small - 1, 0),
            5: at((1, HALO, wide), 0, 0, 0),
            6: at((1, HALO, wide), 0, tall // HALO - 1, 0),
            7: at((1, 1, HALO, local_x), 1, 0, 0, 0),
            8: at((1, 1, HALO, local_x), 1, 0, local_y // HALO - 1, 0),
        },
        moved=6 << 20,
        megabytes=56,
        name="sides",
    )
    above, below = ring(last, "gy", 1), ring(first, "gy", -1)
    band = band_table()
    per, rows = TILE // small, TILE // HALO
    walls = (
        pl.BlockSpec((1, TILE, wide), lambda i: (0, i, 0)),
        pl.BlockSpec((1, HALO, wide), lambda i: (0, jnp.maximum(i * rows - 1, 0), 0)),
        pl.BlockSpec((1, HALO, wide), lambda i: (0, jnp.minimum((i + 1) * rows, steps * rows - 1), 0)),
    )
    by_tile = pl.BlockSpec((parts, 1, TILE, wide), lambda i: (0, 0, i, 0))
    over = pl.BlockSpec((parts, 1, small, wide), lambda i: (0, 0, jnp.maximum(i * per - 1, 0), 0))
    under = pl.BlockSpec(
        (parts, 1, small, wide), lambda i: (0, 0, jnp.minimum((i + 1) * per, steps * per - 1), 0)
    )
    flat = pl.BlockSpec((parts, TILE, wide), lambda i: (0, i, 0))
    quiet, quiet_done = call(
        quiet_step_kernel,
        (has, acoustic, acoustic, acoustic, wall_mask, wall_mask, wall_mask, above, below, sides, band),
        (shaped(parts, tall, wide), shaped(8, LANES)),
        (pltpu.VMEM((parts, high + 2 * HALO, full), F32),) * 2,
        steps=steps,
        specs=dict(enumerate((scalars, by_tile, over, under) + walls)),
        out_specs=(flat, pl.BlockSpec((8, LANES), lambda i: (0, 0))),
        megabytes=56,
        flops=9 * 10**9,
        moved=50 << 20,
        name="quiet_step",
    )
    rows_done = above[:8, :LANES] + below[:8, :LANES]
    lines = pressure_lines(sent, count_y, (beside_done,), (rows_done,), (quiet_done,))
    rise_x, rise_y = refine_tables(weights_x, weights_y, tall, wide)
    operands = (has, lines, velocity, flow_side, wall_mask, wall_mask, wall_mask, above, below, sides, rise_x, rise_y, quiet, band)
    specs = {
        0: scalars,
        2: at((1, 1, local_y, local_x), 1, 0, 0, 0),
        9: at((1, tall, LANES), parts, 0, 0),
        12: flat,
    }
    specs.update({4 + i: spec for i, spec in enumerate(walls)})
    return call(
        source_kernel,
        operands,
        shaped(*acoustic.shape, kind=BF16),
        (pltpu.VMEM((local_y + 2 * HALO, full), F32), pltpu.VMEM((full // LANES, high, LANES), F32)),
        steps=steps,
        specs=specs,
        out_specs=by_tile,
        flops=4 * 10**9,
        moved=16 << 20,
        megabytes=56,
        name="source_step",
    )


def fits(count_x, count_y, velocity, acoustic):
    _, planes, local_y, local_x = velocity
    _, _, tall, wide = acoustic
    length_x, length_y = local_x * count_x, local_y * count_y
    rows = local_y // count_x
    base_x, base_y = length_x // RADIX, length_y // RADIX
    return (
        planes == 1
        and length_x * 2 == count_x * count_y * LANES
        and base_x % (2 * LANES) == 0
        and local_x % base_x == 0
        and rows % 8 == 0
        and base_y % rows == 0
        and base_y % 8 == 0
        and MARGIN * 2 % (8 * count_x) == 0
        and tall == 2 * local_y
        and wide == 2 * local_x
        and tall % TILE == 0
        and wide % (2 * LANES) == 0
    )


def extended(array, sides, width):
    for axis, dim in sides:
        size, length = (lax.axis_size(axis), array.shape[dim])
        up = [(i, (i + 1) % size) for i in range(size - 1)]
        down = [(j, i) for i, j in up]
        last = lax.slice_in_dim(array, length - width, length, axis=dim)
        leading = lax.slice_in_dim(array, 0, width, axis=dim)
        before = lax.ppermute(last, axis, up)
        after = lax.ppermute(leading, axis, down)
        array = jnp.concatenate([before, array, after], axis=dim)
    return array


def gradients(padded):
    height = padded.shape[-2] - 6
    breadth = padded.shape[-1] - 6
    rows_mid = padded[..., 3 : 3 + height, :]
    cols_mid = padded[..., :, 3 : 3 + breadth]
    along_x = jnp.zeros_like(padded[..., 3 : 3 + height, 3 : 3 + breadth])
    along_y = jnp.zeros_like(along_x)
    for index, weight in enumerate(stencil_weights):
        distance = index + 1
        along_x = along_x + weight * (
            rows_mid[..., 3 + distance : 3 + distance + breadth]
            - rows_mid[..., 3 - distance : 3 - distance + breadth]
        )
        along_y = along_y + weight * (
            cols_mid[..., 3 + distance : 3 + distance + height, :]
            - cols_mid[..., 3 - distance : 3 - distance + height, :]
        )
    return (along_x, along_y)


def tendency(padded, source):
    along_x, along_y = gradients(padded)
    diverge = along_x[1] + along_y[2]
    forcing = jnp.stack([-diverge, -along_x[3], -along_y[3], source - diverge])
    return forcing - mean_flow * along_x


def spectral_index(flat, length):
    second = length // 16
    wave = flat // second + 16 * (flat % second)
    return jnp.where(wave < length // 2, wave, wave - length).astype(jnp.float32)


def twiddles(rows_count, cols_count, modulus, sign):
    products = jnp.arange(rows_count)[:, None] * jnp.arange(cols_count)[None, :] % modulus
    angles = 2.0 * math.pi / modulus * products.astype(jnp.float32)
    return (jnp.cos(angles), sign * jnp.sin(angles))


def mix_rows(real_part, imag_part, cosine, sine):
    exact = lax.Precision.HIGHEST
    cos_real = jnp.einsum("ka,...ab->...kb", cosine, real_part, precision=exact)
    cos_imag = jnp.einsum("ka,...ab->...kb", cosine, imag_part, precision=exact)
    sin_real = jnp.einsum("ka,...ab->...kb", sine, real_part, precision=exact)
    sin_imag = jnp.einsum("ka,...ab->...kb", sine, imag_part, precision=exact)
    return (cos_real - sin_imag, cos_imag + sin_real)


def mix_cols(real_part, imag_part, cosine, sine):
    exact = lax.Precision.HIGHEST
    cos_real = jnp.einsum("...kb,bc->...kc", real_part, cosine, precision=exact)
    cos_imag = jnp.einsum("...kb,bc->...kc", imag_part, cosine, precision=exact)
    sin_real = jnp.einsum("...kb,bc->...kc", real_part, sine, precision=exact)
    sin_imag = jnp.einsum("...kb,bc->...kc", imag_part, sine, precision=exact)
    return (cos_real - sin_imag, cos_imag + sin_real)


def rotate(real_part, imag_part, cosine, sine):
    return (real_part * cosine - imag_part * sine, real_part * sine + imag_part * cosine)


def discrete(real_part, imag_part, sign):
    length = real_part.shape[-1]
    second = length // 16
    initial = real_part.shape
    folded = initial[:-1] + (16, second)
    real_part = real_part.reshape(folded)
    imag_part = imag_part.reshape(folded)
    small_cos, small_sin = twiddles(16, 16, 16, sign)
    large_cos, large_sin = twiddles(second, second, second, sign)
    turn_cos, turn_sin = twiddles(16, second, length, sign)
    if sign < 0:
        real_part, imag_part = mix_rows(real_part, imag_part, small_cos, small_sin)
        real_part, imag_part = rotate(real_part, imag_part, turn_cos, turn_sin)
        real_part, imag_part = mix_cols(real_part, imag_part, large_cos, large_sin)
    else:
        real_part, imag_part = mix_cols(real_part, imag_part, large_cos, large_sin)
        real_part, imag_part = rotate(real_part, imag_part, turn_cos, turn_sin)
        real_part, imag_part = mix_rows(real_part, imag_part, small_cos, small_sin)
        real_part = real_part / length
        imag_part = imag_part / length
    return (real_part.reshape(initial), imag_part.reshape(initial))


def transform(stacked, sign, kind):
    if kind == "real_in":
        real_part = stacked
        imag_part = jnp.zeros_like(stacked)
    else:
        half = stacked.shape[0] // 2
        real_part = stacked[:half]
        imag_part = stacked[half:]
    real_out, imag_out = discrete(real_part, imag_part, sign)
    if kind == "real_out":
        return real_out
    return jnp.concatenate([real_out, imag_out], axis=0)


def project(stacked, wave_x, wave_y):
    coef_xx = wave_x * wave_x
    coef_xy = 2.0 * wave_x * wave_y
    coef_yy = wave_y * wave_y
    denominator = wave_x * wave_x + wave_y * wave_y
    positive = denominator > 0
    safe = jnp.where(positive, denominator, 1.0)

    def combine(parts):
        numerator = -(coef_xx * parts[0] + coef_xy * parts[1] + coef_yy * parts[2])
        return jnp.where(positive, numerator / safe, 0.0)

    return jnp.stack([combine(stacked[:3]), combine(stacked[3:])])


def refine(stacked, weights):
    result = jnp.zeros(stacked.shape[:-1] + (2 * stacked.shape[-1],), jnp.float32)
    for offset in range(4):
        result = (
            result
            + jnp.repeat(jnp.roll(stacked, 1 - offset, axis=-1), 2, axis=-1) * weights[offset]
        )
    return result


def lines_x(stacked, action):
    gathered = action(lax.all_to_all(stacked, "gx", split_axis=2, concat_axis=3, tiled=True))
    return lax.all_to_all(gathered, "gx", split_axis=3, concat_axis=2, tiled=True)


def lines_y(stacked, action):
    turned = jnp.swapaxes(stacked, 2, 3)
    gathered = action(lax.all_to_all(turned, "gy", split_axis=2, concat_axis=3, tiled=True))
    returned = lax.all_to_all(gathered, "gy", split_axis=3, concat_axis=2, tiled=True)
    return jnp.swapaxes(returned, 2, 3)


def expand(fields):
    return extended(fields, (("gx", 3), ("gy", 2)), 3)


def shards(velocity, weights_x, weights_y, acoustic, wall_mask):
    acoustic = acoustic.astype(jnp.float32)
    flow_x = velocity[0]
    flow_y = velocity[1]
    tensor = jnp.stack([flow_x * flow_x, flow_x * flow_y, flow_y * flow_y])
    count_gx = lax.axis_size("gx")
    count_gy = lax.axis_size("gy")
    place_x = lax.axis_index("gx")
    place_y = lax.axis_index("gy")
    local_y = tensor.shape[2]
    local_x = tensor.shape[3]
    length_x = local_x * count_gx
    length_y = local_y * count_gy

    def forward_real(portion):
        return transform(portion, -1, "real_in")

    def finish_x(portion):
        return refine(transform(portion, 1, "real_out"), weights_x)

    spectra = lines_x(tensor, forward_real)
    share_x = local_x // count_gy
    line_x = spectral_index(place_x * local_x + place_y * share_x + jnp.arange(share_x), length_x)[
        :, None
    ]
    line_y = spectral_index(jnp.arange(length_y), length_y)[None, :]

    def solve_y(portion):
        solved = project(transform(portion, -1, "complex"), line_x, line_y)
        return refine(transform(solved, 1, "complex"), weights_y)

    pressure = lines_y(spectra, solve_y)
    source = lines_x(pressure, finish_x)[0]
    open_cells = (1 - wall_mask).astype(jnp.float32)
    first_rate = tendency(expand(acoustic), source)
    middle = open_cells * (acoustic + time_step * first_rate)
    second_rate = tendency(expand(middle), source)
    return (open_cells * (acoustic + 0.5 * time_step * (first_rate + second_rate))).astype(
        jnp.bfloat16
    )


def solution(mesh):
    in_specs = (P(None, None, "gy", "gx"), P(), P(), P(None, None, "gy", "gx"), P(None, "gy", "gx"))
    out_specs = P(None, None, "gy", "gx")

    def chosen(velocity, weights_x, weights_y, acoustic, wall_mask):
        sizes = (mesh.shape["gx"], mesh.shape["gy"], velocity.shape, acoustic.shape)
        plan = fast_shards if fits(*sizes) else shards
        return plan(velocity, weights_x, weights_y, acoustic, wall_mask)

    return jax.shard_map(
        chosen, mesh=mesh, in_specs=in_specs, out_specs=out_specs, check_vma=False
    )
```

```python
import functools
import math

import jax
import jax.numpy as jnp
import ml_dtypes
import numpy as np
from jax import lax
from jax.experimental import pallas as pl
from jax.experimental.pallas import tpu as pltpu
from jax.sharding import PartitionSpec as P

stencil_weights = (0.75, -0.15, 1.0 / 60.0)
mean_flow = 0.3
time_step = 0.5
whole_weights = (45.0, -9.0, 1.0)

LANES = 128
RADIX = 8
HALO = 8
MARGIN = 16
TILE = 128
ROOT = math.sqrt(0.5)
BF16 = jnp.bfloat16
F32 = jnp.float32


def halves(table):
    high = table.astype(np.float32).astype(ml_dtypes.bfloat16)
    low = (table - high.astype(np.float64)).astype(np.float32).astype(ml_dtypes.bfloat16)
    return high, low


def packed_columns(cosine, sine):
    half = LANES // 2
    parts = []
    for first in range(0, cosine.shape[1], half):
        parts += [cosine[:, first : first + half], sine[:, first : first + half]]
    return np.concatenate(parts, axis=1)


@functools.lru_cache(maxsize=None)
def x_tables(length):
    base = length // RADIX
    m = np.arange(base)[:, None]
    q = np.arange(base)[None, :]
    angle = 2.0 * np.pi * ((m * q) % base) / base
    cosine, sine = np.cos(angle), np.sin(angle)
    full = np.concatenate([packed_columns(cosine, -sine), packed_columns(sine, cosine)], axis=0)
    half = base // 2
    zero_cos, zero_sin = cosine[:, :half].copy(), -sine[:, :half]
    zero_cos[:, 0] = 0.0
    zero_sin = zero_sin.copy()
    zero_sin[:, 0] = (-1.0) ** np.arange(base)
    zero = packed_columns(zero_cos, zero_sin)
    shifted = 2.0 * np.pi * ((m * (RADIX * q[:, :half] + RADIX // 2)) % length) / length
    middle = packed_columns(np.cos(shifted), -np.sin(shifted))
    turns = 2.0 * np.pi * np.arange(1, RADIX // 2)[:, None] * np.arange(base)[None, :] / length
    return full, zero, middle, np.cos(turns), np.sin(turns)


@functools.lru_cache(maxsize=None)
def y_tables(length):
    base = length // RADIX
    index = np.arange(base)
    angle = 2.0 * np.pi * ((index[:, None] * index[None, :]) % base) / base
    both = np.concatenate([np.cos(angle), np.sin(angle)], axis=0)
    turns = 2.0 * np.pi * np.arange(RADIX)[:, None] * index[None, :] / length
    return both, np.concatenate([np.cos(turns), np.sin(turns)], axis=0).T.astype(np.float32)


@functools.lru_cache(maxsize=None)
def wave_table(length, count):
    slots = LANES // 4
    base = length // RADIX
    waves = []
    for residue in (1, 2, 3):
        waves.append(RADIX * np.arange(base) + residue)
    waves.append(RADIX * np.arange(base // 2))
    waves.append(RADIX * np.arange(base // 2) + RADIX // 2)
    waves = np.concatenate(waves)
    waves = np.where(waves == 0, length // 2, waves)
    waves = np.where(waves < length // 2, waves, waves - length).reshape(count, slots)
    return np.tile(waves, (1, 4)).astype(np.float32)


@functools.lru_cache(maxsize=None)
def band_tables(rows):
    across = np.zeros((4 * LANES, 2 * LANES))
    column = np.arange(2 * LANES)
    down = np.zeros((rows, rows))
    for index, weight in enumerate(whole_weights):
        distance = index + 1
        across[column + LANES + distance, column] = weight
        across[column + LANES - distance, column] = -weight
        down += weight * (np.eye(rows, k=distance) - np.eye(rows, k=-distance))
    return across.astype(ml_dtypes.bfloat16), down.astype(ml_dtypes.bfloat16)


def beside(*tables):
    high, low = halves(np.concatenate(tables, axis=1))
    return np.concatenate([high, low], axis=0)


def split(values):
    high = values.astype(BF16)
    return high, (values - high.astype(F32)).astype(BF16)


def dot(left, right):
    return jnp.dot(left, right, preferred_element_type=F32)


def exact_dot(left, right):
    left_high, left_low = left
    right_high, right_low = right
    return dot(left_high, right_high) + (dot(left_low, right_high) + dot(left_high, right_low))


def lane_index(shape):
    return lax.broadcasted_iota(jnp.int32, shape, len(shape) - 1)


def spin(values, shift):
    return pltpu.roll(values, shift % values.shape[-1], values.ndim - 1)


def lane_tile(values, index):
    return values[:, index * LANES : (index + 1) * LANES]


def x_parts(tables, base):
    wide = 2 * base
    full = (tables[:wide], tables[wide : 2 * wide])
    at = 2 * wide
    high, low = tables[at : at + base], tables[at + base : at + 2 * base]
    return full, (high[:, :base], low[:, :base]), (high[:, base:], low[:, base:])


def edges_kernel(velocity, top, low, top_wall, low_wall, sent, first, last):
    count, _, rows, width = sent.shape
    for e in range(count):
        for c in range(2):
            sent[e, c] = velocity[c, 0, e * rows : (e + 1) * rows, :]
    parts, _, small, _ = top.shape
    blank = jnp.zeros((HALO, first.shape[1] - width), F32)
    for k in range(parts):
        at = slice(k * HALO, (k + 1) * HALO)
        first[at, :] = top[k, 0].astype(F32)[:HALO]
        last[at, :] = low[k, 0].astype(F32)[small - HALO :]
    at = slice(parts * HALO, (parts + 1) * HALO)
    first[at, :] = 1.0 - top_wall[0].astype(F32)
    last[at, :] = 1.0 - low_wall[0].astype(F32)
    at = slice((parts + 1) * HALO, (parts + 2) * HALO)
    first[at, :width] = velocity[1, 0, :HALO, :]
    last[at, :width] = velocity[1, 0, count * rows - HALO :, :]
    first[at, width:] = blank
    last[at, width:] = blank


def columns_kernel(
    has, left, right, left_wall, right_wall, left_flow, right_flow, above, below, to_right, to_left
):
    parts = left.shape[0]
    wide, flow_wide = above.shape[1], above.shape[1] // 2
    gap = jnp.zeros((LANES - 2 * HALO, LANES), F32)

    def tall(k, inner, first, sides):
        at = slice(k * HALO, (k + 1) * HALO)
        over, under = above[at, first : first + LANES], below[at, first : first + LANES]
        return jnp.concatenate([inner, under * sides[1], gap, over * sides[0]], axis=0).T

    for k in range(parts + 1):
        at = slice(k * HALO, (k + 1) * HALO)
        if k < parts:
            near, far = left[k, 0].astype(F32), right[k, 0].astype(F32)
        else:
            near, far = 1.0 - left_wall[0].astype(F32), 1.0 - right_wall[0].astype(F32)
        sides = (has[2], has[3])
        to_left[at, :] = tall(k, near, 0, sides)[:HALO]
        to_right[at, :] = tall(k, far, wide - LANES, sides)[LANES - HALO :]
    k = parts + 1
    at = slice(k * HALO, (k + 1) * HALO)
    size = left_flow.shape[2] + LANES
    blank = jnp.zeros((HALO, to_left.shape[1] - size), F32)
    to_left[at, :size] = tall(k, left_flow[0, 0], 0, (1.0, 1.0))[:HALO]
    to_right[at, :size] = tall(k, right_flow[0, 0], flow_wide - LANES, (1.0, 1.0))[LANES - HALO :]
    to_left[at, size:] = blank
    to_right[at, size:] = blank


def sides_kernel(has, from_left, from_right, sides, flow_side):
    parts, tall, _ = sides.shape
    gap = jnp.zeros((LANES - 2 * HALO, tall), F32)
    for k in range(parts):
        at = slice(k * HALO, (k + 1) * HALO)
        tile = [from_right[at, :] * has[1], gap, from_left[at, :] * has[0]]
        sides[k] = jnp.concatenate(tile, axis=0).T
    at = slice(parts * HALO, (parts + 1) * HALO)
    size = flow_side.shape[0]
    tile = [from_right[at, :size], gap[:, :size], from_left[at, :size]]
    flow_side[...] = jnp.concatenate(tile, axis=0).T


def forward_x_kernel(lines, tables, turns, out, total):
    count, _, rows, local = lines.shape
    base = turns.shape[1]
    per = local // base
    u = [lines[t // per, 0, :, (t % per) * base : (t % per + 1) * base] for t in range(RADIX)]
    v = [lines[t // per, 1, :, (t % per) * base : (t % per + 1) * base] for t in range(RADIX)]
    energy = sum(b * b for b in v)
    energy = jnp.sum(energy.reshape(rows // 8, 8, base), axis=0)
    total[...] = sum(energy[:, k : k + LANES] for k in range(0, base, LANES))
    fields = ([a * a - b * b for a, b in zip(u, v)], [2.0 * a * b for a, b in zip(u, v)])
    zeros, mids, reals, imags = [], [], [[], [], []], [[], [], []]
    for a in fields:
        s04, s26, s15, s37 = a[0] + a[4], a[2] + a[6], a[1] + a[5], a[3] + a[7]
        d04, d26, d15, d37 = a[0] - a[4], a[2] - a[6], a[1] - a[5], a[3] - a[7]
        zeros.append((s04 + s26) + (s15 + s37))
        mids.append((s04 + s26) - (s15 + s37))
        minus, plus = ROOT * (d15 - d37), ROOT * (d15 + d37)
        turned = (
            (d04 + minus, -d26 - plus),
            (s04 - s26, s37 - s15),
            (d04 - minus, d26 - plus),
        )
        for index, (real, imag) in enumerate(turned):
            c, s = turns[index : index + 1, :], turns[index + 3 : index + 4, :]
            reals[index].append(real * c + imag * s)
            imags[index].append(imag * c - real * s)
    stacked = jnp.concatenate(
        [
            jnp.concatenate([jnp.concatenate(reals[i], axis=0) for i in range(3)], axis=0),
            jnp.concatenate([jnp.concatenate(imags[i], axis=0) for i in range(3)], axis=0),
        ],
        axis=1,
    )
    full, zero, middle = x_parts(tables, base)
    full = exact_dot(split(stacked), full)
    zero = exact_dot(split(jnp.concatenate(zeros, axis=0)), zero)
    middle = exact_dot(split(jnp.concatenate(mids, axis=0)), middle)
    low = lane_index((rows, LANES)) % 64 < 32
    place = 0
    blocks = [full[2 * rows * i : 2 * rows * (i + 1)] for i in range(3)] + [zero, middle]
    for block in blocks:
        for first in range(0, block.shape[1], LANES):
            a = block[:rows, first : first + LANES]
            c = block[rows:, first : first + LANES]
            out[place] = jnp.where(low, a, spin(c, 32))
            out[place + 1] = jnp.where(low, spin(a, -32), c)
            place += 2


def eighths(x, turn):
    s04, s26, s15, s37 = x[0] + x[4], x[2] + x[6], x[1] + x[5], x[3] + x[7]
    d04, d26, d15, d37 = x[0] - x[4], x[2] - x[6], x[1] - x[5], x[3] - x[7]
    quarter = turn(s15 - s37)
    spun_26, spun_37 = turn(d26), turn(d37)
    one, three = d15 + spun_37, d15 - spun_37
    spun_one, spun_three = turn(one), turn(three)
    one = ROOT * (one + spun_one)
    three = ROOT * (spun_three - three)
    return [
        (s04 + s26) + (s15 + s37),
        (d04 + spun_26) + one,
        (s04 - s26) + quarter,
        (d04 - spun_26) + three,
        (s04 + s26) - (s15 + s37),
        (d04 + spun_26) - one,
        (s04 - s26) - quarter,
        (d04 - spun_26) - three,
    ]


def solve_y_kernel(count_x, lines, total, wave, both, turns, out, held):
    count, rows, _ = lines.shape
    base = turns.shape[0]
    length = count * rows
    block = count_x * rows
    per = base // rows
    lanes = lane_index((base, LANES))
    sign = jnp.where(lanes < 64, 1.0, -1.0).astype(F32)

    def minus_i(z):
        return spin(z, 64) * sign

    def plus_i(z):
        return spin(z, 64) * -sign

    fields = [
        jnp.concatenate([lines[t * per + k] for k in range(per)], axis=0) for t in range(RADIX)
    ]
    mixed = eighths(fields, minus_i)
    table = turns[...]
    cosines = [table[:, r : r + 1] for r in range(RADIX)]
    sines = [table[:, RADIX + r : RADIX + r + 1] * sign for r in range(RADIX)]
    mixed = [mixed[0]] + [
        mixed[r] * cosines[r] + spin(mixed[r], 64) * sines[r] for r in range(1, RADIX)
    ]
    tables = (both[: 2 * base], both[2 * base :])
    product = exact_dot(tables, split(jnp.concatenate(mixed, axis=1)))
    kx = wave[0:1, :]
    is_first = lanes % 64 < 32
    q = lax.broadcasted_iota(jnp.int32, (base, LANES), 0)
    edge = jnp.float32(-(length // 2))
    solved = []
    for r in range(RADIX):
        at = slice(r * LANES, (r + 1) * LANES)
        spectrum = product[:base, at] + minus_i(product[base:, at])
        k = RADIX * q + r
        ky = jnp.where(k < length // 2, k, k - length).astype(F32)
        cross = jnp.where((kx == edge) == (ky == edge), kx * ky, 0.0)
        symbol = jnp.where(is_first, kx * kx, cross) / (kx * kx + ky * ky)
        terms = symbol * spectrum
        solved.append(terms + spin(terms, -32))
    product = exact_dot(tables, split(jnp.concatenate(solved, axis=1)))
    mixed = []
    for r in range(RADIX):
        at = slice(r * LANES, (r + 1) * LANES)
        value = product[:base, at] + plus_i(product[base:, at])
        if r:
            value = value * cosines[r] - spin(value, 64) * sines[r]
        mixed.append(value)
    for t, values in enumerate(eighths(mixed, plus_i)):
        held[MARGIN + t * base : MARGIN + (t + 1) * base, :] = values
    held[0:MARGIN, :] = held[length : length + MARGIN, :]
    held[length + MARGIN : length + 2 * MARGIN, :] = held[MARGIN : 2 * MARGIN, :]
    spare = total[...] + spin(total[...], 32)
    kept = rows + 2 * MARGIN // count_x
    half = out.shape[1]
    rest = kept - half
    low = lane_index((8, LANES)) % 64 < 32
    for target in range(count):
        start = (target // count_x) * block + (target % count_x) * kept
        for row in range(0, half, 8):
            a = held[start + row : start + row + 8, :]
            if row < rest:
                b = spin(held[start + half + row : start + half + row + 8, :], 32)
            else:
                b = spare
            out[target, row : row + 8, :] = jnp.where(low, a, b)


def inverse_x_kernel(
    kept, scale, lines, tables, turns, out, held
):
    count, half, _ = lines.shape
    base = turns.shape[1]
    length = RADIX * base
    rest = kept - half
    low = lane_index((half, LANES)) % 64 < 32
    groups, spare = [], None
    for first in range(0, count, 2):
        even, odd = lines[first], lines[first + 1]
        a = jnp.where(low, even, spin(odd, 32))
        b = jnp.where(low, spin(even, -32), odd)
        groups.append(jnp.concatenate([a, b[:rest]], axis=0))
        extra = b[rest : rest + 8]
        spare = extra if spare is None else spare + extra
    mean = jnp.sum(spare) * scale
    wide = 2 * base // LANES
    narrow = base // LANES
    stacked = jnp.concatenate(
        [jnp.concatenate(groups[i * wide : (i + 1) * wide], axis=1) for i in range(3)], axis=0
    )
    place = 3 * wide
    zeros = jnp.concatenate(groups[place : place + narrow], axis=1)
    mids = jnp.concatenate(groups[place + narrow : place + 2 * narrow], axis=1)
    full, zero, middle = x_parts(tables, base)
    full = exact_dot(split(stacked), full)
    zero = exact_dot(split(zeros), zero) * scale
    mid = exact_dot(split(mids), middle) * scale
    turned = []
    for i in range(3):
        real = full[i * kept : (i + 1) * kept, :base]
        imag = full[i * kept : (i + 1) * kept, base:]
        c = turns[i : i + 1, :] * (2.0 * scale)
        s = turns[i + 3 : i + 4, :] * (2.0 * scale)
        turned.append((real * c - imag * s, real * s + imag * c))
    for t in range(RADIX):
        value = zero + mid if t % 2 == 0 else zero - mid
        for i, (real, imag) in enumerate(turned):
            eighth = t * (i + 1) % RADIX
            c = (1.0, ROOT, 0.0, -ROOT, -1.0, -ROOT, 0.0, ROOT)[eighth]
            s = (0.0, ROOT, 1.0, ROOT, 0.0, -ROOT, -1.0, -ROOT)[eighth]
            if c:
                value = value + c * real
            if s:
                value = value - s * imag
        held[:, t * base : (t + 1) * base] = mean - value
    targets, _, width = out.shape
    local = width - LANES
    right = lane_index((kept, LANES)) < 64
    for target in range(targets):
        out[target, :, :local] = held[:, target * local : (target + 1) * local]
        after = (target + 1) * local % length
        before = (target * local - LANES) % length
        out[target, :, local:] = jnp.where(
            right, held[:, after : after + LANES], held[:, before : before + LANES]
        )


def slopes_x(parts, band, with_edge):
    tiles = parts[0].shape[-1] // LANES
    pieces = []
    for first in list(range(0, tiles - 1, 2)) + ([tiles - 1] if with_edge else []):
        steps = (-1, 0, 1, 2) if first < tiles - 1 else (-1, 0, 1)
        table = band[...] if first < tiles - 1 else band[: 3 * LANES, :LANES]
        order = [(first + step) % tiles for step in steps]
        piece = None
        for part in parts:
            term = dot(jnp.concatenate([lane_tile(part, t) for t in order], axis=1), table)
            piece = term if piece is None else piece + term
        pieces.append(piece)
    return jnp.concatenate(pieces, axis=1)


def edged(k, side, center, up, down, above, below, sides, has):
    step = pl.program_id(0)
    last = pl.num_programs(0) - 1
    tile, width = center.shape
    tall = sides.shape[1]
    base = pl.multiple_of(step * tile, 8)
    at = slice(k * HALO, (k + 1) * HALO)
    before = pl.multiple_of(jnp.where(step == 0, tall, base) - HALO, 8)
    over = jnp.where(step == 0, above[at, :] * has[2], up)
    under = jnp.where(step == last, below[at, :] * has[3], down)
    rows = (
        (over, sides[side, pl.ds(before, HALO), :]),
        (center, sides[side, pl.ds(base, tile), :]),
        (under, sides[side, pl.ds(pl.multiple_of(base + tile, 8), HALO), :]),
    )
    return jnp.concatenate([jnp.concatenate(pair, axis=1) for pair in rows], axis=0)


def edged_open(k, side, wall, wall_up, wall_down, above, below, sides, has):
    open_cells = [1.0 - ref[0].astype(F32) for ref in (wall, wall_up, wall_down)]
    return edged(k, side, *open_cells, above, below, sides, has)


def quiet_step_kernel(
    has, center, up, down, wall, wall_up, wall_down, above, below, sides, across, along, along_inner, out, mark
):
    parts, _, tile, width = center.shape
    high = tile + 2 * HALO
    opened = edged_open(parts, parts, wall, wall_up, wall_down, above, below, sides, has)
    values = []
    for k in range(parts):
        value = edged(
            k,
            k,
            center[k, 0].astype(F32),
            up[k, 0].astype(F32)[up.shape[2] - HALO :],
            down[k, 0].astype(F32)[:HALO],
            above,
            below,
            sides,
            has,
        )
        values.append(value)

    def drops(x, along_b, along_p):
        diverge = x[1] + along_b
        return (
            diverge + mean_flow * x[0],
            x[3] + mean_flow * x[1],
            along_p + mean_flow * x[2],
            diverge + mean_flow * x[3],
        )

    short = [value.astype(BF16) for value in values]
    x = slopes_x((jnp.concatenate(short, axis=0),), across, True)
    x = [x[k * high : (k + 1) * high] for k in range(parts)]
    table = along[...]
    dropped = drops(x, dot(table, short[2]), dot(table, short[3]))
    middle = [opened * (v - (time_step / 60.0) * d) for v, d in zip(values, dropped)]
    inner = slice(HALO, HALO + tile)
    short = [value[inner].astype(BF16) for value in middle]
    x = slopes_x((jnp.concatenate(short, axis=0),), across, False)
    x = [x[k * tile : (k + 1) * tile] for k in range(parts)]
    table = along_inner[...]
    dropped = drops(x, *(dot(table, middle[k][:, :width].astype(BF16)) for k in (2, 3)))
    shown = opened[inner, :width]
    for k in range(parts):
        start = 0.5 * values[k][inner, :width] - (0.5 * time_step / 60.0) * dropped[k]
        out[k] = shown * start + 0.5 * middle[k][inner, :width]
    mark[...] = jnp.zeros(mark.shape, F32)


def source_kernel(
    has, lines, velocity, flow_side, wall, wall_up, wall_down, above, below, sides, rise_x, rise_y, quiet, across, along_inner, out, raised
):
    step = pl.program_id(0)
    parts, tile, width = quiet.shape

    @pl.when(step == 0)
    def _():
        at = slice((parts + 1) * HALO, (parts + 2) * HALO)
        rows, local = velocity.shape[2:]
        beyond = flow_side.shape[0]
        flow = jnp.concatenate(
            [
                jnp.concatenate([above[at, :local], flow_side[beyond - HALO :, :]], axis=1),
                jnp.concatenate([velocity[0, 0], flow_side[:rows, :]], axis=1),
                jnp.concatenate([below[at, :local], flow_side[rows : rows + HALO, :]], axis=1),
            ],
            axis=0,
        )
        count = lines.shape[0]
        level = jnp.concatenate([lines[k] for k in range(count)], axis=0)
        level = level[MARGIN - HALO : MARGIN - HALO + flow.shape[0]] - flow * flow
        cells = level.shape[1] // LANES
        near = lane_index((level.shape[0], LANES)) < 64
        for k in range(cells):
            after, before = lane_tile(level, (k + 1) % cells), lane_tile(level, (k - 1) % cells)
            around = jnp.concatenate([lane_tile(level, k), jnp.where(near, after, before)], axis=1)
            lanes = 2 * LANES if k < cells - 1 else LANES
            value = split(exact_dot(split(around), split(rise_x[k][:, :lanes])))
            for part in range(2):
                raised[part, :, 2 * k * LANES : 2 * k * LANES + lanes] = value[part]

    start = pl.multiple_of(step * (tile // 2), 16)
    window = [raised[part, pl.ds(start, rise_y.shape[2]), :] for part in range(2)]
    opened = time_step * edged_open(parts, 0, wall, wall_up, wall_down, above, below, sides, has)
    forced = opened * exact_dot(split(rise_y[0]), window)
    inner = slice(HALO, HALO + tile)
    shown = (0.5 / 60.0) * opened[inner, :width]
    x = shown * slopes_x(split(forced[inner]), across, False)
    table = along_inner[...]
    y = sum(dot(table, part) for part in split(forced[:, :width]))
    out[0, 0] = quiet[0].astype(out.dtype)
    out[1, 0] = (quiet[1] - x).astype(out.dtype)
    out[2, 0] = (quiet[2] - shown * y).astype(out.dtype)
    out[3, 0] = (quiet[3] + forced[inner, :width] - mean_flow * x).astype(out.dtype)


def call(
    kernel, operands, outs, scratch=(), steps=0, specs=None, out_specs=None, after=(), megabytes=24, flops=0, moved=0, name=None
):
    count = len(operands)

    def body(*refs):
        kernel(*refs[:count], *refs[count + len(after) :])

    def whole(array):
        zeros = (0,) * len(array.shape)
        return pl.BlockSpec(array.shape, lambda *_: zeros)

    arguments = {}
    chosen = specs or {}
    if steps:
        arguments["grid"] = (steps,)
        in_specs = [chosen.get(i, whole(o)) for i, o in enumerate(operands)]
        arguments["out_specs"] = jax.tree.map(whole, outs) if out_specs is None else out_specs
    else:
        local = pl.BlockSpec(memory_space=pltpu.VMEM)
        in_specs = [chosen.get(i, local) for i in range(count)]
    return pl.pallas_call(
        body,
        out_shape=outs,
        in_specs=in_specs + [pl.BlockSpec(memory_space=pl.ANY)] * len(after),
        scratch_shapes=list(scratch),
        compiler_params=pltpu.CompilerParams(vmem_limit_bytes=megabytes << 20),
        cost_estimate=pl.CostEstimate(flops=flops, bytes_accessed=moved, transcendentals=0),
        name=name,
        **arguments,
    )(*operands, *after)


def ring(array, axis, step):
    size = lax.axis_size(axis)
    return lax.ppermute(array, axis, [(i, (i + step) % size) for i in range(size)])


def shaped(*shape, kind=F32):
    return jax.ShapeDtypeStruct(shape, kind)


def pressure_lines(sent, count_y, spread, stepped):
    count_x, _, rows, local_x = sent.shape
    count = count_x * count_y
    length_x, length_y = local_x * count_x, rows * count
    lines = lax.all_to_all(sent, "gx", 0, 0, tiled=True)
    full, zero, middle, cos_turn, sin_turn = x_tables(length_x)
    turns = np.zeros((8, cos_turn.shape[1]), np.float32)
    turns[0:3], turns[3:6] = cos_turn, sin_turn
    spectra, total = call(
        forward_x_kernel,
        (lines, np.concatenate([beside(full), beside(zero, middle)]), turns),
        (shaped(count, rows, LANES), shaped(8, LANES)),
        flops=10**9,
        moved=4 << 20,
        name="forward_x",
    )
    spectra = lax.all_to_all(spectra, ("gy", "gx"), 0, 0, tiled=True)
    place = lax.axis_index("gy") * count_x + lax.axis_index("gx")
    waves = jnp.asarray(wave_table(length_x, count))
    wave = lax.dynamic_slice(waves, (place, 0), (1, LANES))
    both, turns_y = y_tables(length_y)
    kept = rows + 2 * MARGIN // count_x
    half = (kept // 2 + 8) // 8 * 8
    solved = call(
        functools.partial(solve_y_kernel, count_x),
        (spectra, total, wave, beside(both), turns_y),
        shaped(count, half, LANES),
        (pltpu.VMEM((length_y + 2 * MARGIN, LANES), F32),),
        after=spread,
        flops=4 * 10**9,
        moved=6 << 20,
        name="solve_y",
    )
    solved = lax.all_to_all(solved, ("gy", "gx"), 0, 0, tiled=True)
    back = 2.0 * zero.T
    back[LANES // 2] *= 0.5
    tables = np.concatenate(
        [beside(full.T), beside(back, 2.0 * middle.T)]
    )
    pressed = call(
        functools.partial(inverse_x_kernel, kept, 1.0 / (length_x * length_y)),
        (solved, tables, turns),
        shaped(count_x, kept, local_x + LANES),
        (pltpu.VMEM((kept, length_x), F32),),
        after=stepped,
        flops=10**9,
        moved=4 << 20,
        name="inverse_x",
    )
    return lax.all_to_all(pressed, "gx", 0, 0, tiled=True)


def refine_tables(weights_x, weights_y, tall, wide):
    first = lax.axis_index("gx") * wide
    ends = jnp.concatenate([weights_x[:, -LANES:], weights_x, weights_x[:, :LANES]], axis=1)
    own = lax.dynamic_slice(ends, (0, first), (4, wide + 2 * LANES))
    half = LANES // 2
    edge = jnp.concatenate([own[:, wide + LANES : wide + LANES + half], own[:, half:LANES]], axis=1)
    edge = jnp.pad(edge, ((0, 0), (0, LANES)))
    tiles = wide // (2 * LANES)
    weights = jnp.concatenate([own[:, LANES : wide + LANES], edge], axis=1)
    weights = weights.reshape(4, tiles + 1, 1, 2 * LANES)
    fine = np.arange(2 * LANES)
    targets = np.tile(fine // 2 - 1, (tiles + 1, 1))
    targets[tiles] = np.where(fine < half, fine // 2 - 1, half + fine // 2 - 1)
    cells = lax.broadcasted_iota(jnp.int32, (tiles + 1, 2 * LANES, 2 * LANES), 1)
    targets = jnp.asarray(targets[:, None, :].astype(np.int32))
    rise_x = sum(
        jnp.where(cells == (targets + t) % (2 * LANES), weights[t], 0.0) for t in range(4)
    )
    ends = jnp.concatenate([weights_y[:, -HALO:], weights_y, weights_y[:, :HALO]], axis=1)
    own = lax.dynamic_slice(ends, (0, lax.axis_index("gy") * tall), (4, tall + 2 * HALO))
    high, steps = TILE + 2 * HALO, tall // TILE
    own = jnp.stack([own[:, k * TILE : k * TILE + high] for k in range(steps)], axis=1)
    cells = lax.broadcasted_iota(jnp.int32, (steps, high, high // 2 + HALO), 2)
    targets = lax.broadcasted_iota(jnp.int32, cells.shape, 1) // 2 + (HALO // 2 - 1)
    rise_y = sum(jnp.where(cells == targets + s, own[s][:, :, None], 0.0) for s in range(4))
    return rise_x, rise_y


def fast_shards(velocity, weights_x, weights_y, acoustic, wall_mask):
    parts, _, tall, wide = acoustic.shape
    _, _, local_y, local_x = velocity.shape
    count_x, count_y = lax.axis_size("gx"), lax.axis_size("gy")
    place_x, place_y = lax.axis_index("gx"), lax.axis_index("gy")
    full, high, steps = wide + LANES, TILE + 2 * HALO, tall // TILE
    strips = (parts + 2) * HALO
    small = 2 * HALO
    has = jnp.stack([place_x > 0, place_x < count_x - 1, place_y > 0, place_y < count_y - 1])
    has = has.astype(F32)
    scalars = pl.BlockSpec(memory_space=pltpu.SMEM)

    def at(block, *index):
        return pl.BlockSpec(block, lambda i: index)

    sent, first, last = call(
        edges_kernel,
        (velocity, acoustic, acoustic, wall_mask, wall_mask),
        (
            shaped(count_x, 2, local_y // count_x, local_x),
            shaped(strips, wide),
            shaped(strips, wide),
        ),
        steps=1,
        specs={
            1: at((parts, 1, small, wide), 0, 0, 0, 0),
            2: at((parts, 1, small, wide), 0, 0, tall // small - 1, 0),
            3: at((1, HALO, wide), 0, 0, 0),
            4: at((1, HALO, wide), 0, tall // HALO - 1, 0),
        },
        moved=4 << 20,
        megabytes=56,
        name="edges",
    )
    above, below = ring(last, "gy", 1), ring(first, "gy", -1)
    to_right, to_left = call(
        columns_kernel,
        (has, acoustic, acoustic, wall_mask, wall_mask, velocity, velocity, above, below),
        (shaped(strips, tall + LANES), shaped(strips, tall + LANES)),
        steps=1,
        specs={
            0: scalars,
            1: at((parts, 1, tall, LANES), 0, 0, 0, 0),
            2: at((parts, 1, tall, LANES), 0, 0, 0, wide // LANES - 1),
            3: at((1, tall, LANES), 0, 0, 0),
            4: at((1, tall, LANES), 0, 0, wide // LANES - 1),
            5: at((1, 1, local_y, LANES), 1, 0, 0, 0),
            6: at((1, 1, local_y, LANES), 1, 0, 0, local_x // LANES - 1),
        },
        moved=8 << 20,
        megabytes=56,
        name="columns",
    )
    from_left, from_right = ring(to_right, "gx", 1), ring(to_left, "gx", -1)
    sides, flow_side = call(
        sides_kernel,
        (has, from_left, from_right),
        (shaped(parts + 1, tall + LANES, LANES), shaped(local_y + LANES, LANES)),
        steps=1,
        specs={0: scalars},
        moved=8 << 20,
        megabytes=56,
        name="sides",
    )
    across, along = band_tables(high)
    along_inner = along[HALO : HALO + TILE]
    per, rows = TILE // small, TILE // HALO
    walls = (
        pl.BlockSpec((1, TILE, wide), lambda i: (0, i, 0)),
        pl.BlockSpec((1, HALO, wide), lambda i: (0, jnp.maximum(i * rows - 1, 0), 0)),
        pl.BlockSpec((1, HALO, wide), lambda i: (0, jnp.minimum((i + 1) * rows, steps * rows - 1), 0)),
    )
    by_tile = pl.BlockSpec((parts, 1, TILE, wide), lambda i: (0, 0, i, 0))
    over = pl.BlockSpec((parts, 1, small, wide), lambda i: (0, 0, jnp.maximum(i * per - 1, 0), 0))
    under = pl.BlockSpec(
        (parts, 1, small, wide), lambda i: (0, 0, jnp.minimum((i + 1) * per, steps * per - 1), 0)
    )
    flat = pl.BlockSpec((parts, TILE, wide), lambda i: (0, i, 0))
    quiet, quiet_done = call(
        quiet_step_kernel,
        (has, acoustic, acoustic, acoustic, wall_mask, wall_mask, wall_mask, above, below, sides, across, along, along_inner),
        (shaped(parts, tall, wide), shaped(8, LANES)),
        steps=steps,
        specs=dict(enumerate((scalars, by_tile, over, under) + walls)),
        out_specs=(flat, pl.BlockSpec((8, LANES), lambda i: (0, 0))),
        megabytes=56,
        flops=9 * 10**9,
        moved=50 << 20,
        name="quiet_step",
    )
    beside_done = from_left[:8, :LANES] + from_right[:8, :LANES]
    lines = pressure_lines(sent, count_y, (beside_done,), (quiet_done,))
    rise_x, rise_y = refine_tables(weights_x, weights_y, tall, wide)
    operands = (has, lines, velocity, flow_side, wall_mask, wall_mask, wall_mask, above, below, sides, rise_x, rise_y, quiet, across, along_inner)
    specs = {
        0: scalars,
        2: at((1, 1, local_y, local_x), 1, 0, 0, 0),
        9: at((1, tall + LANES, LANES), parts, 0, 0),
        11: pl.BlockSpec((1,) + rise_y.shape[1:], lambda i: (i, 0, 0)),
        12: flat,
    }
    specs.update({4 + i: spec for i, spec in enumerate(walls)})
    return call(
        source_kernel,
        operands,
        shaped(*acoustic.shape, kind=BF16),
        (pltpu.VMEM((2, local_y + 2 * HALO, full), BF16),),
        steps=steps,
        specs=specs,
        out_specs=by_tile,
        flops=4 * 10**9,
        moved=16 << 20,
        megabytes=56,
        name="source_step",
    )


def fits(count_x, count_y, velocity, acoustic):
    _, planes, local_y, local_x = velocity
    _, _, tall, wide = acoustic
    length_x, length_y = local_x * count_x, local_y * count_y
    rows = local_y // count_x
    base_x, base_y = length_x // RADIX, length_y // RADIX
    return (
        planes == 1
        and length_x * 2 == count_x * count_y * LANES
        and base_x % (2 * LANES) == 0
        and local_x % base_x == 0
        and rows % 8 == 0
        and base_y % rows == 0
        and base_y % 8 == 0
        and MARGIN * 2 % (8 * count_x) == 0
        and tall == 2 * local_y
        and wide == 2 * local_x
        and tall % TILE == 0
        and wide % (2 * LANES) == 0
    )


def extended(array, sides, width):
    for axis, dim in sides:
        size, length = (lax.axis_size(axis), array.shape[dim])
        up = [(i, (i + 1) % size) for i in range(size - 1)]
        down = [(j, i) for i, j in up]
        last = lax.slice_in_dim(array, length - width, length, axis=dim)
        leading = lax.slice_in_dim(array, 0, width, axis=dim)
        before = lax.ppermute(last, axis, up)
        after = lax.ppermute(leading, axis, down)
        array = jnp.concatenate([before, array, after], axis=dim)
    return array


def gradients(padded):
    height = padded.shape[-2] - 6
    breadth = padded.shape[-1] - 6
    rows_mid = padded[..., 3 : 3 + height, :]
    cols_mid = padded[..., :, 3 : 3 + breadth]
    along_x = jnp.zeros_like(padded[..., 3 : 3 + height, 3 : 3 + breadth])
    along_y = jnp.zeros_like(along_x)
    for index, weight in enumerate(stencil_weights):
        distance = index + 1
        along_x = along_x + weight * (
            rows_mid[..., 3 + distance : 3 + distance + breadth]
            - rows_mid[..., 3 - distance : 3 - distance + breadth]
        )
        along_y = along_y + weight * (
            cols_mid[..., 3 + distance : 3 + distance + height, :]
            - cols_mid[..., 3 - distance : 3 - distance + height, :]
        )
    return (along_x, along_y)


def tendency(padded, source):
    along_x, along_y = gradients(padded)
    diverge = along_x[1] + along_y[2]
    forcing = jnp.stack([-diverge, -along_x[3], -along_y[3], source - diverge])
    return forcing - mean_flow * along_x


def spectral_index(flat, length):
    second = length // 16
    wave = flat // second + 16 * (flat % second)
    return jnp.where(wave < length // 2, wave, wave - length).astype(jnp.float32)


def twiddles(rows_count, cols_count, modulus, sign):
    products = jnp.arange(rows_count)[:, None] * jnp.arange(cols_count)[None, :] % modulus
    angles = 2.0 * math.pi / modulus * products.astype(jnp.float32)
    return (jnp.cos(angles), sign * jnp.sin(angles))


def mix_rows(real_part, imag_part, cosine, sine):
    exact = lax.Precision.HIGHEST
    cos_real = jnp.einsum("ka,...ab->...kb", cosine, real_part, precision=exact)
    cos_imag = jnp.einsum("ka,...ab->...kb", cosine, imag_part, precision=exact)
    sin_real = jnp.einsum("ka,...ab->...kb", sine, real_part, precision=exact)
    sin_imag = jnp.einsum("ka,...ab->...kb", sine, imag_part, precision=exact)
    return (cos_real - sin_imag, cos_imag + sin_real)


def mix_cols(real_part, imag_part, cosine, sine):
    exact = lax.Precision.HIGHEST
    cos_real = jnp.einsum("...kb,bc->...kc", real_part, cosine, precision=exact)
    cos_imag = jnp.einsum("...kb,bc->...kc", imag_part, cosine, precision=exact)
    sin_real = jnp.einsum("...kb,bc->...kc", real_part, sine, precision=exact)
    sin_imag = jnp.einsum("...kb,bc->...kc", imag_part, sine, precision=exact)
    return (cos_real - sin_imag, cos_imag + sin_real)


def rotate(real_part, imag_part, cosine, sine):
    return (real_part * cosine - imag_part * sine, real_part * sine + imag_part * cosine)


def discrete(real_part, imag_part, sign):
    length = real_part.shape[-1]
    second = length // 16
    initial = real_part.shape
    folded = initial[:-1] + (16, second)
    real_part = real_part.reshape(folded)
    imag_part = imag_part.reshape(folded)
    small_cos, small_sin = twiddles(16, 16, 16, sign)
    large_cos, large_sin = twiddles(second, second, second, sign)
    turn_cos, turn_sin = twiddles(16, second, length, sign)
    if sign < 0:
        real_part, imag_part = mix_rows(real_part, imag_part, small_cos, small_sin)
        real_part, imag_part = rotate(real_part, imag_part, turn_cos, turn_sin)
        real_part, imag_part = mix_cols(real_part, imag_part, large_cos, large_sin)
    else:
        real_part, imag_part = mix_cols(real_part, imag_part, large_cos, large_sin)
        real_part, imag_part = rotate(real_part, imag_part, turn_cos, turn_sin)
        real_part, imag_part = mix_rows(real_part, imag_part, small_cos, small_sin)
        real_part = real_part / length
        imag_part = imag_part / length
    return (real_part.reshape(initial), imag_part.reshape(initial))


def transform(stacked, sign, kind):
    if kind == "real_in":
        real_part = stacked
        imag_part = jnp.zeros_like(stacked)
    else:
        half = stacked.shape[0] // 2
        real_part = stacked[:half]
        imag_part = stacked[half:]
    real_out, imag_out = discrete(real_part, imag_part, sign)
    if kind == "real_out":
        return real_out
    return jnp.concatenate([real_out, imag_out], axis=0)


def project(stacked, wave_x, wave_y):
    coef_xx = wave_x * wave_x
    coef_xy = 2.0 * wave_x * wave_y
    coef_yy = wave_y * wave_y
    denominator = wave_x * wave_x + wave_y * wave_y
    positive = denominator > 0
    safe = jnp.where(positive, denominator, 1.0)

    def combine(parts):
        numerator = -(coef_xx * parts[0] + coef_xy * parts[1] + coef_yy * parts[2])
        return jnp.where(positive, numerator / safe, 0.0)

    return jnp.stack([combine(stacked[:3]), combine(stacked[3:])])


def refine(stacked, weights):
    result = jnp.zeros(stacked.shape[:-1] + (2 * stacked.shape[-1],), jnp.float32)
    for offset in range(4):
        result = (
            result
            + jnp.repeat(jnp.roll(stacked, 1 - offset, axis=-1), 2, axis=-1) * weights[offset]
        )
    return result


def lines_x(stacked, action):
    gathered = action(lax.all_to_all(stacked, "gx", split_axis=2, concat_axis=3, tiled=True))
    return lax.all_to_all(gathered, "gx", split_axis=3, concat_axis=2, tiled=True)


def lines_y(stacked, action):
    turned = jnp.swapaxes(stacked, 2, 3)
    gathered = action(lax.all_to_all(turned, "gy", split_axis=2, concat_axis=3, tiled=True))
    returned = lax.all_to_all(gathered, "gy", split_axis=3, concat_axis=2, tiled=True)
    return jnp.swapaxes(returned, 2, 3)


def expand(fields):
    return extended(fields, (("gx", 3), ("gy", 2)), 3)


def shards(velocity, weights_x, weights_y, acoustic, wall_mask):
    acoustic = acoustic.astype(jnp.float32)
    flow_x = velocity[0]
    flow_y = velocity[1]
    tensor = jnp.stack([flow_x * flow_x, flow_x * flow_y, flow_y * flow_y])
    count_gx = lax.axis_size("gx")
    count_gy = lax.axis_size("gy")
    place_x = lax.axis_index("gx")
    place_y = lax.axis_index("gy")
    local_y = tensor.shape[2]
    local_x = tensor.shape[3]
    length_x = local_x * count_gx
    length_y = local_y * count_gy

    def forward_real(portion):
        return transform(portion, -1, "real_in")

    def finish_x(portion):
        return refine(transform(portion, 1, "real_out"), weights_x)

    spectra = lines_x(tensor, forward_real)
    share_x = local_x // count_gy
    line_x = spectral_index(place_x * local_x + place_y * share_x + jnp.arange(share_x), length_x)[
        :, None
    ]
    line_y = spectral_index(jnp.arange(length_y), length_y)[None, :]

    def solve_y(portion):
        solved = project(transform(portion, -1, "complex"), line_x, line_y)
        return refine(transform(solved, 1, "complex"), weights_y)

    pressure = lines_y(spectra, solve_y)
    source = lines_x(pressure, finish_x)[0]
    open_cells = (1 - wall_mask).astype(jnp.float32)
    first_rate = tendency(expand(acoustic), source)
    middle = open_cells * (acoustic + time_step * first_rate)
    second_rate = tendency(expand(middle), source)
    return (open_cells * (acoustic + 0.5 * time_step * (first_rate + second_rate))).astype(
        jnp.bfloat16
    )


def solution(mesh):
    in_specs = (P(None, None, "gy", "gx"), P(), P(), P(None, None, "gy", "gx"), P(None, "gy", "gx"))
    out_specs = P(None, None, "gy", "gx")

    def chosen(velocity, weights_x, weights_y, acoustic, wall_mask):
        sizes = (mesh.shape["gx"], mesh.shape["gy"], velocity.shape, acoustic.shape)
        plan = fast_shards if fits(*sizes) else shards
        return plan(velocity, weights_x, weights_y, acoustic, wall_mask)

    return jax.shard_map(
        chosen, mesh=mesh, in_specs=in_specs, out_specs=out_specs, check_vma=False
    )
```

```python
import functools
import math

import jax
import jax.numpy as jnp
import ml_dtypes
import numpy as np
from jax import lax
from jax.experimental import pallas as pl
from jax.experimental.pallas import tpu as pltpu
from jax.sharding import PartitionSpec as P

stencil_weights = (0.75, -0.15, 1.0 / 60.0)
mean_flow = 0.3
time_step = 0.5
whole_weights = (45.0, -9.0, 1.0)

LANES = 128
RADIX = 8
HALO = 8
MARGIN = 16
TILE = 128
ROOT = math.sqrt(0.5)
BF16 = jnp.bfloat16
F32 = jnp.float32


def halves(table):
    high = table.astype(np.float32).astype(ml_dtypes.bfloat16)
    low = (table - high.astype(np.float64)).astype(np.float32).astype(ml_dtypes.bfloat16)
    return high, low


def packed_columns(cosine, sine):
    half = LANES // 2
    parts = []
    for first in range(0, cosine.shape[1], half):
        parts += [cosine[:, first : first + half], sine[:, first : first + half]]
    return np.concatenate(parts, axis=1)


@functools.lru_cache(maxsize=None)
def x_tables(length):
    base = length // RADIX
    m = np.arange(base)[:, None]
    q = np.arange(base)[None, :]
    angle = 2.0 * np.pi * ((m * q) % base) / base
    cosine, sine = np.cos(angle), np.sin(angle)
    full = np.concatenate([packed_columns(cosine, -sine), packed_columns(sine, cosine)], axis=0)
    half = base // 2
    zero_cos, zero_sin = cosine[:, :half].copy(), -sine[:, :half]
    zero_cos[:, 0] = 0.0
    zero_sin = zero_sin.copy()
    zero_sin[:, 0] = (-1.0) ** np.arange(base)
    zero = packed_columns(zero_cos, zero_sin)
    shifted = 2.0 * np.pi * ((m * (RADIX * q[:, :half] + RADIX // 2)) % length) / length
    middle = packed_columns(np.cos(shifted), -np.sin(shifted))
    turns = 2.0 * np.pi * np.arange(1, RADIX // 2)[:, None] * np.arange(base)[None, :] / length
    return full, zero, middle, np.cos(turns), np.sin(turns)


@functools.lru_cache(maxsize=None)
def y_tables(length):
    base = length // RADIX
    index = np.arange(base)
    angle = 2.0 * np.pi * ((index[:, None] * index[None, :]) % base) / base
    both = np.concatenate([np.cos(angle), np.sin(angle)], axis=0)
    turns = 2.0 * np.pi * np.arange(RADIX)[:, None] * index[None, :] / length
    return both, np.concatenate([np.cos(turns), np.sin(turns)], axis=0).T.astype(np.float32)


@functools.lru_cache(maxsize=None)
def wave_table(length, count):
    slots = LANES // 4
    base = length // RADIX
    waves = []
    for residue in (1, 2, 3):
        waves.append(RADIX * np.arange(base) + residue)
    waves.append(RADIX * np.arange(base // 2))
    waves.append(RADIX * np.arange(base // 2) + RADIX // 2)
    waves = np.concatenate(waves)
    waves = np.where(waves == 0, length // 2, waves)
    waves = np.where(waves < length // 2, waves, waves - length).reshape(count, slots)
    return np.tile(waves, (1, 4)).astype(np.float32)


@functools.lru_cache(maxsize=None)
def band_tables(rows):
    across = np.zeros((4 * LANES, 2 * LANES))
    column = np.arange(2 * LANES)
    down = np.zeros((rows, rows))
    for index, weight in enumerate(whole_weights):
        distance = index + 1
        across[column + LANES + distance, column] = weight
        across[column + LANES - distance, column] = -weight
        down += weight * (np.eye(rows, k=distance) - np.eye(rows, k=-distance))
    return across.astype(ml_dtypes.bfloat16), down.astype(ml_dtypes.bfloat16)


def beside(*tables):
    high, low = halves(np.concatenate(tables, axis=1))
    return np.concatenate([high, low], axis=0)


def split(values):
    high = values.astype(BF16)
    return high, (values - high.astype(F32)).astype(BF16)


def dot(left, right):
    return jnp.dot(left, right, preferred_element_type=F32)


def exact_dot(left, right):
    left_high, left_low = left
    right_high, right_low = right
    return dot(left_high, right_high) + (dot(left_low, right_high) + dot(left_high, right_low))


def lane_index(shape):
    return lax.broadcasted_iota(jnp.int32, shape, len(shape) - 1)


def spin(values, shift):
    return pltpu.roll(values, shift % values.shape[-1], values.ndim - 1)


def lane_tile(values, index):
    return values[:, index * LANES : (index + 1) * LANES]


def x_parts(tables, base):
    wide = 2 * base
    full = (tables[:wide], tables[wide : 2 * wide])
    at = 2 * wide
    high, low = tables[at : at + base], tables[at + base : at + 2 * base]
    return full, (high[:, :base], low[:, :base]), (high[:, base:], low[:, base:])


def edges_kernel(place, velocity, top, low, top_wall, low_wall, *outs):
    *sent, first, last = outs
    count = len(sent)
    _, rows, width = sent[0].shape
    for mask, piece in enumerate(sent):
        start = pl.multiple_of((place[0] ^ mask) * rows, 8)
        for c in range(2):
            piece[c] = velocity[c, 0, pl.ds(start, rows), :]
    parts, _, small, _ = top.shape
    blank = jnp.zeros((HALO, first.shape[1] - width), F32)
    for k in range(parts):
        at = slice(k * HALO, (k + 1) * HALO)
        first[at, :] = top[k, 0].astype(F32)[:HALO]
        last[at, :] = low[k, 0].astype(F32)[small - HALO :]
    at = slice(parts * HALO, (parts + 1) * HALO)
    first[at, :] = 1.0 - top_wall[0].astype(F32)
    last[at, :] = 1.0 - low_wall[0].astype(F32)
    at = slice((parts + 1) * HALO, (parts + 2) * HALO)
    first[at, :width] = velocity[1, 0, :HALO, :]
    last[at, :width] = velocity[1, 0, count * rows - HALO :, :]
    first[at, width:] = blank
    last[at, width:] = blank


def columns_kernel(
    has, left, right, left_wall, right_wall, left_flow, right_flow, above, below, to_right, to_left
):
    parts = left.shape[0]
    wide, flow_wide = above.shape[1], above.shape[1] // 2
    gap = jnp.zeros((LANES - 2 * HALO, LANES), F32)

    def tall(k, inner, first, sides):
        at = slice(k * HALO, (k + 1) * HALO)
        over, under = above[at, first : first + LANES], below[at, first : first + LANES]
        return jnp.concatenate([inner, under * sides[1], gap, over * sides[0]], axis=0).T

    for k in range(parts + 1):
        at = slice(k * HALO, (k + 1) * HALO)
        if k < parts:
            near, far = left[k, 0].astype(F32), right[k, 0].astype(F32)
        else:
            near, far = 1.0 - left_wall[0].astype(F32), 1.0 - right_wall[0].astype(F32)
        sides = (has[2], has[3])
        to_left[at, :] = tall(k, near, 0, sides)[:HALO]
        to_right[at, :] = tall(k, far, wide - LANES, sides)[LANES - HALO :]
    k = parts + 1
    at = slice(k * HALO, (k + 1) * HALO)
    size = left_flow.shape[2] + LANES
    blank = jnp.zeros((HALO, to_left.shape[1] - size), F32)
    to_left[at, :size] = tall(k, left_flow[0, 0], 0, (1.0, 1.0))[:HALO]
    to_right[at, :size] = tall(k, right_flow[0, 0], flow_wide - LANES, (1.0, 1.0))[LANES - HALO :]
    to_left[at, size:] = blank
    to_right[at, size:] = blank


def sides_kernel(has, from_left, from_right, sides, flow_side):
    parts, tall, _ = sides.shape
    gap = jnp.zeros((LANES - 2 * HALO, tall), F32)
    for k in range(parts):
        at = slice(k * HALO, (k + 1) * HALO)
        tile = [from_right[at, :] * has[1], gap, from_left[at, :] * has[0]]
        sides[k] = jnp.concatenate(tile, axis=0).T
    at = slice(parts * HALO, (parts + 1) * HALO)
    size = flow_side.shape[0]
    tile = [from_right[at, :size], gap[:, :size], from_left[at, :size]]
    flow_side[...] = jnp.concatenate(tile, axis=0).T


def forward_x_kernel(place, *refs):
    *pieces, tables, turns, out, total, lines = refs
    count, _, rows, local = lines.shape
    for mask, piece in enumerate(pieces):
        lines[place[0] ^ mask] = piece[...]
    base = turns.shape[1]
    per = local // base
    u = [lines[t // per, 0, :, (t % per) * base : (t % per + 1) * base] for t in range(RADIX)]
    v = [lines[t // per, 1, :, (t % per) * base : (t % per + 1) * base] for t in range(RADIX)]
    energy = sum(b * b for b in v)
    energy = jnp.sum(energy.reshape(rows // 8, 8, base), axis=0)
    total[...] = sum(energy[:, k : k + LANES] for k in range(0, base, LANES))
    fields = ([a * a - b * b for a, b in zip(u, v)], [2.0 * a * b for a, b in zip(u, v)])
    zeros, mids, reals, imags = [], [], [[], [], []], [[], [], []]
    for a in fields:
        s04, s26, s15, s37 = a[0] + a[4], a[2] + a[6], a[1] + a[5], a[3] + a[7]
        d04, d26, d15, d37 = a[0] - a[4], a[2] - a[6], a[1] - a[5], a[3] - a[7]
        zeros.append((s04 + s26) + (s15 + s37))
        mids.append((s04 + s26) - (s15 + s37))
        minus, plus = ROOT * (d15 - d37), ROOT * (d15 + d37)
        turned = (
            (d04 + minus, -d26 - plus),
            (s04 - s26, s37 - s15),
            (d04 - minus, d26 - plus),
        )
        for index, (real, imag) in enumerate(turned):
            c, s = turns[index : index + 1, :], turns[index + 3 : index + 4, :]
            reals[index].append(real * c + imag * s)
            imags[index].append(imag * c - real * s)
    stacked = jnp.concatenate(
        [
            jnp.concatenate([jnp.concatenate(reals[i], axis=0) for i in range(3)], axis=0),
            jnp.concatenate([jnp.concatenate(imags[i], axis=0) for i in range(3)], axis=0),
        ],
        axis=1,
    )
    full, zero, middle = x_parts(tables, base)
    full = exact_dot(split(stacked), full)
    zero = exact_dot(split(jnp.concatenate(zeros, axis=0)), zero)
    middle = exact_dot(split(jnp.concatenate(mids, axis=0)), middle)
    low = lane_index((rows, LANES)) % 64 < 32
    target = 0
    blocks = [full[2 * rows * i : 2 * rows * (i + 1)] for i in range(3)] + [zero, middle]
    for block in blocks:
        for first in range(0, block.shape[1], LANES):
            a = block[:rows, first : first + LANES]
            c = block[rows:, first : first + LANES]
            out[target] = jnp.where(low, a, spin(c, 32))
            out[target + 1] = jnp.where(low, spin(a, -32), c)
            target += 2


def eighths(x, turn):
    s04, s26, s15, s37 = x[0] + x[4], x[2] + x[6], x[1] + x[5], x[3] + x[7]
    d04, d26, d15, d37 = x[0] - x[4], x[2] - x[6], x[1] - x[5], x[3] - x[7]
    quarter = turn(s15 - s37)
    spun_26, spun_37 = turn(d26), turn(d37)
    one, three = d15 + spun_37, d15 - spun_37
    spun_one, spun_three = turn(one), turn(three)
    one = ROOT * (one + spun_one)
    three = ROOT * (spun_three - three)
    return [
        (s04 + s26) + (s15 + s37),
        (d04 + spun_26) + one,
        (s04 - s26) + quarter,
        (d04 - spun_26) + three,
        (s04 + s26) - (s15 + s37),
        (d04 + spun_26) - one,
        (s04 - s26) - quarter,
        (d04 - spun_26) - three,
    ]


def solve_y_kernel(count_x, lines, total, wave, both, turns, out, held):
    count, rows, _ = lines.shape
    base = turns.shape[0]
    length = count * rows
    block = count_x * rows
    per = base // rows
    lanes = lane_index((base, LANES))
    sign = jnp.where(lanes < 64, 1.0, -1.0).astype(F32)

    def minus_i(z):
        return spin(z, 64) * sign

    def plus_i(z):
        return spin(z, 64) * -sign

    fields = [
        jnp.concatenate([lines[t * per + k] for k in range(per)], axis=0) for t in range(RADIX)
    ]
    mixed = eighths(fields, minus_i)
    table = turns[...]
    cosines = [table[:, r : r + 1] for r in range(RADIX)]
    sines = [table[:, RADIX + r : RADIX + r + 1] * sign for r in range(RADIX)]
    mixed = [mixed[0]] + [
        mixed[r] * cosines[r] + spin(mixed[r], 64) * sines[r] for r in range(1, RADIX)
    ]
    tables = (both[: 2 * base], both[2 * base :])
    product = exact_dot(tables, split(jnp.concatenate(mixed, axis=1)))
    kx = wave[0:1, :]
    is_first = lanes % 64 < 32
    q = lax.broadcasted_iota(jnp.int32, (base, LANES), 0)
    edge = jnp.float32(-(length // 2))
    solved = []
    for r in range(RADIX):
        at = slice(r * LANES, (r + 1) * LANES)
        spectrum = product[:base, at] + minus_i(product[base:, at])
        k = RADIX * q + r
        ky = jnp.where(k < length // 2, k, k - length).astype(F32)
        cross = jnp.where((kx == edge) == (ky == edge), kx * ky, 0.0)
        symbol = jnp.where(is_first, kx * kx, cross) / (kx * kx + ky * ky)
        terms = symbol * spectrum
        solved.append(terms + spin(terms, -32))
    product = exact_dot(tables, split(jnp.concatenate(solved, axis=1)))
    mixed = []
    for r in range(RADIX):
        at = slice(r * LANES, (r + 1) * LANES)
        value = product[:base, at] + plus_i(product[base:, at])
        if r:
            value = value * cosines[r] - spin(value, 64) * sines[r]
        mixed.append(value)
    for t, values in enumerate(eighths(mixed, plus_i)):
        held[MARGIN + t * base : MARGIN + (t + 1) * base, :] = values
    held[0:MARGIN, :] = held[length : length + MARGIN, :]
    held[length + MARGIN : length + 2 * MARGIN, :] = held[MARGIN : 2 * MARGIN, :]
    spare = total[...] + spin(total[...], 32)
    kept = rows + 2 * MARGIN // count_x
    half = out.shape[1]
    rest = kept - half
    low = lane_index((8, LANES)) % 64 < 32
    for target in range(count):
        start = (target // count_x) * block + (target % count_x) * kept
        for row in range(0, half, 8):
            a = held[start + row : start + row + 8, :]
            if row < rest:
                b = spin(held[start + half + row : start + half + row + 8, :], 32)
            else:
                b = spare
            out[target, row : row + 8, :] = jnp.where(low, a, b)


def inverse_x_kernel(
    kept, scale, place, lines, tables, turns, *refs
):
    *outs, held = refs
    count, half, _ = lines.shape
    base = turns.shape[1]
    length = RADIX * base
    rest = kept - half
    low = lane_index((half, LANES)) % 64 < 32
    groups, spare = [], None
    for first in range(0, count, 2):
        even, odd = lines[first], lines[first + 1]
        a = jnp.where(low, even, spin(odd, 32))
        b = jnp.where(low, spin(even, -32), odd)
        groups.append(jnp.concatenate([a, b[:rest]], axis=0))
        extra = b[rest : rest + 8]
        spare = extra if spare is None else spare + extra
    mean = jnp.sum(spare) * scale
    wide = 2 * base // LANES
    narrow = base // LANES
    stacked = jnp.concatenate(
        [jnp.concatenate(groups[i * wide : (i + 1) * wide], axis=1) for i in range(3)], axis=0
    )
    at = 3 * wide
    zeros = jnp.concatenate(groups[at : at + narrow], axis=1)
    mids = jnp.concatenate(groups[at + narrow : at + 2 * narrow], axis=1)
    full, zero, middle = x_parts(tables, base)
    full = exact_dot(split(stacked), full)
    zero = exact_dot(split(zeros), zero) * scale
    mid = exact_dot(split(mids), middle) * scale
    turned = []
    for i in range(3):
        real = full[i * kept : (i + 1) * kept, :base]
        imag = full[i * kept : (i + 1) * kept, base:]
        c = turns[i : i + 1, :] * (2.0 * scale)
        s = turns[i + 3 : i + 4, :] * (2.0 * scale)
        turned.append((real * c - imag * s, real * s + imag * c))
    for t in range(RADIX):
        value = zero + mid if t % 2 == 0 else zero - mid
        for i, (real, imag) in enumerate(turned):
            eighth = t * (i + 1) % RADIX
            c = (1.0, ROOT, 0.0, -ROOT, -1.0, -ROOT, 0.0, ROOT)[eighth]
            s = (0.0, ROOT, 1.0, ROOT, 0.0, -ROOT, -1.0, -ROOT)[eighth]
            if c:
                value = value + c * real
            if s:
                value = value - s * imag
        held[:, t * base : (t + 1) * base] = mean - value
    targets, local = len(outs), outs[0].shape[1] - LANES
    right = lane_index((kept, LANES)) < 64
    for mask, out in enumerate(outs):
        start = pl.multiple_of((place[0] ^ mask) * local, LANES)
        after = pl.multiple_of(jnp.where(start + local == length, 0, start + local), LANES)
        before = pl.multiple_of(jnp.where(start == 0, length, start) - LANES, LANES)
        out[:, :local] = held[:, pl.ds(start, local)]
        out[:, local:] = jnp.where(
            right, held[:, pl.ds(after, LANES)], held[:, pl.ds(before, LANES)]
        )


def slopes_x(parts, band, with_edge):
    tiles = parts[0].shape[-1] // LANES
    pieces = []
    for first in list(range(0, tiles - 1, 2)) + ([tiles - 1] if with_edge else []):
        steps = (-1, 0, 1, 2) if first < tiles - 1 else (-1, 0, 1)
        table = band[...] if first < tiles - 1 else band[: 3 * LANES, :LANES]
        order = [(first + step) % tiles for step in steps]
        piece = None
        for part in parts:
            term = dot(jnp.concatenate([lane_tile(part, t) for t in order], axis=1), table)
            piece = term if piece is None else piece + term
        pieces.append(piece)
    return jnp.concatenate(pieces, axis=1)


def edged(k, side, center, up, down, above, below, sides, has, first=0):
    step = pl.program_id(0) + first
    tile, width = center.shape
    tall = sides.shape[1]
    last = (tall - LANES) // tile - 1
    base = pl.multiple_of(step * tile, 8)
    at = slice(k * HALO, (k + 1) * HALO)
    before = pl.multiple_of(jnp.where(step == 0, tall, base) - HALO, 8)
    over = jnp.where(step == 0, above[at, :] * has[2], up)
    under = jnp.where(step == last, below[at, :] * has[3], down)
    rows = (
        (over, sides[side, pl.ds(before, HALO), :]),
        (center, sides[side, pl.ds(base, tile), :]),
        (under, sides[side, pl.ds(pl.multiple_of(base + tile, 8), HALO), :]),
    )
    return jnp.concatenate([jnp.concatenate(pair, axis=1) for pair in rows], axis=0)


def edged_open(k, side, wall, wall_up, wall_down, above, below, sides, has, first=0):
    open_cells = [1.0 - ref[0].astype(F32) for ref in (wall, wall_up, wall_down)]
    return edged(k, side, *open_cells, above, below, sides, has, first)


def quiet_step_kernel(
    first, has, center, up, down, wall, wall_up, wall_down, above, below, sides, across, along, along_inner, out, mark
):
    parts, _, tile, width = center.shape
    high = tile + 2 * HALO
    opened = edged_open(parts, parts, wall, wall_up, wall_down, above, below, sides, has, first)
    values = []
    for k in range(parts):
        value = edged(
            k,
            k,
            center[k, 0].astype(F32),
            up[k, 0].astype(F32)[up.shape[2] - HALO :],
            down[k, 0].astype(F32)[:HALO],
            above,
            below,
            sides,
            has,
            first,
        )
        values.append(value)

    def drops(x, along_b, along_p):
        diverge = x[1] + along_b
        return (
            diverge + mean_flow * x[0],
            x[3] + mean_flow * x[1],
            along_p + mean_flow * x[2],
            diverge + mean_flow * x[3],
        )

    short = [value.astype(BF16) for value in values]
    x = slopes_x((jnp.concatenate(short, axis=0),), across, True)
    x = [x[k * high : (k + 1) * high] for k in range(parts)]
    table = along[...]
    dropped = drops(x, dot(table, short[2]), dot(table, short[3]))
    middle = [opened * (v - (time_step / 60.0) * d) for v, d in zip(values, dropped)]
    inner = slice(HALO, HALO + tile)
    x = slopes_x(split(jnp.concatenate([value[inner] for value in middle], axis=0)), across, False)
    x = [x[k * tile : (k + 1) * tile] for k in range(parts)]
    table = along_inner[...]
    y = [sum(dot(table, part) for part in split(middle[k][:, :width])) for k in (2, 3)]
    dropped = drops(x, *y)
    shown = opened[inner, :width]
    for k in range(parts):
        start = 0.5 * values[k][inner, :width] - (0.5 * time_step / 60.0) * dropped[k]
        out[k] = shown * start + 0.5 * middle[k][inner, :width]
    mark[...] = jnp.zeros(mark.shape, F32)


def source_kernel(
    has, place, velocity, flow_side, wall, wall_up, wall_down, above, below, sides, rise_x, rise_y, quiet, across, along_inner, *refs
):
    *lines, out, raised, held = refs
    step = pl.program_id(0)
    parts, tile, width = quiet.shape

    @pl.when(step == 0)
    def _():
        at = slice((parts + 1) * HALO, (parts + 2) * HALO)
        rows, local = velocity.shape[2:]
        beyond = flow_side.shape[0]
        flow = jnp.concatenate(
            [
                jnp.concatenate([above[at, :local], flow_side[beyond - HALO :, :]], axis=1),
                jnp.concatenate([velocity[0, 0], flow_side[:rows, :]], axis=1),
                jnp.concatenate([below[at, :local], flow_side[rows : rows + HALO, :]], axis=1),
            ],
            axis=0,
        )
        kept = lines[0].shape[0]
        for mask, piece in enumerate(lines):
            held[pl.ds(pl.multiple_of((place[0] ^ mask) * kept, 8), kept), :] = piece[...]
        level = held[MARGIN - HALO : MARGIN - HALO + flow.shape[0], :] - flow * flow
        cells = level.shape[1] // LANES
        near = lane_index((level.shape[0], LANES)) < 64
        for k in range(cells):
            after, before = lane_tile(level, (k + 1) % cells), lane_tile(level, (k - 1) % cells)
            around = jnp.concatenate([lane_tile(level, k), jnp.where(near, after, before)], axis=1)
            lanes = 2 * LANES if k < cells - 1 else LANES
            value = split(exact_dot(split(around), split(rise_x[k][:, :lanes])))
            for part in range(2):
                raised[part, :, 2 * k * LANES : 2 * k * LANES + lanes] = value[part]

    start = pl.multiple_of(step * (tile // 2), 16)
    window = [raised[part, pl.ds(start, rise_y.shape[2]), :] for part in range(2)]
    opened = time_step * edged_open(parts, 0, wall, wall_up, wall_down, above, below, sides, has)
    forced = opened * exact_dot(split(rise_y[0]), window)
    inner = slice(HALO, HALO + tile)
    shown = (0.5 / 60.0) * opened[inner, :width]
    x = shown * slopes_x(split(forced[inner]), across, False)
    table = along_inner[...]
    y = sum(dot(table, part) for part in split(forced[:, :width]))
    out[0, 0] = quiet[0].astype(out.dtype)
    out[1, 0] = (quiet[1] - x).astype(out.dtype)
    out[2, 0] = (quiet[2] - shown * y).astype(out.dtype)
    out[3, 0] = (quiet[3] + forced[inner, :width] - mean_flow * x).astype(out.dtype)


def call(
    kernel, operands, outs, scratch=(), steps=0, specs=None, out_specs=None, after=(), aliases=None, megabytes=24, flops=0, moved=0, name=None
):
    count = len(operands)

    def body(*refs):
        kernel(*refs[:count], *refs[count + len(after) :])

    def whole(array):
        zeros = (0,) * len(array.shape)
        return pl.BlockSpec(array.shape, lambda *_: zeros)

    arguments = {}
    chosen = specs or {}
    if steps:
        arguments["grid"] = (steps,)
        in_specs = [chosen.get(i, whole(o)) for i, o in enumerate(operands)]
        arguments["out_specs"] = jax.tree.map(whole, outs) if out_specs is None else out_specs
    else:
        local = pl.BlockSpec(memory_space=pltpu.VMEM)
        in_specs = [chosen.get(i, local) for i in range(count)]
    return pl.pallas_call(
        body,
        out_shape=outs,
        in_specs=in_specs + [pl.BlockSpec(memory_space=pl.ANY)] * len(after),
        scratch_shapes=list(scratch),
        input_output_aliases=aliases or {},
        compiler_params=pltpu.CompilerParams(vmem_limit_bytes=megabytes << 20),
        cost_estimate=pl.CostEstimate(flops=flops, bytes_accessed=moved, transcendentals=0),
        name=name,
        **arguments,
    )(*operands, *after)


def ring(array, axis, step):
    size = lax.axis_size(axis)
    return lax.ppermute(array, axis, [(i, (i + step) % size) for i in range(size)])


def swap(array, axis, mask):
    return lax.ppermute(array, axis, [(i, i ^ mask) for i in range(lax.axis_size(axis))])


def shaped(*shape, kind=F32):
    return jax.ShapeDtypeStruct(shape, kind)


def pressure_lines(sent, place_x, gathered, spread, stepped):
    _, rows, local_x = sent[0].shape
    count_x, count_y = lax.axis_size("gx"), lax.axis_size("gy")
    count = count_x * count_y
    scalars = {0: pl.BlockSpec(memory_space=pltpu.SMEM)}
    length_x, length_y = local_x * count_x, rows * count
    pieces = [piece if mask == 0 else swap(piece, "gx", mask) for mask, piece in enumerate(sent)]
    full, zero, middle, cos_turn, sin_turn = x_tables(length_x)
    turns = np.zeros((8, cos_turn.shape[1]), np.float32)
    turns[0:3], turns[3:6] = cos_turn, sin_turn
    spectra, total = call(
        forward_x_kernel,
        (place_x, *pieces, np.concatenate([beside(full), beside(zero, middle)]), turns),
        (shaped(count, rows, LANES), shaped(8, LANES)),
        (pltpu.VMEM((count_x, 2, rows, local_x), F32),),
        specs=scalars,
        after=gathered,
        flops=10**9,
        moved=4 << 20,
        name="forward_x",
    )
    spectra = lax.all_to_all(spectra, ("gy", "gx"), 0, 0, tiled=True)
    place = lax.axis_index("gy") * count_x + lax.axis_index("gx")
    waves = jnp.asarray(wave_table(length_x, count))
    wave = lax.dynamic_slice(waves, (place, 0), (1, LANES))
    both, turns_y = y_tables(length_y)
    kept = rows + 2 * MARGIN // count_x
    half = (kept // 2 + 8) // 8 * 8
    solved = call(
        functools.partial(solve_y_kernel, count_x),
        (spectra, total, wave, beside(both), turns_y),
        shaped(count, half, LANES),
        (pltpu.VMEM((length_y + 2 * MARGIN, LANES), F32),),
        after=spread,
        flops=4 * 10**9,
        moved=6 << 20,
        name="solve_y",
    )
    solved = lax.all_to_all(solved, ("gy", "gx"), 0, 0, tiled=True)
    back = 2.0 * zero.T
    back[LANES // 2] *= 0.5
    tables = np.concatenate(
        [beside(full.T), beside(back, 2.0 * middle.T)]
    )
    pressed = call(
        functools.partial(inverse_x_kernel, kept, 1.0 / (length_x * length_y)),
        (place_x, solved, tables, turns),
        (shaped(kept, local_x + LANES),) * count_x,
        (pltpu.VMEM((kept, length_x), F32),),
        specs=scalars,
        after=stepped,
        flops=10**9,
        moved=4 << 20,
        name="inverse_x",
    )
    return [piece if mask == 0 else swap(piece, "gx", mask) for mask, piece in enumerate(pressed)]


def refine_tables(weights_x, weights_y, tall, wide):
    first = lax.axis_index("gx") * wide
    ends = jnp.concatenate([weights_x[:, -LANES:], weights_x, weights_x[:, :LANES]], axis=1)
    own = lax.dynamic_slice(ends, (0, first), (4, wide + 2 * LANES))
    half = LANES // 2
    edge = jnp.concatenate([own[:, wide + LANES : wide + LANES + half], own[:, half:LANES]], axis=1)
    edge = jnp.pad(edge, ((0, 0), (0, LANES)))
    tiles = wide // (2 * LANES)
    weights = jnp.concatenate([own[:, LANES : wide + LANES], edge], axis=1)
    weights = weights.reshape(4, tiles + 1, 1, 2 * LANES)
    fine = np.arange(2 * LANES)
    targets = np.tile(fine // 2 - 1, (tiles + 1, 1))
    targets[tiles] = np.where(fine < half, fine // 2 - 1, half + fine // 2 - 1)
    cells = lax.broadcasted_iota(jnp.int32, (tiles + 1, 2 * LANES, 2 * LANES), 1)
    targets = jnp.asarray(targets[:, None, :].astype(np.int32))
    rise_x = sum(
        jnp.where(cells == (targets + t) % (2 * LANES), weights[t], 0.0) for t in range(4)
    )
    ends = jnp.concatenate([weights_y[:, -HALO:], weights_y, weights_y[:, :HALO]], axis=1)
    own = lax.dynamic_slice(ends, (0, lax.axis_index("gy") * tall), (4, tall + 2 * HALO))
    high, steps = TILE + 2 * HALO, tall // TILE
    own = jnp.stack([own[:, k * TILE : k * TILE + high] for k in range(steps)], axis=1)
    cells = lax.broadcasted_iota(jnp.int32, (steps, high, high // 2 + HALO), 2)
    targets = lax.broadcasted_iota(jnp.int32, cells.shape, 1) // 2 + (HALO // 2 - 1)
    rise_y = sum(jnp.where(cells == targets + s, own[s][:, :, None], 0.0) for s in range(4))
    return rise_x, rise_y


def fast_shards(velocity, weights_x, weights_y, acoustic, wall_mask):
    parts, _, tall, wide = acoustic.shape
    _, _, local_y, local_x = velocity.shape
    count_x, count_y = lax.axis_size("gx"), lax.axis_size("gy")
    place_x, place_y = lax.axis_index("gx"), lax.axis_index("gy")
    full, high, steps = wide + LANES, TILE + 2 * HALO, tall // TILE
    strips = (parts + 2) * HALO
    small = 2 * HALO
    has = jnp.stack([place_x > 0, place_x < count_x - 1, place_y > 0, place_y < count_y - 1])
    has = has.astype(F32)
    scalars = pl.BlockSpec(memory_space=pltpu.SMEM)

    def at(block, *index):
        return pl.BlockSpec(block, lambda i: index)

    own = place_x.astype(jnp.int32).reshape(1)
    *sent, first, last = call(
        edges_kernel,
        (own, velocity, acoustic, acoustic, wall_mask, wall_mask),
        (shaped(2, local_y // count_x, local_x),) * count_x + (shaped(strips, wide),) * 2,
        steps=1,
        specs={
            0: scalars,
            2: at((parts, 1, small, wide), 0, 0, 0, 0),
            3: at((parts, 1, small, wide), 0, 0, tall // small - 1, 0),
            4: at((1, HALO, wide), 0, 0, 0),
            5: at((1, HALO, wide), 0, tall // HALO - 1, 0),
        },
        moved=4 << 20,
        megabytes=56,
        name="edges",
    )
    above, below = ring(last, "gy", 1), ring(first, "gy", -1)
    to_right, to_left = call(
        columns_kernel,
        (has, acoustic, acoustic, wall_mask, wall_mask, velocity, velocity, above, below),
        (shaped(strips, tall + LANES), shaped(strips, tall + LANES)),
        steps=1,
        specs={
            0: scalars,
            1: at((parts, 1, tall, LANES), 0, 0, 0, 0),
            2: at((parts, 1, tall, LANES), 0, 0, 0, wide // LANES - 1),
            3: at((1, tall, LANES), 0, 0, 0),
            4: at((1, tall, LANES), 0, 0, wide // LANES - 1),
            5: at((1, 1, local_y, LANES), 1, 0, 0, 0),
            6: at((1, 1, local_y, LANES), 1, 0, 0, local_x // LANES - 1),
        },
        moved=8 << 20,
        megabytes=56,
        name="columns",
    )
    from_left, from_right = ring(to_right, "gx", 1), ring(to_left, "gx", -1)
    sides, flow_side = call(
        sides_kernel,
        (has, from_left, from_right),
        (shaped(parts + 1, tall + LANES, LANES), shaped(local_y + LANES, LANES)),
        steps=1,
        specs={0: scalars},
        moved=8 << 20,
        megabytes=56,
        name="sides",
    )
    across, along = band_tables(high)
    along_inner = along[HALO : HALO + TILE]
    per, rows = TILE // small, TILE // HALO

    def tiled(first):
        walls = (
            pl.BlockSpec((1, TILE, wide), lambda i: (0, i + first, 0)),
            pl.BlockSpec((1, HALO, wide), lambda i: (0, jnp.maximum((i + first) * rows - 1, 0), 0)),
            pl.BlockSpec(
                (1, HALO, wide),
                lambda i: (0, jnp.minimum((i + first + 1) * rows, steps * rows - 1), 0),
            ),
        )
        cells = (
            pl.BlockSpec((parts, 1, TILE, wide), lambda i: (0, 0, i + first, 0)),
            pl.BlockSpec(
                (parts, 1, small, wide), lambda i: (0, 0, jnp.maximum((i + first) * per - 1, 0), 0)
            ),
            pl.BlockSpec(
                (parts, 1, small, wide),
                lambda i: (0, 0, jnp.minimum((i + first + 1) * per, steps * per - 1), 0),
            ),
        )
        return cells, walls, pl.BlockSpec((parts, TILE, wide), lambda i: (0, i + first, 0))

    def quiet_tiles(first, count, before):
        cells, walls, flat = tiled(first)
        operands = (has, acoustic, acoustic, acoustic, wall_mask, wall_mask, wall_mask, above, below, sides)
        operands = operands + (across, along, along_inner)
        return call(
            functools.partial(quiet_step_kernel, first),
            operands,
            (shaped(parts, tall, wide), shaped(8, LANES)),
            steps=count,
            specs=dict(enumerate((scalars,) + cells + walls)),
            out_specs=(flat, pl.BlockSpec((8, LANES), lambda i: (0, 0))),
            after=before,
            aliases={len(operands): 0} if before else None,
            megabytes=56,
            flops=3 * 10**9 * count,
            moved=(12 << 20) * count,
            name="quiet_step",
        )

    early = max(steps * 3 // 4, 1)
    quiet, quiet_done = quiet_tiles(0, early, ())
    if early < steps:
        quiet, _ = quiet_tiles(early, steps - early, (quiet,))
    cells, walls, flat = tiled(0)
    beside_done = from_left[:8, :LANES] + from_right[:8, :LANES]
    rows_done = above[:8, :LANES] + below[:8, :LANES]
    lines = pressure_lines(sent, own, (rows_done,), (beside_done,), (quiet_done,))
    rise_x, rise_y = refine_tables(weights_x, weights_y, tall, wide)
    operands = (has, own, velocity, flow_side, wall_mask, wall_mask, wall_mask, above, below, sides)
    operands = operands + (rise_x, rise_y, quiet, across, along_inner, *lines)
    specs = {
        0: scalars,
        1: scalars,
        2: at((1, 1, local_y, local_x), 1, 0, 0, 0),
        9: at((1, tall + LANES, LANES), parts, 0, 0),
        11: pl.BlockSpec((1,) + rise_y.shape[1:], lambda i: (i, 0, 0)),
        12: flat,
    }
    specs.update({4 + i: spec for i, spec in enumerate(walls)})
    return call(
        source_kernel,
        operands,
        shaped(*acoustic.shape, kind=BF16),
        (
            pltpu.VMEM((2, local_y + 2 * HALO, full), BF16),
            pltpu.VMEM((local_y + 2 * MARGIN, local_x + LANES), F32),
        ),
        steps=steps,
        specs=specs,
        out_specs=cells[0],
        flops=4 * 10**9,
        moved=16 << 20,
        megabytes=56,
        name="source_step",
    )


def fits(count_x, count_y, velocity, acoustic):
    _, planes, local_y, local_x = velocity
    _, _, tall, wide = acoustic
    length_x, length_y = local_x * count_x, local_y * count_y
    rows = local_y // count_x
    base_x, base_y = length_x // RADIX, length_y // RADIX
    return (
        planes == 1
        and length_x * 2 == count_x * count_y * LANES
        and base_x % (2 * LANES) == 0
        and local_x % base_x == 0
        and rows % 8 == 0
        and base_y % rows == 0
        and base_y % 8 == 0
        and MARGIN * 2 % (8 * count_x) == 0
        and tall == 2 * local_y
        and wide == 2 * local_x
        and tall % TILE == 0
        and count_x & (count_x - 1) == 0
        and wide % (2 * LANES) == 0
    )


def extended(array, sides, width):
    for axis, dim in sides:
        size, length = (lax.axis_size(axis), array.shape[dim])
        up = [(i, (i + 1) % size) for i in range(size - 1)]
        down = [(j, i) for i, j in up]
        last = lax.slice_in_dim(array, length - width, length, axis=dim)
        leading = lax.slice_in_dim(array, 0, width, axis=dim)
        before = lax.ppermute(last, axis, up)
        after = lax.ppermute(leading, axis, down)
        array = jnp.concatenate([before, array, after], axis=dim)
    return array


def gradients(padded):
    height = padded.shape[-2] - 6
    breadth = padded.shape[-1] - 6
    rows_mid = padded[..., 3 : 3 + height, :]
    cols_mid = padded[..., :, 3 : 3 + breadth]
    along_x = jnp.zeros_like(padded[..., 3 : 3 + height, 3 : 3 + breadth])
    along_y = jnp.zeros_like(along_x)
    for index, weight in enumerate(stencil_weights):
        distance = index + 1
        along_x = along_x + weight * (
            rows_mid[..., 3 + distance : 3 + distance + breadth]
            - rows_mid[..., 3 - distance : 3 - distance + breadth]
        )
        along_y = along_y + weight * (
            cols_mid[..., 3 + distance : 3 + distance + height, :]
            - cols_mid[..., 3 - distance : 3 - distance + height, :]
        )
    return (along_x, along_y)


def tendency(padded, source):
    along_x, along_y = gradients(padded)
    diverge = along_x[1] + along_y[2]
    forcing = jnp.stack([-diverge, -along_x[3], -along_y[3], source - diverge])
    return forcing - mean_flow * along_x


def spectral_index(flat, length):
    second = length // 16
    wave = flat // second + 16 * (flat % second)
    return jnp.where(wave < length // 2, wave, wave - length).astype(jnp.float32)


def twiddles(rows_count, cols_count, modulus, sign):
    products = jnp.arange(rows_count)[:, None] * jnp.arange(cols_count)[None, :] % modulus
    angles = 2.0 * math.pi / modulus * products.astype(jnp.float32)
    return (jnp.cos(angles), sign * jnp.sin(angles))


def mix_rows(real_part, imag_part, cosine, sine):
    exact = lax.Precision.HIGHEST
    cos_real = jnp.einsum("ka,...ab->...kb", cosine, real_part, precision=exact)
    cos_imag = jnp.einsum("ka,...ab->...kb", cosine, imag_part, precision=exact)
    sin_real = jnp.einsum("ka,...ab->...kb", sine, real_part, precision=exact)
    sin_imag = jnp.einsum("ka,...ab->...kb", sine, imag_part, precision=exact)
    return (cos_real - sin_imag, cos_imag + sin_real)


def mix_cols(real_part, imag_part, cosine, sine):
    exact = lax.Precision.HIGHEST
    cos_real = jnp.einsum("...kb,bc->...kc", real_part, cosine, precision=exact)
    cos_imag = jnp.einsum("...kb,bc->...kc", imag_part, cosine, precision=exact)
    sin_real = jnp.einsum("...kb,bc->...kc", real_part, sine, precision=exact)
    sin_imag = jnp.einsum("...kb,bc->...kc", imag_part, sine, precision=exact)
    return (cos_real - sin_imag, cos_imag + sin_real)


def rotate(real_part, imag_part, cosine, sine):
    return (real_part * cosine - imag_part * sine, real_part * sine + imag_part * cosine)


def discrete(real_part, imag_part, sign):
    length = real_part.shape[-1]
    second = length // 16
    initial = real_part.shape
    folded = initial[:-1] + (16, second)
    real_part = real_part.reshape(folded)
    imag_part = imag_part.reshape(folded)
    small_cos, small_sin = twiddles(16, 16, 16, sign)
    large_cos, large_sin = twiddles(second, second, second, sign)
    turn_cos, turn_sin = twiddles(16, second, length, sign)
    if sign < 0:
        real_part, imag_part = mix_rows(real_part, imag_part, small_cos, small_sin)
        real_part, imag_part = rotate(real_part, imag_part, turn_cos, turn_sin)
        real_part, imag_part = mix_cols(real_part, imag_part, large_cos, large_sin)
    else:
        real_part, imag_part = mix_cols(real_part, imag_part, large_cos, large_sin)
        real_part, imag_part = rotate(real_part, imag_part, turn_cos, turn_sin)
        real_part, imag_part = mix_rows(real_part, imag_part, small_cos, small_sin)
        real_part = real_part / length
        imag_part = imag_part / length
    return (real_part.reshape(initial), imag_part.reshape(initial))


def transform(stacked, sign, kind):
    if kind == "real_in":
        real_part = stacked
        imag_part = jnp.zeros_like(stacked)
    else:
        half = stacked.shape[0] // 2
        real_part = stacked[:half]
        imag_part = stacked[half:]
    real_out, imag_out = discrete(real_part, imag_part, sign)
    if kind == "real_out":
        return real_out
    return jnp.concatenate([real_out, imag_out], axis=0)


def project(stacked, wave_x, wave_y):
    coef_xx = wave_x * wave_x
    coef_xy = 2.0 * wave_x * wave_y
    coef_yy = wave_y * wave_y
    denominator = wave_x * wave_x + wave_y * wave_y
    positive = denominator > 0
    safe = jnp.where(positive, denominator, 1.0)

    def combine(parts):
        numerator = -(coef_xx * parts[0] + coef_xy * parts[1] + coef_yy * parts[2])
        return jnp.where(positive, numerator / safe, 0.0)

    return jnp.stack([combine(stacked[:3]), combine(stacked[3:])])


def refine(stacked, weights):
    result = jnp.zeros(stacked.shape[:-1] + (2 * stacked.shape[-1],), jnp.float32)
    for offset in range(4):
        result = (
            result
            + jnp.repeat(jnp.roll(stacked, 1 - offset, axis=-1), 2, axis=-1) * weights[offset]
        )
    return result


def lines_x(stacked, action):
    gathered = action(lax.all_to_all(stacked, "gx", split_axis=2, concat_axis=3, tiled=True))
    return lax.all_to_all(gathered, "gx", split_axis=3, concat_axis=2, tiled=True)


def lines_y(stacked, action):
    turned = jnp.swapaxes(stacked, 2, 3)
    gathered = action(lax.all_to_all(turned, "gy", split_axis=2, concat_axis=3, tiled=True))
    returned = lax.all_to_all(gathered, "gy", split_axis=3, concat_axis=2, tiled=True)
    return jnp.swapaxes(returned, 2, 3)


def expand(fields):
    return extended(fields, (("gx", 3), ("gy", 2)), 3)


def shards(velocity, weights_x, weights_y, acoustic, wall_mask):
    acoustic = acoustic.astype(jnp.float32)
    flow_x = velocity[0]
    flow_y = velocity[1]
    tensor = jnp.stack([flow_x * flow_x, flow_x * flow_y, flow_y * flow_y])
    count_gx = lax.axis_size("gx")
    count_gy = lax.axis_size("gy")
    place_x = lax.axis_index("gx")
    place_y = lax.axis_index("gy")
    local_y = tensor.shape[2]
    local_x = tensor.shape[3]
    length_x = local_x * count_gx
    length_y = local_y * count_gy

    def forward_real(portion):
        return transform(portion, -1, "real_in")

    def finish_x(portion):
        return refine(transform(portion, 1, "real_out"), weights_x)

    spectra = lines_x(tensor, forward_real)
    share_x = local_x // count_gy
    line_x = spectral_index(place_x * local_x + place_y * share_x + jnp.arange(share_x), length_x)[
        :, None
    ]
    line_y = spectral_index(jnp.arange(length_y), length_y)[None, :]

    def solve_y(portion):
        solved = project(transform(portion, -1, "complex"), line_x, line_y)
        return refine(transform(solved, 1, "complex"), weights_y)

    pressure = lines_y(spectra, solve_y)
    source = lines_x(pressure, finish_x)[0]
    open_cells = (1 - wall_mask).astype(jnp.float32)
    first_rate = tendency(expand(acoustic), source)
    middle = open_cells * (acoustic + time_step * first_rate)
    second_rate = tendency(expand(middle), source)
    return (open_cells * (acoustic + 0.5 * time_step * (first_rate + second_rate))).astype(
        jnp.bfloat16
    )


def solution(mesh):
    in_specs = (P(None, None, "gy", "gx"), P(), P(), P(None, None, "gy", "gx"), P(None, "gy", "gx"))
    out_specs = P(None, None, "gy", "gx")

    def chosen(velocity, weights_x, weights_y, acoustic, wall_mask):
        sizes = (mesh.shape["gx"], mesh.shape["gy"], velocity.shape, acoustic.shape)
        plan = fast_shards if fits(*sizes) else shards
        return plan(velocity, weights_x, weights_y, acoustic, wall_mask)

    return jax.shard_map(
        chosen, mesh=mesh, in_specs=in_specs, out_specs=out_specs, check_vma=False
    )
```

```python
import functools
import math

import jax
import jax.numpy as jnp
import ml_dtypes
import numpy as np
from jax import lax
from jax.experimental import pallas as pl
from jax.experimental.pallas import tpu as pltpu
from jax.sharding import PartitionSpec as P

stencil_weights = (0.75, -0.15, 1.0 / 60.0)
mean_flow = 0.3
time_step = 0.5
whole_weights = (45.0, -9.0, 1.0)

LANES = 128
RADIX = 8
HALO = 8
MARGIN = 16
TILE = 128
ROOT = math.sqrt(0.5)
BF16 = jnp.bfloat16
F32 = jnp.float32


def halves(table):
    high = table.astype(np.float32).astype(ml_dtypes.bfloat16)
    low = (table - high.astype(np.float64)).astype(np.float32).astype(ml_dtypes.bfloat16)
    return high, low


def packed_columns(cosine, sine):
    half = LANES // 2
    parts = []
    for first in range(0, cosine.shape[1], half):
        parts += [cosine[:, first : first + half], sine[:, first : first + half]]
    return np.concatenate(parts, axis=1)


@functools.lru_cache(maxsize=None)
def x_tables(length):
    base = length // RADIX
    m = np.arange(base)[:, None]
    q = np.arange(base)[None, :]
    angle = 2.0 * np.pi * ((m * q) % base) / base
    cosine, sine = np.cos(angle), np.sin(angle)
    full = np.concatenate([packed_columns(cosine, -sine), packed_columns(sine, cosine)], axis=0)
    half = base // 2
    zero_cos, zero_sin = cosine[:, :half].copy(), -sine[:, :half]
    zero_cos[:, 0] = 0.0
    zero_sin = zero_sin.copy()
    zero_sin[:, 0] = (-1.0) ** np.arange(base)
    zero = packed_columns(zero_cos, zero_sin)
    shifted = 2.0 * np.pi * ((m * (RADIX * q[:, :half] + RADIX // 2)) % length) / length
    middle = packed_columns(np.cos(shifted), -np.sin(shifted))
    turns = 2.0 * np.pi * np.arange(1, RADIX // 2)[:, None] * np.arange(base)[None, :] / length
    return full, zero, middle, np.cos(turns), np.sin(turns)


@functools.lru_cache(maxsize=None)
def y_tables(length):
    base = length // RADIX
    index = np.arange(base)
    angle = 2.0 * np.pi * ((index[:, None] * index[None, :]) % base) / base
    both = np.concatenate([np.cos(angle), np.sin(angle)], axis=0)
    turns = 2.0 * np.pi * np.arange(RADIX)[:, None] * index[None, :] / length
    return both, np.concatenate([np.cos(turns), np.sin(turns)], axis=0).T.astype(np.float32)


@functools.lru_cache(maxsize=None)
def wave_table(length, count):
    slots = LANES // 4
    base = length // RADIX
    waves = []
    for residue in (1, 2, 3):
        waves.append(RADIX * np.arange(base) + residue)
    waves.append(RADIX * np.arange(base // 2))
    waves.append(RADIX * np.arange(base // 2) + RADIX // 2)
    waves = np.concatenate(waves)
    waves = np.where(waves == 0, length // 2, waves)
    waves = np.where(waves < length // 2, waves, waves - length).reshape(count, slots)
    return np.tile(waves, (1, 4)).astype(np.float32)


@functools.lru_cache(maxsize=None)
def band_tables(rows):
    across = np.zeros((4 * LANES, 2 * LANES))
    column = np.arange(2 * LANES)
    down = np.zeros((rows, rows))
    for index, weight in enumerate(whole_weights):
        distance = index + 1
        across[column + LANES + distance, column] = weight
        across[column + LANES - distance, column] = -weight
        down += weight * (np.eye(rows, k=distance) - np.eye(rows, k=-distance))
    return across.astype(ml_dtypes.bfloat16), down.astype(ml_dtypes.bfloat16)


def beside(*tables):
    high, low = halves(np.concatenate(tables, axis=1))
    return np.concatenate([high, low], axis=0)


def split(values):
    high = values.astype(BF16)
    return high, (values - high.astype(F32)).astype(BF16)


def dot(left, right):
    return jnp.dot(left, right, preferred_element_type=F32)


def exact_dot(left, right):
    left_high, left_low = left
    right_high, right_low = right
    return dot(left_high, right_high) + (dot(left_low, right_high) + dot(left_high, right_low))


def lane_index(shape):
    return lax.broadcasted_iota(jnp.int32, shape, len(shape) - 1)


def spin(values, shift):
    return pltpu.roll(values, shift % values.shape[-1], values.ndim - 1)


def lane_tile(values, index):
    return values[:, index * LANES : (index + 1) * LANES]


def x_parts(tables, base):
    wide = 2 * base
    full = (tables[:wide], tables[wide : 2 * wide])
    at = 2 * wide
    high, low = tables[at : at + base], tables[at + base : at + 2 * base]
    return full, (high[:, :base], low[:, :base]), (high[:, base:], low[:, base:])


def pieces_kernel(place, velocity, *pieces):
    rows = pieces[0].shape[1]
    for mask, piece in enumerate(pieces):
        start = pl.multiple_of((place[0] ^ mask) * rows, 8)
        for c in range(2):
            piece[c] = velocity[c, 0, pl.ds(start, rows), :]


def rows_kernel(top, low, top_wall, low_wall, top_flow, low_flow, first, last):
    parts, _, small, _ = top.shape
    width = top_flow.shape[3]
    blank = jnp.zeros((HALO, first.shape[1] - width), F32)
    for k in range(parts):
        at = slice(k * HALO, (k + 1) * HALO)
        first[at, :] = top[k, 0].astype(F32)[:HALO]
        last[at, :] = low[k, 0].astype(F32)[small - HALO :]
    at = slice(parts * HALO, (parts + 1) * HALO)
    first[at, :] = 1.0 - top_wall[0].astype(F32)
    last[at, :] = 1.0 - low_wall[0].astype(F32)
    at = slice((parts + 1) * HALO, (parts + 2) * HALO)
    first[at, :width] = top_flow[0, 0]
    last[at, :width] = low_flow[0, 0]
    first[at, width:] = blank
    last[at, width:] = blank


def columns_kernel(
    has, left, right, left_wall, right_wall, left_flow, right_flow, above, below, to_right, to_left
):
    parts = left.shape[0]
    wide, flow_wide = above.shape[1], above.shape[1] // 2
    gap = jnp.zeros((LANES - 2 * HALO, LANES), F32)

    def tall(k, inner, first, sides):
        at = slice(k * HALO, (k + 1) * HALO)
        over, under = above[at, first : first + LANES], below[at, first : first + LANES]
        return jnp.concatenate([inner, under * sides[1], gap, over * sides[0]], axis=0).T

    for k in range(parts + 1):
        at = slice(k * HALO, (k + 1) * HALO)
        if k < parts:
            near, far = left[k, 0].astype(F32), right[k, 0].astype(F32)
        else:
            near, far = 1.0 - left_wall[0].astype(F32), 1.0 - right_wall[0].astype(F32)
        sides = (has[2], has[3])
        to_left[at, :] = tall(k, near, 0, sides)[:HALO]
        to_right[at, :] = tall(k, far, wide - LANES, sides)[LANES - HALO :]
    k = parts + 1
    at = slice(k * HALO, (k + 1) * HALO)
    size = left_flow.shape[2] + LANES
    blank = jnp.zeros((HALO, to_left.shape[1] - size), F32)
    to_left[at, :size] = tall(k, left_flow[0, 0], 0, (1.0, 1.0))[:HALO]
    to_right[at, :size] = tall(k, right_flow[0, 0], flow_wide - LANES, (1.0, 1.0))[LANES - HALO :]
    to_left[at, size:] = blank
    to_right[at, size:] = blank


def sides_kernel(has, velocity, above, below, from_left, from_right, sides, squares):
    parts, tall, _ = sides.shape
    gap = jnp.zeros((LANES - 2 * HALO, tall), F32)
    for k in range(parts):
        at = slice(k * HALO, (k + 1) * HALO)
        tile = [from_right[at, :] * has[1], gap, from_left[at, :] * has[0]]
        sides[k] = jnp.concatenate(tile, axis=0).T
    at = slice(parts * HALO, (parts + 1) * HALO)
    rows, local = velocity.shape[2:]
    size = rows + LANES
    tile = [from_right[at, :size], gap[:, :size], from_left[at, :size]]
    tile = jnp.concatenate(tile, axis=0).T
    tile = tile * tile
    squares[:HALO, :local] = above[at, :local] * above[at, :local]
    squares[HALO : HALO + rows, :local] = velocity[0, 0] * velocity[0, 0]
    squares[HALO + rows :, :local] = below[at, :local] * below[at, :local]
    squares[:HALO, local:] = tile[size - HALO :]
    squares[HALO : HALO + rows, local:] = tile[:rows]
    squares[HALO + rows :, local:] = tile[rows : rows + HALO]


def forward_x_kernel(place, *refs):
    *pieces, tables, turns, out, total, lines = refs
    count, _, rows, local = lines.shape
    for mask, piece in enumerate(pieces):
        lines[place[0] ^ mask] = piece[...]
    base = turns.shape[1]
    per = local // base
    u = [lines[t // per, 0, :, (t % per) * base : (t % per + 1) * base] for t in range(RADIX)]
    v = [lines[t // per, 1, :, (t % per) * base : (t % per + 1) * base] for t in range(RADIX)]
    energy = sum(b * b for b in v)
    energy = jnp.sum(energy.reshape(rows // 8, 8, base), axis=0)
    total[...] = sum(energy[:, k : k + LANES] for k in range(0, base, LANES))
    fields = ([a * a - b * b for a, b in zip(u, v)], [2.0 * a * b for a, b in zip(u, v)])
    zeros, mids, reals, imags = [], [], [[], [], []], [[], [], []]
    for a in fields:
        s04, s26, s15, s37 = a[0] + a[4], a[2] + a[6], a[1] + a[5], a[3] + a[7]
        d04, d26, d15, d37 = a[0] - a[4], a[2] - a[6], a[1] - a[5], a[3] - a[7]
        zeros.append((s04 + s26) + (s15 + s37))
        mids.append((s04 + s26) - (s15 + s37))
        minus, plus = ROOT * (d15 - d37), ROOT * (d15 + d37)
        turned = (
            (d04 + minus, -d26 - plus),
            (s04 - s26, s37 - s15),
            (d04 - minus, d26 - plus),
        )
        for index, (real, imag) in enumerate(turned):
            c, s = turns[index : index + 1, :], turns[index + 3 : index + 4, :]
            reals[index].append(real * c + imag * s)
            imags[index].append(imag * c - real * s)
    stacked = jnp.concatenate(
        [
            jnp.concatenate([jnp.concatenate(reals[i], axis=0) for i in range(3)], axis=0),
            jnp.concatenate([jnp.concatenate(imags[i], axis=0) for i in range(3)], axis=0),
        ],
        axis=1,
    )
    full, zero, middle = x_parts(tables, base)
    full = exact_dot(split(stacked), full)
    zero = exact_dot(split(jnp.concatenate(zeros, axis=0)), zero)
    middle = exact_dot(split(jnp.concatenate(mids, axis=0)), middle)
    low = lane_index((rows, LANES)) % 64 < 32
    target = 0
    blocks = [full[2 * rows * i : 2 * rows * (i + 1)] for i in range(3)] + [zero, middle]
    for block in blocks:
        for first in range(0, block.shape[1], LANES):
            a = block[:rows, first : first + LANES]
            c = block[rows:, first : first + LANES]
            out[target] = jnp.where(low, a, spin(c, 32))
            out[target + 1] = jnp.where(low, spin(a, -32), c)
            target += 2


def eighths(x, turn):
    s04, s26, s15, s37 = x[0] + x[4], x[2] + x[6], x[1] + x[5], x[3] + x[7]
    d04, d26, d15, d37 = x[0] - x[4], x[2] - x[6], x[1] - x[5], x[3] - x[7]
    quarter = turn(s15 - s37)
    spun_26, spun_37 = turn(d26), turn(d37)
    one, three = d15 + spun_37, d15 - spun_37
    spun_one, spun_three = turn(one), turn(three)
    one = ROOT * (one + spun_one)
    three = ROOT * (spun_three - three)
    return [
        (s04 + s26) + (s15 + s37),
        (d04 + spun_26) + one,
        (s04 - s26) + quarter,
        (d04 - spun_26) + three,
        (s04 + s26) - (s15 + s37),
        (d04 + spun_26) - one,
        (s04 - s26) - quarter,
        (d04 - spun_26) - three,
    ]


def solve_y_kernel(count_x, lines, total, wave, both, turns, out, held):
    count, rows, _ = lines.shape
    base = turns.shape[0]
    length = count * rows
    block = count_x * rows
    per = base // rows
    lanes = lane_index((base, LANES))
    sign = jnp.where(lanes < 64, 1.0, -1.0).astype(F32)

    def minus_i(z):
        return spin(z, 64) * sign

    def plus_i(z):
        return spin(z, 64) * -sign

    fields = [
        jnp.concatenate([lines[t * per + k] for k in range(per)], axis=0) for t in range(RADIX)
    ]
    mixed = eighths(fields, minus_i)
    table = turns[...]
    cosines = [table[:, r : r + 1] for r in range(RADIX)]
    sines = [table[:, RADIX + r : RADIX + r + 1] * sign for r in range(RADIX)]
    mixed = [mixed[0]] + [
        mixed[r] * cosines[r] + spin(mixed[r], 64) * sines[r] for r in range(1, RADIX)
    ]
    tables = (both[: 2 * base], both[2 * base :])
    product = exact_dot(tables, split(jnp.concatenate(mixed, axis=1)))
    kx = wave[0:1, :]
    first = lanes % 64 < 32
    edge = jnp.float32(length // 2)
    alone = jnp.where(first, kx * kx, 0.0)
    slope = jnp.where(first | (kx == -edge), 0.0, jnp.broadcast_to(kx, lanes.shape))
    q = lax.broadcasted_iota(jnp.int32, lanes.shape, 0)
    low_ky = RADIX * (q - jnp.where(q < base // 2, 0, base)).astype(F32)
    terms = []
    for r in range(RADIX):
        at = slice(r * LANES, (r + 1) * LANES)
        spectrum = product[:base, at] + minus_i(product[base:, at])
        ky = low_ky + float(r)
        symbol = alone + slope * ky
        if r == 0:
            corner = jnp.where((kx == -edge) & ~first, edge * edge, 0.0)
            symbol = jnp.where(ky == -edge, jnp.where(first, alone, corner), symbol)
        terms.append(symbol * pl.reciprocal(kx * kx + ky * ky) * spectrum)
    pairs = [
        jnp.where(first, low + spin(low, -32), high + spin(high, 32))
        for low, high in zip(terms[:4], terms[4:])
    ]
    product = exact_dot(tables, split(jnp.concatenate(pairs, axis=1)))
    mixed = []
    for r in range(RADIX // 2):
        at = slice(r * LANES, (r + 1) * LANES)
        value = product[:base, at] + plus_i(product[base:, at])
        cosine = jnp.where(first, cosines[r], cosines[r + 4])
        sine = jnp.where(first, sines[r], sines[r + 4])
        value = value * cosine - spin(value, 64) * sine
        value = jnp.where(first, value + spin(value, -32), spin(value, 32) - value)
        if r == 2:
            value = jnp.where(first, value, plus_i(value))
        elif r:
            turned = plus_i(value)
            odd = value + turned if r == 1 else turned - value
            value = jnp.where(first, value, ROOT * odd)
        mixed.append(value)
    even, odd = mixed[0] + mixed[2], mixed[0] - mixed[2]
    side, turned = mixed[1] + mixed[3], plus_i(mixed[1] - mixed[3])
    for t, values in enumerate((even + side, odd + turned, even - side, odd - turned)):
        start = MARGIN + 2 * t * base
        held[start : start + base, :] = values
        held[start + base : start + 2 * base, :] = spin(values, -32)
    held[0:MARGIN, :] = held[length : length + MARGIN, :]
    held[length + MARGIN : length + 2 * MARGIN, :] = held[MARGIN : 2 * MARGIN, :]
    spare = total[...] + spin(total[...], 32)
    kept = rows + 2 * MARGIN // count_x
    half = out.shape[1]
    rest = kept - half
    low = lane_index((8, LANES)) % 64 < 32
    for target in range(count):
        start = (target // count_x) * block + (target % count_x) * kept
        for row in range(0, half, 8):
            a = held[start + row : start + row + 8, :]
            if row < rest:
                b = spin(held[start + half + row : start + half + row + 8, :], 32)
            else:
                b = spare
            out[target, row : row + 8, :] = jnp.where(low, a, b)


def inverse_x_kernel(
    kept, scale, place, lines, tables, turns, *refs
):
    *outs, held = refs
    count, half, _ = lines.shape
    base = turns.shape[1]
    length = RADIX * base
    rest = kept - half
    low = lane_index((half, LANES)) % 64 < 32
    groups, spare = [], None
    for first in range(0, count, 2):
        even, odd = lines[first], lines[first + 1]
        a = jnp.where(low, even, spin(odd, 32))
        b = jnp.where(low, spin(even, -32), odd)
        groups.append(jnp.concatenate([a, b[:rest]], axis=0))
        extra = b[rest : rest + 8]
        spare = extra if spare is None else spare + extra
    mean = jnp.sum(spare) * scale
    wide = 2 * base // LANES
    narrow = base // LANES
    stacked = jnp.concatenate(
        [jnp.concatenate(groups[i * wide : (i + 1) * wide], axis=1) for i in range(3)], axis=0
    )
    at = 3 * wide
    zeros = jnp.concatenate(groups[at : at + narrow], axis=1)
    mids = jnp.concatenate(groups[at + narrow : at + 2 * narrow], axis=1)
    full, zero, middle = x_parts(tables, base)
    full = exact_dot(split(stacked), full)
    zero = exact_dot(split(zeros), zero) * scale
    mid = exact_dot(split(mids), middle) * scale
    turned = []
    for i in range(3):
        real = full[i * kept : (i + 1) * kept, :base]
        imag = full[i * kept : (i + 1) * kept, base:]
        c = turns[i : i + 1, :] * (2.0 * scale)
        s = turns[i + 3 : i + 4, :] * (2.0 * scale)
        turned.append((real * c - imag * s, real * s + imag * c))
    for t in range(RADIX):
        value = zero + mid if t % 2 == 0 else zero - mid
        for i, (real, imag) in enumerate(turned):
            eighth = t * (i + 1) % RADIX
            c = (1.0, ROOT, 0.0, -ROOT, -1.0, -ROOT, 0.0, ROOT)[eighth]
            s = (0.0, ROOT, 1.0, ROOT, 0.0, -ROOT, -1.0, -ROOT)[eighth]
            if c:
                value = value + c * real
            if s:
                value = value - s * imag
        held[:, t * base : (t + 1) * base] = mean - value
    targets, local = len(outs), outs[0].shape[1] - LANES
    right = lane_index((kept, LANES)) < 64
    for mask, out in enumerate(outs):
        start = pl.multiple_of((place[0] ^ mask) * local, LANES)
        after = pl.multiple_of(jnp.where(start + local == length, 0, start + local), LANES)
        before = pl.multiple_of(jnp.where(start == 0, length, start) - LANES, LANES)
        out[:, :local] = held[:, pl.ds(start, local)]
        out[:, local:] = jnp.where(
            right, held[:, pl.ds(after, LANES)], held[:, pl.ds(before, LANES)]
        )


def slopes_x(parts, band, with_edge):
    tiles = parts[0].shape[-1] // LANES
    pieces = []
    for first in list(range(0, tiles - 1, 2)) + ([tiles - 1] if with_edge else []):
        steps = (-1, 0, 1, 2) if first < tiles - 1 else (-1, 0, 1)
        table = band[...] if first < tiles - 1 else band[: 3 * LANES, :LANES]
        order = [(first + step) % tiles for step in steps]
        piece = None
        for part in parts:
            term = dot(jnp.concatenate([lane_tile(part, t) for t in order], axis=1), table)
            piece = term if piece is None else piece + term
        pieces.append(piece)
    return jnp.concatenate(pieces, axis=1)


def edged(k, side, center, up, down, above, below, sides, has, first=0):
    step = pl.program_id(0) + first
    tile, width = center.shape
    tall = sides.shape[1]
    last = (tall - LANES) // tile - 1
    base = pl.multiple_of(step * tile, 8)
    at = slice(k * HALO, (k + 1) * HALO)
    before = pl.multiple_of(jnp.where(step == 0, tall, base) - HALO, 8)
    over = jnp.where(step == 0, above[at, :] * has[2], up)
    under = jnp.where(step == last, below[at, :] * has[3], down)
    rows = (
        (over, sides[side, pl.ds(before, HALO), :]),
        (center, sides[side, pl.ds(base, tile), :]),
        (under, sides[side, pl.ds(pl.multiple_of(base + tile, 8), HALO), :]),
    )
    return jnp.concatenate([jnp.concatenate(pair, axis=1) for pair in rows], axis=0)


def edged_open(k, side, wall, wall_up, wall_down, above, below, sides, has, first=0):
    open_cells = [1.0 - ref[0].astype(F32) for ref in (wall, wall_up, wall_down)]
    return edged(k, side, *open_cells, above, below, sides, has, first)


def quiet_step_kernel(
    first, has, center, up, down, wall, wall_up, wall_down, above, below, sides, across, along, along_inner, out, shown_open
):
    parts, _, tile, width = center.shape
    high = tile + 2 * HALO
    opened = edged_open(parts, parts, wall, wall_up, wall_down, above, below, sides, has, first)
    values = []
    for k in range(parts):
        value = edged(
            k,
            k,
            center[k, 0].astype(F32),
            up[k, 0].astype(F32)[up.shape[2] - HALO :],
            down[k, 0].astype(F32)[:HALO],
            above,
            below,
            sides,
            has,
            first,
        )
        values.append(value)

    def drops(x, along_b, along_p):
        diverge = x[1] + along_b
        return (
            diverge + mean_flow * x[0],
            x[3] + mean_flow * x[1],
            along_p + mean_flow * x[2],
            diverge + mean_flow * x[3],
        )

    short = [value.astype(BF16) for value in values]
    x = slopes_x((jnp.concatenate(short, axis=0),), across, True)
    x = [x[k * high : (k + 1) * high] for k in range(parts)]
    table = along[...]
    dropped = drops(x, dot(table, short[2]), dot(table, short[3]))
    middle = [opened * (v - (time_step / 60.0) * d) for v, d in zip(values, dropped)]
    inner = slice(HALO, HALO + tile)
    x = slopes_x(split(jnp.concatenate([value[inner] for value in middle], axis=0)), across, False)
    x = [x[k * tile : (k + 1) * tile] for k in range(parts)]
    table = along_inner[...]
    y = [sum(dot(table, part) for part in split(middle[k][:, :width])) for k in (2, 3)]
    dropped = drops(x, *y)
    shown = opened[inner, :width]
    for k in range(parts):
        start = 0.5 * values[k][inner, :width] - (0.5 * time_step / 60.0) * dropped[k]
        out[k] = shown * start + 0.5 * middle[k][inner, :width]
    shown_open[0] = opened.astype(BF16)


def source_kernel(place, squares, opened, rise_x, rise_y, quiet, across, along_inner, *refs):
    *lines, out, raised, held = refs
    step = pl.program_id(0)
    _, tile, width = quiet.shape

    @pl.when(step == 0)
    def _():
        kept = lines[0].shape[0]
        for mask, piece in enumerate(lines):
            held[pl.ds(pl.multiple_of((place[0] ^ mask) * kept, 8), kept), :] = piece[...]
        level = held[MARGIN - HALO : MARGIN - HALO + squares.shape[0], :] - squares[...]
        cells = level.shape[1] // LANES
        near = lane_index((level.shape[0], LANES)) < 64
        for k in range(cells):
            after, before = lane_tile(level, (k + 1) % cells), lane_tile(level, (k - 1) % cells)
            around = jnp.concatenate([lane_tile(level, k), jnp.where(near, after, before)], axis=1)
            lanes = 2 * LANES if k < cells - 1 else LANES
            value = split(exact_dot(split(around), split(rise_x[k][:, :lanes])))
            for part in range(2):
                raised[part, :, 2 * k * LANES : 2 * k * LANES + lanes] = value[part]

    start = pl.multiple_of(step * (tile // 2), 16)
    window = [raised[part, pl.ds(start, rise_y.shape[2]), :] for part in range(2)]
    free = time_step * opened[0].astype(F32)
    forced = free * exact_dot(split(rise_y[0]), window)
    inner = slice(HALO, HALO + tile)
    shown = (0.5 / 60.0) * free[inner, :width]
    x = shown * slopes_x(split(forced[inner]), across, False)
    table = along_inner[...]
    y = sum(dot(table, part) for part in split(forced[:, :width]))
    out[0, 0] = quiet[0].astype(out.dtype)
    out[1, 0] = (quiet[1] - x).astype(out.dtype)
    out[2, 0] = (quiet[2] - shown * y).astype(out.dtype)
    out[3, 0] = (quiet[3] + forced[inner, :width] - mean_flow * x).astype(out.dtype)


def call(
    kernel, operands, outs, scratch=(), steps=0, specs=None, out_specs=None, after=(), aliases=None, megabytes=24, flops=0, moved=0, name=None
):
    count = len(operands)

    def body(*refs):
        kernel(*refs[:count], *refs[count + len(after) :])

    def whole(array):
        zeros = (0,) * len(array.shape)
        return pl.BlockSpec(array.shape, lambda *_: zeros)

    arguments = {}
    chosen = specs or {}
    if steps:
        arguments["grid"] = (steps,)
        in_specs = [chosen.get(i, whole(o)) for i, o in enumerate(operands)]
        arguments["out_specs"] = jax.tree.map(whole, outs) if out_specs is None else out_specs
    else:
        local = pl.BlockSpec(memory_space=pltpu.VMEM)
        in_specs = [chosen.get(i, local) for i in range(count)]
    return pl.pallas_call(
        body,
        out_shape=outs,
        in_specs=in_specs + [pl.BlockSpec(memory_space=pl.ANY)] * len(after),
        scratch_shapes=list(scratch),
        input_output_aliases=aliases or {},
        compiler_params=pltpu.CompilerParams(vmem_limit_bytes=megabytes << 20),
        cost_estimate=pl.CostEstimate(flops=flops, bytes_accessed=moved, transcendentals=0),
        name=name,
        **arguments,
    )(*operands, *after)


def ring(array, axis, step):
    size = lax.axis_size(axis)
    return lax.ppermute(array, axis, [(i, (i + step) % size) for i in range(size)])


def swap(array, axis, mask):
    return lax.ppermute(array, axis, [(i, i ^ mask) for i in range(lax.axis_size(axis))])


def shaped(*shape, kind=F32):
    return jax.ShapeDtypeStruct(shape, kind)


def pressure_lines(pieces, place_x, gathered, spread, stepped):
    _, rows, local_x = pieces[0].shape
    count_x, count_y = lax.axis_size("gx"), lax.axis_size("gy")
    count = count_x * count_y
    scalars = {0: pl.BlockSpec(memory_space=pltpu.SMEM)}
    length_x, length_y = local_x * count_x, rows * count
    full, zero, middle, cos_turn, sin_turn = x_tables(length_x)
    turns = np.zeros((8, cos_turn.shape[1]), np.float32)
    turns[0:3], turns[3:6] = cos_turn, sin_turn
    spectra, total = call(
        forward_x_kernel,
        (place_x, *pieces, np.concatenate([beside(full), beside(zero, middle)]), turns),
        (shaped(count, rows, LANES), shaped(8, LANES)),
        (pltpu.VMEM((count_x, 2, rows, local_x), F32),),
        specs=scalars,
        after=gathered,
        flops=10**9,
        moved=4 << 20,
        name="forward_x",
    )
    spectra = lax.all_to_all(spectra, ("gy", "gx"), 0, 0, tiled=True)
    place = lax.axis_index("gy") * count_x + lax.axis_index("gx")
    waves = jnp.asarray(wave_table(length_x, count))
    wave = lax.dynamic_slice(waves, (place, 0), (1, LANES))
    both, turns_y = y_tables(length_y)
    kept = rows + 2 * MARGIN // count_x
    half = (kept // 2 + 8) // 8 * 8
    solved = call(
        functools.partial(solve_y_kernel, count_x),
        (spectra, total, wave, beside(both), turns_y),
        shaped(count, half, LANES),
        (pltpu.VMEM((length_y + 2 * MARGIN, LANES), F32),),
        after=spread,
        megabytes=57,
        flops=4 * 10**9,
        moved=6 << 20,
        name="solve_y",
    )
    solved = lax.all_to_all(solved, ("gy", "gx"), 0, 0, tiled=True)
    back = 2.0 * zero.T
    back[LANES // 2] *= 0.5
    tables = np.concatenate(
        [beside(full.T), beside(back, 2.0 * middle.T)]
    )
    pressed = call(
        functools.partial(inverse_x_kernel, kept, 1.0 / (length_x * length_y)),
        (place_x, solved, tables, turns),
        (shaped(kept, local_x + LANES),) * count_x,
        (pltpu.VMEM((kept, length_x), F32),),
        specs=scalars,
        after=stepped,
        megabytes=57,
        flops=10**9,
        moved=4 << 20,
        name="inverse_x",
    )
    return [piece if mask == 0 else swap(piece, "gx", mask) for mask, piece in enumerate(pressed)]


def refine_tables(weights_x, weights_y, tall, wide):
    first = lax.axis_index("gx") * wide
    ends = jnp.concatenate([weights_x[:, -LANES:], weights_x, weights_x[:, :LANES]], axis=1)
    own = lax.dynamic_slice(ends, (0, first), (4, wide + 2 * LANES))
    half = LANES // 2
    edge = jnp.concatenate([own[:, wide + LANES : wide + LANES + half], own[:, half:LANES]], axis=1)
    edge = jnp.pad(edge, ((0, 0), (0, LANES)))
    tiles = wide // (2 * LANES)
    weights = jnp.concatenate([own[:, LANES : wide + LANES], edge], axis=1)
    weights = weights.reshape(4, tiles + 1, 1, 2 * LANES)
    fine = np.arange(2 * LANES)
    targets = np.tile(fine // 2 - 1, (tiles + 1, 1))
    targets[tiles] = np.where(fine < half, fine // 2 - 1, half + fine // 2 - 1)
    cells = lax.broadcasted_iota(jnp.int32, (tiles + 1, 2 * LANES, 2 * LANES), 1)
    targets = jnp.asarray(targets[:, None, :].astype(np.int32))
    rise_x = sum(
        jnp.where(cells == (targets + t) % (2 * LANES), weights[t], 0.0) for t in range(4)
    )
    ends = jnp.concatenate([weights_y[:, -HALO:], weights_y, weights_y[:, :HALO]], axis=1)
    own = lax.dynamic_slice(ends, (0, lax.axis_index("gy") * tall), (4, tall + 2 * HALO))
    high, steps = TILE + 2 * HALO, tall // TILE
    own = jnp.stack([own[:, k * TILE : k * TILE + high] for k in range(steps)], axis=1)
    cells = lax.broadcasted_iota(jnp.int32, (steps, high, high // 2 + HALO), 2)
    targets = lax.broadcasted_iota(jnp.int32, cells.shape, 1) // 2 + (HALO // 2 - 1)
    rise_y = sum(jnp.where(cells == targets + s, own[s][:, :, None], 0.0) for s in range(4))
    return rise_x, rise_y


def fast_shards(velocity, weights_x, weights_y, acoustic, wall_mask):
    parts, _, tall, wide = acoustic.shape
    _, _, local_y, local_x = velocity.shape
    count_x, count_y = lax.axis_size("gx"), lax.axis_size("gy")
    place_x, place_y = lax.axis_index("gx"), lax.axis_index("gy")
    full, high, steps = wide + LANES, TILE + 2 * HALO, tall // TILE
    strips = (parts + 2) * HALO
    small = 2 * HALO
    has = jnp.stack([place_x > 0, place_x < count_x - 1, place_y > 0, place_y < count_y - 1])
    has = has.astype(F32)
    scalars = pl.BlockSpec(memory_space=pltpu.SMEM)

    def at(block, *index):
        return pl.BlockSpec(block, lambda i: index)

    own = place_x.astype(jnp.int32).reshape(1)
    sent = call(
        pieces_kernel,
        (own, velocity),
        (shaped(2, local_y // count_x, local_x),) * count_x,
        specs={0: scalars},
        moved=2 << 20,
        megabytes=8,
        name="pieces",
    )
    moved = [piece if mask == 0 else swap(piece, "gx", mask) for mask, piece in enumerate(sent)]
    first, last = call(
        rows_kernel,
        (acoustic, acoustic, wall_mask, wall_mask, velocity, velocity),
        (shaped(strips, wide),) * 2,
        steps=1,
        specs={
            0: at((parts, 1, small, wide), 0, 0, 0, 0),
            1: at((parts, 1, small, wide), 0, 0, tall // small - 1, 0),
            2: at((1, HALO, wide), 0, 0, 0),
            3: at((1, HALO, wide), 0, tall // HALO - 1, 0),
            4: at((1, 1, HALO, local_x), 1, 0, 0, 0),
            5: at((1, 1, HALO, local_x), 1, 0, local_y // HALO - 1, 0),
        },
        after=moved[1:2],
        moved=2 << 20,
        megabytes=56,
        name="rows",
    )
    above, below = ring(last, "gy", 1), ring(first, "gy", -1)
    to_right, to_left = call(
        columns_kernel,
        (has, acoustic, acoustic, wall_mask, wall_mask, velocity, velocity, above, below),
        (shaped(strips, tall + LANES), shaped(strips, tall + LANES)),
        steps=1,
        specs={
            0: scalars,
            1: at((parts, 1, tall, LANES), 0, 0, 0, 0),
            2: at((parts, 1, tall, LANES), 0, 0, 0, wide // LANES - 1),
            3: at((1, tall, LANES), 0, 0, 0),
            4: at((1, tall, LANES), 0, 0, wide // LANES - 1),
            5: at((1, 1, local_y, LANES), 1, 0, 0, 0),
            6: at((1, 1, local_y, LANES), 1, 0, 0, local_x // LANES - 1),
        },
        moved=8 << 20,
        megabytes=56,
        name="columns",
    )
    from_left, from_right = ring(to_right, "gx", 1), ring(to_left, "gx", -1)
    sides, squares = call(
        sides_kernel,
        (has, velocity, above, below, from_left, from_right),
        (shaped(parts + 1, tall + LANES, LANES), shaped(local_y + 2 * HALO, local_x + LANES)),
        steps=1,
        specs={0: scalars, 1: at((1, 1, local_y, local_x), 1, 0, 0, 0)},
        moved=8 << 20,
        megabytes=56,
        name="sides",
    )
    across, along = band_tables(high)
    along_inner = along[HALO : HALO + TILE]
    per, rows = TILE // small, TILE // HALO

    def tiled(first):
        walls = (
            pl.BlockSpec((1, TILE, wide), lambda i: (0, i + first, 0)),
            pl.BlockSpec((1, HALO, wide), lambda i: (0, jnp.maximum((i + first) * rows - 1, 0), 0)),
            pl.BlockSpec(
                (1, HALO, wide),
                lambda i: (0, jnp.minimum((i + first + 1) * rows, steps * rows - 1), 0),
            ),
        )
        cells = (
            pl.BlockSpec((parts, 1, TILE, wide), lambda i: (0, 0, i + first, 0)),
            pl.BlockSpec(
                (parts, 1, small, wide), lambda i: (0, 0, jnp.maximum((i + first) * per - 1, 0), 0)
            ),
            pl.BlockSpec(
                (parts, 1, small, wide),
                lambda i: (0, 0, jnp.minimum((i + first + 1) * per, steps * per - 1), 0),
            ),
        )
        return cells, walls, pl.BlockSpec((parts, TILE, wide), lambda i: (0, i + first, 0))

    def quiet_tiles(first, count, before):
        cells, walls, flat = tiled(first)
        operands = (has, acoustic, acoustic, acoustic, wall_mask, wall_mask, wall_mask, above, below, sides)
        operands = operands + (across, along, along_inner)
        return call(
            functools.partial(quiet_step_kernel, first),
            operands,
            (shaped(parts, tall, wide), shaped(steps, high, full, kind=BF16)),
            steps=count,
            specs=dict(enumerate((scalars,) + cells + walls)),
            out_specs=(flat, pl.BlockSpec((1, high, full), lambda i: (i + first, 0, 0))),
            after=before,
            aliases={len(operands): 0, len(operands) + 1: 1} if before else None,
            megabytes=56,
            flops=3 * 10**9 * count,
            moved=(12 << 20) * count,
            name="quiet_step",
        )

    early = (steps + 1) // 2
    begun = quiet_tiles(0, early, ())
    ready = quiet_tiles(early, steps - early, begun) if early < steps else begun
    cells, walls, flat = tiled(0)
    rows_done = above[:8, :LANES] + below[:8, :LANES]
    lines = pressure_lines(moved, own, (rows_done,), begun[:1], ready[:1])
    rise_x, rise_y = refine_tables(weights_x, weights_y, tall, wide)
    quiet, opened = ready
    operands = (own, squares, opened, rise_x, rise_y, quiet, across, along_inner, *lines)
    specs = {
        0: scalars,
        2: pl.BlockSpec((1, high, full), lambda i: (i, 0, 0)),
        4: pl.BlockSpec((1,) + rise_y.shape[1:], lambda i: (i, 0, 0)),
        5: flat,
    }
    return call(
        source_kernel,
        operands,
        shaped(*acoustic.shape, kind=BF16),
        (
            pltpu.VMEM((2, local_y + 2 * HALO, full), BF16),
            pltpu.VMEM((local_y + 2 * MARGIN, local_x + LANES), F32),
        ),
        steps=steps,
        specs=specs,
        out_specs=cells[0],
        flops=4 * 10**9,
        moved=16 << 20,
        megabytes=56,
        name="source_step",
    )


def fits(count_x, count_y, velocity, acoustic):
    _, planes, local_y, local_x = velocity
    _, _, tall, wide = acoustic
    length_x, length_y = local_x * count_x, local_y * count_y
    rows = local_y // count_x
    base_x, base_y = length_x // RADIX, length_y // RADIX
    return (
        planes == 1
        and length_x * 2 == count_x * count_y * LANES
        and base_x % (2 * LANES) == 0
        and local_x % base_x == 0
        and rows % 8 == 0
        and base_y % rows == 0
        and base_y % 8 == 0
        and MARGIN * 2 % (8 * count_x) == 0
        and tall == 2 * local_y
        and wide == 2 * local_x
        and tall % TILE == 0
        and count_x & (count_x - 1) == 0
        and wide % (2 * LANES) == 0
    )


def extended(array, sides, width):
    for axis, dim in sides:
        size, length = (lax.axis_size(axis), array.shape[dim])
        up = [(i, (i + 1) % size) for i in range(size - 1)]
        down = [(j, i) for i, j in up]
        last = lax.slice_in_dim(array, length - width, length, axis=dim)
        leading = lax.slice_in_dim(array, 0, width, axis=dim)
        before = lax.ppermute(last, axis, up)
        after = lax.ppermute(leading, axis, down)
        array = jnp.concatenate([before, array, after], axis=dim)
    return array


def gradients(padded):
    height = padded.shape[-2] - 6
    breadth = padded.shape[-1] - 6
    rows_mid = padded[..., 3 : 3 + height, :]
    cols_mid = padded[..., :, 3 : 3 + breadth]
    along_x = jnp.zeros_like(padded[..., 3 : 3 + height, 3 : 3 + breadth])
    along_y = jnp.zeros_like(along_x)
    for index, weight in enumerate(stencil_weights):
        distance = index + 1
        along_x = along_x + weight * (
            rows_mid[..., 3 + distance : 3 + distance + breadth]
            - rows_mid[..., 3 - distance : 3 - distance + breadth]
        )
        along_y = along_y + weight * (
            cols_mid[..., 3 + distance : 3 + distance + height, :]
            - cols_mid[..., 3 - distance : 3 - distance + height, :]
        )
    return (along_x, along_y)


def tendency(padded, source):
    along_x, along_y = gradients(padded)
    diverge = along_x[1] + along_y[2]
    forcing = jnp.stack([-diverge, -along_x[3], -along_y[3], source - diverge])
    return forcing - mean_flow * along_x


def spectral_index(flat, length):
    second = length // 16
    wave = flat // second + 16 * (flat % second)
    return jnp.where(wave < length // 2, wave, wave - length).astype(jnp.float32)


def twiddles(rows_count, cols_count, modulus, sign):
    products = jnp.arange(rows_count)[:, None] * jnp.arange(cols_count)[None, :] % modulus
    angles = 2.0 * math.pi / modulus * products.astype(jnp.float32)
    return (jnp.cos(angles), sign * jnp.sin(angles))


def mix_rows(real_part, imag_part, cosine, sine):
    exact = lax.Precision.HIGHEST
    cos_real = jnp.einsum("ka,...ab->...kb", cosine, real_part, precision=exact)
    cos_imag = jnp.einsum("ka,...ab->...kb", cosine, imag_part, precision=exact)
    sin_real = jnp.einsum("ka,...ab->...kb", sine, real_part, precision=exact)
    sin_imag = jnp.einsum("ka,...ab->...kb", sine, imag_part, precision=exact)
    return (cos_real - sin_imag, cos_imag + sin_real)


def mix_cols(real_part, imag_part, cosine, sine):
    exact = lax.Precision.HIGHEST
    cos_real = jnp.einsum("...kb,bc->...kc", real_part, cosine, precision=exact)
    cos_imag = jnp.einsum("...kb,bc->...kc", imag_part, cosine, precision=exact)
    sin_real = jnp.einsum("...kb,bc->...kc", real_part, sine, precision=exact)
    sin_imag = jnp.einsum("...kb,bc->...kc", imag_part, sine, precision=exact)
    return (cos_real - sin_imag, cos_imag + sin_real)


def rotate(real_part, imag_part, cosine, sine):
    return (real_part * cosine - imag_part * sine, real_part * sine + imag_part * cosine)


def discrete(real_part, imag_part, sign):
    length = real_part.shape[-1]
    second = length // 16
    initial = real_part.shape
    folded = initial[:-1] + (16, second)
    real_part = real_part.reshape(folded)
    imag_part = imag_part.reshape(folded)
    small_cos, small_sin = twiddles(16, 16, 16, sign)
    large_cos, large_sin = twiddles(second, second, second, sign)
    turn_cos, turn_sin = twiddles(16, second, length, sign)
    if sign < 0:
        real_part, imag_part = mix_rows(real_part, imag_part, small_cos, small_sin)
        real_part, imag_part = rotate(real_part, imag_part, turn_cos, turn_sin)
        real_part, imag_part = mix_cols(real_part, imag_part, large_cos, large_sin)
    else:
        real_part, imag_part = mix_cols(real_part, imag_part, large_cos, large_sin)
        real_part, imag_part = rotate(real_part, imag_part, turn_cos, turn_sin)
        real_part, imag_part = mix_rows(real_part, imag_part, small_cos, small_sin)
        real_part = real_part / length
        imag_part = imag_part / length
    return (real_part.reshape(initial), imag_part.reshape(initial))


def transform(stacked, sign, kind):
    if kind == "real_in":
        real_part = stacked
        imag_part = jnp.zeros_like(stacked)
    else:
        half = stacked.shape[0] // 2
        real_part = stacked[:half]
        imag_part = stacked[half:]
    real_out, imag_out = discrete(real_part, imag_part, sign)
    if kind == "real_out":
        return real_out
    return jnp.concatenate([real_out, imag_out], axis=0)


def project(stacked, wave_x, wave_y):
    coef_xx = wave_x * wave_x
    coef_xy = 2.0 * wave_x * wave_y
    coef_yy = wave_y * wave_y
    denominator = wave_x * wave_x + wave_y * wave_y
    positive = denominator > 0
    safe = jnp.where(positive, denominator, 1.0)

    def combine(parts):
        numerator = -(coef_xx * parts[0] + coef_xy * parts[1] + coef_yy * parts[2])
        return jnp.where(positive, numerator / safe, 0.0)

    return jnp.stack([combine(stacked[:3]), combine(stacked[3:])])


def refine(stacked, weights):
    result = jnp.zeros(stacked.shape[:-1] + (2 * stacked.shape[-1],), jnp.float32)
    for offset in range(4):
        result = (
            result
            + jnp.repeat(jnp.roll(stacked, 1 - offset, axis=-1), 2, axis=-1) * weights[offset]
        )
    return result


def lines_x(stacked, action):
    gathered = action(lax.all_to_all(stacked, "gx", split_axis=2, concat_axis=3, tiled=True))
    return lax.all_to_all(gathered, "gx", split_axis=3, concat_axis=2, tiled=True)


def lines_y(stacked, action):
    turned = jnp.swapaxes(stacked, 2, 3)
    gathered = action(lax.all_to_all(turned, "gy", split_axis=2, concat_axis=3, tiled=True))
    returned = lax.all_to_all(gathered, "gy", split_axis=3, concat_axis=2, tiled=True)
    return jnp.swapaxes(returned, 2, 3)


def expand(fields):
    return extended(fields, (("gx", 3), ("gy", 2)), 3)


def shards(velocity, weights_x, weights_y, acoustic, wall_mask):
    acoustic = acoustic.astype(jnp.float32)
    flow_x = velocity[0]
    flow_y = velocity[1]
    tensor = jnp.stack([flow_x * flow_x, flow_x * flow_y, flow_y * flow_y])
    count_gx = lax.axis_size("gx")
    count_gy = lax.axis_size("gy")
    place_x = lax.axis_index("gx")
    place_y = lax.axis_index("gy")
    local_y = tensor.shape[2]
    local_x = tensor.shape[3]
    length_x = local_x * count_gx
    length_y = local_y * count_gy

    def forward_real(portion):
        return transform(portion, -1, "real_in")

    def finish_x(portion):
        return refine(transform(portion, 1, "real_out"), weights_x)

    spectra = lines_x(tensor, forward_real)
    share_x = local_x // count_gy
    line_x = spectral_index(place_x * local_x + place_y * share_x + jnp.arange(share_x), length_x)[
        :, None
    ]
    line_y = spectral_index(jnp.arange(length_y), length_y)[None, :]

    def solve_y(portion):
        solved = project(transform(portion, -1, "complex"), line_x, line_y)
        return refine(transform(solved, 1, "complex"), weights_y)

    pressure = lines_y(spectra, solve_y)
    source = lines_x(pressure, finish_x)[0]
    open_cells = (1 - wall_mask).astype(jnp.float32)
    first_rate = tendency(expand(acoustic), source)
    middle = open_cells * (acoustic + time_step * first_rate)
    second_rate = tendency(expand(middle), source)
    return (open_cells * (acoustic + 0.5 * time_step * (first_rate + second_rate))).astype(
        jnp.bfloat16
    )


def solution(mesh):
    in_specs = (P(None, None, "gy", "gx"), P(), P(), P(None, None, "gy", "gx"), P(None, "gy", "gx"))
    out_specs = P(None, None, "gy", "gx")

    def chosen(velocity, weights_x, weights_y, acoustic, wall_mask):
        sizes = (mesh.shape["gx"], mesh.shape["gy"], velocity.shape, acoustic.shape)
        plan = fast_shards if fits(*sizes) else shards
        return plan(velocity, weights_x, weights_y, acoustic, wall_mask)

    return jax.shard_map(
        chosen, mesh=mesh, in_specs=in_specs, out_specs=out_specs, check_vma=False
    )
```

```python
import functools
import math

import jax
import jax.numpy as jnp
import ml_dtypes
import numpy as np
from jax import lax
from jax.experimental import pallas as pl
from jax.experimental.pallas import tpu as pltpu
from jax.sharding import PartitionSpec as P

stencil_weights = (0.75, -0.15, 1.0 / 60.0)
mean_flow = 0.3
time_step = 0.5
whole_weights = (45.0, -9.0, 1.0)

LANES = 128
RADIX = 8
HALO = 8
MARGIN = 16
TILE = 128
ROOT = math.sqrt(0.5)
BF16 = jnp.bfloat16
F32 = jnp.float32


def halves(table):
    high = table.astype(np.float32).astype(ml_dtypes.bfloat16)
    low = (table - high.astype(np.float64)).astype(np.float32).astype(ml_dtypes.bfloat16)
    return high, low


def packed_columns(cosine, sine):
    half = LANES // 2
    parts = []
    for first in range(0, cosine.shape[1], half):
        parts += [cosine[:, first : first + half], sine[:, first : first + half]]
    return np.concatenate(parts, axis=1)


@functools.lru_cache(maxsize=None)
def x_tables(length):
    base = length // RADIX
    m = np.arange(base)[:, None]
    q = np.arange(base)[None, :]
    angle = 2.0 * np.pi * ((m * q) % base) / base
    cosine, sine = np.cos(angle), np.sin(angle)
    full = np.concatenate([packed_columns(cosine, -sine), packed_columns(sine, cosine)], axis=0)
    half = base // 2
    zero_cos, zero_sin = cosine[:, :half].copy(), -sine[:, :half]
    zero_cos[:, 0] = 0.0
    zero_sin = zero_sin.copy()
    zero_sin[:, 0] = (-1.0) ** np.arange(base)
    zero = packed_columns(zero_cos, zero_sin)
    shifted = 2.0 * np.pi * ((m * (RADIX * q[:, :half] + RADIX // 2)) % length) / length
    middle = packed_columns(np.cos(shifted), -np.sin(shifted))
    turns = 2.0 * np.pi * np.arange(1, RADIX // 2)[:, None] * np.arange(base)[None, :] / length
    return full, zero, middle, np.cos(turns), np.sin(turns)


@functools.lru_cache(maxsize=None)
def y_tables(length):
    base = length // RADIX
    index = np.arange(base)
    angle = 2.0 * np.pi * ((index[:, None] * index[None, :]) % base) / base
    both = np.concatenate([np.cos(angle), np.sin(angle)], axis=0)
    turns = 2.0 * np.pi * np.arange(RADIX)[:, None] * index[None, :] / length
    return both, np.concatenate([np.cos(turns), np.sin(turns)], axis=0).T.astype(np.float32)


@functools.lru_cache(maxsize=None)
def wave_table(length, count):
    slots = LANES // 4
    base = length // RADIX
    waves = []
    for residue in (1, 2, 3):
        waves.append(RADIX * np.arange(base) + residue)
    waves.append(RADIX * np.arange(base // 2))
    waves.append(RADIX * np.arange(base // 2) + RADIX // 2)
    waves = np.concatenate(waves)
    waves = np.where(waves == 0, length // 2, waves)
    waves = np.where(waves < length // 2, waves, waves - length).reshape(count, slots)
    return np.tile(waves, (1, 4)).astype(np.float32)


@functools.lru_cache(maxsize=None)
def band_tables(rows):
    across = np.zeros((4 * LANES, 2 * LANES))
    column = np.arange(2 * LANES)
    down = np.zeros((rows, rows))
    for index, weight in enumerate(whole_weights):
        distance = index + 1
        across[column + LANES + distance, column] = weight
        across[column + LANES - distance, column] = -weight
        down += weight * (np.eye(rows, k=distance) - np.eye(rows, k=-distance))
    return across.astype(ml_dtypes.bfloat16), down.astype(ml_dtypes.bfloat16)


def beside(*tables):
    high, low = halves(np.concatenate(tables, axis=1))
    return np.concatenate([high, low], axis=0)


def split(values):
    high = values.astype(BF16)
    return high, (values - high.astype(F32)).astype(BF16)


def dot(left, right):
    return jnp.dot(left, right, preferred_element_type=F32)


def exact_dot(left, right):
    left_high, left_low = left
    right_high, right_low = right
    return dot(left_high, right_high) + (dot(left_low, right_high) + dot(left_high, right_low))


def lane_index(shape):
    return lax.broadcasted_iota(jnp.int32, shape, len(shape) - 1)


def spin(values, shift):
    return pltpu.roll(values, shift % values.shape[-1], values.ndim - 1)


def lane_tile(values, index):
    return values[:, index * LANES : (index + 1) * LANES]


def x_parts(tables, base):
    wide = 2 * base
    full = (tables[:wide], tables[wide : 2 * wide])
    at = 2 * wide
    high, low = tables[at : at + base], tables[at + base : at + 2 * base]
    return full, (high[:, :base], low[:, :base]), (high[:, base:], low[:, base:])


def pieces_kernel(place, velocity, *pieces):
    rows = pieces[0].shape[1]
    for mask, piece in enumerate(pieces):
        start = pl.multiple_of((place[0] ^ mask) * rows, 8)
        for c in range(2):
            piece[c] = velocity[c, 0, pl.ds(start, rows), :]


def rows_kernel(top, low, top_wall, low_wall, top_flow, low_flow, first, last):
    parts, _, small, _ = top.shape
    width = top_flow.shape[3]
    blank = jnp.zeros((HALO, first.shape[1] - width), F32)
    for k in range(parts):
        at = slice(k * HALO, (k + 1) * HALO)
        first[at, :] = top[k, 0].astype(F32)[:HALO]
        last[at, :] = low[k, 0].astype(F32)[small - HALO :]
    at = slice(parts * HALO, (parts + 1) * HALO)
    first[at, :] = 1.0 - top_wall[0].astype(F32)
    last[at, :] = 1.0 - low_wall[0].astype(F32)
    at = slice((parts + 1) * HALO, (parts + 2) * HALO)
    first[at, :width] = top_flow[0, 0]
    last[at, :width] = low_flow[0, 0]
    first[at, width:] = blank
    last[at, width:] = blank


def columns_kernel(
    has, left, right, left_wall, right_wall, left_flow, right_flow, above, below, to_right, to_left
):
    parts = left.shape[0]
    wide, flow_wide = above.shape[1], above.shape[1] // 2
    gap = jnp.zeros((LANES - 2 * HALO, LANES), F32)

    def tall(k, inner, first, sides):
        at = slice(k * HALO, (k + 1) * HALO)
        over, under = above[at, first : first + LANES], below[at, first : first + LANES]
        return jnp.concatenate([inner, under * sides[1], gap, over * sides[0]], axis=0).T

    for k in range(parts + 1):
        at = slice(k * HALO, (k + 1) * HALO)
        if k < parts:
            near, far = left[k, 0].astype(F32), right[k, 0].astype(F32)
        else:
            near, far = 1.0 - left_wall[0].astype(F32), 1.0 - right_wall[0].astype(F32)
        sides = (has[2], has[3])
        to_left[at, :] = tall(k, near, 0, sides)[:HALO]
        to_right[at, :] = tall(k, far, wide - LANES, sides)[LANES - HALO :]
    k = parts + 1
    at = slice(k * HALO, (k + 1) * HALO)
    size = left_flow.shape[2] + LANES
    blank = jnp.zeros((HALO, to_left.shape[1] - size), F32)
    to_left[at, :size] = tall(k, left_flow[0, 0], 0, (1.0, 1.0))[:HALO]
    to_right[at, :size] = tall(k, right_flow[0, 0], flow_wide - LANES, (1.0, 1.0))[LANES - HALO :]
    to_left[at, size:] = blank
    to_right[at, size:] = blank


def sides_kernel(has, place, velocity, above, below, from_left, from_right, sides, squares, mark):
    parts, tall, _ = sides.shape
    gap = jnp.zeros((LANES - 2 * HALO, tall), F32)
    for k in range(parts):
        at = slice(k * HALO, (k + 1) * HALO)
        tile = [from_right[at, :] * has[1], gap, from_left[at, :] * has[0]]
        sides[k] = jnp.concatenate(tile, axis=0).T
    at = slice(parts * HALO, (parts + 1) * HALO)
    rows, local = velocity.shape[2:]
    size = rows + LANES
    tile = [from_right[at, :size], gap[:, :size], from_left[at, :size]]
    tile = jnp.concatenate(tile, axis=0).T
    tile = tile * tile
    mark[0] = place[0]
    squares[:HALO, :local] = above[at, :local] * above[at, :local]
    squares[HALO : HALO + rows, :local] = velocity[0, 0] * velocity[0, 0]
    squares[HALO + rows :, :local] = below[at, :local] * below[at, :local]
    squares[:HALO, local:] = tile[size - HALO :]
    squares[HALO : HALO + rows, local:] = tile[:rows]
    squares[HALO + rows :, local:] = tile[rows : rows + HALO]


def forward_x_kernel(place, *refs):
    *pieces, tables, turns, out, total, lines = refs
    count, _, rows, local = lines.shape
    for mask, piece in enumerate(pieces):
        lines[place[0] ^ mask] = piece[...]
    base = turns.shape[1]
    per = local // base
    u = [lines[t // per, 0, :, (t % per) * base : (t % per + 1) * base] for t in range(RADIX)]
    v = [lines[t // per, 1, :, (t % per) * base : (t % per + 1) * base] for t in range(RADIX)]
    energy = sum(b * b for b in v)
    energy = jnp.sum(energy.reshape(rows // 8, 8, base), axis=0)
    total[...] = sum(energy[:, k : k + LANES] for k in range(0, base, LANES))
    fields = ([a * a - b * b for a, b in zip(u, v)], [2.0 * a * b for a, b in zip(u, v)])
    zeros, mids, reals, imags = [], [], [[], [], []], [[], [], []]
    for a in fields:
        s04, s26, s15, s37 = a[0] + a[4], a[2] + a[6], a[1] + a[5], a[3] + a[7]
        d04, d26, d15, d37 = a[0] - a[4], a[2] - a[6], a[1] - a[5], a[3] - a[7]
        zeros.append((s04 + s26) + (s15 + s37))
        mids.append((s04 + s26) - (s15 + s37))
        minus, plus = ROOT * (d15 - d37), ROOT * (d15 + d37)
        turned = (
            (d04 + minus, -d26 - plus),
            (s04 - s26, s37 - s15),
            (d04 - minus, d26 - plus),
        )
        for index, (real, imag) in enumerate(turned):
            c, s = turns[index : index + 1, :], turns[index + 3 : index + 4, :]
            reals[index].append(real * c + imag * s)
            imags[index].append(imag * c - real * s)
    stacked = jnp.concatenate(
        [
            jnp.concatenate([jnp.concatenate(reals[i], axis=0) for i in range(3)], axis=0),
            jnp.concatenate([jnp.concatenate(imags[i], axis=0) for i in range(3)], axis=0),
        ],
        axis=1,
    )
    full, zero, middle = x_parts(tables, base)
    full = exact_dot(split(stacked), full)
    zero = exact_dot(split(jnp.concatenate(zeros, axis=0)), zero)
    middle = exact_dot(split(jnp.concatenate(mids, axis=0)), middle)
    low = lane_index((rows, LANES)) % 64 < 32
    target = 0
    blocks = [full[2 * rows * i : 2 * rows * (i + 1)] for i in range(3)] + [zero, middle]
    for block in blocks:
        for first in range(0, block.shape[1], LANES):
            a = block[:rows, first : first + LANES]
            c = block[rows:, first : first + LANES]
            out[target] = jnp.where(low, a, spin(c, 32))
            out[target + 1] = jnp.where(low, spin(a, -32), c)
            target += 2


def eighths(x, turn):
    s04, s26, s15, s37 = x[0] + x[4], x[2] + x[6], x[1] + x[5], x[3] + x[7]
    d04, d26, d15, d37 = x[0] - x[4], x[2] - x[6], x[1] - x[5], x[3] - x[7]
    quarter = turn(s15 - s37)
    spun_26, spun_37 = turn(d26), turn(d37)
    one, three = d15 + spun_37, d15 - spun_37
    spun_one, spun_three = turn(one), turn(three)
    one = ROOT * (one + spun_one)
    three = ROOT * (spun_three - three)
    return [
        (s04 + s26) + (s15 + s37),
        (d04 + spun_26) + one,
        (s04 - s26) + quarter,
        (d04 - spun_26) + three,
        (s04 + s26) - (s15 + s37),
        (d04 + spun_26) - one,
        (s04 - s26) - quarter,
        (d04 - spun_26) - three,
    ]


def solve_y_kernel(count_x, _, lines, total, wave, both, turns, out, held):
    count, rows, _ = lines.shape
    base = turns.shape[0]
    length = count * rows
    block = count_x * rows
    per = base // rows
    lanes = lane_index((base, LANES))
    sign = jnp.where(lanes < 64, 1.0, -1.0).astype(F32)

    def minus_i(z):
        return spin(z, 64) * sign

    def plus_i(z):
        return spin(z, 64) * -sign

    fields = [
        jnp.concatenate([lines[t * per + k] for k in range(per)], axis=0) for t in range(RADIX)
    ]
    mixed = eighths(fields, minus_i)
    table = turns[...]
    cosines = [table[:, r : r + 1] for r in range(RADIX)]
    sines = [table[:, RADIX + r : RADIX + r + 1] * sign for r in range(RADIX)]
    mixed = [mixed[0]] + [
        mixed[r] * cosines[r] + spin(mixed[r], 64) * sines[r] for r in range(1, RADIX)
    ]
    tables = (both[: 2 * base], both[2 * base :])
    product = exact_dot(tables, split(jnp.concatenate(mixed, axis=1)))
    kx = wave[0:1, :]
    first = lanes % 64 < 32
    edge = jnp.float32(length // 2)
    alone = jnp.where(first, kx * kx, 0.0)
    slope = jnp.where(first | (kx == -edge), 0.0, jnp.broadcast_to(kx, lanes.shape))
    q = lax.broadcasted_iota(jnp.int32, lanes.shape, 0)
    low_ky = RADIX * (q - jnp.where(q < base // 2, 0, base)).astype(F32)
    terms = []
    for r in range(RADIX):
        at = slice(r * LANES, (r + 1) * LANES)
        spectrum = product[:base, at] + minus_i(product[base:, at])
        ky = low_ky + float(r)
        symbol = alone + slope * ky
        if r == 0:
            corner = jnp.where((kx == -edge) & ~first, edge * edge, 0.0)
            symbol = jnp.where(ky == -edge, jnp.where(first, alone, corner), symbol)
        terms.append(symbol * pl.reciprocal(kx * kx + ky * ky) * spectrum)
    pairs = [
        jnp.where(first, low + spin(low, -32), high + spin(high, 32))
        for low, high in zip(terms[:4], terms[4:])
    ]
    product = exact_dot(tables, split(jnp.concatenate(pairs, axis=1)))
    mixed = []
    for r in range(RADIX // 2):
        at = slice(r * LANES, (r + 1) * LANES)
        value = product[:base, at] + plus_i(product[base:, at])
        cosine = jnp.where(first, cosines[r], cosines[r + 4])
        sine = jnp.where(first, sines[r], sines[r + 4])
        value = value * cosine - spin(value, 64) * sine
        value = jnp.where(first, value + spin(value, -32), spin(value, 32) - value)
        if r == 2:
            value = jnp.where(first, value, plus_i(value))
        elif r:
            turned = plus_i(value)
            odd = value + turned if r == 1 else turned - value
            value = jnp.where(first, value, ROOT * odd)
        mixed.append(value)
    even, odd = mixed[0] + mixed[2], mixed[0] - mixed[2]
    side, turned = mixed[1] + mixed[3], plus_i(mixed[1] - mixed[3])
    for t, values in enumerate((even + side, odd + turned, even - side, odd - turned)):
        start = MARGIN + 2 * t * base
        held[start : start + base, :] = values
        held[start + base : start + 2 * base, :] = spin(values, -32)
    held[0:MARGIN, :] = held[length : length + MARGIN, :]
    held[length + MARGIN : length + 2 * MARGIN, :] = held[MARGIN : 2 * MARGIN, :]
    spare = total[...] + spin(total[...], 32)
    kept = rows + 2 * MARGIN // count_x
    half = out.shape[1]
    rest = kept - half
    low = lane_index((8, LANES)) % 64 < 32
    for target in range(count):
        start = (target // count_x) * block + (target % count_x) * kept
        for row in range(0, half, 8):
            a = held[start + row : start + row + 8, :]
            if row < rest:
                b = spin(held[start + half + row : start + half + row + 8, :], 32)
            else:
                b = spare
            out[target, row : row + 8, :] = jnp.where(low, a, b)


def inverse_x_kernel(
    kept, scale, place, lines, tables, turns, *refs
):
    *outs, held = refs
    count, half, _ = lines.shape
    base = turns.shape[1]
    length = RADIX * base
    rest = kept - half
    low = lane_index((half, LANES)) % 64 < 32
    groups, spare = [], None
    for first in range(0, count, 2):
        even, odd = lines[first], lines[first + 1]
        a = jnp.where(low, even, spin(odd, 32))
        b = jnp.where(low, spin(even, -32), odd)
        groups.append(jnp.concatenate([a, b[:rest]], axis=0))
        extra = b[rest : rest + 8]
        spare = extra if spare is None else spare + extra
    mean = jnp.sum(spare) * scale
    wide = 2 * base // LANES
    narrow = base // LANES
    stacked = jnp.concatenate(
        [jnp.concatenate(groups[i * wide : (i + 1) * wide], axis=1) for i in range(3)], axis=0
    )
    at = 3 * wide
    zeros = jnp.concatenate(groups[at : at + narrow], axis=1)
    mids = jnp.concatenate(groups[at + narrow : at + 2 * narrow], axis=1)
    full, zero, middle = x_parts(tables, base)
    full = exact_dot(split(stacked), full)
    zero = exact_dot(split(zeros), zero) * scale
    mid = exact_dot(split(mids), middle) * scale
    turned = []
    for i in range(3):
        real = full[i * kept : (i + 1) * kept, :base]
        imag = full[i * kept : (i + 1) * kept, base:]
        c = turns[i : i + 1, :] * (2.0 * scale)
        s = turns[i + 3 : i + 4, :] * (2.0 * scale)
        turned.append((real * c - imag * s, real * s + imag * c))
    for t in range(RADIX):
        value = zero + mid if t % 2 == 0 else zero - mid
        for i, (real, imag) in enumerate(turned):
            eighth = t * (i + 1) % RADIX
            c = (1.0, ROOT, 0.0, -ROOT, -1.0, -ROOT, 0.0, ROOT)[eighth]
            s = (0.0, ROOT, 1.0, ROOT, 0.0, -ROOT, -1.0, -ROOT)[eighth]
            if c:
                value = value + c * real
            if s:
                value = value - s * imag
        held[:, t * base : (t + 1) * base] = mean - value
    targets, local = len(outs), outs[0].shape[1] - LANES
    right = lane_index((kept, LANES)) < 64
    for mask, out in enumerate(outs):
        start = pl.multiple_of((place[0] ^ mask) * local, LANES)
        after = pl.multiple_of(jnp.where(start + local == length, 0, start + local), LANES)
        before = pl.multiple_of(jnp.where(start == 0, length, start) - LANES, LANES)
        out[:, :local] = held[:, pl.ds(start, local)]
        out[:, local:] = jnp.where(
            right, held[:, pl.ds(after, LANES)], held[:, pl.ds(before, LANES)]
        )


def slopes_x(parts, band, with_edge):
    tiles = parts[0].shape[-1] // LANES
    pieces = []
    for first in list(range(0, tiles - 1, 2)) + ([tiles - 1] if with_edge else []):
        steps = (-1, 0, 1, 2) if first < tiles - 1 else (-1, 0, 1)
        table = band[...] if first < tiles - 1 else band[: 3 * LANES, :LANES]
        order = [(first + step) % tiles for step in steps]
        piece = None
        for part in parts:
            term = dot(jnp.concatenate([lane_tile(part, t) for t in order], axis=1), table)
            piece = term if piece is None else piece + term
        pieces.append(piece)
    return jnp.concatenate(pieces, axis=1)


def slope_y(read):
    value = read(3) - read(-3)
    for index in (0, 1):
        value = value + whole_weights[index] * (read(index + 1) - read(-index - 1))
    return value


def edged(k, side, center, up, down, above, below, sides, has, first=0):
    step = pl.program_id(0) + first
    tile, width = center.shape
    tall = sides.shape[1]
    last = (tall - LANES) // tile - 1
    base = pl.multiple_of(step * tile, 8)
    at = slice(k * HALO, (k + 1) * HALO)
    before = pl.multiple_of(jnp.where(step == 0, tall, base) - HALO, 8)
    over = jnp.where(step == 0, above[at, :] * has[2], up)
    under = jnp.where(step == last, below[at, :] * has[3], down)
    rows = (
        (over, sides[side, pl.ds(before, HALO), :]),
        (center, sides[side, pl.ds(base, tile), :]),
        (under, sides[side, pl.ds(pl.multiple_of(base + tile, 8), HALO), :]),
    )
    return jnp.concatenate([jnp.concatenate(pair, axis=1) for pair in rows], axis=0)


def edged_open(k, side, wall, wall_up, wall_down, above, below, sides, has, first=0):
    open_cells = [1.0 - ref[0].astype(F32) for ref in (wall, wall_up, wall_down)]
    return edged(k, side, *open_cells, above, below, sides, has, first)


def quiet_step_kernel(
    first, has, place, center, up, down, wall, wall_up, wall_down, above, below, sides, across, along, along_inner, out, shown_open, mark
):
    parts, _, tile, width = center.shape
    high = tile + 2 * HALO
    opened = edged_open(parts, parts, wall, wall_up, wall_down, above, below, sides, has, first)
    values = []
    for k in range(parts):
        value = edged(
            k,
            k,
            center[k, 0].astype(F32),
            up[k, 0].astype(F32)[up.shape[2] - HALO :],
            down[k, 0].astype(F32)[:HALO],
            above,
            below,
            sides,
            has,
            first,
        )
        values.append(value)

    def drops(x, along_b, along_p):
        diverge = x[1] + along_b
        return (
            diverge + mean_flow * x[0],
            x[3] + mean_flow * x[1],
            along_p + mean_flow * x[2],
            diverge + mean_flow * x[3],
        )

    short = [value.astype(BF16) for value in values]
    x = slopes_x((jnp.concatenate(short, axis=0),), across, True)
    x = [x[k * high : (k + 1) * high] for k in range(parts)]
    table = along[...]
    dropped = drops(x, dot(table, short[2]), dot(table, short[3]))
    middle = [opened * (v - (time_step / 60.0) * d) for v, d in zip(values, dropped)]
    inner = slice(HALO, HALO + tile)
    x = slopes_x(split(jnp.concatenate([value[inner] for value in middle], axis=0)), across, False)
    x = [x[k * tile : (k + 1) * tile] for k in range(parts)]
    table = along_inner[...]
    y = [sum(dot(table, part) for part in split(middle[k][:, :width])) for k in (2, 3)]
    dropped = drops(x, *y)
    shown = opened[inner, :width]
    for k in range(parts):
        start = 0.5 * values[k][inner, :width] - (0.5 * time_step / 60.0) * dropped[k]
        out[k] = shown * start + 0.5 * middle[k][inner, :width]
    shown_open[0] = opened.astype(BF16)
    mark[0] = place[0]


def source_kernel(place, squares, opened, rise_x, rise_y, quiet, across, *refs):
    *lines, out, squared, cells_open, matrix, rows_matrix, calm, band, held, raised, forced, done, fetched, kept = refs
    steps = done.shape[0]
    tile, width = calm.shape[2:]
    high = tile + 2 * HALO
    rows = lines[0].shape[0]

    def calm_copy(k):
        part = quiet.at[:, pl.ds(k * tile, tile), :]
        return pltpu.make_async_copy(part, calm.at[k % 2], fetched.at[k % 2])

    def done_copy(k):
        part = out.at[:, 0, pl.ds(k * tile, tile), :]
        return pltpu.make_async_copy(done.at[k], part, kept.at[k])

    arrays = [(squares, squared), (rise_x, matrix), (rise_y, rows_matrix), (opened, cells_open), (across, band)]
    copies = [
        pltpu.make_async_copy(source, target, fetched.at[2 + k])
        for k, (source, target) in enumerate(arrays)
    ]
    pieces = [
        pltpu.make_async_copy(
            piece,
            held.at[pl.ds(pl.multiple_of((place[0] ^ mask) * rows, 8), rows), :],
            fetched.at[2 + len(arrays) + mask],
        )
        for mask, piece in enumerate(lines)
    ]
    for copy in pieces + copies:
        copy.start()
    calm_copy(0).start()
    calm_copy(1).start()
    for copy in pieces + copies[:2]:
        copy.wait()

    level = held[MARGIN - HALO : MARGIN - HALO + squared.shape[0], :] - squared[...]
    count = level.shape[1] // LANES
    near = lane_index((level.shape[0], LANES)) < 64
    for k in range(count):
        after, before = lane_tile(level, (k + 1) % count), lane_tile(level, (k - 1) % count)
        around = jnp.concatenate([lane_tile(level, k), jnp.where(near, after, before)], axis=1)
        lanes = 2 * LANES if k < count - 1 else LANES
        value = split(exact_dot(split(around), split(matrix[k][:, :lanes])))
        for part in range(2):
            raised[part, :, 2 * k * LANES : 2 * k * LANES + lanes] = value[part]
    for copy in copies[2:]:
        copy.wait()

    reach = rows_matrix.shape[2] // 3
    third = lane_index((high, 3 * reach)) >= 2 * reach
    for k in range(steps):
        start = k * (tile // 2)
        window = [raised[part, start : start + reach, :] for part in (0, 1, 0)]
        weights = split(rows_matrix[k])
        weights = jnp.where(third, weights[1], weights[0])
        free = time_step * cells_open[k].astype(F32)
        value = free * dot(weights, jnp.concatenate(window, axis=0))
        forced[k % 2] = value
        inner = value[HALO : HALO + tile]
        shown = (0.5 / 60.0) * free[HALO : HALO + tile, :width]
        x = shown * slopes_x(split(inner), band, False)
        y = shown * slope_y(lambda d: forced[k % 2, HALO + d : HALO + d + tile, :width])
        calm_copy(k).wait()
        still = calm.at[k % 2]
        done[k, 0] = still[0].astype(BF16)
        done[k, 1] = (still[1] - x).astype(BF16)
        done[k, 2] = (still[2] - y).astype(BF16)
        done[k, 3] = (still[3] + inner[:, :width] - mean_flow * x).astype(BF16)
        done_copy(k).start()
        if k + 2 < steps:
            calm_copy(k + 2).start()
    for k in range(steps):
        done_copy(k).wait()


def call(
    kernel, operands, outs, scratch=(), steps=0, specs=None, out_specs=None, after=(), aliases=None, megabytes=24, flops=0, moved=0, name=None
):
    count = len(operands)

    def body(*refs):
        kernel(*refs[:count], *refs[count + len(after) :])

    def whole(array):
        zeros = (0,) * len(array.shape)
        return pl.BlockSpec(array.shape, lambda *_: zeros)

    arguments = {}
    chosen = specs or {}
    if steps:
        arguments["grid"] = (steps,)
        in_specs = [chosen.get(i, whole(o)) for i, o in enumerate(operands)]
        arguments["out_specs"] = jax.tree.map(whole, outs) if out_specs is None else out_specs
    else:
        local = pl.BlockSpec(memory_space=pltpu.VMEM)
        in_specs = [chosen.get(i, local) for i in range(count)]
        if out_specs is not None:
            arguments["out_specs"] = out_specs
    return pl.pallas_call(
        body,
        out_shape=outs,
        in_specs=in_specs + [pl.BlockSpec(memory_space=pl.ANY)] * len(after),
        scratch_shapes=list(scratch),
        input_output_aliases=aliases or {},
        compiler_params=pltpu.CompilerParams(vmem_limit_bytes=megabytes << 20),
        cost_estimate=pl.CostEstimate(flops=flops, bytes_accessed=moved, transcendentals=0),
        name=name,
        **arguments,
    )(*operands, *after)


def ring(array, axis, step):
    size = lax.axis_size(axis)
    return lax.ppermute(array, axis, [(i, (i + step) % size) for i in range(size)])


def swap(array, axis, mask):
    return lax.ppermute(array, axis, [(i, i ^ mask) for i in range(lax.axis_size(axis))])


def shaped(*shape, kind=F32):
    return jax.ShapeDtypeStruct(shape, kind)


def pressure_lines(pieces, place_x, gathered, spread, stepped):
    _, rows, local_x = pieces[0].shape
    count_x, count_y = lax.axis_size("gx"), lax.axis_size("gy")
    count = count_x * count_y
    scalars = {0: pl.BlockSpec(memory_space=pltpu.SMEM)}
    length_x, length_y = local_x * count_x, rows * count
    full, zero, middle, cos_turn, sin_turn = x_tables(length_x)
    turns = np.zeros((8, cos_turn.shape[1]), np.float32)
    turns[0:3], turns[3:6] = cos_turn, sin_turn
    spectra, total = call(
        forward_x_kernel,
        (place_x, *pieces, np.concatenate([beside(full), beside(zero, middle)]), turns),
        (shaped(count, rows, LANES), shaped(8, LANES)),
        (pltpu.VMEM((count_x, 2, rows, local_x), F32),),
        specs=scalars,
        after=gathered,
        flops=10**9,
        moved=4 << 20,
        name="forward_x",
    )
    spectra = lax.all_to_all(spectra, ("gy", "gx"), 0, 0, tiled=True)
    place = lax.axis_index("gy") * count_x + lax.axis_index("gx")
    waves = jnp.asarray(wave_table(length_x, count))
    wave = lax.dynamic_slice(waves, (place, 0), (1, LANES))
    both, turns_y = y_tables(length_y)
    kept = rows + 2 * MARGIN // count_x
    half = (kept // 2 + 8) // 8 * 8
    solved = call(
        functools.partial(solve_y_kernel, count_x),
        (spread, spectra, total, wave, beside(both), turns_y),
        shaped(count, half, LANES),
        (pltpu.VMEM((length_y + 2 * MARGIN, LANES), F32),),
        specs=scalars,
        flops=4 * 10**9,
        moved=6 << 20,
        name="solve_y",
    )
    solved = lax.all_to_all(solved, ("gy", "gx"), 0, 0, tiled=True)
    back = 2.0 * zero.T
    back[LANES // 2] *= 0.5
    tables = np.concatenate(
        [beside(full.T), beside(back, 2.0 * middle.T)]
    )
    pressed = call(
        functools.partial(inverse_x_kernel, kept, 1.0 / (length_x * length_y)),
        (stepped, solved, tables, turns),
        (shaped(kept, local_x + LANES),) * count_x,
        (pltpu.VMEM((kept, length_x), F32),),
        specs=scalars,
        flops=10**9,
        moved=4 << 20,
        name="inverse_x",
    )
    return [piece if mask == 0 else swap(piece, "gx", mask) for mask, piece in enumerate(pressed)]


def refine_tables(weights_x, weights_y, tall, wide):
    first = lax.axis_index("gx") * wide
    ends = jnp.concatenate([weights_x[:, -LANES:], weights_x, weights_x[:, :LANES]], axis=1)
    own = lax.dynamic_slice(ends, (0, first), (4, wide + 2 * LANES))
    half = LANES // 2
    edge = jnp.concatenate([own[:, wide + LANES : wide + LANES + half], own[:, half:LANES]], axis=1)
    edge = jnp.pad(edge, ((0, 0), (0, LANES)))
    tiles = wide // (2 * LANES)
    weights = jnp.concatenate([own[:, LANES : wide + LANES], edge], axis=1)
    weights = weights.reshape(4, tiles + 1, 1, 2 * LANES)
    fine = np.arange(2 * LANES)
    targets = np.tile(fine // 2 - 1, (tiles + 1, 1))
    targets[tiles] = np.where(fine < half, fine // 2 - 1, half + fine // 2 - 1)
    cells = lax.broadcasted_iota(jnp.int32, (tiles + 1, 2 * LANES, 2 * LANES), 1)
    targets = jnp.asarray(targets[:, None, :].astype(np.int32))
    rise_x = sum(
        jnp.where(cells == (targets + t) % (2 * LANES), weights[t], 0.0) for t in range(4)
    )
    ends = jnp.concatenate([weights_y[:, -HALO:], weights_y, weights_y[:, :HALO]], axis=1)
    own = lax.dynamic_slice(ends, (0, lax.axis_index("gy") * tall), (4, tall + 2 * HALO))
    high, steps = TILE + 2 * HALO, tall // TILE
    own = jnp.stack([own[:, k * TILE : k * TILE + high] for k in range(steps)], axis=1)
    reach = high // 2 + HALO
    cells = lax.broadcasted_iota(jnp.int32, (steps, high, 3 * reach), 2) % reach
    targets = lax.broadcasted_iota(jnp.int32, cells.shape, 1) // 2 + (HALO // 2 - 1)
    rise_y = sum(jnp.where(cells == targets + s, own[s][:, :, None], 0.0) for s in range(4))
    return rise_x, rise_y


def fast_shards(velocity, weights_x, weights_y, acoustic, wall_mask):
    parts, _, tall, wide = acoustic.shape
    _, _, local_y, local_x = velocity.shape
    count_x, count_y = lax.axis_size("gx"), lax.axis_size("gy")
    place_x, place_y = lax.axis_index("gx"), lax.axis_index("gy")
    full, high, steps = wide + LANES, TILE + 2 * HALO, tall // TILE
    strips = (parts + 2) * HALO
    small = 2 * HALO
    has = jnp.stack([place_x > 0, place_x < count_x - 1, place_y > 0, place_y < count_y - 1])
    has = has.astype(F32)
    scalars = pl.BlockSpec(memory_space=pltpu.SMEM)

    def at(block, *index):
        return pl.BlockSpec(block, lambda i: index)

    own = place_x.astype(jnp.int32).reshape(1)
    sent = call(
        pieces_kernel,
        (own, velocity),
        (shaped(2, local_y // count_x, local_x),) * count_x,
        specs={0: scalars},
        moved=2 << 20,
        megabytes=8,
        name="pieces",
    )
    moved = [piece if mask == 0 else swap(piece, "gx", mask) for mask, piece in enumerate(sent)]
    first, last = call(
        rows_kernel,
        (acoustic, acoustic, wall_mask, wall_mask, velocity, velocity),
        (shaped(strips, wide),) * 2,
        steps=1,
        specs={
            0: at((parts, 1, small, wide), 0, 0, 0, 0),
            1: at((parts, 1, small, wide), 0, 0, tall // small - 1, 0),
            2: at((1, HALO, wide), 0, 0, 0),
            3: at((1, HALO, wide), 0, tall // HALO - 1, 0),
            4: at((1, 1, HALO, local_x), 1, 0, 0, 0),
            5: at((1, 1, HALO, local_x), 1, 0, local_y // HALO - 1, 0),
        },
        after=moved[1:2],
        moved=2 << 20,
        megabytes=54,
        name="rows",
    )
    above, below = ring(last, "gy", 1), ring(first, "gy", -1)
    to_right, to_left = call(
        columns_kernel,
        (has, acoustic, acoustic, wall_mask, wall_mask, velocity, velocity, above, below),
        (shaped(strips, tall + LANES), shaped(strips, tall + LANES)),
        steps=1,
        specs={
            0: scalars,
            1: at((parts, 1, tall, LANES), 0, 0, 0, 0),
            2: at((parts, 1, tall, LANES), 0, 0, 0, wide // LANES - 1),
            3: at((1, tall, LANES), 0, 0, 0),
            4: at((1, tall, LANES), 0, 0, wide // LANES - 1),
            5: at((1, 1, local_y, LANES), 1, 0, 0, 0),
            6: at((1, 1, local_y, LANES), 1, 0, 0, local_x // LANES - 1),
        },
        moved=8 << 20,
        megabytes=54,
        name="columns",
    )
    from_left, from_right = ring(to_right, "gx", 1), ring(to_left, "gx", -1)
    sides, squares, beside = call(
        sides_kernel,
        (has, own, velocity, above, below, from_left, from_right),
        (
            shaped(parts + 1, tall + LANES, LANES),
            shaped(local_y + 2 * HALO, local_x + LANES),
            shaped(1, kind=jnp.int32),
        ),
        steps=1,
        specs={0: scalars, 1: scalars, 2: at((1, 1, local_y, local_x), 1, 0, 0, 0)},
        out_specs=(
            at((parts + 1, tall + LANES, LANES), 0, 0, 0),
            at((local_y + 2 * HALO, local_x + LANES), 0, 0),
            scalars,
        ),
        moved=8 << 20,
        megabytes=54,
        name="sides",
    )
    across, along = band_tables(high)
    along_inner = along[HALO : HALO + TILE]
    per, rows = TILE // small, TILE // HALO

    def tiled(first):
        walls = (
            pl.BlockSpec((1, TILE, wide), lambda i: (0, i + first, 0)),
            pl.BlockSpec((1, HALO, wide), lambda i: (0, jnp.maximum((i + first) * rows - 1, 0), 0)),
            pl.BlockSpec(
                (1, HALO, wide),
                lambda i: (0, jnp.minimum((i + first + 1) * rows, steps * rows - 1), 0),
            ),
        )
        cells = (
            pl.BlockSpec((parts, 1, TILE, wide), lambda i: (0, 0, i + first, 0)),
            pl.BlockSpec(
                (parts, 1, small, wide), lambda i: (0, 0, jnp.maximum((i + first) * per - 1, 0), 0)
            ),
            pl.BlockSpec(
                (parts, 1, small, wide),
                lambda i: (0, 0, jnp.minimum((i + first + 1) * per, steps * per - 1), 0),
            ),
        )
        return cells, walls, pl.BlockSpec((parts, TILE, wide), lambda i: (0, i + first, 0))

    def quiet_tiles(first, count, before):
        cells, walls, flat = tiled(first)
        operands = (has, own, acoustic, acoustic, acoustic, wall_mask, wall_mask, wall_mask, above, below, sides)
        operands = operands + (across, along, along_inner)
        return call(
            functools.partial(quiet_step_kernel, first),
            operands,
            (shaped(parts, tall, wide), shaped(steps, high, full, kind=BF16), shaped(1, kind=jnp.int32)),
            steps=count,
            specs=dict(enumerate((scalars, scalars) + cells + walls)),
            out_specs=(flat, pl.BlockSpec((1, high, full), lambda i: (i + first, 0, 0)), scalars),
            after=before,
            aliases={len(operands): 0, len(operands) + 1: 1} if before else None,
            megabytes=54,
            flops=3 * 10**9 * count,
            moved=(12 << 20) * count,
            name="quiet_step",
        )

    early = max(steps * 3 // 4, 1)
    *begun, stepped = quiet_tiles(0, early, ())
    quiet, opened = begun
    if early < steps:
        quiet, opened, _ = quiet_tiles(early, steps - early, begun)
    rows_done = above[:8, :LANES] + below[:8, :LANES]
    lines = pressure_lines(moved, own, (rows_done,), beside, stepped)
    rise_x, rise_y = refine_tables(weights_x, weights_y, tall, wide)
    operands = (own, squares, opened, rise_x, rise_y, quiet, across, *lines)
    anywhere = pl.BlockSpec(memory_space=pl.ANY)
    specs = {k: anywhere for k in range(1, len(operands))}
    scratch = (
        pltpu.VMEM(squares.shape, F32),
        pltpu.VMEM(opened.shape, BF16),
        pltpu.VMEM(rise_x.shape, F32),
        pltpu.VMEM(rise_y.shape, F32),
        pltpu.VMEM((2, parts, TILE, wide), F32),
        pltpu.VMEM(across.shape, BF16),
        pltpu.VMEM((local_y + 2 * MARGIN, local_x + LANES), F32),
        pltpu.VMEM((2, local_y + 2 * HALO, full), BF16),
        pltpu.VMEM((2, high, full), F32),
        pltpu.VMEM((steps, parts, TILE, wide), BF16),
        pltpu.SemaphoreType.DMA((7 + count_x,)),
        pltpu.SemaphoreType.DMA((steps,)),
    )
    return call(
        source_kernel,
        operands,
        shaped(*acoustic.shape, kind=BF16),
        scratch,
        specs={0: scalars, **specs},
        out_specs=anywhere,
        megabytes=56,
        flops=4 * 10**9,
        moved=16 << 20,
        name="source_step",
    )


def fits(count_x, count_y, velocity, acoustic):
    _, planes, local_y, local_x = velocity
    _, _, tall, wide = acoustic
    length_x, length_y = local_x * count_x, local_y * count_y
    rows = local_y // count_x
    base_x, base_y = length_x // RADIX, length_y // RADIX
    return (
        planes == 1
        and length_x * 2 == count_x * count_y * LANES
        and base_x % (2 * LANES) == 0
        and local_x % base_x == 0
        and rows % 8 == 0
        and base_y % rows == 0
        and base_y % 8 == 0
        and MARGIN * 2 % (8 * count_x) == 0
        and tall == 2 * local_y
        and wide == 2 * local_x
        and tall % TILE == 0
        and tall >= 2 * TILE
        and count_x & (count_x - 1) == 0
        and wide % (2 * LANES) == 0
    )


def extended(array, sides, width):
    for axis, dim in sides:
        size, length = (lax.axis_size(axis), array.shape[dim])
        up = [(i, (i + 1) % size) for i in range(size - 1)]
        down = [(j, i) for i, j in up]
        last = lax.slice_in_dim(array, length - width, length, axis=dim)
        leading = lax.slice_in_dim(array, 0, width, axis=dim)
        before = lax.ppermute(last, axis, up)
        after = lax.ppermute(leading, axis, down)
        array = jnp.concatenate([before, array, after], axis=dim)
    return array


def gradients(padded):
    height = padded.shape[-2] - 6
    breadth = padded.shape[-1] - 6
    rows_mid = padded[..., 3 : 3 + height, :]
    cols_mid = padded[..., :, 3 : 3 + breadth]
    along_x = jnp.zeros_like(padded[..., 3 : 3 + height, 3 : 3 + breadth])
    along_y = jnp.zeros_like(along_x)
    for index, weight in enumerate(stencil_weights):
        distance = index + 1
        along_x = along_x + weight * (
            rows_mid[..., 3 + distance : 3 + distance + breadth]
            - rows_mid[..., 3 - distance : 3 - distance + breadth]
        )
        along_y = along_y + weight * (
            cols_mid[..., 3 + distance : 3 + distance + height, :]
            - cols_mid[..., 3 - distance : 3 - distance + height, :]
        )
    return (along_x, along_y)


def tendency(padded, source):
    along_x, along_y = gradients(padded)
    diverge = along_x[1] + along_y[2]
    forcing = jnp.stack([-diverge, -along_x[3], -along_y[3], source - diverge])
    return forcing - mean_flow * along_x


def spectral_index(flat, length):
    second = length // 16
    wave = flat // second + 16 * (flat % second)
    return jnp.where(wave < length // 2, wave, wave - length).astype(jnp.float32)


def twiddles(rows_count, cols_count, modulus, sign):
    products = jnp.arange(rows_count)[:, None] * jnp.arange(cols_count)[None, :] % modulus
    angles = 2.0 * math.pi / modulus * products.astype(jnp.float32)
    return (jnp.cos(angles), sign * jnp.sin(angles))


def mix_rows(real_part, imag_part, cosine, sine):
    exact = lax.Precision.HIGHEST
    cos_real = jnp.einsum("ka,...ab->...kb", cosine, real_part, precision=exact)
    cos_imag = jnp.einsum("ka,...ab->...kb", cosine, imag_part, precision=exact)
    sin_real = jnp.einsum("ka,...ab->...kb", sine, real_part, precision=exact)
    sin_imag = jnp.einsum("ka,...ab->...kb", sine, imag_part, precision=exact)
    return (cos_real - sin_imag, cos_imag + sin_real)


def mix_cols(real_part, imag_part, cosine, sine):
    exact = lax.Precision.HIGHEST
    cos_real = jnp.einsum("...kb,bc->...kc", real_part, cosine, precision=exact)
    cos_imag = jnp.einsum("...kb,bc->...kc", imag_part, cosine, precision=exact)
    sin_real = jnp.einsum("...kb,bc->...kc", real_part, sine, precision=exact)
    sin_imag = jnp.einsum("...kb,bc->...kc", imag_part, sine, precision=exact)
    return (cos_real - sin_imag, cos_imag + sin_real)


def rotate(real_part, imag_part, cosine, sine):
    return (real_part * cosine - imag_part * sine, real_part * sine + imag_part * cosine)


def discrete(real_part, imag_part, sign):
    length = real_part.shape[-1]
    second = length // 16
    initial = real_part.shape
    folded = initial[:-1] + (16, second)
    real_part = real_part.reshape(folded)
    imag_part = imag_part.reshape(folded)
    small_cos, small_sin = twiddles(16, 16, 16, sign)
    large_cos, large_sin = twiddles(second, second, second, sign)
    turn_cos, turn_sin = twiddles(16, second, length, sign)
    if sign < 0:
        real_part, imag_part = mix_rows(real_part, imag_part, small_cos, small_sin)
        real_part, imag_part = rotate(real_part, imag_part, turn_cos, turn_sin)
        real_part, imag_part = mix_cols(real_part, imag_part, large_cos, large_sin)
    else:
        real_part, imag_part = mix_cols(real_part, imag_part, large_cos, large_sin)
        real_part, imag_part = rotate(real_part, imag_part, turn_cos, turn_sin)
        real_part, imag_part = mix_rows(real_part, imag_part, small_cos, small_sin)
        real_part = real_part / length
        imag_part = imag_part / length
    return (real_part.reshape(initial), imag_part.reshape(initial))


def transform(stacked, sign, kind):
    if kind == "real_in":
        real_part = stacked
        imag_part = jnp.zeros_like(stacked)
    else:
        half = stacked.shape[0] // 2
        real_part = stacked[:half]
        imag_part = stacked[half:]
    real_out, imag_out = discrete(real_part, imag_part, sign)
    if kind == "real_out":
        return real_out
    return jnp.concatenate([real_out, imag_out], axis=0)


def project(stacked, wave_x, wave_y):
    coef_xx = wave_x * wave_x
    coef_xy = 2.0 * wave_x * wave_y
    coef_yy = wave_y * wave_y
    denominator = wave_x * wave_x + wave_y * wave_y
    positive = denominator > 0
    safe = jnp.where(positive, denominator, 1.0)

    def combine(parts):
        numerator = -(coef_xx * parts[0] + coef_xy * parts[1] + coef_yy * parts[2])
        return jnp.where(positive, numerator / safe, 0.0)

    return jnp.stack([combine(stacked[:3]), combine(stacked[3:])])


def refine(stacked, weights):
    result = jnp.zeros(stacked.shape[:-1] + (2 * stacked.shape[-1],), jnp.float32)
    for offset in range(4):
        result = (
            result
            + jnp.repeat(jnp.roll(stacked, 1 - offset, axis=-1), 2, axis=-1) * weights[offset]
        )
    return result


def lines_x(stacked, action):
    gathered = action(lax.all_to_all(stacked, "gx", split_axis=2, concat_axis=3, tiled=True))
    return lax.all_to_all(gathered, "gx", split_axis=3, concat_axis=2, tiled=True)


def lines_y(stacked, action):
    turned = jnp.swapaxes(stacked, 2, 3)
    gathered = action(lax.all_to_all(turned, "gy", split_axis=2, concat_axis=3, tiled=True))
    returned = lax.all_to_all(gathered, "gy", split_axis=3, concat_axis=2, tiled=True)
    return jnp.swapaxes(returned, 2, 3)


def expand(fields):
    return extended(fields, (("gx", 3), ("gy", 2)), 3)


def shards(velocity, weights_x, weights_y, acoustic, wall_mask):
    acoustic = acoustic.astype(jnp.float32)
    flow_x = velocity[0]
    flow_y = velocity[1]
    tensor = jnp.stack([flow_x * flow_x, flow_x * flow_y, flow_y * flow_y])
    count_gx = lax.axis_size("gx")
    count_gy = lax.axis_size("gy")
    place_x = lax.axis_index("gx")
    place_y = lax.axis_index("gy")
    local_y = tensor.shape[2]
    local_x = tensor.shape[3]
    length_x = local_x * count_gx
    length_y = local_y * count_gy

    def forward_real(portion):
        return transform(portion, -1, "real_in")

    def finish_x(portion):
        return refine(transform(portion, 1, "real_out"), weights_x)

    spectra = lines_x(tensor, forward_real)
    share_x = local_x // count_gy
    line_x = spectral_index(place_x * local_x + place_y * share_x + jnp.arange(share_x), length_x)[
        :, None
    ]
    line_y = spectral_index(jnp.arange(length_y), length_y)[None, :]

    def solve_y(portion):
        solved = project(transform(portion, -1, "complex"), line_x, line_y)
        return refine(transform(solved, 1, "complex"), weights_y)

    pressure = lines_y(spectra, solve_y)
    source = lines_x(pressure, finish_x)[0]
    open_cells = (1 - wall_mask).astype(jnp.float32)
    first_rate = tendency(expand(acoustic), source)
    middle = open_cells * (acoustic + time_step * first_rate)
    second_rate = tendency(expand(middle), source)
    return (open_cells * (acoustic + 0.5 * time_step * (first_rate + second_rate))).astype(
        jnp.bfloat16
    )


def solution(mesh):
    in_specs = (P(None, None, "gy", "gx"), P(), P(), P(None, None, "gy", "gx"), P(None, "gy", "gx"))
    out_specs = P(None, None, "gy", "gx")

    def chosen(velocity, weights_x, weights_y, acoustic, wall_mask):
        sizes = (mesh.shape["gx"], mesh.shape["gy"], velocity.shape, acoustic.shape)
        plan = fast_shards if fits(*sizes) else shards
        return plan(velocity, weights_x, weights_y, acoustic, wall_mask)

    return jax.shard_map(
        chosen, mesh=mesh, in_specs=in_specs, out_specs=out_specs, check_vma=False
    )
```

```python
import functools
import math

import jax
import jax.numpy as jnp
import ml_dtypes
import numpy as np
from jax import lax
from jax.experimental import pallas as pl
from jax.experimental.pallas import tpu as pltpu
from jax.sharding import PartitionSpec as P

stencil_weights = (0.75, -0.15, 1.0 / 60.0)
mean_flow = 0.3
time_step = 0.5
whole_weights = (45.0, -9.0, 1.0)

LANES = 128
RADIX = 8
HALO = 8
MARGIN = 16
TILE = 128
ROOT = math.sqrt(0.5)
STRIP = {2: (0, 6), 3: (6, 6), 1: (12, 3), 4: (15, 3), 5: (20, 4)}
STRIP_ROWS = 24
PARTS = 4
BF16 = jnp.bfloat16
F32 = jnp.float32


def halves(table):
    high = table.astype(np.float32).astype(ml_dtypes.bfloat16)
    low = (table - high.astype(np.float64)).astype(np.float32).astype(ml_dtypes.bfloat16)
    return high, low


def packed_columns(cosine, sine):
    half = LANES // 2
    parts = []
    for first in range(0, cosine.shape[1], half):
        parts += [cosine[:, first : first + half], sine[:, first : first + half]]
    return np.concatenate(parts, axis=1)


@functools.lru_cache(maxsize=None)
def x_tables(length):
    base = length // RADIX
    m = np.arange(base)[:, None]
    q = np.arange(base)[None, :]
    angle = 2.0 * np.pi * ((m * q) % base) / base
    cosine, sine = np.cos(angle), np.sin(angle)
    full = np.concatenate([packed_columns(cosine, -sine), packed_columns(sine, cosine)], axis=0)
    half = base // 2
    zero_cos, zero_sin = cosine[:, :half].copy(), -sine[:, :half]
    zero_cos[:, 0] = 0.0
    zero_sin = zero_sin.copy()
    zero_sin[:, 0] = (-1.0) ** np.arange(base)
    zero = packed_columns(zero_cos, zero_sin)
    shifted = 2.0 * np.pi * ((m * (RADIX * q[:, :half] + RADIX // 2)) % length) / length
    middle = packed_columns(np.cos(shifted), -np.sin(shifted))
    turns = 2.0 * np.pi * np.arange(1, RADIX // 2)[:, None] * np.arange(base)[None, :] / length
    return full, zero, middle, np.cos(turns), np.sin(turns)


@functools.lru_cache(maxsize=None)
def y_tables(length):
    base = length // RADIX
    index = np.arange(base)
    angle = 2.0 * np.pi * ((index[:, None] * index[None, :]) % base) / base
    both = np.concatenate([np.cos(angle), np.sin(angle)], axis=0)
    turns = 2.0 * np.pi * np.arange(RADIX)[:, None] * index[None, :] / length
    return both, np.concatenate([np.cos(turns), np.sin(turns)], axis=0).T.astype(np.float32)


@functools.lru_cache(maxsize=None)
def wave_table(length, count):
    slots = LANES // 4
    base = length // RADIX
    waves = []
    for residue in (1, 2, 3):
        waves.append(RADIX * np.arange(base) + residue)
    waves.append(RADIX * np.arange(base // 2))
    waves.append(RADIX * np.arange(base // 2) + RADIX // 2)
    waves = np.concatenate(waves)
    waves = np.where(waves == 0, length // 2, waves)
    waves = np.where(waves < length // 2, waves, waves - length).reshape(count, slots)
    return np.tile(waves, (1, 4)).astype(np.float32)


@functools.lru_cache(maxsize=None)
def band_tables(rows):
    across = np.zeros((4 * LANES, 2 * LANES))
    column = np.arange(2 * LANES)
    down = np.zeros((rows, rows))
    for index, weight in enumerate(whole_weights):
        distance = index + 1
        across[column + LANES + distance, column] = weight
        across[column + LANES - distance, column] = -weight
        down += weight * (np.eye(rows, k=distance) - np.eye(rows, k=-distance))
    return across.astype(ml_dtypes.bfloat16), down.astype(ml_dtypes.bfloat16)


def beside(*tables):
    high, low = halves(np.concatenate(tables, axis=1))
    return np.concatenate([high, low], axis=0)


def split(values):
    high = values.astype(BF16)
    return high, (values - high.astype(F32)).astype(BF16)


def dot(left, right):
    return jnp.dot(left, right, preferred_element_type=F32)


def exact_dot(left, right):
    left_high, left_low = left
    right_high, right_low = right
    return dot(left_high, right_high) + (dot(left_low, right_high) + dot(left_high, right_low))


def lane_index(shape):
    return lax.broadcasted_iota(jnp.int32, shape, len(shape) - 1)


def spin(values, shift):
    return pltpu.roll(values, shift % values.shape[-1], values.ndim - 1)


def lane_tile(values, index):
    return values[:, index * LANES : (index + 1) * LANES]


def x_parts(tables, base):
    wide = 2 * base
    full = (tables[:wide], tables[wide : 2 * wide])
    at = 2 * wide
    high, low = tables[at : at + base], tables[at + base : at + 2 * base]
    return full, (high[:, :base], low[:, :base]), (high[:, base:], low[:, base:])


def pieces_kernel(place, velocity, *pieces):
    rows = pieces[0].shape[1]
    count = len(pieces) // 2
    for k, piece in enumerate(pieces):
        start = (place[0] ^ (k % count)) * (2 * rows) + (k // count) * rows
        for c in range(2):
            piece[c] = velocity[c, 0, pl.ds(pl.multiple_of(start, 8), rows), :]


def rows_kernel(top, low, top_wall, low_wall, top_flow, low_flow, first, last):
    small, width = top.shape[2], top_flow.shape[3]
    first[...] = jnp.zeros(first.shape, F32)
    last[...] = jnp.zeros(last.shape, F32)
    for k, (start, rows) in STRIP.items():
        lanes = slice(0, width) if k == PARTS + 1 else slice(None)
        if k < PARTS:
            upper, lower = top[k, 0].astype(F32)[:HALO], low[k, 0].astype(F32)[small - HALO :]
        elif k == PARTS:
            upper, lower = 1.0 - top_wall[0].astype(F32), 1.0 - low_wall[0].astype(F32)
        else:
            upper, lower = top_flow[0, 0], low_flow[0, 0]
        first[start : start + rows, lanes] = upper[:rows]
        last[start : start + rows, lanes] = lower[HALO - rows :]


def strip(ref, k, upper, lanes=slice(None)):
    if k not in STRIP:
        return jnp.zeros((HALO, ref[0:1, lanes].shape[1]), F32)
    start, rows = STRIP[k]
    values = ref[start : start + rows, lanes]
    blank = jnp.zeros((HALO - rows, values.shape[1]), F32)
    return jnp.concatenate([blank, values] if upper else [values, blank], axis=0)


def columns_kernel(
    has, left, right, left_wall, right_wall, left_flow, right_flow, above, below, to_right, to_left
):
    parts = left.shape[0]
    wide, flow_wide = above.shape[1], above.shape[1] // 2
    gap = jnp.zeros((LANES - 2 * HALO, LANES), F32)

    def tall(k, inner, first, sides):
        lanes = slice(first, first + LANES)
        over, under = strip(above, k, True, lanes), strip(below, k, False, lanes)
        return jnp.concatenate([inner, under * sides[1], gap, over * sides[0]], axis=0).T

    for k in range(parts + 1):
        at = slice(k * HALO, (k + 1) * HALO)
        if k < parts:
            near, far = left[k, 0].astype(F32), right[k, 0].astype(F32)
        else:
            near, far = 1.0 - left_wall[0].astype(F32), 1.0 - right_wall[0].astype(F32)
        sides = (has[2], has[3])
        to_left[at, :] = tall(k, near, 0, sides)[:HALO]
        to_right[at, :] = tall(k, far, wide - LANES, sides)[LANES - HALO :]
    k = parts + 1
    at = slice(k * HALO, (k + 1) * HALO)
    size = left_flow.shape[2] + LANES
    blank = jnp.zeros((HALO, to_left.shape[1] - size), F32)
    to_left[at, :size] = tall(k, left_flow[0, 0], 0, (1.0, 1.0))[:HALO]
    to_right[at, :size] = tall(k, right_flow[0, 0], flow_wide - LANES, (1.0, 1.0))[LANES - HALO :]
    to_left[at, size:] = blank
    to_right[at, size:] = blank


def sides_kernel(has, place, velocity, above, below, from_left, from_right, sides, squares, mark):
    parts, tall, _ = sides.shape
    gap = jnp.zeros((LANES - 2 * HALO, tall), F32)
    for k in range(parts):
        at = slice(k * HALO, (k + 1) * HALO)
        tile = [from_right[at, :] * has[1], gap, from_left[at, :] * has[0]]
        sides[k] = jnp.concatenate(tile, axis=0).T
    at = slice(parts * HALO, (parts + 1) * HALO)
    rows, local = velocity.shape[2:]
    size = rows + LANES
    tile = [from_right[at, :size], gap[:, :size], from_left[at, :size]]
    tile = jnp.concatenate(tile, axis=0).T
    tile = tile * tile
    mark[0] = place[0]
    over, under = (strip(ref, parts, ref is above, slice(0, local)) for ref in (above, below))
    squares[:HALO, :local] = over * over
    squares[HALO : HALO + rows, :local] = velocity[0, 0] * velocity[0, 0]
    squares[HALO + rows :, :local] = under * under
    squares[:HALO, local:] = tile[size - HALO :]
    squares[HALO : HALO + rows, local:] = tile[:rows]
    squares[HALO + rows :, local:] = tile[rows : rows + HALO]


def forward_x_kernel(place, *refs):
    *pieces, tables, turns, out, total, lines = refs
    count, _, rows, local = lines.shape
    for mask, piece in enumerate(pieces):
        lines[place[0] ^ mask] = piece[...]
    base = turns.shape[1]
    per = local // base
    u = [lines[t // per, 0, :, (t % per) * base : (t % per + 1) * base] for t in range(RADIX)]
    v = [lines[t // per, 1, :, (t % per) * base : (t % per + 1) * base] for t in range(RADIX)]
    energy = sum(b * b for b in v)
    energy = jnp.sum(energy.reshape(rows // 8, 8, base), axis=0)
    total[...] = sum(energy[:, k : k + LANES] for k in range(0, base, LANES))
    fields = ([a * a - b * b for a, b in zip(u, v)], [2.0 * a * b for a, b in zip(u, v)])
    zeros, mids, reals, imags = [], [], [[], [], []], [[], [], []]
    for a in fields:
        s04, s26, s15, s37 = a[0] + a[4], a[2] + a[6], a[1] + a[5], a[3] + a[7]
        d04, d26, d15, d37 = a[0] - a[4], a[2] - a[6], a[1] - a[5], a[3] - a[7]
        zeros.append((s04 + s26) + (s15 + s37))
        mids.append((s04 + s26) - (s15 + s37))
        minus, plus = ROOT * (d15 - d37), ROOT * (d15 + d37)
        turned = (
            (d04 + minus, -d26 - plus),
            (s04 - s26, s37 - s15),
            (d04 - minus, d26 - plus),
        )
        for index, (real, imag) in enumerate(turned):
            c, s = turns[index : index + 1, :], turns[index + 3 : index + 4, :]
            reals[index].append(real * c + imag * s)
            imags[index].append(imag * c - real * s)
    stacked = jnp.concatenate(
        [
            jnp.concatenate([jnp.concatenate(reals[i], axis=0) for i in range(3)], axis=0),
            jnp.concatenate([jnp.concatenate(imags[i], axis=0) for i in range(3)], axis=0),
        ],
        axis=1,
    )
    full, zero, middle = x_parts(tables, base)
    full = exact_dot(split(stacked), full)
    zero = exact_dot(split(jnp.concatenate(zeros, axis=0)), zero)
    middle = exact_dot(split(jnp.concatenate(mids, axis=0)), middle)
    low = lane_index((rows, LANES)) % 64 < 32
    target = 0
    blocks = [full[2 * rows * i : 2 * rows * (i + 1)] for i in range(3)] + [zero, middle]
    for block in blocks:
        for first in range(0, block.shape[1], LANES):
            a = block[:rows, first : first + LANES]
            c = block[rows:, first : first + LANES]
            out[target] = jnp.where(low, a, spin(c, 32))
            out[target + 1] = jnp.where(low, spin(a, -32), c)
            target += 2


def eighths(x, turn):
    s04, s26, s15, s37 = x[0] + x[4], x[2] + x[6], x[1] + x[5], x[3] + x[7]
    d04, d26, d15, d37 = x[0] - x[4], x[2] - x[6], x[1] - x[5], x[3] - x[7]
    quarter = turn(s15 - s37)
    spun_26, spun_37 = turn(d26), turn(d37)
    one, three = d15 + spun_37, d15 - spun_37
    spun_one, spun_three = turn(one), turn(three)
    one = ROOT * (one + spun_one)
    three = ROOT * (spun_three - three)
    return [
        (s04 + s26) + (s15 + s37),
        (d04 + spun_26) + one,
        (s04 - s26) + quarter,
        (d04 - spun_26) + three,
        (s04 + s26) - (s15 + s37),
        (d04 + spun_26) - one,
        (s04 - s26) - quarter,
        (d04 - spun_26) - three,
    ]


def solve_y_kernel(count_x, _, early, late, early_total, late_total, wave, both, turns, out, held):
    count, rows, _ = early.shape
    rows *= 2
    base = turns.shape[0]
    length = count * rows
    block = count_x * rows
    per = base // rows
    lanes = lane_index((base, LANES))
    sign = jnp.where(lanes < 64, 1.0, -1.0).astype(F32)

    def minus_i(z):
        return spin(z, 64) * sign

    def plus_i(z):
        return spin(z, 64) * -sign

    fields = [
        jnp.concatenate(
            [half[t * per + k] for k in range(per) for half in (early, late)], axis=0
        )
        for t in range(RADIX)
    ]
    mixed = eighths(fields, minus_i)
    table = turns[...]
    cosines = [table[:, r : r + 1] for r in range(RADIX)]
    sines = [table[:, RADIX + r : RADIX + r + 1] * sign for r in range(RADIX)]
    mixed = [mixed[0]] + [
        mixed[r] * cosines[r] + spin(mixed[r], 64) * sines[r] for r in range(1, RADIX)
    ]
    tables = (both[: 2 * base], both[2 * base :])
    product = exact_dot(tables, split(jnp.concatenate(mixed, axis=1)))
    kx = wave[0:1, :]
    first = lanes % 64 < 32
    edge = jnp.float32(length // 2)
    alone = jnp.where(first, kx * kx, 0.0)
    slope = jnp.where(first | (kx == -edge), 0.0, jnp.broadcast_to(kx, lanes.shape))
    q = lax.broadcasted_iota(jnp.int32, lanes.shape, 0)
    low_ky = RADIX * (q - jnp.where(q < base // 2, 0, base)).astype(F32)
    terms = []
    for r in range(RADIX):
        at = slice(r * LANES, (r + 1) * LANES)
        spectrum = product[:base, at] + minus_i(product[base:, at])
        ky = low_ky + float(r)
        symbol = alone + slope * ky
        if r == 0:
            corner = jnp.where((kx == -edge) & ~first, edge * edge, 0.0)
            symbol = jnp.where(ky == -edge, jnp.where(first, alone, corner), symbol)
        terms.append(symbol * pl.reciprocal(kx * kx + ky * ky) * spectrum)
    pairs = [
        jnp.where(first, low + spin(low, -32), high + spin(high, 32))
        for low, high in zip(terms[:4], terms[4:])
    ]
    product = exact_dot(tables, split(jnp.concatenate(pairs, axis=1)))
    mixed = []
    for r in range(RADIX // 2):
        at = slice(r * LANES, (r + 1) * LANES)
        value = product[:base, at] + plus_i(product[base:, at])
        cosine = jnp.where(first, cosines[r], cosines[r + 4])
        sine = jnp.where(first, sines[r], sines[r + 4])
        value = value * cosine - spin(value, 64) * sine
        value = jnp.where(first, value + spin(value, -32), spin(value, 32) - value)
        if r == 2:
            value = jnp.where(first, value, plus_i(value))
        elif r:
            turned = plus_i(value)
            odd = value + turned if r == 1 else turned - value
            value = jnp.where(first, value, ROOT * odd)
        mixed.append(value)
    even, odd = mixed[0] + mixed[2], mixed[0] - mixed[2]
    side, turned = mixed[1] + mixed[3], plus_i(mixed[1] - mixed[3])
    for t, values in enumerate((even + side, odd + turned, even - side, odd - turned)):
        start = MARGIN + 2 * t * base
        held[start : start + base, :] = values
        held[start + base : start + 2 * base, :] = spin(values, -32)
    held[0:MARGIN, :] = held[length : length + MARGIN, :]
    held[length + MARGIN : length + 2 * MARGIN, :] = held[MARGIN : 2 * MARGIN, :]
    total = early_total[...] + late_total[...]
    spare = total + spin(total, 32)
    kept = rows + 2 * MARGIN // count_x
    half = out.shape[1]
    rest = kept - half
    low = lane_index((8, LANES)) % 64 < 32
    for target in range(count):
        start = (target // count_x) * block + (target % count_x) * kept
        for row in range(0, half, 8):
            a = held[start + row : start + row + 8, :]
            if row < rest:
                b = spin(held[start + half + row : start + half + row + 8, :], 32)
            else:
                b = spare
            out[target, row : row + 8, :] = jnp.where(low, a, b)


def inverse_x_kernel(
    kept, scale, place, lines, tables, turns, *refs
):
    *outs, held = refs
    count, half, _ = lines.shape
    base = turns.shape[1]
    length = RADIX * base
    rest = kept - half
    low = lane_index((half, LANES)) % 64 < 32
    groups, spare = [], None
    for first in range(0, count, 2):
        even, odd = lines[first], lines[first + 1]
        a = jnp.where(low, even, spin(odd, 32))
        b = jnp.where(low, spin(even, -32), odd)
        groups.append(jnp.concatenate([a, b[:rest]], axis=0))
        extra = b[rest : rest + 8]
        spare = extra if spare is None else spare + extra
    mean = jnp.sum(spare) * scale
    wide = 2 * base // LANES
    narrow = base // LANES
    stacked = jnp.concatenate(
        [jnp.concatenate(groups[i * wide : (i + 1) * wide], axis=1) for i in range(3)], axis=0
    )
    at = 3 * wide
    zeros = jnp.concatenate(groups[at : at + narrow], axis=1)
    mids = jnp.concatenate(groups[at + narrow : at + 2 * narrow], axis=1)
    full, zero, middle = x_parts(tables, base)
    full = exact_dot(split(stacked), full)
    zero = exact_dot(split(zeros), zero) * scale
    mid = exact_dot(split(mids), middle) * scale
    turned = []
    for i in range(3):
        real = full[i * kept : (i + 1) * kept, :base]
        imag = full[i * kept : (i + 1) * kept, base:]
        c = turns[i : i + 1, :] * (2.0 * scale)
        s = turns[i + 3 : i + 4, :] * (2.0 * scale)
        turned.append((real * c - imag * s, real * s + imag * c))
    for t in range(RADIX):
        value = zero + mid if t % 2 == 0 else zero - mid
        for i, (real, imag) in enumerate(turned):
            eighth = t * (i + 1) % RADIX
            c = (1.0, ROOT, 0.0, -ROOT, -1.0, -ROOT, 0.0, ROOT)[eighth]
            s = (0.0, ROOT, 1.0, ROOT, 0.0, -ROOT, -1.0, -ROOT)[eighth]
            if c:
                value = value + c * real
            if s:
                value = value - s * imag
        held[:, t * base : (t + 1) * base] = mean - value
    targets, local = len(outs), outs[0].shape[1] - LANES
    right = lane_index((kept, LANES)) < 64
    for mask, out in enumerate(outs):
        start = pl.multiple_of((place[0] ^ mask) * local, LANES)
        after = pl.multiple_of(jnp.where(start + local == length, 0, start + local), LANES)
        before = pl.multiple_of(jnp.where(start == 0, length, start) - LANES, LANES)
        out[:, :local] = held[:, pl.ds(start, local)]
        out[:, local:] = jnp.where(
            right, held[:, pl.ds(after, LANES)], held[:, pl.ds(before, LANES)]
        )


def slopes_x(parts, band, with_edge):
    tiles = parts[0].shape[-1] // LANES
    pieces = []
    for first in list(range(0, tiles - 1, 2)) + ([tiles - 1] if with_edge else []):
        steps = (-1, 0, 1, 2) if first < tiles - 1 else (-1, 0, 1)
        table = band[...] if first < tiles - 1 else band[: 3 * LANES, :LANES]
        order = [(first + step) % tiles for step in steps]
        piece = None
        for part in parts:
            term = dot(jnp.concatenate([lane_tile(part, t) for t in order], axis=1), table)
            piece = term if piece is None else piece + term
        pieces.append(piece)
    return jnp.concatenate(pieces, axis=1)


def slope_y(read):
    value = read(3) - read(-3)
    for index in (0, 1):
        value = value + whole_weights[index] * (read(index + 1) - read(-index - 1))
    return value


def edged(k, side, center, up, down, above, below, sides, has, first=0):
    step = pl.program_id(0) + first
    tile, width = center.shape
    tall = sides.shape[1]
    last = (tall - LANES) // tile - 1
    base = pl.multiple_of(step * tile, 8)
    before = pl.multiple_of(jnp.where(step == 0, tall, base) - HALO, 8)
    over = jnp.where(step == 0, strip(above, k, True) * has[2], up)
    under = jnp.where(step == last, strip(below, k, False) * has[3], down)
    rows = (
        (over, sides[side, pl.ds(before, HALO), :]),
        (center, sides[side, pl.ds(base, tile), :]),
        (under, sides[side, pl.ds(pl.multiple_of(base + tile, 8), HALO), :]),
    )
    return jnp.concatenate([jnp.concatenate(pair, axis=1) for pair in rows], axis=0)


def edged_open(k, side, wall, wall_up, wall_down, above, below, sides, has, first=0):
    open_cells = [1.0 - ref[0].astype(F32) for ref in (wall, wall_up, wall_down)]
    return edged(k, side, *open_cells, above, below, sides, has, first)


def quiet_step_kernel(
    first, has, place, center, up, down, wall, wall_up, wall_down, above, below, sides, across, along, along_inner, out, shown_open, mark
):
    parts, _, tile, width = center.shape
    high = tile + 2 * HALO
    opened = edged_open(parts, parts, wall, wall_up, wall_down, above, below, sides, has, first)
    values = []
    for k in range(parts):
        value = edged(
            k,
            k,
            center[k, 0].astype(F32),
            up[k, 0].astype(F32)[up.shape[2] - HALO :],
            down[k, 0].astype(F32)[:HALO],
            above,
            below,
            sides,
            has,
            first,
        )
        values.append(value)

    def drops(x, along_b, along_p):
        diverge = x[1] + along_b
        return (
            diverge + mean_flow * x[0],
            x[3] + mean_flow * x[1],
            along_p + mean_flow * x[2],
            diverge + mean_flow * x[3],
        )

    short = [value.astype(BF16) for value in values]
    x = slopes_x((jnp.concatenate(short, axis=0),), across, True)
    x = [x[k * high : (k + 1) * high] for k in range(parts)]
    table = along[...]
    dropped = drops(x, dot(table, short[2]), dot(table, short[3]))
    middle = [opened * (v - (time_step / 60.0) * d) for v, d in zip(values, dropped)]
    inner = slice(HALO, HALO + tile)
    x = slopes_x(split(jnp.concatenate([value[inner] for value in middle], axis=0)), across, False)
    x = [x[k * tile : (k + 1) * tile] for k in range(parts)]
    table = along_inner[...]
    y = [sum(dot(table, part) for part in split(middle[k][:, :width])) for k in (2, 3)]
    dropped = drops(x, *y)
    shown = opened[inner, :width]
    for k in range(parts):
        start = 0.5 * values[k][inner, :width] - (0.5 * time_step / 60.0) * dropped[k]
        out[k] = shown * start + 0.5 * middle[k][inner, :width]
    shown_open[0] = opened.astype(BF16)
    mark[0] = place[0]


def source_kernel(place, squares, opened, rise_x, rise_y, quiet, across, *refs):
    *lines, out, squared, cells_open, matrix, rows_matrix, calm, band, held, raised, forced, done, fetched, kept = refs
    steps = done.shape[0]
    tile, width = calm.shape[2:]
    high = tile + 2 * HALO
    rows = lines[0].shape[0]

    def calm_copy(k):
        part = quiet.at[:, pl.ds(k * tile, tile), :]
        return pltpu.make_async_copy(part, calm.at[k % 2], fetched.at[k % 2])

    def done_copy(k):
        part = out.at[:, 0, pl.ds(k * tile, tile), :]
        return pltpu.make_async_copy(done.at[k], part, kept.at[k])

    arrays = [(squares, squared), (rise_x, matrix), (rise_y, rows_matrix), (opened, cells_open), (across, band)]
    copies = [
        pltpu.make_async_copy(source, target, fetched.at[2 + k])
        for k, (source, target) in enumerate(arrays)
    ]
    pieces = [
        pltpu.make_async_copy(
            piece,
            held.at[pl.ds(pl.multiple_of((place[0] ^ mask) * rows, 8), rows), :],
            fetched.at[2 + len(arrays) + mask],
        )
        for mask, piece in enumerate(lines)
    ]
    for copy in pieces + copies:
        copy.start()
    calm_copy(0).start()
    calm_copy(1).start()
    for copy in pieces + copies[:2]:
        copy.wait()

    level = held[MARGIN - HALO : MARGIN - HALO + squared.shape[0], :] - squared[...]
    count = level.shape[1] // LANES
    near = lane_index((level.shape[0], LANES)) < 64
    for k in range(count):
        after, before = lane_tile(level, (k + 1) % count), lane_tile(level, (k - 1) % count)
        around = jnp.concatenate([lane_tile(level, k), jnp.where(near, after, before)], axis=1)
        lanes = 2 * LANES if k < count - 1 else LANES
        value = split(exact_dot(split(around), split(matrix[k][:, :lanes])))
        for part in range(2):
            raised[part, :, 2 * k * LANES : 2 * k * LANES + lanes] = value[part]
    for copy in copies[2:]:
        copy.wait()

    reach = rows_matrix.shape[2] // 3
    third = lane_index((high, 3 * reach)) >= 2 * reach
    for k in range(steps):
        start = k * (tile // 2)
        window = [raised[part, start : start + reach, :] for part in (0, 1, 0)]
        weights = split(rows_matrix[k])
        weights = jnp.where(third, weights[1], weights[0])
        free = time_step * cells_open[k].astype(F32)
        value = free * dot(weights, jnp.concatenate(window, axis=0))
        forced[k % 2] = value
        inner = value[HALO : HALO + tile]
        shown = (0.5 / 60.0) * free[HALO : HALO + tile, :width]
        x = shown * slopes_x(split(inner), band, False)
        y = shown * slope_y(lambda d: forced[k % 2, HALO + d : HALO + d + tile, :width])
        calm_copy(k).wait()
        still = calm.at[k % 2]
        done[k, 0] = still[0].astype(BF16)
        done[k, 1] = (still[1] - x).astype(BF16)
        done[k, 2] = (still[2] - y).astype(BF16)
        done[k, 3] = (still[3] + inner[:, :width] - mean_flow * x).astype(BF16)
        done_copy(k).start()
        if k + 2 < steps:
            calm_copy(k + 2).start()
    for k in range(steps):
        done_copy(k).wait()


def call(
    kernel, operands, outs, scratch=(), steps=0, specs=None, out_specs=None, after=(), aliases=None, megabytes=24, flops=0, moved=0, name=None
):
    count = len(operands)

    def body(*refs):
        kernel(*refs[:count], *refs[count + len(after) :])

    def whole(array):
        zeros = (0,) * len(array.shape)
        return pl.BlockSpec(array.shape, lambda *_: zeros)

    arguments = {}
    chosen = specs or {}
    if steps:
        arguments["grid"] = (steps,)
        in_specs = [chosen.get(i, whole(o)) for i, o in enumerate(operands)]
        arguments["out_specs"] = jax.tree.map(whole, outs) if out_specs is None else out_specs
    else:
        local = pl.BlockSpec(memory_space=pltpu.VMEM)
        in_specs = [chosen.get(i, local) for i in range(count)]
        if out_specs is not None:
            arguments["out_specs"] = out_specs
    return pl.pallas_call(
        body,
        out_shape=outs,
        in_specs=in_specs + [pl.BlockSpec(memory_space=pl.ANY)] * len(after),
        scratch_shapes=list(scratch),
        input_output_aliases=aliases or {},
        compiler_params=pltpu.CompilerParams(vmem_limit_bytes=megabytes << 20),
        cost_estimate=pl.CostEstimate(flops=flops, bytes_accessed=moved, transcendentals=0),
        name=name,
        **arguments,
    )(*operands, *after)


def ring(array, axis, step):
    size = lax.axis_size(axis)
    return lax.ppermute(array, axis, [(i, (i + step) % size) for i in range(size)])


def swap(array, axis, mask):
    return lax.ppermute(array, axis, [(i, i ^ mask) for i in range(lax.axis_size(axis))])


def shaped(*shape, kind=F32):
    return jax.ShapeDtypeStruct(shape, kind)


def pressure_lines(pieces, place_x, gathered, spread, stepped):
    _, rows, local_x = pieces[0][0].shape
    count_x, count_y = lax.axis_size("gx"), lax.axis_size("gy")
    count = count_x * count_y
    scalars = {0: pl.BlockSpec(memory_space=pltpu.SMEM)}
    length_x, length_y = local_x * count_x, 2 * rows * count
    full, zero, middle, cos_turn, sin_turn = x_tables(length_x)
    turns = np.zeros((8, cos_turn.shape[1]), np.float32)
    turns[0:3], turns[3:6] = cos_turn, sin_turn
    forward_tables = np.concatenate([beside(full), beside(zero, middle)])
    halves_sent, totals = [], []
    for part, before in zip(pieces, ((), gathered)):
        spectra, total = call(
            forward_x_kernel,
            (place_x, *part, forward_tables, turns),
            (shaped(count, rows, LANES), shaped(8, LANES)),
            (pltpu.VMEM((count_x, 2, rows, local_x), F32),),
            specs=scalars,
            after=before,
            flops=5 * 10**8,
            moved=3 << 20,
            name="forward_x",
        )
        halves_sent.append(lax.all_to_all(spectra, ("gy", "gx"), 0, 0, tiled=True))
        totals.append(total)
    rows *= 2
    place = lax.axis_index("gy") * count_x + lax.axis_index("gx")
    waves = jnp.asarray(wave_table(length_x, count))
    wave = lax.dynamic_slice(waves, (place, 0), (1, LANES))
    both, turns_y = y_tables(length_y)
    kept = rows + 2 * MARGIN // count_x
    half = (kept // 2 + 8) // 8 * 8
    solved = call(
        functools.partial(solve_y_kernel, count_x),
        (spread, *halves_sent, *totals, wave, beside(both), turns_y),
        shaped(count, half, LANES),
        (pltpu.VMEM((length_y + 2 * MARGIN, LANES), F32),),
        specs=scalars,
        flops=4 * 10**9,
        moved=6 << 20,
        name="solve_y",
    )
    solved = lax.all_to_all(solved, ("gy", "gx"), 0, 0, tiled=True)
    back = 2.0 * zero.T
    back[LANES // 2] *= 0.5
    tables = np.concatenate(
        [beside(full.T), beside(back, 2.0 * middle.T)]
    )
    pressed = call(
        functools.partial(inverse_x_kernel, kept, 1.0 / (length_x * length_y)),
        (stepped, solved, tables, turns),
        (shaped(kept, local_x + LANES),) * count_x,
        (pltpu.VMEM((kept, length_x), F32),),
        specs=scalars,
        flops=10**9,
        moved=4 << 20,
        name="inverse_x",
    )
    return [piece if mask == 0 else swap(piece, "gx", mask) for mask, piece in enumerate(pressed)]


def refine_tables(weights_x, weights_y, tall, wide):
    first = lax.axis_index("gx") * wide
    ends = jnp.concatenate([weights_x[:, -LANES:], weights_x, weights_x[:, :LANES]], axis=1)
    own = lax.dynamic_slice(ends, (0, first), (4, wide + 2 * LANES))
    half = LANES // 2
    edge = jnp.concatenate([own[:, wide + LANES : wide + LANES + half], own[:, half:LANES]], axis=1)
    edge = jnp.pad(edge, ((0, 0), (0, LANES)))
    tiles = wide // (2 * LANES)
    weights = jnp.concatenate([own[:, LANES : wide + LANES], edge], axis=1)
    weights = weights.reshape(4, tiles + 1, 1, 2 * LANES)
    fine = np.arange(2 * LANES)
    targets = np.tile(fine // 2 - 1, (tiles + 1, 1))
    targets[tiles] = np.where(fine < half, fine // 2 - 1, half + fine // 2 - 1)
    cells = lax.broadcasted_iota(jnp.int32, (tiles + 1, 2 * LANES, 2 * LANES), 1)
    targets = jnp.asarray(targets[:, None, :].astype(np.int32))
    rise_x = sum(
        jnp.where(cells == (targets + t) % (2 * LANES), weights[t], 0.0) for t in range(4)
    )
    ends = jnp.concatenate([weights_y[:, -HALO:], weights_y, weights_y[:, :HALO]], axis=1)
    own = lax.dynamic_slice(ends, (0, lax.axis_index("gy") * tall), (4, tall + 2 * HALO))
    high, steps = TILE + 2 * HALO, tall // TILE
    own = jnp.stack([own[:, k * TILE : k * TILE + high] for k in range(steps)], axis=1)
    reach = high // 2 + HALO
    cells = lax.broadcasted_iota(jnp.int32, (steps, high, 3 * reach), 2) % reach
    targets = lax.broadcasted_iota(jnp.int32, cells.shape, 1) // 2 + (HALO // 2 - 1)
    rise_y = sum(jnp.where(cells == targets + s, own[s][:, :, None], 0.0) for s in range(4))
    return rise_x, rise_y


def fast_shards(velocity, weights_x, weights_y, acoustic, wall_mask):
    parts, _, tall, wide = acoustic.shape
    _, _, local_y, local_x = velocity.shape
    count_x, count_y = lax.axis_size("gx"), lax.axis_size("gy")
    place_x, place_y = lax.axis_index("gx"), lax.axis_index("gy")
    full, high, steps = wide + LANES, TILE + 2 * HALO, tall // TILE
    strips = (parts + 2) * HALO
    small = 2 * HALO
    has = jnp.stack([place_x > 0, place_x < count_x - 1, place_y > 0, place_y < count_y - 1])
    has = has.astype(F32)
    scalars = pl.BlockSpec(memory_space=pltpu.SMEM)

    def at(block, *index):
        return pl.BlockSpec(block, lambda i: index)

    own = place_x.astype(jnp.int32).reshape(1)
    sent = call(
        pieces_kernel,
        (own, velocity),
        (shaped(2, local_y // (2 * count_x), local_x),) * (2 * count_x),
        specs={0: scalars},
        moved=2 << 20,
        megabytes=8,
        name="pieces",
    )
    moved = [piece if k % count_x == 0 else swap(piece, "gx", k % count_x) for k, piece in enumerate(sent)]
    moved = (moved[:count_x], moved[count_x:])
    first, last = call(
        rows_kernel,
        (acoustic, acoustic, wall_mask, wall_mask, velocity, velocity),
        (shaped(STRIP_ROWS, wide),) * 2,
        steps=1,
        specs={
            0: at((parts, 1, small, wide), 0, 0, 0, 0),
            1: at((parts, 1, small, wide), 0, 0, tall // small - 1, 0),
            2: at((1, HALO, wide), 0, 0, 0),
            3: at((1, HALO, wide), 0, tall // HALO - 1, 0),
            4: at((1, 1, HALO, local_x), 1, 0, 0, 0),
            5: at((1, 1, HALO, local_x), 1, 0, local_y // HALO - 1, 0),
        },
        after=moved[0][1:2],
        moved=2 << 20,
        megabytes=54,
        name="rows",
    )
    above, below = ring(last, "gy", 1), ring(first, "gy", -1)
    to_right, to_left = call(
        columns_kernel,
        (has, acoustic, acoustic, wall_mask, wall_mask, velocity, velocity, above, below),
        (shaped(strips, tall + LANES), shaped(strips, tall + LANES)),
        steps=1,
        specs={
            0: scalars,
            1: at((parts, 1, tall, LANES), 0, 0, 0, 0),
            2: at((parts, 1, tall, LANES), 0, 0, 0, wide // LANES - 1),
            3: at((1, tall, LANES), 0, 0, 0),
            4: at((1, tall, LANES), 0, 0, wide // LANES - 1),
            5: at((1, 1, local_y, LANES), 1, 0, 0, 0),
            6: at((1, 1, local_y, LANES), 1, 0, 0, local_x // LANES - 1),
        },
        moved=8 << 20,
        megabytes=54,
        name="columns",
    )
    from_left, from_right = ring(to_right, "gx", 1), ring(to_left, "gx", -1)
    sides, squares, beside = call(
        sides_kernel,
        (has, own, velocity, above, below, from_left, from_right),
        (
            shaped(parts + 1, tall + LANES, LANES),
            shaped(local_y + 2 * HALO, local_x + LANES),
            shaped(1, kind=jnp.int32),
        ),
        steps=1,
        specs={0: scalars, 1: scalars, 2: at((1, 1, local_y, local_x), 1, 0, 0, 0)},
        out_specs=(
            at((parts + 1, tall + LANES, LANES), 0, 0, 0),
            at((local_y + 2 * HALO, local_x + LANES), 0, 0),
            scalars,
        ),
        moved=8 << 20,
        megabytes=54,
        name="sides",
    )
    across, along = band_tables(high)
    along_inner = along[HALO : HALO + TILE]
    per, rows = TILE // small, TILE // HALO

    def tiled(first):
        walls = (
            pl.BlockSpec((1, TILE, wide), lambda i: (0, i + first, 0)),
            pl.BlockSpec((1, HALO, wide), lambda i: (0, jnp.maximum((i + first) * rows - 1, 0), 0)),
            pl.BlockSpec(
                (1, HALO, wide),
                lambda i: (0, jnp.minimum((i + first + 1) * rows, steps * rows - 1), 0),
            ),
        )
        cells = (
            pl.BlockSpec((parts, 1, TILE, wide), lambda i: (0, 0, i + first, 0)),
            pl.BlockSpec(
                (parts, 1, small, wide), lambda i: (0, 0, jnp.maximum((i + first) * per - 1, 0), 0)
            ),
            pl.BlockSpec(
                (parts, 1, small, wide),
                lambda i: (0, 0, jnp.minimum((i + first + 1) * per, steps * per - 1), 0),
            ),
        )
        return cells, walls, pl.BlockSpec((parts, TILE, wide), lambda i: (0, i + first, 0))

    def quiet_tiles(first, count, before):
        cells, walls, flat = tiled(first)
        operands = (has, own, acoustic, acoustic, acoustic, wall_mask, wall_mask, wall_mask, above, below, sides)
        operands = operands + (across, along, along_inner)
        return call(
            functools.partial(quiet_step_kernel, first),
            operands,
            (shaped(parts, tall, wide), shaped(steps, high, full, kind=BF16), shaped(1, kind=jnp.int32)),
            steps=count,
            specs=dict(enumerate((scalars, scalars) + cells + walls)),
            out_specs=(flat, pl.BlockSpec((1, high, full), lambda i: (i + first, 0, 0)), scalars),
            after=before,
            aliases={len(operands): 0, len(operands) + 1: 1} if before else None,
            megabytes=54,
            flops=3 * 10**9 * count,
            moved=(12 << 20) * count,
            name="quiet_step",
        )

    early = max(steps * 3 // 4, 1)
    *begun, stepped = quiet_tiles(0, early, ())
    quiet, opened = begun
    if early < steps:
        quiet, opened, _ = quiet_tiles(early, steps - early, begun)
    rows_done = above[:8, :LANES] + below[:8, :LANES]
    lines = pressure_lines(moved, own, (rows_done,), beside, stepped)
    rise_x, rise_y = refine_tables(weights_x, weights_y, tall, wide)
    operands = (own, squares, opened, rise_x, rise_y, quiet, across, *lines)
    anywhere = pl.BlockSpec(memory_space=pl.ANY)
    specs = {k: anywhere for k in range(1, len(operands))}
    scratch = (
        pltpu.VMEM(squares.shape, F32),
        pltpu.VMEM(opened.shape, BF16),
        pltpu.VMEM(rise_x.shape, F32),
        pltpu.VMEM(rise_y.shape, F32),
        pltpu.VMEM((2, parts, TILE, wide), F32),
        pltpu.VMEM(across.shape, BF16),
        pltpu.VMEM((local_y + 2 * MARGIN, local_x + LANES), F32),
        pltpu.VMEM((2, local_y + 2 * HALO, full), BF16),
        pltpu.VMEM((2, high, full), F32),
        pltpu.VMEM((steps, parts, TILE, wide), BF16),
        pltpu.SemaphoreType.DMA((7 + count_x,)),
        pltpu.SemaphoreType.DMA((steps,)),
    )
    return call(
        source_kernel,
        operands,
        shaped(*acoustic.shape, kind=BF16),
        scratch,
        specs={0: scalars, **specs},
        out_specs=anywhere,
        megabytes=56,
        flops=4 * 10**9,
        moved=16 << 20,
        name="source_step",
    )


def fits(count_x, count_y, velocity, acoustic):
    _, planes, local_y, local_x = velocity
    _, _, tall, wide = acoustic
    length_x, length_y = local_x * count_x, local_y * count_y
    rows = local_y // count_x
    base_x, base_y = length_x // RADIX, length_y // RADIX
    return (
        planes == 1
        and acoustic[0] == PARTS
        and length_x * 2 == count_x * count_y * LANES
        and base_x % (2 * LANES) == 0
        and local_x % base_x == 0
        and rows % 16 == 0
        and base_y % rows == 0
        and base_y % 8 == 0
        and MARGIN * 2 % (8 * count_x) == 0
        and tall == 2 * local_y
        and wide == 2 * local_x
        and tall % TILE == 0
        and tall >= 2 * TILE
        and count_x & (count_x - 1) == 0
        and wide % (2 * LANES) == 0
    )


def extended(array, sides, width):
    for axis, dim in sides:
        size, length = (lax.axis_size(axis), array.shape[dim])
        up = [(i, (i + 1) % size) for i in range(size - 1)]
        down = [(j, i) for i, j in up]
        last = lax.slice_in_dim(array, length - width, length, axis=dim)
        leading = lax.slice_in_dim(array, 0, width, axis=dim)
        before = lax.ppermute(last, axis, up)
        after = lax.ppermute(leading, axis, down)
        array = jnp.concatenate([before, array, after], axis=dim)
    return array


def gradients(padded):
    height = padded.shape[-2] - 6
    breadth = padded.shape[-1] - 6
    rows_mid = padded[..., 3 : 3 + height, :]
    cols_mid = padded[..., :, 3 : 3 + breadth]
    along_x = jnp.zeros_like(padded[..., 3 : 3 + height, 3 : 3 + breadth])
    along_y = jnp.zeros_like(along_x)
    for index, weight in enumerate(stencil_weights):
        distance = index + 1
        along_x = along_x + weight * (
            rows_mid[..., 3 + distance : 3 + distance + breadth]
            - rows_mid[..., 3 - distance : 3 - distance + breadth]
        )
        along_y = along_y + weight * (
            cols_mid[..., 3 + distance : 3 + distance + height, :]
            - cols_mid[..., 3 - distance : 3 - distance + height, :]
        )
    return (along_x, along_y)


def tendency(padded, source):
    along_x, along_y = gradients(padded)
    diverge = along_x[1] + along_y[2]
    forcing = jnp.stack([-diverge, -along_x[3], -along_y[3], source - diverge])
    return forcing - mean_flow * along_x


def spectral_index(flat, length):
    second = length // 16
    wave = flat // second + 16 * (flat % second)
    return jnp.where(wave < length // 2, wave, wave - length).astype(jnp.float32)


def twiddles(rows_count, cols_count, modulus, sign):
    products = jnp.arange(rows_count)[:, None] * jnp.arange(cols_count)[None, :] % modulus
    angles = 2.0 * math.pi / modulus * products.astype(jnp.float32)
    return (jnp.cos(angles), sign * jnp.sin(angles))


def mix_rows(real_part, imag_part, cosine, sine):
    exact = lax.Precision.HIGHEST
    cos_real = jnp.einsum("ka,...ab->...kb", cosine, real_part, precision=exact)
    cos_imag = jnp.einsum("ka,...ab->...kb", cosine, imag_part, precision=exact)
    sin_real = jnp.einsum("ka,...ab->...kb", sine, real_part, precision=exact)
    sin_imag = jnp.einsum("ka,...ab->...kb", sine, imag_part, precision=exact)
    return (cos_real - sin_imag, cos_imag + sin_real)


def mix_cols(real_part, imag_part, cosine, sine):
    exact = lax.Precision.HIGHEST
    cos_real = jnp.einsum("...kb,bc->...kc", real_part, cosine, precision=exact)
    cos_imag = jnp.einsum("...kb,bc->...kc", imag_part, cosine, precision=exact)
    sin_real = jnp.einsum("...kb,bc->...kc", real_part, sine, precision=exact)
    sin_imag = jnp.einsum("...kb,bc->...kc", imag_part, sine, precision=exact)
    return (cos_real - sin_imag, cos_imag + sin_real)


def rotate(real_part, imag_part, cosine, sine):
    return (real_part * cosine - imag_part * sine, real_part * sine + imag_part * cosine)


def discrete(real_part, imag_part, sign):
    length = real_part.shape[-1]
    second = length // 16
    initial = real_part.shape
    folded = initial[:-1] + (16, second)
    real_part = real_part.reshape(folded)
    imag_part = imag_part.reshape(folded)
    small_cos, small_sin = twiddles(16, 16, 16, sign)
    large_cos, large_sin = twiddles(second, second, second, sign)
    turn_cos, turn_sin = twiddles(16, second, length, sign)
    if sign < 0:
        real_part, imag_part = mix_rows(real_part, imag_part, small_cos, small_sin)
        real_part, imag_part = rotate(real_part, imag_part, turn_cos, turn_sin)
        real_part, imag_part = mix_cols(real_part, imag_part, large_cos, large_sin)
    else:
        real_part, imag_part = mix_cols(real_part, imag_part, large_cos, large_sin)
        real_part, imag_part = rotate(real_part, imag_part, turn_cos, turn_sin)
        real_part, imag_part = mix_rows(real_part, imag_part, small_cos, small_sin)
        real_part = real_part / length
        imag_part = imag_part / length
    return (real_part.reshape(initial), imag_part.reshape(initial))


def transform(stacked, sign, kind):
    if kind == "real_in":
        real_part = stacked
        imag_part = jnp.zeros_like(stacked)
    else:
        half = stacked.shape[0] // 2
        real_part = stacked[:half]
        imag_part = stacked[half:]
    real_out, imag_out = discrete(real_part, imag_part, sign)
    if kind == "real_out":
        return real_out
    return jnp.concatenate([real_out, imag_out], axis=0)


def project(stacked, wave_x, wave_y):
    coef_xx = wave_x * wave_x
    coef_xy = 2.0 * wave_x * wave_y
    coef_yy = wave_y * wave_y
    denominator = wave_x * wave_x + wave_y * wave_y
    positive = denominator > 0
    safe = jnp.where(positive, denominator, 1.0)

    def combine(parts):
        numerator = -(coef_xx * parts[0] + coef_xy * parts[1] + coef_yy * parts[2])
        return jnp.where(positive, numerator / safe, 0.0)

    return jnp.stack([combine(stacked[:3]), combine(stacked[3:])])


def refine(stacked, weights):
    result = jnp.zeros(stacked.shape[:-1] + (2 * stacked.shape[-1],), jnp.float32)
    for offset in range(4):
        result = (
            result
            + jnp.repeat(jnp.roll(stacked, 1 - offset, axis=-1), 2, axis=-1) * weights[offset]
        )
    return result


def lines_x(stacked, action):
    gathered = action(lax.all_to_all(stacked, "gx", split_axis=2, concat_axis=3, tiled=True))
    return lax.all_to_all(gathered, "gx", split_axis=3, concat_axis=2, tiled=True)


def lines_y(stacked, action):
    turned = jnp.swapaxes(stacked, 2, 3)
    gathered = action(lax.all_to_all(turned, "gy", split_axis=2, concat_axis=3, tiled=True))
    returned = lax.all_to_all(gathered, "gy", split_axis=3, concat_axis=2, tiled=True)
    return jnp.swapaxes(returned, 2, 3)


def expand(fields):
    return extended(fields, (("gx", 3), ("gy", 2)), 3)


def shards(velocity, weights_x, weights_y, acoustic, wall_mask):
    acoustic = acoustic.astype(jnp.float32)
    flow_x = velocity[0]
    flow_y = velocity[1]
    tensor = jnp.stack([flow_x * flow_x, flow_x * flow_y, flow_y * flow_y])
    count_gx = lax.axis_size("gx")
    count_gy = lax.axis_size("gy")
    place_x = lax.axis_index("gx")
    place_y = lax.axis_index("gy")
    local_y = tensor.shape[2]
    local_x = tensor.shape[3]
    length_x = local_x * count_gx
    length_y = local_y * count_gy

    def forward_real(portion):
        return transform(portion, -1, "real_in")

    def finish_x(portion):
        return refine(transform(portion, 1, "real_out"), weights_x)

    spectra = lines_x(tensor, forward_real)
    share_x = local_x // count_gy
    line_x = spectral_index(place_x * local_x + place_y * share_x + jnp.arange(share_x), length_x)[
        :, None
    ]
    line_y = spectral_index(jnp.arange(length_y), length_y)[None, :]

    def solve_y(portion):
        solved = project(transform(portion, -1, "complex"), line_x, line_y)
        return refine(transform(solved, 1, "complex"), weights_y)

    pressure = lines_y(spectra, solve_y)
    source = lines_x(pressure, finish_x)[0]
    open_cells = (1 - wall_mask).astype(jnp.float32)
    first_rate = tendency(expand(acoustic), source)
    middle = open_cells * (acoustic + time_step * first_rate)
    second_rate = tendency(expand(middle), source)
    return (open_cells * (acoustic + 0.5 * time_step * (first_rate + second_rate))).astype(
        jnp.bfloat16
    )


def solution(mesh):
    in_specs = (P(None, None, "gy", "gx"), P(), P(), P(None, None, "gy", "gx"), P(None, "gy", "gx"))
    out_specs = P(None, None, "gy", "gx")

    def chosen(velocity, weights_x, weights_y, acoustic, wall_mask):
        sizes = (mesh.shape["gx"], mesh.shape["gy"], velocity.shape, acoustic.shape)
        plan = fast_shards if fits(*sizes) else shards
        return plan(velocity, weights_x, weights_y, acoustic, wall_mask)

    return jax.shard_map(
        chosen, mesh=mesh, in_specs=in_specs, out_specs=out_specs, check_vma=False
    )
```

```python
import functools
import math

import jax
import jax.numpy as jnp
import ml_dtypes
import numpy as np
from jax import lax
from jax.experimental import pallas as pl
from jax.experimental.pallas import tpu as pltpu
from jax.sharding import PartitionSpec as P

stencil_weights = (0.75, -0.15, 1.0 / 60.0)
mean_flow = 0.3
time_step = 0.5
whole_weights = (45.0, -9.0, 1.0)

LANES = 128
RADIX = 8
HALO = 8
MARGIN = 16
TILE = 128
ROOT = math.sqrt(0.5)
STRIP = {2: (0, 6), 3: (6, 6), 1: (12, 3), 4: (15, 3), 5: (20, 4)}
STRIP_ROWS = 24
PARTS = 4
BF16 = jnp.bfloat16
F32 = jnp.float32


def halves(table):
    high = table.astype(np.float32).astype(ml_dtypes.bfloat16)
    low = (table - high.astype(np.float64)).astype(np.float32).astype(ml_dtypes.bfloat16)
    return high, low


def packed_columns(cosine, sine):
    half = LANES // 2
    parts = []
    for first in range(0, cosine.shape[1], half):
        parts += [cosine[:, first : first + half], sine[:, first : first + half]]
    return np.concatenate(parts, axis=1)


@functools.lru_cache(maxsize=None)
def x_tables(length):
    base = length // RADIX
    m = np.arange(base)[:, None]
    q = np.arange(base)[None, :]
    angle = 2.0 * np.pi * ((m * q) % base) / base
    cosine, sine = np.cos(angle), np.sin(angle)
    full = np.concatenate([packed_columns(cosine, -sine), packed_columns(sine, cosine)], axis=0)
    half = base // 2
    zero_cos, zero_sin = cosine[:, :half].copy(), -sine[:, :half]
    zero_cos[:, 0] = 0.0
    zero_sin = zero_sin.copy()
    zero_sin[:, 0] = (-1.0) ** np.arange(base)
    zero = packed_columns(zero_cos, zero_sin)
    shifted = 2.0 * np.pi * ((m * (RADIX * q[:, :half] + RADIX // 2)) % length) / length
    middle = packed_columns(np.cos(shifted), -np.sin(shifted))
    turns = 2.0 * np.pi * np.arange(1, RADIX // 2)[:, None] * np.arange(base)[None, :] / length
    return full, zero, middle, np.cos(turns), np.sin(turns)


@functools.lru_cache(maxsize=None)
def y_tables(length):
    base = length // RADIX
    index = np.arange(base)
    angle = 2.0 * np.pi * ((index[:, None] * index[None, :]) % base) / base
    both = np.concatenate([np.cos(angle), np.sin(angle)], axis=0)
    turns = 2.0 * np.pi * np.arange(RADIX)[:, None] * index[None, :] / length
    return both, np.concatenate([np.cos(turns), np.sin(turns)], axis=0).T.astype(np.float32)


@functools.lru_cache(maxsize=None)
def wave_table(length, count):
    slots = LANES // 4
    base = length // RADIX
    waves = []
    for residue in (1, 2, 3):
        waves.append(RADIX * np.arange(base) + residue)
    waves.append(RADIX * np.arange(base // 2))
    waves.append(RADIX * np.arange(base // 2) + RADIX // 2)
    waves = np.concatenate(waves)
    waves = np.where(waves == 0, length // 2, waves)
    waves = np.where(waves < length // 2, waves, waves - length).reshape(count, slots)
    return np.tile(waves, (1, 4)).astype(np.float32)


@functools.lru_cache(maxsize=None)
def band_tables(rows):
    across = np.zeros((4 * LANES, 2 * LANES))
    column = np.arange(2 * LANES)
    down = np.zeros((rows, rows))
    for index, weight in enumerate(whole_weights):
        distance = index + 1
        across[column + LANES + distance, column] = weight
        across[column + LANES - distance, column] = -weight
        down += weight * (np.eye(rows, k=distance) - np.eye(rows, k=-distance))
    return across.astype(ml_dtypes.bfloat16), down.astype(ml_dtypes.bfloat16)


def beside(*tables):
    high, low = halves(np.concatenate(tables, axis=1))
    return np.concatenate([high, low], axis=0)


def split(values):
    high = values.astype(BF16)
    return high, (values - high.astype(F32)).astype(BF16)


def dot(left, right):
    return jnp.dot(left, right, preferred_element_type=F32)


def exact_dot(left, right):
    left_high, left_low = left
    right_high, right_low = right
    return dot(left_high, right_high) + (dot(left_low, right_high) + dot(left_high, right_low))


def lane_index(shape):
    return lax.broadcasted_iota(jnp.int32, shape, len(shape) - 1)


def spin(values, shift):
    return pltpu.roll(values, shift % values.shape[-1], values.ndim - 1)


def lane_tile(values, index):
    return values[:, index * LANES : (index + 1) * LANES]


def x_parts(tables, base):
    wide = 2 * base
    full = (tables[:wide], tables[wide : 2 * wide])
    at = 2 * wide
    high, low = tables[at : at + base], tables[at + base : at + 2 * base]
    return full, (high[:, :base], low[:, :base]), (high[:, base:], low[:, base:])


def pieces_kernel(place, velocity, *pieces):
    rows = pieces[0].shape[1]
    count = len(pieces) // 2
    for k, piece in enumerate(pieces):
        start = (place[0] ^ (k % count)) * (2 * rows) + (k // count) * rows
        for c in range(2):
            piece[c] = velocity[c, 0, pl.ds(pl.multiple_of(start, 8), rows), :]


def rows_kernel(top, low, top_wall, low_wall, top_flow, low_flow, first, last):
    small, width = top.shape[2], top_flow.shape[3]
    first[...] = jnp.zeros(first.shape, F32)
    last[...] = jnp.zeros(last.shape, F32)
    for k, (start, rows) in STRIP.items():
        lanes = slice(0, width) if k == PARTS + 1 else slice(None)
        if k < PARTS:
            upper, lower = top[k, 0].astype(F32)[:HALO], low[k, 0].astype(F32)[small - HALO :]
        elif k == PARTS:
            upper, lower = 1.0 - top_wall[0].astype(F32), 1.0 - low_wall[0].astype(F32)
        else:
            upper, lower = top_flow[0, 0], low_flow[0, 0]
        first[start : start + rows, lanes] = upper[:rows]
        last[start : start + rows, lanes] = lower[HALO - rows :]


def strip(ref, k, upper, lanes=slice(None)):
    if k not in STRIP:
        return jnp.zeros((HALO, ref[0:1, lanes].shape[1]), F32)
    start, rows = STRIP[k]
    values = ref[start : start + rows, lanes]
    blank = jnp.zeros((HALO - rows, values.shape[1]), F32)
    return jnp.concatenate([blank, values] if upper else [values, blank], axis=0)


def columns_kernel(
    has, left, right, left_wall, right_wall, left_flow, right_flow, above, below, to_right, to_left
):
    parts = left.shape[0]
    wide, flow_wide = above.shape[1], above.shape[1] // 2
    gap = jnp.zeros((LANES - 2 * HALO, LANES), F32)

    def tall(k, inner, first, sides):
        lanes = slice(first, first + LANES)
        over, under = strip(above, k, True, lanes), strip(below, k, False, lanes)
        return jnp.concatenate([inner, under * sides[1], gap, over * sides[0]], axis=0).T

    for k in range(parts + 1):
        at = slice(k * HALO, (k + 1) * HALO)
        if k < parts:
            near, far = left[k, 0].astype(F32), right[k, 0].astype(F32)
        else:
            near, far = 1.0 - left_wall[0].astype(F32), 1.0 - right_wall[0].astype(F32)
        sides = (has[2], has[3])
        to_left[at, :] = tall(k, near, 0, sides)[:HALO]
        to_right[at, :] = tall(k, far, wide - LANES, sides)[LANES - HALO :]
    k = parts + 1
    at = slice(k * HALO, (k + 1) * HALO)
    size = left_flow.shape[2] + LANES
    blank = jnp.zeros((HALO, to_left.shape[1] - size), F32)
    to_left[at, :size] = tall(k, left_flow[0, 0], 0, (1.0, 1.0))[:HALO]
    to_right[at, :size] = tall(k, right_flow[0, 0], flow_wide - LANES, (1.0, 1.0))[LANES - HALO :]
    to_left[at, size:] = blank
    to_right[at, size:] = blank


def sides_kernel(has, place, velocity, above, below, from_left, from_right, sides, squares, mark):
    parts, tall, _ = sides.shape
    gap = jnp.zeros((LANES - 2 * HALO, tall), F32)
    for k in range(parts):
        at = slice(k * HALO, (k + 1) * HALO)
        tile = [from_right[at, :] * has[1], gap, from_left[at, :] * has[0]]
        sides[k] = jnp.concatenate(tile, axis=0).T
    at = slice(parts * HALO, (parts + 1) * HALO)
    rows, local = velocity.shape[2:]
    size = rows + LANES
    tile = [from_right[at, :size], gap[:, :size], from_left[at, :size]]
    tile = jnp.concatenate(tile, axis=0).T
    tile = tile * tile
    mark[0] = place[0]
    over, under = (strip(ref, parts, ref is above, slice(0, local)) for ref in (above, below))
    squares[:HALO, :local] = over * over
    squares[HALO : HALO + rows, :local] = velocity[0, 0] * velocity[0, 0]
    squares[HALO + rows :, :local] = under * under
    squares[:HALO, local:] = tile[size - HALO :]
    squares[HALO : HALO + rows, local:] = tile[:rows]
    squares[HALO + rows :, local:] = tile[rows : rows + HALO]


def forward_x_kernel(place, *refs):
    *pieces, tables, turns, out, total, lines = refs
    count, _, rows, local = lines.shape
    for mask, piece in enumerate(pieces):
        lines[place[0] ^ mask] = piece[...]
    base = turns.shape[1]
    per = local // base
    u = [lines[t // per, 0, :, (t % per) * base : (t % per + 1) * base] for t in range(RADIX)]
    v = [lines[t // per, 1, :, (t % per) * base : (t % per + 1) * base] for t in range(RADIX)]
    energy = sum(b * b for b in v)
    energy = jnp.sum(energy.reshape(rows // 8, 8, base), axis=0)
    total[...] = sum(energy[:, k : k + LANES] for k in range(0, base, LANES))
    fields = ([a * a - b * b for a, b in zip(u, v)], [2.0 * a * b for a, b in zip(u, v)])
    zeros, mids, reals, imags = [], [], [[], [], []], [[], [], []]
    for a in fields:
        s04, s26, s15, s37 = a[0] + a[4], a[2] + a[6], a[1] + a[5], a[3] + a[7]
        d04, d26, d15, d37 = a[0] - a[4], a[2] - a[6], a[1] - a[5], a[3] - a[7]
        zeros.append((s04 + s26) + (s15 + s37))
        mids.append((s04 + s26) - (s15 + s37))
        minus, plus = ROOT * (d15 - d37), ROOT * (d15 + d37)
        turned = (
            (d04 + minus, -d26 - plus),
            (s04 - s26, s37 - s15),
            (d04 - minus, d26 - plus),
        )
        for index, (real, imag) in enumerate(turned):
            c, s = turns[index : index + 1, :], turns[index + 3 : index + 4, :]
            reals[index].append(real * c + imag * s)
            imags[index].append(imag * c - real * s)
    stacked = jnp.concatenate(
        [
            jnp.concatenate([jnp.concatenate(reals[i], axis=0) for i in range(3)], axis=0),
            jnp.concatenate([jnp.concatenate(imags[i], axis=0) for i in range(3)], axis=0),
        ],
        axis=1,
    )
    full, zero, middle = x_parts(tables, base)
    full = exact_dot(split(stacked), full)
    zero = exact_dot(split(jnp.concatenate(zeros, axis=0)), zero)
    middle = exact_dot(split(jnp.concatenate(mids, axis=0)), middle)
    low = lane_index((rows, LANES)) % 64 < 32
    target = 0
    blocks = [full[2 * rows * i : 2 * rows * (i + 1)] for i in range(3)] + [zero, middle]
    for block in blocks:
        for first in range(0, block.shape[1], LANES):
            a = block[:rows, first : first + LANES]
            c = block[rows:, first : first + LANES]
            out[target] = jnp.where(low, a, spin(c, 32))
            out[target + 1] = jnp.where(low, spin(a, -32), c)
            target += 2


def eighths(x, turn):
    s04, s26, s15, s37 = x[0] + x[4], x[2] + x[6], x[1] + x[5], x[3] + x[7]
    d04, d26, d15, d37 = x[0] - x[4], x[2] - x[6], x[1] - x[5], x[3] - x[7]
    quarter = turn(s15 - s37)
    spun_26, spun_37 = turn(d26), turn(d37)
    one, three = d15 + spun_37, d15 - spun_37
    spun_one, spun_three = turn(one), turn(three)
    one = ROOT * (one + spun_one)
    three = ROOT * (spun_three - three)
    return [
        (s04 + s26) + (s15 + s37),
        (d04 + spun_26) + one,
        (s04 - s26) + quarter,
        (d04 - spun_26) + three,
        (s04 + s26) - (s15 + s37),
        (d04 + spun_26) - one,
        (s04 - s26) - quarter,
        (d04 - spun_26) - three,
    ]


def solve_y_kernel(count_x, _, early, late, early_total, late_total, wave, both, turns, out, held):
    count, rows, _ = early.shape
    rows *= 2
    base = turns.shape[0]
    length = count * rows
    block = count_x * rows
    per = base // rows
    lanes = lane_index((base, LANES))
    sign = jnp.where(lanes < 64, 1.0, -1.0).astype(F32)

    def minus_i(z):
        return spin(z, 64) * sign

    def plus_i(z):
        return spin(z, 64) * -sign

    fields = [
        jnp.concatenate(
            [half[t * per + k] for k in range(per) for half in (early, late)], axis=0
        )
        for t in range(RADIX)
    ]
    mixed = eighths(fields, minus_i)
    table = turns[...]
    cosines = [table[:, r : r + 1] for r in range(RADIX)]
    sines = [table[:, RADIX + r : RADIX + r + 1] * sign for r in range(RADIX)]
    mixed = [mixed[0]] + [
        mixed[r] * cosines[r] + spin(mixed[r], 64) * sines[r] for r in range(1, RADIX)
    ]
    tables = (both[: 2 * base], both[2 * base :])
    product = exact_dot(tables, split(jnp.concatenate(mixed, axis=1)))
    kx = wave[0:1, :]
    first = lanes % 64 < 32
    edge = jnp.float32(length // 2)
    alone = jnp.where(first, kx * kx, 0.0)
    slope = jnp.where(first | (kx == -edge), 0.0, jnp.broadcast_to(kx, lanes.shape))
    q = lax.broadcasted_iota(jnp.int32, lanes.shape, 0)
    low_ky = RADIX * (q - jnp.where(q < base // 2, 0, base)).astype(F32)
    terms = []
    for r in range(RADIX):
        at = slice(r * LANES, (r + 1) * LANES)
        spectrum = product[:base, at] + minus_i(product[base:, at])
        ky = low_ky + float(r)
        symbol = alone + slope * ky
        if r == 0:
            corner = jnp.where((kx == -edge) & ~first, edge * edge, 0.0)
            symbol = jnp.where(ky == -edge, jnp.where(first, alone, corner), symbol)
        terms.append(symbol * pl.reciprocal(kx * kx + ky * ky) * spectrum)
    pairs = [
        jnp.where(first, low + spin(low, -32), high + spin(high, 32))
        for low, high in zip(terms[:4], terms[4:])
    ]
    product = exact_dot(tables, split(jnp.concatenate(pairs, axis=1)))
    mixed = []
    for r in range(RADIX // 2):
        at = slice(r * LANES, (r + 1) * LANES)
        value = product[:base, at] + plus_i(product[base:, at])
        cosine = jnp.where(first, cosines[r], cosines[r + 4])
        sine = jnp.where(first, sines[r], sines[r + 4])
        value = value * cosine - spin(value, 64) * sine
        value = jnp.where(first, value + spin(value, -32), spin(value, 32) - value)
        if r == 2:
            value = jnp.where(first, value, plus_i(value))
        elif r:
            turned = plus_i(value)
            odd = value + turned if r == 1 else turned - value
            value = jnp.where(first, value, ROOT * odd)
        mixed.append(value)
    even, odd = mixed[0] + mixed[2], mixed[0] - mixed[2]
    side, turned = mixed[1] + mixed[3], plus_i(mixed[1] - mixed[3])
    for t, values in enumerate((even + side, odd + turned, even - side, odd - turned)):
        start = MARGIN + 2 * t * base
        held[start : start + base, :] = values
        held[start + base : start + 2 * base, :] = spin(values, -32)
    held[0:MARGIN, :] = held[length : length + MARGIN, :]
    held[length + MARGIN : length + 2 * MARGIN, :] = held[MARGIN : 2 * MARGIN, :]
    total = early_total[...] + late_total[...]
    spare = total + spin(total, 32)
    kept = rows + 2 * MARGIN // count_x
    half = out.shape[1]
    rest = kept - half
    low = lane_index((8, LANES)) % 64 < 32
    for target in range(count):
        start = (target // count_x) * block + (target % count_x) * kept
        for row in range(0, half, 8):
            a = held[start + row : start + row + 8, :]
            if row < rest:
                b = spin(held[start + half + row : start + half + row + 8, :], 32)
            else:
                b = spare
            out[target, row : row + 8, :] = jnp.where(low, a, b)


def inverse_x_kernel(
    kept, scale, place, lines, tables, turns, *refs
):
    *outs, held = refs
    count, half, _ = lines.shape
    base = turns.shape[1]
    length = RADIX * base
    rest = kept - half
    low = lane_index((half, LANES)) % 64 < 32
    groups, spare = [], None
    for first in range(0, count, 2):
        even, odd = lines[first], lines[first + 1]
        a = jnp.where(low, even, spin(odd, 32))
        b = jnp.where(low, spin(even, -32), odd)
        groups.append(jnp.concatenate([a, b[:rest]], axis=0))
        extra = b[rest : rest + 8]
        spare = extra if spare is None else spare + extra
    mean = jnp.sum(spare) * scale
    wide = 2 * base // LANES
    narrow = base // LANES
    stacked = jnp.concatenate(
        [jnp.concatenate(groups[i * wide : (i + 1) * wide], axis=1) for i in range(3)], axis=0
    )
    at = 3 * wide
    zeros = jnp.concatenate(groups[at : at + narrow], axis=1)
    mids = jnp.concatenate(groups[at + narrow : at + 2 * narrow], axis=1)
    full, zero, middle = x_parts(tables, base)
    full = exact_dot(split(stacked), full)
    zero = exact_dot(split(zeros), zero) * scale
    mid = exact_dot(split(mids), middle) * scale
    turned = []
    for i in range(3):
        real = full[i * kept : (i + 1) * kept, :base]
        imag = full[i * kept : (i + 1) * kept, base:]
        c = turns[i : i + 1, :] * (2.0 * scale)
        s = turns[i + 3 : i + 4, :] * (2.0 * scale)
        turned.append((real * c - imag * s, real * s + imag * c))
    for t in range(RADIX):
        value = zero + mid if t % 2 == 0 else zero - mid
        for i, (real, imag) in enumerate(turned):
            eighth = t * (i + 1) % RADIX
            c = (1.0, ROOT, 0.0, -ROOT, -1.0, -ROOT, 0.0, ROOT)[eighth]
            s = (0.0, ROOT, 1.0, ROOT, 0.0, -ROOT, -1.0, -ROOT)[eighth]
            if c:
                value = value + c * real
            if s:
                value = value - s * imag
        held[:, t * base : (t + 1) * base] = mean - value
    targets, local = len(outs), outs[0].shape[1] - LANES
    right = lane_index((kept, LANES)) < 64
    for mask, out in enumerate(outs):
        start = pl.multiple_of((place[0] ^ mask) * local, LANES)
        after = pl.multiple_of(jnp.where(start + local == length, 0, start + local), LANES)
        before = pl.multiple_of(jnp.where(start == 0, length, start) - LANES, LANES)
        out[:, :local] = held[:, pl.ds(start, local)]
        out[:, local:] = jnp.where(
            right, held[:, pl.ds(after, LANES)], held[:, pl.ds(before, LANES)]
        )


def slopes_x(parts, band, with_edge):
    tiles = parts[0].shape[-1] // LANES
    pieces = []
    for first in list(range(0, tiles - 1, 2)) + ([tiles - 1] if with_edge else []):
        steps = (-1, 0, 1, 2) if first < tiles - 1 else (-1, 0, 1)
        table = band[...] if first < tiles - 1 else band[: 3 * LANES, :LANES]
        order = [(first + step) % tiles for step in steps]
        piece = None
        for part in parts:
            term = dot(jnp.concatenate([lane_tile(part, t) for t in order], axis=1), table)
            piece = term if piece is None else piece + term
        pieces.append(piece)
    return jnp.concatenate(pieces, axis=1)


def slope_y(read):
    value = read(3) - read(-3)
    for index in (0, 1):
        value = value + whole_weights[index] * (read(index + 1) - read(-index - 1))
    return value


def edged(k, side, center, up, down, above, below, sides, has, first=0):
    step = pl.program_id(0) + first
    tile, width = center.shape
    tall = sides.shape[1]
    last = (tall - LANES) // tile - 1
    base = pl.multiple_of(step * tile, 8)
    before = pl.multiple_of(jnp.where(step == 0, tall, base) - HALO, 8)
    over = jnp.where(step == 0, strip(above, k, True) * has[2], up)
    under = jnp.where(step == last, strip(below, k, False) * has[3], down)
    rows = (
        (over, sides[side, pl.ds(before, HALO), :]),
        (center, sides[side, pl.ds(base, tile), :]),
        (under, sides[side, pl.ds(pl.multiple_of(base + tile, 8), HALO), :]),
    )
    return jnp.concatenate([jnp.concatenate(pair, axis=1) for pair in rows], axis=0)


def edged_open(k, side, wall, wall_up, wall_down, above, below, sides, has, first=0):
    open_cells = [1.0 - ref[0].astype(F32) for ref in (wall, wall_up, wall_down)]
    return edged(k, side, *open_cells, above, below, sides, has, first)


def quiet_step_kernel(
    first, has, place, center, up, down, wall, wall_up, wall_down, above, below, sides, across, along, along_inner, out, shown_open, mark
):
    parts, _, tile, width = center.shape
    high = tile + 2 * HALO
    opened = edged_open(parts, parts, wall, wall_up, wall_down, above, below, sides, has, first)
    values = []
    for k in range(parts):
        value = edged(
            k,
            k,
            center[k, 0].astype(F32),
            up[k, 0].astype(F32)[up.shape[2] - HALO :],
            down[k, 0].astype(F32)[:HALO],
            above,
            below,
            sides,
            has,
            first,
        )
        values.append(value)

    def drops(x, along_b, along_p):
        diverge = x[1] + along_b
        return (
            diverge + mean_flow * x[0],
            x[3] + mean_flow * x[1],
            along_p + mean_flow * x[2],
            diverge + mean_flow * x[3],
        )

    short = [value.astype(BF16) for value in values]
    x = slopes_x((jnp.concatenate(short, axis=0),), across, True)
    x = [x[k * high : (k + 1) * high] for k in range(parts)]
    table = along[...]
    dropped = drops(x, dot(table, short[2]), dot(table, short[3]))
    middle = [opened * (v - (time_step / 60.0) * d) for v, d in zip(values, dropped)]
    inner = slice(HALO, HALO + tile)
    x = slopes_x(split(jnp.concatenate([value[inner] for value in middle], axis=0)), across, False)
    x = [x[k * tile : (k + 1) * tile] for k in range(parts)]
    table = along_inner[...]
    y = [sum(dot(table, part) for part in split(middle[k][:, :width])) for k in (2, 3)]
    dropped = drops(x, *y)
    shown = opened[inner, :width]
    for k in range(parts):
        start = 0.5 * values[k][inner, :width] - (0.5 * time_step / 60.0) * dropped[k]
        out[k] = shown * start + 0.5 * middle[k][inner, :width]
    shown_open[0] = opened.astype(BF16)
    mark[0] = place[0]


def tables_kernel(place, weights_x, weights_y, rise_x, rise_y):
    tiles, reach_x, lanes = rise_x.shape
    wide, length_x = (tiles - 1) * lanes, weights_x.shape[1]
    first = place[0] * wide
    half = LANES // 2

    def weights(ref, start, size):
        length = ref.shape[1]
        start = jnp.where(start < 0, start + length, jnp.where(start >= length, start - length, start))
        return ref[:, pl.ds(pl.multiple_of(start, LANES), size)]

    cells = lax.broadcasted_iota(jnp.int32, (reach_x, lanes), 0)
    fine = lax.broadcasted_iota(jnp.int32, (reach_x, lanes), 1)
    right, left = weights(weights_x, first + wide, LANES), weights(weights_x, first - LANES, LANES)
    edge = jnp.where(lane_index(right.shape) < half, right, left)
    edge = jnp.concatenate([edge, edge], axis=1)
    for k in range(tiles):
        own = weights(weights_x, first + k * lanes, lanes) if k < tiles - 1 else edge
        target = fine // 2 - 1
        if k == tiles - 1:
            target = jnp.where(fine < half, target, target + half)
        value = jnp.zeros(fine.shape, F32)
        for t in range(4):
            value = jnp.where(cells == (target + t) % reach_x, own[t : t + 1, :], value)
        rise_x[k] = value
    steps, high, reach = rise_y.shape
    tall = steps * TILE
    first = place[1] * tall
    own = [weights(weights_y, first + k * LANES, LANES) for k in range(-1, tall // LANES + 1)]
    own = jnp.concatenate([jnp.concatenate(own, axis=1), jnp.zeros((4, tall + 2 * LANES), F32)], axis=0).T
    cells = lax.broadcasted_iota(jnp.int32, (high, reach), 1) % (reach // 3)
    target = lax.broadcasted_iota(jnp.int32, (high, reach), 0) // 2 + (HALO // 2 - 1)
    for k in range(steps):
        start = LANES - HALO + k * TILE
        value = jnp.zeros((high, reach), F32)
        for t in range(4):
            value = jnp.where(cells == target + t, own[start : start + high, t : t + 1], value)
        rise_y[k] = value


def source_kernel(place, squares, opened, rise_x, rise_y, quiet, across, *refs):
    *lines, out, squared, cells_open, matrix, rows_matrix, calm, band, held, raised, forced, done, fetched, kept = refs
    steps = done.shape[0]
    tile, width = calm.shape[2:]
    high = tile + 2 * HALO
    rows = lines[0].shape[0]

    def calm_copy(k):
        part = quiet.at[:, pl.ds(k * tile, tile), :]
        return pltpu.make_async_copy(part, calm.at[k % 2], fetched.at[k % 2])

    def done_copy(k):
        part = out.at[:, 0, pl.ds(k * tile, tile), :]
        return pltpu.make_async_copy(done.at[k], part, kept.at[k])

    arrays = [(squares, squared), (rise_x, matrix), (rise_y, rows_matrix), (opened, cells_open), (across, band)]
    copies = [
        pltpu.make_async_copy(source, target, fetched.at[2 + k])
        for k, (source, target) in enumerate(arrays)
    ]
    pieces = [
        pltpu.make_async_copy(
            piece,
            held.at[pl.ds(pl.multiple_of((place[0] ^ mask) * rows, 8), rows), :],
            fetched.at[2 + len(arrays) + mask],
        )
        for mask, piece in enumerate(lines)
    ]
    for copy in pieces + copies:
        copy.start()
    calm_copy(0).start()
    calm_copy(1).start()
    for copy in pieces + copies[:2]:
        copy.wait()

    level = held[MARGIN - HALO : MARGIN - HALO + squared.shape[0], :] - squared[...]
    count = level.shape[1] // LANES
    near = lane_index((level.shape[0], LANES)) < 64
    for k in range(count):
        after, before = lane_tile(level, (k + 1) % count), lane_tile(level, (k - 1) % count)
        around = jnp.concatenate([lane_tile(level, k), jnp.where(near, after, before)], axis=1)
        lanes = 2 * LANES if k < count - 1 else LANES
        value = split(exact_dot(split(around), split(matrix[k][:, :lanes])))
        for part in range(2):
            raised[part, :, 2 * k * LANES : 2 * k * LANES + lanes] = value[part]
    for copy in copies[2:]:
        copy.wait()

    reach = rows_matrix.shape[2] // 3
    third = lane_index((high, 3 * reach)) >= 2 * reach
    for k in range(steps):
        start = k * (tile // 2)
        window = [raised[part, start : start + reach, :] for part in (0, 1, 0)]
        weights = split(rows_matrix[k])
        weights = jnp.where(third, weights[1], weights[0])
        free = time_step * cells_open[k].astype(F32)
        value = free * dot(weights, jnp.concatenate(window, axis=0))
        forced[k % 2] = value
        inner = value[HALO : HALO + tile]
        shown = (0.5 / 60.0) * free[HALO : HALO + tile, :width]
        x = shown * slopes_x(split(inner), band, False)
        y = shown * slope_y(lambda d: forced[k % 2, HALO + d : HALO + d + tile, :width])
        calm_copy(k).wait()
        still = calm.at[k % 2]
        done[k, 0] = still[0].astype(BF16)
        done[k, 1] = (still[1] - x).astype(BF16)
        done[k, 2] = (still[2] - y).astype(BF16)
        done[k, 3] = (still[3] + inner[:, :width] - mean_flow * x).astype(BF16)
        done_copy(k).start()
        if k + 2 < steps:
            calm_copy(k + 2).start()
    for k in range(steps):
        done_copy(k).wait()


def call(
    kernel, operands, outs, scratch=(), steps=0, specs=None, out_specs=None, after=(), aliases=None, megabytes=24, flops=0, moved=0, name=None
):
    count = len(operands)

    def body(*refs):
        kernel(*refs[:count], *refs[count + len(after) :])

    def whole(array):
        zeros = (0,) * len(array.shape)
        return pl.BlockSpec(array.shape, lambda *_: zeros)

    arguments = {}
    chosen = specs or {}
    if steps:
        arguments["grid"] = (steps,)
        in_specs = [chosen.get(i, whole(o)) for i, o in enumerate(operands)]
        arguments["out_specs"] = jax.tree.map(whole, outs) if out_specs is None else out_specs
    else:
        local = pl.BlockSpec(memory_space=pltpu.VMEM)
        in_specs = [chosen.get(i, local) for i in range(count)]
        if out_specs is not None:
            arguments["out_specs"] = out_specs
    return pl.pallas_call(
        body,
        out_shape=outs,
        in_specs=in_specs + [pl.BlockSpec(memory_space=pl.ANY)] * len(after),
        scratch_shapes=list(scratch),
        input_output_aliases=aliases or {},
        compiler_params=pltpu.CompilerParams(vmem_limit_bytes=megabytes << 20),
        cost_estimate=pl.CostEstimate(flops=flops, bytes_accessed=moved, transcendentals=0),
        name=name,
        **arguments,
    )(*operands, *after)


def ring(array, axis, step):
    size = lax.axis_size(axis)
    return lax.ppermute(array, axis, [(i, (i + step) % size) for i in range(size)])


def swap(array, axis, mask):
    return lax.ppermute(array, axis, [(i, i ^ mask) for i in range(lax.axis_size(axis))])


def shaped(*shape, kind=F32):
    return jax.ShapeDtypeStruct(shape, kind)


def pressure_lines(pieces, place_x, gathered, spread, stepped):
    _, rows, local_x = pieces[0][0].shape
    count_x, count_y = lax.axis_size("gx"), lax.axis_size("gy")
    count = count_x * count_y
    scalars = {0: pl.BlockSpec(memory_space=pltpu.SMEM)}
    length_x, length_y = local_x * count_x, 2 * rows * count
    full, zero, middle, cos_turn, sin_turn = x_tables(length_x)
    turns = np.zeros((8, cos_turn.shape[1]), np.float32)
    turns[0:3], turns[3:6] = cos_turn, sin_turn
    forward_tables = np.concatenate([beside(full), beside(zero, middle)])
    halves_sent, totals = [], []
    for part, before in zip(pieces, (gathered, ())):
        spectra, total = call(
            forward_x_kernel,
            (place_x, *part, forward_tables, turns),
            (shaped(count, rows, LANES), shaped(8, LANES)),
            (pltpu.VMEM((count_x, 2, rows, local_x), F32),),
            specs=scalars,
            after=before,
            flops=5 * 10**8,
            moved=3 << 20,
            name="forward_x",
        )
        halves_sent.append(lax.all_to_all(spectra, ("gy", "gx"), 0, 0, tiled=True))
        totals.append(total)
    rows *= 2
    place = lax.axis_index("gy") * count_x + lax.axis_index("gx")
    waves = jnp.asarray(wave_table(length_x, count))
    wave = lax.dynamic_slice(waves, (place, 0), (1, LANES))
    both, turns_y = y_tables(length_y)
    kept = rows + 2 * MARGIN // count_x
    half = (kept // 2 + 8) // 8 * 8
    solved = call(
        functools.partial(solve_y_kernel, count_x),
        (spread, *halves_sent, *totals, wave, beside(both), turns_y),
        shaped(count, half, LANES),
        (pltpu.VMEM((length_y + 2 * MARGIN, LANES), F32),),
        specs=scalars,
        flops=4 * 10**9,
        moved=6 << 20,
        name="solve_y",
    )
    solved = lax.all_to_all(solved, ("gy", "gx"), 0, 0, tiled=True)
    back = 2.0 * zero.T
    back[LANES // 2] *= 0.5
    tables = np.concatenate(
        [beside(full.T), beside(back, 2.0 * middle.T)]
    )
    pressed = call(
        functools.partial(inverse_x_kernel, kept, 1.0 / (length_x * length_y)),
        (stepped, solved, tables, turns),
        (shaped(kept, local_x + LANES),) * count_x,
        (pltpu.VMEM((kept, length_x), F32),),
        specs=scalars,
        flops=10**9,
        moved=4 << 20,
        name="inverse_x",
    )
    return [piece if mask == 0 else swap(piece, "gx", mask) for mask, piece in enumerate(pressed)]


def fast_shards(velocity, weights_x, weights_y, acoustic, wall_mask):
    parts, _, tall, wide = acoustic.shape
    _, _, local_y, local_x = velocity.shape
    count_x, count_y = lax.axis_size("gx"), lax.axis_size("gy")
    place_x, place_y = lax.axis_index("gx"), lax.axis_index("gy")
    full, high, steps = wide + LANES, TILE + 2 * HALO, tall // TILE
    strips = (parts + 2) * HALO
    small = 2 * HALO
    has = jnp.stack([place_x > 0, place_x < count_x - 1, place_y > 0, place_y < count_y - 1])
    has = has.astype(F32)
    scalars = pl.BlockSpec(memory_space=pltpu.SMEM)

    def at(block, *index):
        return pl.BlockSpec(block, lambda i: index)

    own = place_x.astype(jnp.int32).reshape(1)
    sent = call(
        pieces_kernel,
        (own, velocity),
        (shaped(2, local_y // (2 * count_x), local_x),) * (2 * count_x),
        specs={0: scalars},
        moved=2 << 20,
        megabytes=8,
        name="pieces",
    )
    moved = [piece if k % count_x == 0 else swap(piece, "gx", k % count_x) for k, piece in enumerate(sent)]
    moved = (moved[:count_x], moved[count_x:])
    first, last = call(
        rows_kernel,
        (acoustic, acoustic, wall_mask, wall_mask, velocity, velocity),
        (shaped(STRIP_ROWS, wide),) * 2,
        steps=1,
        specs={
            0: at((parts, 1, small, wide), 0, 0, 0, 0),
            1: at((parts, 1, small, wide), 0, 0, tall // small - 1, 0),
            2: at((1, HALO, wide), 0, 0, 0),
            3: at((1, HALO, wide), 0, tall // HALO - 1, 0),
            4: at((1, 1, HALO, local_x), 1, 0, 0, 0),
            5: at((1, 1, HALO, local_x), 1, 0, local_y // HALO - 1, 0),
        },
        after=moved[0][1:2],
        moved=2 << 20,
        megabytes=54,
        name="rows",
    )
    above, below = ring(last, "gy", 1), ring(first, "gy", -1)
    to_right, to_left = call(
        columns_kernel,
        (has, acoustic, acoustic, wall_mask, wall_mask, velocity, velocity, above, below),
        (shaped(strips, tall + LANES), shaped(strips, tall + LANES)),
        steps=1,
        specs={
            0: scalars,
            1: at((parts, 1, tall, LANES), 0, 0, 0, 0),
            2: at((parts, 1, tall, LANES), 0, 0, 0, wide // LANES - 1),
            3: at((1, tall, LANES), 0, 0, 0),
            4: at((1, tall, LANES), 0, 0, wide // LANES - 1),
            5: at((1, 1, local_y, LANES), 1, 0, 0, 0),
            6: at((1, 1, local_y, LANES), 1, 0, 0, local_x // LANES - 1),
        },
        moved=8 << 20,
        megabytes=54,
        name="columns",
    )
    from_left, from_right = ring(to_right, "gx", 1), ring(to_left, "gx", -1)
    sides, squares, beside = call(
        sides_kernel,
        (has, own, velocity, above, below, from_left, from_right),
        (
            shaped(parts + 1, tall + LANES, LANES),
            shaped(local_y + 2 * HALO, local_x + LANES),
            shaped(1, kind=jnp.int32),
        ),
        steps=1,
        specs={0: scalars, 1: scalars, 2: at((1, 1, local_y, local_x), 1, 0, 0, 0)},
        out_specs=(
            at((parts + 1, tall + LANES, LANES), 0, 0, 0),
            at((local_y + 2 * HALO, local_x + LANES), 0, 0),
            scalars,
        ),
        moved=8 << 20,
        megabytes=54,
        name="sides",
    )
    across, along = band_tables(high)
    along_inner = along[HALO : HALO + TILE]
    per, rows = TILE // small, TILE // HALO

    def tiled(first):
        walls = (
            pl.BlockSpec((1, TILE, wide), lambda i: (0, i + first, 0)),
            pl.BlockSpec((1, HALO, wide), lambda i: (0, jnp.maximum((i + first) * rows - 1, 0), 0)),
            pl.BlockSpec(
                (1, HALO, wide),
                lambda i: (0, jnp.minimum((i + first + 1) * rows, steps * rows - 1), 0),
            ),
        )
        cells = (
            pl.BlockSpec((parts, 1, TILE, wide), lambda i: (0, 0, i + first, 0)),
            pl.BlockSpec(
                (parts, 1, small, wide), lambda i: (0, 0, jnp.maximum((i + first) * per - 1, 0), 0)
            ),
            pl.BlockSpec(
                (parts, 1, small, wide),
                lambda i: (0, 0, jnp.minimum((i + first + 1) * per, steps * per - 1), 0),
            ),
        )
        return cells, walls, pl.BlockSpec((parts, TILE, wide), lambda i: (0, i + first, 0))

    def quiet_tiles(first, count, before):
        cells, walls, flat = tiled(first)
        operands = (has, own, acoustic, acoustic, acoustic, wall_mask, wall_mask, wall_mask, above, below, sides)
        operands = operands + (across, along, along_inner)
        return call(
            functools.partial(quiet_step_kernel, first),
            operands,
            (shaped(parts, tall, wide), shaped(steps, high, full, kind=BF16), shaped(1, kind=jnp.int32)),
            steps=count,
            specs=dict(enumerate((scalars, scalars) + cells + walls)),
            out_specs=(flat, pl.BlockSpec((1, high, full), lambda i: (i + first, 0, 0)), scalars),
            after=before,
            aliases={len(operands): 0, len(operands) + 1: 1} if before else None,
            megabytes=54,
            flops=3 * 10**9 * count,
            moved=(12 << 20) * count,
            name="quiet_step",
        )

    early = max(steps * 3 // 4, 1)
    *begun, stepped = quiet_tiles(0, early, ())
    quiet, opened = begun
    if early < steps:
        quiet, opened, _ = quiet_tiles(early, steps - early, begun)
    rows_done = above[:8, :LANES] + below[:8, :LANES]
    lines = pressure_lines(moved, own, (rows_done,), beside, stepped)
    tiles = wide // (2 * LANES) + 1
    rise_x, rise_y = call(
        tables_kernel,
        (jnp.stack([place_x, place_y]).astype(jnp.int32), weights_x, weights_y),
        (shaped(tiles, 2 * LANES, 2 * LANES), shaped(steps, high, 3 * (high // 2 + HALO))),
        specs={0: scalars},
        moved=4 << 20,
        megabytes=16,
        name="tables",
    )
    operands = (own, squares, opened, rise_x, rise_y, quiet, across, *lines)
    anywhere = pl.BlockSpec(memory_space=pl.ANY)
    specs = {k: anywhere for k in range(1, len(operands))}
    scratch = (
        pltpu.VMEM(squares.shape, F32),
        pltpu.VMEM(opened.shape, BF16),
        pltpu.VMEM(rise_x.shape, F32),
        pltpu.VMEM(rise_y.shape, F32),
        pltpu.VMEM((2, parts, TILE, wide), F32),
        pltpu.VMEM(across.shape, BF16),
        pltpu.VMEM((local_y + 2 * MARGIN, local_x + LANES), F32),
        pltpu.VMEM((2, local_y + 2 * HALO, full), BF16),
        pltpu.VMEM((2, high, full), F32),
        pltpu.VMEM((steps, parts, TILE, wide), BF16),
        pltpu.SemaphoreType.DMA((7 + count_x,)),
        pltpu.SemaphoreType.DMA((steps,)),
    )
    return call(
        source_kernel,
        operands,
        shaped(*acoustic.shape, kind=BF16),
        scratch,
        specs={0: scalars, **specs},
        out_specs=anywhere,
        megabytes=56,
        flops=4 * 10**9,
        moved=16 << 20,
        name="source_step",
    )


def fits(count_x, count_y, velocity, acoustic):
    _, planes, local_y, local_x = velocity
    _, _, tall, wide = acoustic
    length_x, length_y = local_x * count_x, local_y * count_y
    rows = local_y // count_x
    base_x, base_y = length_x // RADIX, length_y // RADIX
    return (
        planes == 1
        and acoustic[0] == PARTS
        and length_x * 2 == count_x * count_y * LANES
        and base_x % (2 * LANES) == 0
        and local_x % base_x == 0
        and rows % 16 == 0
        and base_y % rows == 0
        and base_y % 8 == 0
        and MARGIN * 2 % (8 * count_x) == 0
        and tall == 2 * local_y
        and wide == 2 * local_x
        and tall % TILE == 0
        and tall % LANES == 0
        and tall >= 2 * TILE
        and count_x & (count_x - 1) == 0
        and wide % (2 * LANES) == 0
    )


def extended(array, sides, width):
    for axis, dim in sides:
        size, length = (lax.axis_size(axis), array.shape[dim])
        up = [(i, (i + 1) % size) for i in range(size - 1)]
        down = [(j, i) for i, j in up]
        last = lax.slice_in_dim(array, length - width, length, axis=dim)
        leading = lax.slice_in_dim(array, 0, width, axis=dim)
        before = lax.ppermute(last, axis, up)
        after = lax.ppermute(leading, axis, down)
        array = jnp.concatenate([before, array, after], axis=dim)
    return array


def gradients(padded):
    height = padded.shape[-2] - 6
    breadth = padded.shape[-1] - 6
    rows_mid = padded[..., 3 : 3 + height, :]
    cols_mid = padded[..., :, 3 : 3 + breadth]
    along_x = jnp.zeros_like(padded[..., 3 : 3 + height, 3 : 3 + breadth])
    along_y = jnp.zeros_like(along_x)
    for index, weight in enumerate(stencil_weights):
        distance = index + 1
        along_x = along_x + weight * (
            rows_mid[..., 3 + distance : 3 + distance + breadth]
            - rows_mid[..., 3 - distance : 3 - distance + breadth]
        )
        along_y = along_y + weight * (
            cols_mid[..., 3 + distance : 3 + distance + height, :]
            - cols_mid[..., 3 - distance : 3 - distance + height, :]
        )
    return (along_x, along_y)


def tendency(padded, source):
    along_x, along_y = gradients(padded)
    diverge = along_x[1] + along_y[2]
    forcing = jnp.stack([-diverge, -along_x[3], -along_y[3], source - diverge])
    return forcing - mean_flow * along_x


def spectral_index(flat, length):
    second = length // 16
    wave = flat // second + 16 * (flat % second)
    return jnp.where(wave < length // 2, wave, wave - length).astype(jnp.float32)


def twiddles(rows_count, cols_count, modulus, sign):
    products = jnp.arange(rows_count)[:, None] * jnp.arange(cols_count)[None, :] % modulus
    angles = 2.0 * math.pi / modulus * products.astype(jnp.float32)
    return (jnp.cos(angles), sign * jnp.sin(angles))


def mix_rows(real_part, imag_part, cosine, sine):
    exact = lax.Precision.HIGHEST
    cos_real = jnp.einsum("ka,...ab->...kb", cosine, real_part, precision=exact)
    cos_imag = jnp.einsum("ka,...ab->...kb", cosine, imag_part, precision=exact)
    sin_real = jnp.einsum("ka,...ab->...kb", sine, real_part, precision=exact)
    sin_imag = jnp.einsum("ka,...ab->...kb", sine, imag_part, precision=exact)
    return (cos_real - sin_imag, cos_imag + sin_real)


def mix_cols(real_part, imag_part, cosine, sine):
    exact = lax.Precision.HIGHEST
    cos_real = jnp.einsum("...kb,bc->...kc", real_part, cosine, precision=exact)
    cos_imag = jnp.einsum("...kb,bc->...kc", imag_part, cosine, precision=exact)
    sin_real = jnp.einsum("...kb,bc->...kc", real_part, sine, precision=exact)
    sin_imag = jnp.einsum("...kb,bc->...kc", imag_part, sine, precision=exact)
    return (cos_real - sin_imag, cos_imag + sin_real)


def rotate(real_part, imag_part, cosine, sine):
    return (real_part * cosine - imag_part * sine, real_part * sine + imag_part * cosine)


def discrete(real_part, imag_part, sign):
    length = real_part.shape[-1]
    second = length // 16
    initial = real_part.shape
    folded = initial[:-1] + (16, second)
    real_part = real_part.reshape(folded)
    imag_part = imag_part.reshape(folded)
    small_cos, small_sin = twiddles(16, 16, 16, sign)
    large_cos, large_sin = twiddles(second, second, second, sign)
    turn_cos, turn_sin = twiddles(16, second, length, sign)
    if sign < 0:
        real_part, imag_part = mix_rows(real_part, imag_part, small_cos, small_sin)
        real_part, imag_part = rotate(real_part, imag_part, turn_cos, turn_sin)
        real_part, imag_part = mix_cols(real_part, imag_part, large_cos, large_sin)
    else:
        real_part, imag_part = mix_cols(real_part, imag_part, large_cos, large_sin)
        real_part, imag_part = rotate(real_part, imag_part, turn_cos, turn_sin)
        real_part, imag_part = mix_rows(real_part, imag_part, small_cos, small_sin)
        real_part = real_part / length
        imag_part = imag_part / length
    return (real_part.reshape(initial), imag_part.reshape(initial))


def transform(stacked, sign, kind):
    if kind == "real_in":
        real_part = stacked
        imag_part = jnp.zeros_like(stacked)
    else:
        half = stacked.shape[0] // 2
        real_part = stacked[:half]
        imag_part = stacked[half:]
    real_out, imag_out = discrete(real_part, imag_part, sign)
    if kind == "real_out":
        return real_out
    return jnp.concatenate([real_out, imag_out], axis=0)


def project(stacked, wave_x, wave_y):
    coef_xx = wave_x * wave_x
    coef_xy = 2.0 * wave_x * wave_y
    coef_yy = wave_y * wave_y
    denominator = wave_x * wave_x + wave_y * wave_y
    positive = denominator > 0
    safe = jnp.where(positive, denominator, 1.0)

    def combine(parts):
        numerator = -(coef_xx * parts[0] + coef_xy * parts[1] + coef_yy * parts[2])
        return jnp.where(positive, numerator / safe, 0.0)

    return jnp.stack([combine(stacked[:3]), combine(stacked[3:])])


def refine(stacked, weights):
    result = jnp.zeros(stacked.shape[:-1] + (2 * stacked.shape[-1],), jnp.float32)
    for offset in range(4):
        result = (
            result
            + jnp.repeat(jnp.roll(stacked, 1 - offset, axis=-1), 2, axis=-1) * weights[offset]
        )
    return result


def lines_x(stacked, action):
    gathered = action(lax.all_to_all(stacked, "gx", split_axis=2, concat_axis=3, tiled=True))
    return lax.all_to_all(gathered, "gx", split_axis=3, concat_axis=2, tiled=True)


def lines_y(stacked, action):
    turned = jnp.swapaxes(stacked, 2, 3)
    gathered = action(lax.all_to_all(turned, "gy", split_axis=2, concat_axis=3, tiled=True))
    returned = lax.all_to_all(gathered, "gy", split_axis=3, concat_axis=2, tiled=True)
    return jnp.swapaxes(returned, 2, 3)


def expand(fields):
    return extended(fields, (("gx", 3), ("gy", 2)), 3)


def shards(velocity, weights_x, weights_y, acoustic, wall_mask):
    acoustic = acoustic.astype(jnp.float32)
    flow_x = velocity[0]
    flow_y = velocity[1]
    tensor = jnp.stack([flow_x * flow_x, flow_x * flow_y, flow_y * flow_y])
    count_gx = lax.axis_size("gx")
    count_gy = lax.axis_size("gy")
    place_x = lax.axis_index("gx")
    place_y = lax.axis_index("gy")
    local_y = tensor.shape[2]
    local_x = tensor.shape[3]
    length_x = local_x * count_gx
    length_y = local_y * count_gy

    def forward_real(portion):
        return transform(portion, -1, "real_in")

    def finish_x(portion):
        return refine(transform(portion, 1, "real_out"), weights_x)

    spectra = lines_x(tensor, forward_real)
    share_x = local_x // count_gy
    line_x = spectral_index(place_x * local_x + place_y * share_x + jnp.arange(share_x), length_x)[
        :, None
    ]
    line_y = spectral_index(jnp.arange(length_y), length_y)[None, :]

    def solve_y(portion):
        solved = project(transform(portion, -1, "complex"), line_x, line_y)
        return refine(transform(solved, 1, "complex"), weights_y)

    pressure = lines_y(spectra, solve_y)
    source = lines_x(pressure, finish_x)[0]
    open_cells = (1 - wall_mask).astype(jnp.float32)
    first_rate = tendency(expand(acoustic), source)
    middle = open_cells * (acoustic + time_step * first_rate)
    second_rate = tendency(expand(middle), source)
    return (open_cells * (acoustic + 0.5 * time_step * (first_rate + second_rate))).astype(
        jnp.bfloat16
    )


def solution(mesh):
    in_specs = (P(None, None, "gy", "gx"), P(), P(), P(None, None, "gy", "gx"), P(None, "gy", "gx"))
    out_specs = P(None, None, "gy", "gx")

    def chosen(velocity, weights_x, weights_y, acoustic, wall_mask):
        sizes = (mesh.shape["gx"], mesh.shape["gy"], velocity.shape, acoustic.shape)
        plan = fast_shards if fits(*sizes) else shards
        return plan(velocity, weights_x, weights_y, acoustic, wall_mask)

    return jax.shard_map(
        chosen, mesh=mesh, in_specs=in_specs, out_specs=out_specs, check_vma=False
    )
```

```python
import functools
import math

import jax
import jax.numpy as jnp
import ml_dtypes
import numpy as np
from jax import lax
from jax.experimental import pallas as pl
from jax.experimental.pallas import tpu as pltpu
from jax.sharding import PartitionSpec as P

stencil_weights = (0.75, -0.15, 1.0 / 60.0)
mean_flow = 0.3
time_step = 0.5
whole_weights = (45.0, -9.0, 1.0)

LANES = 128
RADIX = 8
HALO = 8
MARGIN = 16
TILE = 128
ROOT = math.sqrt(0.5)
STRIP = {2: (0, 6), 3: (6, 6), 1: (12, 3), 4: (15, 3), 5: (20, 4)}
STRIP_ROWS = 24
PARTS = 4
BF16 = jnp.bfloat16
F32 = jnp.float32


def halves(table):
    high = table.astype(np.float32).astype(ml_dtypes.bfloat16)
    low = (table - high.astype(np.float64)).astype(np.float32).astype(ml_dtypes.bfloat16)
    return high, low


def packed_columns(cosine, sine):
    half = LANES // 2
    parts = []
    for first in range(0, cosine.shape[1], half):
        parts += [cosine[:, first : first + half], sine[:, first : first + half]]
    return np.concatenate(parts, axis=1)


@functools.lru_cache(maxsize=None)
def x_tables(length):
    base = length // RADIX
    m = np.arange(base)[:, None]
    q = np.arange(base)[None, :]
    angle = 2.0 * np.pi * ((m * q) % base) / base
    cosine, sine = np.cos(angle), np.sin(angle)
    full = np.concatenate([packed_columns(cosine, -sine), packed_columns(sine, cosine)], axis=0)
    half = base // 2
    zero_cos, zero_sin = cosine[:, :half].copy(), -sine[:, :half]
    zero_cos[:, 0] = 0.0
    zero_sin = zero_sin.copy()
    zero_sin[:, 0] = (-1.0) ** np.arange(base)
    zero = packed_columns(zero_cos, zero_sin)
    shifted = 2.0 * np.pi * ((m * (RADIX * q[:, :half] + RADIX // 2)) % length) / length
    middle = packed_columns(np.cos(shifted), -np.sin(shifted))
    turns = 2.0 * np.pi * np.arange(1, RADIX // 2)[:, None] * np.arange(base)[None, :] / length
    return full, zero, middle, np.cos(turns), np.sin(turns)


@functools.lru_cache(maxsize=None)
def y_tables(length):
    base = length // RADIX
    index = np.arange(base)
    angle = 2.0 * np.pi * ((index[:, None] * index[None, :]) % base) / base
    both = np.concatenate([np.cos(angle), np.sin(angle)], axis=0)
    turns = 2.0 * np.pi * np.arange(RADIX)[:, None] * index[None, :] / length
    turns = np.concatenate([np.cos(turns), np.sin(turns)], axis=0).T
    high, rest = halves(turns)
    low = turns - high.astype(np.float64) - rest.astype(np.float64)
    return both, np.concatenate([high, rest, low.astype(ml_dtypes.bfloat16)], axis=1)


@functools.lru_cache(maxsize=None)
def wave_table(length, count):
    slots = LANES // 4
    base = length // RADIX
    waves = []
    for residue in (1, 2, 3):
        waves.append(RADIX * np.arange(base) + residue)
    waves.append(RADIX * np.arange(base // 2))
    waves.append(RADIX * np.arange(base // 2) + RADIX // 2)
    waves = np.concatenate(waves)
    waves = np.where(waves == 0, length // 2, waves)
    waves = np.where(waves < length // 2, waves, waves - length).reshape(count, slots)
    return np.tile(waves, (1, 4)).astype(np.float32)


@functools.lru_cache(maxsize=None)
def band_tables(rows):
    across = np.zeros((4 * LANES, 2 * LANES))
    column = np.arange(2 * LANES)
    down = np.zeros((rows, rows))
    for index, weight in enumerate(whole_weights):
        distance = index + 1
        across[column + LANES + distance, column] = weight
        across[column + LANES - distance, column] = -weight
        down += weight * (np.eye(rows, k=distance) - np.eye(rows, k=-distance))
    return across.astype(ml_dtypes.bfloat16), down.astype(ml_dtypes.bfloat16)


def beside(*tables):
    high, low = halves(np.concatenate(tables, axis=1))
    return np.concatenate([high, low], axis=0)


def split(values):
    high = values.astype(BF16)
    return high, (values - high.astype(F32)).astype(BF16)


def dot(left, right):
    return jnp.dot(left, right, preferred_element_type=F32)


def exact_dot(left, right):
    left_high, left_low = left
    right_high, right_low = right
    return dot(left_high, right_high) + (dot(left_low, right_high) + dot(left_high, right_low))


def lane_index(shape):
    return lax.broadcasted_iota(jnp.int32, shape, len(shape) - 1)


def spin(values, shift):
    return pltpu.roll(values, shift % values.shape[-1], values.ndim - 1)


def lane_tile(values, index):
    return values[:, index * LANES : (index + 1) * LANES]


def x_parts(tables, base):
    wide = 2 * base
    full = (tables[:wide], tables[wide : 2 * wide])
    at = 2 * wide
    high, low = tables[at : at + base], tables[at + base : at + 2 * base]
    return full, (high[:, :base], low[:, :base]), (high[:, base:], low[:, base:])


def pieces_kernel(place, velocity, *pieces):
    rows = pieces[0].shape[1]
    for mask, piece in enumerate(pieces):
        start = pl.multiple_of((place[0] ^ mask) * rows, 8)
        for c in range(2):
            piece[c] = velocity[c, 0, pl.ds(start, rows), :]


def rows_kernel(top, low, top_wall, low_wall, top_flow, low_flow, first, last):
    small, width = top.shape[2], top_flow.shape[3]
    first[...] = jnp.zeros(first.shape, F32)
    last[...] = jnp.zeros(last.shape, F32)
    for k, (start, rows) in STRIP.items():
        lanes = slice(0, width) if k == PARTS + 1 else slice(None)
        if k < PARTS:
            upper, lower = top[k, 0].astype(F32)[:HALO], low[k, 0].astype(F32)[small - HALO :]
        elif k == PARTS:
            upper, lower = 1.0 - top_wall[0].astype(F32), 1.0 - low_wall[0].astype(F32)
        else:
            upper, lower = top_flow[0, 0], low_flow[0, 0]
        first[start : start + rows, lanes] = upper[:rows]
        last[start : start + rows, lanes] = lower[HALO - rows :]


def strip(ref, k, upper, lanes=slice(None)):
    if k not in STRIP:
        return jnp.zeros((HALO, ref[0:1, lanes].shape[1]), F32)
    start, rows = STRIP[k]
    values = ref[start : start + rows, lanes]
    blank = jnp.zeros((HALO - rows, values.shape[1]), F32)
    return jnp.concatenate([blank, values] if upper else [values, blank], axis=0)


def columns_kernel(
    has, left, right, left_wall, right_wall, left_flow, right_flow, above, below, to_right, to_left
):
    parts = left.shape[0]
    wide, flow_wide = above.shape[1], above.shape[1] // 2
    gap = jnp.zeros((LANES - 2 * HALO, LANES), F32)

    def tall(k, inner, first, sides):
        lanes = slice(first, first + LANES)
        over, under = strip(above, k, True, lanes), strip(below, k, False, lanes)
        return jnp.concatenate([inner, under * sides[1], gap, over * sides[0]], axis=0).T

    for k in range(parts + 1):
        at = slice(k * HALO, (k + 1) * HALO)
        if k < parts:
            near, far = left[k, 0].astype(F32), right[k, 0].astype(F32)
        else:
            near, far = 1.0 - left_wall[0].astype(F32), 1.0 - right_wall[0].astype(F32)
        sides = (has[2], has[3])
        to_left[at, :] = tall(k, near, 0, sides)[:HALO]
        to_right[at, :] = tall(k, far, wide - LANES, sides)[LANES - HALO :]
    k = parts + 1
    at = slice(k * HALO, (k + 1) * HALO)
    size = left_flow.shape[2] + LANES
    blank = jnp.zeros((HALO, to_left.shape[1] - size), F32)
    to_left[at, :size] = tall(k, left_flow[0, 0], 0, (1.0, 1.0))[:HALO]
    to_right[at, :size] = tall(k, right_flow[0, 0], flow_wide - LANES, (1.0, 1.0))[LANES - HALO :]
    to_left[at, size:] = blank
    to_right[at, size:] = blank


def sides_kernel(has, place, velocity, above, below, from_left, from_right, sides, squares, mark):
    parts, tall, _ = sides.shape
    gap = jnp.zeros((LANES - 2 * HALO, tall), F32)
    for k in range(parts):
        at = slice(k * HALO, (k + 1) * HALO)
        tile = [from_right[at, :] * has[1], gap, from_left[at, :] * has[0]]
        sides[k] = jnp.concatenate(tile, axis=0).T
    at = slice(parts * HALO, (parts + 1) * HALO)
    rows, local = velocity.shape[2:]
    size = rows + LANES
    tile = [from_right[at, :size], gap[:, :size], from_left[at, :size]]
    tile = jnp.concatenate(tile, axis=0).T
    tile = tile * tile
    mark[0] = place[0]
    over, under = (strip(ref, parts, ref is above, slice(0, local)) for ref in (above, below))
    squares[:HALO, :local] = over * over
    squares[HALO : HALO + rows, :local] = velocity[0, 0] * velocity[0, 0]
    squares[HALO + rows :, :local] = under * under
    squares[:HALO, local:] = tile[size - HALO :]
    squares[HALO : HALO + rows, local:] = tile[:rows]
    squares[HALO + rows :, local:] = tile[rows : rows + HALO]


def forward_x_kernel(place, *refs):
    *pieces, tables, turns, out, total, lines = refs
    count, _, rows, local = lines.shape
    for mask, piece in enumerate(pieces):
        lines[place[0] ^ mask] = piece[...]
    base = turns.shape[1]
    per = local // base
    u = [lines[t // per, 0, :, (t % per) * base : (t % per + 1) * base] for t in range(RADIX)]
    v = [lines[t // per, 1, :, (t % per) * base : (t % per + 1) * base] for t in range(RADIX)]
    energy = sum(b * b for b in v)
    energy = jnp.sum(energy.reshape(rows // 8, 8, base), axis=0)
    total[...] = sum(energy[:, k : k + LANES] for k in range(0, base, LANES))
    fields = ([a * a - b * b for a, b in zip(u, v)], [2.0 * a * b for a, b in zip(u, v)])
    zeros, mids, reals, imags = [], [], [[], [], []], [[], [], []]
    for a in fields:
        s04, s26, s15, s37 = a[0] + a[4], a[2] + a[6], a[1] + a[5], a[3] + a[7]
        d04, d26, d15, d37 = a[0] - a[4], a[2] - a[6], a[1] - a[5], a[3] - a[7]
        zeros.append((s04 + s26) + (s15 + s37))
        mids.append((s04 + s26) - (s15 + s37))
        minus, plus = ROOT * (d15 - d37), ROOT * (d15 + d37)
        turned = (
            (d04 + minus, -d26 - plus),
            (s04 - s26, s37 - s15),
            (d04 - minus, d26 - plus),
        )
        for index, (real, imag) in enumerate(turned):
            c, s = turns[index : index + 1, :], turns[index + 3 : index + 4, :]
            reals[index].append(real * c + imag * s)
            imags[index].append(imag * c - real * s)
    stacked = jnp.concatenate(
        [
            jnp.concatenate([jnp.concatenate(reals[i], axis=0) for i in range(3)], axis=0),
            jnp.concatenate([jnp.concatenate(imags[i], axis=0) for i in range(3)], axis=0),
        ],
        axis=1,
    )
    full, zero, middle = x_parts(tables, base)
    full = exact_dot(split(stacked), full)
    zero = exact_dot(split(jnp.concatenate(zeros, axis=0)), zero)
    middle = exact_dot(split(jnp.concatenate(mids, axis=0)), middle)
    low = lane_index((rows, LANES)) % 64 < 32
    target = 0
    blocks = [full[2 * rows * i : 2 * rows * (i + 1)] for i in range(3)] + [zero, middle]
    for block in blocks:
        for first in range(0, block.shape[1], LANES):
            a = block[:rows, first : first + LANES]
            c = block[rows:, first : first + LANES]
            out[target] = jnp.where(low, a, spin(c, 32))
            out[target + 1] = jnp.where(low, spin(a, -32), c)
            target += 2


def eighths(x, turn):
    s04, s26, s15, s37 = x[0] + x[4], x[2] + x[6], x[1] + x[5], x[3] + x[7]
    d04, d26, d15, d37 = x[0] - x[4], x[2] - x[6], x[1] - x[5], x[3] - x[7]
    quarter = turn(s15 - s37)
    spun_26, spun_37 = turn(d26), turn(d37)
    one, three = d15 + spun_37, d15 - spun_37
    spun_one, spun_three = turn(one), turn(three)
    one = ROOT * (one + spun_one)
    three = ROOT * (spun_three - three)
    return [
        (s04 + s26) + (s15 + s37),
        (d04 + spun_26) + one,
        (s04 - s26) + quarter,
        (d04 - spun_26) + three,
        (s04 + s26) - (s15 + s37),
        (d04 + spun_26) - one,
        (s04 - s26) - quarter,
        (d04 - spun_26) - three,
    ]


def solve_y_kernel(count_x, _, lines, total, wave, both, turns, out, held, spread):
    count, rows, _ = lines.shape
    base = turns.shape[0]
    length = count * rows
    block = count_x * rows
    per = base // rows
    lanes = lane_index((base, LANES))
    sign = jnp.where(lanes < 64, 1.0, -1.0).astype(F32)

    def minus_i(z):
        return spin(z, 64) * sign

    def plus_i(z):
        return spin(z, 64) * -sign

    fields = [
        jnp.concatenate([lines[t * per + k] for k in range(per)], axis=0) for t in range(RADIX)
    ]
    mixed = eighths(fields, minus_i)
    terms, columns = turns.shape[1], 2 * RADIX
    picked = lax.broadcasted_iota(jnp.int32, (terms, columns * LANES), 0) % columns
    lane = lane_index(picked.shape)
    value = jnp.where((lane >= RADIX * LANES) & (lane % LANES >= 64), -1.0, 1.0)
    spread[...] = dot(turns[...], jnp.where(picked == lane // LANES, value, 0.0).astype(BF16))
    cosines = [spread[:, r * LANES : (r + 1) * LANES] for r in range(RADIX)]
    sines = [spread[:, (r + RADIX) * LANES : (r + RADIX + 1) * LANES] for r in range(RADIX)]
    mixed = [mixed[0]] + [
        mixed[r] * cosines[r] + spin(mixed[r], 64) * sines[r] for r in range(1, RADIX)
    ]
    tables = (both[: 2 * base], both[2 * base :])
    product = exact_dot(tables, split(jnp.concatenate(mixed, axis=1)))
    kx = wave[0:1, :]
    first = lanes % 64 < 32
    edge = jnp.float32(length // 2)
    alone = jnp.where(first, kx * kx, 0.0)
    slope = jnp.where(first | (kx == -edge), 0.0, jnp.broadcast_to(kx, lanes.shape))
    q = lax.broadcasted_iota(jnp.int32, lanes.shape, 0)
    low_ky = RADIX * (q - jnp.where(q < base // 2, 0, base)).astype(F32)
    terms = []
    for r in range(RADIX):
        at = slice(r * LANES, (r + 1) * LANES)
        spectrum = product[:base, at] + minus_i(product[base:, at])
        ky = low_ky + float(r)
        symbol = alone + slope * ky
        if r == 0:
            corner = jnp.where((kx == -edge) & ~first, edge * edge, 0.0)
            symbol = jnp.where(ky == -edge, jnp.where(first, alone, corner), symbol)
        terms.append(symbol * pl.reciprocal(kx * kx + ky * ky) * spectrum)
    pairs = [
        jnp.where(first, low + spin(low, -32), high + spin(high, 32))
        for low, high in zip(terms[:4], terms[4:])
    ]
    product = exact_dot(tables, split(jnp.concatenate(pairs, axis=1)))
    mixed = []
    for r in range(RADIX // 2):
        at = slice(r * LANES, (r + 1) * LANES)
        value = product[:base, at] + plus_i(product[base:, at])
        cosine = jnp.where(first, cosines[r], cosines[r + 4])
        sine = jnp.where(first, sines[r], sines[r + 4])
        value = value * cosine - spin(value, 64) * sine
        value = jnp.where(first, value + spin(value, -32), spin(value, 32) - value)
        if r == 2:
            value = jnp.where(first, value, plus_i(value))
        elif r:
            turned = plus_i(value)
            odd = value + turned if r == 1 else turned - value
            value = jnp.where(first, value, ROOT * odd)
        mixed.append(value)
    even, odd = mixed[0] + mixed[2], mixed[0] - mixed[2]
    side, turned = mixed[1] + mixed[3], plus_i(mixed[1] - mixed[3])
    for t, values in enumerate((even + side, odd + turned, even - side, odd - turned)):
        start = MARGIN + 2 * t * base
        held[start : start + base, :] = values
        held[start + base : start + 2 * base, :] = spin(values, -32)
    held[0:MARGIN, :] = held[length : length + MARGIN, :]
    held[length + MARGIN : length + 2 * MARGIN, :] = held[MARGIN : 2 * MARGIN, :]
    spare = total[...] + spin(total[...], 32)
    kept = rows + 2 * MARGIN // count_x
    half = out.shape[1]
    rest = kept - half
    low = lane_index((8, LANES)) % 64 < 32
    for target in range(count):
        start = (target // count_x) * block + (target % count_x) * kept
        for row in range(0, half, 8):
            a = held[start + row : start + row + 8, :]
            if row < rest:
                b = spin(held[start + half + row : start + half + row + 8, :], 32)
            else:
                b = spare
            out[target, row : row + 8, :] = jnp.where(low, a, b)


def inverse_x_kernel(
    kept, scale, place, lines, tables, turns, *refs
):
    *outs, held = refs
    count, half, _ = lines.shape
    base = turns.shape[1]
    length = RADIX * base
    rest = kept - half
    low = lane_index((half, LANES)) % 64 < 32
    groups, spare = [], None
    for first in range(0, count, 2):
        even, odd = lines[first], lines[first + 1]
        a = jnp.where(low, even, spin(odd, 32))
        b = jnp.where(low, spin(even, -32), odd)
        groups.append(jnp.concatenate([a, b[:rest]], axis=0))
        extra = b[rest : rest + 8]
        spare = extra if spare is None else spare + extra
    mean = jnp.sum(spare) * scale
    wide = 2 * base // LANES
    narrow = base // LANES
    stacked = jnp.concatenate(
        [jnp.concatenate(groups[i * wide : (i + 1) * wide], axis=1) for i in range(3)], axis=0
    )
    at = 3 * wide
    zeros = jnp.concatenate(groups[at : at + narrow], axis=1)
    mids = jnp.concatenate(groups[at + narrow : at + 2 * narrow], axis=1)
    full, zero, middle = x_parts(tables, base)
    full = exact_dot(split(stacked), full)
    zero = exact_dot(split(zeros), zero) * scale
    mid = exact_dot(split(mids), middle) * scale
    turned = []
    for i in range(3):
        real = full[i * kept : (i + 1) * kept, :base]
        imag = full[i * kept : (i + 1) * kept, base:]
        c = turns[i : i + 1, :] * (2.0 * scale)
        s = turns[i + 3 : i + 4, :] * (2.0 * scale)
        turned.append((real * c - imag * s, real * s + imag * c))
    for t in range(RADIX):
        value = zero + mid if t % 2 == 0 else zero - mid
        for i, (real, imag) in enumerate(turned):
            eighth = t * (i + 1) % RADIX
            c = (1.0, ROOT, 0.0, -ROOT, -1.0, -ROOT, 0.0, ROOT)[eighth]
            s = (0.0, ROOT, 1.0, ROOT, 0.0, -ROOT, -1.0, -ROOT)[eighth]
            if c:
                value = value + c * real
            if s:
                value = value - s * imag
        held[:, t * base : (t + 1) * base] = mean - value
    targets, local = len(outs), outs[0].shape[1] - LANES
    right = lane_index((kept, LANES)) < 64
    for mask, out in enumerate(outs):
        start = pl.multiple_of((place[0] ^ mask) * local, LANES)
        after = pl.multiple_of(jnp.where(start + local == length, 0, start + local), LANES)
        before = pl.multiple_of(jnp.where(start == 0, length, start) - LANES, LANES)
        out[:, :local] = held[:, pl.ds(start, local)]
        out[:, local:] = jnp.where(
            right, held[:, pl.ds(after, LANES)], held[:, pl.ds(before, LANES)]
        )


def slopes_x(parts, band, with_edge):
    tiles = parts[0].shape[-1] // LANES
    pieces = []
    for first in list(range(0, tiles - 1, 2)) + ([tiles - 1] if with_edge else []):
        steps = (-1, 0, 1, 2) if first < tiles - 1 else (-1, 0, 1)
        table = band[...] if first < tiles - 1 else band[: 3 * LANES, :LANES]
        order = [(first + step) % tiles for step in steps]
        piece = None
        for part in parts:
            term = dot(jnp.concatenate([lane_tile(part, t) for t in order], axis=1), table)
            piece = term if piece is None else piece + term
        pieces.append(piece)
    return jnp.concatenate(pieces, axis=1)


def slope_y(read):
    value = read(3) - read(-3)
    for index in (0, 1):
        value = value + whole_weights[index] * (read(index + 1) - read(-index - 1))
    return value


def edged(k, side, center, up, down, above, below, sides, has, first=0):
    step = pl.program_id(0) + first
    tile, width = center.shape
    tall = sides.shape[1]
    last = (tall - LANES) // tile - 1
    base = pl.multiple_of(step * tile, 8)
    before = pl.multiple_of(jnp.where(step == 0, tall, base) - HALO, 8)
    over = jnp.where(step == 0, strip(above, k, True) * has[2], up)
    under = jnp.where(step == last, strip(below, k, False) * has[3], down)
    rows = (
        (over, sides[side, pl.ds(before, HALO), :]),
        (center, sides[side, pl.ds(base, tile), :]),
        (under, sides[side, pl.ds(pl.multiple_of(base + tile, 8), HALO), :]),
    )
    return jnp.concatenate([jnp.concatenate(pair, axis=1) for pair in rows], axis=0)


def edged_open(k, side, wall, wall_up, wall_down, above, below, sides, has, first=0):
    open_cells = [1.0 - ref[0].astype(F32) for ref in (wall, wall_up, wall_down)]
    return edged(k, side, *open_cells, above, below, sides, has, first)


def quiet_step_kernel(
    first, has, place, center, up, down, wall, wall_up, wall_down, above, below, sides, across, along, along_inner, out, shown_open, mark
):
    parts, _, tile, width = center.shape
    high = tile + 2 * HALO
    opened = edged_open(parts, parts, wall, wall_up, wall_down, above, below, sides, has, first)
    values = []
    for k in range(parts):
        value = edged(
            k,
            k,
            center[k, 0].astype(F32),
            up[k, 0].astype(F32)[up.shape[2] - HALO :],
            down[k, 0].astype(F32)[:HALO],
            above,
            below,
            sides,
            has,
            first,
        )
        values.append(value)

    def drops(x, along_b, along_p):
        diverge = x[1] + along_b
        return (
            diverge + mean_flow * x[0],
            x[3] + mean_flow * x[1],
            along_p + mean_flow * x[2],
            diverge + mean_flow * x[3],
        )

    short = [value.astype(BF16) for value in values]
    x = slopes_x((jnp.concatenate(short, axis=0),), across, True)
    x = [x[k * high : (k + 1) * high] for k in range(parts)]
    table = along[...]
    dropped = drops(x, dot(table, short[2]), dot(table, short[3]))
    middle = [opened * (v - (time_step / 60.0) * d) for v, d in zip(values, dropped)]
    inner = slice(HALO, HALO + tile)
    x = slopes_x(split(jnp.concatenate([value[inner] for value in middle], axis=0)), across, False)
    x = [x[k * tile : (k + 1) * tile] for k in range(parts)]
    table = along_inner[...]
    y = [sum(dot(table, part) for part in split(middle[k][:, :width])) for k in (2, 3)]
    dropped = drops(x, *y)
    shown = opened[inner, :width]
    for k in range(parts):
        start = 0.5 * values[k][inner, :width] - (0.5 * time_step / 60.0) * dropped[k]
        out[k] = shown * start + 0.5 * middle[k][inner, :width]
    shown_open[0] = opened.astype(BF16)
    mark[0] = place[0]


def tables_kernel(place, weights_x, weights_y, rise_x, rise_y):
    tiles, reach_x, lanes = rise_x.shape
    wide, length_x = (tiles - 1) * lanes, weights_x.shape[1]
    first = place[0] * wide
    half = LANES // 2

    def weights(ref, start, size):
        length = ref.shape[1]
        start = jnp.where(start < 0, start + length, jnp.where(start >= length, start - length, start))
        return ref[:, pl.ds(pl.multiple_of(start, LANES), size)]

    cells = lax.broadcasted_iota(jnp.int32, (reach_x, lanes), 0)
    fine = lax.broadcasted_iota(jnp.int32, (reach_x, lanes), 1)
    right, left = weights(weights_x, first + wide, LANES), weights(weights_x, first - LANES, LANES)
    edge = jnp.where(lane_index(right.shape) < half, right, left)
    edge = jnp.concatenate([edge, edge], axis=1)
    for k in range(tiles):
        own = weights(weights_x, first + k * lanes, lanes) if k < tiles - 1 else edge
        target = fine // 2 - 1
        if k == tiles - 1:
            target = jnp.where(fine < half, target, target + half)
        value = jnp.zeros(fine.shape, F32)
        for t in range(4):
            value = jnp.where(cells == (target + t) % reach_x, own[t : t + 1, :], value)
        rise_x[k] = value
    steps, high, reach = rise_y.shape
    tall = steps * TILE
    first = place[1] * tall
    own = [weights(weights_y, first + k * LANES, LANES) for k in range(-1, tall // LANES + 1)]
    own = jnp.concatenate([jnp.concatenate(own, axis=1), jnp.zeros((4, tall + 2 * LANES), F32)], axis=0).T
    cells = lax.broadcasted_iota(jnp.int32, (high, reach), 1) % (reach // 3)
    target = lax.broadcasted_iota(jnp.int32, (high, reach), 0) // 2 + (HALO // 2 - 1)
    for k in range(steps):
        start = LANES - HALO + k * TILE
        value = jnp.zeros((high, reach), F32)
        for t in range(4):
            value = jnp.where(cells == target + t, own[start : start + high, t : t + 1], value)
        rise_y[k] = value


def source_kernel(place, squares, opened, rise_x, rise_y, quiet, across, *refs):
    *lines, out, squared, cells_open, matrix, rows_matrix, calm, band, held, raised, forced, done, fetched, kept = refs
    steps = done.shape[0]
    tile, width = calm.shape[2:]
    high = tile + 2 * HALO
    rows = lines[0].shape[0]

    def calm_copy(k):
        part = quiet.at[:, pl.ds(k * tile, tile), :]
        return pltpu.make_async_copy(part, calm.at[k % 2], fetched.at[k % 2])

    def done_copy(k):
        part = out.at[:, 0, pl.ds(k * tile, tile), :]
        return pltpu.make_async_copy(done.at[k], part, kept.at[k])

    arrays = [(squares, squared), (rise_x, matrix), (rise_y, rows_matrix), (opened, cells_open), (across, band)]
    copies = [
        pltpu.make_async_copy(source, target, fetched.at[2 + k])
        for k, (source, target) in enumerate(arrays)
    ]
    pieces = [
        pltpu.make_async_copy(
            piece,
            held.at[pl.ds(pl.multiple_of((place[0] ^ mask) * rows, 8), rows), :],
            fetched.at[2 + len(arrays) + mask],
        )
        for mask, piece in enumerate(lines)
    ]
    for copy in pieces + copies:
        copy.start()
    calm_copy(0).start()
    calm_copy(1).start()
    for copy in pieces + copies[:1]:
        copy.wait()

    level = held[MARGIN - HALO : MARGIN - HALO + squared.shape[0], :] - squared[...]
    count = level.shape[1] // LANES
    near = lane_index((level.shape[0], LANES)) < 64
    around = []
    for k in range(count):
        after, before = lane_tile(level, (k + 1) % count), lane_tile(level, (k - 1) % count)
        around.append(split(jnp.concatenate([lane_tile(level, k), jnp.where(near, after, before)], axis=1)))
    copies[1].wait()
    for k in range(count):
        lanes = 2 * LANES if k < count - 1 else LANES
        value = split(exact_dot(around[k], split(matrix[k][:, :lanes])))
        for part in range(2):
            raised[part, :, 2 * k * LANES : 2 * k * LANES + lanes] = value[part]
    for copy in copies[2:]:
        copy.wait()

    reach = rows_matrix.shape[2] // 3
    third = lane_index((high, 3 * reach)) >= 2 * reach
    for k in range(steps):
        start = k * (tile // 2)
        window = [raised[part, start : start + reach, :] for part in (0, 1, 0)]
        weights = split(rows_matrix[k])
        weights = jnp.where(third, weights[1], weights[0])
        free = time_step * cells_open[k].astype(F32)
        value = free * dot(weights, jnp.concatenate(window, axis=0))
        forced[k % 2] = value
        inner = value[HALO : HALO + tile]
        shown = (0.5 / 60.0) * free[HALO : HALO + tile, :width]
        x = shown * slopes_x(split(inner), band, False)
        y = shown * slope_y(lambda d: forced[k % 2, HALO + d : HALO + d + tile, :width])
        calm_copy(k).wait()
        still = calm.at[k % 2]
        done[k, 0] = still[0].astype(BF16)
        done[k, 1] = (still[1] - x).astype(BF16)
        done[k, 2] = (still[2] - y).astype(BF16)
        done[k, 3] = (still[3] + inner[:, :width] - mean_flow * x).astype(BF16)
        done_copy(k).start()
        if k + 2 < steps:
            calm_copy(k + 2).start()
    for k in range(steps):
        done_copy(k).wait()


def call(
    kernel, operands, outs, scratch=(), steps=0, specs=None, out_specs=None, after=(), aliases=None, megabytes=24, flops=0, moved=0, name=None
):
    count = len(operands)

    def body(*refs):
        kernel(*refs[:count], *refs[count + len(after) :])

    def whole(array):
        zeros = (0,) * len(array.shape)
        return pl.BlockSpec(array.shape, lambda *_: zeros)

    arguments = {}
    chosen = specs or {}
    if steps:
        arguments["grid"] = (steps,)
        in_specs = [chosen.get(i, whole(o)) for i, o in enumerate(operands)]
        arguments["out_specs"] = jax.tree.map(whole, outs) if out_specs is None else out_specs
    else:
        local = pl.BlockSpec(memory_space=pltpu.VMEM)
        in_specs = [chosen.get(i, local) for i in range(count)]
        if out_specs is not None:
            arguments["out_specs"] = out_specs
    return pl.pallas_call(
        body,
        out_shape=outs,
        in_specs=in_specs + [pl.BlockSpec(memory_space=pl.ANY)] * len(after),
        scratch_shapes=list(scratch),
        input_output_aliases=aliases or {},
        compiler_params=pltpu.CompilerParams(vmem_limit_bytes=megabytes << 20),
        cost_estimate=pl.CostEstimate(flops=flops, bytes_accessed=moved, transcendentals=0),
        name=name,
        **arguments,
    )(*operands, *after)


def ring(array, axis, step):
    size = lax.axis_size(axis)
    return lax.ppermute(array, axis, [(i, (i + step) % size) for i in range(size)])


def swap(array, axis, mask):
    return lax.ppermute(array, axis, [(i, i ^ mask) for i in range(lax.axis_size(axis))])


def shaped(*shape, kind=F32):
    return jax.ShapeDtypeStruct(shape, kind)


def pressure_lines(pieces, place_x, gathered, spread, stepped):
    _, rows, local_x = pieces[0].shape
    count_x, count_y = lax.axis_size("gx"), lax.axis_size("gy")
    count = count_x * count_y
    scalars = {0: pl.BlockSpec(memory_space=pltpu.SMEM)}
    length_x, length_y = local_x * count_x, rows * count
    full, zero, middle, cos_turn, sin_turn = x_tables(length_x)
    turns = np.zeros((8, cos_turn.shape[1]), np.float32)
    turns[0:3], turns[3:6] = cos_turn, sin_turn
    spectra, total = call(
        forward_x_kernel,
        (place_x, *pieces, np.concatenate([beside(full), beside(zero, middle)]), turns),
        (shaped(count, rows, LANES), shaped(8, LANES)),
        (pltpu.VMEM((count_x, 2, rows, local_x), F32),),
        specs=scalars,
        after=gathered,
        flops=10**9,
        moved=4 << 20,
        name="forward_x",
    )
    spectra = lax.all_to_all(spectra, ("gy", "gx"), 0, 0, tiled=True)
    place = lax.axis_index("gy") * count_x + lax.axis_index("gx")
    waves = jnp.asarray(wave_table(length_x, count))
    wave = lax.dynamic_slice(waves, (place, 0), (1, LANES))
    both, turns_y = y_tables(length_y)
    kept = rows + 2 * MARGIN // count_x
    half = (kept // 2 + 8) // 8 * 8
    solved = call(
        functools.partial(solve_y_kernel, count_x),
        (spread, spectra, total, wave, beside(both), turns_y),
        shaped(count, half, LANES),
        (
            pltpu.VMEM((length_y + 2 * MARGIN, LANES), F32),
            pltpu.VMEM((length_y // RADIX, 2 * RADIX * LANES), F32),
        ),
        specs=scalars,
        flops=4 * 10**9,
        moved=6 << 20,
        name="solve_y",
    )
    solved = lax.all_to_all(solved, ("gy", "gx"), 0, 0, tiled=True)
    back = 2.0 * zero.T
    back[LANES // 2] *= 0.5
    tables = np.concatenate(
        [beside(full.T), beside(back, 2.0 * middle.T)]
    )
    pressed = call(
        functools.partial(inverse_x_kernel, kept, 1.0 / (length_x * length_y)),
        (stepped, solved, tables, turns),
        (shaped(kept, local_x + LANES),) * count_x,
        (pltpu.VMEM((kept, length_x), F32),),
        specs=scalars,
        flops=10**9,
        moved=4 << 20,
        name="inverse_x",
    )
    return [piece if mask == 0 else swap(piece, "gx", mask) for mask, piece in enumerate(pressed)]


def fast_shards(velocity, weights_x, weights_y, acoustic, wall_mask):
    parts, _, tall, wide = acoustic.shape
    _, _, local_y, local_x = velocity.shape
    count_x, count_y = lax.axis_size("gx"), lax.axis_size("gy")
    place_x, place_y = lax.axis_index("gx"), lax.axis_index("gy")
    full, high, steps = wide + LANES, TILE + 2 * HALO, tall // TILE
    strips = (parts + 2) * HALO
    small = 2 * HALO
    has = jnp.stack([place_x > 0, place_x < count_x - 1, place_y > 0, place_y < count_y - 1])
    has = has.astype(F32)
    scalars = pl.BlockSpec(memory_space=pltpu.SMEM)

    def at(block, *index):
        return pl.BlockSpec(block, lambda i: index)

    own = place_x.astype(jnp.int32).reshape(1)
    sent = call(
        pieces_kernel,
        (own, velocity),
        (shaped(2, local_y // count_x, local_x),) * count_x,
        specs={0: scalars},
        moved=2 << 20,
        megabytes=8,
        name="pieces",
    )
    moved = [piece if mask == 0 else swap(piece, "gx", mask) for mask, piece in enumerate(sent)]
    first, last = call(
        rows_kernel,
        (acoustic, acoustic, wall_mask, wall_mask, velocity, velocity),
        (shaped(STRIP_ROWS, wide),) * 2,
        steps=1,
        specs={
            0: at((parts, 1, small, wide), 0, 0, 0, 0),
            1: at((parts, 1, small, wide), 0, 0, tall // small - 1, 0),
            2: at((1, HALO, wide), 0, 0, 0),
            3: at((1, HALO, wide), 0, tall // HALO - 1, 0),
            4: at((1, 1, HALO, local_x), 1, 0, 0, 0),
            5: at((1, 1, HALO, local_x), 1, 0, local_y // HALO - 1, 0),
        },
        after=moved[1:2],
        moved=2 << 20,
        megabytes=54,
        name="rows",
    )
    above, below = ring(last, "gy", 1), ring(first, "gy", -1)
    to_right, to_left = call(
        columns_kernel,
        (has, acoustic, acoustic, wall_mask, wall_mask, velocity, velocity, above, below),
        (shaped(strips, tall + LANES), shaped(strips, tall + LANES)),
        steps=1,
        specs={
            0: scalars,
            1: at((parts, 1, tall, LANES), 0, 0, 0, 0),
            2: at((parts, 1, tall, LANES), 0, 0, 0, wide // LANES - 1),
            3: at((1, tall, LANES), 0, 0, 0),
            4: at((1, tall, LANES), 0, 0, wide // LANES - 1),
            5: at((1, 1, local_y, LANES), 1, 0, 0, 0),
            6: at((1, 1, local_y, LANES), 1, 0, 0, local_x // LANES - 1),
        },
        moved=8 << 20,
        megabytes=54,
        name="columns",
    )
    from_left, from_right = ring(to_right, "gx", 1), ring(to_left, "gx", -1)
    sides, squares, beside = call(
        sides_kernel,
        (has, own, velocity, above, below, from_left, from_right),
        (
            shaped(parts + 1, tall + LANES, LANES),
            shaped(local_y + 2 * HALO, local_x + LANES),
            shaped(1, kind=jnp.int32),
        ),
        steps=1,
        specs={0: scalars, 1: scalars, 2: at((1, 1, local_y, local_x), 1, 0, 0, 0)},
        out_specs=(
            at((parts + 1, tall + LANES, LANES), 0, 0, 0),
            at((local_y + 2 * HALO, local_x + LANES), 0, 0),
            scalars,
        ),
        moved=8 << 20,
        megabytes=54,
        name="sides",
    )
    across, along = band_tables(high)
    along_inner = along[HALO : HALO + TILE]
    per, rows = TILE // small, TILE // HALO

    def tiled(first):
        walls = (
            pl.BlockSpec((1, TILE, wide), lambda i: (0, i + first, 0)),
            pl.BlockSpec((1, HALO, wide), lambda i: (0, jnp.maximum((i + first) * rows - 1, 0), 0)),
            pl.BlockSpec(
                (1, HALO, wide),
                lambda i: (0, jnp.minimum((i + first + 1) * rows, steps * rows - 1), 0),
            ),
        )
        cells = (
            pl.BlockSpec((parts, 1, TILE, wide), lambda i: (0, 0, i + first, 0)),
            pl.BlockSpec(
                (parts, 1, small, wide), lambda i: (0, 0, jnp.maximum((i + first) * per - 1, 0), 0)
            ),
            pl.BlockSpec(
                (parts, 1, small, wide),
                lambda i: (0, 0, jnp.minimum((i + first + 1) * per, steps * per - 1), 0),
            ),
        )
        return cells, walls, pl.BlockSpec((parts, TILE, wide), lambda i: (0, i + first, 0))

    def quiet_tiles(first, count, before):
        cells, walls, flat = tiled(first)
        operands = (has, own, acoustic, acoustic, acoustic, wall_mask, wall_mask, wall_mask, above, below, sides)
        operands = operands + (across, along, along_inner)
        return call(
            functools.partial(quiet_step_kernel, first),
            operands,
            (shaped(parts, tall, wide), shaped(steps, high, full, kind=BF16), shaped(1, kind=jnp.int32)),
            steps=count,
            specs=dict(enumerate((scalars, scalars) + cells + walls)),
            out_specs=(flat, pl.BlockSpec((1, high, full), lambda i: (i + first, 0, 0)), scalars),
            after=before,
            aliases={len(operands): 0, len(operands) + 1: 1} if before else None,
            megabytes=54,
            flops=3 * 10**9 * count,
            moved=(12 << 20) * count,
            name="quiet_step",
        )

    early = max(steps * 3 // 4, 1)
    *begun, stepped = quiet_tiles(0, early, ())
    quiet, opened = begun
    if early < steps:
        quiet, opened, _ = quiet_tiles(early, steps - early, begun)
    rows_done = above[:8, :LANES] + below[:8, :LANES]
    lines = pressure_lines(moved, own, (rows_done,), beside, stepped)
    tiles = wide // (2 * LANES) + 1
    rise_x, rise_y = call(
        tables_kernel,
        (jnp.stack([place_x, place_y]).astype(jnp.int32), weights_x, weights_y),
        (shaped(tiles, 2 * LANES, 2 * LANES), shaped(steps, high, 3 * (high // 2 + HALO))),
        specs={0: scalars},
        moved=4 << 20,
        megabytes=54,
        name="tables",
    )
    operands = (own, squares, opened, rise_x, rise_y, quiet, across, *lines)
    anywhere = pl.BlockSpec(memory_space=pl.ANY)
    specs = {k: anywhere for k in range(1, len(operands))}
    scratch = (
        pltpu.VMEM(squares.shape, F32),
        pltpu.VMEM(opened.shape, BF16),
        pltpu.VMEM(rise_x.shape, F32),
        pltpu.VMEM(rise_y.shape, F32),
        pltpu.VMEM((2, parts, TILE, wide), F32),
        pltpu.VMEM(across.shape, BF16),
        pltpu.VMEM((local_y + 2 * MARGIN, local_x + LANES), F32),
        pltpu.VMEM((2, local_y + 2 * HALO, full), BF16),
        pltpu.VMEM((2, high, full), F32),
        pltpu.VMEM((steps, parts, TILE, wide), BF16),
        pltpu.SemaphoreType.DMA((7 + count_x,)),
        pltpu.SemaphoreType.DMA((steps,)),
    )
    return call(
        source_kernel,
        operands,
        shaped(*acoustic.shape, kind=BF16),
        scratch,
        specs={0: scalars, **specs},
        out_specs=anywhere,
        megabytes=56,
        flops=4 * 10**9,
        moved=16 << 20,
        name="source_step",
    )


def fits(count_x, count_y, velocity, acoustic):
    _, planes, local_y, local_x = velocity
    _, _, tall, wide = acoustic
    length_x, length_y = local_x * count_x, local_y * count_y
    rows = local_y // count_x
    base_x, base_y = length_x // RADIX, length_y // RADIX
    return (
        planes == 1
        and acoustic[0] == PARTS
        and length_x * 2 == count_x * count_y * LANES
        and base_x % (2 * LANES) == 0
        and local_x % base_x == 0
        and rows % 8 == 0
        and base_y % rows == 0
        and base_y % 8 == 0
        and MARGIN * 2 % (8 * count_x) == 0
        and tall == 2 * local_y
        and wide == 2 * local_x
        and tall % TILE == 0
        and tall % LANES == 0
        and tall >= 2 * TILE
        and count_x & (count_x - 1) == 0
        and wide % (2 * LANES) == 0
    )


def extended(array, sides, width):
    for axis, dim in sides:
        size, length = (lax.axis_size(axis), array.shape[dim])
        up = [(i, (i + 1) % size) for i in range(size - 1)]
        down = [(j, i) for i, j in up]
        last = lax.slice_in_dim(array, length - width, length, axis=dim)
        leading = lax.slice_in_dim(array, 0, width, axis=dim)
        before = lax.ppermute(last, axis, up)
        after = lax.ppermute(leading, axis, down)
        array = jnp.concatenate([before, array, after], axis=dim)
    return array


def gradients(padded):
    height = padded.shape[-2] - 6
    breadth = padded.shape[-1] - 6
    rows_mid = padded[..., 3 : 3 + height, :]
    cols_mid = padded[..., :, 3 : 3 + breadth]
    along_x = jnp.zeros_like(padded[..., 3 : 3 + height, 3 : 3 + breadth])
    along_y = jnp.zeros_like(along_x)
    for index, weight in enumerate(stencil_weights):
        distance = index + 1
        along_x = along_x + weight * (
            rows_mid[..., 3 + distance : 3 + distance + breadth]
            - rows_mid[..., 3 - distance : 3 - distance + breadth]
        )
        along_y = along_y + weight * (
            cols_mid[..., 3 + distance : 3 + distance + height, :]
            - cols_mid[..., 3 - distance : 3 - distance + height, :]
        )
    return (along_x, along_y)


def tendency(padded, source):
    along_x, along_y = gradients(padded)
    diverge = along_x[1] + along_y[2]
    forcing = jnp.stack([-diverge, -along_x[3], -along_y[3], source - diverge])
    return forcing - mean_flow * along_x


def spectral_index(flat, length):
    second = length // 16
    wave = flat // second + 16 * (flat % second)
    return jnp.where(wave < length // 2, wave, wave - length).astype(jnp.float32)


def twiddles(rows_count, cols_count, modulus, sign):
    products = jnp.arange(rows_count)[:, None] * jnp.arange(cols_count)[None, :] % modulus
    angles = 2.0 * math.pi / modulus * products.astype(jnp.float32)
    return (jnp.cos(angles), sign * jnp.sin(angles))


def mix_rows(real_part, imag_part, cosine, sine):
    exact = lax.Precision.HIGHEST
    cos_real = jnp.einsum("ka,...ab->...kb", cosine, real_part, precision=exact)
    cos_imag = jnp.einsum("ka,...ab->...kb", cosine, imag_part, precision=exact)
    sin_real = jnp.einsum("ka,...ab->...kb", sine, real_part, precision=exact)
    sin_imag = jnp.einsum("ka,...ab->...kb", sine, imag_part, precision=exact)
    return (cos_real - sin_imag, cos_imag + sin_real)


def mix_cols(real_part, imag_part, cosine, sine):
    exact = lax.Precision.HIGHEST
    cos_real = jnp.einsum("...kb,bc->...kc", real_part, cosine, precision=exact)
    cos_imag = jnp.einsum("...kb,bc->...kc", imag_part, cosine, precision=exact)
    sin_real = jnp.einsum("...kb,bc->...kc", real_part, sine, precision=exact)
    sin_imag = jnp.einsum("...kb,bc->...kc", imag_part, sine, precision=exact)
    return (cos_real - sin_imag, cos_imag + sin_real)


def rotate(real_part, imag_part, cosine, sine):
    return (real_part * cosine - imag_part * sine, real_part * sine + imag_part * cosine)


def discrete(real_part, imag_part, sign):
    length = real_part.shape[-1]
    second = length // 16
    initial = real_part.shape
    folded = initial[:-1] + (16, second)
    real_part = real_part.reshape(folded)
    imag_part = imag_part.reshape(folded)
    small_cos, small_sin = twiddles(16, 16, 16, sign)
    large_cos, large_sin = twiddles(second, second, second, sign)
    turn_cos, turn_sin = twiddles(16, second, length, sign)
    if sign < 0:
        real_part, imag_part = mix_rows(real_part, imag_part, small_cos, small_sin)
        real_part, imag_part = rotate(real_part, imag_part, turn_cos, turn_sin)
        real_part, imag_part = mix_cols(real_part, imag_part, large_cos, large_sin)
    else:
        real_part, imag_part = mix_cols(real_part, imag_part, large_cos, large_sin)
        real_part, imag_part = rotate(real_part, imag_part, turn_cos, turn_sin)
        real_part, imag_part = mix_rows(real_part, imag_part, small_cos, small_sin)
        real_part = real_part / length
        imag_part = imag_part / length
    return (real_part.reshape(initial), imag_part.reshape(initial))


def transform(stacked, sign, kind):
    if kind == "real_in":
        real_part = stacked
        imag_part = jnp.zeros_like(stacked)
    else:
        half = stacked.shape[0] // 2
        real_part = stacked[:half]
        imag_part = stacked[half:]
    real_out, imag_out = discrete(real_part, imag_part, sign)
    if kind == "real_out":
        return real_out
    return jnp.concatenate([real_out, imag_out], axis=0)


def project(stacked, wave_x, wave_y):
    coef_xx = wave_x * wave_x
    coef_xy = 2.0 * wave_x * wave_y
    coef_yy = wave_y * wave_y
    denominator = wave_x * wave_x + wave_y * wave_y
    positive = denominator > 0
    safe = jnp.where(positive, denominator, 1.0)

    def combine(parts):
        numerator = -(coef_xx * parts[0] + coef_xy * parts[1] + coef_yy * parts[2])
        return jnp.where(positive, numerator / safe, 0.0)

    return jnp.stack([combine(stacked[:3]), combine(stacked[3:])])


def refine(stacked, weights):
    result = jnp.zeros(stacked.shape[:-1] + (2 * stacked.shape[-1],), jnp.float32)
    for offset in range(4):
        result = (
            result
            + jnp.repeat(jnp.roll(stacked, 1 - offset, axis=-1), 2, axis=-1) * weights[offset]
        )
    return result


def lines_x(stacked, action):
    gathered = action(lax.all_to_all(stacked, "gx", split_axis=2, concat_axis=3, tiled=True))
    return lax.all_to_all(gathered, "gx", split_axis=3, concat_axis=2, tiled=True)


def lines_y(stacked, action):
    turned = jnp.swapaxes(stacked, 2, 3)
    gathered = action(lax.all_to_all(turned, "gy", split_axis=2, concat_axis=3, tiled=True))
    returned = lax.all_to_all(gathered, "gy", split_axis=3, concat_axis=2, tiled=True)
    return jnp.swapaxes(returned, 2, 3)


def expand(fields):
    return extended(fields, (("gx", 3), ("gy", 2)), 3)


def shards(velocity, weights_x, weights_y, acoustic, wall_mask):
    acoustic = acoustic.astype(jnp.float32)
    flow_x = velocity[0]
    flow_y = velocity[1]
    tensor = jnp.stack([flow_x * flow_x, flow_x * flow_y, flow_y * flow_y])
    count_gx = lax.axis_size("gx")
    count_gy = lax.axis_size("gy")
    place_x = lax.axis_index("gx")
    place_y = lax.axis_index("gy")
    local_y = tensor.shape[2]
    local_x = tensor.shape[3]
    length_x = local_x * count_gx
    length_y = local_y * count_gy

    def forward_real(portion):
        return transform(portion, -1, "real_in")

    def finish_x(portion):
        return refine(transform(portion, 1, "real_out"), weights_x)

    spectra = lines_x(tensor, forward_real)
    share_x = local_x // count_gy
    line_x = spectral_index(place_x * local_x + place_y * share_x + jnp.arange(share_x), length_x)[
        :, None
    ]
    line_y = spectral_index(jnp.arange(length_y), length_y)[None, :]

    def solve_y(portion):
        solved = project(transform(portion, -1, "complex"), line_x, line_y)
        return refine(transform(solved, 1, "complex"), weights_y)

    pressure = lines_y(spectra, solve_y)
    source = lines_x(pressure, finish_x)[0]
    open_cells = (1 - wall_mask).astype(jnp.float32)
    first_rate = tendency(expand(acoustic), source)
    middle = open_cells * (acoustic + time_step * first_rate)
    second_rate = tendency(expand(middle), source)
    return (open_cells * (acoustic + 0.5 * time_step * (first_rate + second_rate))).astype(
        jnp.bfloat16
    )


def solution(mesh):
    in_specs = (P(None, None, "gy", "gx"), P(), P(), P(None, None, "gy", "gx"), P(None, "gy", "gx"))
    out_specs = P(None, None, "gy", "gx")

    def chosen(velocity, weights_x, weights_y, acoustic, wall_mask):
        sizes = (mesh.shape["gx"], mesh.shape["gy"], velocity.shape, acoustic.shape)
        plan = fast_shards if fits(*sizes) else shards
        return plan(velocity, weights_x, weights_y, acoustic, wall_mask)

    return jax.shard_map(
        chosen, mesh=mesh, in_specs=in_specs, out_specs=out_specs, check_vma=False
    )
```

```python
import functools
import math

import jax
import jax.numpy as jnp
import ml_dtypes
import numpy as np
from jax import lax
from jax.experimental import pallas as pl
from jax.experimental.pallas import tpu as pltpu
from jax.sharding import PartitionSpec as P

stencil_weights = (0.75, -0.15, 1.0 / 60.0)
mean_flow = 0.3
time_step = 0.5
whole_weights = (45.0, -9.0, 1.0)

LANES = 128
RADIX = 8
HALO = 8
MARGIN = 16
TILE = 128
ROOT = math.sqrt(0.5)
STRIP = {2: (0, 6), 3: (6, 6), 1: (12, 3), 4: (15, 3), 5: (20, 4)}
STRIP_ROWS = 24
PARTS = 4
BF16 = jnp.bfloat16
F32 = jnp.float32


def halves(table):
    high = table.astype(np.float32).astype(ml_dtypes.bfloat16)
    low = (table - high.astype(np.float64)).astype(np.float32).astype(ml_dtypes.bfloat16)
    return high, low


def packed_columns(cosine, sine):
    half = LANES // 2
    parts = []
    for first in range(0, cosine.shape[1], half):
        parts += [cosine[:, first : first + half], sine[:, first : first + half]]
    return np.concatenate(parts, axis=1)


@functools.lru_cache(maxsize=None)
def x_tables(length):
    base = length // RADIX
    m = np.arange(base)[:, None]
    q = np.arange(base)[None, :]
    angle = 2.0 * np.pi * ((m * q) % base) / base
    cosine, sine = np.cos(angle), np.sin(angle)
    full = np.concatenate([packed_columns(cosine, -sine), packed_columns(sine, cosine)], axis=0)
    half = base // 2
    zero_cos, zero_sin = cosine[:, :half].copy(), -sine[:, :half]
    zero_cos[:, 0] = 0.0
    zero_sin = zero_sin.copy()
    zero_sin[:, 0] = (-1.0) ** np.arange(base)
    zero = packed_columns(zero_cos, zero_sin)
    shifted = 2.0 * np.pi * ((m * (RADIX * q[:, :half] + RADIX // 2)) % length) / length
    middle = packed_columns(np.cos(shifted), -np.sin(shifted))
    turns = 2.0 * np.pi * np.arange(1, RADIX // 2)[:, None] * np.arange(base)[None, :] / length
    return full, zero, middle, np.cos(turns), np.sin(turns)


@functools.lru_cache(maxsize=None)
def y_tables(length):
    base = length // RADIX
    index = np.arange(base)
    angle = 2.0 * np.pi * ((index[:, None] * index[None, :]) % base) / base
    both = np.concatenate([np.cos(angle), np.sin(angle)], axis=0)
    turns = 2.0 * np.pi * np.arange(RADIX)[:, None] * index[None, :] / length
    turns = np.concatenate([np.cos(turns), np.sin(turns)], axis=0).T
    high, rest = halves(turns)
    low = turns - high.astype(np.float64) - rest.astype(np.float64)
    return both, np.concatenate([high, rest, low.astype(ml_dtypes.bfloat16)], axis=1)


@functools.lru_cache(maxsize=None)
def wave_table(length, count):
    slots = LANES // 4
    base = length // RADIX
    waves = []
    for residue in (1, 2, 3):
        waves.append(RADIX * np.arange(base) + residue)
    waves.append(RADIX * np.arange(base // 2))
    waves.append(RADIX * np.arange(base // 2) + RADIX // 2)
    waves = np.concatenate(waves)
    waves = np.where(waves == 0, length // 2, waves)
    waves = np.where(waves < length // 2, waves, waves - length).reshape(count, slots)
    return np.tile(waves, (1, 4)).astype(np.float32)


@functools.lru_cache(maxsize=None)
def band_tables(rows):
    across = np.zeros((4 * LANES, 2 * LANES))
    column = np.arange(2 * LANES)
    down = np.zeros((rows, rows))
    for index, weight in enumerate(whole_weights):
        distance = index + 1
        across[column + LANES + distance, column] = weight
        across[column + LANES - distance, column] = -weight
        down += weight * (np.eye(rows, k=distance) - np.eye(rows, k=-distance))
    return across.astype(ml_dtypes.bfloat16), down.astype(ml_dtypes.bfloat16)


def beside(*tables):
    high, low = halves(np.concatenate(tables, axis=1))
    return np.concatenate([high, low], axis=0)


def split(values):
    high = values.astype(BF16)
    return high, (values - high.astype(F32)).astype(BF16)


def dot(left, right):
    return jnp.dot(left, right, preferred_element_type=F32)


def exact_dot(left, right):
    left_high, left_low = left
    right_high, right_low = right
    return dot(left_high, right_high) + (dot(left_low, right_high) + dot(left_high, right_low))


def lane_index(shape):
    return lax.broadcasted_iota(jnp.int32, shape, len(shape) - 1)


def spin(values, shift):
    return pltpu.roll(values, shift % values.shape[-1], values.ndim - 1)


def lane_tile(values, index):
    return values[:, index * LANES : (index + 1) * LANES]


def x_parts(tables, base):
    wide = 2 * base
    full = (tables[:wide], tables[wide : 2 * wide])
    at = 2 * wide
    high, low = tables[at : at + base], tables[at + base : at + 2 * base]
    return full, (high[:, :base], low[:, :base]), (high[:, base:], low[:, base:])


def pieces_kernel(place, velocity, *pieces):
    rows = pieces[0].shape[1]
    for mask, piece in enumerate(pieces):
        start = pl.multiple_of((place[0] ^ mask) * rows, 8)
        for c in range(2):
            piece[c] = velocity[c, 0, pl.ds(start, rows), :]


def rows_kernel(top, low, top_wall, low_wall, top_flow, low_flow, first, last):
    small, width = top.shape[2], top_flow.shape[3]
    first[...] = jnp.zeros(first.shape, F32)
    last[...] = jnp.zeros(last.shape, F32)
    for k, (start, rows) in STRIP.items():
        lanes = slice(0, width) if k == PARTS + 1 else slice(None)
        if k < PARTS:
            upper, lower = top[k, 0].astype(F32)[:HALO], low[k, 0].astype(F32)[small - HALO :]
        elif k == PARTS:
            upper, lower = 1.0 - top_wall[0].astype(F32), 1.0 - low_wall[0].astype(F32)
        else:
            upper, lower = top_flow[0, 0], low_flow[0, 0]
        first[start : start + rows, lanes] = upper[:rows]
        last[start : start + rows, lanes] = lower[HALO - rows :]


def strip(ref, k, upper, lanes=slice(None)):
    if k not in STRIP:
        return jnp.zeros((HALO, ref[0:1, lanes].shape[1]), F32)
    start, rows = STRIP[k]
    values = ref[start : start + rows, lanes]
    blank = jnp.zeros((HALO - rows, values.shape[1]), F32)
    return jnp.concatenate([blank, values] if upper else [values, blank], axis=0)


def columns_kernel(
    has, left, right, left_wall, right_wall, left_flow, right_flow, above, below, to_right, to_left
):
    parts = left.shape[0]
    wide, flow_wide = above.shape[1], above.shape[1] // 2
    gap = jnp.zeros((LANES - 2 * HALO, LANES), F32)

    def tall(k, inner, first, sides):
        lanes = slice(first, first + LANES)
        over, under = strip(above, k, True, lanes), strip(below, k, False, lanes)
        return jnp.concatenate([inner, under * sides[1], gap, over * sides[0]], axis=0).T

    for k in range(parts + 1):
        at = slice(k * HALO, (k + 1) * HALO)
        if k < parts:
            near, far = left[k, 0].astype(F32), right[k, 0].astype(F32)
        else:
            near, far = 1.0 - left_wall[0].astype(F32), 1.0 - right_wall[0].astype(F32)
        sides = (has[2], has[3])
        to_left[at, :] = tall(k, near, 0, sides)[:HALO]
        to_right[at, :] = tall(k, far, wide - LANES, sides)[LANES - HALO :]
    k = parts + 1
    at = slice(k * HALO, (k + 1) * HALO)
    size = left_flow.shape[2] + LANES
    blank = jnp.zeros((HALO, to_left.shape[1] - size), F32)
    to_left[at, :size] = tall(k, left_flow[0, 0], 0, (1.0, 1.0))[:HALO]
    to_right[at, :size] = tall(k, right_flow[0, 0], flow_wide - LANES, (1.0, 1.0))[LANES - HALO :]
    to_left[at, size:] = blank
    to_right[at, size:] = blank


def sides_kernel(has, place, velocity, above, below, from_left, from_right, sides, squares, mark):
    parts, tall, _ = sides.shape
    gap = jnp.zeros((LANES - 2 * HALO, tall), F32)
    for k in range(parts):
        at = slice(k * HALO, (k + 1) * HALO)
        tile = [from_right[at, :] * has[1], gap, from_left[at, :] * has[0]]
        sides[k] = jnp.concatenate(tile, axis=0).T
    at = slice(parts * HALO, (parts + 1) * HALO)
    rows, local = velocity.shape[2:]
    size = rows + LANES
    tile = [from_right[at, :size], gap[:, :size], from_left[at, :size]]
    tile = jnp.concatenate(tile, axis=0).T
    tile = tile * tile
    mark[0] = place[0]
    over, under = (strip(ref, parts, ref is above, slice(0, local)) for ref in (above, below))
    squares[:HALO, :local] = over * over
    squares[HALO : HALO + rows, :local] = velocity[0, 0] * velocity[0, 0]
    squares[HALO + rows :, :local] = under * under
    squares[:HALO, local:] = tile[size - HALO :]
    squares[HALO : HALO + rows, local:] = tile[:rows]
    squares[HALO + rows :, local:] = tile[rows : rows + HALO]


def forward_x_kernel(place, *refs):
    *pieces, tables, turns, out, total, lines = refs
    count, _, rows, local = lines.shape
    for mask, piece in enumerate(pieces):
        lines[place[0] ^ mask] = piece[...]
    base = turns.shape[1]
    per = local // base
    u = [lines[t // per, 0, :, (t % per) * base : (t % per + 1) * base] for t in range(RADIX)]
    v = [lines[t // per, 1, :, (t % per) * base : (t % per + 1) * base] for t in range(RADIX)]
    energy = sum(b * b for b in v)
    energy = jnp.sum(energy.reshape(rows // 8, 8, base), axis=0)
    total[...] = sum(energy[:, k : k + LANES] for k in range(0, base, LANES))
    fields = ([a * a - b * b for a, b in zip(u, v)], [2.0 * a * b for a, b in zip(u, v)])
    zeros, mids, reals, imags = [], [], [[], [], []], [[], [], []]
    for a in fields:
        s04, s26, s15, s37 = a[0] + a[4], a[2] + a[6], a[1] + a[5], a[3] + a[7]
        d04, d26, d15, d37 = a[0] - a[4], a[2] - a[6], a[1] - a[5], a[3] - a[7]
        zeros.append((s04 + s26) + (s15 + s37))
        mids.append((s04 + s26) - (s15 + s37))
        minus, plus = ROOT * (d15 - d37), ROOT * (d15 + d37)
        turned = (
            (d04 + minus, -d26 - plus),
            (s04 - s26, s37 - s15),
            (d04 - minus, d26 - plus),
        )
        for index, (real, imag) in enumerate(turned):
            c, s = turns[index : index + 1, :], turns[index + 3 : index + 4, :]
            reals[index].append(real * c + imag * s)
            imags[index].append(imag * c - real * s)
    stacked = jnp.concatenate(
        [
            jnp.concatenate([jnp.concatenate(reals[i], axis=0) for i in range(3)], axis=0),
            jnp.concatenate([jnp.concatenate(imags[i], axis=0) for i in range(3)], axis=0),
        ],
        axis=1,
    )
    full, zero, middle = x_parts(tables, base)
    full = exact_dot(split(stacked), full)
    zero = exact_dot(split(jnp.concatenate(zeros, axis=0)), zero)
    middle = exact_dot(split(jnp.concatenate(mids, axis=0)), middle)
    low = lane_index((rows, LANES)) % 64 < 32
    target = 0
    blocks = [full[2 * rows * i : 2 * rows * (i + 1)] for i in range(3)] + [zero, middle]
    for block in blocks:
        for first in range(0, block.shape[1], LANES):
            a = block[:rows, first : first + LANES]
            c = block[rows:, first : first + LANES]
            out[target] = jnp.where(low, a, spin(c, 32))
            out[target + 1] = jnp.where(low, spin(a, -32), c)
            target += 2


def eighths(x, turn):
    s04, s26, s15, s37 = x[0] + x[4], x[2] + x[6], x[1] + x[5], x[3] + x[7]
    d04, d26, d15, d37 = x[0] - x[4], x[2] - x[6], x[1] - x[5], x[3] - x[7]
    quarter = turn(s15 - s37)
    spun_26, spun_37 = turn(d26), turn(d37)
    one, three = d15 + spun_37, d15 - spun_37
    spun_one, spun_three = turn(one), turn(three)
    one = ROOT * (one + spun_one)
    three = ROOT * (spun_three - three)
    return [
        (s04 + s26) + (s15 + s37),
        (d04 + spun_26) + one,
        (s04 - s26) + quarter,
        (d04 - spun_26) + three,
        (s04 + s26) - (s15 + s37),
        (d04 + spun_26) - one,
        (s04 - s26) - quarter,
        (d04 - spun_26) - three,
    ]


def solve_y_kernel(count_x, _, lines, total, wave, both, turns, out, held, spread):
    count, rows, _ = lines.shape
    base = turns.shape[0]
    length = count * rows
    block = count_x * rows
    per = base // rows
    lanes = lane_index((base, LANES))
    sign = jnp.where(lanes < 64, 1.0, -1.0).astype(F32)

    def minus_i(z):
        return spin(z, 64) * sign

    def plus_i(z):
        return spin(z, 64) * -sign

    fields = [
        jnp.concatenate([lines[t * per + k] for k in range(per)], axis=0) for t in range(RADIX)
    ]
    mixed = eighths(fields, minus_i)
    terms, columns = turns.shape[1], 2 * RADIX
    picked = lax.broadcasted_iota(jnp.int32, (terms, columns * LANES), 0) % columns
    lane = lane_index(picked.shape)
    value = jnp.where((lane >= RADIX * LANES) & (lane % LANES >= 64), -1.0, 1.0)
    spread[...] = dot(turns[...], jnp.where(picked == lane // LANES, value, 0.0).astype(BF16))
    cosines = [spread[:, r * LANES : (r + 1) * LANES] for r in range(RADIX)]
    sines = [spread[:, (r + RADIX) * LANES : (r + RADIX + 1) * LANES] for r in range(RADIX)]
    mixed = [mixed[0]] + [
        mixed[r] * cosines[r] + spin(mixed[r], 64) * sines[r] for r in range(1, RADIX)
    ]
    tables = (both[: 2 * base], both[2 * base :])
    product = exact_dot(tables, split(jnp.concatenate(mixed, axis=1)))
    kx = wave[0:1, :]
    first = lanes % 64 < 32
    edge = jnp.float32(length // 2)
    alone = jnp.where(first, kx * kx, 0.0)
    slope = jnp.where(first | (kx == -edge), 0.0, jnp.broadcast_to(kx, lanes.shape))
    q = lax.broadcasted_iota(jnp.int32, lanes.shape, 0)
    low_ky = RADIX * (q - jnp.where(q < base // 2, 0, base)).astype(F32)
    terms = []
    for r in range(RADIX):
        at = slice(r * LANES, (r + 1) * LANES)
        spectrum = product[:base, at] + minus_i(product[base:, at])
        ky = low_ky + float(r)
        symbol = alone + slope * ky
        if r == 0:
            corner = jnp.where((kx == -edge) & ~first, edge * edge, 0.0)
            symbol = jnp.where(ky == -edge, jnp.where(first, alone, corner), symbol)
        terms.append(symbol * pl.reciprocal(kx * kx + ky * ky) * spectrum)
    pairs = [
        jnp.where(first, low + spin(low, -32), high + spin(high, 32))
        for low, high in zip(terms[:4], terms[4:])
    ]
    product = exact_dot(tables, split(jnp.concatenate(pairs, axis=1)))
    mixed = []
    for r in range(RADIX // 2):
        at = slice(r * LANES, (r + 1) * LANES)
        value = product[:base, at] + plus_i(product[base:, at])
        cosine = jnp.where(first, cosines[r], cosines[r + 4])
        sine = jnp.where(first, sines[r], sines[r + 4])
        value = value * cosine - spin(value, 64) * sine
        value = jnp.where(first, value + spin(value, -32), spin(value, 32) - value)
        if r == 2:
            value = jnp.where(first, value, plus_i(value))
        elif r:
            turned = plus_i(value)
            odd = value + turned if r == 1 else turned - value
            value = jnp.where(first, value, ROOT * odd)
        mixed.append(value)
    even, odd = mixed[0] + mixed[2], mixed[0] - mixed[2]
    side, turned = mixed[1] + mixed[3], plus_i(mixed[1] - mixed[3])
    for t, values in enumerate((even + side, odd + turned, even - side, odd - turned)):
        start = MARGIN + 2 * t * base
        held[start : start + base, :] = values
        held[start + base : start + 2 * base, :] = spin(values, -32)
    held[0:MARGIN, :] = held[length : length + MARGIN, :]
    held[length + MARGIN : length + 2 * MARGIN, :] = held[MARGIN : 2 * MARGIN, :]
    spare = total[...] + spin(total[...], 32)
    kept = rows + 2 * MARGIN // count_x
    half = out.shape[1]
    rest = kept - half
    low = lane_index((8, LANES)) % 64 < 32
    for target in range(count):
        start = (target // count_x) * block + (target % count_x) * kept
        for row in range(0, half, 8):
            a = held[start + row : start + row + 8, :]
            if row < rest:
                b = spin(held[start + half + row : start + half + row + 8, :], 32)
            else:
                b = spare
            out[target, row : row + 8, :] = jnp.where(low, a, b)


def inverse_x_kernel(
    kept, scale, place, lines, tables, turns, *refs
):
    *outs, held = refs
    count, half, _ = lines.shape
    base = turns.shape[1]
    length = RADIX * base
    rest = kept - half
    low = lane_index((half, LANES)) % 64 < 32
    groups, spare = [], None
    for first in range(0, count, 2):
        even, odd = lines[first], lines[first + 1]
        a = jnp.where(low, even, spin(odd, 32))
        b = jnp.where(low, spin(even, -32), odd)
        groups.append(jnp.concatenate([a, b[:rest]], axis=0))
        extra = b[rest : rest + 8]
        spare = extra if spare is None else spare + extra
    mean = jnp.sum(spare) * scale
    wide = 2 * base // LANES
    narrow = base // LANES
    stacked = jnp.concatenate(
        [jnp.concatenate(groups[i * wide : (i + 1) * wide], axis=1) for i in range(3)], axis=0
    )
    at = 3 * wide
    zeros = jnp.concatenate(groups[at : at + narrow], axis=1)
    mids = jnp.concatenate(groups[at + narrow : at + 2 * narrow], axis=1)
    full, zero, middle = x_parts(tables, base)
    full = exact_dot(split(stacked), full)
    zero = exact_dot(split(zeros), zero) * scale
    mid = exact_dot(split(mids), middle) * scale
    turned = []
    for i in range(3):
        real = full[i * kept : (i + 1) * kept, :base]
        imag = full[i * kept : (i + 1) * kept, base:]
        c = turns[i : i + 1, :] * (2.0 * scale)
        s = turns[i + 3 : i + 4, :] * (2.0 * scale)
        turned.append((real * c - imag * s, real * s + imag * c))
    for t in range(RADIX):
        value = zero + mid if t % 2 == 0 else zero - mid
        for i, (real, imag) in enumerate(turned):
            eighth = t * (i + 1) % RADIX
            c = (1.0, ROOT, 0.0, -ROOT, -1.0, -ROOT, 0.0, ROOT)[eighth]
            s = (0.0, ROOT, 1.0, ROOT, 0.0, -ROOT, -1.0, -ROOT)[eighth]
            if c:
                value = value + c * real
            if s:
                value = value - s * imag
        held[:, t * base : (t + 1) * base] = mean - value
    targets, local = len(outs), outs[0].shape[1] - LANES
    right = lane_index((kept, LANES)) < 64
    for mask, out in enumerate(outs):
        start = pl.multiple_of((place[0] ^ mask) * local, LANES)
        after = pl.multiple_of(jnp.where(start + local == length, 0, start + local), LANES)
        before = pl.multiple_of(jnp.where(start == 0, length, start) - LANES, LANES)
        out[:, :local] = held[:, pl.ds(start, local)]
        out[:, local:] = jnp.where(
            right, held[:, pl.ds(after, LANES)], held[:, pl.ds(before, LANES)]
        )


def slopes_x(parts, band, with_edge):
    tiles = parts[0].shape[-1] // LANES
    pieces = []
    for first in list(range(0, tiles - 1, 2)) + ([tiles - 1] if with_edge else []):
        steps = (-1, 0, 1, 2) if first < tiles - 1 else (-1, 0, 1)
        table = band[...] if first < tiles - 1 else band[: 3 * LANES, :LANES]
        order = [(first + step) % tiles for step in steps]
        piece = None
        for part in parts:
            term = dot(jnp.concatenate([lane_tile(part, t) for t in order], axis=1), table)
            piece = term if piece is None else piece + term
        pieces.append(piece)
    return jnp.concatenate(pieces, axis=1)


def slope_y(read):
    value = read(3) - read(-3)
    for index in (0, 1):
        value = value + whole_weights[index] * (read(index + 1) - read(-index - 1))
    return value


def edged(k, side, center, up, down, above, below, sides, has, first=0):
    step = pl.program_id(0) + first
    tile, width = center.shape
    tall = sides.shape[1]
    last = (tall - LANES) // tile - 1
    base = pl.multiple_of(step * tile, 8)
    before = pl.multiple_of(jnp.where(step == 0, tall, base) - HALO, 8)
    over = jnp.where(step == 0, strip(above, k, True) * has[2], up)
    under = jnp.where(step == last, strip(below, k, False) * has[3], down)
    rows = (
        (over, sides[side, pl.ds(before, HALO), :]),
        (center, sides[side, pl.ds(base, tile), :]),
        (under, sides[side, pl.ds(pl.multiple_of(base + tile, 8), HALO), :]),
    )
    return jnp.concatenate([jnp.concatenate(pair, axis=1) for pair in rows], axis=0)


def edged_open(k, side, wall, wall_up, wall_down, above, below, sides, has, first=0):
    open_cells = [1.0 - ref[0].astype(F32) for ref in (wall, wall_up, wall_down)]
    return edged(k, side, *open_cells, above, below, sides, has, first)


def quiet_step_kernel(
    first, has, place, center, up, down, wall, wall_up, wall_down, above, below, sides, across, along, along_inner, calm, density, shown_open, mark
):
    parts, _, tile, width = center.shape
    high = tile + 2 * HALO
    opened = edged_open(parts, parts, wall, wall_up, wall_down, above, below, sides, has, first)
    values = []
    for k in range(parts):
        value = edged(
            k,
            k,
            center[k, 0].astype(F32),
            up[k, 0].astype(F32)[up.shape[2] - HALO :],
            down[k, 0].astype(F32)[:HALO],
            above,
            below,
            sides,
            has,
            first,
        )
        values.append(value)

    def drops(x, along_b, along_p):
        diverge = x[1] + along_b
        return (
            diverge + mean_flow * x[0],
            x[3] + mean_flow * x[1],
            along_p + mean_flow * x[2],
            diverge + mean_flow * x[3],
        )

    short = [value.astype(BF16) for value in values]
    x = slopes_x((jnp.concatenate(short, axis=0),), across, True)
    x = [x[k * high : (k + 1) * high] for k in range(parts)]
    table = along[...]
    dropped = drops(x, dot(table, short[2]), dot(table, short[3]))
    middle = [opened * (v - (time_step / 60.0) * d) for v, d in zip(values, dropped)]
    inner = slice(HALO, HALO + tile)
    x = slopes_x(split(jnp.concatenate([value[inner] for value in middle], axis=0)), across, False)
    x = [x[k * tile : (k + 1) * tile] for k in range(parts)]
    table = along_inner[...]
    y = [sum(dot(table, part) for part in split(middle[k][:, :width])) for k in (2, 3)]
    dropped = drops(x, *y)
    shown = opened[inner, :width]
    for k in range(parts):
        start = 0.5 * values[k][inner, :width] - (0.5 * time_step / 60.0) * dropped[k]
        value = shown * start + 0.5 * middle[k][inner, :width]
        if k == 0:
            density[0, 0] = value.astype(BF16)
        else:
            calm[k - 1] = value
    shown_open[0] = opened.astype(BF16)
    mark[0] = place[0]


def tables_kernel(place, weights_x, weights_y, rise_x, rise_y):
    tiles, reach_x, lanes = rise_x.shape
    wide, length_x = (tiles - 1) * lanes, weights_x.shape[1]
    first = place[0] * wide
    half = LANES // 2

    def weights(ref, start, size):
        length = ref.shape[1]
        start = jnp.where(start < 0, start + length, jnp.where(start >= length, start - length, start))
        return ref[:, pl.ds(pl.multiple_of(start, LANES), size)]

    cells = lax.broadcasted_iota(jnp.int32, (reach_x, lanes), 0)
    fine = lax.broadcasted_iota(jnp.int32, (reach_x, lanes), 1)
    right, left = weights(weights_x, first + wide, LANES), weights(weights_x, first - LANES, LANES)
    edge = jnp.where(lane_index(right.shape) < half, right, left)
    edge = jnp.concatenate([edge, edge], axis=1)
    for k in range(tiles):
        own = weights(weights_x, first + k * lanes, lanes) if k < tiles - 1 else edge
        target = fine // 2 - 1
        if k == tiles - 1:
            target = jnp.where(fine < half, target, target + half)
        value = jnp.zeros(fine.shape, F32)
        for t in range(4):
            value = jnp.where(cells == (target + t) % reach_x, own[t : t + 1, :], value)
        rise_x[k] = value
    steps, high, reach = rise_y.shape
    tall = steps * TILE
    first = place[1] * tall
    own = [weights(weights_y, first + k * LANES, LANES) for k in range(-1, tall // LANES + 1)]
    own = jnp.concatenate([jnp.concatenate(own, axis=1), jnp.zeros((4, tall + 2 * LANES), F32)], axis=0).T
    cells = lax.broadcasted_iota(jnp.int32, (high, reach), 1) % (reach // 3)
    target = lax.broadcasted_iota(jnp.int32, (high, reach), 0) // 2 + (HALO // 2 - 1)
    for k in range(steps):
        start = LANES - HALO + k * TILE
        value = jnp.zeros((high, reach), F32)
        for t in range(4):
            value = jnp.where(cells == target + t, own[start : start + high, t : t + 1], value)
        rise_y[k] = value


def source_kernel(place, squares, opened, rise_x, rise_y, quiet, across, _, *refs):
    *lines, out, squared, cells_open, matrix, rows_matrix, calm, band, held, raised, forced, done, fetched, kept = refs
    steps = done.shape[0]
    tile, width = calm.shape[2:]
    high = tile + 2 * HALO
    rows = lines[0].shape[0]

    def calm_copy(k):
        part = quiet.at[:, pl.ds(k * tile, tile), :]
        return pltpu.make_async_copy(part, calm.at[k % 2], fetched.at[k % 2])

    def done_copy(k):
        part = out.at[1:, 0, pl.ds(k * tile, tile), :]
        return pltpu.make_async_copy(done.at[k], part, kept.at[k])

    arrays = [(squares, squared), (rise_x, matrix), (rise_y, rows_matrix), (opened, cells_open), (across, band)]
    copies = [
        pltpu.make_async_copy(source, target, fetched.at[2 + k])
        for k, (source, target) in enumerate(arrays)
    ]
    pieces = [
        pltpu.make_async_copy(
            piece,
            held.at[pl.ds(pl.multiple_of((place[0] ^ mask) * rows, 8), rows), :],
            fetched.at[2 + len(arrays) + mask],
        )
        for mask, piece in enumerate(lines)
    ]
    for copy in pieces + copies:
        copy.start()
    calm_copy(0).start()
    calm_copy(1).start()
    for copy in pieces + copies[:1]:
        copy.wait()

    level = held[MARGIN - HALO : MARGIN - HALO + squared.shape[0], :] - squared[...]
    count = level.shape[1] // LANES
    near = lane_index((level.shape[0], LANES)) < 64
    around = []
    for k in range(count):
        after, before = lane_tile(level, (k + 1) % count), lane_tile(level, (k - 1) % count)
        around.append(split(jnp.concatenate([lane_tile(level, k), jnp.where(near, after, before)], axis=1)))
    copies[1].wait()
    for k in range(count):
        lanes = 2 * LANES if k < count - 1 else LANES
        value = split(exact_dot(around[k], split(matrix[k][:, :lanes])))
        for part in range(2):
            raised[part, :, 2 * k * LANES : 2 * k * LANES + lanes] = value[part]
    for copy in copies[2:]:
        copy.wait()

    reach = rows_matrix.shape[2] // 3
    third = lane_index((high, 3 * reach)) >= 2 * reach
    for k in range(steps):
        start = k * (tile // 2)
        window = [raised[part, start : start + reach, :] for part in (0, 1, 0)]
        weights = split(rows_matrix[k])
        weights = jnp.where(third, weights[1], weights[0])
        free = time_step * cells_open[k].astype(F32)
        value = free * dot(weights, jnp.concatenate(window, axis=0))
        forced[k % 2] = value
        inner = value[HALO : HALO + tile]
        shown = (0.5 / 60.0) * free[HALO : HALO + tile, :width]
        x = shown * slopes_x(split(inner), band, False)
        y = shown * slope_y(lambda d: forced[k % 2, HALO + d : HALO + d + tile, :width])
        calm_copy(k).wait()
        still = calm.at[k % 2]
        done[k, 0] = (still[0] - x).astype(BF16)
        done[k, 1] = (still[1] - y).astype(BF16)
        done[k, 2] = (still[2] + inner[:, :width] - mean_flow * x).astype(BF16)
        done_copy(k).start()
        if k + 2 < steps:
            calm_copy(k + 2).start()
    for k in range(steps):
        done_copy(k).wait()


def call(
    kernel, operands, outs, scratch=(), steps=0, specs=None, out_specs=None, after=(), aliases=None, megabytes=24, flops=0, moved=0, name=None
):
    count = len(operands)

    def body(*refs):
        kernel(*refs[:count], *refs[count + len(after) :])

    def whole(array):
        zeros = (0,) * len(array.shape)
        return pl.BlockSpec(array.shape, lambda *_: zeros)

    arguments = {}
    chosen = specs or {}
    if steps:
        arguments["grid"] = (steps,)
        in_specs = [chosen.get(i, whole(o)) for i, o in enumerate(operands)]
        arguments["out_specs"] = jax.tree.map(whole, outs) if out_specs is None else out_specs
    else:
        local = pl.BlockSpec(memory_space=pltpu.VMEM)
        in_specs = [chosen.get(i, local) for i in range(count)]
        if out_specs is not None:
            arguments["out_specs"] = out_specs
    return pl.pallas_call(
        body,
        out_shape=outs,
        in_specs=in_specs + [pl.BlockSpec(memory_space=pl.ANY)] * len(after),
        scratch_shapes=list(scratch),
        input_output_aliases=aliases or {},
        compiler_params=pltpu.CompilerParams(vmem_limit_bytes=megabytes << 20),
        cost_estimate=pl.CostEstimate(flops=flops, bytes_accessed=moved, transcendentals=0),
        name=name,
        **arguments,
    )(*operands, *after)


def ring(array, axis, step):
    size = lax.axis_size(axis)
    return lax.ppermute(array, axis, [(i, (i + step) % size) for i in range(size)])


def swap(array, axis, mask):
    return lax.ppermute(array, axis, [(i, i ^ mask) for i in range(lax.axis_size(axis))])


def shaped(*shape, kind=F32):
    return jax.ShapeDtypeStruct(shape, kind)


def pressure_lines(pieces, place_x, gathered, spread, stepped):
    _, rows, local_x = pieces[0].shape
    count_x, count_y = lax.axis_size("gx"), lax.axis_size("gy")
    count = count_x * count_y
    scalars = {0: pl.BlockSpec(memory_space=pltpu.SMEM)}
    length_x, length_y = local_x * count_x, rows * count
    full, zero, middle, cos_turn, sin_turn = x_tables(length_x)
    turns = np.zeros((8, cos_turn.shape[1]), np.float32)
    turns[0:3], turns[3:6] = cos_turn, sin_turn
    spectra, total = call(
        forward_x_kernel,
        (place_x, *pieces, np.concatenate([beside(full), beside(zero, middle)]), turns),
        (shaped(count, rows, LANES), shaped(8, LANES)),
        (pltpu.VMEM((count_x, 2, rows, local_x), F32),),
        specs=scalars,
        after=gathered,
        flops=10**9,
        moved=4 << 20,
        name="forward_x",
    )
    spectra = lax.all_to_all(spectra, ("gy", "gx"), 0, 0, tiled=True)
    place = lax.axis_index("gy") * count_x + lax.axis_index("gx")
    waves = jnp.asarray(wave_table(length_x, count))
    wave = lax.dynamic_slice(waves, (place, 0), (1, LANES))
    both, turns_y = y_tables(length_y)
    kept = rows + 2 * MARGIN // count_x
    half = (kept // 2 + 8) // 8 * 8
    solved = call(
        functools.partial(solve_y_kernel, count_x),
        (spread, spectra, total, wave, beside(both), turns_y),
        shaped(count, half, LANES),
        (
            pltpu.VMEM((length_y + 2 * MARGIN, LANES), F32),
            pltpu.VMEM((length_y // RADIX, 2 * RADIX * LANES), F32),
        ),
        specs=scalars,
        flops=4 * 10**9,
        moved=6 << 20,
        name="solve_y",
    )
    solved = lax.all_to_all(solved, ("gy", "gx"), 0, 0, tiled=True)
    back = 2.0 * zero.T
    back[LANES // 2] *= 0.5
    tables = np.concatenate(
        [beside(full.T), beside(back, 2.0 * middle.T)]
    )
    pressed = call(
        functools.partial(inverse_x_kernel, kept, 1.0 / (length_x * length_y)),
        (stepped, solved, tables, turns),
        (shaped(kept, local_x + LANES),) * count_x,
        (pltpu.VMEM((kept, length_x), F32),),
        specs=scalars,
        flops=10**9,
        moved=4 << 20,
        name="inverse_x",
    )
    return [piece if mask == 0 else swap(piece, "gx", mask) for mask, piece in enumerate(pressed)]


def fast_shards(velocity, weights_x, weights_y, acoustic, wall_mask):
    parts, _, tall, wide = acoustic.shape
    _, _, local_y, local_x = velocity.shape
    count_x, count_y = lax.axis_size("gx"), lax.axis_size("gy")
    place_x, place_y = lax.axis_index("gx"), lax.axis_index("gy")
    full, high, steps = wide + LANES, TILE + 2 * HALO, tall // TILE
    strips = (parts + 2) * HALO
    small = 2 * HALO
    has = jnp.stack([place_x > 0, place_x < count_x - 1, place_y > 0, place_y < count_y - 1])
    has = has.astype(F32)
    scalars = pl.BlockSpec(memory_space=pltpu.SMEM)

    def at(block, *index):
        return pl.BlockSpec(block, lambda i: index)

    own = place_x.astype(jnp.int32).reshape(1)
    sent = call(
        pieces_kernel,
        (own, velocity),
        (shaped(2, local_y // count_x, local_x),) * count_x,
        specs={0: scalars},
        moved=2 << 20,
        megabytes=8,
        name="pieces",
    )
    moved = [piece if mask == 0 else swap(piece, "gx", mask) for mask, piece in enumerate(sent)]
    first, last = call(
        rows_kernel,
        (acoustic, acoustic, wall_mask, wall_mask, velocity, velocity),
        (shaped(STRIP_ROWS, wide),) * 2,
        steps=1,
        specs={
            0: at((parts, 1, small, wide), 0, 0, 0, 0),
            1: at((parts, 1, small, wide), 0, 0, tall // small - 1, 0),
            2: at((1, HALO, wide), 0, 0, 0),
            3: at((1, HALO, wide), 0, tall // HALO - 1, 0),
            4: at((1, 1, HALO, local_x), 1, 0, 0, 0),
            5: at((1, 1, HALO, local_x), 1, 0, local_y // HALO - 1, 0),
        },
        after=moved[1:2],
        moved=2 << 20,
        megabytes=54,
        name="rows",
    )
    above, below = ring(last, "gy", 1), ring(first, "gy", -1)
    to_right, to_left = call(
        columns_kernel,
        (has, acoustic, acoustic, wall_mask, wall_mask, velocity, velocity, above, below),
        (shaped(strips, tall + LANES), shaped(strips, tall + LANES)),
        steps=1,
        specs={
            0: scalars,
            1: at((parts, 1, tall, LANES), 0, 0, 0, 0),
            2: at((parts, 1, tall, LANES), 0, 0, 0, wide // LANES - 1),
            3: at((1, tall, LANES), 0, 0, 0),
            4: at((1, tall, LANES), 0, 0, wide // LANES - 1),
            5: at((1, 1, local_y, LANES), 1, 0, 0, 0),
            6: at((1, 1, local_y, LANES), 1, 0, 0, local_x // LANES - 1),
        },
        moved=8 << 20,
        megabytes=54,
        name="columns",
    )
    from_left, from_right = ring(to_right, "gx", 1), ring(to_left, "gx", -1)
    sides, squares, beside = call(
        sides_kernel,
        (has, own, velocity, above, below, from_left, from_right),
        (
            shaped(parts + 1, tall + LANES, LANES),
            shaped(local_y + 2 * HALO, local_x + LANES),
            shaped(1, kind=jnp.int32),
        ),
        steps=1,
        specs={0: scalars, 1: scalars, 2: at((1, 1, local_y, local_x), 1, 0, 0, 0)},
        out_specs=(
            at((parts + 1, tall + LANES, LANES), 0, 0, 0),
            at((local_y + 2 * HALO, local_x + LANES), 0, 0),
            scalars,
        ),
        moved=8 << 20,
        megabytes=54,
        name="sides",
    )
    across, along = band_tables(high)
    along_inner = along[HALO : HALO + TILE]
    per, rows = TILE // small, TILE // HALO

    def tiled(first):
        walls = (
            pl.BlockSpec((1, TILE, wide), lambda i: (0, i + first, 0)),
            pl.BlockSpec((1, HALO, wide), lambda i: (0, jnp.maximum((i + first) * rows - 1, 0), 0)),
            pl.BlockSpec(
                (1, HALO, wide),
                lambda i: (0, jnp.minimum((i + first + 1) * rows, steps * rows - 1), 0),
            ),
        )
        cells = (
            pl.BlockSpec((parts, 1, TILE, wide), lambda i: (0, 0, i + first, 0)),
            pl.BlockSpec(
                (parts, 1, small, wide), lambda i: (0, 0, jnp.maximum((i + first) * per - 1, 0), 0)
            ),
            pl.BlockSpec(
                (parts, 1, small, wide),
                lambda i: (0, 0, jnp.minimum((i + first + 1) * per, steps * per - 1), 0),
            ),
        )
        return cells, walls

    def quiet_tiles(first, count, before):
        cells, walls = tiled(first)
        operands = (has, own, acoustic, acoustic, acoustic, wall_mask, wall_mask, wall_mask, above, below, sides)
        operands = operands + (across, along, along_inner)
        return call(
            functools.partial(quiet_step_kernel, first),
            operands,
            (
                shaped(parts - 1, tall, wide),
                shaped(*acoustic.shape, kind=BF16),
                shaped(steps, high, full, kind=BF16),
                shaped(1, kind=jnp.int32),
            ),
            steps=count,
            specs=dict(enumerate((scalars, scalars) + cells + walls)),
            out_specs=(
                pl.BlockSpec((parts - 1, TILE, wide), lambda i: (0, i + first, 0)),
                pl.BlockSpec((1, 1, TILE, wide), lambda i: (0, 0, i + first, 0)),
                pl.BlockSpec((1, high, full), lambda i: (i + first, 0, 0)),
                scalars,
            ),
            after=before,
            aliases={len(operands) + k: k for k in range(len(before))},
            megabytes=54,
            flops=3 * 10**9 * count,
            moved=(12 << 20) * count,
            name="quiet_step",
        )

    early = max(steps * 3 // 4, 1)
    *begun, stepped = quiet_tiles(0, early, ())
    if early < steps:
        *begun, _ = quiet_tiles(early, steps - early, begun)
    quiet, final, opened = begun
    lines = pressure_lines(moved, own, (above, below), beside, stepped)
    tiles = wide // (2 * LANES) + 1
    rise_x, rise_y = call(
        tables_kernel,
        (jnp.stack([place_x, place_y]).astype(jnp.int32), weights_x, weights_y),
        (shaped(tiles, 2 * LANES, 2 * LANES), shaped(steps, high, 3 * (high // 2 + HALO))),
        specs={0: scalars},
        moved=4 << 20,
        megabytes=54,
        name="tables",
    )
    operands = (own, squares, opened, rise_x, rise_y, quiet, across, final, *lines)
    anywhere = pl.BlockSpec(memory_space=pl.ANY)
    specs = {k: anywhere for k in range(1, len(operands))}
    scratch = (
        pltpu.VMEM(squares.shape, F32),
        pltpu.VMEM(opened.shape, BF16),
        pltpu.VMEM(rise_x.shape, F32),
        pltpu.VMEM(rise_y.shape, F32),
        pltpu.VMEM((2, parts - 1, TILE, wide), F32),
        pltpu.VMEM(across.shape, BF16),
        pltpu.VMEM((local_y + 2 * MARGIN, local_x + LANES), F32),
        pltpu.VMEM((2, local_y + 2 * HALO, full), BF16),
        pltpu.VMEM((2, high, full), F32),
        pltpu.VMEM((steps, parts - 1, TILE, wide), BF16),
        pltpu.SemaphoreType.DMA((7 + count_x,)),
        pltpu.SemaphoreType.DMA((steps,)),
    )
    return call(
        source_kernel,
        operands,
        shaped(*acoustic.shape, kind=BF16),
        scratch,
        specs={0: scalars, **specs},
        out_specs=anywhere,
        aliases={7: 0},
        megabytes=56,
        flops=4 * 10**9,
        moved=16 << 20,
        name="source_step",
    )


def fits(count_x, count_y, velocity, acoustic):
    _, planes, local_y, local_x = velocity
    _, _, tall, wide = acoustic
    length_x, length_y = local_x * count_x, local_y * count_y
    rows = local_y // count_x
    base_x, base_y = length_x // RADIX, length_y // RADIX
    return (
        planes == 1
        and acoustic[0] == PARTS
        and length_x * 2 == count_x * count_y * LANES
        and base_x % (2 * LANES) == 0
        and local_x % base_x == 0
        and rows % 8 == 0
        and base_y % rows == 0
        and base_y % 8 == 0
        and MARGIN * 2 % (8 * count_x) == 0
        and tall == 2 * local_y
        and wide == 2 * local_x
        and tall % TILE == 0
        and tall % LANES == 0
        and tall >= 2 * TILE
        and count_x & (count_x - 1) == 0
        and wide % (2 * LANES) == 0
    )


def extended(array, sides, width):
    for axis, dim in sides:
        size, length = (lax.axis_size(axis), array.shape[dim])
        up = [(i, (i + 1) % size) for i in range(size - 1)]
        down = [(j, i) for i, j in up]
        last = lax.slice_in_dim(array, length - width, length, axis=dim)
        leading = lax.slice_in_dim(array, 0, width, axis=dim)
        before = lax.ppermute(last, axis, up)
        after = lax.ppermute(leading, axis, down)
        array = jnp.concatenate([before, array, after], axis=dim)
    return array


def gradients(padded):
    height = padded.shape[-2] - 6
    breadth = padded.shape[-1] - 6
    rows_mid = padded[..., 3 : 3 + height, :]
    cols_mid = padded[..., :, 3 : 3 + breadth]
    along_x = jnp.zeros_like(padded[..., 3 : 3 + height, 3 : 3 + breadth])
    along_y = jnp.zeros_like(along_x)
    for index, weight in enumerate(stencil_weights):
        distance = index + 1
        along_x = along_x + weight * (
            rows_mid[..., 3 + distance : 3 + distance + breadth]
            - rows_mid[..., 3 - distance : 3 - distance + breadth]
        )
        along_y = along_y + weight * (
            cols_mid[..., 3 + distance : 3 + distance + height, :]
            - cols_mid[..., 3 - distance : 3 - distance + height, :]
        )
    return (along_x, along_y)


def tendency(padded, source):
    along_x, along_y = gradients(padded)
    diverge = along_x[1] + along_y[2]
    forcing = jnp.stack([-diverge, -along_x[3], -along_y[3], source - diverge])
    return forcing - mean_flow * along_x


def spectral_index(flat, length):
    second = length // 16
    wave = flat // second + 16 * (flat % second)
    return jnp.where(wave < length // 2, wave, wave - length).astype(jnp.float32)


def twiddles(rows_count, cols_count, modulus, sign):
    products = jnp.arange(rows_count)[:, None] * jnp.arange(cols_count)[None, :] % modulus
    angles = 2.0 * math.pi / modulus * products.astype(jnp.float32)
    return (jnp.cos(angles), sign * jnp.sin(angles))


def mix_rows(real_part, imag_part, cosine, sine):
    exact = lax.Precision.HIGHEST
    cos_real = jnp.einsum("ka,...ab->...kb", cosine, real_part, precision=exact)
    cos_imag = jnp.einsum("ka,...ab->...kb", cosine, imag_part, precision=exact)
    sin_real = jnp.einsum("ka,...ab->...kb", sine, real_part, precision=exact)
    sin_imag = jnp.einsum("ka,...ab->...kb", sine, imag_part, precision=exact)
    return (cos_real - sin_imag, cos_imag + sin_real)


def mix_cols(real_part, imag_part, cosine, sine):
    exact = lax.Precision.HIGHEST
    cos_real = jnp.einsum("...kb,bc->...kc", real_part, cosine, precision=exact)
    cos_imag = jnp.einsum("...kb,bc->...kc", imag_part, cosine, precision=exact)
    sin_real = jnp.einsum("...kb,bc->...kc", real_part, sine, precision=exact)
    sin_imag = jnp.einsum("...kb,bc->...kc", imag_part, sine, precision=exact)
    return (cos_real - sin_imag, cos_imag + sin_real)


def rotate(real_part, imag_part, cosine, sine):
    return (real_part * cosine - imag_part * sine, real_part * sine + imag_part * cosine)


def discrete(real_part, imag_part, sign):
    length = real_part.shape[-1]
    second = length // 16
    initial = real_part.shape
    folded = initial[:-1] + (16, second)
    real_part = real_part.reshape(folded)
    imag_part = imag_part.reshape(folded)
    small_cos, small_sin = twiddles(16, 16, 16, sign)
    large_cos, large_sin = twiddles(second, second, second, sign)
    turn_cos, turn_sin = twiddles(16, second, length, sign)
    if sign < 0:
        real_part, imag_part = mix_rows(real_part, imag_part, small_cos, small_sin)
        real_part, imag_part = rotate(real_part, imag_part, turn_cos, turn_sin)
        real_part, imag_part = mix_cols(real_part, imag_part, large_cos, large_sin)
    else:
        real_part, imag_part = mix_cols(real_part, imag_part, large_cos, large_sin)
        real_part, imag_part = rotate(real_part, imag_part, turn_cos, turn_sin)
        real_part, imag_part = mix_rows(real_part, imag_part, small_cos, small_sin)
        real_part = real_part / length
        imag_part = imag_part / length
    return (real_part.reshape(initial), imag_part.reshape(initial))


def transform(stacked, sign, kind):
    if kind == "real_in":
        real_part = stacked
        imag_part = jnp.zeros_like(stacked)
    else:
        half = stacked.shape[0] // 2
        real_part = stacked[:half]
        imag_part = stacked[half:]
    real_out, imag_out = discrete(real_part, imag_part, sign)
    if kind == "real_out":
        return real_out
    return jnp.concatenate([real_out, imag_out], axis=0)


def project(stacked, wave_x, wave_y):
    coef_xx = wave_x * wave_x
    coef_xy = 2.0 * wave_x * wave_y
    coef_yy = wave_y * wave_y
    denominator = wave_x * wave_x + wave_y * wave_y
    positive = denominator > 0
    safe = jnp.where(positive, denominator, 1.0)

    def combine(parts):
        numerator = -(coef_xx * parts[0] + coef_xy * parts[1] + coef_yy * parts[2])
        return jnp.where(positive, numerator / safe, 0.0)

    return jnp.stack([combine(stacked[:3]), combine(stacked[3:])])


def refine(stacked, weights):
    result = jnp.zeros(stacked.shape[:-1] + (2 * stacked.shape[-1],), jnp.float32)
    for offset in range(4):
        result = (
            result
            + jnp.repeat(jnp.roll(stacked, 1 - offset, axis=-1), 2, axis=-1) * weights[offset]
        )
    return result


def lines_x(stacked, action):
    gathered = action(lax.all_to_all(stacked, "gx", split_axis=2, concat_axis=3, tiled=True))
    return lax.all_to_all(gathered, "gx", split_axis=3, concat_axis=2, tiled=True)


def lines_y(stacked, action):
    turned = jnp.swapaxes(stacked, 2, 3)
    gathered = action(lax.all_to_all(turned, "gy", split_axis=2, concat_axis=3, tiled=True))
    returned = lax.all_to_all(gathered, "gy", split_axis=3, concat_axis=2, tiled=True)
    return jnp.swapaxes(returned, 2, 3)


def expand(fields):
    return extended(fields, (("gx", 3), ("gy", 2)), 3)


def shards(velocity, weights_x, weights_y, acoustic, wall_mask):
    acoustic = acoustic.astype(jnp.float32)
    flow_x = velocity[0]
    flow_y = velocity[1]
    tensor = jnp.stack([flow_x * flow_x, flow_x * flow_y, flow_y * flow_y])
    count_gx = lax.axis_size("gx")
    count_gy = lax.axis_size("gy")
    place_x = lax.axis_index("gx")
    place_y = lax.axis_index("gy")
    local_y = tensor.shape[2]
    local_x = tensor.shape[3]
    length_x = local_x * count_gx
    length_y = local_y * count_gy

    def forward_real(portion):
        return transform(portion, -1, "real_in")

    def finish_x(portion):
        return refine(transform(portion, 1, "real_out"), weights_x)

    spectra = lines_x(tensor, forward_real)
    share_x = local_x // count_gy
    line_x = spectral_index(place_x * local_x + place_y * share_x + jnp.arange(share_x), length_x)[
        :, None
    ]
    line_y = spectral_index(jnp.arange(length_y), length_y)[None, :]

    def solve_y(portion):
        solved = project(transform(portion, -1, "complex"), line_x, line_y)
        return refine(transform(solved, 1, "complex"), weights_y)

    pressure = lines_y(spectra, solve_y)
    source = lines_x(pressure, finish_x)[0]
    open_cells = (1 - wall_mask).astype(jnp.float32)
    first_rate = tendency(expand(acoustic), source)
    middle = open_cells * (acoustic + time_step * first_rate)
    second_rate = tendency(expand(middle), source)
    return (open_cells * (acoustic + 0.5 * time_step * (first_rate + second_rate))).astype(
        jnp.bfloat16
    )


def solution(mesh):
    in_specs = (P(None, None, "gy", "gx"), P(), P(), P(None, None, "gy", "gx"), P(None, "gy", "gx"))
    out_specs = P(None, None, "gy", "gx")

    def chosen(velocity, weights_x, weights_y, acoustic, wall_mask):
        sizes = (mesh.shape["gx"], mesh.shape["gy"], velocity.shape, acoustic.shape)
        plan = fast_shards if fits(*sizes) else shards
        return plan(velocity, weights_x, weights_y, acoustic, wall_mask)

    return jax.shard_map(
        chosen, mesh=mesh, in_specs=in_specs, out_specs=out_specs, check_vma=False
    )
```

```python
import functools
import math

import jax
import jax.numpy as jnp
import ml_dtypes
import numpy as np
from jax import lax
from jax.experimental import pallas as pl
from jax.experimental.pallas import tpu as pltpu
from jax.sharding import PartitionSpec as P

stencil_weights = (0.75, -0.15, 1.0 / 60.0)
mean_flow = 0.3
time_step = 0.5
whole_weights = (45.0, -9.0, 1.0)

LANES = 128
RADIX = 8
HALO = 8
MARGIN = 16
TILE = 128
ROOT = math.sqrt(0.5)
STRIP = {2: (0, 6), 3: (6, 6), 1: (12, 3), 4: (15, 3), 5: (20, 4)}
STRIP_ROWS = 24
PARTS = 4
BF16 = jnp.bfloat16
F32 = jnp.float32


def halves(table):
    high = table.astype(np.float32).astype(ml_dtypes.bfloat16)
    low = (table - high.astype(np.float64)).astype(np.float32).astype(ml_dtypes.bfloat16)
    return high, low


def packed_columns(cosine, sine):
    half = LANES // 2
    parts = []
    for first in range(0, cosine.shape[1], half):
        parts += [cosine[:, first : first + half], sine[:, first : first + half]]
    return np.concatenate(parts, axis=1)


@functools.lru_cache(maxsize=None)
def x_tables(length):
    base = length // RADIX
    m = np.arange(base)[:, None]
    q = np.arange(base)[None, :]
    angle = 2.0 * np.pi * ((m * q) % base) / base
    cosine, sine = np.cos(angle), np.sin(angle)
    full = np.concatenate([packed_columns(cosine, -sine), packed_columns(sine, cosine)], axis=0)
    half = base // 2
    zero_cos, zero_sin = cosine[:, :half].copy(), -sine[:, :half]
    zero_cos[:, 0] = 0.0
    zero_sin = zero_sin.copy()
    zero_sin[:, 0] = (-1.0) ** np.arange(base)
    zero = packed_columns(zero_cos, zero_sin)
    shifted = 2.0 * np.pi * ((m * (RADIX * q[:, :half] + RADIX // 2)) % length) / length
    middle = packed_columns(np.cos(shifted), -np.sin(shifted))
    turns = 2.0 * np.pi * np.arange(1, RADIX // 2)[:, None] * np.arange(base)[None, :] / length
    return full, zero, middle, np.cos(turns), np.sin(turns)


@functools.lru_cache(maxsize=None)
def y_tables(length):
    base = length // RADIX
    index = np.arange(base)
    angle = 2.0 * np.pi * ((index[:, None] * index[None, :]) % base) / base
    both = np.concatenate([np.cos(angle), np.sin(angle)], axis=0)
    turns = 2.0 * np.pi * np.arange(RADIX)[:, None] * index[None, :] / length
    turns = np.concatenate([np.cos(turns), np.sin(turns)], axis=0).T
    high, rest = halves(turns)
    low = turns - high.astype(np.float64) - rest.astype(np.float64)
    return both, np.concatenate([high, rest, low.astype(ml_dtypes.bfloat16)], axis=1)


@functools.lru_cache(maxsize=None)
def wave_table(length, count):
    slots = LANES // 4
    base = length // RADIX
    waves = []
    for residue in (1, 2, 3):
        waves.append(RADIX * np.arange(base) + residue)
    waves.append(RADIX * np.arange(base // 2))
    waves.append(RADIX * np.arange(base // 2) + RADIX // 2)
    waves = np.concatenate(waves)
    waves = np.where(waves == 0, length // 2, waves)
    waves = np.where(waves < length // 2, waves, waves - length).reshape(count, slots)
    return np.tile(waves, (1, 4)).astype(np.float32)


@functools.lru_cache(maxsize=None)
def band_tables(rows):
    across = np.zeros((4 * LANES, 2 * LANES))
    column = np.arange(2 * LANES)
    down = np.zeros((rows, rows))
    for index, weight in enumerate(whole_weights):
        distance = index + 1
        across[column + LANES + distance, column] = weight
        across[column + LANES - distance, column] = -weight
        down += weight * (np.eye(rows, k=distance) - np.eye(rows, k=-distance))
    return across.astype(ml_dtypes.bfloat16), down.astype(ml_dtypes.bfloat16)


def beside(*tables):
    high, low = halves(np.concatenate(tables, axis=1))
    return np.concatenate([high, low], axis=0)


def split(values):
    high = values.astype(BF16)
    return high, (values - high.astype(F32)).astype(BF16)


def dot(left, right):
    return jnp.dot(left, right, preferred_element_type=F32)


def exact_dot(left, right):
    left_high, left_low = left
    right_high, right_low = right
    return dot(left_high, right_high) + (dot(left_low, right_high) + dot(left_high, right_low))


def lane_index(shape):
    return lax.broadcasted_iota(jnp.int32, shape, len(shape) - 1)


def spin(values, shift):
    return pltpu.roll(values, shift % values.shape[-1], values.ndim - 1)


def lane_tile(values, index):
    return values[:, index * LANES : (index + 1) * LANES]


def x_parts(tables, base):
    wide = 2 * base
    full = (tables[:wide], tables[wide : 2 * wide])
    at = 2 * wide
    high, low = tables[at : at + base], tables[at + base : at + 2 * base]
    return full, (high[:, :base], low[:, :base]), (high[:, base:], low[:, base:])


def pieces_kernel(place, velocity, *pieces):
    rows = pieces[0].shape[1]
    for mask, piece in enumerate(pieces):
        start = pl.multiple_of((place[0] ^ mask) * rows, 8)
        for c in range(2):
            piece[c] = velocity[c, 0, pl.ds(start, rows), :]


def rows_kernel(place, top, low, top_wall, low_wall, top_flow, low_flow, first, last, mark):
    small, width = top.shape[2], top_flow.shape[3]
    mark[0] = place[0]
    first[...] = jnp.zeros(first.shape, F32)
    last[...] = jnp.zeros(last.shape, F32)
    for k, (start, rows) in STRIP.items():
        lanes = slice(0, width) if k == PARTS + 1 else slice(None)
        if k < PARTS:
            upper, lower = top[k, 0].astype(F32)[:HALO], low[k, 0].astype(F32)[small - HALO :]
        elif k == PARTS:
            upper, lower = 1.0 - top_wall[0].astype(F32), 1.0 - low_wall[0].astype(F32)
        else:
            upper, lower = top_flow[0, 0], low_flow[0, 0]
        first[start : start + rows, lanes] = upper[:rows]
        last[start : start + rows, lanes] = lower[HALO - rows :]


def strip(ref, k, upper, lanes=slice(None)):
    if k not in STRIP:
        return jnp.zeros((HALO, ref[0:1, lanes].shape[1]), F32)
    start, rows = STRIP[k]
    values = ref[start : start + rows, lanes]
    blank = jnp.zeros((HALO - rows, values.shape[1]), F32)
    return jnp.concatenate([blank, values] if upper else [values, blank], axis=0)


def columns_kernel(
    has, left, right, left_wall, right_wall, left_flow, right_flow, above, below, to_right, to_left
):
    parts = left.shape[0]
    wide, flow_wide = above.shape[1], above.shape[1] // 2
    gap = jnp.zeros((LANES - 2 * HALO, LANES), F32)

    def tall(k, inner, first, sides):
        lanes = slice(first, first + LANES)
        over, under = strip(above, k, True, lanes), strip(below, k, False, lanes)
        return jnp.concatenate([inner, under * sides[1], gap, over * sides[0]], axis=0).T

    for k in range(parts + 1):
        at = slice(k * HALO, (k + 1) * HALO)
        if k < parts:
            near, far = left[k, 0].astype(F32), right[k, 0].astype(F32)
        else:
            near, far = 1.0 - left_wall[0].astype(F32), 1.0 - right_wall[0].astype(F32)
        sides = (has[2], has[3])
        to_left[at, :] = tall(k, near, 0, sides)[:HALO]
        to_right[at, :] = tall(k, far, wide - LANES, sides)[LANES - HALO :]
    k = parts + 1
    at = slice(k * HALO, (k + 1) * HALO)
    size = left_flow.shape[2] + LANES
    blank = jnp.zeros((HALO, to_left.shape[1] - size), F32)
    to_left[at, :size] = tall(k, left_flow[0, 0], 0, (1.0, 1.0))[:HALO]
    to_right[at, :size] = tall(k, right_flow[0, 0], flow_wide - LANES, (1.0, 1.0))[LANES - HALO :]
    to_left[at, size:] = blank
    to_right[at, size:] = blank


def sides_kernel(has, place, velocity, above, below, from_left, from_right, sides, squares, mark):
    parts, tall, _ = sides.shape
    gap = jnp.zeros((LANES - 2 * HALO, tall), F32)
    for k in range(parts):
        at = slice(k * HALO, (k + 1) * HALO)
        tile = [from_right[at, :] * has[1], gap, from_left[at, :] * has[0]]
        sides[k] = jnp.concatenate(tile, axis=0).T
    at = slice(parts * HALO, (parts + 1) * HALO)
    rows, local = velocity.shape[2:]
    size = rows + LANES
    tile = [from_right[at, :size], gap[:, :size], from_left[at, :size]]
    tile = jnp.concatenate(tile, axis=0).T
    tile = tile * tile
    mark[0] = place[0]
    over, under = (strip(ref, parts, ref is above, slice(0, local)) for ref in (above, below))
    squares[:HALO, :local] = over * over
    squares[HALO : HALO + rows, :local] = velocity[0, 0] * velocity[0, 0]
    squares[HALO + rows :, :local] = under * under
    squares[:HALO, local:] = tile[size - HALO :]
    squares[HALO : HALO + rows, local:] = tile[:rows]
    squares[HALO + rows :, local:] = tile[rows : rows + HALO]


def forward_x_kernel(place, *refs):
    *pieces, tables, turns, out, total, lines, made, sent = refs
    count, _, rows, local = lines.shape
    for mask, piece in enumerate(pieces):
        lines[place[0] ^ mask] = piece[...]
    base = turns.shape[1]
    per = local // base
    u = [lines[t // per, 0, :, (t % per) * base : (t % per + 1) * base] for t in range(RADIX)]
    v = [lines[t // per, 1, :, (t % per) * base : (t % per + 1) * base] for t in range(RADIX)]
    energy = sum(b * b for b in v)
    energy = jnp.sum(energy.reshape(rows // 8, 8, base), axis=0)
    total[...] = sum(energy[:, k : k + LANES] for k in range(0, base, LANES))
    fields = ([a * a - b * b for a, b in zip(u, v)], [2.0 * a * b for a, b in zip(u, v)])
    zeros, mids, reals, imags = [], [], [[], [], []], [[], [], []]
    for a in fields:
        s04, s26, s15, s37 = a[0] + a[4], a[2] + a[6], a[1] + a[5], a[3] + a[7]
        d04, d26, d15, d37 = a[0] - a[4], a[2] - a[6], a[1] - a[5], a[3] - a[7]
        zeros.append((s04 + s26) + (s15 + s37))
        mids.append((s04 + s26) - (s15 + s37))
        minus, plus = ROOT * (d15 - d37), ROOT * (d15 + d37)
        turned = (
            (d04 + minus, -d26 - plus),
            (s04 - s26, s37 - s15),
            (d04 - minus, d26 - plus),
        )
        for index, (real, imag) in enumerate(turned):
            c, s = turns[index : index + 1, :], turns[index + 3 : index + 4, :]
            reals[index].append(real * c + imag * s)
            imags[index].append(imag * c - real * s)
    stacked = jnp.concatenate(
        [
            jnp.concatenate([jnp.concatenate(reals[i], axis=0) for i in range(3)], axis=0),
            jnp.concatenate([jnp.concatenate(imags[i], axis=0) for i in range(3)], axis=0),
        ],
        axis=1,
    )
    full, zero, middle = x_parts(tables, base)
    full = exact_dot(split(stacked), full)
    zero = exact_dot(split(jnp.concatenate(zeros, axis=0)), zero)
    middle = exact_dot(split(jnp.concatenate(mids, axis=0)), middle)
    low = lane_index((rows, LANES)) % 64 < 32
    target, copies = 0, []
    blocks = [full[2 * rows * i : 2 * rows * (i + 1)] for i in range(3)] + [zero, middle]
    for block in blocks:
        start = target
        for first in range(0, block.shape[1], LANES):
            a = block[:rows, first : first + LANES]
            c = block[rows:, first : first + LANES]
            made[target] = jnp.where(low, a, spin(c, 32))
            made[target + 1] = jnp.where(low, spin(a, -32), c)
            target += 2
        group = pl.ds(start, target - start)
        copies.append(pltpu.make_async_copy(made.at[group], out.at[group], sent.at[len(copies)]))
        copies[-1].start()
    for copy in copies:
        copy.wait()


def eighths(x, turn):
    s04, s26, s15, s37 = x[0] + x[4], x[2] + x[6], x[1] + x[5], x[3] + x[7]
    d04, d26, d15, d37 = x[0] - x[4], x[2] - x[6], x[1] - x[5], x[3] - x[7]
    quarter = turn(s15 - s37)
    spun_26, spun_37 = turn(d26), turn(d37)
    one, three = d15 + spun_37, d15 - spun_37
    spun_one, spun_three = turn(one), turn(three)
    one = ROOT * (one + spun_one)
    three = ROOT * (spun_three - three)
    return [
        (s04 + s26) + (s15 + s37),
        (d04 + spun_26) + one,
        (s04 - s26) + quarter,
        (d04 - spun_26) + three,
        (s04 + s26) - (s15 + s37),
        (d04 + spun_26) - one,
        (s04 - s26) - quarter,
        (d04 - spun_26) - three,
    ]


def solve_y_kernel(count_x, _, lines, total, wave, both, turns, out, held, spread, made, sent):
    count, rows, _ = lines.shape
    base = turns.shape[0]
    length = count * rows
    block = count_x * rows
    per = base // rows
    lanes = lane_index((base, LANES))
    sign = jnp.where(lanes < 64, 1.0, -1.0).astype(F32)

    def minus_i(z):
        return spin(z, 64) * sign

    def plus_i(z):
        return spin(z, 64) * -sign

    fields = [
        jnp.concatenate([lines[t * per + k] for k in range(per)], axis=0) for t in range(RADIX)
    ]
    mixed = eighths(fields, minus_i)
    terms, columns = turns.shape[1], 2 * RADIX
    picked = lax.broadcasted_iota(jnp.int32, (terms, columns * LANES), 0) % columns
    lane = lane_index(picked.shape)
    value = jnp.where((lane >= RADIX * LANES) & (lane % LANES >= 64), -1.0, 1.0)
    spread[...] = dot(turns[...], jnp.where(picked == lane // LANES, value, 0.0).astype(BF16))
    cosines = [spread[:, r * LANES : (r + 1) * LANES] for r in range(RADIX)]
    sines = [spread[:, (r + RADIX) * LANES : (r + RADIX + 1) * LANES] for r in range(RADIX)]
    mixed = [mixed[0]] + [
        mixed[r] * cosines[r] + spin(mixed[r], 64) * sines[r] for r in range(1, RADIX)
    ]
    tables = (both[: 2 * base], both[2 * base :])
    product = exact_dot(tables, split(jnp.concatenate(mixed, axis=1)))
    kx = wave[0:1, :]
    first = lanes % 64 < 32
    edge = jnp.float32(length // 2)
    alone = jnp.where(first, kx * kx, 0.0)
    slope = jnp.where(first | (kx == -edge), 0.0, jnp.broadcast_to(kx, lanes.shape))
    q = lax.broadcasted_iota(jnp.int32, lanes.shape, 0)
    low_ky = RADIX * (q - jnp.where(q < base // 2, 0, base)).astype(F32)
    terms = []
    for r in range(RADIX):
        at = slice(r * LANES, (r + 1) * LANES)
        spectrum = product[:base, at] + minus_i(product[base:, at])
        ky = low_ky + float(r)
        symbol = alone + slope * ky
        if r == 0:
            corner = jnp.where((kx == -edge) & ~first, edge * edge, 0.0)
            symbol = jnp.where(ky == -edge, jnp.where(first, alone, corner), symbol)
        terms.append(symbol * pl.reciprocal(kx * kx + ky * ky) * spectrum)
    pairs = [
        jnp.where(first, low + spin(low, -32), high + spin(high, 32))
        for low, high in zip(terms[:4], terms[4:])
    ]
    product = exact_dot(tables, split(jnp.concatenate(pairs, axis=1)))
    mixed = []
    for r in range(RADIX // 2):
        at = slice(r * LANES, (r + 1) * LANES)
        value = product[:base, at] + plus_i(product[base:, at])
        cosine = jnp.where(first, cosines[r], cosines[r + 4])
        sine = jnp.where(first, sines[r], sines[r + 4])
        value = value * cosine - spin(value, 64) * sine
        value = jnp.where(first, value + spin(value, -32), spin(value, 32) - value)
        if r == 2:
            value = jnp.where(first, value, plus_i(value))
        elif r:
            turned = plus_i(value)
            odd = value + turned if r == 1 else turned - value
            value = jnp.where(first, value, ROOT * odd)
        mixed.append(value)
    even, odd = mixed[0] + mixed[2], mixed[0] - mixed[2]
    side, turned = mixed[1] + mixed[3], plus_i(mixed[1] - mixed[3])
    for t, values in enumerate((even + side, odd + turned, even - side, odd - turned)):
        start = MARGIN + 2 * t * base
        held[start : start + base, :] = values
        held[start + base : start + 2 * base, :] = spin(values, -32)
    held[0:MARGIN, :] = held[length : length + MARGIN, :]
    held[length + MARGIN : length + 2 * MARGIN, :] = held[MARGIN : 2 * MARGIN, :]
    spare = total[...] + spin(total[...], 32)
    kept = rows + 2 * MARGIN // count_x
    half = made.shape[1]
    rest = kept - half
    low = lane_index((8, LANES)) % 64 < 32
    copies = []
    for target in range(count):
        start = (target // count_x) * block + (target % count_x) * kept
        for row in range(0, half, 8):
            a = held[start + row : start + row + 8, :]
            if row < rest:
                b = spin(held[start + half + row : start + half + row + 8, :], 32)
            else:
                b = spare
            made[target, row : row + 8, :] = jnp.where(low, a, b)
        if (target + 1) % RADIX == 0:
            group = pl.ds(target + 1 - RADIX, RADIX)
            copies.append(pltpu.make_async_copy(made.at[group], out.at[group], sent.at[len(copies)]))
            copies[-1].start()
    for copy in copies:
        copy.wait()


def inverse_x_kernel(
    kept, scale, place, lines, tables, turns, *refs
):
    *outs, held = refs
    count, half, _ = lines.shape
    base = turns.shape[1]
    length = RADIX * base
    rest = kept - half
    low = lane_index((half, LANES)) % 64 < 32
    groups, spare = [], None
    for first in range(0, count, 2):
        even, odd = lines[first], lines[first + 1]
        a = jnp.where(low, even, spin(odd, 32))
        b = jnp.where(low, spin(even, -32), odd)
        groups.append(jnp.concatenate([a, b[:rest]], axis=0))
        extra = b[rest : rest + 8]
        spare = extra if spare is None else spare + extra
    mean = jnp.sum(spare) * scale
    wide = 2 * base // LANES
    narrow = base // LANES
    stacked = jnp.concatenate(
        [jnp.concatenate(groups[i * wide : (i + 1) * wide], axis=1) for i in range(3)], axis=0
    )
    at = 3 * wide
    zeros = jnp.concatenate(groups[at : at + narrow], axis=1)
    mids = jnp.concatenate(groups[at + narrow : at + 2 * narrow], axis=1)
    full, zero, middle = x_parts(tables, base)
    full = exact_dot(split(stacked), full)
    zero = exact_dot(split(zeros), zero) * scale
    mid = exact_dot(split(mids), middle) * scale
    turned = []
    for i in range(3):
        real = full[i * kept : (i + 1) * kept, :base]
        imag = full[i * kept : (i + 1) * kept, base:]
        c = turns[i : i + 1, :] * (2.0 * scale)
        s = turns[i + 3 : i + 4, :] * (2.0 * scale)
        turned.append((real * c - imag * s, real * s + imag * c))
    for t in range(RADIX):
        value = zero + mid if t % 2 == 0 else zero - mid
        for i, (real, imag) in enumerate(turned):
            eighth = t * (i + 1) % RADIX
            c = (1.0, ROOT, 0.0, -ROOT, -1.0, -ROOT, 0.0, ROOT)[eighth]
            s = (0.0, ROOT, 1.0, ROOT, 0.0, -ROOT, -1.0, -ROOT)[eighth]
            if c:
                value = value + c * real
            if s:
                value = value - s * imag
        held[:, t * base : (t + 1) * base] = mean - value
    targets, local = len(outs), outs[0].shape[1] - LANES
    right = lane_index((kept, LANES)) < 64
    for mask, out in enumerate(outs):
        start = pl.multiple_of((place[0] ^ mask) * local, LANES)
        after = pl.multiple_of(jnp.where(start + local == length, 0, start + local), LANES)
        before = pl.multiple_of(jnp.where(start == 0, length, start) - LANES, LANES)
        out[:, :local] = held[:, pl.ds(start, local)]
        out[:, local:] = jnp.where(
            right, held[:, pl.ds(after, LANES)], held[:, pl.ds(before, LANES)]
        )


def slopes_x(parts, band, with_edge):
    tiles = parts[0].shape[-1] // LANES
    pieces = []
    for first in list(range(0, tiles - 1, 2)) + ([tiles - 1] if with_edge else []):
        steps = (-1, 0, 1, 2) if first < tiles - 1 else (-1, 0, 1)
        table = band[...] if first < tiles - 1 else band[: 3 * LANES, :LANES]
        order = [(first + step) % tiles for step in steps]
        piece = None
        for part in parts:
            term = dot(jnp.concatenate([lane_tile(part, t) for t in order], axis=1), table)
            piece = term if piece is None else piece + term
        pieces.append(piece)
    return jnp.concatenate(pieces, axis=1)


def slope_y(read):
    value = read(3) - read(-3)
    for index in (0, 1):
        value = value + whole_weights[index] * (read(index + 1) - read(-index - 1))
    return value


def edged(k, side, center, up, down, above, below, sides, has, first=0):
    step = pl.program_id(0) + first
    tile, width = center.shape
    tall = sides.shape[1]
    last = (tall - LANES) // tile - 1
    base = pl.multiple_of(step * tile, 8)
    before = pl.multiple_of(jnp.where(step == 0, tall, base) - HALO, 8)
    over = jnp.where(step == 0, strip(above, k, True) * has[2], up)
    under = jnp.where(step == last, strip(below, k, False) * has[3], down)
    rows = (
        (over, sides[side, pl.ds(before, HALO), :]),
        (center, sides[side, pl.ds(base, tile), :]),
        (under, sides[side, pl.ds(pl.multiple_of(base + tile, 8), HALO), :]),
    )
    return jnp.concatenate([jnp.concatenate(pair, axis=1) for pair in rows], axis=0)


def edged_open(k, side, wall, wall_up, wall_down, above, below, sides, has, first=0):
    open_cells = [1.0 - ref[0].astype(F32) for ref in (wall, wall_up, wall_down)]
    return edged(k, side, *open_cells, above, below, sides, has, first)


def quiet_step_kernel(
    first, has, place, center, up, down, wall, wall_up, wall_down, above, below, sides, across, along, along_inner, calm, density, shown_open, mark
):
    parts, _, tile, width = center.shape
    high = tile + 2 * HALO
    opened = edged_open(parts, parts, wall, wall_up, wall_down, above, below, sides, has, first)
    values = []
    for k in range(parts):
        value = edged(
            k,
            k,
            center[k, 0].astype(F32),
            up[k, 0].astype(F32)[up.shape[2] - HALO :],
            down[k, 0].astype(F32)[:HALO],
            above,
            below,
            sides,
            has,
            first,
        )
        values.append(value)

    def drops(x, along_b, along_p):
        diverge = x[1] + along_b
        return (
            diverge + mean_flow * x[0],
            x[3] + mean_flow * x[1],
            along_p + mean_flow * x[2],
            diverge + mean_flow * x[3],
        )

    short = [value.astype(BF16) for value in values]
    x = slopes_x((jnp.concatenate(short, axis=0),), across, True)
    x = [x[k * high : (k + 1) * high] for k in range(parts)]
    table = along[...]
    dropped = drops(x, dot(table, short[2]), dot(table, short[3]))
    middle = [opened * (v - (time_step / 60.0) * d) for v, d in zip(values, dropped)]
    inner = slice(HALO, HALO + tile)
    x = slopes_x(split(jnp.concatenate([value[inner] for value in middle], axis=0)), across, False)
    x = [x[k * tile : (k + 1) * tile] for k in range(parts)]
    table = along_inner[...]
    y = [sum(dot(table, part) for part in split(middle[k][:, :width])) for k in (2, 3)]
    dropped = drops(x, *y)
    shown = opened[inner, :width]
    for k in range(parts):
        start = 0.5 * values[k][inner, :width] - (0.5 * time_step / 60.0) * dropped[k]
        value = shown * start + 0.5 * middle[k][inner, :width]
        if k == 0:
            density[0, 0] = value.astype(BF16)
        else:
            calm[k - 1] = value
    shown_open[0] = opened.astype(BF16)
    mark[0] = place[0]


def tables_kernel(place, weights_x, weights_y, rise_x, rise_y):
    tiles, reach_x, lanes = rise_x.shape
    wide, length_x = (tiles - 1) * lanes, weights_x.shape[1]
    first = place[0] * wide
    half = LANES // 2

    def weights(ref, start, size):
        length = ref.shape[1]
        start = jnp.where(start < 0, start + length, jnp.where(start >= length, start - length, start))
        return ref[:, pl.ds(pl.multiple_of(start, LANES), size)]

    cells = lax.broadcasted_iota(jnp.int32, (reach_x, lanes), 0)
    fine = lax.broadcasted_iota(jnp.int32, (reach_x, lanes), 1)
    right, left = weights(weights_x, first + wide, LANES), weights(weights_x, first - LANES, LANES)
    edge = jnp.where(lane_index(right.shape) < half, right, left)
    edge = jnp.concatenate([edge, edge], axis=1)
    for k in range(tiles):
        own = weights(weights_x, first + k * lanes, lanes) if k < tiles - 1 else edge
        target = fine // 2 - 1
        if k == tiles - 1:
            target = jnp.where(fine < half, target, target + half)
        value = jnp.zeros(fine.shape, F32)
        for t in range(4):
            value = jnp.where(cells == (target + t) % reach_x, own[t : t + 1, :], value)
        rise_x[k] = value
    steps, high, reach = rise_y.shape
    tall = steps * TILE
    first = place[1] * tall
    own = [weights(weights_y, first + k * LANES, LANES) for k in range(-1, tall // LANES + 1)]
    own = jnp.concatenate([jnp.concatenate(own, axis=1), jnp.zeros((4, tall + 2 * LANES), F32)], axis=0).T
    cells = lax.broadcasted_iota(jnp.int32, (high, reach), 1) % (reach // 3)
    target = lax.broadcasted_iota(jnp.int32, (high, reach), 0) // 2 + (HALO // 2 - 1)
    for k in range(steps):
        start = LANES - HALO + k * TILE
        value = jnp.zeros((high, reach), F32)
        for t in range(4):
            value = jnp.where(cells == target + t, own[start : start + high, t : t + 1], value)
        rise_y[k] = value


def source_kernel(place, squares, opened, rise_x, rise_y, quiet, across, _, *refs):
    *lines, out, squared, cells_open, matrix, rows_matrix, calm, band, held, raised, forced, done, fetched, kept = refs
    steps = done.shape[0]
    tile, width = calm.shape[2:]
    high = tile + 2 * HALO
    rows = lines[0].shape[0]

    def calm_copy(k):
        part = quiet.at[:, pl.ds(k * tile, tile), :]
        return pltpu.make_async_copy(part, calm.at[k % 2], fetched.at[k % 2])

    def done_copy(k):
        part = out.at[1:, 0, pl.ds(k * tile, tile), :]
        return pltpu.make_async_copy(done.at[k], part, kept.at[k])

    arrays = [(squares, squared), (rise_x, matrix), (rise_y, rows_matrix), (opened, cells_open), (across, band)]
    copies = [
        pltpu.make_async_copy(source, target, fetched.at[2 + k])
        for k, (source, target) in enumerate(arrays)
    ]
    pieces = [
        pltpu.make_async_copy(
            piece,
            held.at[pl.ds(pl.multiple_of((place[0] ^ mask) * rows, 8), rows), :],
            fetched.at[2 + len(arrays) + mask],
        )
        for mask, piece in enumerate(lines)
    ]
    for copy in pieces + copies:
        copy.start()
    calm_copy(0).start()
    calm_copy(1).start()
    for copy in pieces + copies[:1]:
        copy.wait()

    level = held[MARGIN - HALO : MARGIN - HALO + squared.shape[0], :] - squared[...]
    count = level.shape[1] // LANES
    near = lane_index((level.shape[0], LANES)) < 64
    around = []
    for k in range(count):
        after, before = lane_tile(level, (k + 1) % count), lane_tile(level, (k - 1) % count)
        around.append(split(jnp.concatenate([lane_tile(level, k), jnp.where(near, after, before)], axis=1)))
    copies[1].wait()
    for k in range(count):
        lanes = 2 * LANES if k < count - 1 else LANES
        value = split(exact_dot(around[k], split(matrix[k][:, :lanes])))
        for part in range(2):
            raised[part, :, 2 * k * LANES : 2 * k * LANES + lanes] = value[part]
    for copy in copies[2:]:
        copy.wait()

    reach = rows_matrix.shape[2] // 3
    third = lane_index((high, 3 * reach)) >= 2 * reach
    for k in range(steps):
        start = k * (tile // 2)
        window = [raised[part, start : start + reach, :] for part in (0, 1, 0)]
        weights = split(rows_matrix[k])
        weights = jnp.where(third, weights[1], weights[0])
        free = time_step * cells_open[k].astype(F32)
        value = free * dot(weights, jnp.concatenate(window, axis=0))
        forced[k % 2] = value
        inner = value[HALO : HALO + tile]
        shown = (0.5 / 60.0) * free[HALO : HALO + tile, :width]
        x = shown * slopes_x(split(inner), band, False)
        y = shown * slope_y(lambda d: forced[k % 2, HALO + d : HALO + d + tile, :width])
        calm_copy(k).wait()
        still = calm.at[k % 2]
        done[k, 0] = (still[0] - x).astype(BF16)
        done[k, 1] = (still[1] - y).astype(BF16)
        done[k, 2] = (still[2] + inner[:, :width] - mean_flow * x).astype(BF16)
        done_copy(k).start()
        if k + 2 < steps:
            calm_copy(k + 2).start()
    for k in range(steps):
        done_copy(k).wait()


def call(
    kernel, operands, outs, scratch=(), steps=0, specs=None, out_specs=None, after=(), aliases=None, megabytes=24, flops=0, moved=0, name=None
):
    count = len(operands)

    def body(*refs):
        kernel(*refs[:count], *refs[count + len(after) :])

    def whole(array):
        zeros = (0,) * len(array.shape)
        return pl.BlockSpec(array.shape, lambda *_: zeros)

    arguments = {}
    chosen = specs or {}
    if steps:
        arguments["grid"] = (steps,)
        in_specs = [chosen.get(i, whole(o)) for i, o in enumerate(operands)]
        arguments["out_specs"] = jax.tree.map(whole, outs) if out_specs is None else out_specs
    else:
        local = pl.BlockSpec(memory_space=pltpu.VMEM)
        in_specs = [chosen.get(i, local) for i in range(count)]
        if out_specs is not None:
            arguments["out_specs"] = out_specs
    return pl.pallas_call(
        body,
        out_shape=outs,
        in_specs=in_specs + [pl.BlockSpec(memory_space=pl.ANY)] * len(after),
        scratch_shapes=list(scratch),
        input_output_aliases=aliases or {},
        compiler_params=pltpu.CompilerParams(vmem_limit_bytes=megabytes << 20),
        cost_estimate=pl.CostEstimate(flops=flops, bytes_accessed=moved, transcendentals=0),
        name=name,
        **arguments,
    )(*operands, *after)


def ring(array, axis, step):
    size = lax.axis_size(axis)
    return lax.ppermute(array, axis, [(i, (i + step) % size) for i in range(size)])


def swap(array, axis, mask):
    return lax.ppermute(array, axis, [(i, i ^ mask) for i in range(lax.axis_size(axis))])


def shaped(*shape, kind=F32):
    return jax.ShapeDtypeStruct(shape, kind)


def pressure_lines(pieces, place_x, gathered, spread, stepped):
    _, rows, local_x = pieces[0].shape
    count_x, count_y = lax.axis_size("gx"), lax.axis_size("gy")
    count = count_x * count_y
    scalars = {0: pl.BlockSpec(memory_space=pltpu.SMEM)}
    length_x, length_y = local_x * count_x, rows * count
    full, zero, middle, cos_turn, sin_turn = x_tables(length_x)
    turns = np.zeros((8, cos_turn.shape[1]), np.float32)
    turns[0:3], turns[3:6] = cos_turn, sin_turn
    spectra, total = call(
        forward_x_kernel,
        (place_x, *pieces, np.concatenate([beside(full), beside(zero, middle)]), turns),
        (shaped(count, rows, LANES), shaped(8, LANES)),
        (
            pltpu.VMEM((count_x, 2, rows, local_x), F32),
            pltpu.VMEM((count, rows, LANES), F32),
            pltpu.SemaphoreType.DMA((5,)),
        ),
        specs=scalars,
        out_specs=(pl.BlockSpec(memory_space=pl.ANY), pl.BlockSpec(memory_space=pltpu.VMEM)),
        after=gathered,
        flops=10**9,
        moved=4 << 20,
        name="forward_x",
    )
    spectra = lax.all_to_all(spectra, ("gy", "gx"), 0, 0, tiled=True)
    place = lax.axis_index("gy") * count_x + lax.axis_index("gx")
    waves = jnp.asarray(wave_table(length_x, count))
    wave = lax.dynamic_slice(waves, (place, 0), (1, LANES))
    both, turns_y = y_tables(length_y)
    kept = rows + 2 * MARGIN // count_x
    half = (kept // 2 + 8) // 8 * 8
    solved = call(
        functools.partial(solve_y_kernel, count_x),
        (spread, spectra, total, wave, beside(both), turns_y),
        shaped(count, half, LANES),
        (
            pltpu.VMEM((length_y + 2 * MARGIN, LANES), F32),
            pltpu.VMEM((length_y // RADIX, 2 * RADIX * LANES), F32),
            pltpu.VMEM((count, half, LANES), F32),
            pltpu.SemaphoreType.DMA((count // RADIX,)),
        ),
        specs=scalars,
        out_specs=pl.BlockSpec(memory_space=pl.ANY),
        flops=4 * 10**9,
        moved=6 << 20,
        name="solve_y",
    )
    solved = lax.all_to_all(solved, ("gy", "gx"), 0, 0, tiled=True)
    back = 2.0 * zero.T
    back[LANES // 2] *= 0.5
    tables = np.concatenate(
        [beside(full.T), beside(back, 2.0 * middle.T)]
    )
    pressed = call(
        functools.partial(inverse_x_kernel, kept, 1.0 / (length_x * length_y)),
        (stepped, solved, tables, turns),
        (shaped(kept, local_x + LANES),) * count_x,
        (pltpu.VMEM((kept, length_x), F32),),
        specs=scalars,
        flops=10**9,
        moved=4 << 20,
        name="inverse_x",
    )
    return [piece if mask == 0 else swap(piece, "gx", mask) for mask, piece in enumerate(pressed)]


def fast_shards(velocity, weights_x, weights_y, acoustic, wall_mask):
    parts, _, tall, wide = acoustic.shape
    _, _, local_y, local_x = velocity.shape
    count_x, count_y = lax.axis_size("gx"), lax.axis_size("gy")
    place_x, place_y = lax.axis_index("gx"), lax.axis_index("gy")
    full, high, steps = wide + LANES, TILE + 2 * HALO, tall // TILE
    strips = (parts + 2) * HALO
    small = 2 * HALO
    has = jnp.stack([place_x > 0, place_x < count_x - 1, place_y > 0, place_y < count_y - 1])
    has = has.astype(F32)
    scalars = pl.BlockSpec(memory_space=pltpu.SMEM)

    def at(block, *index):
        return pl.BlockSpec(block, lambda i: index)

    own = place_x.astype(jnp.int32).reshape(1)
    first, last, cut = call(
        rows_kernel,
        (own, acoustic, acoustic, wall_mask, wall_mask, velocity, velocity),
        (shaped(STRIP_ROWS, wide),) * 2 + (shaped(1, kind=jnp.int32),),
        steps=1,
        specs={
            0: scalars,
            1: at((parts, 1, small, wide), 0, 0, 0, 0),
            2: at((parts, 1, small, wide), 0, 0, tall // small - 1, 0),
            3: at((1, HALO, wide), 0, 0, 0),
            4: at((1, HALO, wide), 0, tall // HALO - 1, 0),
            5: at((1, 1, HALO, local_x), 1, 0, 0, 0),
            6: at((1, 1, HALO, local_x), 1, 0, local_y // HALO - 1, 0),
        },
        out_specs=(at((STRIP_ROWS, wide), 0, 0),) * 2 + (scalars,),
        moved=2 << 20,
        megabytes=54,
        name="rows",
    )
    sent = call(
        pieces_kernel,
        (cut, velocity),
        (shaped(2, local_y // count_x, local_x),) * count_x,
        specs={0: scalars},
        moved=2 << 20,
        megabytes=8,
        name="pieces",
    )
    moved = [piece if mask == 0 else swap(piece, "gx", mask) for mask, piece in enumerate(sent)]
    above, below = ring(last, "gy", 1), ring(first, "gy", -1)
    to_right, to_left = call(
        columns_kernel,
        (has, acoustic, acoustic, wall_mask, wall_mask, velocity, velocity, above, below),
        (shaped(strips, tall + LANES), shaped(strips, tall + LANES)),
        steps=1,
        specs={
            0: scalars,
            1: at((parts, 1, tall, LANES), 0, 0, 0, 0),
            2: at((parts, 1, tall, LANES), 0, 0, 0, wide // LANES - 1),
            3: at((1, tall, LANES), 0, 0, 0),
            4: at((1, tall, LANES), 0, 0, wide // LANES - 1),
            5: at((1, 1, local_y, LANES), 1, 0, 0, 0),
            6: at((1, 1, local_y, LANES), 1, 0, 0, local_x // LANES - 1),
        },
        moved=8 << 20,
        megabytes=54,
        name="columns",
    )
    from_left, from_right = ring(to_right, "gx", 1), ring(to_left, "gx", -1)
    sides, squares, beside = call(
        sides_kernel,
        (has, own, velocity, above, below, from_left, from_right),
        (
            shaped(parts + 1, tall + LANES, LANES),
            shaped(local_y + 2 * HALO, local_x + LANES),
            shaped(1, kind=jnp.int32),
        ),
        steps=1,
        specs={0: scalars, 1: scalars, 2: at((1, 1, local_y, local_x), 1, 0, 0, 0)},
        out_specs=(
            at((parts + 1, tall + LANES, LANES), 0, 0, 0),
            at((local_y + 2 * HALO, local_x + LANES), 0, 0),
            scalars,
        ),
        moved=8 << 20,
        megabytes=54,
        name="sides",
    )
    across, along = band_tables(high)
    along_inner = along[HALO : HALO + TILE]
    per, rows = TILE // small, TILE // HALO

    def tiled(first):
        walls = (
            pl.BlockSpec((1, TILE, wide), lambda i: (0, i + first, 0)),
            pl.BlockSpec((1, HALO, wide), lambda i: (0, jnp.maximum((i + first) * rows - 1, 0), 0)),
            pl.BlockSpec(
                (1, HALO, wide),
                lambda i: (0, jnp.minimum((i + first + 1) * rows, steps * rows - 1), 0),
            ),
        )
        cells = (
            pl.BlockSpec((parts, 1, TILE, wide), lambda i: (0, 0, i + first, 0)),
            pl.BlockSpec(
                (parts, 1, small, wide), lambda i: (0, 0, jnp.maximum((i + first) * per - 1, 0), 0)
            ),
            pl.BlockSpec(
                (parts, 1, small, wide),
                lambda i: (0, 0, jnp.minimum((i + first + 1) * per, steps * per - 1), 0),
            ),
        )
        return cells, walls

    def quiet_tiles(first, count, before):
        cells, walls = tiled(first)
        operands = (has, own, acoustic, acoustic, acoustic, wall_mask, wall_mask, wall_mask, above, below, sides)
        operands = operands + (across, along, along_inner)
        return call(
            functools.partial(quiet_step_kernel, first),
            operands,
            (
                shaped(parts - 1, tall, wide),
                shaped(*acoustic.shape, kind=BF16),
                shaped(steps, high, full, kind=BF16),
                shaped(1, kind=jnp.int32),
            ),
            steps=count,
            specs=dict(enumerate((scalars, scalars) + cells + walls)),
            out_specs=(
                pl.BlockSpec((parts - 1, TILE, wide), lambda i: (0, i + first, 0)),
                pl.BlockSpec((1, 1, TILE, wide), lambda i: (0, 0, i + first, 0)),
                pl.BlockSpec((1, high, full), lambda i: (i + first, 0, 0)),
                scalars,
            ),
            after=before,
            aliases={len(operands) + k: k for k in range(len(before))},
            megabytes=54 if first == 0 else 53,
            flops=3 * 10**9 * count,
            moved=(12 << 20) * count,
            name="quiet_step",
        )

    early = max(steps * 3 // 4, 1)
    *begun, stepped = quiet_tiles(0, early, ())
    if early < steps:
        *begun, _ = quiet_tiles(early, steps - early, begun)
    quiet, final, opened = begun
    lines = pressure_lines(moved, own, (above, below), beside, stepped)
    tiles = wide // (2 * LANES) + 1
    rise_x, rise_y = call(
        tables_kernel,
        (jnp.stack([place_x, place_y]).astype(jnp.int32), weights_x, weights_y),
        (shaped(tiles, 2 * LANES, 2 * LANES), shaped(steps, high, 3 * (high // 2 + HALO))),
        specs={0: scalars},
        moved=4 << 20,
        megabytes=54,
        name="tables",
    )
    operands = (own, squares, opened, rise_x, rise_y, quiet, across, final, *lines)
    anywhere = pl.BlockSpec(memory_space=pl.ANY)
    specs = {k: anywhere for k in range(1, len(operands))}
    scratch = (
        pltpu.VMEM(squares.shape, F32),
        pltpu.VMEM(opened.shape, BF16),
        pltpu.VMEM(rise_x.shape, F32),
        pltpu.VMEM(rise_y.shape, F32),
        pltpu.VMEM((2, parts - 1, TILE, wide), F32),
        pltpu.VMEM(across.shape, BF16),
        pltpu.VMEM((local_y + 2 * MARGIN, local_x + LANES), F32),
        pltpu.VMEM((2, local_y + 2 * HALO, full), BF16),
        pltpu.VMEM((2, high, full), F32),
        pltpu.VMEM((steps, parts - 1, TILE, wide), BF16),
        pltpu.SemaphoreType.DMA((7 + count_x,)),
        pltpu.SemaphoreType.DMA((steps,)),
    )
    return call(
        source_kernel,
        operands,
        shaped(*acoustic.shape, kind=BF16),
        scratch,
        specs={0: scalars, **specs},
        out_specs=anywhere,
        aliases={7: 0},
        megabytes=55,
        flops=4 * 10**9,
        moved=16 << 20,
        name="source_step",
    )


def fits(count_x, count_y, velocity, acoustic):
    _, planes, local_y, local_x = velocity
    _, _, tall, wide = acoustic
    length_x, length_y = local_x * count_x, local_y * count_y
    rows = local_y // count_x
    base_x, base_y = length_x // RADIX, length_y // RADIX
    return (
        planes == 1
        and acoustic[0] == PARTS
        and length_x * 2 == count_x * count_y * LANES
        and base_x % (2 * LANES) == 0
        and local_x % base_x == 0
        and rows % 8 == 0
        and base_y % rows == 0
        and base_y % 8 == 0
        and count_x * count_y % RADIX == 0
        and MARGIN * 2 % (8 * count_x) == 0
        and tall == 2 * local_y
        and wide == 2 * local_x
        and tall % TILE == 0
        and tall % LANES == 0
        and tall >= 2 * TILE
        and count_x & (count_x - 1) == 0
        and wide % (2 * LANES) == 0
    )


def extended(array, sides, width):
    for axis, dim in sides:
        size, length = (lax.axis_size(axis), array.shape[dim])
        up = [(i, (i + 1) % size) for i in range(size - 1)]
        down = [(j, i) for i, j in up]
        last = lax.slice_in_dim(array, length - width, length, axis=dim)
        leading = lax.slice_in_dim(array, 0, width, axis=dim)
        before = lax.ppermute(last, axis, up)
        after = lax.ppermute(leading, axis, down)
        array = jnp.concatenate([before, array, after], axis=dim)
    return array


def gradients(padded):
    height = padded.shape[-2] - 6
    breadth = padded.shape[-1] - 6
    rows_mid = padded[..., 3 : 3 + height, :]
    cols_mid = padded[..., :, 3 : 3 + breadth]
    along_x = jnp.zeros_like(padded[..., 3 : 3 + height, 3 : 3 + breadth])
    along_y = jnp.zeros_like(along_x)
    for index, weight in enumerate(stencil_weights):
        distance = index + 1
        along_x = along_x + weight * (
            rows_mid[..., 3 + distance : 3 + distance + breadth]
            - rows_mid[..., 3 - distance : 3 - distance + breadth]
        )
        along_y = along_y + weight * (
            cols_mid[..., 3 + distance : 3 + distance + height, :]
            - cols_mid[..., 3 - distance : 3 - distance + height, :]
        )
    return (along_x, along_y)


def tendency(padded, source):
    along_x, along_y = gradients(padded)
    diverge = along_x[1] + along_y[2]
    forcing = jnp.stack([-diverge, -along_x[3], -along_y[3], source - diverge])
    return forcing - mean_flow * along_x


def spectral_index(flat, length):
    second = length // 16
    wave = flat // second + 16 * (flat % second)
    return jnp.where(wave < length // 2, wave, wave - length).astype(jnp.float32)


def twiddles(rows_count, cols_count, modulus, sign):
    products = jnp.arange(rows_count)[:, None] * jnp.arange(cols_count)[None, :] % modulus
    angles = 2.0 * math.pi / modulus * products.astype(jnp.float32)
    return (jnp.cos(angles), sign * jnp.sin(angles))


def mix_rows(real_part, imag_part, cosine, sine):
    exact = lax.Precision.HIGHEST
    cos_real = jnp.einsum("ka,...ab->...kb", cosine, real_part, precision=exact)
    cos_imag = jnp.einsum("ka,...ab->...kb", cosine, imag_part, precision=exact)
    sin_real = jnp.einsum("ka,...ab->...kb", sine, real_part, precision=exact)
    sin_imag = jnp.einsum("ka,...ab->...kb", sine, imag_part, precision=exact)
    return (cos_real - sin_imag, cos_imag + sin_real)


def mix_cols(real_part, imag_part, cosine, sine):
    exact = lax.Precision.HIGHEST
    cos_real = jnp.einsum("...kb,bc->...kc", real_part, cosine, precision=exact)
    cos_imag = jnp.einsum("...kb,bc->...kc", imag_part, cosine, precision=exact)
    sin_real = jnp.einsum("...kb,bc->...kc", real_part, sine, precision=exact)
    sin_imag = jnp.einsum("...kb,bc->...kc", imag_part, sine, precision=exact)
    return (cos_real - sin_imag, cos_imag + sin_real)


def rotate(real_part, imag_part, cosine, sine):
    return (real_part * cosine - imag_part * sine, real_part * sine + imag_part * cosine)


def discrete(real_part, imag_part, sign):
    length = real_part.shape[-1]
    second = length // 16
    initial = real_part.shape
    folded = initial[:-1] + (16, second)
    real_part = real_part.reshape(folded)
    imag_part = imag_part.reshape(folded)
    small_cos, small_sin = twiddles(16, 16, 16, sign)
    large_cos, large_sin = twiddles(second, second, second, sign)
    turn_cos, turn_sin = twiddles(16, second, length, sign)
    if sign < 0:
        real_part, imag_part = mix_rows(real_part, imag_part, small_cos, small_sin)
        real_part, imag_part = rotate(real_part, imag_part, turn_cos, turn_sin)
        real_part, imag_part = mix_cols(real_part, imag_part, large_cos, large_sin)
    else:
        real_part, imag_part = mix_cols(real_part, imag_part, large_cos, large_sin)
        real_part, imag_part = rotate(real_part, imag_part, turn_cos, turn_sin)
        real_part, imag_part = mix_rows(real_part, imag_part, small_cos, small_sin)
        real_part = real_part / length
        imag_part = imag_part / length
    return (real_part.reshape(initial), imag_part.reshape(initial))


def transform(stacked, sign, kind):
    if kind == "real_in":
        real_part = stacked
        imag_part = jnp.zeros_like(stacked)
    else:
        half = stacked.shape[0] // 2
        real_part = stacked[:half]
        imag_part = stacked[half:]
    real_out, imag_out = discrete(real_part, imag_part, sign)
    if kind == "real_out":
        return real_out
    return jnp.concatenate([real_out, imag_out], axis=0)


def project(stacked, wave_x, wave_y):
    coef_xx = wave_x * wave_x
    coef_xy = 2.0 * wave_x * wave_y
    coef_yy = wave_y * wave_y
    denominator = wave_x * wave_x + wave_y * wave_y
    positive = denominator > 0
    safe = jnp.where(positive, denominator, 1.0)

    def combine(parts):
        numerator = -(coef_xx * parts[0] + coef_xy * parts[1] + coef_yy * parts[2])
        return jnp.where(positive, numerator / safe, 0.0)

    return jnp.stack([combine(stacked[:3]), combine(stacked[3:])])


def refine(stacked, weights):
    result = jnp.zeros(stacked.shape[:-1] + (2 * stacked.shape[-1],), jnp.float32)
    for offset in range(4):
        result = (
            result
            + jnp.repeat(jnp.roll(stacked, 1 - offset, axis=-1), 2, axis=-1) * weights[offset]
        )
    return result


def lines_x(stacked, action):
    gathered = action(lax.all_to_all(stacked, "gx", split_axis=2, concat_axis=3, tiled=True))
    return lax.all_to_all(gathered, "gx", split_axis=3, concat_axis=2, tiled=True)


def lines_y(stacked, action):
    turned = jnp.swapaxes(stacked, 2, 3)
    gathered = action(lax.all_to_all(turned, "gy", split_axis=2, concat_axis=3, tiled=True))
    returned = lax.all_to_all(gathered, "gy", split_axis=3, concat_axis=2, tiled=True)
    return jnp.swapaxes(returned, 2, 3)


def expand(fields):
    return extended(fields, (("gx", 3), ("gy", 2)), 3)


def shards(velocity, weights_x, weights_y, acoustic, wall_mask):
    acoustic = acoustic.astype(jnp.float32)
    flow_x = velocity[0]
    flow_y = velocity[1]
    tensor = jnp.stack([flow_x * flow_x, flow_x * flow_y, flow_y * flow_y])
    count_gx = lax.axis_size("gx")
    count_gy = lax.axis_size("gy")
    place_x = lax.axis_index("gx")
    place_y = lax.axis_index("gy")
    local_y = tensor.shape[2]
    local_x = tensor.shape[3]
    length_x = local_x * count_gx
    length_y = local_y * count_gy

    def forward_real(portion):
        return transform(portion, -1, "real_in")

    def finish_x(portion):
        return refine(transform(portion, 1, "real_out"), weights_x)

    spectra = lines_x(tensor, forward_real)
    share_x = local_x // count_gy
    line_x = spectral_index(place_x * local_x + place_y * share_x + jnp.arange(share_x), length_x)[
        :, None
    ]
    line_y = spectral_index(jnp.arange(length_y), length_y)[None, :]

    def solve_y(portion):
        solved = project(transform(portion, -1, "complex"), line_x, line_y)
        return refine(transform(solved, 1, "complex"), weights_y)

    pressure = lines_y(spectra, solve_y)
    source = lines_x(pressure, finish_x)[0]
    open_cells = (1 - wall_mask).astype(jnp.float32)
    first_rate = tendency(expand(acoustic), source)
    middle = open_cells * (acoustic + time_step * first_rate)
    second_rate = tendency(expand(middle), source)
    return (open_cells * (acoustic + 0.5 * time_step * (first_rate + second_rate))).astype(
        jnp.bfloat16
    )


def solution(mesh):
    in_specs = (P(None, None, "gy", "gx"), P(), P(), P(None, None, "gy", "gx"), P(None, "gy", "gx"))
    out_specs = P(None, None, "gy", "gx")

    def chosen(velocity, weights_x, weights_y, acoustic, wall_mask):
        sizes = (mesh.shape["gx"], mesh.shape["gy"], velocity.shape, acoustic.shape)
        plan = fast_shards if fits(*sizes) else shards
        return plan(velocity, weights_x, weights_y, acoustic, wall_mask)

    return jax.shard_map(
        chosen, mesh=mesh, in_specs=in_specs, out_specs=out_specs, check_vma=False
    )
```

```python
import functools
import math

import jax
import jax.numpy as jnp
import ml_dtypes
import numpy as np
from jax import lax
from jax.experimental import pallas as pl
from jax.experimental.pallas import tpu as pltpu
from jax.sharding import PartitionSpec as P

stencil_weights = (0.75, -0.15, 1.0 / 60.0)
mean_flow = 0.3
time_step = 0.5
whole_weights = (45.0, -9.0, 1.0)

LANES = 128
RADIX = 8
HALO = 8
MARGIN = 16
TILE = 128
ROOT = math.sqrt(0.5)
STRIP = {2: (0, 6), 3: (6, 6), 1: (12, 3), 4: (15, 3), 5: (20, 4)}
STRIP_ROWS = 24
PARTS = 4
BF16 = jnp.bfloat16
F32 = jnp.float32


def halves(table):
    high = table.astype(np.float32).astype(ml_dtypes.bfloat16)
    low = (table - high.astype(np.float64)).astype(np.float32).astype(ml_dtypes.bfloat16)
    return high, low


def packed_columns(cosine, sine):
    half = LANES // 2
    parts = []
    for first in range(0, cosine.shape[1], half):
        parts += [cosine[:, first : first + half], sine[:, first : first + half]]
    return np.concatenate(parts, axis=1)


@functools.lru_cache(maxsize=None)
def x_tables(length):
    base = length // RADIX
    m = np.arange(base)[:, None]
    q = np.arange(base)[None, :]
    angle = 2.0 * np.pi * ((m * q) % base) / base
    cosine, sine = np.cos(angle), np.sin(angle)
    full = np.concatenate([packed_columns(cosine, -sine), packed_columns(sine, cosine)], axis=0)
    half = base // 2
    zero_cos, zero_sin = cosine[:, :half].copy(), -sine[:, :half]
    zero_cos[:, 0] = 0.0
    zero_sin = zero_sin.copy()
    zero_sin[:, 0] = (-1.0) ** np.arange(base)
    zero = packed_columns(zero_cos, zero_sin)
    shifted = 2.0 * np.pi * ((m * (RADIX * q[:, :half] + RADIX // 2)) % length) / length
    middle = packed_columns(np.cos(shifted), -np.sin(shifted))
    turns = 2.0 * np.pi * np.arange(1, RADIX // 2)[:, None] * np.arange(base)[None, :] / length
    return full, zero, middle, np.cos(turns), np.sin(turns)


@functools.lru_cache(maxsize=None)
def y_tables(length):
    base = length // RADIX
    index = np.arange(base)
    angle = 2.0 * np.pi * ((index[:, None] * index[None, :]) % base) / base
    both = np.concatenate([np.cos(angle), np.sin(angle)], axis=0)
    turns = 2.0 * np.pi * np.arange(RADIX)[:, None] * index[None, :] / length
    turns = np.concatenate([np.cos(turns), np.sin(turns)], axis=0).T
    high, rest = halves(turns)
    low = turns - high.astype(np.float64) - rest.astype(np.float64)
    return both, np.concatenate([high, rest, low.astype(ml_dtypes.bfloat16)], axis=1)


@functools.lru_cache(maxsize=None)
def wave_table(length, count):
    slots = LANES // 4
    base = length // RADIX
    waves = []
    for residue in (1, 2, 3):
        waves.append(RADIX * np.arange(base) + residue)
    waves.append(RADIX * np.arange(base // 2))
    waves.append(RADIX * np.arange(base // 2) + RADIX // 2)
    waves = np.concatenate(waves)
    waves = np.where(waves == 0, length // 2, waves)
    waves = np.where(waves < length // 2, waves, waves - length).reshape(count, slots)
    return np.tile(waves, (1, 4)).astype(np.float32)


@functools.lru_cache(maxsize=None)
def band_tables(rows):
    across = np.zeros((4 * LANES, 2 * LANES))
    column = np.arange(2 * LANES)
    down = np.zeros((rows, rows))
    for index, weight in enumerate(whole_weights):
        distance = index + 1
        across[column + LANES + distance, column] = weight
        across[column + LANES - distance, column] = -weight
        down += weight * (np.eye(rows, k=distance) - np.eye(rows, k=-distance))
    return across.astype(ml_dtypes.bfloat16), down.astype(ml_dtypes.bfloat16)


def beside(*tables):
    high, low = halves(np.concatenate(tables, axis=1))
    return np.concatenate([high, low], axis=0)


def split(values):
    high = values.astype(BF16)
    return high, (values - high.astype(F32)).astype(BF16)


def dot(left, right):
    return jnp.dot(left, right, preferred_element_type=F32)


def exact_dot(left, right):
    left_high, left_low = left
    right_high, right_low = right
    return dot(left_high, right_high) + (dot(left_low, right_high) + dot(left_high, right_low))


def lane_index(shape):
    return lax.broadcasted_iota(jnp.int32, shape, len(shape) - 1)


def spin(values, shift):
    return pltpu.roll(values, shift % values.shape[-1], values.ndim - 1)


def lane_tile(values, index):
    return values[:, index * LANES : (index + 1) * LANES]


def x_parts(tables, base):
    wide = 2 * base
    full = (tables[:wide], tables[wide : 2 * wide])
    at = 2 * wide
    high, low = tables[at : at + base], tables[at + base : at + 2 * base]
    return full, (high[:, :base], low[:, :base]), (high[:, base:], low[:, base:])


def pieces_kernel(place, velocity, *pieces):
    rows = pieces[0].shape[1]
    for mask, piece in enumerate(pieces):
        start = pl.multiple_of((place[0] ^ mask) * rows, 8)
        for c in range(2):
            piece[c] = velocity[c, 0, pl.ds(start, rows), :]


def rows_kernel(place, top, low, top_wall, low_wall, top_flow, low_flow, first, last, mark):
    small, width = top.shape[2], top_flow.shape[3]
    mark[0] = place[0]
    first[...] = jnp.zeros(first.shape, F32)
    last[...] = jnp.zeros(last.shape, F32)
    for k, (start, rows) in STRIP.items():
        lanes = slice(0, width) if k == PARTS + 1 else slice(None)
        if k < PARTS:
            upper, lower = top[k, 0].astype(F32)[:HALO], low[k, 0].astype(F32)[small - HALO :]
        elif k == PARTS:
            upper, lower = 1.0 - top_wall[0].astype(F32), 1.0 - low_wall[0].astype(F32)
        else:
            upper, lower = top_flow[0, 0], low_flow[0, 0]
        first[start : start + rows, lanes] = upper[:rows]
        last[start : start + rows, lanes] = lower[HALO - rows :]


def strip(ref, k, upper, lanes=slice(None)):
    if k not in STRIP:
        return jnp.zeros((HALO, ref[0:1, lanes].shape[1]), F32)
    start, rows = STRIP[k]
    values = ref[start : start + rows, lanes]
    blank = jnp.zeros((HALO - rows, values.shape[1]), F32)
    return jnp.concatenate([blank, values] if upper else [values, blank], axis=0)


def columns_kernel(
    has, left, right, left_wall, right_wall, left_flow, right_flow, above, below, to_right, to_left
):
    parts = left.shape[0]
    wide, flow_wide = above.shape[1], above.shape[1] // 2
    gap = jnp.zeros((LANES - 2 * HALO, LANES), F32)

    def tall(k, inner, first, sides):
        lanes = slice(first, first + LANES)
        over, under = strip(above, k, True, lanes), strip(below, k, False, lanes)
        return jnp.concatenate([inner, under * sides[1], gap, over * sides[0]], axis=0).T

    for k in range(parts + 1):
        at = slice(k * HALO, (k + 1) * HALO)
        if k < parts:
            near, far = left[k, 0].astype(F32), right[k, 0].astype(F32)
        else:
            near, far = 1.0 - left_wall[0].astype(F32), 1.0 - right_wall[0].astype(F32)
        sides = (has[2], has[3])
        to_left[at, :] = tall(k, near, 0, sides)[:HALO]
        to_right[at, :] = tall(k, far, wide - LANES, sides)[LANES - HALO :]
    k = parts + 1
    at = slice(k * HALO, (k + 1) * HALO)
    size = left_flow.shape[2] + LANES
    blank = jnp.zeros((HALO, to_left.shape[1] - size), F32)
    to_left[at, :size] = tall(k, left_flow[0, 0], 0, (1.0, 1.0))[:HALO]
    to_right[at, :size] = tall(k, right_flow[0, 0], flow_wide - LANES, (1.0, 1.0))[LANES - HALO :]
    to_left[at, size:] = blank
    to_right[at, size:] = blank


def sides_kernel(has, place, velocity, above, below, from_left, from_right, sides, squares, mark):
    parts, tall, _ = sides.shape
    gap = jnp.zeros((LANES - 2 * HALO, tall), F32)
    for k in range(parts):
        at = slice(k * HALO, (k + 1) * HALO)
        tile = [from_right[at, :] * has[1], gap, from_left[at, :] * has[0]]
        sides[k] = jnp.concatenate(tile, axis=0).T
    at = slice(parts * HALO, (parts + 1) * HALO)
    rows, local = velocity.shape[2:]
    size = rows + LANES
    tile = [from_right[at, :size], gap[:, :size], from_left[at, :size]]
    tile = jnp.concatenate(tile, axis=0).T
    tile = tile * tile
    mark[0] = place[0]
    over, under = (strip(ref, parts, ref is above, slice(0, local)) for ref in (above, below))
    squares[:HALO, :local] = over * over
    squares[HALO : HALO + rows, :local] = velocity[0, 0] * velocity[0, 0]
    squares[HALO + rows :, :local] = under * under
    squares[:HALO, local:] = tile[size - HALO :]
    squares[HALO : HALO + rows, local:] = tile[:rows]
    squares[HALO + rows :, local:] = tile[rows : rows + HALO]


def forward_x_kernel(place, *refs):
    *pieces, tables, turns, out, total, lines, made, sent = refs
    count, _, rows, local = lines.shape
    for mask, piece in enumerate(pieces):
        lines[place[0] ^ mask] = piece[...]
    base = turns.shape[1]
    per = local // base
    u = [lines[t // per, 0, :, (t % per) * base : (t % per + 1) * base] for t in range(RADIX)]
    v = [lines[t // per, 1, :, (t % per) * base : (t % per + 1) * base] for t in range(RADIX)]
    energy = sum(b * b for b in v)
    energy = jnp.sum(energy.reshape(rows // 8, 8, base), axis=0)
    total[...] = sum(energy[:, k : k + LANES] for k in range(0, base, LANES))
    fields = ([a * a - b * b for a, b in zip(u, v)], [2.0 * a * b for a, b in zip(u, v)])
    zeros, mids, reals, imags = [], [], [[], [], []], [[], [], []]
    for a in fields:
        s04, s26, s15, s37 = a[0] + a[4], a[2] + a[6], a[1] + a[5], a[3] + a[7]
        d04, d26, d15, d37 = a[0] - a[4], a[2] - a[6], a[1] - a[5], a[3] - a[7]
        zeros.append((s04 + s26) + (s15 + s37))
        mids.append((s04 + s26) - (s15 + s37))
        minus, plus = ROOT * (d15 - d37), ROOT * (d15 + d37)
        turned = (
            (d04 + minus, -d26 - plus),
            (s04 - s26, s37 - s15),
            (d04 - minus, d26 - plus),
        )
        for index, (real, imag) in enumerate(turned):
            c, s = turns[index : index + 1, :], turns[index + 3 : index + 4, :]
            reals[index].append(real * c + imag * s)
            imags[index].append(imag * c - real * s)
    stacked = jnp.concatenate(
        [
            jnp.concatenate([jnp.concatenate(reals[i], axis=0) for i in range(3)], axis=0),
            jnp.concatenate([jnp.concatenate(imags[i], axis=0) for i in range(3)], axis=0),
        ],
        axis=1,
    )
    full, zero, middle = x_parts(tables, base)
    full = exact_dot(split(stacked), full)
    zero = exact_dot(split(jnp.concatenate(zeros, axis=0)), zero)
    middle = exact_dot(split(jnp.concatenate(mids, axis=0)), middle)
    low = lane_index((rows, LANES)) % 64 < 32
    target, copies = 0, []
    blocks = [full[2 * rows * i : 2 * rows * (i + 1)] for i in range(3)] + [zero, middle]
    for block in blocks:
        start = target
        for first in range(0, block.shape[1], LANES):
            a = block[:rows, first : first + LANES]
            c = block[rows:, first : first + LANES]
            made[target] = jnp.where(low, a, spin(c, 32))
            made[target + 1] = jnp.where(low, spin(a, -32), c)
            target += 2
        group = pl.ds(start, target - start)
        copies.append(pltpu.make_async_copy(made.at[group], out.at[group], sent.at[len(copies)]))
        copies[-1].start()
    for copy in copies:
        copy.wait()


def eighths(x, turn):
    s04, s26, s15, s37 = x[0] + x[4], x[2] + x[6], x[1] + x[5], x[3] + x[7]
    d04, d26, d15, d37 = x[0] - x[4], x[2] - x[6], x[1] - x[5], x[3] - x[7]
    quarter = turn(s15 - s37)
    spun_26, spun_37 = turn(d26), turn(d37)
    one, three = d15 + spun_37, d15 - spun_37
    spun_one, spun_three = turn(one), turn(three)
    one = ROOT * (one + spun_one)
    three = ROOT * (spun_three - three)
    return [
        (s04 + s26) + (s15 + s37),
        (d04 + spun_26) + one,
        (s04 - s26) + quarter,
        (d04 - spun_26) + three,
        (s04 + s26) - (s15 + s37),
        (d04 + spun_26) - one,
        (s04 - s26) - quarter,
        (d04 - spun_26) - three,
    ]


def solve_y_kernel(count_x, _, lines, total, wave, both, turns, out, held, spread, made, sent):
    count, rows, _ = lines.shape
    base = turns.shape[0]
    length = count * rows
    block = count_x * rows
    per = base // rows
    lanes = lane_index((base, LANES))
    sign = jnp.where(lanes < 64, 1.0, -1.0).astype(F32)

    def minus_i(z):
        return spin(z, 64) * sign

    def plus_i(z):
        return spin(z, 64) * -sign

    fields = [
        jnp.concatenate([lines[t * per + k] for k in range(per)], axis=0) for t in range(RADIX)
    ]
    mixed = eighths(fields, minus_i)
    terms, columns = turns.shape[1], 2 * RADIX
    picked = lax.broadcasted_iota(jnp.int32, (terms, columns * LANES), 0) % columns
    lane = lane_index(picked.shape)
    value = jnp.where((lane >= RADIX * LANES) & (lane % LANES >= 64), -1.0, 1.0)
    spread[...] = dot(turns[...], jnp.where(picked == lane // LANES, value, 0.0).astype(BF16))
    cosines = [spread[:, r * LANES : (r + 1) * LANES] for r in range(RADIX)]
    sines = [spread[:, (r + RADIX) * LANES : (r + RADIX + 1) * LANES] for r in range(RADIX)]
    mixed = [mixed[0]] + [
        mixed[r] * cosines[r] + spin(mixed[r], 64) * sines[r] for r in range(1, RADIX)
    ]
    tables = (both[: 2 * base], both[2 * base :])
    product = exact_dot(tables, split(jnp.concatenate(mixed, axis=1)))
    kx = wave[0:1, :]
    first = lanes % 64 < 32
    edge = jnp.float32(length // 2)
    alone = jnp.where(first, kx * kx, 0.0)
    slope = jnp.where(first | (kx == -edge), 0.0, jnp.broadcast_to(kx, lanes.shape))
    q = lax.broadcasted_iota(jnp.int32, lanes.shape, 0)
    low_ky = RADIX * (q - jnp.where(q < base // 2, 0, base)).astype(F32)
    terms = []
    for r in range(RADIX):
        at = slice(r * LANES, (r + 1) * LANES)
        spectrum = product[:base, at] + minus_i(product[base:, at])
        ky = low_ky + float(r)
        symbol = alone + slope * ky
        if r == 0:
            corner = jnp.where((kx == -edge) & ~first, edge * edge, 0.0)
            symbol = jnp.where(ky == -edge, jnp.where(first, alone, corner), symbol)
        terms.append(symbol * pl.reciprocal(kx * kx + ky * ky) * spectrum)
    pairs = [
        jnp.where(first, low + spin(low, -32), high + spin(high, 32))
        for low, high in zip(terms[:4], terms[4:])
    ]
    product = exact_dot(tables, split(jnp.concatenate(pairs, axis=1)))
    mixed = []
    for r in range(RADIX // 2):
        at = slice(r * LANES, (r + 1) * LANES)
        value = product[:base, at] + plus_i(product[base:, at])
        cosine = jnp.where(first, cosines[r], cosines[r + 4])
        sine = jnp.where(first, sines[r], sines[r + 4])
        value = value * cosine - spin(value, 64) * sine
        value = jnp.where(first, value + spin(value, -32), spin(value, 32) - value)
        if r == 2:
            value = jnp.where(first, value, plus_i(value))
        elif r:
            turned = plus_i(value)
            odd = value + turned if r == 1 else turned - value
            value = jnp.where(first, value, ROOT * odd)
        mixed.append(value)
    even, odd = mixed[0] + mixed[2], mixed[0] - mixed[2]
    side, turned = mixed[1] + mixed[3], plus_i(mixed[1] - mixed[3])
    for t, values in enumerate((even + side, odd + turned, even - side, odd - turned)):
        start = MARGIN + 2 * t * base
        held[start : start + base, :] = values
        held[start + base : start + 2 * base, :] = spin(values, -32)
    held[0:MARGIN, :] = held[length : length + MARGIN, :]
    held[length + MARGIN : length + 2 * MARGIN, :] = held[MARGIN : 2 * MARGIN, :]
    spare = total[...] + spin(total[...], 32)
    kept = rows + 2 * MARGIN // count_x
    half = made.shape[1]
    rest = kept - half
    low = lane_index((8, LANES)) % 64 < 32
    copies = []
    for target in range(count):
        start = (target // count_x) * block + (target % count_x) * kept
        for row in range(0, half, 8):
            a = held[start + row : start + row + 8, :]
            if row < rest:
                b = spin(held[start + half + row : start + half + row + 8, :], 32)
            else:
                b = spare
            made[target, row : row + 8, :] = jnp.where(low, a, b)
        if (target + 1) % RADIX == 0:
            group = pl.ds(target + 1 - RADIX, RADIX)
            copies.append(pltpu.make_async_copy(made.at[group], out.at[group], sent.at[len(copies)]))
            copies[-1].start()
    for copy in copies:
        copy.wait()


def inverse_x_kernel(
    kept, scale, place, lines, tables, turns, *refs
):
    *outs, held = refs
    count, half, _ = lines.shape
    base = turns.shape[1]
    length = RADIX * base
    rest = kept - half
    low = lane_index((half, LANES)) % 64 < 32
    groups, spare = [], None
    for first in range(0, count, 2):
        even, odd = lines[first], lines[first + 1]
        a = jnp.where(low, even, spin(odd, 32))
        b = jnp.where(low, spin(even, -32), odd)
        groups.append(jnp.concatenate([a, b[:rest]], axis=0))
        extra = b[rest : rest + 8]
        spare = extra if spare is None else spare + extra
    mean = jnp.sum(spare) * scale
    wide = 2 * base // LANES
    narrow = base // LANES
    stacked = jnp.concatenate(
        [jnp.concatenate(groups[i * wide : (i + 1) * wide], axis=1) for i in range(3)], axis=0
    )
    at = 3 * wide
    zeros = jnp.concatenate(groups[at : at + narrow], axis=1)
    mids = jnp.concatenate(groups[at + narrow : at + 2 * narrow], axis=1)
    full, zero, middle = x_parts(tables, base)
    full = exact_dot(split(stacked), full)
    zero = exact_dot(split(zeros), zero) * scale
    mid = exact_dot(split(mids), middle) * scale
    turned = []
    for i in range(3):
        real = full[i * kept : (i + 1) * kept, :base]
        imag = full[i * kept : (i + 1) * kept, base:]
        c = turns[i : i + 1, :] * (2.0 * scale)
        s = turns[i + 3 : i + 4, :] * (2.0 * scale)
        turned.append((real * c - imag * s, real * s + imag * c))
    for t in range(RADIX):
        value = zero + mid if t % 2 == 0 else zero - mid
        for i, (real, imag) in enumerate(turned):
            eighth = t * (i + 1) % RADIX
            c = (1.0, ROOT, 0.0, -ROOT, -1.0, -ROOT, 0.0, ROOT)[eighth]
            s = (0.0, ROOT, 1.0, ROOT, 0.0, -ROOT, -1.0, -ROOT)[eighth]
            if c:
                value = value + c * real
            if s:
                value = value - s * imag
        held[:, t * base : (t + 1) * base] = mean - value
    targets, local = len(outs), outs[0].shape[1] - LANES
    right = lane_index((kept, LANES)) < 64
    for mask, out in enumerate(outs):
        start = pl.multiple_of((place[0] ^ mask) * local, LANES)
        after = pl.multiple_of(jnp.where(start + local == length, 0, start + local), LANES)
        before = pl.multiple_of(jnp.where(start == 0, length, start) - LANES, LANES)
        out[:, :local] = held[:, pl.ds(start, local)]
        out[:, local:] = jnp.where(
            right, held[:, pl.ds(after, LANES)], held[:, pl.ds(before, LANES)]
        )


def slopes_x(parts, band, with_edge):
    tiles = parts[0].shape[-1] // LANES
    pieces = []
    for first in list(range(0, tiles - 1, 2)) + ([tiles - 1] if with_edge else []):
        steps = (-1, 0, 1, 2) if first < tiles - 1 else (-1, 0, 1)
        table = band[...] if first < tiles - 1 else band[: 3 * LANES, :LANES]
        order = [(first + step) % tiles for step in steps]
        piece = None
        for part in parts:
            term = dot(jnp.concatenate([lane_tile(part, t) for t in order], axis=1), table)
            piece = term if piece is None else piece + term
        pieces.append(piece)
    return jnp.concatenate(pieces, axis=1)


def slope_y(read):
    value = read(3) - read(-3)
    for index in (0, 1):
        value = value + whole_weights[index] * (read(index + 1) - read(-index - 1))
    return value


def edged(k, side, center, up, down, above, below, sides, has, first=0):
    step = pl.program_id(0) + first
    tile, width = center.shape
    tall = sides.shape[1]
    last = (tall - LANES) // tile - 1
    base = pl.multiple_of(step * tile, 8)
    before = pl.multiple_of(jnp.where(step == 0, tall, base) - HALO, 8)
    over = jnp.where(step == 0, strip(above, k, True) * has[2], up)
    under = jnp.where(step == last, strip(below, k, False) * has[3], down)
    rows = (
        (over, sides[side, pl.ds(before, HALO), :]),
        (center, sides[side, pl.ds(base, tile), :]),
        (under, sides[side, pl.ds(pl.multiple_of(base + tile, 8), HALO), :]),
    )
    return jnp.concatenate([jnp.concatenate(pair, axis=1) for pair in rows], axis=0)


def edged_open(k, side, wall, wall_up, wall_down, above, below, sides, has, first=0):
    open_cells = [1.0 - ref[0].astype(F32) for ref in (wall, wall_up, wall_down)]
    return edged(k, side, *open_cells, above, below, sides, has, first)


def quiet_step_kernel(
    first, has, place, center, up, down, wall, wall_up, wall_down, above, below, sides, across, along, along_inner, calm, density, shown_open, mark
):
    parts, _, tile, width = center.shape
    high = tile + 2 * HALO
    opened = edged_open(parts, parts, wall, wall_up, wall_down, above, below, sides, has, first)
    values = []
    for k in range(parts):
        value = edged(
            k,
            k,
            center[k, 0].astype(F32),
            up[k, 0].astype(F32)[up.shape[2] - HALO :],
            down[k, 0].astype(F32)[:HALO],
            above,
            below,
            sides,
            has,
            first,
        )
        values.append(value)

    def drops(x, along_b, along_p):
        diverge = x[1] + along_b
        return (
            diverge + mean_flow * x[0],
            x[3] + mean_flow * x[1],
            along_p + mean_flow * x[2],
            diverge + mean_flow * x[3],
        )

    short = [value.astype(BF16) for value in values]
    x = slopes_x((jnp.concatenate(short, axis=0),), across, True)
    x = [x[k * high : (k + 1) * high] for k in range(parts)]
    table = along[...]
    dropped = drops(x, dot(table, short[2]), dot(table, short[3]))
    middle = [opened * (v - (time_step / 60.0) * d) for v, d in zip(values, dropped)]
    inner = slice(HALO, HALO + tile)
    x = slopes_x(split(jnp.concatenate([value[inner] for value in middle], axis=0)), across, False)
    x = [x[k * tile : (k + 1) * tile] for k in range(parts)]
    table = along_inner[...]
    y = [sum(dot(table, part) for part in split(middle[k][:, :width])) for k in (2, 3)]
    dropped = drops(x, *y)
    shown = opened[inner, :width]
    for k in range(parts):
        start = 0.5 * values[k][inner, :width] - (0.5 * time_step / 60.0) * dropped[k]
        value = shown * start + 0.5 * middle[k][inner, :width]
        if k == 0:
            density[0, 0] = value.astype(BF16)
        else:
            calm[k - 1] = value
    shown_open[0] = opened.astype(BF16)
    mark[0] = place[0]


def tables_kernel(place, weights_x, weights_y, rise_x, rise_y, mark):
    mark[0] = place[0]
    tiles, reach_x, lanes = rise_x.shape
    wide, length_x = (tiles - 1) * lanes, weights_x.shape[1]
    first = place[0] * wide
    half = LANES // 2

    def weights(ref, start, size):
        length = ref.shape[1]
        start = jnp.where(start < 0, start + length, jnp.where(start >= length, start - length, start))
        return ref[:, pl.ds(pl.multiple_of(start, LANES), size)]

    cells = lax.broadcasted_iota(jnp.int32, (reach_x, lanes), 0)
    fine = lax.broadcasted_iota(jnp.int32, (reach_x, lanes), 1)
    right, left = weights(weights_x, first + wide, LANES), weights(weights_x, first - LANES, LANES)
    edge = jnp.where(lane_index(right.shape) < half, right, left)
    edge = jnp.concatenate([edge, edge], axis=1)
    for k in range(tiles):
        own = weights(weights_x, first + k * lanes, lanes) if k < tiles - 1 else edge
        target = fine // 2 - 1
        if k == tiles - 1:
            target = jnp.where(fine < half, target, target + half)
        value = jnp.zeros(fine.shape, F32)
        for t in range(4):
            value = jnp.where(cells == (target + t) % reach_x, own[t : t + 1, :], value)
        rise_x[k] = value
    steps, high, reach = rise_y.shape
    tall = steps * TILE
    first = place[1] * tall
    own = [weights(weights_y, first + k * LANES, LANES) for k in range(-1, tall // LANES + 1)]
    own = jnp.concatenate([jnp.concatenate(own, axis=1), jnp.zeros((4, tall + 2 * LANES), F32)], axis=0).T
    cells = lax.broadcasted_iota(jnp.int32, (high, reach), 1) % (reach // 3)
    target = lax.broadcasted_iota(jnp.int32, (high, reach), 0) // 2 + (HALO // 2 - 1)
    for k in range(steps):
        start = LANES - HALO + k * TILE
        value = jnp.zeros((high, reach), F32)
        for t in range(4):
            value = jnp.where(cells == target + t, own[start : start + high, t : t + 1], value)
        rise_y[k] = value


def source_kernel(place, squares, opened, rise_x, rise_y, quiet, across, _, *refs):
    *lines, out, squared, cells_open, matrix, rows_matrix, calm, band, held, raised, forced, done, fetched, kept = refs
    steps = done.shape[0]
    tile, width = calm.shape[2:]
    high = tile + 2 * HALO
    rows = lines[0].shape[0]

    def tile_copies(k):
        part = quiet.at[:, pl.ds(k * tile, tile), :]
        return (
            pltpu.make_async_copy(part, calm.at[k % 2], fetched.at[k % 2]),
            pltpu.make_async_copy(opened.at[k], cells_open.at[k % 2], fetched.at[2 + k % 2]),
        )

    def done_copy(k):
        part = out.at[1:, 0, pl.ds(k * tile, tile), :]
        return pltpu.make_async_copy(done.at[k], part, kept.at[k])

    arrays = ((squares, squared), (rise_x, matrix), (rise_y, rows_matrix), (across, band))
    copies = [
        pltpu.make_async_copy(source, target, fetched.at[4 + k])
        for k, (source, target) in enumerate(arrays)
    ]
    pieces = [
        pltpu.make_async_copy(
            piece,
            held.at[pl.ds(pl.multiple_of((place[0] ^ mask) * rows, 8), rows), :],
            fetched.at[4 + len(arrays) + mask],
        )
        for mask, piece in enumerate(lines)
    ]
    for copy in pieces + copies[:2]:
        copy.start()
    for copy in pieces + copies[:1]:
        copy.wait()

    level = held[MARGIN - HALO : MARGIN - HALO + squared.shape[0], :] - squared[...]
    count = level.shape[1] // LANES
    near = lane_index((level.shape[0], LANES)) < 64
    around = []
    for k in range(count):
        after, before = lane_tile(level, (k + 1) % count), lane_tile(level, (k - 1) % count)
        around.append(split(jnp.concatenate([lane_tile(level, k), jnp.where(near, after, before)], axis=1)))
    copies[1].wait()
    for copy in (copies[2], *tile_copies(0), copies[3], *tile_copies(1)):
        copy.start()
    for k in range(count):
        lanes = 2 * LANES if k < count - 1 else LANES
        value = split(exact_dot(around[k], split(matrix[k][:, :lanes])))
        for part in range(2):
            raised[part, :, 2 * k * LANES : 2 * k * LANES + lanes] = value[part]
    for copy in copies[2:]:
        copy.wait()

    reach = rows_matrix.shape[2] // 3
    third = lane_index((high, 3 * reach)) >= 2 * reach
    for k in range(steps):
        start = k * (tile // 2)
        window = [raised[part, start : start + reach, :] for part in (0, 1, 0)]
        weights = split(rows_matrix[k])
        weights = jnp.where(third, weights[1], weights[0])
        calm_here, open_here = tile_copies(k)
        open_here.wait()
        free = time_step * cells_open[k % 2].astype(F32)
        value = free * dot(weights, jnp.concatenate(window, axis=0))
        forced[k % 2] = value
        inner = value[HALO : HALO + tile]
        shown = (0.5 / 60.0) * free[HALO : HALO + tile, :width]
        x = shown * slopes_x(split(inner), band, False)
        y = shown * slope_y(lambda d: forced[k % 2, HALO + d : HALO + d + tile, :width])
        calm_here.wait()
        still = calm.at[k % 2]
        done[k, 0] = (still[0] - x).astype(BF16)
        done[k, 1] = (still[1] - y).astype(BF16)
        done[k, 2] = (still[2] + inner[:, :width] - mean_flow * x).astype(BF16)
        done_copy(k).start()
        if k + 2 < steps:
            for copy in tile_copies(k + 2):
                copy.start()
    for k in range(steps):
        done_copy(k).wait()


def call(
    kernel, operands, outs, scratch=(), steps=0, specs=None, out_specs=None, after=(), aliases=None, megabytes=24, flops=0, moved=0, name=None
):
    count = len(operands)

    def body(*refs):
        kernel(*refs[:count], *refs[count + len(after) :])

    def whole(array):
        zeros = (0,) * len(array.shape)
        return pl.BlockSpec(array.shape, lambda *_: zeros)

    arguments = {}
    chosen = specs or {}
    if steps:
        arguments["grid"] = (steps,)
        in_specs = [chosen.get(i, whole(o)) for i, o in enumerate(operands)]
        arguments["out_specs"] = jax.tree.map(whole, outs) if out_specs is None else out_specs
    else:
        local = pl.BlockSpec(memory_space=pltpu.VMEM)
        in_specs = [chosen.get(i, local) for i in range(count)]
        if out_specs is not None:
            arguments["out_specs"] = out_specs
    return pl.pallas_call(
        body,
        out_shape=outs,
        in_specs=in_specs + [pl.BlockSpec(memory_space=pl.ANY)] * len(after),
        scratch_shapes=list(scratch),
        input_output_aliases=aliases or {},
        compiler_params=pltpu.CompilerParams(vmem_limit_bytes=megabytes << 20),
        cost_estimate=pl.CostEstimate(flops=flops, bytes_accessed=moved, transcendentals=0),
        name=name,
        **arguments,
    )(*operands, *after)


def ring(array, axis, step):
    size = lax.axis_size(axis)
    return lax.ppermute(array, axis, [(i, (i + step) % size) for i in range(size)])


def swap(array, axis, mask):
    return lax.ppermute(array, axis, [(i, i ^ mask) for i in range(lax.axis_size(axis))])


def shaped(*shape, kind=F32):
    return jax.ShapeDtypeStruct(shape, kind)


def pressure_lines(pieces, place_x, gathered, spread, stepped):
    _, rows, local_x = pieces[0].shape
    count_x, count_y = lax.axis_size("gx"), lax.axis_size("gy")
    count = count_x * count_y
    scalars = {0: pl.BlockSpec(memory_space=pltpu.SMEM)}
    length_x, length_y = local_x * count_x, rows * count
    full, zero, middle, cos_turn, sin_turn = x_tables(length_x)
    turns = np.zeros((8, cos_turn.shape[1]), np.float32)
    turns[0:3], turns[3:6] = cos_turn, sin_turn
    spectra, total = call(
        forward_x_kernel,
        (place_x, *pieces, np.concatenate([beside(full), beside(zero, middle)]), turns),
        (shaped(count, rows, LANES), shaped(8, LANES)),
        (
            pltpu.VMEM((count_x, 2, rows, local_x), F32),
            pltpu.VMEM((count, rows, LANES), F32),
            pltpu.SemaphoreType.DMA((5,)),
        ),
        specs=scalars,
        out_specs=(pl.BlockSpec(memory_space=pl.ANY), pl.BlockSpec(memory_space=pltpu.VMEM)),
        after=gathered,
        flops=10**9,
        moved=4 << 20,
        name="forward_x",
    )
    spectra = lax.all_to_all(spectra, ("gy", "gx"), 0, 0, tiled=True)
    place = lax.axis_index("gy") * count_x + lax.axis_index("gx")
    waves = jnp.asarray(wave_table(length_x, count))
    wave = lax.dynamic_slice(waves, (place, 0), (1, LANES))
    both, turns_y = y_tables(length_y)
    kept = rows + 2 * MARGIN // count_x
    half = (kept // 2 + 8) // 8 * 8
    solved = call(
        functools.partial(solve_y_kernel, count_x),
        (spread, spectra, total, wave, beside(both), turns_y),
        shaped(count, half, LANES),
        (
            pltpu.VMEM((length_y + 2 * MARGIN, LANES), F32),
            pltpu.VMEM((length_y // RADIX, 2 * RADIX * LANES), F32),
            pltpu.VMEM((count, half, LANES), F32),
            pltpu.SemaphoreType.DMA((count // RADIX,)),
        ),
        specs=scalars,
        out_specs=pl.BlockSpec(memory_space=pl.ANY),
        flops=4 * 10**9,
        moved=6 << 20,
        name="solve_y",
    )
    solved = lax.all_to_all(solved, ("gy", "gx"), 0, 0, tiled=True)
    back = 2.0 * zero.T
    back[LANES // 2] *= 0.5
    tables = np.concatenate(
        [beside(full.T), beside(back, 2.0 * middle.T)]
    )
    pressed = call(
        functools.partial(inverse_x_kernel, kept, 1.0 / (length_x * length_y)),
        (stepped, solved, tables, turns),
        (shaped(kept, local_x + LANES),) * count_x,
        (pltpu.VMEM((kept, length_x), F32),),
        specs=scalars,
        flops=10**9,
        moved=4 << 20,
        name="inverse_x",
    )
    return [piece if mask == 0 else swap(piece, "gx", mask) for mask, piece in enumerate(pressed)]


def fast_shards(velocity, weights_x, weights_y, acoustic, wall_mask):
    parts, _, tall, wide = acoustic.shape
    _, _, local_y, local_x = velocity.shape
    count_x, count_y = lax.axis_size("gx"), lax.axis_size("gy")
    place_x, place_y = lax.axis_index("gx"), lax.axis_index("gy")
    full, high, steps = wide + LANES, TILE + 2 * HALO, tall // TILE
    strips = (parts + 2) * HALO
    small = 2 * HALO
    has = jnp.stack([place_x > 0, place_x < count_x - 1, place_y > 0, place_y < count_y - 1])
    has = has.astype(F32)
    scalars = pl.BlockSpec(memory_space=pltpu.SMEM)

    def at(block, *index):
        return pl.BlockSpec(block, lambda i: index)

    own = place_x.astype(jnp.int32).reshape(1)
    first, last, cut = call(
        rows_kernel,
        (own, acoustic, acoustic, wall_mask, wall_mask, velocity, velocity),
        (shaped(STRIP_ROWS, wide),) * 2 + (shaped(1, kind=jnp.int32),),
        steps=1,
        specs={
            0: scalars,
            1: at((parts, 1, small, wide), 0, 0, 0, 0),
            2: at((parts, 1, small, wide), 0, 0, tall // small - 1, 0),
            3: at((1, HALO, wide), 0, 0, 0),
            4: at((1, HALO, wide), 0, tall // HALO - 1, 0),
            5: at((1, 1, HALO, local_x), 1, 0, 0, 0),
            6: at((1, 1, HALO, local_x), 1, 0, local_y // HALO - 1, 0),
        },
        out_specs=(at((STRIP_ROWS, wide), 0, 0),) * 2 + (scalars,),
        moved=2 << 20,
        megabytes=54,
        name="rows",
    )
    sent = call(
        pieces_kernel,
        (cut, velocity),
        (shaped(2, local_y // count_x, local_x),) * count_x,
        specs={0: scalars},
        moved=2 << 20,
        megabytes=8,
        name="pieces",
    )
    moved = [piece if mask == 0 else swap(piece, "gx", mask) for mask, piece in enumerate(sent)]
    above, below = ring(last, "gy", 1), ring(first, "gy", -1)
    to_right, to_left = call(
        columns_kernel,
        (has, acoustic, acoustic, wall_mask, wall_mask, velocity, velocity, above, below),
        (shaped(strips, tall + LANES), shaped(strips, tall + LANES)),
        steps=1,
        specs={
            0: scalars,
            1: at((parts, 1, tall, LANES), 0, 0, 0, 0),
            2: at((parts, 1, tall, LANES), 0, 0, 0, wide // LANES - 1),
            3: at((1, tall, LANES), 0, 0, 0),
            4: at((1, tall, LANES), 0, 0, wide // LANES - 1),
            5: at((1, 1, local_y, LANES), 1, 0, 0, 0),
            6: at((1, 1, local_y, LANES), 1, 0, 0, local_x // LANES - 1),
        },
        moved=8 << 20,
        megabytes=54,
        name="columns",
    )
    from_left, from_right = ring(to_right, "gx", 1), ring(to_left, "gx", -1)
    local_memory = pl.BlockSpec(memory_space=pltpu.VMEM)
    tiles = wide // (2 * LANES) + 1
    rise_x, rise_y, listed = call(
        tables_kernel,
        (jnp.stack([place_x, place_y]).astype(jnp.int32), weights_x, weights_y),
        (
            shaped(tiles, 2 * LANES, 2 * LANES),
            shaped(steps, high, 3 * (high // 2 + HALO)),
            shaped(1, kind=jnp.int32),
        ),
        specs={0: scalars},
        out_specs=(local_memory, local_memory, scalars),
        moved=4 << 20,
        megabytes=54,
        name="tables",
    )
    sides, squares, beside = call(
        sides_kernel,
        (has, listed, velocity, above, below, from_left, from_right),
        (
            shaped(parts + 1, tall + LANES, LANES),
            shaped(local_y + 2 * HALO, local_x + LANES),
            shaped(1, kind=jnp.int32),
        ),
        steps=1,
        specs={0: scalars, 1: scalars, 2: at((1, 1, local_y, local_x), 1, 0, 0, 0)},
        out_specs=(
            at((parts + 1, tall + LANES, LANES), 0, 0, 0),
            at((local_y + 2 * HALO, local_x + LANES), 0, 0),
            scalars,
        ),
        moved=8 << 20,
        megabytes=54,
        name="sides",
    )
    across, along = band_tables(high)
    along_inner = along[HALO : HALO + TILE]
    per, rows = TILE // small, TILE // HALO

    def tiled(first):
        walls = (
            pl.BlockSpec((1, TILE, wide), lambda i: (0, i + first, 0)),
            pl.BlockSpec((1, HALO, wide), lambda i: (0, jnp.maximum((i + first) * rows - 1, 0), 0)),
            pl.BlockSpec(
                (1, HALO, wide),
                lambda i: (0, jnp.minimum((i + first + 1) * rows, steps * rows - 1), 0),
            ),
        )
        cells = (
            pl.BlockSpec((parts, 1, TILE, wide), lambda i: (0, 0, i + first, 0)),
            pl.BlockSpec(
                (parts, 1, small, wide), lambda i: (0, 0, jnp.maximum((i + first) * per - 1, 0), 0)
            ),
            pl.BlockSpec(
                (parts, 1, small, wide),
                lambda i: (0, 0, jnp.minimum((i + first + 1) * per, steps * per - 1), 0),
            ),
        )
        return cells, walls

    def quiet_tiles(first, count, before):
        cells, walls = tiled(first)
        operands = (has, own, acoustic, acoustic, acoustic, wall_mask, wall_mask, wall_mask, above, below, sides)
        operands = operands + (across, along, along_inner)
        return call(
            functools.partial(quiet_step_kernel, first),
            operands,
            (
                shaped(parts - 1, tall, wide),
                shaped(*acoustic.shape, kind=BF16),
                shaped(steps, high, full, kind=BF16),
                shaped(1, kind=jnp.int32),
            ),
            steps=count,
            specs=dict(enumerate((scalars, scalars) + cells + walls)),
            out_specs=(
                pl.BlockSpec((parts - 1, TILE, wide), lambda i: (0, i + first, 0)),
                pl.BlockSpec((1, 1, TILE, wide), lambda i: (0, 0, i + first, 0)),
                pl.BlockSpec((1, high, full), lambda i: (i + first, 0, 0)),
                scalars,
            ),
            after=before,
            aliases={len(operands) + k: k for k in range(len(before))},
            megabytes=54 if first == 0 else 53,
            flops=3 * 10**9 * count,
            moved=(12 << 20) * count,
            name="quiet_step",
        )

    early = max(steps * 3 // 4, 1)
    *begun, stepped = quiet_tiles(0, early, ())
    if early < steps:
        *begun, _ = quiet_tiles(early, steps - early, begun)
    quiet, final, opened = begun
    lines = pressure_lines(moved, own, (above, below), beside, stepped)
    operands = (own, squares, opened, rise_x, rise_y, quiet, across, final, *lines)
    anywhere = pl.BlockSpec(memory_space=pl.ANY)
    specs = {k: anywhere for k in range(1, len(operands))}
    scratch = (
        pltpu.VMEM(squares.shape, F32),
        pltpu.VMEM((2,) + opened.shape[1:], BF16),
        pltpu.VMEM(rise_x.shape, F32),
        pltpu.VMEM(rise_y.shape, F32),
        pltpu.VMEM((2, parts - 1, TILE, wide), F32),
        pltpu.VMEM(across.shape, BF16),
        pltpu.VMEM((local_y + 2 * MARGIN, local_x + LANES), F32),
        pltpu.VMEM((2, local_y + 2 * HALO, full), BF16),
        pltpu.VMEM((2, high, full), F32),
        pltpu.VMEM((steps, parts - 1, TILE, wide), BF16),
        pltpu.SemaphoreType.DMA((8 + count_x,)),
        pltpu.SemaphoreType.DMA((steps,)),
    )
    return call(
        source_kernel,
        operands,
        shaped(*acoustic.shape, kind=BF16),
        scratch,
        specs={0: scalars, **specs},
        out_specs=anywhere,
        aliases={7: 0},
        megabytes=55,
        flops=4 * 10**9,
        moved=16 << 20,
        name="source_step",
    )


def fits(count_x, count_y, velocity, acoustic):
    _, planes, local_y, local_x = velocity
    _, _, tall, wide = acoustic
    length_x, length_y = local_x * count_x, local_y * count_y
    rows = local_y // count_x
    base_x, base_y = length_x // RADIX, length_y // RADIX
    return (
        planes == 1
        and acoustic[0] == PARTS
        and length_x * 2 == count_x * count_y * LANES
        and base_x % (2 * LANES) == 0
        and local_x % base_x == 0
        and rows % 8 == 0
        and base_y % rows == 0
        and base_y % 8 == 0
        and count_x * count_y % RADIX == 0
        and MARGIN * 2 % (8 * count_x) == 0
        and tall == 2 * local_y
        and wide == 2 * local_x
        and tall % TILE == 0
        and tall % LANES == 0
        and tall >= 2 * TILE
        and count_x & (count_x - 1) == 0
        and wide % (2 * LANES) == 0
    )


def extended(array, sides, width):
    for axis, dim in sides:
        size, length = (lax.axis_size(axis), array.shape[dim])
        up = [(i, (i + 1) % size) for i in range(size - 1)]
        down = [(j, i) for i, j in up]
        last = lax.slice_in_dim(array, length - width, length, axis=dim)
        leading = lax.slice_in_dim(array, 0, width, axis=dim)
        before = lax.ppermute(last, axis, up)
        after = lax.ppermute(leading, axis, down)
        array = jnp.concatenate([before, array, after], axis=dim)
    return array


def gradients(padded):
    height = padded.shape[-2] - 6
    breadth = padded.shape[-1] - 6
    rows_mid = padded[..., 3 : 3 + height, :]
    cols_mid = padded[..., :, 3 : 3 + breadth]
    along_x = jnp.zeros_like(padded[..., 3 : 3 + height, 3 : 3 + breadth])
    along_y = jnp.zeros_like(along_x)
    for index, weight in enumerate(stencil_weights):
        distance = index + 1
        along_x = along_x + weight * (
            rows_mid[..., 3 + distance : 3 + distance + breadth]
            - rows_mid[..., 3 - distance : 3 - distance + breadth]
        )
        along_y = along_y + weight * (
            cols_mid[..., 3 + distance : 3 + distance + height, :]
            - cols_mid[..., 3 - distance : 3 - distance + height, :]
        )
    return (along_x, along_y)


def tendency(padded, source):
    along_x, along_y = gradients(padded)
    diverge = along_x[1] + along_y[2]
    forcing = jnp.stack([-diverge, -along_x[3], -along_y[3], source - diverge])
    return forcing - mean_flow * along_x


def spectral_index(flat, length):
    second = length // 16
    wave = flat // second + 16 * (flat % second)
    return jnp.where(wave < length // 2, wave, wave - length).astype(jnp.float32)


def twiddles(rows_count, cols_count, modulus, sign):
    products = jnp.arange(rows_count)[:, None] * jnp.arange(cols_count)[None, :] % modulus
    angles = 2.0 * math.pi / modulus * products.astype(jnp.float32)
    return (jnp.cos(angles), sign * jnp.sin(angles))


def mix_rows(real_part, imag_part, cosine, sine):
    exact = lax.Precision.HIGHEST
    cos_real = jnp.einsum("ka,...ab->...kb", cosine, real_part, precision=exact)
    cos_imag = jnp.einsum("ka,...ab->...kb", cosine, imag_part, precision=exact)
    sin_real = jnp.einsum("ka,...ab->...kb", sine, real_part, precision=exact)
    sin_imag = jnp.einsum("ka,...ab->...kb", sine, imag_part, precision=exact)
    return (cos_real - sin_imag, cos_imag + sin_real)


def mix_cols(real_part, imag_part, cosine, sine):
    exact = lax.Precision.HIGHEST
    cos_real = jnp.einsum("...kb,bc->...kc", real_part, cosine, precision=exact)
    cos_imag = jnp.einsum("...kb,bc->...kc", imag_part, cosine, precision=exact)
    sin_real = jnp.einsum("...kb,bc->...kc", real_part, sine, precision=exact)
    sin_imag = jnp.einsum("...kb,bc->...kc", imag_part, sine, precision=exact)
    return (cos_real - sin_imag, cos_imag + sin_real)


def rotate(real_part, imag_part, cosine, sine):
    return (real_part * cosine - imag_part * sine, real_part * sine + imag_part * cosine)


def discrete(real_part, imag_part, sign):
    length = real_part.shape[-1]
    second = length // 16
    initial = real_part.shape
    folded = initial[:-1] + (16, second)
    real_part = real_part.reshape(folded)
    imag_part = imag_part.reshape(folded)
    small_cos, small_sin = twiddles(16, 16, 16, sign)
    large_cos, large_sin = twiddles(second, second, second, sign)
    turn_cos, turn_sin = twiddles(16, second, length, sign)
    if sign < 0:
        real_part, imag_part = mix_rows(real_part, imag_part, small_cos, small_sin)
        real_part, imag_part = rotate(real_part, imag_part, turn_cos, turn_sin)
        real_part, imag_part = mix_cols(real_part, imag_part, large_cos, large_sin)
    else:
        real_part, imag_part = mix_cols(real_part, imag_part, large_cos, large_sin)
        real_part, imag_part = rotate(real_part, imag_part, turn_cos, turn_sin)
        real_part, imag_part = mix_rows(real_part, imag_part, small_cos, small_sin)
        real_part = real_part / length
        imag_part = imag_part / length
    return (real_part.reshape(initial), imag_part.reshape(initial))


def transform(stacked, sign, kind):
    if kind == "real_in":
        real_part = stacked
        imag_part = jnp.zeros_like(stacked)
    else:
        half = stacked.shape[0] // 2
        real_part = stacked[:half]
        imag_part = stacked[half:]
    real_out, imag_out = discrete(real_part, imag_part, sign)
    if kind == "real_out":
        return real_out
    return jnp.concatenate([real_out, imag_out], axis=0)


def project(stacked, wave_x, wave_y):
    coef_xx = wave_x * wave_x
    coef_xy = 2.0 * wave_x * wave_y
    coef_yy = wave_y * wave_y
    denominator = wave_x * wave_x + wave_y * wave_y
    positive = denominator > 0
    safe = jnp.where(positive, denominator, 1.0)

    def combine(parts):
        numerator = -(coef_xx * parts[0] + coef_xy * parts[1] + coef_yy * parts[2])
        return jnp.where(positive, numerator / safe, 0.0)

    return jnp.stack([combine(stacked[:3]), combine(stacked[3:])])


def refine(stacked, weights):
    result = jnp.zeros(stacked.shape[:-1] + (2 * stacked.shape[-1],), jnp.float32)
    for offset in range(4):
        result = (
            result
            + jnp.repeat(jnp.roll(stacked, 1 - offset, axis=-1), 2, axis=-1) * weights[offset]
        )
    return result


def lines_x(stacked, action):
    gathered = action(lax.all_to_all(stacked, "gx", split_axis=2, concat_axis=3, tiled=True))
    return lax.all_to_all(gathered, "gx", split_axis=3, concat_axis=2, tiled=True)


def lines_y(stacked, action):
    turned = jnp.swapaxes(stacked, 2, 3)
    gathered = action(lax.all_to_all(turned, "gy", split_axis=2, concat_axis=3, tiled=True))
    returned = lax.all_to_all(gathered, "gy", split_axis=3, concat_axis=2, tiled=True)
    return jnp.swapaxes(returned, 2, 3)


def expand(fields):
    return extended(fields, (("gx", 3), ("gy", 2)), 3)


def shards(velocity, weights_x, weights_y, acoustic, wall_mask):
    acoustic = acoustic.astype(jnp.float32)
    flow_x = velocity[0]
    flow_y = velocity[1]
    tensor = jnp.stack([flow_x * flow_x, flow_x * flow_y, flow_y * flow_y])
    count_gx = lax.axis_size("gx")
    count_gy = lax.axis_size("gy")
    place_x = lax.axis_index("gx")
    place_y = lax.axis_index("gy")
    local_y = tensor.shape[2]
    local_x = tensor.shape[3]
    length_x = local_x * count_gx
    length_y = local_y * count_gy

    def forward_real(portion):
        return transform(portion, -1, "real_in")

    def finish_x(portion):
        return refine(transform(portion, 1, "real_out"), weights_x)

    spectra = lines_x(tensor, forward_real)
    share_x = local_x // count_gy
    line_x = spectral_index(place_x * local_x + place_y * share_x + jnp.arange(share_x), length_x)[
        :, None
    ]
    line_y = spectral_index(jnp.arange(length_y), length_y)[None, :]

    def solve_y(portion):
        solved = project(transform(portion, -1, "complex"), line_x, line_y)
        return refine(transform(solved, 1, "complex"), weights_y)

    pressure = lines_y(spectra, solve_y)
    source = lines_x(pressure, finish_x)[0]
    open_cells = (1 - wall_mask).astype(jnp.float32)
    first_rate = tendency(expand(acoustic), source)
    middle = open_cells * (acoustic + time_step * first_rate)
    second_rate = tendency(expand(middle), source)
    return (open_cells * (acoustic + 0.5 * time_step * (first_rate + second_rate))).astype(
        jnp.bfloat16
    )


def solution(mesh):
    in_specs = (P(None, None, "gy", "gx"), P(), P(), P(None, None, "gy", "gx"), P(None, "gy", "gx"))
    out_specs = P(None, None, "gy", "gx")

    def chosen(velocity, weights_x, weights_y, acoustic, wall_mask):
        sizes = (mesh.shape["gx"], mesh.shape["gy"], velocity.shape, acoustic.shape)
        plan = fast_shards if fits(*sizes) else shards
        return plan(velocity, weights_x, weights_y, acoustic, wall_mask)

    return jax.shard_map(
        chosen, mesh=mesh, in_specs=in_specs, out_specs=out_specs, check_vma=False
    )
```

```python
import functools
import math

import jax
import jax.numpy as jnp
import ml_dtypes
import numpy as np
from jax import lax
from jax.experimental import pallas as pl
from jax.experimental.pallas import tpu as pltpu
from jax.sharding import PartitionSpec as P

stencil_weights = (0.75, -0.15, 1.0 / 60.0)
mean_flow = 0.3
time_step = 0.5
whole_weights = (45.0, -9.0, 1.0)

LANES = 128
RADIX = 8
HALO = 8
MARGIN = 16
TILE = 128
ROOT = math.sqrt(0.5)
STRIP = {2: (0, 6), 3: (6, 6), 1: (12, 3), 4: (15, 3), 5: (20, 4)}
STRIP_ROWS = 24
PARTS = 4
BF16 = jnp.bfloat16
F32 = jnp.float32


def halves(table):
    high = table.astype(np.float32).astype(ml_dtypes.bfloat16)
    low = (table - high.astype(np.float64)).astype(np.float32).astype(ml_dtypes.bfloat16)
    return high, low


def packed_columns(cosine, sine):
    half = LANES // 2
    parts = []
    for first in range(0, cosine.shape[1], half):
        parts += [cosine[:, first : first + half], sine[:, first : first + half]]
    return np.concatenate(parts, axis=1)


@functools.lru_cache(maxsize=None)
def x_tables(length):
    base = length // RADIX
    m = np.arange(base)[:, None]
    q = np.arange(base)[None, :]
    angle = 2.0 * np.pi * ((m * q) % base) / base
    cosine, sine = np.cos(angle), np.sin(angle)
    full = np.concatenate([packed_columns(cosine, -sine), packed_columns(sine, cosine)], axis=0)
    half = base // 2
    zero_cos, zero_sin = cosine[:, :half].copy(), -sine[:, :half]
    zero_cos[:, 0] = 0.0
    zero_sin = zero_sin.copy()
    zero_sin[:, 0] = (-1.0) ** np.arange(base)
    zero = packed_columns(zero_cos, zero_sin)
    shifted = 2.0 * np.pi * ((m * (RADIX * q[:, :half] + RADIX // 2)) % length) / length
    middle = packed_columns(np.cos(shifted), -np.sin(shifted))
    turns = 2.0 * np.pi * np.arange(1, RADIX // 2)[:, None] * np.arange(base)[None, :] / length
    return full, zero, middle, np.cos(turns), np.sin(turns)


@functools.lru_cache(maxsize=None)
def y_tables(length):
    base = length // RADIX
    index = np.arange(base)
    angle = 2.0 * np.pi * ((index[:, None] * index[None, :]) % base) / base
    both = np.concatenate([np.cos(angle), np.sin(angle)], axis=0)
    turns = 2.0 * np.pi * np.arange(RADIX)[:, None] * index[None, :] / length
    turns = np.concatenate([np.cos(turns), np.sin(turns)], axis=0).T
    high, rest = halves(turns)
    low = turns - high.astype(np.float64) - rest.astype(np.float64)
    return both, np.concatenate([high, rest, low.astype(ml_dtypes.bfloat16)], axis=1)


@functools.lru_cache(maxsize=None)
def wave_table(length, count):
    slots = LANES // 4
    base = length // RADIX
    waves = []
    for residue in (1, 2, 3):
        waves.append(RADIX * np.arange(base) + residue)
    waves.append(RADIX * np.arange(base // 2))
    waves.append(RADIX * np.arange(base // 2) + RADIX // 2)
    waves = np.concatenate(waves)
    waves = np.where(waves == 0, length // 2, waves)
    waves = np.where(waves < length // 2, waves, waves - length).reshape(count, slots)
    return np.tile(waves, (1, 4)).astype(np.float32)


@functools.lru_cache(maxsize=None)
def band_tables(rows):
    across = np.zeros((4 * LANES, 2 * LANES))
    column = np.arange(2 * LANES)
    down = np.zeros((rows, rows))
    for index, weight in enumerate(whole_weights):
        distance = index + 1
        across[column + LANES + distance, column] = weight
        across[column + LANES - distance, column] = -weight
        down += weight * (np.eye(rows, k=distance) - np.eye(rows, k=-distance))
    return across.astype(ml_dtypes.bfloat16), down.astype(ml_dtypes.bfloat16)


def beside(*tables):
    high, low = halves(np.concatenate(tables, axis=1))
    return np.concatenate([high, low], axis=0)


def split(values):
    high = values.astype(BF16)
    return high, (values - high.astype(F32)).astype(BF16)


def dot(left, right):
    return jnp.dot(left, right, preferred_element_type=F32)


def exact_dot(left, right):
    left_high, left_low = left
    right_high, right_low = right
    return dot(left_high, right_high) + (dot(left_low, right_high) + dot(left_high, right_low))


def lane_index(shape):
    return lax.broadcasted_iota(jnp.int32, shape, len(shape) - 1)


def spin(values, shift):
    return pltpu.roll(values, shift % values.shape[-1], values.ndim - 1)


def lane_tile(values, index):
    return values[:, index * LANES : (index + 1) * LANES]


def x_parts(tables, base):
    wide = 2 * base
    full = (tables[:wide], tables[wide : 2 * wide])
    at = 2 * wide
    high, low = tables[at : at + base], tables[at + base : at + 2 * base]
    return full, (high[:, :base], low[:, :base]), (high[:, base:], low[:, base:])


def pieces_kernel(place, velocity, *pieces):
    rows = pieces[0].shape[1]
    for mask, piece in enumerate(pieces):
        start = pl.multiple_of((place[0] ^ mask) * rows, 8)
        for c in range(2):
            piece[c] = velocity[c, 0, pl.ds(start, rows), :]


def rows_kernel(top, low, top_wall, low_wall, top_flow, low_flow, first, last):
    small, width = top.shape[2], top_flow.shape[3]
    first[...] = jnp.zeros(first.shape, F32)
    last[...] = jnp.zeros(last.shape, F32)
    for k, (start, rows) in STRIP.items():
        lanes = slice(0, width) if k == PARTS + 1 else slice(None)
        if k < PARTS:
            upper, lower = top[k, 0].astype(F32)[:HALO], low[k, 0].astype(F32)[small - HALO :]
        elif k == PARTS:
            upper, lower = 1.0 - top_wall[0].astype(F32), 1.0 - low_wall[0].astype(F32)
        else:
            upper, lower = top_flow[0, 0], low_flow[0, 0]
        first[start : start + rows, lanes] = upper[:rows]
        last[start : start + rows, lanes] = lower[HALO - rows :]


def strip(ref, k, upper, lanes=slice(None)):
    if k not in STRIP:
        return jnp.zeros((HALO, ref[0:1, lanes].shape[1]), F32)
    start, rows = STRIP[k]
    values = ref[start : start + rows, lanes]
    blank = jnp.zeros((HALO - rows, values.shape[1]), F32)
    return jnp.concatenate([blank, values] if upper else [values, blank], axis=0)


def columns_kernel(
    has, left, right, left_wall, right_wall, left_flow, right_flow, above, below, to_right, to_left
):
    parts = left.shape[0]
    wide, flow_wide = above.shape[1], above.shape[1] // 2
    gap = jnp.zeros((LANES - 2 * HALO, LANES), F32)

    def tall(k, inner, first, sides):
        lanes = slice(first, first + LANES)
        over, under = strip(above, k, True, lanes), strip(below, k, False, lanes)
        return jnp.concatenate([inner, under * sides[1], gap, over * sides[0]], axis=0).T

    for k in range(parts + 1):
        at = slice(k * HALO, (k + 1) * HALO)
        if k < parts:
            near, far = left[k, 0].astype(F32), right[k, 0].astype(F32)
        else:
            near, far = 1.0 - left_wall[0].astype(F32), 1.0 - right_wall[0].astype(F32)
        sides = (has[2], has[3])
        to_left[at, :] = tall(k, near, 0, sides)[:HALO]
        to_right[at, :] = tall(k, far, wide - LANES, sides)[LANES - HALO :]
    k = parts + 1
    at = slice(k * HALO, (k + 1) * HALO)
    size = left_flow.shape[2] + LANES
    blank = jnp.zeros((HALO, to_left.shape[1] - size), F32)
    to_left[at, :size] = tall(k, left_flow[0, 0], 0, (1.0, 1.0))[:HALO]
    to_right[at, :size] = tall(k, right_flow[0, 0], flow_wide - LANES, (1.0, 1.0))[LANES - HALO :]
    to_left[at, size:] = blank
    to_right[at, size:] = blank


def sides_kernel(has, place, velocity, above, below, from_left, from_right, sides, squares, mark):
    parts, tall, _ = sides.shape
    gap = jnp.zeros((LANES - 2 * HALO, tall), F32)
    for k in range(parts):
        at = slice(k * HALO, (k + 1) * HALO)
        tile = [from_right[at, :] * has[1], gap, from_left[at, :] * has[0]]
        sides[k] = jnp.concatenate(tile, axis=0).T
    at = slice(parts * HALO, (parts + 1) * HALO)
    rows, local = velocity.shape[2:]
    size = rows + LANES
    tile = [from_right[at, :size], gap[:, :size], from_left[at, :size]]
    tile = jnp.concatenate(tile, axis=0).T
    tile = tile * tile
    mark[0] = place[0]
    over, under = (strip(ref, parts, ref is above, slice(0, local)) for ref in (above, below))
    squares[:HALO, :local] = over * over
    squares[HALO : HALO + rows, :local] = velocity[0, 0] * velocity[0, 0]
    squares[HALO + rows :, :local] = under * under
    squares[:HALO, local:] = tile[size - HALO :]
    squares[HALO : HALO + rows, local:] = tile[:rows]
    squares[HALO + rows :, local:] = tile[rows : rows + HALO]


def forward_x_kernel(place, *refs):
    *pieces, tables, turns, out, total, lines, made, sent = refs
    count, _, rows, local = lines.shape
    for mask, piece in enumerate(pieces):
        lines[place[0] ^ mask] = piece[...]
    base = turns.shape[1]
    per = local // base
    u = [lines[t // per, 0, :, (t % per) * base : (t % per + 1) * base] for t in range(RADIX)]
    v = [lines[t // per, 1, :, (t % per) * base : (t % per + 1) * base] for t in range(RADIX)]
    energy = sum(b * b for b in v)
    energy = jnp.sum(energy.reshape(rows // 8, 8, base), axis=0)
    total[...] = sum(energy[:, k : k + LANES] for k in range(0, base, LANES))
    fields = ([a * a - b * b for a, b in zip(u, v)], [2.0 * a * b for a, b in zip(u, v)])
    zeros, mids, reals, imags = [], [], [[], [], []], [[], [], []]
    for a in fields:
        s04, s26, s15, s37 = a[0] + a[4], a[2] + a[6], a[1] + a[5], a[3] + a[7]
        d04, d26, d15, d37 = a[0] - a[4], a[2] - a[6], a[1] - a[5], a[3] - a[7]
        zeros.append((s04 + s26) + (s15 + s37))
        mids.append((s04 + s26) - (s15 + s37))
        minus, plus = ROOT * (d15 - d37), ROOT * (d15 + d37)
        turned = (
            (d04 + minus, -d26 - plus),
            (s04 - s26, s37 - s15),
            (d04 - minus, d26 - plus),
        )
        for index, (real, imag) in enumerate(turned):
            c, s = turns[index : index + 1, :], turns[index + 3 : index + 4, :]
            reals[index].append(real * c + imag * s)
            imags[index].append(imag * c - real * s)
    stacked = jnp.concatenate(
        [
            jnp.concatenate([jnp.concatenate(reals[i], axis=0) for i in range(3)], axis=0),
            jnp.concatenate([jnp.concatenate(imags[i], axis=0) for i in range(3)], axis=0),
        ],
        axis=1,
    )
    full, zero, middle = x_parts(tables, base)
    full = exact_dot(split(stacked), full)
    zero = exact_dot(split(jnp.concatenate(zeros, axis=0)), zero)
    middle = exact_dot(split(jnp.concatenate(mids, axis=0)), middle)
    low = lane_index((rows, LANES)) % 64 < 32
    target, copies = 0, []
    blocks = [full[2 * rows * i : 2 * rows * (i + 1)] for i in range(3)] + [zero, middle]
    for block in blocks:
        start = target
        for first in range(0, block.shape[1], LANES):
            a = block[:rows, first : first + LANES]
            c = block[rows:, first : first + LANES]
            made[target] = jnp.where(low, a, spin(c, 32))
            made[target + 1] = jnp.where(low, spin(a, -32), c)
            target += 2
        group = pl.ds(start, target - start)
        copies.append(pltpu.make_async_copy(made.at[group], out.at[group], sent.at[len(copies)]))
        copies[-1].start()
    for copy in copies:
        copy.wait()


def eighths(x, turn):
    s04, s26, s15, s37 = x[0] + x[4], x[2] + x[6], x[1] + x[5], x[3] + x[7]
    d04, d26, d15, d37 = x[0] - x[4], x[2] - x[6], x[1] - x[5], x[3] - x[7]
    quarter = turn(s15 - s37)
    spun_26, spun_37 = turn(d26), turn(d37)
    one, three = d15 + spun_37, d15 - spun_37
    spun_one, spun_three = turn(one), turn(three)
    one = ROOT * (one + spun_one)
    three = ROOT * (spun_three - three)
    return [
        (s04 + s26) + (s15 + s37),
        (d04 + spun_26) + one,
        (s04 - s26) + quarter,
        (d04 - spun_26) + three,
        (s04 + s26) - (s15 + s37),
        (d04 + spun_26) - one,
        (s04 - s26) - quarter,
        (d04 - spun_26) - three,
    ]


def solve_y_kernel(count_x, _, lines, total, wave, both, turns, out, held, spread, made, sent):
    count, rows, _ = lines.shape
    base = turns.shape[0]
    length = count * rows
    block = count_x * rows
    per = base // rows
    lanes = lane_index((base, LANES))
    sign = jnp.where(lanes < 64, 1.0, -1.0).astype(F32)

    def minus_i(z):
        return spin(z, 64) * sign

    def plus_i(z):
        return spin(z, 64) * -sign

    fields = [
        jnp.concatenate([lines[t * per + k] for k in range(per)], axis=0) for t in range(RADIX)
    ]
    mixed = eighths(fields, minus_i)
    terms, columns = turns.shape[1], 2 * RADIX
    picked = lax.broadcasted_iota(jnp.int32, (terms, columns * LANES), 0) % columns
    lane = lane_index(picked.shape)
    value = jnp.where((lane >= RADIX * LANES) & (lane % LANES >= 64), -1.0, 1.0)
    spread[...] = dot(turns[...], jnp.where(picked == lane // LANES, value, 0.0).astype(BF16))
    cosines = [spread[:, r * LANES : (r + 1) * LANES] for r in range(RADIX)]
    sines = [spread[:, (r + RADIX) * LANES : (r + RADIX + 1) * LANES] for r in range(RADIX)]
    mixed = [mixed[0]] + [
        mixed[r] * cosines[r] + spin(mixed[r], 64) * sines[r] for r in range(1, RADIX)
    ]
    tables = (both[: 2 * base], both[2 * base :])
    product = exact_dot(tables, split(jnp.concatenate(mixed, axis=1)))
    kx = wave[0:1, :]
    first = lanes % 64 < 32
    edge = jnp.float32(length // 2)
    alone = jnp.where(first, kx * kx, 0.0)
    slope = jnp.where(first | (kx == -edge), 0.0, jnp.broadcast_to(kx, lanes.shape))
    q = lax.broadcasted_iota(jnp.int32, lanes.shape, 0)
    low_ky = RADIX * (q - jnp.where(q < base // 2, 0, base)).astype(F32)
    terms = []
    for r in range(RADIX):
        at = slice(r * LANES, (r + 1) * LANES)
        spectrum = product[:base, at] + minus_i(product[base:, at])
        ky = low_ky + float(r)
        symbol = alone + slope * ky
        if r == 0:
            corner = jnp.where((kx == -edge) & ~first, edge * edge, 0.0)
            symbol = jnp.where(ky == -edge, jnp.where(first, alone, corner), symbol)
        terms.append(symbol * pl.reciprocal(kx * kx + ky * ky) * spectrum)
    pairs = [
        jnp.where(first, low + spin(low, -32), high + spin(high, 32))
        for low, high in zip(terms[:4], terms[4:])
    ]
    product = exact_dot(tables, split(jnp.concatenate(pairs, axis=1)))
    mixed = []
    for r in range(RADIX // 2):
        at = slice(r * LANES, (r + 1) * LANES)
        value = product[:base, at] + plus_i(product[base:, at])
        cosine = jnp.where(first, cosines[r], cosines[r + 4])
        sine = jnp.where(first, sines[r], sines[r + 4])
        value = value * cosine - spin(value, 64) * sine
        value = jnp.where(first, value + spin(value, -32), spin(value, 32) - value)
        if r == 2:
            value = jnp.where(first, value, plus_i(value))
        elif r:
            turned = plus_i(value)
            odd = value + turned if r == 1 else turned - value
            value = jnp.where(first, value, ROOT * odd)
        mixed.append(value)
    even, odd = mixed[0] + mixed[2], mixed[0] - mixed[2]
    side, turned = mixed[1] + mixed[3], plus_i(mixed[1] - mixed[3])
    for t, values in enumerate((even + side, odd + turned, even - side, odd - turned)):
        start = MARGIN + 2 * t * base
        held[start : start + base, :] = values
        held[start + base : start + 2 * base, :] = spin(values, -32)
    held[0:MARGIN, :] = held[length : length + MARGIN, :]
    held[length + MARGIN : length + 2 * MARGIN, :] = held[MARGIN : 2 * MARGIN, :]
    spare = total[...] + spin(total[...], 32)
    kept = rows + 2 * MARGIN // count_x
    half = made.shape[1]
    rest = kept - half
    low = lane_index((8, LANES)) % 64 < 32
    copies = []
    for target in range(count):
        start = (target // count_x) * block + (target % count_x) * kept
        for row in range(0, half, 8):
            a = held[start + row : start + row + 8, :]
            if row < rest:
                b = spin(held[start + half + row : start + half + row + 8, :], 32)
            else:
                b = spare
            made[target, row : row + 8, :] = jnp.where(low, a, b)
        if (target + 1) % RADIX == 0:
            group = pl.ds(target + 1 - RADIX, RADIX)
            copies.append(pltpu.make_async_copy(made.at[group], out.at[group], sent.at[len(copies)]))
            copies[-1].start()
    for copy in copies:
        copy.wait()


def inverse_x_kernel(
    kept, scale, place, lines, tables, turns, *refs
):
    *outs, held = refs
    count, half, _ = lines.shape
    base = turns.shape[1]
    length = RADIX * base
    rest = kept - half
    low = lane_index((half, LANES)) % 64 < 32
    groups, spare = [], None
    for first in range(0, count, 2):
        even, odd = lines[first], lines[first + 1]
        a = jnp.where(low, even, spin(odd, 32))
        b = jnp.where(low, spin(even, -32), odd)
        groups.append(jnp.concatenate([a, b[:rest]], axis=0))
        extra = b[rest : rest + 8]
        spare = extra if spare is None else spare + extra
    mean = jnp.sum(spare) * scale
    wide = 2 * base // LANES
    narrow = base // LANES
    stacked = jnp.concatenate(
        [jnp.concatenate(groups[i * wide : (i + 1) * wide], axis=1) for i in range(3)], axis=0
    )
    at = 3 * wide
    zeros = jnp.concatenate(groups[at : at + narrow], axis=1)
    mids = jnp.concatenate(groups[at + narrow : at + 2 * narrow], axis=1)
    full, zero, middle = x_parts(tables, base)
    full = exact_dot(split(stacked), full)
    zero = exact_dot(split(zeros), zero) * scale
    mid = exact_dot(split(mids), middle) * scale
    turned = []
    for i in range(3):
        real = full[i * kept : (i + 1) * kept, :base]
        imag = full[i * kept : (i + 1) * kept, base:]
        c = turns[i : i + 1, :] * (2.0 * scale)
        s = turns[i + 3 : i + 4, :] * (2.0 * scale)
        turned.append((real * c - imag * s, real * s + imag * c))
    for t in range(RADIX):
        value = zero + mid if t % 2 == 0 else zero - mid
        for i, (real, imag) in enumerate(turned):
            eighth = t * (i + 1) % RADIX
            c = (1.0, ROOT, 0.0, -ROOT, -1.0, -ROOT, 0.0, ROOT)[eighth]
            s = (0.0, ROOT, 1.0, ROOT, 0.0, -ROOT, -1.0, -ROOT)[eighth]
            if c:
                value = value + c * real
            if s:
                value = value - s * imag
        held[:, t * base : (t + 1) * base] = mean - value
    targets, local = len(outs), outs[0].shape[1] - LANES
    right = lane_index((kept, LANES)) < 64
    for mask, out in enumerate(outs):
        start = pl.multiple_of((place[0] ^ mask) * local, LANES)
        after = pl.multiple_of(jnp.where(start + local == length, 0, start + local), LANES)
        before = pl.multiple_of(jnp.where(start == 0, length, start) - LANES, LANES)
        out[:, :local] = held[:, pl.ds(start, local)]
        out[:, local:] = jnp.where(
            right, held[:, pl.ds(after, LANES)], held[:, pl.ds(before, LANES)]
        )


def slopes_x(parts, band, with_edge):
    tiles = parts[0].shape[-1] // LANES
    pieces = []
    for first in list(range(0, tiles - 1, 2)) + ([tiles - 1] if with_edge else []):
        steps = (-1, 0, 1, 2) if first < tiles - 1 else (-1, 0, 1)
        table = band[...] if first < tiles - 1 else band[: 3 * LANES, :LANES]
        order = [(first + step) % tiles for step in steps]
        piece = None
        for part in parts:
            term = dot(jnp.concatenate([lane_tile(part, t) for t in order], axis=1), table)
            piece = term if piece is None else piece + term
        pieces.append(piece)
    return jnp.concatenate(pieces, axis=1)


def slope_y(read):
    value = read(3) - read(-3)
    for index in (0, 1):
        value = value + whole_weights[index] * (read(index + 1) - read(-index - 1))
    return value


def edged(k, side, center, up, down, above, below, sides, has, first=0):
    step = pl.program_id(0) + first
    tile, width = center.shape
    tall = sides.shape[1]
    last = (tall - LANES) // tile - 1
    base = pl.multiple_of(step * tile, 8)
    before = pl.multiple_of(jnp.where(step == 0, tall, base) - HALO, 8)
    over = jnp.where(step == 0, strip(above, k, True) * has[2], up)
    under = jnp.where(step == last, strip(below, k, False) * has[3], down)
    rows = (
        (over, sides[side, pl.ds(before, HALO), :]),
        (center, sides[side, pl.ds(base, tile), :]),
        (under, sides[side, pl.ds(pl.multiple_of(base + tile, 8), HALO), :]),
    )
    return jnp.concatenate([jnp.concatenate(pair, axis=1) for pair in rows], axis=0)


def edged_open(k, side, wall, wall_up, wall_down, above, below, sides, has, first=0):
    open_cells = [1.0 - ref[0].astype(F32) for ref in (wall, wall_up, wall_down)]
    return edged(k, side, *open_cells, above, below, sides, has, first)


def quiet_step_kernel(
    first, has, place, center, up, down, wall, wall_up, wall_down, above, below, sides, across, along, along_inner, calm, density, shown_open, mark
):
    parts, _, tile, width = center.shape
    high = tile + 2 * HALO
    opened = edged_open(parts, parts, wall, wall_up, wall_down, above, below, sides, has, first)
    values = []
    for k in range(parts):
        value = edged(
            k,
            k,
            center[k, 0].astype(F32),
            up[k, 0].astype(F32)[up.shape[2] - HALO :],
            down[k, 0].astype(F32)[:HALO],
            above,
            below,
            sides,
            has,
            first,
        )
        values.append(value)

    def drops(x, along_b, along_p):
        diverge = x[1] + along_b
        return (
            diverge + mean_flow * x[0],
            x[3] + mean_flow * x[1],
            along_p + mean_flow * x[2],
            diverge + mean_flow * x[3],
        )

    short = [value.astype(BF16) for value in values]
    x = slopes_x((jnp.concatenate(short, axis=0),), across, True)
    x = [x[k * high : (k + 1) * high] for k in range(parts)]
    table = along[...]
    dropped = drops(x, dot(table, short[2]), dot(table, short[3]))
    middle = [opened * (v - (time_step / 60.0) * d) for v, d in zip(values, dropped)]
    inner = slice(HALO, HALO + tile)
    x = slopes_x(split(jnp.concatenate([value[inner] for value in middle], axis=0)), across, False)
    x = [x[k * tile : (k + 1) * tile] for k in range(parts)]
    table = along_inner[...]
    y = [sum(dot(table, part) for part in split(middle[k][:, :width])) for k in (2, 3)]
    dropped = drops(x, *y)
    shown = opened[inner, :width]
    for k in range(parts):
        start = 0.5 * values[k][inner, :width] - (0.5 * time_step / 60.0) * dropped[k]
        value = shown * start + 0.5 * middle[k][inner, :width]
        if k == 0:
            density[0, 0] = value.astype(BF16)
        else:
            calm[k - 1] = value
    shown_open[0] = opened.astype(BF16)
    mark[0] = place[0]


def tables_kernel(place, weights_x, weights_y, rise_x, rise_y, mark):
    mark[0] = place[0]
    tiles, reach_x, lanes = rise_x.shape
    wide, length_x = (tiles - 1) * lanes, weights_x.shape[1]
    first = place[0] * wide
    half = LANES // 2

    def weights(ref, start, size):
        length = ref.shape[1]
        start = jnp.where(start < 0, start + length, jnp.where(start >= length, start - length, start))
        return ref[:, pl.ds(pl.multiple_of(start, LANES), size)]

    cells = lax.broadcasted_iota(jnp.int32, (reach_x, lanes), 0)
    fine = lax.broadcasted_iota(jnp.int32, (reach_x, lanes), 1)
    right, left = weights(weights_x, first + wide, LANES), weights(weights_x, first - LANES, LANES)
    edge = jnp.where(lane_index(right.shape) < half, right, left)
    edge = jnp.concatenate([edge, edge], axis=1)
    for k in range(tiles):
        own = weights(weights_x, first + k * lanes, lanes) if k < tiles - 1 else edge
        target = fine // 2 - 1
        if k == tiles - 1:
            target = jnp.where(fine < half, target, target + half)
        value = jnp.zeros(fine.shape, F32)
        for t in range(4):
            value = jnp.where(cells == (target + t) % reach_x, own[t : t + 1, :], value)
        rise_x[k] = value
    steps, high, reach = rise_y.shape
    tall = steps * TILE
    first = place[1] * tall
    own = [weights(weights_y, first + k * LANES, LANES) for k in range(-1, tall // LANES + 1)]
    own = jnp.concatenate([jnp.concatenate(own, axis=1), jnp.zeros((4, tall + 2 * LANES), F32)], axis=0).T
    cells = lax.broadcasted_iota(jnp.int32, (high, reach), 1) % (reach // 3)
    target = lax.broadcasted_iota(jnp.int32, (high, reach), 0) // 2 + (HALO // 2 - 1)
    for k in range(steps):
        start = LANES - HALO + k * TILE
        value = jnp.zeros((high, reach), F32)
        for t in range(4):
            value = jnp.where(cells == target + t, own[start : start + high, t : t + 1], value)
        rise_y[k] = value


def source_kernel(place, squares, opened, rise_x, rise_y, quiet, across, _, *refs):
    *lines, out, squared, cells_open, matrix, rows_matrix, calm, band, held, raised, forced, done, fetched, kept = refs
    steps = done.shape[0]
    tile, width = calm.shape[2:]
    high = tile + 2 * HALO
    rows = lines[0].shape[0]

    def tile_copies(k):
        part = quiet.at[:, pl.ds(k * tile, tile), :]
        return (
            pltpu.make_async_copy(part, calm.at[k % 2], fetched.at[k % 2]),
            pltpu.make_async_copy(opened.at[k], cells_open.at[k % 2], fetched.at[2 + k % 2]),
        )

    def done_copy(k):
        part = out.at[1:, 0, pl.ds(k * tile, tile), :]
        return pltpu.make_async_copy(done.at[k], part, kept.at[k])

    arrays = ((squares, squared), (rise_x, matrix), (rise_y, rows_matrix), (across, band))
    copies = [
        pltpu.make_async_copy(source, target, fetched.at[4 + k])
        for k, (source, target) in enumerate(arrays)
    ]
    pieces = [
        pltpu.make_async_copy(
            piece,
            held.at[pl.ds(pl.multiple_of((place[0] ^ mask) * rows, 8), rows), :],
            fetched.at[4 + len(arrays) + mask],
        )
        for mask, piece in enumerate(lines)
    ]
    for copy in (*pieces, *copies, *tile_copies(0), *tile_copies(1)):
        copy.start()
    for copy in pieces + copies[:1]:
        copy.wait()

    level = held[MARGIN - HALO : MARGIN - HALO + squared.shape[0], :] - squared[...]
    count = level.shape[1] // LANES
    near = lane_index((level.shape[0], LANES)) < 64
    around = []
    for k in range(count):
        after, before = lane_tile(level, (k + 1) % count), lane_tile(level, (k - 1) % count)
        around.append(split(jnp.concatenate([lane_tile(level, k), jnp.where(near, after, before)], axis=1)))
    copies[1].wait()
    for k in range(count):
        lanes = 2 * LANES if k < count - 1 else LANES
        value = split(exact_dot(around[k], split(matrix[k][:, :lanes])))
        for part in range(2):
            raised[part, :, 2 * k * LANES : 2 * k * LANES + lanes] = value[part]
    for copy in copies[2:]:
        copy.wait()

    reach = rows_matrix.shape[2] // 3
    third = lane_index((high, 3 * reach)) >= 2 * reach
    for k in range(steps):
        start = k * (tile // 2)
        window = [raised[part, start : start + reach, :] for part in (0, 1, 0)]
        weights = split(rows_matrix[k])
        weights = jnp.where(third, weights[1], weights[0])
        calm_here, open_here = tile_copies(k)
        open_here.wait()
        free = time_step * cells_open[k % 2].astype(F32)
        value = free * dot(weights, jnp.concatenate(window, axis=0))
        forced[k % 2] = value
        inner = value[HALO : HALO + tile]
        shown = (0.5 / 60.0) * free[HALO : HALO + tile, :width]
        x = shown * slopes_x(split(inner), band, False)
        y = shown * slope_y(lambda d: forced[k % 2, HALO + d : HALO + d + tile, :width])
        calm_here.wait()
        still = calm.at[k % 2]
        done[k, 0] = (still[0] - x).astype(BF16)
        done[k, 1] = (still[1] - y).astype(BF16)
        done[k, 2] = (still[2] + inner[:, :width] - mean_flow * x).astype(BF16)
        done_copy(k).start()
        if k + 2 < steps:
            for copy in tile_copies(k + 2):
                copy.start()
    for k in range(steps):
        done_copy(k).wait()


def call(
    kernel, operands, outs, scratch=(), steps=0, specs=None, out_specs=None, after=(), aliases=None, megabytes=24, flops=0, moved=0, name=None
):
    count = len(operands)

    def body(*refs):
        kernel(*refs[:count], *refs[count + len(after) :])

    def whole(array):
        zeros = (0,) * len(array.shape)
        return pl.BlockSpec(array.shape, lambda *_: zeros)

    arguments = {}
    chosen = specs or {}
    if steps:
        arguments["grid"] = (steps,)
        in_specs = [chosen.get(i, whole(o)) for i, o in enumerate(operands)]
        arguments["out_specs"] = jax.tree.map(whole, outs) if out_specs is None else out_specs
    else:
        local = pl.BlockSpec(memory_space=pltpu.VMEM)
        in_specs = [chosen.get(i, local) for i in range(count)]
        if out_specs is not None:
            arguments["out_specs"] = out_specs
    return pl.pallas_call(
        body,
        out_shape=outs,
        in_specs=in_specs + [pl.BlockSpec(memory_space=pl.ANY)] * len(after),
        scratch_shapes=list(scratch),
        input_output_aliases=aliases or {},
        compiler_params=pltpu.CompilerParams(vmem_limit_bytes=megabytes << 20),
        cost_estimate=pl.CostEstimate(flops=flops, bytes_accessed=moved, transcendentals=0),
        name=name,
        **arguments,
    )(*operands, *after)


def ring(array, axis, step):
    size = lax.axis_size(axis)
    return lax.ppermute(array, axis, [(i, (i + step) % size) for i in range(size)])


def swap(array, axis, mask):
    return lax.ppermute(array, axis, [(i, i ^ mask) for i in range(lax.axis_size(axis))])


def shaped(*shape, kind=F32):
    return jax.ShapeDtypeStruct(shape, kind)


def pressure_lines(pieces, place_x, gathered, spread, stepped):
    _, rows, local_x = pieces[0].shape
    count_x, count_y = lax.axis_size("gx"), lax.axis_size("gy")
    count = count_x * count_y
    scalars = {0: pl.BlockSpec(memory_space=pltpu.SMEM)}
    length_x, length_y = local_x * count_x, rows * count
    full, zero, middle, cos_turn, sin_turn = x_tables(length_x)
    turns = np.zeros((8, cos_turn.shape[1]), np.float32)
    turns[0:3], turns[3:6] = cos_turn, sin_turn
    spectra, total = call(
        forward_x_kernel,
        (place_x, *pieces, np.concatenate([beside(full), beside(zero, middle)]), turns),
        (shaped(count, rows, LANES), shaped(8, LANES)),
        (
            pltpu.VMEM((count_x, 2, rows, local_x), F32),
            pltpu.VMEM((count, rows, LANES), F32),
            pltpu.SemaphoreType.DMA((5,)),
        ),
        specs=scalars,
        out_specs=(pl.BlockSpec(memory_space=pl.ANY), pl.BlockSpec(memory_space=pltpu.VMEM)),
        after=gathered,
        flops=10**9,
        moved=4 << 20,
        name="forward_x",
    )
    spectra = lax.all_to_all(spectra, ("gy", "gx"), 0, 0, tiled=True)
    place = lax.axis_index("gy") * count_x + lax.axis_index("gx")
    waves = jnp.asarray(wave_table(length_x, count))
    wave = lax.dynamic_slice(waves, (place, 0), (1, LANES))
    both, turns_y = y_tables(length_y)
    kept = rows + 2 * MARGIN // count_x
    half = (kept // 2 + 8) // 8 * 8
    solved = call(
        functools.partial(solve_y_kernel, count_x),
        (spread, spectra, total, wave, beside(both), turns_y),
        shaped(count, half, LANES),
        (
            pltpu.VMEM((length_y + 2 * MARGIN, LANES), F32),
            pltpu.VMEM((length_y // RADIX, 2 * RADIX * LANES), F32),
            pltpu.VMEM((count, half, LANES), F32),
            pltpu.SemaphoreType.DMA((count // RADIX,)),
        ),
        specs=scalars,
        out_specs=pl.BlockSpec(memory_space=pl.ANY),
        flops=4 * 10**9,
        moved=6 << 20,
        name="solve_y",
    )
    solved = lax.all_to_all(solved, ("gy", "gx"), 0, 0, tiled=True)
    back = 2.0 * zero.T
    back[LANES // 2] *= 0.5
    tables = np.concatenate(
        [beside(full.T), beside(back, 2.0 * middle.T)]
    )
    pressed = call(
        functools.partial(inverse_x_kernel, kept, 1.0 / (length_x * length_y)),
        (stepped, solved, tables, turns),
        (shaped(kept, local_x + LANES),) * count_x,
        (pltpu.VMEM((kept, length_x), F32),),
        specs=scalars,
        flops=10**9,
        moved=4 << 20,
        name="inverse_x",
    )
    return [piece if mask == 0 else swap(piece, "gx", mask) for mask, piece in enumerate(pressed)]


def fast_shards(velocity, weights_x, weights_y, acoustic, wall_mask):
    parts, _, tall, wide = acoustic.shape
    _, _, local_y, local_x = velocity.shape
    count_x, count_y = lax.axis_size("gx"), lax.axis_size("gy")
    place_x, place_y = lax.axis_index("gx"), lax.axis_index("gy")
    full, high, steps = wide + LANES, TILE + 2 * HALO, tall // TILE
    strips = (parts + 2) * HALO
    small = 2 * HALO
    has = jnp.stack([place_x > 0, place_x < count_x - 1, place_y > 0, place_y < count_y - 1])
    has = has.astype(F32)
    scalars = pl.BlockSpec(memory_space=pltpu.SMEM)

    def at(block, *index):
        return pl.BlockSpec(block, lambda i: index)

    own = place_x.astype(jnp.int32).reshape(1)
    sent = call(
        pieces_kernel,
        (own, velocity),
        (shaped(2, local_y // count_x, local_x),) * count_x,
        specs={0: scalars},
        moved=2 << 20,
        megabytes=8,
        name="pieces",
    )
    moved = [piece if mask == 0 else swap(piece, "gx", mask) for mask, piece in enumerate(sent)]
    first, last = call(
        rows_kernel,
        (acoustic, acoustic, wall_mask, wall_mask, velocity, velocity),
        (shaped(STRIP_ROWS, wide),) * 2,
        steps=1,
        specs={
            0: at((parts, 1, small, wide), 0, 0, 0, 0),
            1: at((parts, 1, small, wide), 0, 0, tall // small - 1, 0),
            2: at((1, HALO, wide), 0, 0, 0),
            3: at((1, HALO, wide), 0, tall // HALO - 1, 0),
            4: at((1, 1, HALO, local_x), 1, 0, 0, 0),
            5: at((1, 1, HALO, local_x), 1, 0, local_y // HALO - 1, 0),
        },
        after=moved[1:2],
        moved=2 << 20,
        megabytes=50,
        name="rows",
    )
    above, below = ring(last, "gy", 1), ring(first, "gy", -1)
    to_right, to_left = call(
        columns_kernel,
        (has, acoustic, acoustic, wall_mask, wall_mask, velocity, velocity, above, below),
        (shaped(strips, tall + LANES), shaped(strips, tall + LANES)),
        steps=1,
        specs={
            0: scalars,
            1: at((parts, 1, tall, LANES), 0, 0, 0, 0),
            2: at((parts, 1, tall, LANES), 0, 0, 0, wide // LANES - 1),
            3: at((1, tall, LANES), 0, 0, 0),
            4: at((1, tall, LANES), 0, 0, wide // LANES - 1),
            5: at((1, 1, local_y, LANES), 1, 0, 0, 0),
            6: at((1, 1, local_y, LANES), 1, 0, 0, local_x // LANES - 1),
        },
        moved=8 << 20,
        megabytes=54,
        name="columns",
    )
    from_left, from_right = ring(to_right, "gx", 1), ring(to_left, "gx", -1)
    local_memory = pl.BlockSpec(memory_space=pltpu.VMEM)
    tiles = wide // (2 * LANES) + 1
    rise_x, rise_y, listed = call(
        tables_kernel,
        (jnp.stack([place_x, place_y]).astype(jnp.int32), weights_x, weights_y),
        (
            shaped(tiles, 2 * LANES, 2 * LANES),
            shaped(steps, high, 3 * (high // 2 + HALO)),
            shaped(1, kind=jnp.int32),
        ),
        specs={0: scalars},
        out_specs=(local_memory, local_memory, scalars),
        moved=4 << 20,
        megabytes=54,
        name="tables",
    )
    sides, squares, beside = call(
        sides_kernel,
        (has, listed, velocity, above, below, from_left, from_right),
        (
            shaped(parts + 1, tall + LANES, LANES),
            shaped(local_y + 2 * HALO, local_x + LANES),
            shaped(1, kind=jnp.int32),
        ),
        steps=1,
        specs={0: scalars, 1: scalars, 2: at((1, 1, local_y, local_x), 1, 0, 0, 0)},
        out_specs=(
            at((parts + 1, tall + LANES, LANES), 0, 0, 0),
            at((local_y + 2 * HALO, local_x + LANES), 0, 0),
            scalars,
        ),
        moved=8 << 20,
        megabytes=54,
        name="sides",
    )
    across, along = band_tables(high)
    along_inner = along[HALO : HALO + TILE]
    per, rows = TILE // small, TILE // HALO

    def tiled(first):
        walls = (
            pl.BlockSpec((1, TILE, wide), lambda i: (0, i + first, 0)),
            pl.BlockSpec((1, HALO, wide), lambda i: (0, jnp.maximum((i + first) * rows - 1, 0), 0)),
            pl.BlockSpec(
                (1, HALO, wide),
                lambda i: (0, jnp.minimum((i + first + 1) * rows, steps * rows - 1), 0),
            ),
        )
        cells = (
            pl.BlockSpec((parts, 1, TILE, wide), lambda i: (0, 0, i + first, 0)),
            pl.BlockSpec(
                (parts, 1, small, wide), lambda i: (0, 0, jnp.maximum((i + first) * per - 1, 0), 0)
            ),
            pl.BlockSpec(
                (parts, 1, small, wide),
                lambda i: (0, 0, jnp.minimum((i + first + 1) * per, steps * per - 1), 0),
            ),
        )
        return cells, walls

    def quiet_tiles(first, count, before):
        cells, walls = tiled(first)
        operands = (has, own, acoustic, acoustic, acoustic, wall_mask, wall_mask, wall_mask, above, below, sides)
        operands = operands + (across, along, along_inner)
        return call(
            functools.partial(quiet_step_kernel, first),
            operands,
            (
                shaped(parts - 1, tall, wide),
                shaped(*acoustic.shape, kind=BF16),
                shaped(steps, high, full, kind=BF16),
                shaped(1, kind=jnp.int32),
            ),
            steps=count,
            specs=dict(enumerate((scalars, scalars) + cells + walls)),
            out_specs=(
                pl.BlockSpec((parts - 1, TILE, wide), lambda i: (0, i + first, 0)),
                pl.BlockSpec((1, 1, TILE, wide), lambda i: (0, 0, i + first, 0)),
                pl.BlockSpec((1, high, full), lambda i: (i + first, 0, 0)),
                scalars,
            ),
            after=before,
            aliases={len(operands) + k: k for k in range(len(before))},
            megabytes=54,
            flops=3 * 10**9 * count,
            moved=(12 << 20) * count,
            name="quiet_step",
        )

    early = max(steps * 3 // 4, 1)
    *begun, stepped = quiet_tiles(0, early, ())
    if early < steps:
        *begun, _ = quiet_tiles(early, steps - early, begun)
    quiet, final, opened = begun
    lines = pressure_lines(moved, own, (above, below), beside, stepped)
    operands = (own, squares, opened, rise_x, rise_y, quiet, across, final, *lines)
    anywhere = pl.BlockSpec(memory_space=pl.ANY)
    specs = {k: anywhere for k in range(1, len(operands))}
    scratch = (
        pltpu.VMEM(squares.shape, F32),
        pltpu.VMEM((2,) + opened.shape[1:], BF16),
        pltpu.VMEM(rise_x.shape, F32),
        pltpu.VMEM(rise_y.shape, F32),
        pltpu.VMEM((2, parts - 1, TILE, wide), F32),
        pltpu.VMEM(across.shape, BF16),
        pltpu.VMEM((local_y + 2 * MARGIN, local_x + LANES), F32),
        pltpu.VMEM((2, local_y + 2 * HALO, full), BF16),
        pltpu.VMEM((2, high, full), F32),
        pltpu.VMEM((steps, parts - 1, TILE, wide), BF16),
        pltpu.SemaphoreType.DMA((8 + count_x,)),
        pltpu.SemaphoreType.DMA((steps,)),
    )
    return call(
        source_kernel,
        operands,
        shaped(*acoustic.shape, kind=BF16),
        scratch,
        specs={0: scalars, **specs},
        out_specs=anywhere,
        aliases={7: 0},
        megabytes=56,
        flops=4 * 10**9,
        moved=16 << 20,
        name="source_step",
    )


def fits(count_x, count_y, velocity, acoustic):
    _, planes, local_y, local_x = velocity
    _, _, tall, wide = acoustic
    length_x, length_y = local_x * count_x, local_y * count_y
    rows = local_y // count_x
    base_x, base_y = length_x // RADIX, length_y // RADIX
    return (
        planes == 1
        and acoustic[0] == PARTS
        and length_x * 2 == count_x * count_y * LANES
        and base_x % (2 * LANES) == 0
        and local_x % base_x == 0
        and rows % 8 == 0
        and base_y % rows == 0
        and base_y % 8 == 0
        and count_x * count_y % RADIX == 0
        and MARGIN * 2 % (8 * count_x) == 0
        and tall == 2 * local_y
        and wide == 2 * local_x
        and tall % TILE == 0
        and tall % LANES == 0
        and tall >= 2 * TILE
        and count_x & (count_x - 1) == 0
        and wide % (2 * LANES) == 0
    )


def extended(array, sides, width):
    for axis, dim in sides:
        size, length = (lax.axis_size(axis), array.shape[dim])
        up = [(i, (i + 1) % size) for i in range(size - 1)]
        down = [(j, i) for i, j in up]
        last = lax.slice_in_dim(array, length - width, length, axis=dim)
        leading = lax.slice_in_dim(array, 0, width, axis=dim)
        before = lax.ppermute(last, axis, up)
        after = lax.ppermute(leading, axis, down)
        array = jnp.concatenate([before, array, after], axis=dim)
    return array


def gradients(padded):
    height = padded.shape[-2] - 6
    breadth = padded.shape[-1] - 6
    rows_mid = padded[..., 3 : 3 + height, :]
    cols_mid = padded[..., :, 3 : 3 + breadth]
    along_x = jnp.zeros_like(padded[..., 3 : 3 + height, 3 : 3 + breadth])
    along_y = jnp.zeros_like(along_x)
    for index, weight in enumerate(stencil_weights):
        distance = index + 1
        along_x = along_x + weight * (
            rows_mid[..., 3 + distance : 3 + distance + breadth]
            - rows_mid[..., 3 - distance : 3 - distance + breadth]
        )
        along_y = along_y + weight * (
            cols_mid[..., 3 + distance : 3 + distance + height, :]
            - cols_mid[..., 3 - distance : 3 - distance + height, :]
        )
    return (along_x, along_y)


def tendency(padded, source):
    along_x, along_y = gradients(padded)
    diverge = along_x[1] + along_y[2]
    forcing = jnp.stack([-diverge, -along_x[3], -along_y[3], source - diverge])
    return forcing - mean_flow * along_x


def spectral_index(flat, length):
    second = length // 16
    wave = flat // second + 16 * (flat % second)
    return jnp.where(wave < length // 2, wave, wave - length).astype(jnp.float32)


def twiddles(rows_count, cols_count, modulus, sign):
    products = jnp.arange(rows_count)[:, None] * jnp.arange(cols_count)[None, :] % modulus
    angles = 2.0 * math.pi / modulus * products.astype(jnp.float32)
    return (jnp.cos(angles), sign * jnp.sin(angles))


def mix_rows(real_part, imag_part, cosine, sine):
    exact = lax.Precision.HIGHEST
    cos_real = jnp.einsum("ka,...ab->...kb", cosine, real_part, precision=exact)
    cos_imag = jnp.einsum("ka,...ab->...kb", cosine, imag_part, precision=exact)
    sin_real = jnp.einsum("ka,...ab->...kb", sine, real_part, precision=exact)
    sin_imag = jnp.einsum("ka,...ab->...kb", sine, imag_part, precision=exact)
    return (cos_real - sin_imag, cos_imag + sin_real)


def mix_cols(real_part, imag_part, cosine, sine):
    exact = lax.Precision.HIGHEST
    cos_real = jnp.einsum("...kb,bc->...kc", real_part, cosine, precision=exact)
    cos_imag = jnp.einsum("...kb,bc->...kc", imag_part, cosine, precision=exact)
    sin_real = jnp.einsum("...kb,bc->...kc", real_part, sine, precision=exact)
    sin_imag = jnp.einsum("...kb,bc->...kc", imag_part, sine, precision=exact)
    return (cos_real - sin_imag, cos_imag + sin_real)


def rotate(real_part, imag_part, cosine, sine):
    return (real_part * cosine - imag_part * sine, real_part * sine + imag_part * cosine)


def discrete(real_part, imag_part, sign):
    length = real_part.shape[-1]
    second = length // 16
    initial = real_part.shape
    folded = initial[:-1] + (16, second)
    real_part = real_part.reshape(folded)
    imag_part = imag_part.reshape(folded)
    small_cos, small_sin = twiddles(16, 16, 16, sign)
    large_cos, large_sin = twiddles(second, second, second, sign)
    turn_cos, turn_sin = twiddles(16, second, length, sign)
    if sign < 0:
        real_part, imag_part = mix_rows(real_part, imag_part, small_cos, small_sin)
        real_part, imag_part = rotate(real_part, imag_part, turn_cos, turn_sin)
        real_part, imag_part = mix_cols(real_part, imag_part, large_cos, large_sin)
    else:
        real_part, imag_part = mix_cols(real_part, imag_part, large_cos, large_sin)
        real_part, imag_part = rotate(real_part, imag_part, turn_cos, turn_sin)
        real_part, imag_part = mix_rows(real_part, imag_part, small_cos, small_sin)
        real_part = real_part / length
        imag_part = imag_part / length
    return (real_part.reshape(initial), imag_part.reshape(initial))


def transform(stacked, sign, kind):
    if kind == "real_in":
        real_part = stacked
        imag_part = jnp.zeros_like(stacked)
    else:
        half = stacked.shape[0] // 2
        real_part = stacked[:half]
        imag_part = stacked[half:]
    real_out, imag_out = discrete(real_part, imag_part, sign)
    if kind == "real_out":
        return real_out
    return jnp.concatenate([real_out, imag_out], axis=0)


def project(stacked, wave_x, wave_y):
    coef_xx = wave_x * wave_x
    coef_xy = 2.0 * wave_x * wave_y
    coef_yy = wave_y * wave_y
    denominator = wave_x * wave_x + wave_y * wave_y
    positive = denominator > 0
    safe = jnp.where(positive, denominator, 1.0)

    def combine(parts):
        numerator = -(coef_xx * parts[0] + coef_xy * parts[1] + coef_yy * parts[2])
        return jnp.where(positive, numerator / safe, 0.0)

    return jnp.stack([combine(stacked[:3]), combine(stacked[3:])])


def refine(stacked, weights):
    result = jnp.zeros(stacked.shape[:-1] + (2 * stacked.shape[-1],), jnp.float32)
    for offset in range(4):
        result = (
            result
            + jnp.repeat(jnp.roll(stacked, 1 - offset, axis=-1), 2, axis=-1) * weights[offset]
        )
    return result


def lines_x(stacked, action):
    gathered = action(lax.all_to_all(stacked, "gx", split_axis=2, concat_axis=3, tiled=True))
    return lax.all_to_all(gathered, "gx", split_axis=3, concat_axis=2, tiled=True)


def lines_y(stacked, action):
    turned = jnp.swapaxes(stacked, 2, 3)
    gathered = action(lax.all_to_all(turned, "gy", split_axis=2, concat_axis=3, tiled=True))
    returned = lax.all_to_all(gathered, "gy", split_axis=3, concat_axis=2, tiled=True)
    return jnp.swapaxes(returned, 2, 3)


def expand(fields):
    return extended(fields, (("gx", 3), ("gy", 2)), 3)


def shards(velocity, weights_x, weights_y, acoustic, wall_mask):
    acoustic = acoustic.astype(jnp.float32)
    flow_x = velocity[0]
    flow_y = velocity[1]
    tensor = jnp.stack([flow_x * flow_x, flow_x * flow_y, flow_y * flow_y])
    count_gx = lax.axis_size("gx")
    count_gy = lax.axis_size("gy")
    place_x = lax.axis_index("gx")
    place_y = lax.axis_index("gy")
    local_y = tensor.shape[2]
    local_x = tensor.shape[3]
    length_x = local_x * count_gx
    length_y = local_y * count_gy

    def forward_real(portion):
        return transform(portion, -1, "real_in")

    def finish_x(portion):
        return refine(transform(portion, 1, "real_out"), weights_x)

    spectra = lines_x(tensor, forward_real)
    share_x = local_x // count_gy
    line_x = spectral_index(place_x * local_x + place_y * share_x + jnp.arange(share_x), length_x)[
        :, None
    ]
    line_y = spectral_index(jnp.arange(length_y), length_y)[None, :]

    def solve_y(portion):
        solved = project(transform(portion, -1, "complex"), line_x, line_y)
        return refine(transform(solved, 1, "complex"), weights_y)

    pressure = lines_y(spectra, solve_y)
    source = lines_x(pressure, finish_x)[0]
    open_cells = (1 - wall_mask).astype(jnp.float32)
    first_rate = tendency(expand(acoustic), source)
    middle = open_cells * (acoustic + time_step * first_rate)
    second_rate = tendency(expand(middle), source)
    return (open_cells * (acoustic + 0.5 * time_step * (first_rate + second_rate))).astype(
        jnp.bfloat16
    )


def solution(mesh):
    in_specs = (P(None, None, "gy", "gx"), P(), P(), P(None, None, "gy", "gx"), P(None, "gy", "gx"))
    out_specs = P(None, None, "gy", "gx")

    def chosen(velocity, weights_x, weights_y, acoustic, wall_mask):
        sizes = (mesh.shape["gx"], mesh.shape["gy"], velocity.shape, acoustic.shape)
        plan = fast_shards if fits(*sizes) else shards
        return plan(velocity, weights_x, weights_y, acoustic, wall_mask)

    return jax.shard_map(
        chosen, mesh=mesh, in_specs=in_specs, out_specs=out_specs, check_vma=False
    )
```

```python
import functools
import math

import jax
import jax.numpy as jnp
import ml_dtypes
import numpy as np
from jax import lax
from jax.experimental import pallas as pl
from jax.experimental.pallas import tpu as pltpu
from jax.sharding import PartitionSpec as P

stencil_weights = (0.75, -0.15, 1.0 / 60.0)
mean_flow = 0.3
time_step = 0.5
whole_weights = (45.0, -9.0, 1.0)

LANES = 128
RADIX = 8
HALO = 8
MARGIN = 16
TILE = 128
ROOT = math.sqrt(0.5)
STRIP = {2: (0, 6), 3: (6, 6), 1: (12, 3), 4: (15, 3), 5: (20, 4)}
STRIP_ROWS = 24
PARTS = 4
BF16 = jnp.bfloat16
F32 = jnp.float32


def halves(table):
    high = table.astype(np.float32).astype(ml_dtypes.bfloat16)
    low = (table - high.astype(np.float64)).astype(np.float32).astype(ml_dtypes.bfloat16)
    return high, low


def packed_columns(cosine, sine):
    half = LANES // 2
    parts = []
    for first in range(0, cosine.shape[1], half):
        parts += [cosine[:, first : first + half], sine[:, first : first + half]]
    return np.concatenate(parts, axis=1)


@functools.lru_cache(maxsize=None)
def x_tables(length):
    base = length // RADIX
    m = np.arange(base)[:, None]
    q = np.arange(base)[None, :]
    angle = 2.0 * np.pi * ((m * q) % base) / base
    cosine, sine = np.cos(angle), np.sin(angle)
    full = np.concatenate([packed_columns(cosine, -sine), packed_columns(sine, cosine)], axis=0)
    half = base // 2
    zero_cos, zero_sin = cosine[:, :half].copy(), -sine[:, :half]
    zero_cos[:, 0] = 0.0
    zero_sin = zero_sin.copy()
    zero_sin[:, 0] = (-1.0) ** np.arange(base)
    zero = packed_columns(zero_cos, zero_sin)
    shifted = 2.0 * np.pi * ((m * (RADIX * q[:, :half] + RADIX // 2)) % length) / length
    middle = packed_columns(np.cos(shifted), -np.sin(shifted))
    turns = 2.0 * np.pi * np.arange(1, RADIX // 2)[:, None] * np.arange(base)[None, :] / length
    return full, zero, middle, np.cos(turns), np.sin(turns)


@functools.lru_cache(maxsize=None)
def y_tables(length):
    base = length // RADIX
    index = np.arange(base)
    angle = 2.0 * np.pi * ((index[:, None] * index[None, :]) % base) / base
    both = np.concatenate([np.cos(angle), np.sin(angle)], axis=0)
    turns = 2.0 * np.pi * np.arange(RADIX)[:, None] * index[None, :] / length
    turns = np.concatenate([np.cos(turns), np.sin(turns)], axis=0).T
    high, rest = halves(turns)
    low = turns - high.astype(np.float64) - rest.astype(np.float64)
    return both, np.concatenate([high, rest, low.astype(ml_dtypes.bfloat16)], axis=1)


@functools.lru_cache(maxsize=None)
def wave_table(length, count):
    slots = LANES // 4
    base = length // RADIX
    waves = []
    for residue in (1, 2, 3):
        waves.append(RADIX * np.arange(base) + residue)
    waves.append(RADIX * np.arange(base // 2))
    waves.append(RADIX * np.arange(base // 2) + RADIX // 2)
    waves = np.concatenate(waves)
    waves = np.where(waves == 0, length // 2, waves)
    waves = np.where(waves < length // 2, waves, waves - length).reshape(count, slots)
    return np.tile(waves, (1, 4)).astype(np.float32)


@functools.lru_cache(maxsize=None)
def band_tables(rows):
    across = np.zeros((4 * LANES, 2 * LANES))
    column = np.arange(2 * LANES)
    down = np.zeros((rows, rows))
    for index, weight in enumerate(whole_weights):
        distance = index + 1
        across[column + LANES + distance, column] = weight
        across[column + LANES - distance, column] = -weight
        down += weight * (np.eye(rows, k=distance) - np.eye(rows, k=-distance))
    return across.astype(ml_dtypes.bfloat16), down.astype(ml_dtypes.bfloat16)


def beside(*tables):
    high, low = halves(np.concatenate(tables, axis=1))
    return np.concatenate([high, low], axis=0)


def partner_order(count):
    half = count // 2
    return [mask for near in range(half) for mask in (near + half, near)]


def split(values):
    high = values.astype(BF16)
    return high, (values - high.astype(F32)).astype(BF16)


def dot(left, right):
    return jnp.dot(left, right, preferred_element_type=F32)


def exact_dot(left, right):
    left_high, left_low = left
    right_high, right_low = right
    return dot(left_high, right_high) + (dot(left_low, right_high) + dot(left_high, right_low))


def lane_index(shape):
    return lax.broadcasted_iota(jnp.int32, shape, len(shape) - 1)


def spin(values, shift):
    return pltpu.roll(values, shift % values.shape[-1], values.ndim - 1)


def lane_tile(values, index):
    return values[:, index * LANES : (index + 1) * LANES]


def x_parts(tables, base):
    wide = 2 * base
    full = (tables[:wide], tables[wide : 2 * wide])
    at = 2 * wide
    high, low = tables[at : at + base], tables[at + base : at + 2 * base]
    return full, (high[:, :base], low[:, :base]), (high[:, base:], low[:, base:])


def pieces_kernel(place, velocity, *pieces):
    rows = pieces[0].shape[1]
    for mask, piece in enumerate(pieces):
        start = pl.multiple_of((place[0] ^ mask) * rows, 8)
        for c in range(2):
            piece[c] = velocity[c, 0, pl.ds(start, rows), :]


def rows_kernel(top, low, top_wall, low_wall, top_flow, low_flow, first, last):
    small, width = top.shape[2], top_flow.shape[3]
    first[...] = jnp.zeros(first.shape, F32)
    last[...] = jnp.zeros(last.shape, F32)
    for k, (start, rows) in STRIP.items():
        lanes = slice(0, width) if k == PARTS + 1 else slice(None)
        if k < PARTS:
            upper, lower = top[k, 0].astype(F32)[:HALO], low[k, 0].astype(F32)[small - HALO :]
        elif k == PARTS:
            upper, lower = 1.0 - top_wall[0].astype(F32), 1.0 - low_wall[0].astype(F32)
        else:
            upper, lower = top_flow[0, 0], low_flow[0, 0]
        first[start : start + rows, lanes] = upper[:rows]
        last[start : start + rows, lanes] = lower[HALO - rows :]


def strip(ref, k, upper, lanes=slice(None)):
    if k not in STRIP:
        return jnp.zeros((HALO, ref[0:1, lanes].shape[1]), F32)
    start, rows = STRIP[k]
    values = ref[start : start + rows, lanes]
    blank = jnp.zeros((HALO - rows, values.shape[1]), F32)
    return jnp.concatenate([blank, values] if upper else [values, blank], axis=0)


def columns_kernel(
    has, left, right, left_wall, right_wall, left_flow, right_flow, above, below, to_right, to_left
):
    parts = left.shape[0]
    wide, flow_wide = above.shape[1], above.shape[1] // 2
    gap = jnp.zeros((LANES - 2 * HALO, LANES), F32)

    def tall(k, inner, first, sides):
        lanes = slice(first, first + LANES)
        over, under = strip(above, k, True, lanes), strip(below, k, False, lanes)
        return jnp.concatenate([inner, under * sides[1], gap, over * sides[0]], axis=0).T

    for k in range(parts + 1):
        at = slice(k * HALO, (k + 1) * HALO)
        if k < parts:
            near, far = left[k, 0].astype(F32), right[k, 0].astype(F32)
        else:
            near, far = 1.0 - left_wall[0].astype(F32), 1.0 - right_wall[0].astype(F32)
        sides = (has[2], has[3])
        to_left[at, :] = tall(k, near, 0, sides)[:HALO]
        to_right[at, :] = tall(k, far, wide - LANES, sides)[LANES - HALO :]
    k = parts + 1
    at = slice(k * HALO, (k + 1) * HALO)
    size = left_flow.shape[2] + LANES
    blank = jnp.zeros((HALO, to_left.shape[1] - size), F32)
    to_left[at, :size] = tall(k, left_flow[0, 0], 0, (1.0, 1.0))[:HALO]
    to_right[at, :size] = tall(k, right_flow[0, 0], flow_wide - LANES, (1.0, 1.0))[LANES - HALO :]
    to_left[at, size:] = blank
    to_right[at, size:] = blank


def sides_kernel(has, place, velocity, above, below, from_left, from_right, sides, squares, mark):
    parts, tall, _ = sides.shape
    gap = jnp.zeros((LANES - 2 * HALO, tall), F32)
    for k in range(parts):
        at = slice(k * HALO, (k + 1) * HALO)
        tile = [from_right[at, :] * has[1], gap, from_left[at, :] * has[0]]
        sides[k] = jnp.concatenate(tile, axis=0).T
    at = slice(parts * HALO, (parts + 1) * HALO)
    rows, local = velocity.shape[2:]
    size = rows + LANES
    tile = [from_right[at, :size], gap[:, :size], from_left[at, :size]]
    tile = jnp.concatenate(tile, axis=0).T
    tile = tile * tile
    mark[0] = place[0]
    over, under = (strip(ref, parts, ref is above, slice(0, local)) for ref in (above, below))
    squares[:HALO, :local] = over * over
    squares[HALO : HALO + rows, :local] = velocity[0, 0] * velocity[0, 0]
    squares[HALO + rows :, :local] = under * under
    squares[:HALO, local:] = tile[size - HALO :]
    squares[HALO : HALO + rows, local:] = tile[:rows]
    squares[HALO + rows :, local:] = tile[rows : rows + HALO]


def forward_x_kernel(groups, place, *refs):
    refs, (lines, made) = refs[:-2], refs[-2:]
    pieces, (tables, turns), outs, total = refs[:groups], refs[groups : groups + 2], refs[groups + 2 : -1], refs[-1]
    count, _, rows, local = lines.shape
    for mask, piece in enumerate(pieces):
        lines[place[0] ^ mask] = piece[...]
    base = turns.shape[1]
    per = local // base
    u = [lines[t // per, 0, :, (t % per) * base : (t % per + 1) * base] for t in range(RADIX)]
    v = [lines[t // per, 1, :, (t % per) * base : (t % per + 1) * base] for t in range(RADIX)]
    energy = sum(b * b for b in v)
    energy = jnp.sum(energy.reshape(rows // 8, 8, base), axis=0)
    total[...] = sum(energy[:, k : k + LANES] for k in range(0, base, LANES))
    fields = ([a * a - b * b for a, b in zip(u, v)], [2.0 * a * b for a, b in zip(u, v)])
    zeros, mids, reals, imags = [], [], [[], [], []], [[], [], []]
    for a in fields:
        s04, s26, s15, s37 = a[0] + a[4], a[2] + a[6], a[1] + a[5], a[3] + a[7]
        d04, d26, d15, d37 = a[0] - a[4], a[2] - a[6], a[1] - a[5], a[3] - a[7]
        zeros.append((s04 + s26) + (s15 + s37))
        mids.append((s04 + s26) - (s15 + s37))
        minus, plus = ROOT * (d15 - d37), ROOT * (d15 + d37)
        turned = (
            (d04 + minus, -d26 - plus),
            (s04 - s26, s37 - s15),
            (d04 - minus, d26 - plus),
        )
        for index, (real, imag) in enumerate(turned):
            c, s = turns[index : index + 1, :], turns[index + 3 : index + 4, :]
            reals[index].append(real * c + imag * s)
            imags[index].append(imag * c - real * s)
    stacked = jnp.concatenate(
        [
            jnp.concatenate([jnp.concatenate(reals[i], axis=0) for i in range(3)], axis=0),
            jnp.concatenate([jnp.concatenate(imags[i], axis=0) for i in range(3)], axis=0),
        ],
        axis=1,
    )
    full, zero, middle = x_parts(tables, base)
    full = exact_dot(split(stacked), full)
    zero = exact_dot(split(jnp.concatenate(zeros, axis=0)), zero)
    middle = exact_dot(split(jnp.concatenate(mids, axis=0)), middle)
    low = lane_index((rows, LANES)) % 64 < 32
    target = 0
    blocks = [full[2 * rows * i : 2 * rows * (i + 1)] for i in range(3)] + [zero, middle]
    for block in blocks:
        for first in range(0, block.shape[1], LANES):
            a = block[:rows, first : first + LANES]
            c = block[rows:, first : first + LANES]
            made[target] = jnp.where(low, a, spin(c, 32))
            made[target + 1] = jnp.where(low, spin(a, -32), c)
            target += 2
    for mask, out in zip(partner_order(len(outs)), outs):
        out[...] = made[place[1] ^ mask]


def eighths(x, turn):
    s04, s26, s15, s37 = x[0] + x[4], x[2] + x[6], x[1] + x[5], x[3] + x[7]
    d04, d26, d15, d37 = x[0] - x[4], x[2] - x[6], x[1] - x[5], x[3] - x[7]
    quarter = turn(s15 - s37)
    spun_26, spun_37 = turn(d26), turn(d37)
    one, three = d15 + spun_37, d15 - spun_37
    spun_one, spun_three = turn(one), turn(three)
    one = ROOT * (one + spun_one)
    three = ROOT * (spun_three - three)
    return [
        (s04 + s26) + (s15 + s37),
        (d04 + spun_26) + one,
        (s04 - s26) + quarter,
        (d04 - spun_26) + three,
        (s04 + s26) - (s15 + s37),
        (d04 + spun_26) - one,
        (s04 - s26) - quarter,
        (d04 - spun_26) - three,
    ]


def solve_y_kernel(count_x, _, place, *refs):
    *pieces, total, wave, both, turns, out, held, spread, made, lines, sent = refs
    count, rows, _ = lines.shape
    for mask, piece in zip(partner_order(count), pieces):
        lines[place[0] ^ mask] = piece[...]
    base = turns.shape[0]
    length = count * rows
    block = count_x * rows
    per = base // rows
    lanes = lane_index((base, LANES))
    sign = jnp.where(lanes < 64, 1.0, -1.0).astype(F32)

    def minus_i(z):
        return spin(z, 64) * sign

    def plus_i(z):
        return spin(z, 64) * -sign

    fields = [
        jnp.concatenate([lines[t * per + k] for k in range(per)], axis=0) for t in range(RADIX)
    ]
    mixed = eighths(fields, minus_i)
    terms, columns = turns.shape[1], 2 * RADIX
    picked = lax.broadcasted_iota(jnp.int32, (terms, columns * LANES), 0) % columns
    lane = lane_index(picked.shape)
    value = jnp.where((lane >= RADIX * LANES) & (lane % LANES >= 64), -1.0, 1.0)
    spread[...] = dot(turns[...], jnp.where(picked == lane // LANES, value, 0.0).astype(BF16))
    cosines = [spread[:, r * LANES : (r + 1) * LANES] for r in range(RADIX)]
    sines = [spread[:, (r + RADIX) * LANES : (r + RADIX + 1) * LANES] for r in range(RADIX)]
    mixed = [mixed[0]] + [
        mixed[r] * cosines[r] + spin(mixed[r], 64) * sines[r] for r in range(1, RADIX)
    ]
    tables = (both[: 2 * base], both[2 * base :])
    product = exact_dot(tables, split(jnp.concatenate(mixed, axis=1)))
    kx = wave[0:1, :]
    first = lanes % 64 < 32
    edge = jnp.float32(length // 2)
    alone = jnp.where(first, kx * kx, 0.0)
    slope = jnp.where(first | (kx == -edge), 0.0, jnp.broadcast_to(kx, lanes.shape))
    q = lax.broadcasted_iota(jnp.int32, lanes.shape, 0)
    low_ky = RADIX * (q - jnp.where(q < base // 2, 0, base)).astype(F32)
    terms = []
    for r in range(RADIX):
        at = slice(r * LANES, (r + 1) * LANES)
        spectrum = product[:base, at] + minus_i(product[base:, at])
        ky = low_ky + float(r)
        symbol = alone + slope * ky
        if r == 0:
            corner = jnp.where((kx == -edge) & ~first, edge * edge, 0.0)
            symbol = jnp.where(ky == -edge, jnp.where(first, alone, corner), symbol)
        terms.append(symbol * pl.reciprocal(kx * kx + ky * ky) * spectrum)
    pairs = [
        jnp.where(first, low + spin(low, -32), high + spin(high, 32))
        for low, high in zip(terms[:4], terms[4:])
    ]
    product = exact_dot(tables, split(jnp.concatenate(pairs, axis=1)))
    mixed = []
    for r in range(RADIX // 2):
        at = slice(r * LANES, (r + 1) * LANES)
        value = product[:base, at] + plus_i(product[base:, at])
        cosine = jnp.where(first, cosines[r], cosines[r + 4])
        sine = jnp.where(first, sines[r], sines[r + 4])
        value = value * cosine - spin(value, 64) * sine
        value = jnp.where(first, value + spin(value, -32), spin(value, 32) - value)
        if r == 2:
            value = jnp.where(first, value, plus_i(value))
        elif r:
            turned = plus_i(value)
            odd = value + turned if r == 1 else turned - value
            value = jnp.where(first, value, ROOT * odd)
        mixed.append(value)
    even, odd = mixed[0] + mixed[2], mixed[0] - mixed[2]
    side, turned = mixed[1] + mixed[3], plus_i(mixed[1] - mixed[3])
    for t, values in enumerate((even + side, odd + turned, even - side, odd - turned)):
        start = MARGIN + 2 * t * base
        held[start : start + base, :] = values
        held[start + base : start + 2 * base, :] = spin(values, -32)
    held[0:MARGIN, :] = held[length : length + MARGIN, :]
    held[length + MARGIN : length + 2 * MARGIN, :] = held[MARGIN : 2 * MARGIN, :]
    spare = total[...] + spin(total[...], 32)
    kept = rows + 2 * MARGIN // count_x
    half = made.shape[1]
    rest = kept - half
    low = lane_index((8, LANES)) % 64 < 32
    copies = []
    for target in range(count):
        start = (target // count_x) * block + (target % count_x) * kept
        for row in range(0, half, 8):
            a = held[start + row : start + row + 8, :]
            if row < rest:
                b = spin(held[start + half + row : start + half + row + 8, :], 32)
            else:
                b = spare
            made[target, row : row + 8, :] = jnp.where(low, a, b)
        if (target + 1) % RADIX == 0:
            group = pl.ds(target + 1 - RADIX, RADIX)
            copies.append(pltpu.make_async_copy(made.at[group], out.at[group], sent.at[len(copies)]))
            copies[-1].start()
    for copy in copies:
        copy.wait()


def inverse_x_kernel(
    kept, scale, place, lines, tables, turns, *refs
):
    *outs, held = refs
    count, half, _ = lines.shape
    base = turns.shape[1]
    length = RADIX * base
    rest = kept - half
    low = lane_index((half, LANES)) % 64 < 32
    groups, spare = [], None
    for first in range(0, count, 2):
        even, odd = lines[first], lines[first + 1]
        a = jnp.where(low, even, spin(odd, 32))
        b = jnp.where(low, spin(even, -32), odd)
        groups.append(jnp.concatenate([a, b[:rest]], axis=0))
        extra = b[rest : rest + 8]
        spare = extra if spare is None else spare + extra
    mean = jnp.sum(spare) * scale
    wide = 2 * base // LANES
    narrow = base // LANES
    stacked = jnp.concatenate(
        [jnp.concatenate(groups[i * wide : (i + 1) * wide], axis=1) for i in range(3)], axis=0
    )
    at = 3 * wide
    zeros = jnp.concatenate(groups[at : at + narrow], axis=1)
    mids = jnp.concatenate(groups[at + narrow : at + 2 * narrow], axis=1)
    full, zero, middle = x_parts(tables, base)
    full = exact_dot(split(stacked), full)
    zero = exact_dot(split(zeros), zero) * scale
    mid = exact_dot(split(mids), middle) * scale
    turned = []
    for i in range(3):
        real = full[i * kept : (i + 1) * kept, :base]
        imag = full[i * kept : (i + 1) * kept, base:]
        c = turns[i : i + 1, :] * (2.0 * scale)
        s = turns[i + 3 : i + 4, :] * (2.0 * scale)
        turned.append((real * c - imag * s, real * s + imag * c))
    for t in range(RADIX):
        value = zero + mid if t % 2 == 0 else zero - mid
        for i, (real, imag) in enumerate(turned):
            eighth = t * (i + 1) % RADIX
            c = (1.0, ROOT, 0.0, -ROOT, -1.0, -ROOT, 0.0, ROOT)[eighth]
            s = (0.0, ROOT, 1.0, ROOT, 0.0, -ROOT, -1.0, -ROOT)[eighth]
            if c:
                value = value + c * real
            if s:
                value = value - s * imag
        held[:, t * base : (t + 1) * base] = mean - value
    targets, local = len(outs), outs[0].shape[1] - LANES
    right = lane_index((kept, LANES)) < 64
    for mask, out in enumerate(outs):
        start = pl.multiple_of((place[0] ^ mask) * local, LANES)
        after = pl.multiple_of(jnp.where(start + local == length, 0, start + local), LANES)
        before = pl.multiple_of(jnp.where(start == 0, length, start) - LANES, LANES)
        out[:, :local] = held[:, pl.ds(start, local)]
        out[:, local:] = jnp.where(
            right, held[:, pl.ds(after, LANES)], held[:, pl.ds(before, LANES)]
        )


def slopes_x(parts, band, with_edge):
    tiles = parts[0].shape[-1] // LANES
    pieces = []
    for first in list(range(0, tiles - 1, 2)) + ([tiles - 1] if with_edge else []):
        steps = (-1, 0, 1, 2) if first < tiles - 1 else (-1, 0, 1)
        table = band[...] if first < tiles - 1 else band[: 3 * LANES, :LANES]
        order = [(first + step) % tiles for step in steps]
        piece = None
        for part in parts:
            term = dot(jnp.concatenate([lane_tile(part, t) for t in order], axis=1), table)
            piece = term if piece is None else piece + term
        pieces.append(piece)
    return jnp.concatenate(pieces, axis=1)


def slope_y(read):
    value = read(3) - read(-3)
    for index in (0, 1):
        value = value + whole_weights[index] * (read(index + 1) - read(-index - 1))
    return value


def edged(k, side, center, up, down, above, below, sides, has, first=0):
    step = pl.program_id(0) + first
    tile, width = center.shape
    tall = sides.shape[1]
    last = (tall - LANES) // tile - 1
    base = pl.multiple_of(step * tile, 8)
    before = pl.multiple_of(jnp.where(step == 0, tall, base) - HALO, 8)
    over = jnp.where(step == 0, strip(above, k, True) * has[2], up)
    under = jnp.where(step == last, strip(below, k, False) * has[3], down)
    rows = (
        (over, sides[side, pl.ds(before, HALO), :]),
        (center, sides[side, pl.ds(base, tile), :]),
        (under, sides[side, pl.ds(pl.multiple_of(base + tile, 8), HALO), :]),
    )
    return jnp.concatenate([jnp.concatenate(pair, axis=1) for pair in rows], axis=0)


def edged_open(k, side, wall, wall_up, wall_down, above, below, sides, has, first=0):
    open_cells = [1.0 - ref[0].astype(F32) for ref in (wall, wall_up, wall_down)]
    return edged(k, side, *open_cells, above, below, sides, has, first)


def quiet_step_kernel(
    first, has, place, center, up, down, wall, wall_up, wall_down, above, below, sides, across, along, along_inner, calm, density, shown_open, mark
):
    parts, _, tile, width = center.shape
    high = tile + 2 * HALO
    opened = edged_open(parts, parts, wall, wall_up, wall_down, above, below, sides, has, first)
    values = []
    for k in range(parts):
        value = edged(
            k,
            k,
            center[k, 0].astype(F32),
            up[k, 0].astype(F32)[up.shape[2] - HALO :],
            down[k, 0].astype(F32)[:HALO],
            above,
            below,
            sides,
            has,
            first,
        )
        values.append(value)

    def drops(x, along_b, along_p):
        diverge = x[1] + along_b
        return (
            diverge + mean_flow * x[0],
            x[3] + mean_flow * x[1],
            along_p + mean_flow * x[2],
            diverge + mean_flow * x[3],
        )

    short = [value.astype(BF16) for value in values]
    x = slopes_x((jnp.concatenate(short, axis=0),), across, True)
    x = [x[k * high : (k + 1) * high] for k in range(parts)]
    table = along[...]
    dropped = drops(x, dot(table, short[2]), dot(table, short[3]))
    middle = [opened * (v - (time_step / 60.0) * d) for v, d in zip(values, dropped)]
    inner = slice(HALO, HALO + tile)
    x = slopes_x(split(jnp.concatenate([value[inner] for value in middle], axis=0)), across, False)
    x = [x[k * tile : (k + 1) * tile] for k in range(parts)]
    table = along_inner[...]
    y = [sum(dot(table, part) for part in split(middle[k][:, :width])) for k in (2, 3)]
    dropped = drops(x, *y)
    shown = opened[inner, :width]
    for k in range(parts):
        start = 0.5 * values[k][inner, :width] - (0.5 * time_step / 60.0) * dropped[k]
        value = shown * start + 0.5 * middle[k][inner, :width]
        if k == 0:
            density[0, 0] = value.astype(BF16)
        else:
            calm[k - 1] = value
    shown_open[0] = opened.astype(BF16)
    mark[0] = place[0]


def tables_kernel(place, weights_x, weights_y, rise_x, rise_y, mark):
    mark[0] = place[0]
    tiles, reach_x, lanes = rise_x.shape
    wide, length_x = (tiles - 1) * lanes, weights_x.shape[1]
    first = place[0] * wide
    half = LANES // 2

    def weights(ref, start, size):
        length = ref.shape[1]
        start = jnp.where(start < 0, start + length, jnp.where(start >= length, start - length, start))
        return ref[:, pl.ds(pl.multiple_of(start, LANES), size)]

    cells = lax.broadcasted_iota(jnp.int32, (reach_x, lanes), 0)
    fine = lax.broadcasted_iota(jnp.int32, (reach_x, lanes), 1)
    right, left = weights(weights_x, first + wide, LANES), weights(weights_x, first - LANES, LANES)
    edge = jnp.where(lane_index(right.shape) < half, right, left)
    edge = jnp.concatenate([edge, edge], axis=1)
    for k in range(tiles):
        own = weights(weights_x, first + k * lanes, lanes) if k < tiles - 1 else edge
        target = fine // 2 - 1
        if k == tiles - 1:
            target = jnp.where(fine < half, target, target + half)
        value = jnp.zeros(fine.shape, F32)
        for t in range(4):
            value = jnp.where(cells == (target + t) % reach_x, own[t : t + 1, :], value)
        rise_x[k] = value
    steps, high, reach = rise_y.shape
    tall = steps * TILE
    first = place[1] * tall
    own = [weights(weights_y, first + k * LANES, LANES) for k in range(-1, tall // LANES + 1)]
    own = jnp.concatenate([jnp.concatenate(own, axis=1), jnp.zeros((4, tall + 2 * LANES), F32)], axis=0).T
    cells = lax.broadcasted_iota(jnp.int32, (high, reach), 1) % (reach // 3)
    target = lax.broadcasted_iota(jnp.int32, (high, reach), 0) // 2 + (HALO // 2 - 1)
    for k in range(steps):
        start = LANES - HALO + k * TILE
        value = jnp.zeros((high, reach), F32)
        for t in range(4):
            value = jnp.where(cells == target + t, own[start : start + high, t : t + 1], value)
        rise_y[k] = value


def source_kernel(place, squares, opened, rise_x, rise_y, quiet, across, _, *refs):
    *lines, out, squared, cells_open, matrix, rows_matrix, calm, band, held, raised, forced, done, fetched, kept = refs
    steps = done.shape[0]
    tile, width = calm.shape[2:]
    high = tile + 2 * HALO
    rows = lines[0].shape[0]

    def tile_copies(k):
        part = quiet.at[:, pl.ds(k * tile, tile), :]
        return (
            pltpu.make_async_copy(part, calm.at[k % 2], fetched.at[k % 2]),
            pltpu.make_async_copy(opened.at[k], cells_open.at[k % 2], fetched.at[2 + k % 2]),
        )

    def done_copy(k):
        part = out.at[1:, 0, pl.ds(k * tile, tile), :]
        return pltpu.make_async_copy(done.at[k], part, kept.at[k])

    arrays = ((squares, squared), (rise_x, matrix), (rise_y, rows_matrix), (across, band))
    copies = [
        pltpu.make_async_copy(source, target, fetched.at[4 + k])
        for k, (source, target) in enumerate(arrays)
    ]
    pieces = [
        pltpu.make_async_copy(
            piece,
            held.at[pl.ds(pl.multiple_of((place[0] ^ mask) * rows, 8), rows), :],
            fetched.at[4 + len(arrays) + mask],
        )
        for mask, piece in enumerate(lines)
    ]
    for copy in (*pieces, *copies, *tile_copies(0), *tile_copies(1)):
        copy.start()
    for copy in pieces + copies[:1]:
        copy.wait()

    level = held[MARGIN - HALO : MARGIN - HALO + squared.shape[0], :] - squared[...]
    count = level.shape[1] // LANES
    near = lane_index((level.shape[0], LANES)) < 64
    around = []
    for k in range(count):
        after, before = lane_tile(level, (k + 1) % count), lane_tile(level, (k - 1) % count)
        around.append(split(jnp.concatenate([lane_tile(level, k), jnp.where(near, after, before)], axis=1)))
    copies[1].wait()
    for k in range(count):
        lanes = 2 * LANES if k < count - 1 else LANES
        value = split(exact_dot(around[k], split(matrix[k][:, :lanes])))
        for part in range(2):
            raised[part, :, 2 * k * LANES : 2 * k * LANES + lanes] = value[part]
    for copy in copies[2:]:
        copy.wait()

    reach = rows_matrix.shape[2] // 3
    third = lane_index((high, 3 * reach)) >= 2 * reach
    for k in range(steps):
        start = k * (tile // 2)
        window = [raised[part, start : start + reach, :] for part in (0, 1, 0)]
        weights = split(rows_matrix[k])
        weights = jnp.where(third, weights[1], weights[0])
        calm_here, open_here = tile_copies(k)
        open_here.wait()
        free = time_step * cells_open[k % 2].astype(F32)
        value = free * dot(weights, jnp.concatenate(window, axis=0))
        forced[k % 2] = value
        inner = value[HALO : HALO + tile]
        shown = (0.5 / 60.0) * free[HALO : HALO + tile, :width]
        x = shown * slopes_x(split(inner), band, False)
        y = shown * slope_y(lambda d: forced[k % 2, HALO + d : HALO + d + tile, :width])
        calm_here.wait()
        still = calm.at[k % 2]
        done[k, 0] = (still[0] - x).astype(BF16)
        done[k, 1] = (still[1] - y).astype(BF16)
        done[k, 2] = (still[2] + inner[:, :width] - mean_flow * x).astype(BF16)
        done_copy(k).start()
        if k + 2 < steps:
            for copy in tile_copies(k + 2):
                copy.start()
    for k in range(steps):
        done_copy(k).wait()


def call(
    kernel, operands, outs, scratch=(), steps=0, specs=None, out_specs=None, after=(), aliases=None, megabytes=24, flops=0, moved=0, name=None
):
    count = len(operands)

    def body(*refs):
        kernel(*refs[:count], *refs[count + len(after) :])

    def whole(array):
        zeros = (0,) * len(array.shape)
        return pl.BlockSpec(array.shape, lambda *_: zeros)

    arguments = {}
    chosen = specs or {}
    if steps:
        arguments["grid"] = (steps,)
        in_specs = [chosen.get(i, whole(o)) for i, o in enumerate(operands)]
        arguments["out_specs"] = jax.tree.map(whole, outs) if out_specs is None else out_specs
    else:
        local = pl.BlockSpec(memory_space=pltpu.VMEM)
        in_specs = [chosen.get(i, local) for i in range(count)]
        if out_specs is not None:
            arguments["out_specs"] = out_specs
    return pl.pallas_call(
        body,
        out_shape=outs,
        in_specs=in_specs + [pl.BlockSpec(memory_space=pl.ANY)] * len(after),
        scratch_shapes=list(scratch),
        input_output_aliases=aliases or {},
        compiler_params=pltpu.CompilerParams(vmem_limit_bytes=megabytes << 20),
        cost_estimate=pl.CostEstimate(flops=flops, bytes_accessed=moved, transcendentals=0),
        name=name,
        **arguments,
    )(*operands, *after)


def ring(array, axis, step):
    size = lax.axis_size(axis)
    return lax.ppermute(array, axis, [(i, (i + step) % size) for i in range(size)])


def swap(array, axis, mask):
    return lax.ppermute(array, axis, [(i, i ^ mask) for i in range(lax.axis_size(axis))])


def shaped(*shape, kind=F32):
    return jax.ShapeDtypeStruct(shape, kind)


def pressure_lines(pieces, place_x, gathered, spread, stepped):
    _, rows, local_x = pieces[0].shape
    count_x, count_y = lax.axis_size("gx"), lax.axis_size("gy")
    count = count_x * count_y
    scalars = {0: pl.BlockSpec(memory_space=pltpu.SMEM)}
    length_x, length_y = local_x * count_x, rows * count
    full, zero, middle, cos_turn, sin_turn = x_tables(length_x)
    turns = np.zeros((8, cos_turn.shape[1]), np.float32)
    turns[0:3], turns[3:6] = cos_turn, sin_turn
    place = lax.axis_index("gy") * count_x + lax.axis_index("gx")
    both_places = jnp.concatenate([place_x, place.astype(jnp.int32).reshape(1)])
    *spectra, total = call(
        functools.partial(forward_x_kernel, len(pieces)),
        (both_places, *pieces, np.concatenate([beside(full), beside(zero, middle)]), turns),
        (shaped(rows, LANES),) * count + (shaped(8, LANES),),
        (
            pltpu.VMEM((count_x, 2, rows, local_x), F32),
            pltpu.VMEM((count, rows, LANES), F32),
        ),
        specs=scalars,
        after=gathered,
        flops=10**9,
        moved=4 << 20,
        name="forward_x",
    )
    spectra = [
        swap(piece, ("gx", "gy"), mask % count_x * count_y + mask // count_x) if mask else piece
        for mask, piece in zip(partner_order(count), spectra)
    ]
    waves = jnp.asarray(wave_table(length_x, count))
    wave = lax.dynamic_slice(waves, (place, 0), (1, LANES))
    both, turns_y = y_tables(length_y)
    kept = rows + 2 * MARGIN // count_x
    half = (kept // 2 + 8) // 8 * 8
    solved = call(
        functools.partial(solve_y_kernel, count_x),
        (spread, both_places[1:], *spectra, total, wave, beside(both), turns_y),
        shaped(count, half, LANES),
        (
            pltpu.VMEM((length_y + 2 * MARGIN, LANES), F32),
            pltpu.VMEM((length_y // RADIX, 2 * RADIX * LANES), F32),
            pltpu.VMEM((count, half, LANES), F32),
            pltpu.VMEM((count, rows, LANES), F32),
            pltpu.SemaphoreType.DMA((count // RADIX,)),
        ),
        specs={**scalars, 1: scalars[0]},
        out_specs=pl.BlockSpec(memory_space=pl.ANY),
        flops=4 * 10**9,
        moved=6 << 20,
        name="solve_y",
    )
    solved = lax.all_to_all(solved, ("gy", "gx"), 0, 0, tiled=True)
    back = 2.0 * zero.T
    back[LANES // 2] *= 0.5
    tables = np.concatenate(
        [beside(full.T), beside(back, 2.0 * middle.T)]
    )
    pressed = call(
        functools.partial(inverse_x_kernel, kept, 1.0 / (length_x * length_y)),
        (stepped, solved, tables, turns),
        (shaped(kept, local_x + LANES),) * count_x,
        (pltpu.VMEM((kept, length_x), F32),),
        specs=scalars,
        flops=10**9,
        moved=4 << 20,
        name="inverse_x",
    )
    return [piece if mask == 0 else swap(piece, "gx", mask) for mask, piece in enumerate(pressed)]


def fast_shards(velocity, weights_x, weights_y, acoustic, wall_mask):
    parts, _, tall, wide = acoustic.shape
    _, _, local_y, local_x = velocity.shape
    count_x, count_y = lax.axis_size("gx"), lax.axis_size("gy")
    place_x, place_y = lax.axis_index("gx"), lax.axis_index("gy")
    full, high, steps = wide + LANES, TILE + 2 * HALO, tall // TILE
    strips = (parts + 2) * HALO
    small = 2 * HALO
    has = jnp.stack([place_x > 0, place_x < count_x - 1, place_y > 0, place_y < count_y - 1])
    has = has.astype(F32)
    scalars = pl.BlockSpec(memory_space=pltpu.SMEM)

    def at(block, *index):
        return pl.BlockSpec(block, lambda i: index)

    own = place_x.astype(jnp.int32).reshape(1)
    sent = call(
        pieces_kernel,
        (own, velocity),
        (shaped(2, local_y // count_x, local_x),) * count_x,
        specs={0: scalars},
        moved=2 << 20,
        megabytes=8,
        name="pieces",
    )
    moved = [piece if mask == 0 else swap(piece, "gx", mask) for mask, piece in enumerate(sent)]
    first, last = call(
        rows_kernel,
        (acoustic, acoustic, wall_mask, wall_mask, velocity, velocity),
        (shaped(STRIP_ROWS, wide),) * 2,
        steps=1,
        specs={
            0: at((parts, 1, small, wide), 0, 0, 0, 0),
            1: at((parts, 1, small, wide), 0, 0, tall // small - 1, 0),
            2: at((1, HALO, wide), 0, 0, 0),
            3: at((1, HALO, wide), 0, tall // HALO - 1, 0),
            4: at((1, 1, HALO, local_x), 1, 0, 0, 0),
            5: at((1, 1, HALO, local_x), 1, 0, local_y // HALO - 1, 0),
        },
        after=moved[1:2],
        moved=2 << 20,
        megabytes=50,
        name="rows",
    )
    above, below = ring(last, "gy", 1), ring(first, "gy", -1)
    to_right, to_left = call(
        columns_kernel,
        (has, acoustic, acoustic, wall_mask, wall_mask, velocity, velocity, above, below),
        (shaped(strips, tall + LANES), shaped(strips, tall + LANES)),
        steps=1,
        specs={
            0: scalars,
            1: at((parts, 1, tall, LANES), 0, 0, 0, 0),
            2: at((parts, 1, tall, LANES), 0, 0, 0, wide // LANES - 1),
            3: at((1, tall, LANES), 0, 0, 0),
            4: at((1, tall, LANES), 0, 0, wide // LANES - 1),
            5: at((1, 1, local_y, LANES), 1, 0, 0, 0),
            6: at((1, 1, local_y, LANES), 1, 0, 0, local_x // LANES - 1),
        },
        moved=8 << 20,
        megabytes=54,
        name="columns",
    )
    from_left, from_right = ring(to_right, "gx", 1), ring(to_left, "gx", -1)
    local_memory = pl.BlockSpec(memory_space=pltpu.VMEM)
    tiles = wide // (2 * LANES) + 1
    rise_x, rise_y, listed = call(
        tables_kernel,
        (jnp.stack([place_x, place_y]).astype(jnp.int32), weights_x, weights_y),
        (
            shaped(tiles, 2 * LANES, 2 * LANES),
            shaped(steps, high, 3 * (high // 2 + HALO)),
            shaped(1, kind=jnp.int32),
        ),
        specs={0: scalars},
        out_specs=(local_memory, local_memory, scalars),
        moved=4 << 20,
        megabytes=54,
        name="tables",
    )
    sides, squares, beside = call(
        sides_kernel,
        (has, listed, velocity, above, below, from_left, from_right),
        (
            shaped(parts + 1, tall + LANES, LANES),
            shaped(local_y + 2 * HALO, local_x + LANES),
            shaped(1, kind=jnp.int32),
        ),
        steps=1,
        specs={0: scalars, 1: scalars, 2: at((1, 1, local_y, local_x), 1, 0, 0, 0)},
        out_specs=(
            at((parts + 1, tall + LANES, LANES), 0, 0, 0),
            at((local_y + 2 * HALO, local_x + LANES), 0, 0),
            scalars,
        ),
        moved=8 << 20,
        megabytes=54,
        name="sides",
    )
    across, along = band_tables(high)
    along_inner = along[HALO : HALO + TILE]
    per, rows = TILE // small, TILE // HALO

    def tiled(first):
        walls = (
            pl.BlockSpec((1, TILE, wide), lambda i: (0, i + first, 0)),
            pl.BlockSpec((1, HALO, wide), lambda i: (0, jnp.maximum((i + first) * rows - 1, 0), 0)),
            pl.BlockSpec(
                (1, HALO, wide),
                lambda i: (0, jnp.minimum((i + first + 1) * rows, steps * rows - 1), 0),
            ),
        )
        cells = (
            pl.BlockSpec((parts, 1, TILE, wide), lambda i: (0, 0, i + first, 0)),
            pl.BlockSpec(
                (parts, 1, small, wide), lambda i: (0, 0, jnp.maximum((i + first) * per - 1, 0), 0)
            ),
            pl.BlockSpec(
                (parts, 1, small, wide),
                lambda i: (0, 0, jnp.minimum((i + first + 1) * per, steps * per - 1), 0),
            ),
        )
        return cells, walls

    def quiet_tiles(first, count, before):
        cells, walls = tiled(first)
        operands = (has, own, acoustic, acoustic, acoustic, wall_mask, wall_mask, wall_mask, above, below, sides)
        operands = operands + (across, along, along_inner)
        return call(
            functools.partial(quiet_step_kernel, first),
            operands,
            (
                shaped(parts - 1, tall, wide),
                shaped(*acoustic.shape, kind=BF16),
                shaped(steps, high, full, kind=BF16),
                shaped(1, kind=jnp.int32),
            ),
            steps=count,
            specs=dict(enumerate((scalars, scalars) + cells + walls)),
            out_specs=(
                pl.BlockSpec((parts - 1, TILE, wide), lambda i: (0, i + first, 0)),
                pl.BlockSpec((1, 1, TILE, wide), lambda i: (0, 0, i + first, 0)),
                pl.BlockSpec((1, high, full), lambda i: (i + first, 0, 0)),
                scalars,
            ),
            after=before,
            aliases={len(operands) + k: k for k in range(len(before))},
            megabytes=54,
            flops=3 * 10**9 * count,
            moved=(12 << 20) * count,
            name="quiet_step",
        )

    early = max(steps * 3 // 4, 1)
    *begun, stepped = quiet_tiles(0, early, ())
    if early < steps:
        *begun, _ = quiet_tiles(early, steps - early, begun)
    quiet, final, opened = begun
    lines = pressure_lines(moved, own, (above, below), beside, stepped)
    operands = (own, squares, opened, rise_x, rise_y, quiet, across, final, *lines)
    anywhere = pl.BlockSpec(memory_space=pl.ANY)
    specs = {k: anywhere for k in range(1, len(operands))}
    scratch = (
        pltpu.VMEM(squares.shape, F32),
        pltpu.VMEM((2,) + opened.shape[1:], BF16),
        pltpu.VMEM(rise_x.shape, F32),
        pltpu.VMEM(rise_y.shape, F32),
        pltpu.VMEM((2, parts - 1, TILE, wide), F32),
        pltpu.VMEM(across.shape, BF16),
        pltpu.VMEM((local_y + 2 * MARGIN, local_x + LANES), F32),
        pltpu.VMEM((2, local_y + 2 * HALO, full), BF16),
        pltpu.VMEM((2, high, full), F32),
        pltpu.VMEM((steps, parts - 1, TILE, wide), BF16),
        pltpu.SemaphoreType.DMA((8 + count_x,)),
        pltpu.SemaphoreType.DMA((steps,)),
    )
    return call(
        source_kernel,
        operands,
        shaped(*acoustic.shape, kind=BF16),
        scratch,
        specs={0: scalars, **specs},
        out_specs=anywhere,
        aliases={7: 0},
        megabytes=56,
        flops=4 * 10**9,
        moved=16 << 20,
        name="source_step",
    )


def fits(count_x, count_y, velocity, acoustic):
    _, planes, local_y, local_x = velocity
    _, _, tall, wide = acoustic
    length_x, length_y = local_x * count_x, local_y * count_y
    rows = local_y // count_x
    base_x, base_y = length_x // RADIX, length_y // RADIX
    return (
        planes == 1
        and acoustic[0] == PARTS
        and length_x * 2 == count_x * count_y * LANES
        and base_x % (2 * LANES) == 0
        and local_x % base_x == 0
        and rows % 8 == 0
        and base_y % rows == 0
        and base_y % 8 == 0
        and count_x * count_y % RADIX == 0
        and MARGIN * 2 % (8 * count_x) == 0
        and tall == 2 * local_y
        and wide == 2 * local_x
        and tall % TILE == 0
        and tall % LANES == 0
        and tall >= 2 * TILE
        and count_x & (count_x - 1) == 0
        and count_y & (count_y - 1) == 0
        and wide % (2 * LANES) == 0
    )


def extended(array, sides, width):
    for axis, dim in sides:
        size, length = (lax.axis_size(axis), array.shape[dim])
        up = [(i, (i + 1) % size) for i in range(size - 1)]
        down = [(j, i) for i, j in up]
        last = lax.slice_in_dim(array, length - width, length, axis=dim)
        leading = lax.slice_in_dim(array, 0, width, axis=dim)
        before = lax.ppermute(last, axis, up)
        after = lax.ppermute(leading, axis, down)
        array = jnp.concatenate([before, array, after], axis=dim)
    return array


def gradients(padded):
    height = padded.shape[-2] - 6
    breadth = padded.shape[-1] - 6
    rows_mid = padded[..., 3 : 3 + height, :]
    cols_mid = padded[..., :, 3 : 3 + breadth]
    along_x = jnp.zeros_like(padded[..., 3 : 3 + height, 3 : 3 + breadth])
    along_y = jnp.zeros_like(along_x)
    for index, weight in enumerate(stencil_weights):
        distance = index + 1
        along_x = along_x + weight * (
            rows_mid[..., 3 + distance : 3 + distance + breadth]
            - rows_mid[..., 3 - distance : 3 - distance + breadth]
        )
        along_y = along_y + weight * (
            cols_mid[..., 3 + distance : 3 + distance + height, :]
            - cols_mid[..., 3 - distance : 3 - distance + height, :]
        )
    return (along_x, along_y)


def tendency(padded, source):
    along_x, along_y = gradients(padded)
    diverge = along_x[1] + along_y[2]
    forcing = jnp.stack([-diverge, -along_x[3], -along_y[3], source - diverge])
    return forcing - mean_flow * along_x


def spectral_index(flat, length):
    second = length // 16
    wave = flat // second + 16 * (flat % second)
    return jnp.where(wave < length // 2, wave, wave - length).astype(jnp.float32)


def twiddles(rows_count, cols_count, modulus, sign):
    products = jnp.arange(rows_count)[:, None] * jnp.arange(cols_count)[None, :] % modulus
    angles = 2.0 * math.pi / modulus * products.astype(jnp.float32)
    return (jnp.cos(angles), sign * jnp.sin(angles))


def mix_rows(real_part, imag_part, cosine, sine):
    exact = lax.Precision.HIGHEST
    cos_real = jnp.einsum("ka,...ab->...kb", cosine, real_part, precision=exact)
    cos_imag = jnp.einsum("ka,...ab->...kb", cosine, imag_part, precision=exact)
    sin_real = jnp.einsum("ka,...ab->...kb", sine, real_part, precision=exact)
    sin_imag = jnp.einsum("ka,...ab->...kb", sine, imag_part, precision=exact)
    return (cos_real - sin_imag, cos_imag + sin_real)


def mix_cols(real_part, imag_part, cosine, sine):
    exact = lax.Precision.HIGHEST
    cos_real = jnp.einsum("...kb,bc->...kc", real_part, cosine, precision=exact)
    cos_imag = jnp.einsum("...kb,bc->...kc", imag_part, cosine, precision=exact)
    sin_real = jnp.einsum("...kb,bc->...kc", real_part, sine, precision=exact)
    sin_imag = jnp.einsum("...kb,bc->...kc", imag_part, sine, precision=exact)
    return (cos_real - sin_imag, cos_imag + sin_real)


def rotate(real_part, imag_part, cosine, sine):
    return (real_part * cosine - imag_part * sine, real_part * sine + imag_part * cosine)


def discrete(real_part, imag_part, sign):
    length = real_part.shape[-1]
    second = length // 16
    initial = real_part.shape
    folded = initial[:-1] + (16, second)
    real_part = real_part.reshape(folded)
    imag_part = imag_part.reshape(folded)
    small_cos, small_sin = twiddles(16, 16, 16, sign)
    large_cos, large_sin = twiddles(second, second, second, sign)
    turn_cos, turn_sin = twiddles(16, second, length, sign)
    if sign < 0:
        real_part, imag_part = mix_rows(real_part, imag_part, small_cos, small_sin)
        real_part, imag_part = rotate(real_part, imag_part, turn_cos, turn_sin)
        real_part, imag_part = mix_cols(real_part, imag_part, large_cos, large_sin)
    else:
        real_part, imag_part = mix_cols(real_part, imag_part, large_cos, large_sin)
        real_part, imag_part = rotate(real_part, imag_part, turn_cos, turn_sin)
        real_part, imag_part = mix_rows(real_part, imag_part, small_cos, small_sin)
        real_part = real_part / length
        imag_part = imag_part / length
    return (real_part.reshape(initial), imag_part.reshape(initial))


def transform(stacked, sign, kind):
    if kind == "real_in":
        real_part = stacked
        imag_part = jnp.zeros_like(stacked)
    else:
        half = stacked.shape[0] // 2
        real_part = stacked[:half]
        imag_part = stacked[half:]
    real_out, imag_out = discrete(real_part, imag_part, sign)
    if kind == "real_out":
        return real_out
    return jnp.concatenate([real_out, imag_out], axis=0)


def project(stacked, wave_x, wave_y):
    coef_xx = wave_x * wave_x
    coef_xy = 2.0 * wave_x * wave_y
    coef_yy = wave_y * wave_y
    denominator = wave_x * wave_x + wave_y * wave_y
    positive = denominator > 0
    safe = jnp.where(positive, denominator, 1.0)

    def combine(parts):
        numerator = -(coef_xx * parts[0] + coef_xy * parts[1] + coef_yy * parts[2])
        return jnp.where(positive, numerator / safe, 0.0)

    return jnp.stack([combine(stacked[:3]), combine(stacked[3:])])


def refine(stacked, weights):
    result = jnp.zeros(stacked.shape[:-1] + (2 * stacked.shape[-1],), jnp.float32)
    for offset in range(4):
        result = (
            result
            + jnp.repeat(jnp.roll(stacked, 1 - offset, axis=-1), 2, axis=-1) * weights[offset]
        )
    return result


def lines_x(stacked, action):
    gathered = action(lax.all_to_all(stacked, "gx", split_axis=2, concat_axis=3, tiled=True))
    return lax.all_to_all(gathered, "gx", split_axis=3, concat_axis=2, tiled=True)


def lines_y(stacked, action):
    turned = jnp.swapaxes(stacked, 2, 3)
    gathered = action(lax.all_to_all(turned, "gy", split_axis=2, concat_axis=3, tiled=True))
    returned = lax.all_to_all(gathered, "gy", split_axis=3, concat_axis=2, tiled=True)
    return jnp.swapaxes(returned, 2, 3)


def expand(fields):
    return extended(fields, (("gx", 3), ("gy", 2)), 3)


def shards(velocity, weights_x, weights_y, acoustic, wall_mask):
    acoustic = acoustic.astype(jnp.float32)
    flow_x = velocity[0]
    flow_y = velocity[1]
    tensor = jnp.stack([flow_x * flow_x, flow_x * flow_y, flow_y * flow_y])
    count_gx = lax.axis_size("gx")
    count_gy = lax.axis_size("gy")
    place_x = lax.axis_index("gx")
    place_y = lax.axis_index("gy")
    local_y = tensor.shape[2]
    local_x = tensor.shape[3]
    length_x = local_x * count_gx
    length_y = local_y * count_gy

    def forward_real(portion):
        return transform(portion, -1, "real_in")

    def finish_x(portion):
        return refine(transform(portion, 1, "real_out"), weights_x)

    spectra = lines_x(tensor, forward_real)
    share_x = local_x // count_gy
    line_x = spectral_index(place_x * local_x + place_y * share_x + jnp.arange(share_x), length_x)[
        :, None
    ]
    line_y = spectral_index(jnp.arange(length_y), length_y)[None, :]

    def solve_y(portion):
        solved = project(transform(portion, -1, "complex"), line_x, line_y)
        return refine(transform(solved, 1, "complex"), weights_y)

    pressure = lines_y(spectra, solve_y)
    source = lines_x(pressure, finish_x)[0]
    open_cells = (1 - wall_mask).astype(jnp.float32)
    first_rate = tendency(expand(acoustic), source)
    middle = open_cells * (acoustic + time_step * first_rate)
    second_rate = tendency(expand(middle), source)
    return (open_cells * (acoustic + 0.5 * time_step * (first_rate + second_rate))).astype(
        jnp.bfloat16
    )


def solution(mesh):
    in_specs = (P(None, None, "gy", "gx"), P(), P(), P(None, None, "gy", "gx"), P(None, "gy", "gx"))
    out_specs = P(None, None, "gy", "gx")

    def chosen(velocity, weights_x, weights_y, acoustic, wall_mask):
        sizes = (mesh.shape["gx"], mesh.shape["gy"], velocity.shape, acoustic.shape)
        plan = fast_shards if fits(*sizes) else shards
        return plan(velocity, weights_x, weights_y, acoustic, wall_mask)

    return jax.shard_map(
        chosen, mesh=mesh, in_specs=in_specs, out_specs=out_specs, check_vma=False
    )
```

```python
import functools
import math

import jax
import jax.numpy as jnp
import ml_dtypes
import numpy as np
from jax import lax
from jax.experimental import pallas as pl
from jax.experimental.pallas import tpu as pltpu
from jax.sharding import PartitionSpec as P

stencil_weights = (0.75, -0.15, 1.0 / 60.0)
mean_flow = 0.3
time_step = 0.5
whole_weights = (45.0, -9.0, 1.0)

LANES = 128
RADIX = 8
HALO = 8
MARGIN = 16
TILE = 128
ROOT = math.sqrt(0.5)
STRIP = {2: (0, 6), 3: (6, 6), 1: (12, 3), 4: (15, 3), 5: (20, 4)}
STRIP_ROWS = 24
PARTS = 4
BF16 = jnp.bfloat16
F32 = jnp.float32


def halves(table):
    high = table.astype(np.float32).astype(ml_dtypes.bfloat16)
    low = (table - high.astype(np.float64)).astype(np.float32).astype(ml_dtypes.bfloat16)
    return high, low


def packed_columns(cosine, sine):
    half = LANES // 2
    parts = []
    for first in range(0, cosine.shape[1], half):
        parts += [cosine[:, first : first + half], sine[:, first : first + half]]
    return np.concatenate(parts, axis=1)


@functools.lru_cache(maxsize=None)
def x_tables(length):
    base = length // RADIX
    m = np.arange(base)[:, None]
    q = np.arange(base)[None, :]
    angle = 2.0 * np.pi * ((m * q) % base) / base
    cosine, sine = np.cos(angle), np.sin(angle)
    full = np.concatenate([packed_columns(cosine, -sine), packed_columns(sine, cosine)], axis=0)
    half = base // 2
    zero_cos, zero_sin = cosine[:, :half].copy(), -sine[:, :half]
    zero_cos[:, 0] = 0.0
    zero_sin = zero_sin.copy()
    zero_sin[:, 0] = (-1.0) ** np.arange(base)
    zero = packed_columns(zero_cos, zero_sin)
    shifted = 2.0 * np.pi * ((m * (RADIX * q[:, :half] + RADIX // 2)) % length) / length
    middle = packed_columns(np.cos(shifted), -np.sin(shifted))
    turns = 2.0 * np.pi * np.arange(1, RADIX // 2)[:, None] * np.arange(base)[None, :] / length
    return full, zero, middle, np.cos(turns), np.sin(turns)


@functools.lru_cache(maxsize=None)
def y_tables(length):
    base = length // RADIX
    index = np.arange(base)
    angle = 2.0 * np.pi * ((index[:, None] * index[None, :]) % base) / base
    both = np.concatenate([np.cos(angle), np.sin(angle)], axis=0)
    turns = 2.0 * np.pi * np.arange(RADIX)[:, None] * index[None, :] / length
    turns = np.concatenate([np.cos(turns), np.sin(turns)], axis=0).T
    high, rest = halves(turns)
    low = turns - high.astype(np.float64) - rest.astype(np.float64)
    return both, np.concatenate([high, rest, low.astype(ml_dtypes.bfloat16)], axis=1)


@functools.lru_cache(maxsize=None)
def wave_table(length, count):
    slots = LANES // 4
    base = length // RADIX
    waves = []
    for residue in (1, 2, 3):
        waves.append(RADIX * np.arange(base) + residue)
    waves.append(RADIX * np.arange(base // 2))
    waves.append(RADIX * np.arange(base // 2) + RADIX // 2)
    waves = np.concatenate(waves)
    waves = np.where(waves == 0, length // 2, waves)
    waves = np.where(waves < length // 2, waves, waves - length).reshape(count, slots)
    return np.tile(waves, (1, 4)).astype(np.float32)


@functools.lru_cache(maxsize=None)
def band_tables(rows):
    across = np.zeros((4 * LANES, 2 * LANES))
    column = np.arange(2 * LANES)
    down = np.zeros((rows, rows))
    for index, weight in enumerate(whole_weights):
        distance = index + 1
        across[column + LANES + distance, column] = weight
        across[column + LANES - distance, column] = -weight
        down += weight * (np.eye(rows, k=distance) - np.eye(rows, k=-distance))
    return across.astype(ml_dtypes.bfloat16), down.astype(ml_dtypes.bfloat16)


def beside(*tables):
    high, low = halves(np.concatenate(tables, axis=1))
    return np.concatenate([high, low], axis=0)


def split(values):
    high = values.astype(BF16)
    return high, (values - high.astype(F32)).astype(BF16)


def dot(left, right):
    return jnp.dot(left, right, preferred_element_type=F32)


def exact_dot(left, right):
    left_high, left_low = left
    right_high, right_low = right
    return dot(left_high, right_high) + (dot(left_low, right_high) + dot(left_high, right_low))


def lane_index(shape):
    return lax.broadcasted_iota(jnp.int32, shape, len(shape) - 1)


def spin(values, shift):
    return pltpu.roll(values, shift % values.shape[-1], values.ndim - 1)


def lane_tile(values, index):
    return values[:, index * LANES : (index + 1) * LANES]


def x_parts(tables, base):
    wide = 2 * base
    full = (tables[:wide], tables[wide : 2 * wide])
    at = 2 * wide
    high, low = tables[at : at + base], tables[at + base : at + 2 * base]
    return full, (high[:, :base], low[:, :base]), (high[:, base:], low[:, base:])


def pieces_kernel(velocity, *pieces):
    rows = pieces[0].shape[1]
    place = lax.axis_index("gx")
    for mask, piece in enumerate(pieces):
        start = pl.multiple_of((place ^ mask) * rows, 8)
        for c in range(2):
            piece[c] = velocity[c, 0, pl.ds(start, rows), :]


def rows_kernel(top, low, top_wall, low_wall, top_flow, low_flow, first, last):
    small, width = top.shape[2], top_flow.shape[3]
    first[...] = jnp.zeros(first.shape, F32)
    last[...] = jnp.zeros(last.shape, F32)
    for k, (start, rows) in STRIP.items():
        lanes = slice(0, width) if k == PARTS + 1 else slice(None)
        if k < PARTS:
            upper, lower = top[k, 0].astype(F32)[:HALO], low[k, 0].astype(F32)[small - HALO :]
        elif k == PARTS:
            upper, lower = 1.0 - top_wall[0].astype(F32), 1.0 - low_wall[0].astype(F32)
        else:
            upper, lower = top_flow[0, 0], low_flow[0, 0]
        first[start : start + rows, lanes] = upper[:rows]
        last[start : start + rows, lanes] = lower[HALO - rows :]


def strip(ref, k, upper, lanes=slice(None)):
    if k not in STRIP:
        return jnp.zeros((HALO, ref[0:1, lanes].shape[1]), F32)
    start, rows = STRIP[k]
    values = ref[start : start + rows, lanes]
    blank = jnp.zeros((HALO - rows, values.shape[1]), F32)
    return jnp.concatenate([blank, values] if upper else [values, blank], axis=0)


def columns_kernel(
    has, left, right, left_wall, right_wall, left_flow, right_flow, above, below, to_right, to_left
):
    parts = left.shape[0]
    wide, flow_wide = above.shape[1], above.shape[1] // 2
    gap = jnp.zeros((LANES - 2 * HALO, LANES), F32)

    def tall(k, inner, first, sides):
        lanes = slice(first, first + LANES)
        over, under = strip(above, k, True, lanes), strip(below, k, False, lanes)
        return jnp.concatenate([inner, under * sides[1], gap, over * sides[0]], axis=0).T

    for k in range(parts + 1):
        at = slice(k * HALO, (k + 1) * HALO)
        if k < parts:
            near, far = left[k, 0].astype(F32), right[k, 0].astype(F32)
        else:
            near, far = 1.0 - left_wall[0].astype(F32), 1.0 - right_wall[0].astype(F32)
        sides = (has[2], has[3])
        to_left[at, :] = tall(k, near, 0, sides)[:HALO]
        to_right[at, :] = tall(k, far, wide - LANES, sides)[LANES - HALO :]
    k = parts + 1
    at = slice(k * HALO, (k + 1) * HALO)
    size = left_flow.shape[2] + LANES
    blank = jnp.zeros((HALO, to_left.shape[1] - size), F32)
    to_left[at, :size] = tall(k, left_flow[0, 0], 0, (1.0, 1.0))[:HALO]
    to_right[at, :size] = tall(k, right_flow[0, 0], flow_wide - LANES, (1.0, 1.0))[LANES - HALO :]
    to_left[at, size:] = blank
    to_right[at, size:] = blank


def sides_kernel(has, place, velocity, above, below, from_left, from_right, sides, squares, mark):
    parts, tall, _ = sides.shape
    gap = jnp.zeros((LANES - 2 * HALO, tall), F32)
    for k in range(parts):
        at = slice(k * HALO, (k + 1) * HALO)
        tile = [from_right[at, :] * has[1], gap, from_left[at, :] * has[0]]
        sides[k] = jnp.concatenate(tile, axis=0).T
    at = slice(parts * HALO, (parts + 1) * HALO)
    rows, local = velocity.shape[2:]
    size = rows + LANES
    tile = [from_right[at, :size], gap[:, :size], from_left[at, :size]]
    tile = jnp.concatenate(tile, axis=0).T
    tile = tile * tile
    mark[0] = place[0]
    over, under = (strip(ref, parts, ref is above, slice(0, local)) for ref in (above, below))
    squares[:HALO, :local] = over * over
    squares[HALO : HALO + rows, :local] = velocity[0, 0] * velocity[0, 0]
    squares[HALO + rows :, :local] = under * under
    squares[:HALO, local:] = tile[size - HALO :]
    squares[HALO : HALO + rows, local:] = tile[:rows]
    squares[HALO + rows :, local:] = tile[rows : rows + HALO]


def forward_x_kernel(*refs):
    *pieces, tables, turns, out, total, lines, made, sent = refs
    count, _, rows, local = lines.shape
    place = lax.axis_index("gx")
    for mask, piece in enumerate(pieces):
        lines[place ^ mask] = piece[...]
    base = turns.shape[1]
    per = local // base
    u = [lines[t // per, 0, :, (t % per) * base : (t % per + 1) * base] for t in range(RADIX)]
    v = [lines[t // per, 1, :, (t % per) * base : (t % per + 1) * base] for t in range(RADIX)]
    energy = sum(b * b for b in v)
    energy = jnp.sum(energy.reshape(rows // 8, 8, base), axis=0)
    total[...] = sum(energy[:, k : k + LANES] for k in range(0, base, LANES))
    fields = ([a * a - b * b for a, b in zip(u, v)], [2.0 * a * b for a, b in zip(u, v)])
    zeros, mids, reals, imags = [], [], [[], [], []], [[], [], []]
    for a in fields:
        s04, s26, s15, s37 = a[0] + a[4], a[2] + a[6], a[1] + a[5], a[3] + a[7]
        d04, d26, d15, d37 = a[0] - a[4], a[2] - a[6], a[1] - a[5], a[3] - a[7]
        zeros.append((s04 + s26) + (s15 + s37))
        mids.append((s04 + s26) - (s15 + s37))
        minus, plus = ROOT * (d15 - d37), ROOT * (d15 + d37)
        turned = (
            (d04 + minus, -d26 - plus),
            (s04 - s26, s37 - s15),
            (d04 - minus, d26 - plus),
        )
        for index, (real, imag) in enumerate(turned):
            c, s = turns[index : index + 1, :], turns[index + 3 : index + 4, :]
            reals[index].append(real * c + imag * s)
            imags[index].append(imag * c - real * s)
    stacked = jnp.concatenate(
        [
            jnp.concatenate([jnp.concatenate(reals[i], axis=0) for i in range(3)], axis=0),
            jnp.concatenate([jnp.concatenate(imags[i], axis=0) for i in range(3)], axis=0),
        ],
        axis=1,
    )
    full, zero, middle = x_parts(tables, base)
    full = exact_dot(split(stacked), full)
    zero = exact_dot(split(jnp.concatenate(zeros, axis=0)), zero)
    middle = exact_dot(split(jnp.concatenate(mids, axis=0)), middle)
    low = lane_index((rows, LANES)) % 64 < 32
    target, copies = 0, []
    blocks = [full[2 * rows * i : 2 * rows * (i + 1)] for i in range(3)] + [zero, middle]
    for block in blocks:
        start = target
        for first in range(0, block.shape[1], LANES):
            a = block[:rows, first : first + LANES]
            c = block[rows:, first : first + LANES]
            made[target] = jnp.where(low, a, spin(c, 32))
            made[target + 1] = jnp.where(low, spin(a, -32), c)
            target += 2
        group = pl.ds(start, target - start)
        copies.append(pltpu.make_async_copy(made.at[group], out.at[group], sent.at[len(copies)]))
        copies[-1].start()
    for copy in copies:
        copy.wait()


def eighths(x, turn):
    s04, s26, s15, s37 = x[0] + x[4], x[2] + x[6], x[1] + x[5], x[3] + x[7]
    d04, d26, d15, d37 = x[0] - x[4], x[2] - x[6], x[1] - x[5], x[3] - x[7]
    quarter = turn(s15 - s37)
    spun_26, spun_37 = turn(d26), turn(d37)
    one, three = d15 + spun_37, d15 - spun_37
    spun_one, spun_three = turn(one), turn(three)
    one = ROOT * (one + spun_one)
    three = ROOT * (spun_three - three)
    return [
        (s04 + s26) + (s15 + s37),
        (d04 + spun_26) + one,
        (s04 - s26) + quarter,
        (d04 - spun_26) + three,
        (s04 + s26) - (s15 + s37),
        (d04 + spun_26) - one,
        (s04 - s26) - quarter,
        (d04 - spun_26) - three,
    ]


def solve_y_kernel(count_x, _, lines, total, wave, both, turns, out, held, spread, made, sent):
    count, rows, _ = lines.shape
    base = turns.shape[0]
    length = count * rows
    block = count_x * rows
    per = base // rows
    lanes = lane_index((base, LANES))
    sign = jnp.where(lanes < 64, 1.0, -1.0).astype(F32)

    def minus_i(z):
        return spin(z, 64) * sign

    def plus_i(z):
        return spin(z, 64) * -sign

    fields = [
        jnp.concatenate([lines[t * per + k] for k in range(per)], axis=0) for t in range(RADIX)
    ]
    mixed = eighths(fields, minus_i)
    terms, columns = turns.shape[1], 2 * RADIX
    picked = lax.broadcasted_iota(jnp.int32, (terms, columns * LANES), 0) % columns
    lane = lane_index(picked.shape)
    value = jnp.where((lane >= RADIX * LANES) & (lane % LANES >= 64), -1.0, 1.0)
    spread[...] = dot(turns[...], jnp.where(picked == lane // LANES, value, 0.0).astype(BF16))
    cosines = [spread[:, r * LANES : (r + 1) * LANES] for r in range(RADIX)]
    sines = [spread[:, (r + RADIX) * LANES : (r + RADIX + 1) * LANES] for r in range(RADIX)]
    mixed = [mixed[0]] + [
        mixed[r] * cosines[r] + spin(mixed[r], 64) * sines[r] for r in range(1, RADIX)
    ]
    tables = (both[: 2 * base], both[2 * base :])
    product = exact_dot(tables, split(jnp.concatenate(mixed, axis=1)))
    kx = wave[0:1, :]
    first = lanes % 64 < 32
    edge = jnp.float32(length // 2)
    alone = jnp.where(first, kx * kx, 0.0)
    slope = jnp.where(first | (kx == -edge), 0.0, jnp.broadcast_to(kx, lanes.shape))
    q = lax.broadcasted_iota(jnp.int32, lanes.shape, 0)
    low_ky = RADIX * (q - jnp.where(q < base // 2, 0, base)).astype(F32)
    terms = []
    for r in range(RADIX):
        at = slice(r * LANES, (r + 1) * LANES)
        spectrum = product[:base, at] + minus_i(product[base:, at])
        ky = low_ky + float(r)
        symbol = alone + slope * ky
        if r == 0:
            corner = jnp.where((kx == -edge) & ~first, edge * edge, 0.0)
            symbol = jnp.where(ky == -edge, jnp.where(first, alone, corner), symbol)
        terms.append(symbol * pl.reciprocal(kx * kx + ky * ky) * spectrum)
    pairs = [
        jnp.where(first, low + spin(low, -32), high + spin(high, 32))
        for low, high in zip(terms[:4], terms[4:])
    ]
    product = exact_dot(tables, split(jnp.concatenate(pairs, axis=1)))
    mixed = []
    for r in range(RADIX // 2):
        at = slice(r * LANES, (r + 1) * LANES)
        value = product[:base, at] + plus_i(product[base:, at])
        cosine = jnp.where(first, cosines[r], cosines[r + 4])
        sine = jnp.where(first, sines[r], sines[r + 4])
        value = value * cosine - spin(value, 64) * sine
        value = jnp.where(first, value + spin(value, -32), spin(value, 32) - value)
        if r == 2:
            value = jnp.where(first, value, plus_i(value))
        elif r:
            turned = plus_i(value)
            odd = value + turned if r == 1 else turned - value
            value = jnp.where(first, value, ROOT * odd)
        mixed.append(value)
    even, odd = mixed[0] + mixed[2], mixed[0] - mixed[2]
    side, turned = mixed[1] + mixed[3], plus_i(mixed[1] - mixed[3])
    for t, values in enumerate((even + side, odd + turned, even - side, odd - turned)):
        start = MARGIN + 2 * t * base
        held[start : start + base, :] = values
        held[start + base : start + 2 * base, :] = spin(values, -32)
    held[0:MARGIN, :] = held[length : length + MARGIN, :]
    held[length + MARGIN : length + 2 * MARGIN, :] = held[MARGIN : 2 * MARGIN, :]
    spare = total[...] + spin(total[...], 32)
    kept = rows + 2 * MARGIN // count_x
    half = made.shape[1]
    rest = kept - half
    low = lane_index((8, LANES)) % 64 < 32
    copies = []
    for target in range(count):
        start = (target // count_x) * block + (target % count_x) * kept
        for row in range(0, half, 8):
            a = held[start + row : start + row + 8, :]
            if row < rest:
                b = spin(held[start + half + row : start + half + row + 8, :], 32)
            else:
                b = spare
            made[target, row : row + 8, :] = jnp.where(low, a, b)
        if (target + 1) % RADIX == 0:
            group = pl.ds(target + 1 - RADIX, RADIX)
            copies.append(pltpu.make_async_copy(made.at[group], out.at[group], sent.at[len(copies)]))
            copies[-1].start()
    for copy in copies:
        copy.wait()


def inverse_x_kernel(
    kept, scale, place, lines, tables, turns, *refs
):
    *outs, held = refs
    count, half, _ = lines.shape
    base = turns.shape[1]
    length = RADIX * base
    rest = kept - half
    low = lane_index((half, LANES)) % 64 < 32
    groups, spare = [], None
    for first in range(0, count, 2):
        even, odd = lines[first], lines[first + 1]
        a = jnp.where(low, even, spin(odd, 32))
        b = jnp.where(low, spin(even, -32), odd)
        groups.append(jnp.concatenate([a, b[:rest]], axis=0))
        extra = b[rest : rest + 8]
        spare = extra if spare is None else spare + extra
    mean = jnp.sum(spare) * scale
    wide = 2 * base // LANES
    narrow = base // LANES
    stacked = jnp.concatenate(
        [jnp.concatenate(groups[i * wide : (i + 1) * wide], axis=1) for i in range(3)], axis=0
    )
    at = 3 * wide
    zeros = jnp.concatenate(groups[at : at + narrow], axis=1)
    mids = jnp.concatenate(groups[at + narrow : at + 2 * narrow], axis=1)
    full, zero, middle = x_parts(tables, base)
    full = exact_dot(split(stacked), full)
    zero = exact_dot(split(zeros), zero) * scale
    mid = exact_dot(split(mids), middle) * scale
    turned = []
    for i in range(3):
        real = full[i * kept : (i + 1) * kept, :base]
        imag = full[i * kept : (i + 1) * kept, base:]
        c = turns[i : i + 1, :] * (2.0 * scale)
        s = turns[i + 3 : i + 4, :] * (2.0 * scale)
        turned.append((real * c - imag * s, real * s + imag * c))
    for t in range(RADIX):
        value = zero + mid if t % 2 == 0 else zero - mid
        for i, (real, imag) in enumerate(turned):
            eighth = t * (i + 1) % RADIX
            c = (1.0, ROOT, 0.0, -ROOT, -1.0, -ROOT, 0.0, ROOT)[eighth]
            s = (0.0, ROOT, 1.0, ROOT, 0.0, -ROOT, -1.0, -ROOT)[eighth]
            if c:
                value = value + c * real
            if s:
                value = value - s * imag
        held[:, t * base : (t + 1) * base] = mean - value
    targets, local = len(outs), outs[0].shape[1] - LANES
    right = lane_index((kept, LANES)) < 64
    for mask, out in enumerate(outs):
        start = pl.multiple_of((place[0] ^ mask) * local, LANES)
        after = pl.multiple_of(jnp.where(start + local == length, 0, start + local), LANES)
        before = pl.multiple_of(jnp.where(start == 0, length, start) - LANES, LANES)
        out[:, :local] = held[:, pl.ds(start, local)]
        out[:, local:] = jnp.where(
            right, held[:, pl.ds(after, LANES)], held[:, pl.ds(before, LANES)]
        )


def slopes_x(parts, band, with_edge):
    tiles = parts[0].shape[-1] // LANES
    pieces = []
    for first in list(range(0, tiles - 1, 2)) + ([tiles - 1] if with_edge else []):
        steps = (-1, 0, 1, 2) if first < tiles - 1 else (-1, 0, 1)
        table = band[...] if first < tiles - 1 else band[: 3 * LANES, :LANES]
        order = [(first + step) % tiles for step in steps]
        piece = None
        for part in parts:
            term = dot(jnp.concatenate([lane_tile(part, t) for t in order], axis=1), table)
            piece = term if piece is None else piece + term
        pieces.append(piece)
    return jnp.concatenate(pieces, axis=1)


def slope_y(read):
    value = read(3) - read(-3)
    for index in (0, 1):
        value = value + whole_weights[index] * (read(index + 1) - read(-index - 1))
    return value


def edged(k, side, center, up, down, above, below, sides, has, first=0):
    step = pl.program_id(0) + first
    tile, width = center.shape
    tall = sides.shape[1]
    last = (tall - LANES) // tile - 1
    base = pl.multiple_of(step * tile, 8)
    before = pl.multiple_of(jnp.where(step == 0, tall, base) - HALO, 8)
    over = jnp.where(step == 0, strip(above, k, True) * has[2], up)
    under = jnp.where(step == last, strip(below, k, False) * has[3], down)
    rows = (
        (over, sides[side, pl.ds(before, HALO), :]),
        (center, sides[side, pl.ds(base, tile), :]),
        (under, sides[side, pl.ds(pl.multiple_of(base + tile, 8), HALO), :]),
    )
    return jnp.concatenate([jnp.concatenate(pair, axis=1) for pair in rows], axis=0)


def edged_open(k, side, wall, wall_up, wall_down, above, below, sides, has, first=0):
    open_cells = [1.0 - ref[0].astype(F32) for ref in (wall, wall_up, wall_down)]
    return edged(k, side, *open_cells, above, below, sides, has, first)


def quiet_step_kernel(
    first, has, place, center, up, down, wall, wall_up, wall_down, above, below, sides, across, along, along_inner, calm, density, shown_open, mark
):
    parts, _, tile, width = center.shape
    high = tile + 2 * HALO
    opened = edged_open(parts, parts, wall, wall_up, wall_down, above, below, sides, has, first)
    values = []
    for k in range(parts):
        value = edged(
            k,
            k,
            center[k, 0].astype(F32),
            up[k, 0].astype(F32)[up.shape[2] - HALO :],
            down[k, 0].astype(F32)[:HALO],
            above,
            below,
            sides,
            has,
            first,
        )
        values.append(value)

    def drops(x, along_b, along_p):
        diverge = x[1] + along_b
        return (
            diverge + mean_flow * x[0],
            x[3] + mean_flow * x[1],
            along_p + mean_flow * x[2],
            diverge + mean_flow * x[3],
        )

    short = [value.astype(BF16) for value in values]
    x = slopes_x((jnp.concatenate(short, axis=0),), across, True)
    x = [x[k * high : (k + 1) * high] for k in range(parts)]
    table = along[...]
    dropped = drops(x, dot(table, short[2]), dot(table, short[3]))
    middle = [opened * (v - (time_step / 60.0) * d) for v, d in zip(values, dropped)]
    inner = slice(HALO, HALO + tile)
    x = slopes_x(split(jnp.concatenate([value[inner] for value in middle], axis=0)), across, False)
    x = [x[k * tile : (k + 1) * tile] for k in range(parts)]
    table = along_inner[...]
    y = [sum(dot(table, part) for part in split(middle[k][:, :width])) for k in (2, 3)]
    dropped = drops(x, *y)
    shown = opened[inner, :width]
    for k in range(parts):
        start = 0.5 * values[k][inner, :width] - (0.5 * time_step / 60.0) * dropped[k]
        value = shown * start + 0.5 * middle[k][inner, :width]
        if k == 0:
            density[0, 0] = value.astype(BF16)
        else:
            calm[k - 1] = value
    shown_open[0] = (time_step * opened).astype(BF16)
    mark[0] = place[0]


def tables_kernel(place, weights_x, weights_y, rise_x, rise_y, mark):
    mark[0] = place[0]
    _, tiles, reach_x, lanes = rise_x.shape
    wide, length_x = (tiles - 1) * lanes, weights_x.shape[1]
    first = place[0] * wide
    half = LANES // 2

    def weights(ref, start, size):
        length = ref.shape[1]
        start = jnp.where(start < 0, start + length, jnp.where(start >= length, start - length, start))
        return ref[:, pl.ds(pl.multiple_of(start, LANES), size)]

    cells = lax.broadcasted_iota(jnp.int32, (reach_x, lanes), 0)
    fine = lax.broadcasted_iota(jnp.int32, (reach_x, lanes), 1)
    right, left = weights(weights_x, first + wide, LANES), weights(weights_x, first - LANES, LANES)
    edge = jnp.where(lane_index(right.shape) < half, right, left)
    edge = jnp.concatenate([edge, edge], axis=1)
    for k in range(tiles):
        own = weights(weights_x, first + k * lanes, lanes) if k < tiles - 1 else edge
        target = fine // 2 - 1
        if k == tiles - 1:
            target = jnp.where(fine < half, target, target + half)
        value = jnp.zeros(fine.shape, F32)
        for t in range(4):
            value = jnp.where(cells == (target + t) % reach_x, own[t : t + 1, :], value)
        rise_x[0, k], rise_x[1, k] = split(value)
    steps, high, reach = rise_y.shape
    tall = steps * TILE
    first = place[1] * tall
    own = [weights(weights_y, first + k * LANES, LANES) for k in range(-1, tall // LANES + 1)]
    own = jnp.concatenate([jnp.concatenate(own, axis=1), jnp.zeros((4, tall + 2 * LANES), F32)], axis=0).T
    cells = lax.broadcasted_iota(jnp.int32, (high, reach), 1)
    last = cells >= reach // 3 * 2
    cells = cells % (reach // 3)
    target = lax.broadcasted_iota(jnp.int32, (high, reach), 0) // 2 + (HALO // 2 - 1)
    for k in range(steps):
        start = LANES - HALO + k * TILE
        value = jnp.zeros((high, reach), F32)
        for t in range(4):
            value = jnp.where(cells == target + t, own[start : start + high, t : t + 1], value)
        upper, lower = split(value)
        rise_y[k] = jnp.where(last, lower, upper)


def source_kernel(squares, opened, rise_x, rise_y, quiet, across, _, *refs):
    *lines, out, squared, cells_open, matrix, rows_matrix, calm, band, held, raised, forced, done, fetched, kept = refs
    steps = done.shape[0]
    tile, width = calm.shape[2:]
    high = tile + 2 * HALO
    rows = lines[0].shape[0]
    place = lax.axis_index("gx")

    def tile_copies(k):
        part = quiet.at[:, pl.ds(k * tile, tile), :]
        return (
            pltpu.make_async_copy(part, calm.at[k % 2], fetched.at[k % 2]),
            pltpu.make_async_copy(opened.at[k], cells_open.at[k % 2], fetched.at[2 + k % 2]),
        )

    def done_copy(k):
        part = out.at[1:, 0, pl.ds(k * tile, tile), :]
        return pltpu.make_async_copy(done.at[k], part, kept.at[k])

    arrays = ((squares, squared), (rise_x, matrix), (rise_y, rows_matrix), (across, band))
    copies = [
        pltpu.make_async_copy(source, target, fetched.at[4 + k])
        for k, (source, target) in enumerate(arrays)
    ]
    pieces = [
        pltpu.make_async_copy(
            piece,
            held.at[pl.ds(pl.multiple_of((place ^ mask) * rows, 8), rows), :],
            fetched.at[4 + len(arrays) + mask],
        )
        for mask, piece in enumerate(lines)
    ]
    for copy in (*pieces, *copies, *tile_copies(0), *tile_copies(1)):
        copy.start()
    for copy in pieces + copies[:1]:
        copy.wait()

    level = held[MARGIN - HALO : MARGIN - HALO + squared.shape[0], :] - squared[...]
    count = level.shape[1] // LANES
    near = lane_index((level.shape[0], LANES)) < 64
    around = []
    for k in range(count):
        after, before = lane_tile(level, (k + 1) % count), lane_tile(level, (k - 1) % count)
        around.append(split(jnp.concatenate([lane_tile(level, k), jnp.where(near, after, before)], axis=1)))
    copies[1].wait()
    for k in range(count):
        lanes = 2 * LANES if k < count - 1 else LANES
        value = split(exact_dot(around[k], [matrix[part, k, :, :lanes] for part in range(2)]))
        for part in range(2):
            raised[part, :, 2 * k * LANES : 2 * k * LANES + lanes] = value[part]
    for copy in copies[2:]:
        copy.wait()

    reach = rows_matrix.shape[2] // 3
    for k in range(steps):
        start = k * (tile // 2)
        window = [raised[part, start : start + reach, :] for part in (0, 1, 0)]
        calm_here, open_here = tile_copies(k)
        open_here.wait()
        free = cells_open[k % 2].astype(F32)
        value = free * dot(rows_matrix[k], jnp.concatenate(window, axis=0))
        forced[k % 2] = value
        inner = value[HALO : HALO + tile]
        shown = (0.5 / 60.0) * free[HALO : HALO + tile, :width]
        x = shown * slopes_x(split(inner), band, False)
        y = shown * slope_y(lambda d: forced[k % 2, HALO + d : HALO + d + tile, :width])
        calm_here.wait()
        still = calm.at[k % 2]
        done[k, 0] = (still[0] - x).astype(BF16)
        done[k, 1] = (still[1] - y).astype(BF16)
        done[k, 2] = (still[2] + inner[:, :width] - mean_flow * x).astype(BF16)
        done_copy(k).start()
        if k + 2 < steps:
            for copy in tile_copies(k + 2):
                copy.start()
    for k in range(steps):
        done_copy(k).wait()


def call(
    kernel, operands, outs, scratch=(), steps=0, specs=None, out_specs=None, after=(), aliases=None, megabytes=24, flops=0, moved=0, name=None
):
    count = len(operands)

    def body(*refs):
        kernel(*refs[:count], *refs[count + len(after) :])

    def whole(array):
        zeros = (0,) * len(array.shape)
        return pl.BlockSpec(array.shape, lambda *_: zeros)

    arguments = {}
    chosen = specs or {}
    if steps:
        arguments["grid"] = (steps,)
        in_specs = [chosen.get(i, whole(o)) for i, o in enumerate(operands)]
        arguments["out_specs"] = jax.tree.map(whole, outs) if out_specs is None else out_specs
    else:
        local = pl.BlockSpec(memory_space=pltpu.VMEM)
        in_specs = [chosen.get(i, local) for i in range(count)]
        if out_specs is not None:
            arguments["out_specs"] = out_specs
    return pl.pallas_call(
        body,
        out_shape=outs,
        in_specs=in_specs + [pl.BlockSpec(memory_space=pl.ANY)] * len(after),
        scratch_shapes=list(scratch),
        input_output_aliases=aliases or {},
        compiler_params=pltpu.CompilerParams(vmem_limit_bytes=megabytes << 20),
        cost_estimate=pl.CostEstimate(flops=flops, bytes_accessed=moved, transcendentals=0),
        name=name,
        **arguments,
    )(*operands, *after)


def ring(array, axis, step):
    size = lax.axis_size(axis)
    return lax.ppermute(array, axis, [(i, (i + step) % size) for i in range(size)])


def swap(array, axis, mask):
    return lax.ppermute(array, axis, [(i, i ^ mask) for i in range(lax.axis_size(axis))])


def shaped(*shape, kind=F32):
    return jax.ShapeDtypeStruct(shape, kind)


def pressure_lines(pieces, gathered, spread, stepped):
    _, rows, local_x = pieces[0].shape
    count_x, count_y = lax.axis_size("gx"), lax.axis_size("gy")
    count = count_x * count_y
    scalars = {0: pl.BlockSpec(memory_space=pltpu.SMEM)}
    length_x, length_y = local_x * count_x, rows * count
    full, zero, middle, cos_turn, sin_turn = x_tables(length_x)
    turns = np.zeros((8, cos_turn.shape[1]), np.float32)
    turns[0:3], turns[3:6] = cos_turn, sin_turn
    spectra, total = call(
        forward_x_kernel,
        (*pieces, np.concatenate([beside(full), beside(zero, middle)]), turns),
        (shaped(count, rows, LANES), shaped(8, LANES)),
        (
            pltpu.VMEM((count_x, 2, rows, local_x), F32),
            pltpu.VMEM((count, rows, LANES), F32),
            pltpu.SemaphoreType.DMA((5,)),
        ),
        out_specs=(pl.BlockSpec(memory_space=pl.ANY), pl.BlockSpec(memory_space=pltpu.VMEM)),
        after=gathered,
        flops=10**9,
        moved=4 << 20,
        name="forward_x",
    )
    spectra = lax.all_to_all(spectra, ("gy", "gx"), 0, 0, tiled=True)
    place = lax.axis_index("gy") * count_x + lax.axis_index("gx")
    waves = jnp.asarray(wave_table(length_x, count))
    wave = lax.dynamic_slice(waves, (place, 0), (1, LANES))
    both, turns_y = y_tables(length_y)
    kept = rows + 2 * MARGIN // count_x
    half = (kept // 2 + 8) // 8 * 8
    solved = call(
        functools.partial(solve_y_kernel, count_x),
        (spread, spectra, total, wave, beside(both), turns_y),
        shaped(count, half, LANES),
        (
            pltpu.VMEM((length_y + 2 * MARGIN, LANES), F32),
            pltpu.VMEM((length_y // RADIX, 2 * RADIX * LANES), F32),
            pltpu.VMEM((count, half, LANES), F32),
            pltpu.SemaphoreType.DMA((count // RADIX,)),
        ),
        specs=scalars,
        out_specs=pl.BlockSpec(memory_space=pl.ANY),
        flops=4 * 10**9,
        moved=6 << 20,
        name="solve_y",
    )
    solved = lax.all_to_all(solved, ("gy", "gx"), 0, 0, tiled=True)
    back = 2.0 * zero.T
    back[LANES // 2] *= 0.5
    tables = np.concatenate(
        [beside(full.T), beside(back, 2.0 * middle.T)]
    )
    pressed = call(
        functools.partial(inverse_x_kernel, kept, 1.0 / (length_x * length_y)),
        (stepped, solved, tables, turns),
        (shaped(kept, local_x + LANES),) * count_x,
        (pltpu.VMEM((kept, length_x), F32),),
        specs=scalars,
        flops=10**9,
        moved=4 << 20,
        name="inverse_x",
    )
    return [piece if mask == 0 else swap(piece, "gx", mask) for mask, piece in enumerate(pressed)]


def fast_shards(velocity, weights_x, weights_y, acoustic, wall_mask):
    parts, _, tall, wide = acoustic.shape
    _, _, local_y, local_x = velocity.shape
    count_x, count_y = lax.axis_size("gx"), lax.axis_size("gy")
    place_x, place_y = lax.axis_index("gx"), lax.axis_index("gy")
    full, high, steps = wide + LANES, TILE + 2 * HALO, tall // TILE
    strips = (parts + 2) * HALO
    small = 2 * HALO
    has = jnp.stack([place_x > 0, place_x < count_x - 1, place_y > 0, place_y < count_y - 1])
    has = has.astype(F32)
    scalars = pl.BlockSpec(memory_space=pltpu.SMEM)

    def at(block, *index):
        return pl.BlockSpec(block, lambda i: index)

    own = place_x.astype(jnp.int32).reshape(1)
    sent = call(
        pieces_kernel,
        (velocity,),
        (shaped(2, local_y // count_x, local_x),) * count_x,
        moved=2 << 20,
        megabytes=8,
        name="pieces",
    )
    moved = [piece if mask == 0 else swap(piece, "gx", mask) for mask, piece in enumerate(sent)]
    first, last = call(
        rows_kernel,
        (acoustic, acoustic, wall_mask, wall_mask, velocity, velocity),
        (shaped(STRIP_ROWS, wide),) * 2,
        steps=1,
        specs={
            0: at((parts, 1, small, wide), 0, 0, 0, 0),
            1: at((parts, 1, small, wide), 0, 0, tall // small - 1, 0),
            2: at((1, HALO, wide), 0, 0, 0),
            3: at((1, HALO, wide), 0, tall // HALO - 1, 0),
            4: at((1, 1, HALO, local_x), 1, 0, 0, 0),
            5: at((1, 1, HALO, local_x), 1, 0, local_y // HALO - 1, 0),
        },
        after=moved[1:2],
        moved=2 << 20,
        megabytes=50,
        name="rows",
    )
    above, below = ring(last, "gy", 1), ring(first, "gy", -1)
    to_right, to_left = call(
        columns_kernel,
        (has, acoustic, acoustic, wall_mask, wall_mask, velocity, velocity, above, below),
        (shaped(strips, tall + LANES), shaped(strips, tall + LANES)),
        steps=1,
        specs={
            0: scalars,
            1: at((parts, 1, tall, LANES), 0, 0, 0, 0),
            2: at((parts, 1, tall, LANES), 0, 0, 0, wide // LANES - 1),
            3: at((1, tall, LANES), 0, 0, 0),
            4: at((1, tall, LANES), 0, 0, wide // LANES - 1),
            5: at((1, 1, local_y, LANES), 1, 0, 0, 0),
            6: at((1, 1, local_y, LANES), 1, 0, 0, local_x // LANES - 1),
        },
        moved=8 << 20,
        megabytes=54,
        name="columns",
    )
    from_left, from_right = ring(to_right, "gx", 1), ring(to_left, "gx", -1)
    local_memory = pl.BlockSpec(memory_space=pltpu.VMEM)
    tiles = wide // (2 * LANES) + 1
    rise_x, rise_y, listed = call(
        tables_kernel,
        (jnp.stack([place_x, place_y]).astype(jnp.int32), weights_x, weights_y),
        (
            shaped(2, tiles, 2 * LANES, 2 * LANES, kind=BF16),
            shaped(steps, high, 3 * (high // 2 + HALO), kind=BF16),
            shaped(1, kind=jnp.int32),
        ),
        specs={0: scalars},
        out_specs=(local_memory, local_memory, scalars),
        moved=4 << 20,
        megabytes=54,
        name="tables",
    )
    sides, squares, beside = call(
        sides_kernel,
        (has, listed, velocity, above, below, from_left, from_right),
        (
            shaped(parts + 1, tall + LANES, LANES),
            shaped(local_y + 2 * HALO, local_x + LANES),
            shaped(1, kind=jnp.int32),
        ),
        steps=1,
        specs={0: scalars, 1: scalars, 2: at((1, 1, local_y, local_x), 1, 0, 0, 0)},
        out_specs=(
            at((parts + 1, tall + LANES, LANES), 0, 0, 0),
            at((local_y + 2 * HALO, local_x + LANES), 0, 0),
            scalars,
        ),
        moved=8 << 20,
        megabytes=54,
        name="sides",
    )
    across, along = band_tables(high)
    along_inner = along[HALO : HALO + TILE]
    per, rows = TILE // small, TILE // HALO

    def tiled(first):
        walls = (
            pl.BlockSpec((1, TILE, wide), lambda i: (0, i + first, 0)),
            pl.BlockSpec((1, HALO, wide), lambda i: (0, jnp.maximum((i + first) * rows - 1, 0), 0)),
            pl.BlockSpec(
                (1, HALO, wide),
                lambda i: (0, jnp.minimum((i + first + 1) * rows, steps * rows - 1), 0),
            ),
        )
        cells = (
            pl.BlockSpec((parts, 1, TILE, wide), lambda i: (0, 0, i + first, 0)),
            pl.BlockSpec(
                (parts, 1, small, wide), lambda i: (0, 0, jnp.maximum((i + first) * per - 1, 0), 0)
            ),
            pl.BlockSpec(
                (parts, 1, small, wide),
                lambda i: (0, 0, jnp.minimum((i + first + 1) * per, steps * per - 1), 0),
            ),
        )
        return cells, walls

    def quiet_tiles(first, count, before):
        cells, walls = tiled(first)
        operands = (has, own, acoustic, acoustic, acoustic, wall_mask, wall_mask, wall_mask, above, below, sides)
        operands = operands + (across, along, along_inner)
        return call(
            functools.partial(quiet_step_kernel, first),
            operands,
            (
                shaped(parts - 1, tall, wide),
                shaped(*acoustic.shape, kind=BF16),
                shaped(steps, high, full, kind=BF16),
                shaped(1, kind=jnp.int32),
            ),
            steps=count,
            specs=dict(enumerate((scalars, scalars) + cells + walls)),
            out_specs=(
                pl.BlockSpec((parts - 1, TILE, wide), lambda i: (0, i + first, 0)),
                pl.BlockSpec((1, 1, TILE, wide), lambda i: (0, 0, i + first, 0)),
                pl.BlockSpec((1, high, full), lambda i: (i + first, 0, 0)),
                scalars,
            ),
            after=before,
            aliases={len(operands) + k: k for k in range(len(before))},
            megabytes=54 if first == 0 else 50,
            flops=3 * 10**9 * count,
            moved=(12 << 20) * count,
            name="quiet_step",
        )

    early = max(steps * 3 // 4, 1)
    *begun, stepped = quiet_tiles(0, early, ())
    if early < steps:
        *begun, _ = quiet_tiles(early, steps - early, begun)
    quiet, final, opened = begun
    lines = pressure_lines(moved, (above, below), beside, stepped)
    operands = (squares, opened, rise_x, rise_y, quiet, across, final, *lines)
    anywhere = pl.BlockSpec(memory_space=pl.ANY)
    specs = {k: anywhere for k in range(len(operands))}
    scratch = (
        pltpu.VMEM(squares.shape, F32),
        pltpu.VMEM((2,) + opened.shape[1:], BF16),
        pltpu.VMEM(rise_x.shape, BF16),
        pltpu.VMEM(rise_y.shape, BF16),
        pltpu.VMEM((2, parts - 1, TILE, wide), F32),
        pltpu.VMEM(across.shape, BF16),
        pltpu.VMEM((local_y + 2 * MARGIN, local_x + LANES), F32),
        pltpu.VMEM((2, local_y + 2 * HALO, full), BF16),
        pltpu.VMEM((2, high, full), F32),
        pltpu.VMEM((steps, parts - 1, TILE, wide), BF16),
        pltpu.SemaphoreType.DMA((8 + count_x,)),
        pltpu.SemaphoreType.DMA((steps,)),
    )
    return call(
        source_kernel,
        operands,
        shaped(*acoustic.shape, kind=BF16),
        scratch,
        specs=specs,
        out_specs=anywhere,
        aliases={6: 0},
        megabytes=56,
        flops=4 * 10**9,
        moved=16 << 20,
        name="source_step",
    )


def fits(count_x, count_y, velocity, acoustic):
    _, planes, local_y, local_x = velocity
    _, _, tall, wide = acoustic
    length_x, length_y = local_x * count_x, local_y * count_y
    rows = local_y // count_x
    base_x, base_y = length_x // RADIX, length_y // RADIX
    return (
        planes == 1
        and acoustic[0] == PARTS
        and length_x * 2 == count_x * count_y * LANES
        and base_x % (2 * LANES) == 0
        and local_x % base_x == 0
        and rows % 8 == 0
        and base_y % rows == 0
        and base_y % 8 == 0
        and count_x * count_y % RADIX == 0
        and MARGIN * 2 % (8 * count_x) == 0
        and tall == 2 * local_y
        and wide == 2 * local_x
        and tall % TILE == 0
        and tall % LANES == 0
        and tall >= 2 * TILE
        and count_x & (count_x - 1) == 0
        and wide % (2 * LANES) == 0
    )


def extended(array, sides, width):
    for axis, dim in sides:
        size, length = (lax.axis_size(axis), array.shape[dim])
        up = [(i, (i + 1) % size) for i in range(size - 1)]
        down = [(j, i) for i, j in up]
        last = lax.slice_in_dim(array, length - width, length, axis=dim)
        leading = lax.slice_in_dim(array, 0, width, axis=dim)
        before = lax.ppermute(last, axis, up)
        after = lax.ppermute(leading, axis, down)
        array = jnp.concatenate([before, array, after], axis=dim)
    return array


def gradients(padded):
    height = padded.shape[-2] - 6
    breadth = padded.shape[-1] - 6
    rows_mid = padded[..., 3 : 3 + height, :]
    cols_mid = padded[..., :, 3 : 3 + breadth]
    along_x = jnp.zeros_like(padded[..., 3 : 3 + height, 3 : 3 + breadth])
    along_y = jnp.zeros_like(along_x)
    for index, weight in enumerate(stencil_weights):
        distance = index + 1
        along_x = along_x + weight * (
            rows_mid[..., 3 + distance : 3 + distance + breadth]
            - rows_mid[..., 3 - distance : 3 - distance + breadth]
        )
        along_y = along_y + weight * (
            cols_mid[..., 3 + distance : 3 + distance + height, :]
            - cols_mid[..., 3 - distance : 3 - distance + height, :]
        )
    return (along_x, along_y)


def tendency(padded, source):
    along_x, along_y = gradients(padded)
    diverge = along_x[1] + along_y[2]
    forcing = jnp.stack([-diverge, -along_x[3], -along_y[3], source - diverge])
    return forcing - mean_flow * along_x


def spectral_index(flat, length):
    second = length // 16
    wave = flat // second + 16 * (flat % second)
    return jnp.where(wave < length // 2, wave, wave - length).astype(jnp.float32)


def twiddles(rows_count, cols_count, modulus, sign):
    products = jnp.arange(rows_count)[:, None] * jnp.arange(cols_count)[None, :] % modulus
    angles = 2.0 * math.pi / modulus * products.astype(jnp.float32)
    return (jnp.cos(angles), sign * jnp.sin(angles))


def mix_rows(real_part, imag_part, cosine, sine):
    exact = lax.Precision.HIGHEST
    cos_real = jnp.einsum("ka,...ab->...kb", cosine, real_part, precision=exact)
    cos_imag = jnp.einsum("ka,...ab->...kb", cosine, imag_part, precision=exact)
    sin_real = jnp.einsum("ka,...ab->...kb", sine, real_part, precision=exact)
    sin_imag = jnp.einsum("ka,...ab->...kb", sine, imag_part, precision=exact)
    return (cos_real - sin_imag, cos_imag + sin_real)


def mix_cols(real_part, imag_part, cosine, sine):
    exact = lax.Precision.HIGHEST
    cos_real = jnp.einsum("...kb,bc->...kc", real_part, cosine, precision=exact)
    cos_imag = jnp.einsum("...kb,bc->...kc", imag_part, cosine, precision=exact)
    sin_real = jnp.einsum("...kb,bc->...kc", real_part, sine, precision=exact)
    sin_imag = jnp.einsum("...kb,bc->...kc", imag_part, sine, precision=exact)
    return (cos_real - sin_imag, cos_imag + sin_real)


def rotate(real_part, imag_part, cosine, sine):
    return (real_part * cosine - imag_part * sine, real_part * sine + imag_part * cosine)


def discrete(real_part, imag_part, sign):
    length = real_part.shape[-1]
    second = length // 16
    initial = real_part.shape
    folded = initial[:-1] + (16, second)
    real_part = real_part.reshape(folded)
    imag_part = imag_part.reshape(folded)
    small_cos, small_sin = twiddles(16, 16, 16, sign)
    large_cos, large_sin = twiddles(second, second, second, sign)
    turn_cos, turn_sin = twiddles(16, second, length, sign)
    if sign < 0:
        real_part, imag_part = mix_rows(real_part, imag_part, small_cos, small_sin)
        real_part, imag_part = rotate(real_part, imag_part, turn_cos, turn_sin)
        real_part, imag_part = mix_cols(real_part, imag_part, large_cos, large_sin)
    else:
        real_part, imag_part = mix_cols(real_part, imag_part, large_cos, large_sin)
        real_part, imag_part = rotate(real_part, imag_part, turn_cos, turn_sin)
        real_part, imag_part = mix_rows(real_part, imag_part, small_cos, small_sin)
        real_part = real_part / length
        imag_part = imag_part / length
    return (real_part.reshape(initial), imag_part.reshape(initial))


def transform(stacked, sign, kind):
    if kind == "real_in":
        real_part = stacked
        imag_part = jnp.zeros_like(stacked)
    else:
        half = stacked.shape[0] // 2
        real_part = stacked[:half]
        imag_part = stacked[half:]
    real_out, imag_out = discrete(real_part, imag_part, sign)
    if kind == "real_out":
        return real_out
    return jnp.concatenate([real_out, imag_out], axis=0)


def project(stacked, wave_x, wave_y):
    coef_xx = wave_x * wave_x
    coef_xy = 2.0 * wave_x * wave_y
    coef_yy = wave_y * wave_y
    denominator = wave_x * wave_x + wave_y * wave_y
    positive = denominator > 0
    safe = jnp.where(positive, denominator, 1.0)

    def combine(parts):
        numerator = -(coef_xx * parts[0] + coef_xy * parts[1] + coef_yy * parts[2])
        return jnp.where(positive, numerator / safe, 0.0)

    return jnp.stack([combine(stacked[:3]), combine(stacked[3:])])


def refine(stacked, weights):
    result = jnp.zeros(stacked.shape[:-1] + (2 * stacked.shape[-1],), jnp.float32)
    for offset in range(4):
        result = (
            result
            + jnp.repeat(jnp.roll(stacked, 1 - offset, axis=-1), 2, axis=-1) * weights[offset]
        )
    return result


def lines_x(stacked, action):
    gathered = action(lax.all_to_all(stacked, "gx", split_axis=2, concat_axis=3, tiled=True))
    return lax.all_to_all(gathered, "gx", split_axis=3, concat_axis=2, tiled=True)


def lines_y(stacked, action):
    turned = jnp.swapaxes(stacked, 2, 3)
    gathered = action(lax.all_to_all(turned, "gy", split_axis=2, concat_axis=3, tiled=True))
    returned = lax.all_to_all(gathered, "gy", split_axis=3, concat_axis=2, tiled=True)
    return jnp.swapaxes(returned, 2, 3)


def expand(fields):
    return extended(fields, (("gx", 3), ("gy", 2)), 3)


def shards(velocity, weights_x, weights_y, acoustic, wall_mask):
    acoustic = acoustic.astype(jnp.float32)
    flow_x = velocity[0]
    flow_y = velocity[1]
    tensor = jnp.stack([flow_x * flow_x, flow_x * flow_y, flow_y * flow_y])
    count_gx = lax.axis_size("gx")
    count_gy = lax.axis_size("gy")
    place_x = lax.axis_index("gx")
    place_y = lax.axis_index("gy")
    local_y = tensor.shape[2]
    local_x = tensor.shape[3]
    length_x = local_x * count_gx
    length_y = local_y * count_gy

    def forward_real(portion):
        return transform(portion, -1, "real_in")

    def finish_x(portion):
        return refine(transform(portion, 1, "real_out"), weights_x)

    spectra = lines_x(tensor, forward_real)
    share_x = local_x // count_gy
    line_x = spectral_index(place_x * local_x + place_y * share_x + jnp.arange(share_x), length_x)[
        :, None
    ]
    line_y = spectral_index(jnp.arange(length_y), length_y)[None, :]

    def solve_y(portion):
        solved = project(transform(portion, -1, "complex"), line_x, line_y)
        return refine(transform(solved, 1, "complex"), weights_y)

    pressure = lines_y(spectra, solve_y)
    source = lines_x(pressure, finish_x)[0]
    open_cells = (1 - wall_mask).astype(jnp.float32)
    first_rate = tendency(expand(acoustic), source)
    middle = open_cells * (acoustic + time_step * first_rate)
    second_rate = tendency(expand(middle), source)
    return (open_cells * (acoustic + 0.5 * time_step * (first_rate + second_rate))).astype(
        jnp.bfloat16
    )


def solution(mesh):
    in_specs = (P(None, None, "gy", "gx"), P(), P(), P(None, None, "gy", "gx"), P(None, "gy", "gx"))
    out_specs = P(None, None, "gy", "gx")

    def chosen(velocity, weights_x, weights_y, acoustic, wall_mask):
        sizes = (mesh.shape["gx"], mesh.shape["gy"], velocity.shape, acoustic.shape)
        plan = fast_shards if fits(*sizes) else shards
        return plan(velocity, weights_x, weights_y, acoustic, wall_mask)

    return jax.shard_map(
        chosen, mesh=mesh, in_specs=in_specs, out_specs=out_specs, check_vma=False
    )
```

```python
import functools
import math

import jax
import jax.numpy as jnp
import ml_dtypes
import numpy as np
from jax import lax
from jax.experimental import pallas as pl
from jax.experimental.pallas import tpu as pltpu
from jax.sharding import PartitionSpec as P

stencil_weights = (0.75, -0.15, 1.0 / 60.0)
mean_flow = 0.3
time_step = 0.5
whole_weights = (45.0, -9.0, 1.0)

LANES = 128
RADIX = 8
HALO = 8
MARGIN = 16
TILE = 128
ROOT = math.sqrt(0.5)
STRIP = {2: (0, 6), 3: (6, 6), 1: (12, 3), 4: (15, 3), 5: (20, 4)}
STRIP_ROWS = 24
PARTS = 4
BF16 = jnp.bfloat16
F32 = jnp.float32


def halves(table):
    high = table.astype(np.float32).astype(ml_dtypes.bfloat16)
    low = (table - high.astype(np.float64)).astype(np.float32).astype(ml_dtypes.bfloat16)
    return high, low


def packed_columns(cosine, sine):
    half = LANES // 2
    parts = []
    for first in range(0, cosine.shape[1], half):
        parts += [cosine[:, first : first + half], sine[:, first : first + half]]
    return np.concatenate(parts, axis=1)


@functools.lru_cache(maxsize=None)
def x_tables(length):
    base = length // RADIX
    m = np.arange(base)[:, None]
    q = np.arange(base)[None, :]
    angle = 2.0 * np.pi * ((m * q) % base) / base
    cosine, sine = np.cos(angle), np.sin(angle)
    full = np.concatenate([packed_columns(cosine, -sine), packed_columns(sine, cosine)], axis=0)
    half = base // 2
    zero_cos, zero_sin = cosine[:, :half].copy(), -sine[:, :half]
    zero_cos[:, 0] = 0.0
    zero_sin = zero_sin.copy()
    zero_sin[:, 0] = (-1.0) ** np.arange(base)
    zero = packed_columns(zero_cos, zero_sin)
    shifted = 2.0 * np.pi * ((m * (RADIX * q[:, :half] + RADIX // 2)) % length) / length
    middle = packed_columns(np.cos(shifted), -np.sin(shifted))
    turns = 2.0 * np.pi * np.arange(1, RADIX // 2)[:, None] * np.arange(base)[None, :] / length
    return full, zero, middle, np.cos(turns), np.sin(turns)


@functools.lru_cache(maxsize=None)
def y_tables(length):
    base = length // RADIX
    index = np.arange(base)
    angle = 2.0 * np.pi * ((index[:, None] * index[None, :]) % base) / base
    both = np.concatenate([np.cos(angle), np.sin(angle)], axis=0)
    turns = 2.0 * np.pi * np.arange(RADIX)[:, None] * index[None, :] / length
    turns = np.concatenate([np.cos(turns), np.sin(turns)], axis=0).T
    high, rest = halves(turns)
    low = turns - high.astype(np.float64) - rest.astype(np.float64)
    return both, np.concatenate([high, rest, low.astype(ml_dtypes.bfloat16)], axis=1)


@functools.lru_cache(maxsize=None)
def wave_table(length, count):
    slots = LANES // 4
    base = length // RADIX
    waves = []
    for residue in (1, 2, 3):
        waves.append(RADIX * np.arange(base) + residue)
    waves.append(RADIX * np.arange(base // 2))
    waves.append(RADIX * np.arange(base // 2) + RADIX // 2)
    waves = np.concatenate(waves)
    waves = np.where(waves == 0, length // 2, waves)
    waves = np.where(waves < length // 2, waves, waves - length).reshape(count, slots)
    return np.tile(waves, (1, 4)).astype(np.float32)


@functools.lru_cache(maxsize=None)
def band_tables(rows):
    across = np.zeros((4 * LANES, 2 * LANES))
    column = np.arange(2 * LANES)
    down = np.zeros((rows, rows))
    for index, weight in enumerate(whole_weights):
        distance = index + 1
        across[column + LANES + distance, column] = weight
        across[column + LANES - distance, column] = -weight
        down += weight * (np.eye(rows, k=distance) - np.eye(rows, k=-distance))
    return across.astype(ml_dtypes.bfloat16), down.astype(ml_dtypes.bfloat16)


def beside(*tables):
    high, low = halves(np.concatenate(tables, axis=1))
    return np.concatenate([high, low], axis=0)


def split(values):
    high = values.astype(BF16)
    return high, (values - high.astype(F32)).astype(BF16)


def dot(left, right):
    return jnp.dot(left, right, preferred_element_type=F32)


def exact_dot(left, right):
    left_high, left_low = left
    right_high, right_low = right
    return dot(left_high, right_high) + (dot(left_low, right_high) + dot(left_high, right_low))


def lane_index(shape):
    return lax.broadcasted_iota(jnp.int32, shape, len(shape) - 1)


def spin(values, shift):
    return pltpu.roll(values, shift % values.shape[-1], values.ndim - 1)


def lane_tile(values, index):
    return values[:, index * LANES : (index + 1) * LANES]


def x_parts(tables, base):
    wide = 2 * base
    full = (tables[:wide], tables[wide : 2 * wide])
    at = 2 * wide
    high, low = tables[at : at + base], tables[at + base : at + 2 * base]
    return full, (high[:, :base], low[:, :base]), (high[:, base:], low[:, base:])


def pieces_kernel(velocity, *pieces):
    rows = pieces[0].shape[1]
    place = lax.axis_index("gx")
    for mask, piece in enumerate(pieces):
        start = pl.multiple_of((place ^ mask) * rows, 8)
        for c in range(2):
            piece[c] = velocity[c, 0, pl.ds(start, rows), :]


def rows_kernel(top, low, top_wall, low_wall, top_flow, low_flow, first, last):
    small, width = top.shape[2], top_flow.shape[3]
    first[...] = jnp.zeros(first.shape, F32)
    last[...] = jnp.zeros(last.shape, F32)
    for k, (start, rows) in STRIP.items():
        lanes = slice(0, width) if k == PARTS + 1 else slice(None)
        if k < PARTS:
            upper, lower = top[k, 0].astype(F32)[:HALO], low[k, 0].astype(F32)[small - HALO :]
        elif k == PARTS:
            upper, lower = 1.0 - top_wall[0].astype(F32), 1.0 - low_wall[0].astype(F32)
        else:
            upper, lower = top_flow[0, 0], low_flow[0, 0]
        first[start : start + rows, lanes] = upper[:rows]
        last[start : start + rows, lanes] = lower[HALO - rows :]


def strip(ref, k, upper, lanes=slice(None)):
    if k not in STRIP:
        return jnp.zeros((HALO, ref[0:1, lanes].shape[1]), F32)
    start, rows = STRIP[k]
    values = ref[start : start + rows, lanes]
    blank = jnp.zeros((HALO - rows, values.shape[1]), F32)
    return jnp.concatenate([blank, values] if upper else [values, blank], axis=0)


def columns_kernel(
    has, left, right, left_wall, right_wall, left_flow, right_flow, above, below, to_right, to_left
):
    parts = left.shape[0]
    wide, flow_wide = above.shape[1], above.shape[1] // 2
    gap = jnp.zeros((LANES - 2 * HALO, LANES), F32)

    def tall(k, inner, first, sides):
        lanes = slice(first, first + LANES)
        over, under = strip(above, k, True, lanes), strip(below, k, False, lanes)
        return jnp.concatenate([inner, under * sides[1], gap, over * sides[0]], axis=0).T

    for k in range(parts + 1):
        at = slice(k * HALO, (k + 1) * HALO)
        if k < parts:
            near, far = left[k, 0].astype(F32), right[k, 0].astype(F32)
        else:
            near, far = 1.0 - left_wall[0].astype(F32), 1.0 - right_wall[0].astype(F32)
        sides = (has[2], has[3])
        to_left[at, :] = tall(k, near, 0, sides)[:HALO]
        to_right[at, :] = tall(k, far, wide - LANES, sides)[LANES - HALO :]
    k = parts + 1
    at = slice(k * HALO, (k + 1) * HALO)
    size = left_flow.shape[2] + LANES
    blank = jnp.zeros((HALO, to_left.shape[1] - size), F32)
    to_left[at, :size] = tall(k, left_flow[0, 0], 0, (1.0, 1.0))[:HALO]
    to_right[at, :size] = tall(k, right_flow[0, 0], flow_wide - LANES, (1.0, 1.0))[LANES - HALO :]
    to_left[at, size:] = blank
    to_right[at, size:] = blank


def sides_kernel(has, place, velocity, above, below, from_left, from_right, sides, squares, mark):
    parts, tall, _ = sides.shape
    gap = jnp.zeros((LANES - 2 * HALO, tall), F32)
    for k in range(parts):
        at = slice(k * HALO, (k + 1) * HALO)
        tile = [from_right[at, :] * has[1], gap, from_left[at, :] * has[0]]
        sides[k] = jnp.concatenate(tile, axis=0).T
    at = slice(parts * HALO, (parts + 1) * HALO)
    rows, local = velocity.shape[2:]
    size = rows + LANES
    tile = [from_right[at, :size], gap[:, :size], from_left[at, :size]]
    tile = jnp.concatenate(tile, axis=0).T
    tile = tile * tile
    mark[0] = place[0]
    over, under = (strip(ref, parts, ref is above, slice(0, local)) for ref in (above, below))
    squares[:HALO, :local] = over * over
    squares[HALO : HALO + rows, :local] = velocity[0, 0] * velocity[0, 0]
    squares[HALO + rows :, :local] = under * under
    squares[:HALO, local:] = tile[size - HALO :]
    squares[HALO : HALO + rows, local:] = tile[:rows]
    squares[HALO + rows :, local:] = tile[rows : rows + HALO]


def forward_x_kernel(*refs):
    *pieces, tables, turns, out, total, lines, made, sent = refs
    count, _, rows, local = lines.shape
    place = lax.axis_index("gx")
    for mask, piece in enumerate(pieces):
        lines[place ^ mask] = piece[...]
    base = turns.shape[1]
    per = local // base
    u = [lines[t // per, 0, :, (t % per) * base : (t % per + 1) * base] for t in range(RADIX)]
    v = [lines[t // per, 1, :, (t % per) * base : (t % per + 1) * base] for t in range(RADIX)]
    energy = sum(b * b for b in v)
    energy = jnp.sum(energy.reshape(rows // 8, 8, base), axis=0)
    total[...] = sum(energy[:, k : k + LANES] for k in range(0, base, LANES))
    fields = ([a * a - b * b for a, b in zip(u, v)], [2.0 * a * b for a, b in zip(u, v)])
    zeros, mids, reals, imags = [], [], [[], [], []], [[], [], []]
    for a in fields:
        s04, s26, s15, s37 = a[0] + a[4], a[2] + a[6], a[1] + a[5], a[3] + a[7]
        d04, d26, d15, d37 = a[0] - a[4], a[2] - a[6], a[1] - a[5], a[3] - a[7]
        zeros.append((s04 + s26) + (s15 + s37))
        mids.append((s04 + s26) - (s15 + s37))
        minus, plus = ROOT * (d15 - d37), ROOT * (d15 + d37)
        turned = (
            (d04 + minus, -d26 - plus),
            (s04 - s26, s37 - s15),
            (d04 - minus, d26 - plus),
        )
        for index, (real, imag) in enumerate(turned):
            c, s = turns[index : index + 1, :], turns[index + 3 : index + 4, :]
            reals[index].append(real * c + imag * s)
            imags[index].append(imag * c - real * s)
    stacked = jnp.concatenate(
        [
            jnp.concatenate([jnp.concatenate(reals[i], axis=0) for i in range(3)], axis=0),
            jnp.concatenate([jnp.concatenate(imags[i], axis=0) for i in range(3)], axis=0),
        ],
        axis=1,
    )
    full, zero, middle = x_parts(tables, base)
    full = exact_dot(split(stacked), full)
    zero = exact_dot(split(jnp.concatenate(zeros, axis=0)), zero)
    middle = exact_dot(split(jnp.concatenate(mids, axis=0)), middle)
    low = lane_index((rows, LANES)) % 64 < 32
    target, copies = 0, []
    blocks = [full[2 * rows * i : 2 * rows * (i + 1)] for i in range(3)] + [zero, middle]
    for block in blocks:
        start = target
        for first in range(0, block.shape[1], LANES):
            a = block[:rows, first : first + LANES]
            c = block[rows:, first : first + LANES]
            made[target] = jnp.where(low, a, spin(c, 32))
            made[target + 1] = jnp.where(low, spin(a, -32), c)
            target += 2
        group = pl.ds(start, target - start)
        copies.append(pltpu.make_async_copy(made.at[group], out.at[group], sent.at[len(copies)]))
        copies[-1].start()
    for copy in copies:
        copy.wait()


def eighths(x, turn):
    s04, s26, s15, s37 = x[0] + x[4], x[2] + x[6], x[1] + x[5], x[3] + x[7]
    d04, d26, d15, d37 = x[0] - x[4], x[2] - x[6], x[1] - x[5], x[3] - x[7]
    quarter = turn(s15 - s37)
    spun_26, spun_37 = turn(d26), turn(d37)
    one, three = d15 + spun_37, d15 - spun_37
    spun_one, spun_three = turn(one), turn(three)
    one = ROOT * (one + spun_one)
    three = ROOT * (spun_three - three)
    return [
        (s04 + s26) + (s15 + s37),
        (d04 + spun_26) + one,
        (s04 - s26) + quarter,
        (d04 - spun_26) + three,
        (s04 + s26) - (s15 + s37),
        (d04 + spun_26) - one,
        (s04 - s26) - quarter,
        (d04 - spun_26) - three,
    ]


def solve_y_kernel(count_x, _, lines, total, wave, both, turns, out, held, spread, made, sent):
    count, rows, _ = lines.shape
    base = turns.shape[0]
    length = count * rows
    block = count_x * rows
    per = base // rows
    lanes = lane_index((base, LANES))
    sign = jnp.where(lanes < 64, 1.0, -1.0).astype(F32)

    def minus_i(z):
        return spin(z, 64) * sign

    def plus_i(z):
        return spin(z, 64) * -sign

    fields = [
        jnp.concatenate([lines[t * per + k] for k in range(per)], axis=0) for t in range(RADIX)
    ]
    mixed = eighths(fields, minus_i)
    terms, columns = turns.shape[1], 2 * RADIX
    picked = lax.broadcasted_iota(jnp.int32, (terms, columns * LANES), 0) % columns
    lane = lane_index(picked.shape)
    value = jnp.where((lane >= RADIX * LANES) & (lane % LANES >= 64), -1.0, 1.0)
    spread[...] = dot(turns[...], jnp.where(picked == lane // LANES, value, 0.0).astype(BF16))
    cosines = [spread[:, r * LANES : (r + 1) * LANES] for r in range(RADIX)]
    sines = [spread[:, (r + RADIX) * LANES : (r + RADIX + 1) * LANES] for r in range(RADIX)]
    mixed = [mixed[0]] + [
        mixed[r] * cosines[r] + spin(mixed[r], 64) * sines[r] for r in range(1, RADIX)
    ]
    tables = (both[: 2 * base], both[2 * base :])
    product = exact_dot(tables, split(jnp.concatenate(mixed, axis=1)))
    kx = wave[0:1, :]
    first = lanes % 64 < 32
    edge = jnp.float32(length // 2)
    square_kx = kx * kx
    alone = jnp.where(first, square_kx, 0.0)
    slope = jnp.where(first | (kx == -edge), 0.0, jnp.broadcast_to(kx, lanes.shape))
    q = lax.broadcasted_iota(jnp.int32, lanes.shape, 0)
    low_ky = RADIX * (q - jnp.where(q < base // 2, 0, base)).astype(F32)
    terms = []
    for r in range(RADIX):
        at = slice(r * LANES, (r + 1) * LANES)
        spectrum = product[:base, at] + minus_i(product[base:, at])
        ky = low_ky + float(r)
        symbol = alone + slope * ky
        if r == 0:
            corner = jnp.where((kx == -edge) & ~first, edge * edge, 0.0)
            symbol = jnp.where(ky == -edge, jnp.where(first, alone, corner), symbol)
        square = square_kx + ky * ky
        guess = pl.reciprocal(square, approx=True)
        terms.append(symbol * (guess * (2.0 - square * guess)) * spectrum)
    pairs = [
        jnp.where(first, low + spin(low, -32), high + spin(high, 32))
        for low, high in zip(terms[:4], terms[4:])
    ]
    product = exact_dot(tables, split(jnp.concatenate(pairs, axis=1)))
    mixed = []
    for r in range(RADIX // 2):
        at = slice(r * LANES, (r + 1) * LANES)
        value = product[:base, at] + plus_i(product[base:, at])
        cosine = jnp.where(first, cosines[r], cosines[r + 4])
        sine = jnp.where(first, sines[r], sines[r + 4])
        value = value * cosine - spin(value, 64) * sine
        value = jnp.where(first, value + spin(value, -32), spin(value, 32) - value)
        if r == 2:
            value = jnp.where(first, value, plus_i(value))
        elif r:
            turned = plus_i(value)
            odd = value + turned if r == 1 else turned - value
            value = jnp.where(first, value, ROOT * odd)
        mixed.append(value)
    even, odd = mixed[0] + mixed[2], mixed[0] - mixed[2]
    side, turned = mixed[1] + mixed[3], plus_i(mixed[1] - mixed[3])
    for t, values in enumerate((even + side, odd + turned, even - side, odd - turned)):
        start = MARGIN + 2 * t * base
        held[start : start + base, :] = values
        held[start + base : start + 2 * base, :] = spin(values, -32)
    held[0:MARGIN, :] = held[length : length + MARGIN, :]
    held[length + MARGIN : length + 2 * MARGIN, :] = held[MARGIN : 2 * MARGIN, :]
    spare = total[...] + spin(total[...], 32)
    kept = rows + 2 * MARGIN // count_x
    half = made.shape[1]
    rest = kept - half
    low = lane_index((8, LANES)) % 64 < 32
    copies = []
    for target in range(count):
        start = (target // count_x) * block + (target % count_x) * kept
        for row in range(0, half, 8):
            a = held[start + row : start + row + 8, :]
            if row < rest:
                b = spin(held[start + half + row : start + half + row + 8, :], 32)
            else:
                b = spare
            made[target, row : row + 8, :] = jnp.where(low, a, b)
        if (target + 1) % RADIX == 0:
            group = pl.ds(target + 1 - RADIX, RADIX)
            copies.append(pltpu.make_async_copy(made.at[group], out.at[group], sent.at[len(copies)]))
            copies[-1].start()
    for copy in copies:
        copy.wait()


def inverse_x_kernel(
    kept, scale, place, lines, tables, turns, *refs
):
    *outs, held = refs
    count, half, _ = lines.shape
    base = turns.shape[1]
    length = RADIX * base
    rest = kept - half
    low = lane_index((half, LANES)) % 64 < 32
    groups, spare = [], None
    for first in range(0, count, 2):
        even, odd = lines[first], lines[first + 1]
        a = jnp.where(low, even, spin(odd, 32))
        b = jnp.where(low, spin(even, -32), odd)
        groups.append(jnp.concatenate([a, b[:rest]], axis=0))
        extra = b[rest : rest + 8]
        spare = extra if spare is None else spare + extra
    mean = jnp.sum(spare) * scale
    wide = 2 * base // LANES
    narrow = base // LANES
    stacked = jnp.concatenate(
        [jnp.concatenate(groups[i * wide : (i + 1) * wide], axis=1) for i in range(3)], axis=0
    )
    at = 3 * wide
    zeros = jnp.concatenate(groups[at : at + narrow], axis=1)
    mids = jnp.concatenate(groups[at + narrow : at + 2 * narrow], axis=1)
    full, zero, middle = x_parts(tables, base)
    full = exact_dot(split(stacked), full)
    zero = exact_dot(split(zeros), zero) * scale
    mid = exact_dot(split(mids), middle) * scale
    turned = []
    for i in range(3):
        real = full[i * kept : (i + 1) * kept, :base]
        imag = full[i * kept : (i + 1) * kept, base:]
        c = turns[i : i + 1, :] * (2.0 * scale)
        s = turns[i + 3 : i + 4, :] * (2.0 * scale)
        turned.append((real * c - imag * s, real * s + imag * c))
    for t in range(RADIX):
        value = zero + mid if t % 2 == 0 else zero - mid
        for i, (real, imag) in enumerate(turned):
            eighth = t * (i + 1) % RADIX
            c = (1.0, ROOT, 0.0, -ROOT, -1.0, -ROOT, 0.0, ROOT)[eighth]
            s = (0.0, ROOT, 1.0, ROOT, 0.0, -ROOT, -1.0, -ROOT)[eighth]
            if c:
                value = value + c * real
            if s:
                value = value - s * imag
        held[:, t * base : (t + 1) * base] = mean - value
    targets, local = len(outs), outs[0].shape[1] - LANES
    right = lane_index((kept, LANES)) < 64
    for mask, out in enumerate(outs):
        start = pl.multiple_of((place[0] ^ mask) * local, LANES)
        after = pl.multiple_of(jnp.where(start + local == length, 0, start + local), LANES)
        before = pl.multiple_of(jnp.where(start == 0, length, start) - LANES, LANES)
        out[:, :local] = held[:, pl.ds(start, local)]
        out[:, local:] = jnp.where(
            right, held[:, pl.ds(after, LANES)], held[:, pl.ds(before, LANES)]
        )


def slopes_x(parts, band, with_edge):
    tiles = parts[0].shape[-1] // LANES
    pieces = []
    for first in list(range(0, tiles - 1, 2)) + ([tiles - 1] if with_edge else []):
        steps = (-1, 0, 1, 2) if first < tiles - 1 else (-1, 0, 1)
        table = band[...] if first < tiles - 1 else band[: 3 * LANES, :LANES]
        order = [(first + step) % tiles for step in steps]
        piece = None
        for part in parts:
            term = dot(jnp.concatenate([lane_tile(part, t) for t in order], axis=1), table)
            piece = term if piece is None else piece + term
        pieces.append(piece)
    return jnp.concatenate(pieces, axis=1)


def edged(k, side, center, up, down, above, below, sides, has, first=0):
    step = pl.program_id(0) + first
    tile, width = center.shape
    tall = sides.shape[1]
    last = (tall - LANES) // tile - 1
    base = pl.multiple_of(step * tile, 8)
    before = pl.multiple_of(jnp.where(step == 0, tall, base) - HALO, 8)
    over = jnp.where(step == 0, strip(above, k, True) * has[2], up)
    under = jnp.where(step == last, strip(below, k, False) * has[3], down)
    rows = (
        (over, sides[side, pl.ds(before, HALO), :]),
        (center, sides[side, pl.ds(base, tile), :]),
        (under, sides[side, pl.ds(pl.multiple_of(base + tile, 8), HALO), :]),
    )
    return jnp.concatenate([jnp.concatenate(pair, axis=1) for pair in rows], axis=0)


def edged_open(k, side, wall, wall_up, wall_down, above, below, sides, has, first=0):
    open_cells = [1.0 - ref[0].astype(F32) for ref in (wall, wall_up, wall_down)]
    return edged(k, side, *open_cells, above, below, sides, has, first)


def quiet_step_kernel(
    first, has, place, center, up, down, wall, wall_up, wall_down, above, below, sides, across, along, along_inner, calm, density, shown_open, mark
):
    parts, _, tile, width = center.shape
    high = tile + 2 * HALO
    opened = edged_open(parts, parts, wall, wall_up, wall_down, above, below, sides, has, first)
    values = []
    for k in range(parts):
        value = edged(
            k,
            k,
            center[k, 0].astype(F32),
            up[k, 0].astype(F32)[up.shape[2] - HALO :],
            down[k, 0].astype(F32)[:HALO],
            above,
            below,
            sides,
            has,
            first,
        )
        values.append(value)

    def drops(x, along_b, along_p):
        diverge = x[1] + along_b
        return (
            diverge + mean_flow * x[0],
            x[3] + mean_flow * x[1],
            along_p + mean_flow * x[2],
            diverge + mean_flow * x[3],
        )

    short = [value.astype(BF16) for value in values]
    x = slopes_x((jnp.concatenate(short, axis=0),), across, True)
    x = [x[k * high : (k + 1) * high] for k in range(parts)]
    table = along[...]
    dropped = drops(x, dot(table, short[2]), dot(table, short[3]))
    middle = [opened * (v - (time_step / 60.0) * d) for v, d in zip(values, dropped)]
    inner = slice(HALO, HALO + tile)
    x = slopes_x(split(jnp.concatenate([value[inner] for value in middle], axis=0)), across, False)
    x = [x[k * tile : (k + 1) * tile] for k in range(parts)]
    table = along_inner[...]
    y = [sum(dot(table, part) for part in split(middle[k][:, :width])) for k in (2, 3)]
    dropped = drops(x, *y)
    shown = opened[inner, :width]
    for k in range(parts):
        start = 0.5 * values[k][inner, :width] - (0.5 * time_step / 60.0) * dropped[k]
        value = shown * start + 0.5 * middle[k][inner, :width]
        if k == 0:
            density[0, 0] = value.astype(BF16)
        else:
            calm[k - 1] = value
    shown_open[0] = (time_step * opened).astype(BF16)
    mark[0] = place[0]


def tables_kernel(place, weights_x, weights_y, rise_x, rise_y, mark):
    mark[0] = place[0]
    _, tiles, reach_x, lanes = rise_x.shape
    wide, length_x = (tiles - 1) * lanes, weights_x.shape[1]
    first = place[0] * wide
    half = LANES // 2

    def weights(ref, start, size):
        length = ref.shape[1]
        start = jnp.where(start < 0, start + length, jnp.where(start >= length, start - length, start))
        return ref[:, pl.ds(pl.multiple_of(start, LANES), size)]

    cells = lax.broadcasted_iota(jnp.int32, (reach_x, lanes), 0)
    fine = lax.broadcasted_iota(jnp.int32, (reach_x, lanes), 1)
    right, left = weights(weights_x, first + wide, LANES), weights(weights_x, first - LANES, LANES)
    edge = jnp.where(lane_index(right.shape) < half, right, left)
    edge = jnp.concatenate([edge, edge], axis=1)
    for k in range(tiles):
        own = weights(weights_x, first + k * lanes, lanes) if k < tiles - 1 else edge
        target = fine // 2 - 1
        if k == tiles - 1:
            target = jnp.where(fine < half, target, target + half)
        value = jnp.zeros(fine.shape, F32)
        for t in range(4):
            value = jnp.where(cells == (target + t) % reach_x, own[t : t + 1, :], value)
        rise_x[0, k], rise_x[1, k] = split(value)
    steps, high, reach = rise_y.shape
    tall = steps * TILE
    first = place[1] * tall
    own = [weights(weights_y, first + k * LANES, LANES) for k in range(-1, tall // LANES + 1)]
    own = jnp.concatenate([jnp.concatenate(own, axis=1), jnp.zeros((4, tall + 2 * LANES), F32)], axis=0).T
    cells = lax.broadcasted_iota(jnp.int32, (high, reach), 1)
    last = cells >= reach // 3 * 2
    cells = cells % (reach // 3)
    target = lax.broadcasted_iota(jnp.int32, (high, reach), 0) // 2 + (HALO // 2 - 1)
    for k in range(steps):
        start = LANES - HALO + k * TILE
        value = jnp.zeros((high, reach), F32)
        for t in range(4):
            value = jnp.where(cells == target + t, own[start : start + high, t : t + 1], value)
        upper, lower = split(value)
        rise_y[k] = jnp.where(last, lower, upper)


def source_kernel(squares, opened, rise_x, rise_y, quiet, across, along, _, *refs):
    *lines, out, squared, cells_open, matrix, rows_matrix, calm, band, column, held, raised, done, fetched, kept = refs
    steps = done.shape[0]
    tile, width = calm.shape[2:]
    high = tile + 2 * HALO
    rows = lines[0].shape[0]
    place = lax.axis_index("gx")

    def tile_copies(k):
        part = quiet.at[:, pl.ds(k * tile, tile), :]
        return (
            pltpu.make_async_copy(part, calm.at[k % 2], fetched.at[k % 2]),
            pltpu.make_async_copy(opened.at[k], cells_open.at[k % 2], fetched.at[2 + k % 2]),
        )

    def done_copy(k):
        part = out.at[1:, 0, pl.ds(k * tile, tile), :]
        return pltpu.make_async_copy(done.at[k], part, kept.at[k])

    arrays = ((squares, squared), (rise_x, matrix), (rise_y, rows_matrix), (across, band), (along, column))
    copies = [
        pltpu.make_async_copy(source, target, fetched.at[4 + k])
        for k, (source, target) in enumerate(arrays)
    ]
    pieces = [
        pltpu.make_async_copy(
            piece,
            held.at[pl.ds(pl.multiple_of((place ^ mask) * rows, 8), rows), :],
            fetched.at[4 + len(arrays) + mask],
        )
        for mask, piece in enumerate(lines)
    ]
    for copy in (*pieces, *copies, *tile_copies(0), *tile_copies(1)):
        copy.start()
    for copy in pieces + copies[:1]:
        copy.wait()

    level = held[MARGIN - HALO : MARGIN - HALO + squared.shape[0], :] - squared[...]
    count = level.shape[1] // LANES
    near = lane_index((level.shape[0], LANES)) < 64
    around = []
    for k in range(count):
        after, before = lane_tile(level, (k + 1) % count), lane_tile(level, (k - 1) % count)
        around.append(split(jnp.concatenate([lane_tile(level, k), jnp.where(near, after, before)], axis=1)))
    copies[1].wait()
    for k in range(count):
        lanes = 2 * LANES if k < count - 1 else LANES
        value = split(exact_dot(around[k], [matrix[part, k, :, :lanes] for part in range(2)]))
        for part in range(2):
            raised[part, :, 2 * k * LANES : 2 * k * LANES + lanes] = value[part]
    for copy in copies[2:]:
        copy.wait()

    reach = rows_matrix.shape[2] // 3
    for k in range(steps):
        start = k * (tile // 2)
        window = [raised[part, start : start + reach, :] for part in (0, 1, 0)]
        calm_here, open_here = tile_copies(k)
        open_here.wait()
        free = cells_open[k % 2].astype(F32)
        value = free * dot(rows_matrix[k], jnp.concatenate(window, axis=0))
        inner = value[HALO : HALO + tile]
        shown = (0.5 / 60.0) * free[HALO : HALO + tile, :width]
        x = shown * slopes_x(split(inner), band, False)
        y = shown * sum(dot(column[...], part) for part in split(value[:, :width]))
        calm_here.wait()
        still = calm.at[k % 2]
        done[k, 0] = (still[0] - x).astype(BF16)
        done[k, 1] = (still[1] - y).astype(BF16)
        done[k, 2] = (still[2] + inner[:, :width] - mean_flow * x).astype(BF16)
        done_copy(k).start()
        if k + 2 < steps:
            for copy in tile_copies(k + 2):
                copy.start()
    for k in range(steps):
        done_copy(k).wait()


def call(
    kernel, operands, outs, scratch=(), steps=0, specs=None, out_specs=None, after=(), aliases=None, megabytes=24, flops=0, moved=0, name=None
):
    count = len(operands)

    def body(*refs):
        kernel(*refs[:count], *refs[count + len(after) :])

    def whole(array):
        zeros = (0,) * len(array.shape)
        return pl.BlockSpec(array.shape, lambda *_: zeros)

    arguments = {}
    chosen = specs or {}
    if steps:
        arguments["grid"] = (steps,)
        in_specs = [chosen.get(i, whole(o)) for i, o in enumerate(operands)]
        arguments["out_specs"] = jax.tree.map(whole, outs) if out_specs is None else out_specs
    else:
        local = pl.BlockSpec(memory_space=pltpu.VMEM)
        in_specs = [chosen.get(i, local) for i in range(count)]
        if out_specs is not None:
            arguments["out_specs"] = out_specs
    return pl.pallas_call(
        body,
        out_shape=outs,
        in_specs=in_specs + [pl.BlockSpec(memory_space=pl.ANY)] * len(after),
        scratch_shapes=list(scratch),
        input_output_aliases=aliases or {},
        compiler_params=pltpu.CompilerParams(vmem_limit_bytes=megabytes << 20),
        cost_estimate=pl.CostEstimate(flops=flops, bytes_accessed=moved, transcendentals=0),
        name=name,
        **arguments,
    )(*operands, *after)


def ring(array, axis, step):
    size = lax.axis_size(axis)
    return lax.ppermute(array, axis, [(i, (i + step) % size) for i in range(size)])


def swap(array, axis, mask):
    return lax.ppermute(array, axis, [(i, i ^ mask) for i in range(lax.axis_size(axis))])


def shaped(*shape, kind=F32):
    return jax.ShapeDtypeStruct(shape, kind)


def pressure_lines(pieces, gathered, spread, stepped):
    _, rows, local_x = pieces[0].shape
    count_x, count_y = lax.axis_size("gx"), lax.axis_size("gy")
    count = count_x * count_y
    scalars = {0: pl.BlockSpec(memory_space=pltpu.SMEM)}
    length_x, length_y = local_x * count_x, rows * count
    full, zero, middle, cos_turn, sin_turn = x_tables(length_x)
    turns = np.zeros((8, cos_turn.shape[1]), np.float32)
    turns[0:3], turns[3:6] = cos_turn, sin_turn
    spectra, total = call(
        forward_x_kernel,
        (*pieces, np.concatenate([beside(full), beside(zero, middle)]), turns),
        (shaped(count, rows, LANES), shaped(8, LANES)),
        (
            pltpu.VMEM((count_x, 2, rows, local_x), F32),
            pltpu.VMEM((count, rows, LANES), F32),
            pltpu.SemaphoreType.DMA((5,)),
        ),
        out_specs=(pl.BlockSpec(memory_space=pl.ANY), pl.BlockSpec(memory_space=pltpu.VMEM)),
        after=gathered,
        flops=10**9,
        moved=4 << 20,
        name="forward_x",
    )
    spectra = lax.all_to_all(spectra, ("gy", "gx"), 0, 0, tiled=True)
    place = lax.axis_index("gy") * count_x + lax.axis_index("gx")
    waves = jnp.asarray(wave_table(length_x, count))
    wave = lax.dynamic_slice(waves, (place, 0), (1, LANES))
    both, turns_y = y_tables(length_y)
    kept = rows + 2 * MARGIN // count_x
    half = (kept // 2 + 8) // 8 * 8
    solved = call(
        functools.partial(solve_y_kernel, count_x),
        (spread, spectra, total, wave, beside(both), turns_y),
        shaped(count, half, LANES),
        (
            pltpu.VMEM((length_y + 2 * MARGIN, LANES), F32),
            pltpu.VMEM((length_y // RADIX, 2 * RADIX * LANES), F32),
            pltpu.VMEM((count, half, LANES), F32),
            pltpu.SemaphoreType.DMA((count // RADIX,)),
        ),
        specs=scalars,
        out_specs=pl.BlockSpec(memory_space=pl.ANY),
        flops=4 * 10**9,
        moved=6 << 20,
        name="solve_y",
    )
    solved = lax.all_to_all(solved, ("gy", "gx"), 0, 0, tiled=True)
    back = 2.0 * zero.T
    back[LANES // 2] *= 0.5
    tables = np.concatenate(
        [beside(full.T), beside(back, 2.0 * middle.T)]
    )
    pressed = call(
        functools.partial(inverse_x_kernel, kept, 1.0 / (length_x * length_y)),
        (stepped, solved, tables, turns),
        (shaped(kept, local_x + LANES),) * count_x,
        (pltpu.VMEM((kept, length_x), F32),),
        specs=scalars,
        flops=10**9,
        moved=4 << 20,
        name="inverse_x",
    )
    return [piece if mask == 0 else swap(piece, "gx", mask) for mask, piece in enumerate(pressed)]


def fast_shards(velocity, weights_x, weights_y, acoustic, wall_mask):
    parts, _, tall, wide = acoustic.shape
    _, _, local_y, local_x = velocity.shape
    count_x, count_y = lax.axis_size("gx"), lax.axis_size("gy")
    place_x, place_y = lax.axis_index("gx"), lax.axis_index("gy")
    full, high, steps = wide + LANES, TILE + 2 * HALO, tall // TILE
    strips = (parts + 2) * HALO
    small = 2 * HALO
    has = jnp.stack([place_x > 0, place_x < count_x - 1, place_y > 0, place_y < count_y - 1])
    has = has.astype(F32)
    scalars = pl.BlockSpec(memory_space=pltpu.SMEM)

    def at(block, *index):
        return pl.BlockSpec(block, lambda i: index)

    own = place_x.astype(jnp.int32).reshape(1)
    sent = call(
        pieces_kernel,
        (velocity,),
        (shaped(2, local_y // count_x, local_x),) * count_x,
        moved=2 << 20,
        megabytes=8,
        name="pieces",
    )
    moved = [piece if mask == 0 else swap(piece, "gx", mask) for mask, piece in enumerate(sent)]
    first, last = call(
        rows_kernel,
        (acoustic, acoustic, wall_mask, wall_mask, velocity, velocity),
        (shaped(STRIP_ROWS, wide),) * 2,
        steps=1,
        specs={
            0: at((parts, 1, small, wide), 0, 0, 0, 0),
            1: at((parts, 1, small, wide), 0, 0, tall // small - 1, 0),
            2: at((1, HALO, wide), 0, 0, 0),
            3: at((1, HALO, wide), 0, tall // HALO - 1, 0),
            4: at((1, 1, HALO, local_x), 1, 0, 0, 0),
            5: at((1, 1, HALO, local_x), 1, 0, local_y // HALO - 1, 0),
        },
        after=moved[1:2],
        moved=2 << 20,
        megabytes=50,
        name="rows",
    )
    above, below = ring(last, "gy", 1), ring(first, "gy", -1)
    to_right, to_left = call(
        columns_kernel,
        (has, acoustic, acoustic, wall_mask, wall_mask, velocity, velocity, above, below),
        (shaped(strips, tall + LANES), shaped(strips, tall + LANES)),
        steps=1,
        specs={
            0: scalars,
            1: at((parts, 1, tall, LANES), 0, 0, 0, 0),
            2: at((parts, 1, tall, LANES), 0, 0, 0, wide // LANES - 1),
            3: at((1, tall, LANES), 0, 0, 0),
            4: at((1, tall, LANES), 0, 0, wide // LANES - 1),
            5: at((1, 1, local_y, LANES), 1, 0, 0, 0),
            6: at((1, 1, local_y, LANES), 1, 0, 0, local_x // LANES - 1),
        },
        moved=8 << 20,
        megabytes=54,
        name="columns",
    )
    from_left, from_right = ring(to_right, "gx", 1), ring(to_left, "gx", -1)
    local_memory = pl.BlockSpec(memory_space=pltpu.VMEM)
    tiles = wide // (2 * LANES) + 1
    rise_x, rise_y, listed = call(
        tables_kernel,
        (jnp.stack([place_x, place_y]).astype(jnp.int32), weights_x, weights_y),
        (
            shaped(2, tiles, 2 * LANES, 2 * LANES, kind=BF16),
            shaped(steps, high, 3 * (high // 2 + HALO), kind=BF16),
            shaped(1, kind=jnp.int32),
        ),
        specs={0: scalars},
        out_specs=(local_memory, local_memory, scalars),
        moved=4 << 20,
        megabytes=54,
        name="tables",
    )
    sides, squares, beside = call(
        sides_kernel,
        (has, listed, velocity, above, below, from_left, from_right),
        (
            shaped(parts + 1, tall + LANES, LANES),
            shaped(local_y + 2 * HALO, local_x + LANES),
            shaped(1, kind=jnp.int32),
        ),
        steps=1,
        specs={0: scalars, 1: scalars, 2: at((1, 1, local_y, local_x), 1, 0, 0, 0)},
        out_specs=(
            at((parts + 1, tall + LANES, LANES), 0, 0, 0),
            at((local_y + 2 * HALO, local_x + LANES), 0, 0),
            scalars,
        ),
        moved=8 << 20,
        megabytes=54,
        name="sides",
    )
    across, along = band_tables(high)
    along_inner = along[HALO : HALO + TILE]
    per, rows = TILE // small, TILE // HALO

    def tiled(first):
        walls = (
            pl.BlockSpec((1, TILE, wide), lambda i: (0, i + first, 0)),
            pl.BlockSpec((1, HALO, wide), lambda i: (0, jnp.maximum((i + first) * rows - 1, 0), 0)),
            pl.BlockSpec(
                (1, HALO, wide),
                lambda i: (0, jnp.minimum((i + first + 1) * rows, steps * rows - 1), 0),
            ),
        )
        cells = (
            pl.BlockSpec((parts, 1, TILE, wide), lambda i: (0, 0, i + first, 0)),
            pl.BlockSpec(
                (parts, 1, small, wide), lambda i: (0, 0, jnp.maximum((i + first) * per - 1, 0), 0)
            ),
            pl.BlockSpec(
                (parts, 1, small, wide),
                lambda i: (0, 0, jnp.minimum((i + first + 1) * per, steps * per - 1), 0),
            ),
        )
        return cells, walls

    def quiet_tiles(first, count, before):
        cells, walls = tiled(first)
        operands = (has, own, acoustic, acoustic, acoustic, wall_mask, wall_mask, wall_mask, above, below, sides)
        operands = operands + (across, along, along_inner)
        return call(
            functools.partial(quiet_step_kernel, first),
            operands,
            (
                shaped(parts - 1, tall, wide),
                shaped(*acoustic.shape, kind=BF16),
                shaped(steps, high, full, kind=BF16),
                shaped(1, kind=jnp.int32),
            ),
            steps=count,
            specs=dict(enumerate((scalars, scalars) + cells + walls)),
            out_specs=(
                pl.BlockSpec((parts - 1, TILE, wide), lambda i: (0, i + first, 0)),
                pl.BlockSpec((1, 1, TILE, wide), lambda i: (0, 0, i + first, 0)),
                pl.BlockSpec((1, high, full), lambda i: (i + first, 0, 0)),
                scalars,
            ),
            after=before,
            aliases={len(operands) + k: k for k in range(len(before))},
            megabytes=54,
            flops=3 * 10**9 * count,
            moved=(12 << 20) * count,
            name="quiet_step",
        )

    early = max(steps * 3 // 4, 1)
    *begun, stepped = quiet_tiles(0, early, ())
    if early < steps:
        *begun, _ = quiet_tiles(early, steps - early, begun)
    quiet, final, opened = begun
    lines = pressure_lines(moved, (above, below), beside, stepped)
    operands = (squares, opened, rise_x, rise_y, quiet, across, along_inner, final, *lines)
    anywhere = pl.BlockSpec(memory_space=pl.ANY)
    specs = {k: anywhere for k in range(len(operands))}
    scratch = (
        pltpu.VMEM(squares.shape, F32),
        pltpu.VMEM((2,) + opened.shape[1:], BF16),
        pltpu.VMEM(rise_x.shape, BF16),
        pltpu.VMEM(rise_y.shape, BF16),
        pltpu.VMEM((2, parts - 1, TILE, wide), F32),
        pltpu.VMEM(across.shape, BF16),
        pltpu.VMEM(along_inner.shape, BF16),
        pltpu.VMEM((local_y + 2 * MARGIN, local_x + LANES), F32),
        pltpu.VMEM((2, local_y + 2 * HALO, full), BF16),
        pltpu.VMEM((steps, parts - 1, TILE, wide), BF16),
        pltpu.SemaphoreType.DMA((9 + count_x,)),
        pltpu.SemaphoreType.DMA((steps,)),
    )
    return call(
        source_kernel,
        operands,
        shaped(*acoustic.shape, kind=BF16),
        scratch,
        specs=specs,
        out_specs=anywhere,
        aliases={7: 0},
        megabytes=56,
        flops=4 * 10**9,
        moved=16 << 20,
        name="source_step",
    )


def fits(count_x, count_y, velocity, acoustic):
    _, planes, local_y, local_x = velocity
    _, _, tall, wide = acoustic
    length_x, length_y = local_x * count_x, local_y * count_y
    rows = local_y // count_x
    base_x, base_y = length_x // RADIX, length_y // RADIX
    return (
        planes == 1
        and acoustic[0] == PARTS
        and length_x * 2 == count_x * count_y * LANES
        and base_x % (2 * LANES) == 0
        and local_x % base_x == 0
        and rows % 8 == 0
        and base_y % rows == 0
        and base_y % 8 == 0
        and count_x * count_y % RADIX == 0
        and MARGIN * 2 % (8 * count_x) == 0
        and tall == 2 * local_y
        and wide == 2 * local_x
        and tall % TILE == 0
        and tall % LANES == 0
        and tall >= 2 * TILE
        and count_x & (count_x - 1) == 0
        and wide % (2 * LANES) == 0
    )


def extended(array, sides, width):
    for axis, dim in sides:
        size, length = (lax.axis_size(axis), array.shape[dim])
        up = [(i, (i + 1) % size) for i in range(size - 1)]
        down = [(j, i) for i, j in up]
        last = lax.slice_in_dim(array, length - width, length, axis=dim)
        leading = lax.slice_in_dim(array, 0, width, axis=dim)
        before = lax.ppermute(last, axis, up)
        after = lax.ppermute(leading, axis, down)
        array = jnp.concatenate([before, array, after], axis=dim)
    return array


def gradients(padded):
    height = padded.shape[-2] - 6
    breadth = padded.shape[-1] - 6
    rows_mid = padded[..., 3 : 3 + height, :]
    cols_mid = padded[..., :, 3 : 3 + breadth]
    along_x = jnp.zeros_like(padded[..., 3 : 3 + height, 3 : 3 + breadth])
    along_y = jnp.zeros_like(along_x)
    for index, weight in enumerate(stencil_weights):
        distance = index + 1
        along_x = along_x + weight * (
            rows_mid[..., 3 + distance : 3 + distance + breadth]
            - rows_mid[..., 3 - distance : 3 - distance + breadth]
        )
        along_y = along_y + weight * (
            cols_mid[..., 3 + distance : 3 + distance + height, :]
            - cols_mid[..., 3 - distance : 3 - distance + height, :]
        )
    return (along_x, along_y)


def tendency(padded, source):
    along_x, along_y = gradients(padded)
    diverge = along_x[1] + along_y[2]
    forcing = jnp.stack([-diverge, -along_x[3], -along_y[3], source - diverge])
    return forcing - mean_flow * along_x


def spectral_index(flat, length):
    second = length // 16
    wave = flat // second + 16 * (flat % second)
    return jnp.where(wave < length // 2, wave, wave - length).astype(jnp.float32)


def twiddles(rows_count, cols_count, modulus, sign):
    products = jnp.arange(rows_count)[:, None] * jnp.arange(cols_count)[None, :] % modulus
    angles = 2.0 * math.pi / modulus * products.astype(jnp.float32)
    return (jnp.cos(angles), sign * jnp.sin(angles))


def mix_rows(real_part, imag_part, cosine, sine):
    exact = lax.Precision.HIGHEST
    cos_real = jnp.einsum("ka,...ab->...kb", cosine, real_part, precision=exact)
    cos_imag = jnp.einsum("ka,...ab->...kb", cosine, imag_part, precision=exact)
    sin_real = jnp.einsum("ka,...ab->...kb", sine, real_part, precision=exact)
    sin_imag = jnp.einsum("ka,...ab->...kb", sine, imag_part, precision=exact)
    return (cos_real - sin_imag, cos_imag + sin_real)


def mix_cols(real_part, imag_part, cosine, sine):
    exact = lax.Precision.HIGHEST
    cos_real = jnp.einsum("...kb,bc->...kc", real_part, cosine, precision=exact)
    cos_imag = jnp.einsum("...kb,bc->...kc", imag_part, cosine, precision=exact)
    sin_real = jnp.einsum("...kb,bc->...kc", real_part, sine, precision=exact)
    sin_imag = jnp.einsum("...kb,bc->...kc", imag_part, sine, precision=exact)
    return (cos_real - sin_imag, cos_imag + sin_real)


def rotate(real_part, imag_part, cosine, sine):
    return (real_part * cosine - imag_part * sine, real_part * sine + imag_part * cosine)


def discrete(real_part, imag_part, sign):
    length = real_part.shape[-1]
    second = length // 16
    initial = real_part.shape
    folded = initial[:-1] + (16, second)
    real_part = real_part.reshape(folded)
    imag_part = imag_part.reshape(folded)
    small_cos, small_sin = twiddles(16, 16, 16, sign)
    large_cos, large_sin = twiddles(second, second, second, sign)
    turn_cos, turn_sin = twiddles(16, second, length, sign)
    if sign < 0:
        real_part, imag_part = mix_rows(real_part, imag_part, small_cos, small_sin)
        real_part, imag_part = rotate(real_part, imag_part, turn_cos, turn_sin)
        real_part, imag_part = mix_cols(real_part, imag_part, large_cos, large_sin)
    else:
        real_part, imag_part = mix_cols(real_part, imag_part, large_cos, large_sin)
        real_part, imag_part = rotate(real_part, imag_part, turn_cos, turn_sin)
        real_part, imag_part = mix_rows(real_part, imag_part, small_cos, small_sin)
        real_part = real_part / length
        imag_part = imag_part / length
    return (real_part.reshape(initial), imag_part.reshape(initial))


def transform(stacked, sign, kind):
    if kind == "real_in":
        real_part = stacked
        imag_part = jnp.zeros_like(stacked)
    else:
        half = stacked.shape[0] // 2
        real_part = stacked[:half]
        imag_part = stacked[half:]
    real_out, imag_out = discrete(real_part, imag_part, sign)
    if kind == "real_out":
        return real_out
    return jnp.concatenate([real_out, imag_out], axis=0)


def project(stacked, wave_x, wave_y):
    coef_xx = wave_x * wave_x
    coef_xy = 2.0 * wave_x * wave_y
    coef_yy = wave_y * wave_y
    denominator = wave_x * wave_x + wave_y * wave_y
    positive = denominator > 0
    safe = jnp.where(positive, denominator, 1.0)

    def combine(parts):
        numerator = -(coef_xx * parts[0] + coef_xy * parts[1] + coef_yy * parts[2])
        return jnp.where(positive, numerator / safe, 0.0)

    return jnp.stack([combine(stacked[:3]), combine(stacked[3:])])


def refine(stacked, weights):
    result = jnp.zeros(stacked.shape[:-1] + (2 * stacked.shape[-1],), jnp.float32)
    for offset in range(4):
        result = (
            result
            + jnp.repeat(jnp.roll(stacked, 1 - offset, axis=-1), 2, axis=-1) * weights[offset]
        )
    return result


def lines_x(stacked, action):
    gathered = action(lax.all_to_all(stacked, "gx", split_axis=2, concat_axis=3, tiled=True))
    return lax.all_to_all(gathered, "gx", split_axis=3, concat_axis=2, tiled=True)


def lines_y(stacked, action):
    turned = jnp.swapaxes(stacked, 2, 3)
    gathered = action(lax.all_to_all(turned, "gy", split_axis=2, concat_axis=3, tiled=True))
    returned = lax.all_to_all(gathered, "gy", split_axis=3, concat_axis=2, tiled=True)
    return jnp.swapaxes(returned, 2, 3)


def expand(fields):
    return extended(fields, (("gx", 3), ("gy", 2)), 3)


def shards(velocity, weights_x, weights_y, acoustic, wall_mask):
    acoustic = acoustic.astype(jnp.float32)
    flow_x = velocity[0]
    flow_y = velocity[1]
    tensor = jnp.stack([flow_x * flow_x, flow_x * flow_y, flow_y * flow_y])
    count_gx = lax.axis_size("gx")
    count_gy = lax.axis_size("gy")
    place_x = lax.axis_index("gx")
    place_y = lax.axis_index("gy")
    local_y = tensor.shape[2]
    local_x = tensor.shape[3]
    length_x = local_x * count_gx
    length_y = local_y * count_gy

    def forward_real(portion):
        return transform(portion, -1, "real_in")

    def finish_x(portion):
        return refine(transform(portion, 1, "real_out"), weights_x)

    spectra = lines_x(tensor, forward_real)
    share_x = local_x // count_gy
    line_x = spectral_index(place_x * local_x + place_y * share_x + jnp.arange(share_x), length_x)[
        :, None
    ]
    line_y = spectral_index(jnp.arange(length_y), length_y)[None, :]

    def solve_y(portion):
        solved = project(transform(portion, -1, "complex"), line_x, line_y)
        return refine(transform(solved, 1, "complex"), weights_y)

    pressure = lines_y(spectra, solve_y)
    source = lines_x(pressure, finish_x)[0]
    open_cells = (1 - wall_mask).astype(jnp.float32)
    first_rate = tendency(expand(acoustic), source)
    middle = open_cells * (acoustic + time_step * first_rate)
    second_rate = tendency(expand(middle), source)
    return (open_cells * (acoustic + 0.5 * time_step * (first_rate + second_rate))).astype(
        jnp.bfloat16
    )


def solution(mesh):
    in_specs = (P(None, None, "gy", "gx"), P(), P(), P(None, None, "gy", "gx"), P(None, "gy", "gx"))
    out_specs = P(None, None, "gy", "gx")

    def chosen(velocity, weights_x, weights_y, acoustic, wall_mask):
        sizes = (mesh.shape["gx"], mesh.shape["gy"], velocity.shape, acoustic.shape)
        plan = fast_shards if fits(*sizes) else shards
        return plan(velocity, weights_x, weights_y, acoustic, wall_mask)

    return jax.shard_map(
        chosen, mesh=mesh, in_specs=in_specs, out_specs=out_specs, check_vma=False
    )
```

```python
import functools
import math

import jax
import jax.numpy as jnp
import ml_dtypes
import numpy as np
from jax import lax
from jax.experimental import pallas as pl
from jax.experimental.pallas import tpu as pltpu
from jax.sharding import PartitionSpec as P

stencil_weights = (0.75, -0.15, 1.0 / 60.0)
mean_flow = 0.3
time_step = 0.5
whole_weights = (45.0, -9.0, 1.0)

LANES = 128
RADIX = 8
HALO = 8
MARGIN = 16
TILE = 128
ROOT = math.sqrt(0.5)
STRIP = {2: (0, 6), 3: (6, 6), 1: (12, 3), 4: (15, 3), 5: (20, 4)}
STRIP_ROWS = 24
PARTS = 4
BF16 = jnp.bfloat16
F32 = jnp.float32


def halves(table):
    high = table.astype(np.float32).astype(ml_dtypes.bfloat16)
    low = (table - high.astype(np.float64)).astype(np.float32).astype(ml_dtypes.bfloat16)
    return high, low


def packed_columns(cosine, sine):
    half = LANES // 2
    parts = []
    for first in range(0, cosine.shape[1], half):
        parts += [cosine[:, first : first + half], sine[:, first : first + half]]
    return np.concatenate(parts, axis=1)


@functools.lru_cache(maxsize=None)
def x_tables(length):
    base = length // RADIX
    m = np.arange(base)[:, None]
    q = np.arange(base)[None, :]
    angle = 2.0 * np.pi * ((m * q) % base) / base
    cosine, sine = np.cos(angle), np.sin(angle)
    full = np.concatenate([packed_columns(cosine, -sine), packed_columns(sine, cosine)], axis=0)
    half = base // 2
    zero_cos, zero_sin = cosine[:, :half].copy(), -sine[:, :half]
    zero_cos[:, 0] = 0.0
    zero_sin = zero_sin.copy()
    zero_sin[:, 0] = (-1.0) ** np.arange(base)
    zero = packed_columns(zero_cos, zero_sin)
    shifted = 2.0 * np.pi * ((m * (RADIX * q[:, :half] + RADIX // 2)) % length) / length
    middle = packed_columns(np.cos(shifted), -np.sin(shifted))
    turns = 2.0 * np.pi * np.arange(1, RADIX // 2)[:, None] * np.arange(base)[None, :] / length
    return full, zero, middle, np.cos(turns), np.sin(turns)


@functools.lru_cache(maxsize=None)
def y_tables(length):
    base = length // RADIX
    index = np.arange(base)
    angle = 2.0 * np.pi * ((index[:, None] * index[None, :]) % base) / base
    both = np.concatenate([np.cos(angle), np.sin(angle)], axis=0)
    turns = 2.0 * np.pi * np.arange(RADIX)[:, None] * index[None, :] / length
    turns = np.concatenate([np.cos(turns), np.sin(turns)], axis=0).T
    high, rest = halves(turns)
    low = turns - high.astype(np.float64) - rest.astype(np.float64)
    return both, np.concatenate([high, rest, low.astype(ml_dtypes.bfloat16)], axis=1)


@functools.lru_cache(maxsize=None)
def wave_table(length, count):
    slots = LANES // 4
    base = length // RADIX
    waves = []
    for residue in (1, 2, 3):
        waves.append(RADIX * np.arange(base) + residue)
    waves.append(RADIX * np.arange(base // 2))
    waves.append(RADIX * np.arange(base // 2) + RADIX // 2)
    waves = np.concatenate(waves)
    waves = np.where(waves == 0, length // 2, waves)
    waves = np.where(waves < length // 2, waves, waves - length).reshape(count, slots)
    return np.tile(waves, (1, 4)).astype(np.float32)


@functools.lru_cache(maxsize=None)
def band_tables(rows):
    across = np.zeros((4 * LANES, 2 * LANES))
    column = np.arange(2 * LANES)
    down = np.zeros((rows, rows))
    for index, weight in enumerate(whole_weights):
        distance = index + 1
        across[column + LANES + distance, column] = weight
        across[column + LANES - distance, column] = -weight
        down += weight * (np.eye(rows, k=distance) - np.eye(rows, k=-distance))
    return across.astype(ml_dtypes.bfloat16), down.astype(ml_dtypes.bfloat16)


def beside(*tables):
    high, low = halves(np.concatenate(tables, axis=1))
    return np.concatenate([high, low], axis=0)


def split(values):
    high = values.astype(BF16)
    return high, (values - high.astype(F32)).astype(BF16)


def dot(left, right):
    return jnp.dot(left, right, preferred_element_type=F32)


def exact_dot(left, right):
    left_high, left_low = left
    right_high, right_low = right
    return dot(left_high, right_high) + (dot(left_low, right_high) + dot(left_high, right_low))


def lane_index(shape):
    return lax.broadcasted_iota(jnp.int32, shape, len(shape) - 1)


def spin(values, shift):
    return pltpu.roll(values, shift % values.shape[-1], values.ndim - 1)


def lane_tile(values, index):
    return values[:, index * LANES : (index + 1) * LANES]


def x_parts(tables, base):
    wide = 2 * base
    full = (tables[:wide], tables[wide : 2 * wide])
    at = 2 * wide
    high, low = tables[at : at + base], tables[at + base : at + 2 * base]
    return full, (high[:, :base], low[:, :base]), (high[:, base:], low[:, base:])


def pieces_kernel(velocity, *pieces):
    rows = pieces[0].shape[1]
    place = lax.axis_index("gx")
    for mask, piece in enumerate(pieces):
        start = pl.multiple_of((place ^ mask) * rows, 8)
        for c in range(2):
            piece[c] = velocity[c, 0, pl.ds(start, rows), :]


def rows_kernel(top, low, top_wall, low_wall, top_flow, low_flow, first, last):
    small, width = top.shape[2], top_flow.shape[3]
    first[...] = jnp.zeros(first.shape, F32)
    last[...] = jnp.zeros(last.shape, F32)
    for k, (start, rows) in STRIP.items():
        lanes = slice(0, width) if k == PARTS + 1 else slice(None)
        if k < PARTS:
            upper, lower = top[k, 0].astype(F32)[:HALO], low[k, 0].astype(F32)[small - HALO :]
        elif k == PARTS:
            upper, lower = 1.0 - top_wall[0].astype(F32), 1.0 - low_wall[0].astype(F32)
        else:
            upper, lower = top_flow[0, 0], low_flow[0, 0]
        first[start : start + rows, lanes] = upper[:rows]
        last[start : start + rows, lanes] = lower[HALO - rows :]


def strip(ref, k, upper, lanes=slice(None)):
    if k not in STRIP:
        return jnp.zeros((HALO, ref[0:1, lanes].shape[1]), F32)
    start, rows = STRIP[k]
    values = ref[start : start + rows, lanes]
    blank = jnp.zeros((HALO - rows, values.shape[1]), F32)
    return jnp.concatenate([blank, values] if upper else [values, blank], axis=0)


def columns_kernel(
    has, left, right, left_wall, right_wall, left_flow, right_flow, above, below, to_right, to_left
):
    parts = left.shape[0]
    wide, flow_wide = above.shape[1], above.shape[1] // 2
    gap = jnp.zeros((LANES - 2 * HALO, LANES), F32)

    def tall(k, inner, first, sides):
        lanes = slice(first, first + LANES)
        over, under = strip(above, k, True, lanes), strip(below, k, False, lanes)
        return jnp.concatenate([inner, under * sides[1], gap, over * sides[0]], axis=0).T

    for k in range(parts + 1):
        at = slice(k * HALO, (k + 1) * HALO)
        if k < parts:
            near, far = left[k, 0].astype(F32), right[k, 0].astype(F32)
        else:
            near, far = 1.0 - left_wall[0].astype(F32), 1.0 - right_wall[0].astype(F32)
        sides = (has[2], has[3])
        to_left[at, :] = tall(k, near, 0, sides)[:HALO]
        to_right[at, :] = tall(k, far, wide - LANES, sides)[LANES - HALO :]
    k = parts + 1
    at = slice(k * HALO, (k + 1) * HALO)
    size = left_flow.shape[2] + LANES
    blank = jnp.zeros((HALO, to_left.shape[1] - size), F32)
    to_left[at, :size] = tall(k, left_flow[0, 0], 0, (1.0, 1.0))[:HALO]
    to_right[at, :size] = tall(k, right_flow[0, 0], flow_wide - LANES, (1.0, 1.0))[LANES - HALO :]
    to_left[at, size:] = blank
    to_right[at, size:] = blank


def sides_kernel(has, place, velocity, above, below, from_left, from_right, sides, squares, mark):
    parts, tall, _ = sides.shape
    gap = jnp.zeros((LANES - 2 * HALO, tall), F32)
    for k in range(parts):
        at = slice(k * HALO, (k + 1) * HALO)
        tile = [from_right[at, :] * has[1], gap, from_left[at, :] * has[0]]
        sides[k] = jnp.concatenate(tile, axis=0).T
    at = slice(parts * HALO, (parts + 1) * HALO)
    rows, local = velocity.shape[2:]
    size = rows + LANES
    tile = [from_right[at, :size], gap[:, :size], from_left[at, :size]]
    tile = jnp.concatenate(tile, axis=0).T
    tile = tile * tile
    mark[0] = place[0]
    over, under = (strip(ref, parts, ref is above, slice(0, local)) for ref in (above, below))
    squares[:HALO, :local] = over * over
    squares[HALO : HALO + rows, :local] = velocity[0, 0] * velocity[0, 0]
    squares[HALO + rows :, :local] = under * under
    squares[:HALO, local:] = tile[size - HALO :]
    squares[HALO : HALO + rows, local:] = tile[:rows]
    squares[HALO + rows :, local:] = tile[rows : rows + HALO]


def forward_x_kernel(*refs):
    *pieces, tables, turns, out, total, lines, made, sent = refs
    count, _, rows, local = lines.shape
    place = lax.axis_index("gx")
    for mask, piece in enumerate(pieces):
        lines[place ^ mask] = piece[...]
    base = turns.shape[1]
    per = local // base
    u = [lines[t // per, 0, :, (t % per) * base : (t % per + 1) * base] for t in range(RADIX)]
    v = [lines[t // per, 1, :, (t % per) * base : (t % per + 1) * base] for t in range(RADIX)]
    energy = sum(b * b for b in v)
    energy = jnp.sum(energy.reshape(rows // 8, 8, base), axis=0)
    total[...] = sum(energy[:, k : k + LANES] for k in range(0, base, LANES))
    fields = ([a * a - b * b for a, b in zip(u, v)], [2.0 * a * b for a, b in zip(u, v)])
    zeros, mids, reals, imags = [], [], [[], [], []], [[], [], []]
    for a in fields:
        s04, s26, s15, s37 = a[0] + a[4], a[2] + a[6], a[1] + a[5], a[3] + a[7]
        d04, d26, d15, d37 = a[0] - a[4], a[2] - a[6], a[1] - a[5], a[3] - a[7]
        zeros.append((s04 + s26) + (s15 + s37))
        mids.append((s04 + s26) - (s15 + s37))
        minus, plus = ROOT * (d15 - d37), ROOT * (d15 + d37)
        turned = (
            (d04 + minus, -d26 - plus),
            (s04 - s26, s37 - s15),
            (d04 - minus, d26 - plus),
        )
        for index, (real, imag) in enumerate(turned):
            c, s = turns[index : index + 1, :], turns[index + 3 : index + 4, :]
            reals[index].append(real * c + imag * s)
            imags[index].append(imag * c - real * s)
    stacked = jnp.concatenate(
        [
            jnp.concatenate([jnp.concatenate(reals[i], axis=0) for i in range(3)], axis=0),
            jnp.concatenate([jnp.concatenate(imags[i], axis=0) for i in range(3)], axis=0),
        ],
        axis=1,
    )
    full, zero, middle = x_parts(tables, base)
    full = exact_dot(split(stacked), full)
    zero = exact_dot(split(jnp.concatenate(zeros, axis=0)), zero)
    middle = exact_dot(split(jnp.concatenate(mids, axis=0)), middle)
    low = lane_index((rows, LANES)) % 64 < 32
    target, copies = 0, []
    blocks = [full[2 * rows * i : 2 * rows * (i + 1)] for i in range(3)] + [zero, middle]
    for block in blocks:
        start = target
        for first in range(0, block.shape[1], LANES):
            a = block[:rows, first : first + LANES]
            c = block[rows:, first : first + LANES]
            made[target] = jnp.where(low, a, spin(c, 32))
            made[target + 1] = jnp.where(low, spin(a, -32), c)
            target += 2
        group = pl.ds(start, target - start)
        copies.append(pltpu.make_async_copy(made.at[group], out.at[group], sent.at[len(copies)]))
        copies[-1].start()
    for copy in copies:
        copy.wait()


def eighths(x, turn):
    s04, s26, s15, s37 = x[0] + x[4], x[2] + x[6], x[1] + x[5], x[3] + x[7]
    d04, d26, d15, d37 = x[0] - x[4], x[2] - x[6], x[1] - x[5], x[3] - x[7]
    quarter = turn(s15 - s37)
    spun_26, spun_37 = turn(d26), turn(d37)
    one, three = d15 + spun_37, d15 - spun_37
    spun_one, spun_three = turn(one), turn(three)
    one = ROOT * (one + spun_one)
    three = ROOT * (spun_three - three)
    return [
        (s04 + s26) + (s15 + s37),
        (d04 + spun_26) + one,
        (s04 - s26) + quarter,
        (d04 - spun_26) + three,
        (s04 + s26) - (s15 + s37),
        (d04 + spun_26) - one,
        (s04 - s26) - quarter,
        (d04 - spun_26) - three,
    ]


def solve_y_kernel(count_x, lines, total, wave, both, turns, out, held, spread, made, sent):
    count, rows, _ = lines.shape
    base = turns.shape[0]
    length = count * rows
    block = count_x * rows
    per = base // rows
    lanes = lane_index((base, LANES))
    sign = jnp.where(lanes < 64, 1.0, -1.0).astype(F32)

    def minus_i(z):
        return spin(z, 64) * sign

    def plus_i(z):
        return spin(z, 64) * -sign

    fields = [
        jnp.concatenate([lines[t * per + k] for k in range(per)], axis=0) for t in range(RADIX)
    ]
    mixed = eighths(fields, minus_i)
    terms, columns = turns.shape[1], 2 * RADIX
    picked = lax.broadcasted_iota(jnp.int32, (terms, columns * LANES), 0) % columns
    lane = lane_index(picked.shape)
    value = jnp.where((lane >= RADIX * LANES) & (lane % LANES >= 64), -1.0, 1.0)
    spread[...] = dot(turns[...], jnp.where(picked == lane // LANES, value, 0.0).astype(BF16))
    cosines = [spread[:, r * LANES : (r + 1) * LANES] for r in range(RADIX)]
    sines = [spread[:, (r + RADIX) * LANES : (r + RADIX + 1) * LANES] for r in range(RADIX)]
    mixed = [mixed[0]] + [
        mixed[r] * cosines[r] + spin(mixed[r], 64) * sines[r] for r in range(1, RADIX)
    ]
    tables = (both[: 2 * base], both[2 * base :])
    product = exact_dot(tables, split(jnp.concatenate(mixed, axis=1)))
    kx = wave[0:1, :]
    first = lanes % 64 < 32
    edge = jnp.float32(length // 2)
    square_kx = kx * kx
    alone = jnp.where(first, square_kx, 0.0)
    slope = jnp.where(first | (kx == -edge), 0.0, jnp.broadcast_to(kx, lanes.shape))
    q = lax.broadcasted_iota(jnp.int32, lanes.shape, 0)
    low_ky = RADIX * (q - jnp.where(q < base // 2, 0, base)).astype(F32)
    terms = []
    for r in range(RADIX):
        at = slice(r * LANES, (r + 1) * LANES)
        spectrum = product[:base, at] + minus_i(product[base:, at])
        ky = low_ky + float(r)
        symbol = alone + slope * ky
        if r == 0:
            corner = jnp.where((kx == -edge) & ~first, edge * edge, 0.0)
            symbol = jnp.where(ky == -edge, jnp.where(first, alone, corner), symbol)
        square = square_kx + ky * ky
        guess = pl.reciprocal(square, approx=True)
        terms.append(symbol * (guess * (2.0 - square * guess)) * spectrum)
    pairs = [
        jnp.where(first, low + spin(low, -32), high + spin(high, 32))
        for low, high in zip(terms[:4], terms[4:])
    ]
    product = exact_dot(tables, split(jnp.concatenate(pairs, axis=1)))
    mixed = []
    for r in range(RADIX // 2):
        at = slice(r * LANES, (r + 1) * LANES)
        value = product[:base, at] + plus_i(product[base:, at])
        cosine = jnp.where(first, cosines[r], cosines[r + 4])
        sine = jnp.where(first, sines[r], sines[r + 4])
        value = value * cosine - spin(value, 64) * sine
        value = jnp.where(first, value + spin(value, -32), spin(value, 32) - value)
        if r == 2:
            value = jnp.where(first, value, plus_i(value))
        elif r:
            turned = plus_i(value)
            odd = value + turned if r == 1 else turned - value
            value = jnp.where(first, value, ROOT * odd)
        mixed.append(value)
    even, odd = mixed[0] + mixed[2], mixed[0] - mixed[2]
    side, turned = mixed[1] + mixed[3], plus_i(mixed[1] - mixed[3])
    for t, values in enumerate((even + side, odd + turned, even - side, odd - turned)):
        start = MARGIN + 2 * t * base
        held[start : start + base, :] = values
        held[start + base : start + 2 * base, :] = spin(values, -32)
    held[0:MARGIN, :] = held[length : length + MARGIN, :]
    held[length + MARGIN : length + 2 * MARGIN, :] = held[MARGIN : 2 * MARGIN, :]
    spare = total[...] + spin(total[...], 32)
    kept = rows + 2 * MARGIN // count_x
    half = made.shape[1]
    rest = kept - half
    low = lane_index((8, LANES)) % 64 < 32
    copies = []
    for target in range(count):
        start = (target // count_x) * block + (target % count_x) * kept
        for row in range(0, half, 8):
            a = held[start + row : start + row + 8, :]
            if row < rest:
                b = spin(held[start + half + row : start + half + row + 8, :], 32)
            else:
                b = spare
            made[target, row : row + 8, :] = jnp.where(low, a, b)
        if (target + 1) % RADIX == 0:
            group = pl.ds(target + 1 - RADIX, RADIX)
            copies.append(pltpu.make_async_copy(made.at[group], out.at[group], sent.at[len(copies)]))
            copies[-1].start()
    for copy in copies:
        copy.wait()


def inverse_x_kernel(
    kept, scale, lines, tables, turns, *refs
):
    kept_out, *outs, held, own, sent = refs
    outs = [own] + outs
    place = lax.axis_index("gx")
    count, half, _ = lines.shape
    base = turns.shape[1]
    length = RADIX * base
    rest = kept - half
    low = lane_index((half, LANES)) % 64 < 32
    groups, spare = [], None
    for first in range(0, count, 2):
        even, odd = lines[first], lines[first + 1]
        a = jnp.where(low, even, spin(odd, 32))
        b = jnp.where(low, spin(even, -32), odd)
        groups.append(jnp.concatenate([a, b[:rest]], axis=0))
        extra = b[rest : rest + 8]
        spare = extra if spare is None else spare + extra
    mean = jnp.sum(spare) * scale
    wide = 2 * base // LANES
    narrow = base // LANES
    stacked = jnp.concatenate(
        [jnp.concatenate(groups[i * wide : (i + 1) * wide], axis=1) for i in range(3)], axis=0
    )
    at = 3 * wide
    zeros = jnp.concatenate(groups[at : at + narrow], axis=1)
    mids = jnp.concatenate(groups[at + narrow : at + 2 * narrow], axis=1)
    full, zero, middle = x_parts(tables, base)
    full = exact_dot(split(stacked), full)
    zero = exact_dot(split(zeros), zero) * scale
    mid = exact_dot(split(mids), middle) * scale
    turned = []
    for i in range(3):
        real = full[i * kept : (i + 1) * kept, :base]
        imag = full[i * kept : (i + 1) * kept, base:]
        c = turns[i : i + 1, :] * (2.0 * scale)
        s = turns[i + 3 : i + 4, :] * (2.0 * scale)
        turned.append((real * c - imag * s, real * s + imag * c))
    for t in range(RADIX):
        value = zero + mid if t % 2 == 0 else zero - mid
        for i, (real, imag) in enumerate(turned):
            eighth = t * (i + 1) % RADIX
            c = (1.0, ROOT, 0.0, -ROOT, -1.0, -ROOT, 0.0, ROOT)[eighth]
            s = (0.0, ROOT, 1.0, ROOT, 0.0, -ROOT, -1.0, -ROOT)[eighth]
            if c:
                value = value + c * real
            if s:
                value = value - s * imag
        held[:, t * base : (t + 1) * base] = mean - value
    targets, local = len(outs), outs[0].shape[1] - LANES
    right = lane_index((kept, LANES)) < 64
    for mask, out in enumerate(outs):
        start = pl.multiple_of((place ^ mask) * local, LANES)
        after = pl.multiple_of(jnp.where(start + local == length, 0, start + local), LANES)
        before = pl.multiple_of(jnp.where(start == 0, length, start) - LANES, LANES)
        out[:, :local] = held[:, pl.ds(start, local)]
        out[:, local:] = jnp.where(
            right, held[:, pl.ds(after, LANES)], held[:, pl.ds(before, LANES)]
        )
        if mask == 0:
            copy = pltpu.make_async_copy(own, kept_out, sent)
            copy.start()
    copy.wait()


def slopes_x(parts, band, with_edge):
    tiles = parts[0].shape[-1] // LANES
    pieces = []
    for first in list(range(0, tiles - 1, 2)) + ([tiles - 1] if with_edge else []):
        steps = (-1, 0, 1, 2) if first < tiles - 1 else (-1, 0, 1)
        table = band[...] if first < tiles - 1 else band[: 3 * LANES, :LANES]
        order = [(first + step) % tiles for step in steps]
        piece = None
        for part in parts:
            term = dot(jnp.concatenate([lane_tile(part, t) for t in order], axis=1), table)
            piece = term if piece is None else piece + term
        pieces.append(piece)
    return jnp.concatenate(pieces, axis=1)


def edged(k, side, center, up, down, above, below, sides, has, first=0):
    step = pl.program_id(0) + first
    tile, width = center.shape
    tall = sides.shape[1]
    last = (tall - LANES) // tile - 1
    base = pl.multiple_of(step * tile, 8)
    before = pl.multiple_of(jnp.where(step == 0, tall, base) - HALO, 8)
    over = jnp.where(step == 0, strip(above, k, True) * has[2], up)
    under = jnp.where(step == last, strip(below, k, False) * has[3], down)
    rows = (
        (over, sides[side, pl.ds(before, HALO), :]),
        (center, sides[side, pl.ds(base, tile), :]),
        (under, sides[side, pl.ds(pl.multiple_of(base + tile, 8), HALO), :]),
    )
    return jnp.concatenate([jnp.concatenate(pair, axis=1) for pair in rows], axis=0)


def edged_open(k, side, wall, wall_up, wall_down, above, below, sides, has, first=0):
    open_cells = [1.0 - ref[0].astype(F32) for ref in (wall, wall_up, wall_down)]
    return edged(k, side, *open_cells, above, below, sides, has, first)


def quiet_step_kernel(
    first, has, place, center, up, down, wall, wall_up, wall_down, above, below, sides, across, along, along_inner, calm, density, shown_open, mark
):
    parts, _, tile, width = center.shape
    high = tile + 2 * HALO
    opened = edged_open(parts, parts, wall, wall_up, wall_down, above, below, sides, has, first)
    values = []
    for k in range(parts):
        value = edged(
            k,
            k,
            center[k, 0].astype(F32),
            up[k, 0].astype(F32)[up.shape[2] - HALO :],
            down[k, 0].astype(F32)[:HALO],
            above,
            below,
            sides,
            has,
            first,
        )
        values.append(value)

    def drops(x, along_b, along_p):
        diverge = x[1] + along_b
        return (
            diverge + mean_flow * x[0],
            x[3] + mean_flow * x[1],
            along_p + mean_flow * x[2],
            diverge + mean_flow * x[3],
        )

    short = [value.astype(BF16) for value in values]
    x = slopes_x((jnp.concatenate(short, axis=0),), across, True)
    x = [x[k * high : (k + 1) * high] for k in range(parts)]
    table = along[...]
    dropped = drops(x, dot(table, short[2]), dot(table, short[3]))
    middle = [opened * (v - (time_step / 60.0) * d) for v, d in zip(values, dropped)]
    inner = slice(HALO, HALO + tile)
    x = slopes_x(split(jnp.concatenate([value[inner] for value in middle], axis=0)), across, False)
    x = [x[k * tile : (k + 1) * tile] for k in range(parts)]
    table = along_inner[...]
    y = [sum(dot(table, part) for part in split(middle[k][:, :width])) for k in (2, 3)]
    dropped = drops(x, *y)
    shown = opened[inner, :width]
    for k in range(parts):
        start = 0.5 * values[k][inner, :width] - (0.5 * time_step / 60.0) * dropped[k]
        value = shown * start + 0.5 * middle[k][inner, :width]
        if k == 0:
            density[0, 0] = value.astype(BF16)
        else:
            calm[k - 1] = value
    shown_open[0] = (time_step * opened).astype(BF16)
    mark[0] = place[0]


def own_weights(ref, start, size):
    length = ref.shape[1]
    start = jnp.where(start < 0, start + length, jnp.where(start >= length, start - length, start))
    return ref[:, pl.ds(pl.multiple_of(start, LANES), size)]


def columns_table(ref, place, tiles):
    lanes = 2 * LANES
    wide = (tiles - 1) * lanes
    first = place * wide
    half = LANES // 2
    cells = lax.broadcasted_iota(jnp.int32, (lanes, lanes), 0)
    fine = lax.broadcasted_iota(jnp.int32, (lanes, lanes), 1)
    right, left = own_weights(ref, first + wide, LANES), own_weights(ref, first - LANES, LANES)
    edge = jnp.where(lane_index(right.shape) < half, right, left)
    edge = jnp.concatenate([edge, edge], axis=1)
    tables = []
    for k in range(tiles):
        own = own_weights(ref, first + k * lanes, lanes) if k < tiles - 1 else edge
        target = fine // 2 - 1
        if k == tiles - 1:
            target = jnp.where(fine < half, target, target + half)
        value = jnp.zeros(fine.shape, F32)
        for t in range(4):
            value = jnp.where(cells == (target + t) % lanes, own[t : t + 1, :], value)
        tables.append(split(value))
    return tables


def tables_kernel(place, weights_y, rise_y, mark):
    mark[0] = place[0]
    steps, high, reach = rise_y.shape
    tall = steps * TILE
    first = place[1] * tall
    own = [own_weights(weights_y, first + k * LANES, LANES) for k in range(-1, tall // LANES + 1)]
    own = jnp.concatenate([jnp.concatenate(own, axis=1), jnp.zeros((4, tall + 2 * LANES), F32)], axis=0).T
    cells = lax.broadcasted_iota(jnp.int32, (high, reach), 1)
    last = cells >= reach // 3 * 2
    cells = cells % (reach // 3)
    target = lax.broadcasted_iota(jnp.int32, (high, reach), 0) // 2 + (HALO // 2 - 1)
    for k in range(steps):
        start = LANES - HALO + k * TILE
        value = jnp.zeros((high, reach), F32)
        for t in range(4):
            value = jnp.where(cells == target + t, own[start : start + high, t : t + 1], value)
        upper, lower = split(value)
        rise_y[k] = jnp.where(last, lower, upper)


def source_kernel(weights_x, squares, opened, rise_y, quiet, across, along, _, *refs):
    *lines, out, squared, cells_open, rows_matrix, calm, band, column, held, raised, done, fetched, kept = refs
    steps = done.shape[0]
    tile, width = calm.shape[2:]
    high = tile + 2 * HALO
    rows = lines[0].shape[0]
    place = lax.axis_index("gx")

    def tile_copies(k):
        part = quiet.at[:, pl.ds(k * tile, tile), :]
        return (
            pltpu.make_async_copy(part, calm.at[k % 2], fetched.at[k % 2]),
            pltpu.make_async_copy(opened.at[k], cells_open.at[k % 2], fetched.at[2 + k % 2]),
        )

    def done_copy(k):
        part = out.at[1:, 0, pl.ds(k * tile, tile), :]
        return pltpu.make_async_copy(done.at[k], part, kept.at[k])

    arrays = ((squares, squared), (rise_y, rows_matrix), (across, band), (along, column))
    copies = [
        pltpu.make_async_copy(source, target, fetched.at[4 + k])
        for k, (source, target) in enumerate(arrays)
    ]
    pieces = [
        pltpu.make_async_copy(
            piece,
            held.at[pl.ds(pl.multiple_of((place ^ mask) * rows, 8), rows), :],
            fetched.at[4 + len(arrays) + mask],
        )
        for mask, piece in enumerate(lines)
    ]
    for copy in (*pieces, *copies, *tile_copies(0), *tile_copies(1)):
        copy.start()
    count = squares.shape[1] // LANES
    matrix = columns_table(weights_x, place, count)
    for copy in pieces + copies[:1]:
        copy.wait()

    level = held[MARGIN - HALO : MARGIN - HALO + squared.shape[0], :] - squared[...]
    near = lane_index((level.shape[0], LANES)) < 64
    around = []
    for k in range(count):
        after, before = lane_tile(level, (k + 1) % count), lane_tile(level, (k - 1) % count)
        around.append(split(jnp.concatenate([lane_tile(level, k), jnp.where(near, after, before)], axis=1)))
    for k in range(count):
        lanes = 2 * LANES if k < count - 1 else LANES
        value = split(exact_dot(around[k], [part[:, :lanes] for part in matrix[k]]))
        for part in range(2):
            raised[part, :, 2 * k * LANES : 2 * k * LANES + lanes] = value[part]
    for copy in copies[1:]:
        copy.wait()

    reach = rows_matrix.shape[2] // 3
    for k in range(steps):
        start = k * (tile // 2)
        window = [raised[part, start : start + reach, :] for part in (0, 1, 0)]
        calm_here, open_here = tile_copies(k)
        open_here.wait()
        free = cells_open[k % 2].astype(F32)
        value = free * dot(rows_matrix[k], jnp.concatenate(window, axis=0))
        inner = value[HALO : HALO + tile]
        shown = (0.5 / 60.0) * free[HALO : HALO + tile, :width]
        x = shown * slopes_x(split(inner), band, False)
        y = shown * sum(dot(column[...], part) for part in split(value[:, :width]))
        calm_here.wait()
        still = calm.at[k % 2]
        done[k, 0] = (still[0] - x).astype(BF16)
        done[k, 1] = (still[1] - y).astype(BF16)
        done[k, 2] = (still[2] + inner[:, :width] - mean_flow * x).astype(BF16)
        done_copy(k).start()
        if k + 2 < steps:
            for copy in tile_copies(k + 2):
                copy.start()
    for k in range(steps):
        done_copy(k).wait()


def call(
    kernel, operands, outs, scratch=(), steps=0, specs=None, out_specs=None, after=(), aliases=None, megabytes=24, flops=0, moved=0, name=None
):
    count = len(operands)

    def body(*refs):
        kernel(*refs[:count], *refs[count + len(after) :])

    def whole(array):
        zeros = (0,) * len(array.shape)
        return pl.BlockSpec(array.shape, lambda *_: zeros)

    arguments = {}
    chosen = specs or {}
    if steps:
        arguments["grid"] = (steps,)
        in_specs = [chosen.get(i, whole(o)) for i, o in enumerate(operands)]
        arguments["out_specs"] = jax.tree.map(whole, outs) if out_specs is None else out_specs
    else:
        local = pl.BlockSpec(memory_space=pltpu.VMEM)
        in_specs = [chosen.get(i, local) for i in range(count)]
        if out_specs is not None:
            arguments["out_specs"] = out_specs
    return pl.pallas_call(
        body,
        out_shape=outs,
        in_specs=in_specs + [pl.BlockSpec(memory_space=pl.ANY)] * len(after),
        scratch_shapes=list(scratch),
        input_output_aliases=aliases or {},
        compiler_params=pltpu.CompilerParams(vmem_limit_bytes=megabytes << 20),
        cost_estimate=pl.CostEstimate(flops=flops, bytes_accessed=moved, transcendentals=0),
        name=name,
        **arguments,
    )(*operands, *after)


def ring(array, axis, step):
    size = lax.axis_size(axis)
    return lax.ppermute(array, axis, [(i, (i + step) % size) for i in range(size)])


def swap(array, axis, mask):
    return lax.ppermute(array, axis, [(i, i ^ mask) for i in range(lax.axis_size(axis))])


def shaped(*shape, kind=F32):
    return jax.ShapeDtypeStruct(shape, kind)


def pressure_lines(pieces, gathered, spread, stepped):
    _, rows, local_x = pieces[0].shape
    count_x, count_y = lax.axis_size("gx"), lax.axis_size("gy")
    count = count_x * count_y
    length_x, length_y = local_x * count_x, rows * count
    full, zero, middle, cos_turn, sin_turn = x_tables(length_x)
    turns = np.zeros((8, cos_turn.shape[1]), np.float32)
    turns[0:3], turns[3:6] = cos_turn, sin_turn
    spectra, total = call(
        forward_x_kernel,
        (*pieces, np.concatenate([beside(full), beside(zero, middle)]), turns),
        (shaped(count, rows, LANES), shaped(8, LANES)),
        (
            pltpu.VMEM((count_x, 2, rows, local_x), F32),
            pltpu.VMEM((count, rows, LANES), F32),
            pltpu.SemaphoreType.DMA((5,)),
        ),
        out_specs=(pl.BlockSpec(memory_space=pl.ANY), pl.BlockSpec(memory_space=pltpu.VMEM)),
        after=gathered,
        flops=10**9,
        moved=4 << 20,
        name="forward_x",
    )
    spectra = lax.all_to_all(spectra, ("gy", "gx"), 0, 0, tiled=True)
    place = lax.axis_index("gy") * count_x + spread[0]
    waves = jnp.asarray(wave_table(length_x, count))
    wave = lax.dynamic_slice(waves, (place, 0), (1, LANES))
    both, turns_y = y_tables(length_y)
    kept = rows + 2 * MARGIN // count_x
    half = (kept // 2 + 8) // 8 * 8
    solved = call(
        functools.partial(solve_y_kernel, count_x),
        (spectra, total, wave, beside(both), turns_y),
        shaped(count, half, LANES),
        (
            pltpu.VMEM((length_y + 2 * MARGIN, LANES), F32),
            pltpu.VMEM((length_y // RADIX, 2 * RADIX * LANES), F32),
            pltpu.VMEM((count, half, LANES), F32),
            pltpu.SemaphoreType.DMA((count // RADIX,)),
        ),
        out_specs=pl.BlockSpec(memory_space=pl.ANY),
        flops=4 * 10**9,
        moved=6 << 20,
        name="solve_y",
    )
    solved = lax.all_to_all(solved, ("gy", "gx"), 0, 0, tiled=True)
    back = 2.0 * zero.T
    back[LANES // 2] *= 0.5
    tables = np.concatenate(
        [beside(full.T), beside(back, 2.0 * middle.T)]
    )
    again = jnp.asarray(np.tile(turns, (count_x, 1, 1)))
    again = lax.dynamic_slice(again, (stepped[0], 0, 0), (1,) + turns.shape)
    pressed = call(
        functools.partial(inverse_x_kernel, kept, 1.0 / (length_x * length_y)),
        (solved, tables, again[0]),
        (shaped(kept, local_x + LANES),) * count_x,
        (
            pltpu.VMEM((kept, length_x), F32),
            pltpu.VMEM((kept, local_x + LANES), F32),
            pltpu.SemaphoreType.DMA(()),
        ),
        out_specs=(pl.BlockSpec(memory_space=pl.ANY),) + (pl.BlockSpec(memory_space=pltpu.VMEM),) * (count_x - 1),
        flops=10**9,
        moved=4 << 20,
        name="inverse_x",
    )
    return [piece if mask == 0 else swap(piece, "gx", mask) for mask, piece in enumerate(pressed)]


def fast_shards(velocity, weights_x, weights_y, acoustic, wall_mask):
    parts, _, tall, wide = acoustic.shape
    _, _, local_y, local_x = velocity.shape
    count_x, count_y = lax.axis_size("gx"), lax.axis_size("gy")
    place_x, place_y = lax.axis_index("gx"), lax.axis_index("gy")
    full, high, steps = wide + LANES, TILE + 2 * HALO, tall // TILE
    strips = (parts + 2) * HALO
    small = 2 * HALO
    has = jnp.stack([place_x > 0, place_x < count_x - 1, place_y > 0, place_y < count_y - 1])
    has = has.astype(F32)
    scalars = pl.BlockSpec(memory_space=pltpu.SMEM)

    def at(block, *index):
        return pl.BlockSpec(block, lambda i: index)

    own = place_x.astype(jnp.int32).reshape(1)
    sent = call(
        pieces_kernel,
        (velocity,),
        (shaped(2, local_y // count_x, local_x),) * count_x,
        moved=2 << 20,
        megabytes=8,
        name="pieces",
    )
    moved = [piece if mask == 0 else swap(piece, "gx", mask) for mask, piece in enumerate(sent)]
    first, last = call(
        rows_kernel,
        (acoustic, acoustic, wall_mask, wall_mask, velocity, velocity),
        (shaped(STRIP_ROWS, wide),) * 2,
        steps=1,
        specs={
            0: at((parts, 1, small, wide), 0, 0, 0, 0),
            1: at((parts, 1, small, wide), 0, 0, tall // small - 1, 0),
            2: at((1, HALO, wide), 0, 0, 0),
            3: at((1, HALO, wide), 0, tall // HALO - 1, 0),
            4: at((1, 1, HALO, local_x), 1, 0, 0, 0),
            5: at((1, 1, HALO, local_x), 1, 0, local_y // HALO - 1, 0),
        },
        after=moved[1:2],
        moved=2 << 20,
        megabytes=50,
        name="rows",
    )
    above, below = ring(last, "gy", 1), ring(first, "gy", -1)
    to_right, to_left = call(
        columns_kernel,
        (has, acoustic, acoustic, wall_mask, wall_mask, velocity, velocity, above, below),
        (shaped(strips, tall + LANES), shaped(strips, tall + LANES)),
        steps=1,
        specs={
            0: scalars,
            1: at((parts, 1, tall, LANES), 0, 0, 0, 0),
            2: at((parts, 1, tall, LANES), 0, 0, 0, wide // LANES - 1),
            3: at((1, tall, LANES), 0, 0, 0),
            4: at((1, tall, LANES), 0, 0, wide // LANES - 1),
            5: at((1, 1, local_y, LANES), 1, 0, 0, 0),
            6: at((1, 1, local_y, LANES), 1, 0, 0, local_x // LANES - 1),
        },
        moved=8 << 20,
        megabytes=54,
        name="columns",
    )
    from_left, from_right = ring(to_right, "gx", 1), ring(to_left, "gx", -1)
    rise_y, listed = call(
        tables_kernel,
        (jnp.stack([place_x, place_y]).astype(jnp.int32), weights_y),
        (shaped(steps, high, 3 * (high // 2 + HALO), kind=BF16), shaped(1, kind=jnp.int32)),
        specs={0: scalars},
        out_specs=(pl.BlockSpec(memory_space=pltpu.VMEM), scalars),
        moved=2 << 20,
        megabytes=54,
        name="tables",
    )
    sides, squares, beside = call(
        sides_kernel,
        (has, listed, velocity, above, below, from_left, from_right),
        (
            shaped(parts + 1, tall + LANES, LANES),
            shaped(local_y + 2 * HALO, local_x + LANES),
            shaped(1, kind=jnp.int32),
        ),
        steps=1,
        specs={0: scalars, 1: scalars, 2: at((1, 1, local_y, local_x), 1, 0, 0, 0)},
        out_specs=(
            at((parts + 1, tall + LANES, LANES), 0, 0, 0),
            at((local_y + 2 * HALO, local_x + LANES), 0, 0),
            scalars,
        ),
        moved=8 << 20,
        megabytes=54,
        name="sides",
    )
    across, along = band_tables(high)
    along_inner = along[HALO : HALO + TILE]
    per, rows = TILE // small, TILE // HALO

    def tiled(first):
        walls = (
            pl.BlockSpec((1, TILE, wide), lambda i: (0, i + first, 0)),
            pl.BlockSpec((1, HALO, wide), lambda i: (0, jnp.maximum((i + first) * rows - 1, 0), 0)),
            pl.BlockSpec(
                (1, HALO, wide),
                lambda i: (0, jnp.minimum((i + first + 1) * rows, steps * rows - 1), 0),
            ),
        )
        cells = (
            pl.BlockSpec((parts, 1, TILE, wide), lambda i: (0, 0, i + first, 0)),
            pl.BlockSpec(
                (parts, 1, small, wide), lambda i: (0, 0, jnp.maximum((i + first) * per - 1, 0), 0)
            ),
            pl.BlockSpec(
                (parts, 1, small, wide),
                lambda i: (0, 0, jnp.minimum((i + first + 1) * per, steps * per - 1), 0),
            ),
        )
        return cells, walls

    def quiet_tiles(first, count, before):
        cells, walls = tiled(first)
        operands = (has, own, acoustic, acoustic, acoustic, wall_mask, wall_mask, wall_mask, above, below, sides)
        operands = operands + (across, along, along_inner)
        return call(
            functools.partial(quiet_step_kernel, first),
            operands,
            (
                shaped(parts - 1, tall, wide),
                shaped(*acoustic.shape, kind=BF16),
                shaped(steps, high, full, kind=BF16),
                shaped(1, kind=jnp.int32),
            ),
            steps=count,
            specs=dict(enumerate((scalars, scalars) + cells + walls)),
            out_specs=(
                pl.BlockSpec((parts - 1, TILE, wide), lambda i: (0, i + first, 0)),
                pl.BlockSpec((1, 1, TILE, wide), lambda i: (0, 0, i + first, 0)),
                pl.BlockSpec((1, high, full), lambda i: (i + first, 0, 0)),
                scalars,
            ),
            after=before,
            aliases={len(operands) + k: k for k in range(len(before))},
            megabytes=54,
            flops=3 * 10**9 * count,
            moved=(12 << 20) * count,
            name="quiet_step",
        )

    early = max(steps * 3 // 4, 1)
    *begun, stepped = quiet_tiles(0, early, ())
    if early < steps:
        *begun, _ = quiet_tiles(early, steps - early, begun)
    quiet, final, opened = begun
    lines = pressure_lines(moved, (above, below), beside, stepped)
    operands = (weights_x, squares, opened, rise_y, quiet, across, along_inner, final, *lines)
    anywhere = pl.BlockSpec(memory_space=pl.ANY)
    specs = {k: anywhere for k in range(1, len(operands))}
    scratch = (
        pltpu.VMEM(squares.shape, F32),
        pltpu.VMEM((2,) + opened.shape[1:], BF16),
        pltpu.VMEM(rise_y.shape, BF16),
        pltpu.VMEM((2, parts - 1, TILE, wide), F32),
        pltpu.VMEM(across.shape, BF16),
        pltpu.VMEM(along_inner.shape, BF16),
        pltpu.VMEM((local_y + 2 * MARGIN, local_x + LANES), F32),
        pltpu.VMEM((2, local_y + 2 * HALO, full), BF16),
        pltpu.VMEM((steps, parts - 1, TILE, wide), BF16),
        pltpu.SemaphoreType.DMA((8 + count_x,)),
        pltpu.SemaphoreType.DMA((steps,)),
    )
    return call(
        source_kernel,
        operands,
        shaped(*acoustic.shape, kind=BF16),
        scratch,
        specs=specs,
        out_specs=anywhere,
        aliases={7: 0},
        megabytes=56,
        flops=4 * 10**9,
        moved=16 << 20,
        name="source_step",
    )


def fits(count_x, count_y, velocity, acoustic):
    _, planes, local_y, local_x = velocity
    _, _, tall, wide = acoustic
    length_x, length_y = local_x * count_x, local_y * count_y
    rows = local_y // count_x
    base_x, base_y = length_x // RADIX, length_y // RADIX
    return (
        planes == 1
        and acoustic[0] == PARTS
        and length_x * 2 == count_x * count_y * LANES
        and base_x % (2 * LANES) == 0
        and local_x % base_x == 0
        and rows % 8 == 0
        and base_y % rows == 0
        and base_y % 8 == 0
        and count_x * count_y % RADIX == 0
        and MARGIN * 2 % (8 * count_x) == 0
        and tall == 2 * local_y
        and wide == 2 * local_x
        and tall % TILE == 0
        and tall % LANES == 0
        and tall >= 2 * TILE
        and count_x & (count_x - 1) == 0
        and wide % (2 * LANES) == 0
    )


def extended(array, sides, width):
    for axis, dim in sides:
        size, length = (lax.axis_size(axis), array.shape[dim])
        up = [(i, (i + 1) % size) for i in range(size - 1)]
        down = [(j, i) for i, j in up]
        last = lax.slice_in_dim(array, length - width, length, axis=dim)
        leading = lax.slice_in_dim(array, 0, width, axis=dim)
        before = lax.ppermute(last, axis, up)
        after = lax.ppermute(leading, axis, down)
        array = jnp.concatenate([before, array, after], axis=dim)
    return array


def gradients(padded):
    height = padded.shape[-2] - 6
    breadth = padded.shape[-1] - 6
    rows_mid = padded[..., 3 : 3 + height, :]
    cols_mid = padded[..., :, 3 : 3 + breadth]
    along_x = jnp.zeros_like(padded[..., 3 : 3 + height, 3 : 3 + breadth])
    along_y = jnp.zeros_like(along_x)
    for index, weight in enumerate(stencil_weights):
        distance = index + 1
        along_x = along_x + weight * (
            rows_mid[..., 3 + distance : 3 + distance + breadth]
            - rows_mid[..., 3 - distance : 3 - distance + breadth]
        )
        along_y = along_y + weight * (
            cols_mid[..., 3 + distance : 3 + distance + height, :]
            - cols_mid[..., 3 - distance : 3 - distance + height, :]
        )
    return (along_x, along_y)


def tendency(padded, source):
    along_x, along_y = gradients(padded)
    diverge = along_x[1] + along_y[2]
    forcing = jnp.stack([-diverge, -along_x[3], -along_y[3], source - diverge])
    return forcing - mean_flow * along_x


def spectral_index(flat, length):
    second = length // 16
    wave = flat // second + 16 * (flat % second)
    return jnp.where(wave < length // 2, wave, wave - length).astype(jnp.float32)


def twiddles(rows_count, cols_count, modulus, sign):
    products = jnp.arange(rows_count)[:, None] * jnp.arange(cols_count)[None, :] % modulus
    angles = 2.0 * math.pi / modulus * products.astype(jnp.float32)
    return (jnp.cos(angles), sign * jnp.sin(angles))


def mix_rows(real_part, imag_part, cosine, sine):
    exact = lax.Precision.HIGHEST
    cos_real = jnp.einsum("ka,...ab->...kb", cosine, real_part, precision=exact)
    cos_imag = jnp.einsum("ka,...ab->...kb", cosine, imag_part, precision=exact)
    sin_real = jnp.einsum("ka,...ab->...kb", sine, real_part, precision=exact)
    sin_imag = jnp.einsum("ka,...ab->...kb", sine, imag_part, precision=exact)
    return (cos_real - sin_imag, cos_imag + sin_real)


def mix_cols(real_part, imag_part, cosine, sine):
    exact = lax.Precision.HIGHEST
    cos_real = jnp.einsum("...kb,bc->...kc", real_part, cosine, precision=exact)
    cos_imag = jnp.einsum("...kb,bc->...kc", imag_part, cosine, precision=exact)
    sin_real = jnp.einsum("...kb,bc->...kc", real_part, sine, precision=exact)
    sin_imag = jnp.einsum("...kb,bc->...kc", imag_part, sine, precision=exact)
    return (cos_real - sin_imag, cos_imag + sin_real)


def rotate(real_part, imag_part, cosine, sine):
    return (real_part * cosine - imag_part * sine, real_part * sine + imag_part * cosine)


def discrete(real_part, imag_part, sign):
    length = real_part.shape[-1]
    second = length // 16
    initial = real_part.shape
    folded = initial[:-1] + (16, second)
    real_part = real_part.reshape(folded)
    imag_part = imag_part.reshape(folded)
    small_cos, small_sin = twiddles(16, 16, 16, sign)
    large_cos, large_sin = twiddles(second, second, second, sign)
    turn_cos, turn_sin = twiddles(16, second, length, sign)
    if sign < 0:
        real_part, imag_part = mix_rows(real_part, imag_part, small_cos, small_sin)
        real_part, imag_part = rotate(real_part, imag_part, turn_cos, turn_sin)
        real_part, imag_part = mix_cols(real_part, imag_part, large_cos, large_sin)
    else:
        real_part, imag_part = mix_cols(real_part, imag_part, large_cos, large_sin)
        real_part, imag_part = rotate(real_part, imag_part, turn_cos, turn_sin)
        real_part, imag_part = mix_rows(real_part, imag_part, small_cos, small_sin)
        real_part = real_part / length
        imag_part = imag_part / length
    return (real_part.reshape(initial), imag_part.reshape(initial))


def transform(stacked, sign, kind):
    if kind == "real_in":
        real_part = stacked
        imag_part = jnp.zeros_like(stacked)
    else:
        half = stacked.shape[0] // 2
        real_part = stacked[:half]
        imag_part = stacked[half:]
    real_out, imag_out = discrete(real_part, imag_part, sign)
    if kind == "real_out":
        return real_out
    return jnp.concatenate([real_out, imag_out], axis=0)


def project(stacked, wave_x, wave_y):
    coef_xx = wave_x * wave_x
    coef_xy = 2.0 * wave_x * wave_y
    coef_yy = wave_y * wave_y
    denominator = wave_x * wave_x + wave_y * wave_y
    positive = denominator > 0
    safe = jnp.where(positive, denominator, 1.0)

    def combine(parts):
        numerator = -(coef_xx * parts[0] + coef_xy * parts[1] + coef_yy * parts[2])
        return jnp.where(positive, numerator / safe, 0.0)

    return jnp.stack([combine(stacked[:3]), combine(stacked[3:])])


def refine(stacked, weights):
    result = jnp.zeros(stacked.shape[:-1] + (2 * stacked.shape[-1],), jnp.float32)
    for offset in range(4):
        result = (
            result
            + jnp.repeat(jnp.roll(stacked, 1 - offset, axis=-1), 2, axis=-1) * weights[offset]
        )
    return result


def lines_x(stacked, action):
    gathered = action(lax.all_to_all(stacked, "gx", split_axis=2, concat_axis=3, tiled=True))
    return lax.all_to_all(gathered, "gx", split_axis=3, concat_axis=2, tiled=True)


def lines_y(stacked, action):
    turned = jnp.swapaxes(stacked, 2, 3)
    gathered = action(lax.all_to_all(turned, "gy", split_axis=2, concat_axis=3, tiled=True))
    returned = lax.all_to_all(gathered, "gy", split_axis=3, concat_axis=2, tiled=True)
    return jnp.swapaxes(returned, 2, 3)


def expand(fields):
    return extended(fields, (("gx", 3), ("gy", 2)), 3)


def shards(velocity, weights_x, weights_y, acoustic, wall_mask):
    acoustic = acoustic.astype(jnp.float32)
    flow_x = velocity[0]
    flow_y = velocity[1]
    tensor = jnp.stack([flow_x * flow_x, flow_x * flow_y, flow_y * flow_y])
    count_gx = lax.axis_size("gx")
    count_gy = lax.axis_size("gy")
    place_x = lax.axis_index("gx")
    place_y = lax.axis_index("gy")
    local_y = tensor.shape[2]
    local_x = tensor.shape[3]
    length_x = local_x * count_gx
    length_y = local_y * count_gy

    def forward_real(portion):
        return transform(portion, -1, "real_in")

    def finish_x(portion):
        return refine(transform(portion, 1, "real_out"), weights_x)

    spectra = lines_x(tensor, forward_real)
    share_x = local_x // count_gy
    line_x = spectral_index(place_x * local_x + place_y * share_x + jnp.arange(share_x), length_x)[
        :, None
    ]
    line_y = spectral_index(jnp.arange(length_y), length_y)[None, :]

    def solve_y(portion):
        solved = project(transform(portion, -1, "complex"), line_x, line_y)
        return refine(transform(solved, 1, "complex"), weights_y)

    pressure = lines_y(spectra, solve_y)
    source = lines_x(pressure, finish_x)[0]
    open_cells = (1 - wall_mask).astype(jnp.float32)
    first_rate = tendency(expand(acoustic), source)
    middle = open_cells * (acoustic + time_step * first_rate)
    second_rate = tendency(expand(middle), source)
    return (open_cells * (acoustic + 0.5 * time_step * (first_rate + second_rate))).astype(
        jnp.bfloat16
    )


def solution(mesh):
    in_specs = (P(None, None, "gy", "gx"), P(), P(), P(None, None, "gy", "gx"), P(None, "gy", "gx"))
    out_specs = P(None, None, "gy", "gx")

    def chosen(velocity, weights_x, weights_y, acoustic, wall_mask):
        sizes = (mesh.shape["gx"], mesh.shape["gy"], velocity.shape, acoustic.shape)
        plan = fast_shards if fits(*sizes) else shards
        return plan(velocity, weights_x, weights_y, acoustic, wall_mask)

    return jax.shard_map(
        chosen, mesh=mesh, in_specs=in_specs, out_specs=out_specs, check_vma=False
    )
```

```python
import functools
import math

import jax
import jax.numpy as jnp
import ml_dtypes
import numpy as np
from jax import lax
from jax.experimental import pallas as pl
from jax.experimental.pallas import tpu as pltpu
from jax.sharding import PartitionSpec as P

stencil_weights = (0.75, -0.15, 1.0 / 60.0)
mean_flow = 0.3
time_step = 0.5
whole_weights = (45.0, -9.0, 1.0)

LANES = 128
RADIX = 8
HALO = 8
MARGIN = 16
TILE = 128
ROOT = math.sqrt(0.5)
STRIP = {2: (0, 6), 3: (6, 6), 1: (12, 3), 4: (15, 3), 5: (20, 4)}
STRIP_ROWS = 24
PARTS = 4
BF16 = jnp.bfloat16
F32 = jnp.float32


def halves(table):
    high = table.astype(np.float32).astype(ml_dtypes.bfloat16)
    low = (table - high.astype(np.float64)).astype(np.float32).astype(ml_dtypes.bfloat16)
    return high, low


def packed_columns(cosine, sine):
    half = LANES // 2
    parts = []
    for first in range(0, cosine.shape[1], half):
        parts += [cosine[:, first : first + half], sine[:, first : first + half]]
    return np.concatenate(parts, axis=1)


@functools.lru_cache(maxsize=None)
def x_tables(length):
    base = length // RADIX
    m = np.arange(base)[:, None]
    q = np.arange(base)[None, :]
    angle = 2.0 * np.pi * ((m * q) % base) / base
    cosine, sine = np.cos(angle), np.sin(angle)
    full = np.concatenate([packed_columns(cosine, -sine), packed_columns(sine, cosine)], axis=0)
    half = base // 2
    zero_cos, zero_sin = cosine[:, :half].copy(), -sine[:, :half]
    zero_cos[:, 0] = 0.0
    zero_sin = zero_sin.copy()
    zero_sin[:, 0] = (-1.0) ** np.arange(base)
    zero = packed_columns(zero_cos, zero_sin)
    shifted = 2.0 * np.pi * ((m * (RADIX * q[:, :half] + RADIX // 2)) % length) / length
    middle = packed_columns(np.cos(shifted), -np.sin(shifted))
    turns = 2.0 * np.pi * np.arange(1, RADIX // 2)[:, None] * np.arange(base)[None, :] / length
    return full, zero, middle, np.cos(turns), np.sin(turns)


@functools.lru_cache(maxsize=None)
def y_tables(length):
    base = length // RADIX
    index = np.arange(base)
    angle = 2.0 * np.pi * ((index[:, None] * index[None, :]) % base) / base
    both = np.concatenate([np.cos(angle), np.sin(angle)], axis=0)
    turns = 2.0 * np.pi * np.arange(RADIX)[:, None] * index[None, :] / length
    turns = np.concatenate([np.cos(turns), np.sin(turns)], axis=0).T
    high, rest = halves(turns)
    low = turns - high.astype(np.float64) - rest.astype(np.float64)
    return both, np.concatenate([high, rest, low.astype(ml_dtypes.bfloat16)], axis=1)


@functools.lru_cache(maxsize=None)
def wave_table(length, count):
    slots = LANES // 4
    base = length // RADIX
    waves = []
    for residue in (1, 2, 3):
        waves.append(RADIX * np.arange(base) + residue)
    waves.append(RADIX * np.arange(base // 2))
    waves.append(RADIX * np.arange(base // 2) + RADIX // 2)
    waves = np.concatenate(waves)
    waves = np.where(waves == 0, length // 2, waves)
    waves = np.where(waves < length // 2, waves, waves - length).reshape(count, slots)
    return np.tile(waves, (1, 4)).astype(np.float32)


@functools.lru_cache(maxsize=None)
def band_tables(rows):
    across = np.zeros((4 * LANES, 2 * LANES))
    column = np.arange(2 * LANES)
    down = np.zeros((rows, rows))
    for index, weight in enumerate(whole_weights):
        distance = index + 1
        across[column + LANES + distance, column] = weight
        across[column + LANES - distance, column] = -weight
        down += weight * (np.eye(rows, k=distance) - np.eye(rows, k=-distance))
    return across.astype(ml_dtypes.bfloat16), down.astype(ml_dtypes.bfloat16)


def beside(*tables):
    high, low = halves(np.concatenate(tables, axis=1))
    return np.concatenate([high, low], axis=0)


def split(values):
    high = values.astype(BF16)
    return high, (values - high.astype(F32)).astype(BF16)


def dot(left, right):
    return jnp.dot(left, right, preferred_element_type=F32)


def exact_dot(left, right):
    left_high, left_low = left
    right_high, right_low = right
    return dot(left_high, right_high) + (dot(left_low, right_high) + dot(left_high, right_low))


def lane_index(shape):
    return lax.broadcasted_iota(jnp.int32, shape, len(shape) - 1)


def spin(values, shift):
    return pltpu.roll(values, shift % values.shape[-1], values.ndim - 1)


def lane_tile(values, index):
    return values[:, index * LANES : (index + 1) * LANES]


def x_parts(tables, base):
    wide = 2 * base
    full = (tables[:wide], tables[wide : 2 * wide])
    at = 2 * wide
    high, low = tables[at : at + base], tables[at + base : at + 2 * base]
    return full, (high[:, :base], low[:, :base]), (high[:, base:], low[:, base:])


def pieces_kernel(velocity, *pieces):
    rows = pieces[0].shape[1]
    place = lax.axis_index("gx")
    for mask, piece in enumerate(pieces):
        start = pl.multiple_of((place ^ mask) * rows, 8)
        for c in range(2):
            piece[c] = velocity[c, 0, pl.ds(start, rows), :]


def rows_kernel(top, low, top_wall, low_wall, top_flow, low_flow, first, last):
    small, width = top.shape[2], top_flow.shape[3]
    first[...] = jnp.zeros(first.shape, F32)
    last[...] = jnp.zeros(last.shape, F32)
    for k, (start, rows) in STRIP.items():
        lanes = slice(0, width) if k == PARTS + 1 else slice(None)
        if k < PARTS:
            upper, lower = top[k, 0].astype(F32)[:HALO], low[k, 0].astype(F32)[small - HALO :]
        elif k == PARTS:
            upper, lower = 1.0 - top_wall[0].astype(F32), 1.0 - low_wall[0].astype(F32)
        else:
            upper, lower = top_flow[0, 0], low_flow[0, 0]
        first[start : start + rows, lanes] = upper[:rows]
        last[start : start + rows, lanes] = lower[HALO - rows :]


def strip(ref, k, upper, lanes=slice(None)):
    if k not in STRIP:
        return jnp.zeros((HALO, ref[0:1, lanes].shape[1]), F32)
    start, rows = STRIP[k]
    values = ref[start : start + rows, lanes]
    blank = jnp.zeros((HALO - rows, values.shape[1]), F32)
    return jnp.concatenate([blank, values] if upper else [values, blank], axis=0)


def columns_kernel(
    has, left, right, left_wall, right_wall, left_flow, right_flow, above, below, to_right, to_left
):
    parts = left.shape[0]
    wide, flow_wide = above.shape[1], above.shape[1] // 2
    gap = jnp.zeros((LANES - 2 * HALO, LANES), F32)

    def tall(k, inner, first, sides):
        lanes = slice(first, first + LANES)
        over, under = strip(above, k, True, lanes), strip(below, k, False, lanes)
        return jnp.concatenate([inner, under * sides[1], gap, over * sides[0]], axis=0).T

    for k in range(parts + 1):
        at = slice(k * HALO, (k + 1) * HALO)
        if k < parts:
            near, far = left[k, 0].astype(F32), right[k, 0].astype(F32)
        else:
            near, far = 1.0 - left_wall[0].astype(F32), 1.0 - right_wall[0].astype(F32)
        sides = (has[2], has[3])
        to_left[at, :] = tall(k, near, 0, sides)[:HALO]
        to_right[at, :] = tall(k, far, wide - LANES, sides)[LANES - HALO :]
    k = parts + 1
    at = slice(k * HALO, (k + 1) * HALO)
    size = left_flow.shape[2] + LANES
    blank = jnp.zeros((HALO, to_left.shape[1] - size), F32)
    to_left[at, :size] = tall(k, left_flow[0, 0], 0, (1.0, 1.0))[:HALO]
    to_right[at, :size] = tall(k, right_flow[0, 0], flow_wide - LANES, (1.0, 1.0))[LANES - HALO :]
    to_left[at, size:] = blank
    to_right[at, size:] = blank


def sides_kernel(has, place, velocity, above, below, from_left, from_right, sides, squares, mark):
    parts, tall, _ = sides.shape
    gap = jnp.zeros((LANES - 2 * HALO, tall), F32)
    for k in range(parts):
        at = slice(k * HALO, (k + 1) * HALO)
        tile = [from_right[at, :] * has[1], gap, from_left[at, :] * has[0]]
        sides[k] = jnp.concatenate(tile, axis=0).T
    at = slice(parts * HALO, (parts + 1) * HALO)
    rows, local = velocity.shape[2:]
    size = rows + LANES
    tile = [from_right[at, :size], gap[:, :size], from_left[at, :size]]
    tile = jnp.concatenate(tile, axis=0).T
    tile = tile * tile
    mark[0] = place[0]
    over, under = (strip(ref, parts, ref is above, slice(0, local)) for ref in (above, below))
    squares[:HALO, :local] = over * over
    squares[HALO : HALO + rows, :local] = velocity[0, 0] * velocity[0, 0]
    squares[HALO + rows :, :local] = under * under
    squares[:HALO, local:] = tile[size - HALO :]
    squares[HALO : HALO + rows, local:] = tile[:rows]
    squares[HALO + rows :, local:] = tile[rows : rows + HALO]


def forward_x_kernel(*refs):
    *pieces, tables, turns, out, total, lines, made, sent = refs
    count, _, rows, local = lines.shape
    place = lax.axis_index("gx")
    for mask, piece in enumerate(pieces):
        lines[place ^ mask] = piece[...]
    base = turns.shape[1]
    per = local // base
    u = [lines[t // per, 0, :, (t % per) * base : (t % per + 1) * base] for t in range(RADIX)]
    v = [lines[t // per, 1, :, (t % per) * base : (t % per + 1) * base] for t in range(RADIX)]
    energy = sum(b * b for b in v)
    energy = jnp.sum(energy.reshape(rows // 8, 8, base), axis=0)
    total[...] = sum(energy[:, k : k + LANES] for k in range(0, base, LANES))
    fields = ([a * a - b * b for a, b in zip(u, v)], [2.0 * a * b for a, b in zip(u, v)])
    zeros, mids, reals, imags = [], [], [[], [], []], [[], [], []]
    for a in fields:
        s04, s26, s15, s37 = a[0] + a[4], a[2] + a[6], a[1] + a[5], a[3] + a[7]
        d04, d26, d15, d37 = a[0] - a[4], a[2] - a[6], a[1] - a[5], a[3] - a[7]
        zeros.append((s04 + s26) + (s15 + s37))
        mids.append((s04 + s26) - (s15 + s37))
        minus, plus = ROOT * (d15 - d37), ROOT * (d15 + d37)
        turned = (
            (d04 + minus, -d26 - plus),
            (s04 - s26, s37 - s15),
            (d04 - minus, d26 - plus),
        )
        for index, (real, imag) in enumerate(turned):
            c, s = turns[index : index + 1, :], turns[index + 3 : index + 4, :]
            reals[index].append(real * c + imag * s)
            imags[index].append(imag * c - real * s)
    stacked = jnp.concatenate(
        [
            jnp.concatenate([jnp.concatenate(reals[i], axis=0) for i in range(3)], axis=0),
            jnp.concatenate([jnp.concatenate(imags[i], axis=0) for i in range(3)], axis=0),
        ],
        axis=1,
    )
    full, zero, middle = x_parts(tables, base)
    full = exact_dot(split(stacked), full)
    zero = exact_dot(split(jnp.concatenate(zeros, axis=0)), zero)
    middle = exact_dot(split(jnp.concatenate(mids, axis=0)), middle)
    low = lane_index((rows, LANES)) % 64 < 32
    target, copies = 0, []
    blocks = [full[2 * rows * i : 2 * rows * (i + 1)] for i in range(3)] + [zero, middle]
    for block in blocks:
        start = target
        for first in range(0, block.shape[1], LANES):
            a = block[:rows, first : first + LANES]
            c = block[rows:, first : first + LANES]
            made[target] = jnp.where(low, a, spin(c, 32))
            made[target + 1] = jnp.where(low, spin(a, -32), c)
            target += 2
        group = pl.ds(start, target - start)
        copies.append(pltpu.make_async_copy(made.at[group], out.at[group], sent.at[len(copies)]))
        copies[-1].start()
    for copy in copies:
        copy.wait()


def eighths(x, turn):
    s04, s26, s15, s37 = x[0] + x[4], x[2] + x[6], x[1] + x[5], x[3] + x[7]
    d04, d26, d15, d37 = x[0] - x[4], x[2] - x[6], x[1] - x[5], x[3] - x[7]
    quarter = turn(s15 - s37)
    spun_26, spun_37 = turn(d26), turn(d37)
    one, three = d15 + spun_37, d15 - spun_37
    spun_one, spun_three = turn(one), turn(three)
    one = ROOT * (one + spun_one)
    three = ROOT * (spun_three - three)
    return [
        (s04 + s26) + (s15 + s37),
        (d04 + spun_26) + one,
        (s04 - s26) + quarter,
        (d04 - spun_26) + three,
        (s04 + s26) - (s15 + s37),
        (d04 + spun_26) - one,
        (s04 - s26) - quarter,
        (d04 - spun_26) - three,
    ]


def solve_y_kernel(count_x, lines, total, wave, both, turns, out, held, spread, made, sent):
    count, rows, _ = lines.shape
    base = turns.shape[0]
    length = count * rows
    block = count_x * rows
    per = base // rows
    lanes = lane_index((base, LANES))
    sign = jnp.where(lanes < 64, 1.0, -1.0).astype(F32)

    def minus_i(z):
        return spin(z, 64) * sign

    def plus_i(z):
        return spin(z, 64) * -sign

    fields = [
        jnp.concatenate([lines[t * per + k] for k in range(per)], axis=0) for t in range(RADIX)
    ]
    mixed = eighths(fields, minus_i)
    terms, columns = turns.shape[1], 2 * RADIX
    picked = lax.broadcasted_iota(jnp.int32, (terms, columns * LANES), 0) % columns
    lane = lane_index(picked.shape)
    value = jnp.where((lane >= RADIX * LANES) & (lane % LANES >= 64), -1.0, 1.0)
    spread[...] = dot(turns[...], jnp.where(picked == lane // LANES, value, 0.0).astype(BF16))
    cosines = [spread[:, r * LANES : (r + 1) * LANES] for r in range(RADIX)]
    sines = [spread[:, (r + RADIX) * LANES : (r + RADIX + 1) * LANES] for r in range(RADIX)]
    mixed = [mixed[0]] + [
        mixed[r] * cosines[r] + spin(mixed[r], 64) * sines[r] for r in range(1, RADIX)
    ]
    tables = (both[: 2 * base], both[2 * base :])
    product = exact_dot(tables, split(jnp.concatenate(mixed, axis=1)))
    kx = wave[0:1, :]
    first = lanes % 64 < 32
    edge = jnp.float32(length // 2)
    square_kx = kx * kx
    alone = jnp.where(first, square_kx, 0.0)
    slope = jnp.where(first | (kx == -edge), 0.0, jnp.broadcast_to(kx, lanes.shape))
    q = lax.broadcasted_iota(jnp.int32, lanes.shape, 0)
    low_ky = RADIX * (q - jnp.where(q < base // 2, 0, base)).astype(F32)
    terms = []
    for r in range(RADIX):
        at = slice(r * LANES, (r + 1) * LANES)
        spectrum = product[:base, at] + minus_i(product[base:, at])
        ky = low_ky + float(r)
        symbol = alone + slope * ky
        if r == 0:
            corner = jnp.where((kx == -edge) & ~first, edge * edge, 0.0)
            symbol = jnp.where(ky == -edge, jnp.where(first, alone, corner), symbol)
        square = square_kx + ky * ky
        guess = pl.reciprocal(square, approx=True)
        terms.append(symbol * (guess * (2.0 - square * guess)) * spectrum)
    pairs = [
        jnp.where(first, low + spin(low, -32), high + spin(high, 32))
        for low, high in zip(terms[:4], terms[4:])
    ]
    product = exact_dot(tables, split(jnp.concatenate(pairs, axis=1)))
    mixed = []
    for r in range(RADIX // 2):
        at = slice(r * LANES, (r + 1) * LANES)
        value = product[:base, at] + plus_i(product[base:, at])
        cosine = jnp.where(first, cosines[r], cosines[r + 4])
        sine = jnp.where(first, sines[r], sines[r + 4])
        value = value * cosine - spin(value, 64) * sine
        value = jnp.where(first, value + spin(value, -32), spin(value, 32) - value)
        if r == 2:
            value = jnp.where(first, value, plus_i(value))
        elif r:
            turned = plus_i(value)
            odd = value + turned if r == 1 else turned - value
            value = jnp.where(first, value, ROOT * odd)
        mixed.append(value)
    even, odd = mixed[0] + mixed[2], mixed[0] - mixed[2]
    side, turned = mixed[1] + mixed[3], plus_i(mixed[1] - mixed[3])
    for t, values in enumerate((even + side, odd + turned, even - side, odd - turned)):
        start = MARGIN + 2 * t * base
        held[start : start + base, :] = values
        held[start + base : start + 2 * base, :] = spin(values, -32)
    held[0:MARGIN, :] = held[length : length + MARGIN, :]
    held[length + MARGIN : length + 2 * MARGIN, :] = held[MARGIN : 2 * MARGIN, :]
    spare = total[...] + spin(total[...], 32)
    kept = rows + 2 * MARGIN // count_x
    half = made.shape[1]
    rest = kept - half
    low = lane_index((8, LANES)) % 64 < 32
    copies = []
    for target in range(count):
        start = (target // count_x) * block + (target % count_x) * kept
        for row in range(0, half, 8):
            a = held[start + row : start + row + 8, :]
            if row < rest:
                b = spin(held[start + half + row : start + half + row + 8, :], 32)
            else:
                b = spare
            made[target, row : row + 8, :] = jnp.where(low, a, b)
        if (target + 1) % RADIX == 0:
            group = pl.ds(target + 1 - RADIX, RADIX)
            copies.append(pltpu.make_async_copy(made.at[group], out.at[group], sent.at[len(copies)]))
            copies[-1].start()
    for copy in copies:
        copy.wait()


def inverse_x_kernel(
    kept, scale, lines, tables, turns, *refs
):
    *outs, held = refs
    place = lax.axis_index("gx")
    count, half, _ = lines.shape
    base = turns.shape[1]
    length = RADIX * base
    rest = kept - half
    low = lane_index((half, LANES)) % 64 < 32
    groups, spare = [], None
    for first in range(0, count, 2):
        even, odd = lines[first], lines[first + 1]
        a = jnp.where(low, even, spin(odd, 32))
        b = jnp.where(low, spin(even, -32), odd)
        groups.append(jnp.concatenate([a, b[:rest]], axis=0))
        extra = b[rest : rest + 8]
        spare = extra if spare is None else spare + extra
    mean = jnp.sum(spare) * scale
    wide = 2 * base // LANES
    narrow = base // LANES
    stacked = jnp.concatenate(
        [jnp.concatenate(groups[i * wide : (i + 1) * wide], axis=1) for i in range(3)], axis=0
    )
    at = 3 * wide
    zeros = jnp.concatenate(groups[at : at + narrow], axis=1)
    mids = jnp.concatenate(groups[at + narrow : at + 2 * narrow], axis=1)
    full, zero, middle = x_parts(tables, base)
    full = exact_dot(split(stacked), full)
    zero = exact_dot(split(zeros), zero) * scale
    mid = exact_dot(split(mids), middle) * scale
    turned = []
    for i in range(3):
        real = full[i * kept : (i + 1) * kept, :base]
        imag = full[i * kept : (i + 1) * kept, base:]
        c = turns[i : i + 1, :] * (2.0 * scale)
        s = turns[i + 3 : i + 4, :] * (2.0 * scale)
        turned.append((real * c - imag * s, real * s + imag * c))
    for t in range(RADIX):
        value = zero + mid if t % 2 == 0 else zero - mid
        for i, (real, imag) in enumerate(turned):
            eighth = t * (i + 1) % RADIX
            c = (1.0, ROOT, 0.0, -ROOT, -1.0, -ROOT, 0.0, ROOT)[eighth]
            s = (0.0, ROOT, 1.0, ROOT, 0.0, -ROOT, -1.0, -ROOT)[eighth]
            if c:
                value = value + c * real
            if s:
                value = value - s * imag
        held[:, t * base : (t + 1) * base] = mean - value
    targets, local = len(outs), outs[0].shape[1] - LANES
    right = lane_index((kept, LANES)) < 64
    for mask, out in enumerate(outs):
        start = pl.multiple_of((place ^ mask) * local, LANES)
        after = pl.multiple_of(jnp.where(start + local == length, 0, start + local), LANES)
        before = pl.multiple_of(jnp.where(start == 0, length, start) - LANES, LANES)
        out[:, :local] = held[:, pl.ds(start, local)]
        out[:, local:] = jnp.where(
            right, held[:, pl.ds(after, LANES)], held[:, pl.ds(before, LANES)]
        )


def slopes_x(parts, band, with_edge):
    tiles = parts[0].shape[-1] // LANES
    pieces = []
    for first in list(range(0, tiles - 1, 2)) + ([tiles - 1] if with_edge else []):
        steps = (-1, 0, 1, 2) if first < tiles - 1 else (-1, 0, 1)
        table = band[...] if first < tiles - 1 else band[: 3 * LANES, :LANES]
        order = [(first + step) % tiles for step in steps]
        piece = None
        for part in parts:
            term = dot(jnp.concatenate([lane_tile(part, t) for t in order], axis=1), table)
            piece = term if piece is None else piece + term
        pieces.append(piece)
    return jnp.concatenate(pieces, axis=1)


def slope_y(read):
    value = read(3) - read(-3)
    for index in (0, 1):
        value = value + whole_weights[index] * (read(index + 1) - read(-index - 1))
    return value


def edged(k, side, center, up, down, above, below, sides, has, first=0):
    step = pl.program_id(0) + first
    tile, width = center.shape
    tall = sides.shape[1]
    last = (tall - LANES) // tile - 1
    base = pl.multiple_of(step * tile, 8)
    before = pl.multiple_of(jnp.where(step == 0, tall, base) - HALO, 8)
    over = jnp.where(step == 0, strip(above, k, True) * has[2], up)
    under = jnp.where(step == last, strip(below, k, False) * has[3], down)
    rows = (
        (over, sides[side, pl.ds(before, HALO), :]),
        (center, sides[side, pl.ds(base, tile), :]),
        (under, sides[side, pl.ds(pl.multiple_of(base + tile, 8), HALO), :]),
    )
    return jnp.concatenate([jnp.concatenate(pair, axis=1) for pair in rows], axis=0)


def edged_open(k, side, wall, wall_up, wall_down, above, below, sides, has, first=0):
    open_cells = [1.0 - ref[0].astype(F32) for ref in (wall, wall_up, wall_down)]
    return edged(k, side, *open_cells, above, below, sides, has, first)


def quiet_step_kernel(
    first, has, place, center, up, down, wall, wall_up, wall_down, above, below, sides, across, along, along_inner, calm, density, shown_open, mark
):
    parts, _, tile, width = center.shape
    high = tile + 2 * HALO
    opened = edged_open(parts, parts, wall, wall_up, wall_down, above, below, sides, has, first)
    values = []
    for k in range(parts):
        value = edged(
            k,
            k,
            center[k, 0].astype(F32),
            up[k, 0].astype(F32)[up.shape[2] - HALO :],
            down[k, 0].astype(F32)[:HALO],
            above,
            below,
            sides,
            has,
            first,
        )
        values.append(value)

    def drops(x, along_b, along_p):
        diverge = x[1] + along_b
        return (
            diverge + mean_flow * x[0],
            x[3] + mean_flow * x[1],
            along_p + mean_flow * x[2],
            diverge + mean_flow * x[3],
        )

    short = [value.astype(BF16) for value in values]
    x = slopes_x((jnp.concatenate(short, axis=0),), across, True)
    x = [x[k * high : (k + 1) * high] for k in range(parts)]
    table = along[...]
    dropped = drops(x, dot(table, short[2]), dot(table, short[3]))
    middle = [opened * (v - (time_step / 60.0) * d) for v, d in zip(values, dropped)]
    inner = slice(HALO, HALO + tile)
    x = slopes_x(split(jnp.concatenate([value[inner] for value in middle], axis=0)), across, False)
    x = [x[k * tile : (k + 1) * tile] for k in range(parts)]
    table = along_inner[...]
    y = [sum(dot(table, part) for part in split(middle[k][:, :width])) for k in (2, 3)]
    dropped = drops(x, *y)
    shown = opened[inner, :width]
    for k in range(parts):
        start = 0.5 * values[k][inner, :width] - (0.5 * time_step / 60.0) * dropped[k]
        value = shown * start + 0.5 * middle[k][inner, :width]
        if k == 0:
            density[0, 0] = value.astype(BF16)
        else:
            calm[k - 1] = value
    shown_open[0] = (time_step * opened).astype(BF16)
    mark[0] = place[0]


def tables_kernel(place, weights_x, weights_y, rise_x, rise_y, mark):
    mark[0] = place[0]
    _, tiles, reach_x, lanes = rise_x.shape
    wide, length_x = (tiles - 1) * lanes, weights_x.shape[1]
    first = place[0] * wide
    half = LANES // 2

    def weights(ref, start, size):
        length = ref.shape[1]
        start = jnp.where(start < 0, start + length, jnp.where(start >= length, start - length, start))
        return ref[:, pl.ds(pl.multiple_of(start, LANES), size)]

    cells = lax.broadcasted_iota(jnp.int32, (reach_x, lanes), 0)
    fine = lax.broadcasted_iota(jnp.int32, (reach_x, lanes), 1)
    right, left = weights(weights_x, first + wide, LANES), weights(weights_x, first - LANES, LANES)
    edge = jnp.where(lane_index(right.shape) < half, right, left)
    edge = jnp.concatenate([edge, edge], axis=1)
    for k in range(tiles):
        own = weights(weights_x, first + k * lanes, lanes) if k < tiles - 1 else edge
        target = fine // 2 - 1
        if k == tiles - 1:
            target = jnp.where(fine < half, target, target + half)
        value = jnp.zeros(fine.shape, F32)
        for t in range(4):
            value = jnp.where(cells == (target + t) % reach_x, own[t : t + 1, :], value)
        rise_x[0, k], rise_x[1, k] = split(value)
    steps, high, reach = rise_y.shape
    tall = steps * TILE
    first = place[1] * tall
    own = [weights(weights_y, first + k * LANES, LANES) for k in range(-1, tall // LANES + 1)]
    own = jnp.concatenate([jnp.concatenate(own, axis=1), jnp.zeros((4, tall + 2 * LANES), F32)], axis=0).T
    cells = lax.broadcasted_iota(jnp.int32, (high, reach), 1)
    last = cells >= reach // 3 * 2
    cells = cells % (reach // 3)
    target = lax.broadcasted_iota(jnp.int32, (high, reach), 0) // 2 + (HALO // 2 - 1)
    for k in range(steps):
        start = LANES - HALO + k * TILE
        value = jnp.zeros((high, reach), F32)
        for t in range(4):
            value = jnp.where(cells == target + t, own[start : start + high, t : t + 1], value)
        upper, lower = split(value)
        rise_y[k] = jnp.where(last, lower, upper)


def source_kernel(squares, opened, rise_x, rise_y, quiet, across, _, *refs):
    *lines, out, squared, cells_open, matrix, rows_matrix, calm, band, held, raised, forced, done, fetched, kept = refs
    steps = done.shape[0]
    tile, width = calm.shape[2:]
    high = tile + 2 * HALO
    rows = lines[0].shape[0]
    place = lax.axis_index("gx")

    def tile_copies(k):
        part = quiet.at[:, pl.ds(k * tile, tile), :]
        return (
            pltpu.make_async_copy(part, calm.at[k % 2], fetched.at[k % 2]),
            pltpu.make_async_copy(opened.at[k], cells_open.at[k % 2], fetched.at[2 + k % 2]),
        )

    def done_copy(k):
        part = out.at[1:, 0, pl.ds(k * tile, tile), :]
        return pltpu.make_async_copy(done.at[k], part, kept.at[k])

    arrays = ((squares, squared), (rise_x, matrix), (rise_y, rows_matrix), (across, band))
    copies = [
        pltpu.make_async_copy(source, target, fetched.at[4 + k])
        for k, (source, target) in enumerate(arrays)
    ]
    pieces = [
        pltpu.make_async_copy(
            piece,
            held.at[pl.ds(pl.multiple_of((place ^ mask) * rows, 8), rows), :],
            fetched.at[4 + len(arrays) + mask],
        )
        for mask, piece in enumerate(lines)
    ]
    for copy in (*pieces, *copies, *tile_copies(0), *tile_copies(1)):
        copy.start()
    for copy in pieces + copies[:1]:
        copy.wait()

    level = held[MARGIN - HALO : MARGIN - HALO + squared.shape[0], :] - squared[...]
    count = level.shape[1] // LANES
    near = lane_index((level.shape[0], LANES)) < 64
    around = []
    for k in range(count):
        after, before = lane_tile(level, (k + 1) % count), lane_tile(level, (k - 1) % count)
        around.append(split(jnp.concatenate([lane_tile(level, k), jnp.where(near, after, before)], axis=1)))
    copies[1].wait()
    for k in range(count):
        lanes = 2 * LANES if k < count - 1 else LANES
        value = split(exact_dot(around[k], [matrix[part, k, :, :lanes] for part in range(2)]))
        for part in range(2):
            raised[part, :, 2 * k * LANES : 2 * k * LANES + lanes] = value[part]
    for copy in copies[2:]:
        copy.wait()

    reach = rows_matrix.shape[2] // 3
    for k in range(steps):
        start = k * (tile // 2)
        window = [raised[part, start : start + reach, :] for part in (0, 1, 0)]
        calm_here, open_here = tile_copies(k)
        open_here.wait()
        free = cells_open[k % 2].astype(F32)
        value = free * dot(rows_matrix[k], jnp.concatenate(window, axis=0))
        forced[k % 2] = value
        inner = value[HALO : HALO + tile]
        shown = (0.5 / 60.0) * free[HALO : HALO + tile, :width]
        x = shown * slopes_x(split(inner), band, False)
        y = shown * slope_y(lambda d: forced[k % 2, HALO + d : HALO + d + tile, :width])
        calm_here.wait()
        still = calm.at[k % 2]
        done[k, 0] = (still[0] - x).astype(BF16)
        done[k, 1] = (still[1] - y).astype(BF16)
        done[k, 2] = (still[2] + inner[:, :width] - mean_flow * x).astype(BF16)
        done_copy(k).start()
        if k + 2 < steps:
            for copy in tile_copies(k + 2):
                copy.start()
    for k in range(steps):
        done_copy(k).wait()


def call(
    kernel, operands, outs, scratch=(), steps=0, specs=None, out_specs=None, after=(), aliases=None, megabytes=24, flops=0, moved=0, name=None
):
    count = len(operands)

    def body(*refs):
        kernel(*refs[:count], *refs[count + len(after) :])

    def whole(array):
        zeros = (0,) * len(array.shape)
        return pl.BlockSpec(array.shape, lambda *_: zeros)

    arguments = {}
    chosen = specs or {}
    if steps:
        arguments["grid"] = (steps,)
        in_specs = [chosen.get(i, whole(o)) for i, o in enumerate(operands)]
        arguments["out_specs"] = jax.tree.map(whole, outs) if out_specs is None else out_specs
    else:
        local = pl.BlockSpec(memory_space=pltpu.VMEM)
        in_specs = [chosen.get(i, local) for i in range(count)]
        if out_specs is not None:
            arguments["out_specs"] = out_specs
    return pl.pallas_call(
        body,
        out_shape=outs,
        in_specs=in_specs + [pl.BlockSpec(memory_space=pl.ANY)] * len(after),
        scratch_shapes=list(scratch),
        input_output_aliases=aliases or {},
        compiler_params=pltpu.CompilerParams(vmem_limit_bytes=megabytes << 20),
        cost_estimate=pl.CostEstimate(flops=flops, bytes_accessed=moved, transcendentals=0),
        name=name,
        **arguments,
    )(*operands, *after)


def ring(array, axis, step):
    size = lax.axis_size(axis)
    return lax.ppermute(array, axis, [(i, (i + step) % size) for i in range(size)])


def swap(array, axis, mask):
    return lax.ppermute(array, axis, [(i, i ^ mask) for i in range(lax.axis_size(axis))])


def shaped(*shape, kind=F32):
    return jax.ShapeDtypeStruct(shape, kind)


def pressure_lines(pieces, gathered, spread, stepped):
    _, rows, local_x = pieces[0].shape
    count_x, count_y = lax.axis_size("gx"), lax.axis_size("gy")
    count = count_x * count_y
    length_x, length_y = local_x * count_x, rows * count
    full, zero, middle, cos_turn, sin_turn = x_tables(length_x)
    turns = np.zeros((8, cos_turn.shape[1]), np.float32)
    turns[0:3], turns[3:6] = cos_turn, sin_turn
    spectra, total = call(
        forward_x_kernel,
        (*pieces, np.concatenate([beside(full), beside(zero, middle)]), turns),
        (shaped(count, rows, LANES), shaped(8, LANES)),
        (
            pltpu.VMEM((count_x, 2, rows, local_x), F32),
            pltpu.VMEM((count, rows, LANES), F32),
            pltpu.SemaphoreType.DMA((5,)),
        ),
        out_specs=(pl.BlockSpec(memory_space=pl.ANY), pl.BlockSpec(memory_space=pltpu.VMEM)),
        after=gathered,
        flops=10**9,
        moved=4 << 20,
        name="forward_x",
    )
    spectra = lax.all_to_all(spectra, ("gy", "gx"), 0, 0, tiled=True)
    place = lax.axis_index("gy") * count_x + spread[0]
    waves = jnp.asarray(wave_table(length_x, count))
    wave = lax.dynamic_slice(waves, (place, 0), (1, LANES))
    both, turns_y = y_tables(length_y)
    kept = rows + 2 * MARGIN // count_x
    half = (kept // 2 + 8) // 8 * 8
    solved = call(
        functools.partial(solve_y_kernel, count_x),
        (spectra, total, wave, beside(both), turns_y),
        shaped(count, half, LANES),
        (
            pltpu.VMEM((length_y + 2 * MARGIN, LANES), F32),
            pltpu.VMEM((length_y // RADIX, 2 * RADIX * LANES), F32),
            pltpu.VMEM((count, half, LANES), F32),
            pltpu.SemaphoreType.DMA((count // RADIX,)),
        ),
        out_specs=pl.BlockSpec(memory_space=pl.ANY),
        flops=4 * 10**9,
        moved=6 << 20,
        name="solve_y",
    )
    solved = lax.all_to_all(solved, ("gy", "gx"), 0, 0, tiled=True)
    back = 2.0 * zero.T
    back[LANES // 2] *= 0.5
    tables = np.concatenate(
        [beside(full.T), beside(back, 2.0 * middle.T)]
    )
    again = jnp.asarray(np.tile(turns, (count_x, 1, 1)))
    again = lax.dynamic_slice(again, (stepped[0], 0, 0), (1,) + turns.shape)
    pressed = call(
        functools.partial(inverse_x_kernel, kept, 1.0 / (length_x * length_y)),
        (solved, tables, again[0]),
        (shaped(kept, local_x + LANES),) * count_x,
        (pltpu.VMEM((kept, length_x), F32),),
        flops=10**9,
        moved=4 << 20,
        name="inverse_x",
    )
    return [piece if mask == 0 else swap(piece, "gx", mask) for mask, piece in enumerate(pressed)]


def fast_shards(velocity, weights_x, weights_y, acoustic, wall_mask):
    parts, _, tall, wide = acoustic.shape
    _, _, local_y, local_x = velocity.shape
    count_x, count_y = lax.axis_size("gx"), lax.axis_size("gy")
    place_x, place_y = lax.axis_index("gx"), lax.axis_index("gy")
    full, high, steps = wide + LANES, TILE + 2 * HALO, tall // TILE
    strips = (parts + 2) * HALO
    small = 2 * HALO
    has = jnp.stack([place_x > 0, place_x < count_x - 1, place_y > 0, place_y < count_y - 1])
    has = has.astype(F32)
    scalars = pl.BlockSpec(memory_space=pltpu.SMEM)

    def at(block, *index):
        return pl.BlockSpec(block, lambda i: index)

    own = place_x.astype(jnp.int32).reshape(1)
    sent = call(
        pieces_kernel,
        (velocity,),
        (shaped(2, local_y // count_x, local_x),) * count_x,
        moved=2 << 20,
        megabytes=8,
        name="pieces",
    )
    moved = [piece if mask == 0 else swap(piece, "gx", mask) for mask, piece in enumerate(sent)]
    first, last = call(
        rows_kernel,
        (acoustic, acoustic, wall_mask, wall_mask, velocity, velocity),
        (shaped(STRIP_ROWS, wide),) * 2,
        steps=1,
        specs={
            0: at((parts, 1, small, wide), 0, 0, 0, 0),
            1: at((parts, 1, small, wide), 0, 0, tall // small - 1, 0),
            2: at((1, HALO, wide), 0, 0, 0),
            3: at((1, HALO, wide), 0, tall // HALO - 1, 0),
            4: at((1, 1, HALO, local_x), 1, 0, 0, 0),
            5: at((1, 1, HALO, local_x), 1, 0, local_y // HALO - 1, 0),
        },
        after=moved[1:2],
        moved=2 << 20,
        megabytes=50,
        name="rows",
    )
    above, below = ring(last, "gy", 1), ring(first, "gy", -1)
    to_right, to_left = call(
        columns_kernel,
        (has, acoustic, acoustic, wall_mask, wall_mask, velocity, velocity, above, below),
        (shaped(strips, tall + LANES), shaped(strips, tall + LANES)),
        steps=1,
        specs={
            0: scalars,
            1: at((parts, 1, tall, LANES), 0, 0, 0, 0),
            2: at((parts, 1, tall, LANES), 0, 0, 0, wide // LANES - 1),
            3: at((1, tall, LANES), 0, 0, 0),
            4: at((1, tall, LANES), 0, 0, wide // LANES - 1),
            5: at((1, 1, local_y, LANES), 1, 0, 0, 0),
            6: at((1, 1, local_y, LANES), 1, 0, 0, local_x // LANES - 1),
        },
        moved=8 << 20,
        megabytes=54,
        name="columns",
    )
    from_left, from_right = ring(to_right, "gx", 1), ring(to_left, "gx", -1)
    local_memory = pl.BlockSpec(memory_space=pltpu.VMEM)
    tiles = wide // (2 * LANES) + 1
    rise_x, rise_y, listed = call(
        tables_kernel,
        (jnp.stack([place_x, place_y]).astype(jnp.int32), weights_x, weights_y),
        (
            shaped(2, tiles, 2 * LANES, 2 * LANES, kind=BF16),
            shaped(steps, high, 3 * (high // 2 + HALO), kind=BF16),
            shaped(1, kind=jnp.int32),
        ),
        specs={0: scalars},
        out_specs=(local_memory, local_memory, scalars),
        moved=4 << 20,
        megabytes=54,
        name="tables",
    )
    sides, squares, beside = call(
        sides_kernel,
        (has, listed, velocity, above, below, from_left, from_right),
        (
            shaped(parts + 1, tall + LANES, LANES),
            shaped(local_y + 2 * HALO, local_x + LANES),
            shaped(1, kind=jnp.int32),
        ),
        steps=1,
        specs={0: scalars, 1: scalars, 2: at((1, 1, local_y, local_x), 1, 0, 0, 0)},
        out_specs=(
            at((parts + 1, tall + LANES, LANES), 0, 0, 0),
            at((local_y + 2 * HALO, local_x + LANES), 0, 0),
            scalars,
        ),
        moved=8 << 20,
        megabytes=54,
        name="sides",
    )
    across, along = band_tables(high)
    along_inner = along[HALO : HALO + TILE]
    per, rows = TILE // small, TILE // HALO

    def tiled(first):
        walls = (
            pl.BlockSpec((1, TILE, wide), lambda i: (0, i + first, 0)),
            pl.BlockSpec((1, HALO, wide), lambda i: (0, jnp.maximum((i + first) * rows - 1, 0), 0)),
            pl.BlockSpec(
                (1, HALO, wide),
                lambda i: (0, jnp.minimum((i + first + 1) * rows, steps * rows - 1), 0),
            ),
        )
        cells = (
            pl.BlockSpec((parts, 1, TILE, wide), lambda i: (0, 0, i + first, 0)),
            pl.BlockSpec(
                (parts, 1, small, wide), lambda i: (0, 0, jnp.maximum((i + first) * per - 1, 0), 0)
            ),
            pl.BlockSpec(
                (parts, 1, small, wide),
                lambda i: (0, 0, jnp.minimum((i + first + 1) * per, steps * per - 1), 0),
            ),
        )
        return cells, walls

    def quiet_tiles(first, count, before):
        cells, walls = tiled(first)
        operands = (has, own, acoustic, acoustic, acoustic, wall_mask, wall_mask, wall_mask, above, below, sides)
        operands = operands + (across, along, along_inner)
        return call(
            functools.partial(quiet_step_kernel, first),
            operands,
            (
                shaped(parts - 1, tall, wide),
                shaped(*acoustic.shape, kind=BF16),
                shaped(steps, high, full, kind=BF16),
                shaped(1, kind=jnp.int32),
            ),
            steps=count,
            specs=dict(enumerate((scalars, scalars) + cells + walls)),
            out_specs=(
                pl.BlockSpec((parts - 1, TILE, wide), lambda i: (0, i + first, 0)),
                pl.BlockSpec((1, 1, TILE, wide), lambda i: (0, 0, i + first, 0)),
                pl.BlockSpec((1, high, full), lambda i: (i + first, 0, 0)),
                scalars,
            ),
            after=before,
            aliases={len(operands) + k: k for k in range(len(before))},
            megabytes=54,
            flops=3 * 10**9 * count,
            moved=(12 << 20) * count,
            name="quiet_step",
        )

    early = max(steps * 3 // 4, 1)
    *begun, stepped = quiet_tiles(0, early, ())
    if early < steps:
        *begun, _ = quiet_tiles(early, steps - early, begun)
    quiet, final, opened = begun
    lines = pressure_lines(moved, (above, below), beside, stepped)
    operands = (squares, opened, rise_x, rise_y, quiet, across, final, *lines)
    anywhere = pl.BlockSpec(memory_space=pl.ANY)
    specs = {k: anywhere for k in range(len(operands))}
    scratch = (
        pltpu.VMEM(squares.shape, F32),
        pltpu.VMEM((2,) + opened.shape[1:], BF16),
        pltpu.VMEM(rise_x.shape, BF16),
        pltpu.VMEM(rise_y.shape, BF16),
        pltpu.VMEM((2, parts - 1, TILE, wide), F32),
        pltpu.VMEM(across.shape, BF16),
        pltpu.VMEM((local_y + 2 * MARGIN, local_x + LANES), F32),
        pltpu.VMEM((2, local_y + 2 * HALO, full), BF16),
        pltpu.VMEM((2, high, full), F32),
        pltpu.VMEM((steps, parts - 1, TILE, wide), BF16),
        pltpu.SemaphoreType.DMA((8 + count_x,)),
        pltpu.SemaphoreType.DMA((steps,)),
    )
    return call(
        source_kernel,
        operands,
        shaped(*acoustic.shape, kind=BF16),
        scratch,
        specs=specs,
        out_specs=anywhere,
        aliases={6: 0},
        megabytes=56,
        flops=4 * 10**9,
        moved=16 << 20,
        name="source_step",
    )


def fits(count_x, count_y, velocity, acoustic):
    _, planes, local_y, local_x = velocity
    _, _, tall, wide = acoustic
    length_x, length_y = local_x * count_x, local_y * count_y
    rows = local_y // count_x
    base_x, base_y = length_x // RADIX, length_y // RADIX
    return (
        planes == 1
        and acoustic[0] == PARTS
        and length_x * 2 == count_x * count_y * LANES
        and base_x % (2 * LANES) == 0
        and local_x % base_x == 0
        and rows % 8 == 0
        and base_y % rows == 0
        and base_y % 8 == 0
        and count_x * count_y % RADIX == 0
        and MARGIN * 2 % (8 * count_x) == 0
        and tall == 2 * local_y
        and wide == 2 * local_x
        and tall % TILE == 0
        and tall % LANES == 0
        and tall >= 2 * TILE
        and count_x & (count_x - 1) == 0
        and wide % (2 * LANES) == 0
    )


def extended(array, sides, width):
    for axis, dim in sides:
        size, length = (lax.axis_size(axis), array.shape[dim])
        up = [(i, (i + 1) % size) for i in range(size - 1)]
        down = [(j, i) for i, j in up]
        last = lax.slice_in_dim(array, length - width, length, axis=dim)
        leading = lax.slice_in_dim(array, 0, width, axis=dim)
        before = lax.ppermute(last, axis, up)
        after = lax.ppermute(leading, axis, down)
        array = jnp.concatenate([before, array, after], axis=dim)
    return array


def gradients(padded):
    height = padded.shape[-2] - 6
    breadth = padded.shape[-1] - 6
    rows_mid = padded[..., 3 : 3 + height, :]
    cols_mid = padded[..., :, 3 : 3 + breadth]
    along_x = jnp.zeros_like(padded[..., 3 : 3 + height, 3 : 3 + breadth])
    along_y = jnp.zeros_like(along_x)
    for index, weight in enumerate(stencil_weights):
        distance = index + 1
        along_x = along_x + weight * (
            rows_mid[..., 3 + distance : 3 + distance + breadth]
            - rows_mid[..., 3 - distance : 3 - distance + breadth]
        )
        along_y = along_y + weight * (
            cols_mid[..., 3 + distance : 3 + distance + height, :]
            - cols_mid[..., 3 - distance : 3 - distance + height, :]
        )
    return (along_x, along_y)


def tendency(padded, source):
    along_x, along_y = gradients(padded)
    diverge = along_x[1] + along_y[2]
    forcing = jnp.stack([-diverge, -along_x[3], -along_y[3], source - diverge])
    return forcing - mean_flow * along_x


def spectral_index(flat, length):
    second = length // 16
    wave = flat // second + 16 * (flat % second)
    return jnp.where(wave < length // 2, wave, wave - length).astype(jnp.float32)


def twiddles(rows_count, cols_count, modulus, sign):
    products = jnp.arange(rows_count)[:, None] * jnp.arange(cols_count)[None, :] % modulus
    angles = 2.0 * math.pi / modulus * products.astype(jnp.float32)
    return (jnp.cos(angles), sign * jnp.sin(angles))


def mix_rows(real_part, imag_part, cosine, sine):
    exact = lax.Precision.HIGHEST
    cos_real = jnp.einsum("ka,...ab->...kb", cosine, real_part, precision=exact)
    cos_imag = jnp.einsum("ka,...ab->...kb", cosine, imag_part, precision=exact)
    sin_real = jnp.einsum("ka,...ab->...kb", sine, real_part, precision=exact)
    sin_imag = jnp.einsum("ka,...ab->...kb", sine, imag_part, precision=exact)
    return (cos_real - sin_imag, cos_imag + sin_real)


def mix_cols(real_part, imag_part, cosine, sine):
    exact = lax.Precision.HIGHEST
    cos_real = jnp.einsum("...kb,bc->...kc", real_part, cosine, precision=exact)
    cos_imag = jnp.einsum("...kb,bc->...kc", imag_part, cosine, precision=exact)
    sin_real = jnp.einsum("...kb,bc->...kc", real_part, sine, precision=exact)
    sin_imag = jnp.einsum("...kb,bc->...kc", imag_part, sine, precision=exact)
    return (cos_real - sin_imag, cos_imag + sin_real)


def rotate(real_part, imag_part, cosine, sine):
    return (real_part * cosine - imag_part * sine, real_part * sine + imag_part * cosine)


def discrete(real_part, imag_part, sign):
    length = real_part.shape[-1]
    second = length // 16
    initial = real_part.shape
    folded = initial[:-1] + (16, second)
    real_part = real_part.reshape(folded)
    imag_part = imag_part.reshape(folded)
    small_cos, small_sin = twiddles(16, 16, 16, sign)
    large_cos, large_sin = twiddles(second, second, second, sign)
    turn_cos, turn_sin = twiddles(16, second, length, sign)
    if sign < 0:
        real_part, imag_part = mix_rows(real_part, imag_part, small_cos, small_sin)
        real_part, imag_part = rotate(real_part, imag_part, turn_cos, turn_sin)
        real_part, imag_part = mix_cols(real_part, imag_part, large_cos, large_sin)
    else:
        real_part, imag_part = mix_cols(real_part, imag_part, large_cos, large_sin)
        real_part, imag_part = rotate(real_part, imag_part, turn_cos, turn_sin)
        real_part, imag_part = mix_rows(real_part, imag_part, small_cos, small_sin)
        real_part = real_part / length
        imag_part = imag_part / length
    return (real_part.reshape(initial), imag_part.reshape(initial))


def transform(stacked, sign, kind):
    if kind == "real_in":
        real_part = stacked
        imag_part = jnp.zeros_like(stacked)
    else:
        half = stacked.shape[0] // 2
        real_part = stacked[:half]
        imag_part = stacked[half:]
    real_out, imag_out = discrete(real_part, imag_part, sign)
    if kind == "real_out":
        return real_out
    return jnp.concatenate([real_out, imag_out], axis=0)


def project(stacked, wave_x, wave_y):
    coef_xx = wave_x * wave_x
    coef_xy = 2.0 * wave_x * wave_y
    coef_yy = wave_y * wave_y
    denominator = wave_x * wave_x + wave_y * wave_y
    positive = denominator > 0
    safe = jnp.where(positive, denominator, 1.0)

    def combine(parts):
        numerator = -(coef_xx * parts[0] + coef_xy * parts[1] + coef_yy * parts[2])
        return jnp.where(positive, numerator / safe, 0.0)

    return jnp.stack([combine(stacked[:3]), combine(stacked[3:])])


def refine(stacked, weights):
    result = jnp.zeros(stacked.shape[:-1] + (2 * stacked.shape[-1],), jnp.float32)
    for offset in range(4):
        result = (
            result
            + jnp.repeat(jnp.roll(stacked, 1 - offset, axis=-1), 2, axis=-1) * weights[offset]
        )
    return result


def lines_x(stacked, action):
    gathered = action(lax.all_to_all(stacked, "gx", split_axis=2, concat_axis=3, tiled=True))
    return lax.all_to_all(gathered, "gx", split_axis=3, concat_axis=2, tiled=True)


def lines_y(stacked, action):
    turned = jnp.swapaxes(stacked, 2, 3)
    gathered = action(lax.all_to_all(turned, "gy", split_axis=2, concat_axis=3, tiled=True))
    returned = lax.all_to_all(gathered, "gy", split_axis=3, concat_axis=2, tiled=True)
    return jnp.swapaxes(returned, 2, 3)


def expand(fields):
    return extended(fields, (("gx", 3), ("gy", 2)), 3)


def shards(velocity, weights_x, weights_y, acoustic, wall_mask):
    acoustic = acoustic.astype(jnp.float32)
    flow_x = velocity[0]
    flow_y = velocity[1]
    tensor = jnp.stack([flow_x * flow_x, flow_x * flow_y, flow_y * flow_y])
    count_gx = lax.axis_size("gx")
    count_gy = lax.axis_size("gy")
    place_x = lax.axis_index("gx")
    place_y = lax.axis_index("gy")
    local_y = tensor.shape[2]
    local_x = tensor.shape[3]
    length_x = local_x * count_gx
    length_y = local_y * count_gy

    def forward_real(portion):
        return transform(portion, -1, "real_in")

    def finish_x(portion):
        return refine(transform(portion, 1, "real_out"), weights_x)

    spectra = lines_x(tensor, forward_real)
    share_x = local_x // count_gy
    line_x = spectral_index(place_x * local_x + place_y * share_x + jnp.arange(share_x), length_x)[
        :, None
    ]
    line_y = spectral_index(jnp.arange(length_y), length_y)[None, :]

    def solve_y(portion):
        solved = project(transform(portion, -1, "complex"), line_x, line_y)
        return refine(transform(solved, 1, "complex"), weights_y)

    pressure = lines_y(spectra, solve_y)
    source = lines_x(pressure, finish_x)[0]
    open_cells = (1 - wall_mask).astype(jnp.float32)
    first_rate = tendency(expand(acoustic), source)
    middle = open_cells * (acoustic + time_step * first_rate)
    second_rate = tendency(expand(middle), source)
    return (open_cells * (acoustic + 0.5 * time_step * (first_rate + second_rate))).astype(
        jnp.bfloat16
    )


def solution(mesh):
    in_specs = (P(None, None, "gy", "gx"), P(), P(), P(None, None, "gy", "gx"), P(None, "gy", "gx"))
    out_specs = P(None, None, "gy", "gx")

    def chosen(velocity, weights_x, weights_y, acoustic, wall_mask):
        sizes = (mesh.shape["gx"], mesh.shape["gy"], velocity.shape, acoustic.shape)
        plan = fast_shards if fits(*sizes) else shards
        return plan(velocity, weights_x, weights_y, acoustic, wall_mask)

    return jax.shard_map(
        chosen, mesh=mesh, in_specs=in_specs, out_specs=out_specs, check_vma=False
    )
```

```python
import functools
import math

import jax
import jax.numpy as jnp
import ml_dtypes
import numpy as np
from jax import lax
from jax.experimental import pallas as pl
from jax.experimental.pallas import tpu as pltpu
from jax.sharding import PartitionSpec as P

stencil_weights = (0.75, -0.15, 1.0 / 60.0)
mean_flow = 0.3
time_step = 0.5
whole_weights = (45.0, -9.0, 1.0)

LANES = 128
RADIX = 8
HALO = 8
MARGIN = 16
TILE = 128
ROOT = math.sqrt(0.5)
STRIP = {2: (0, 6), 3: (6, 6), 1: (12, 3), 4: (15, 3), 5: (20, 4)}
STRIP_ROWS = 24
PARTS = 4
BF16 = jnp.bfloat16
F32 = jnp.float32


def halves(table):
    high = table.astype(np.float32).astype(ml_dtypes.bfloat16)
    low = (table - high.astype(np.float64)).astype(np.float32).astype(ml_dtypes.bfloat16)
    return high, low


def packed_columns(cosine, sine):
    half = LANES // 2
    parts = []
    for first in range(0, cosine.shape[1], half):
        parts += [cosine[:, first : first + half], sine[:, first : first + half]]
    return np.concatenate(parts, axis=1)


@functools.lru_cache(maxsize=None)
def x_tables(length):
    base = length // RADIX
    m = np.arange(base)[:, None]
    q = np.arange(base)[None, :]
    angle = 2.0 * np.pi * ((m * q) % base) / base
    cosine, sine = np.cos(angle), np.sin(angle)
    full = np.concatenate([packed_columns(cosine, -sine), packed_columns(sine, cosine)], axis=0)
    half = base // 2
    zero_cos, zero_sin = cosine[:, :half].copy(), -sine[:, :half]
    zero_cos[:, 0] = 0.0
    zero_sin = zero_sin.copy()
    zero_sin[:, 0] = (-1.0) ** np.arange(base)
    zero = packed_columns(zero_cos, zero_sin)
    shifted = 2.0 * np.pi * ((m * (RADIX * q[:, :half] + RADIX // 2)) % length) / length
    middle = packed_columns(np.cos(shifted), -np.sin(shifted))
    turns = 2.0 * np.pi * np.arange(1, RADIX // 2)[:, None] * np.arange(base)[None, :] / length
    return full, zero, middle, np.cos(turns), np.sin(turns)


@functools.lru_cache(maxsize=None)
def y_tables(length):
    base = length // RADIX
    index = np.arange(base)
    angle = 2.0 * np.pi * ((index[:, None] * index[None, :]) % base) / base
    both = np.concatenate([np.cos(angle), np.sin(angle)], axis=0)
    turns = 2.0 * np.pi * np.arange(RADIX)[:, None] * index[None, :] / length
    turns = np.concatenate([np.cos(turns), np.sin(turns)], axis=0).T
    high, rest = halves(turns)
    low = turns - high.astype(np.float64) - rest.astype(np.float64)
    return both, np.concatenate([high, rest, low.astype(ml_dtypes.bfloat16)], axis=1)


@functools.lru_cache(maxsize=None)
def wave_table(length, count):
    slots = LANES // 4
    base = length // RADIX
    waves = []
    for residue in (1, 2, 3):
        waves.append(RADIX * np.arange(base) + residue)
    waves.append(RADIX * np.arange(base // 2))
    waves.append(RADIX * np.arange(base // 2) + RADIX // 2)
    waves = np.concatenate(waves)
    waves = np.where(waves == 0, length // 2, waves)
    waves = np.where(waves < length // 2, waves, waves - length).reshape(count, slots)
    return np.tile(waves, (1, 4)).astype(np.float32)


@functools.lru_cache(maxsize=None)
def band_tables(rows):
    across = np.zeros((4 * LANES, 2 * LANES))
    column = np.arange(2 * LANES)
    down = np.zeros((rows, rows))
    for index, weight in enumerate(whole_weights):
        distance = index + 1
        across[column + LANES + distance, column] = weight
        across[column + LANES - distance, column] = -weight
        down += weight * (np.eye(rows, k=distance) - np.eye(rows, k=-distance))
    return across.astype(ml_dtypes.bfloat16), down.astype(ml_dtypes.bfloat16)


def beside(*tables):
    high, low = halves(np.concatenate(tables, axis=1))
    return np.concatenate([high, low], axis=0)


def split(values):
    high = values.astype(BF16)
    return high, (values - high.astype(F32)).astype(BF16)


def dot(left, right):
    return jnp.dot(left, right, preferred_element_type=F32)


def exact_dot(left, right):
    left_high, left_low = left
    right_high, right_low = right
    return dot(left_high, right_high) + (dot(left_low, right_high) + dot(left_high, right_low))


def lane_index(shape):
    return lax.broadcasted_iota(jnp.int32, shape, len(shape) - 1)


def spin(values, shift):
    return pltpu.roll(values, shift % values.shape[-1], values.ndim - 1)


def lane_tile(values, index):
    return values[:, index * LANES : (index + 1) * LANES]


def x_parts(tables, base):
    wide = 2 * base
    full = (tables[:wide], tables[wide : 2 * wide])
    at = 2 * wide
    high, low = tables[at : at + base], tables[at + base : at + 2 * base]
    return full, (high[:, :base], low[:, :base]), (high[:, base:], low[:, base:])


def pieces_kernel(velocity, *pieces):
    rows = pieces[0].shape[1]
    place = lax.axis_index("gx")
    for mask, piece in enumerate(pieces):
        start = pl.multiple_of((place ^ mask) * rows, 8)
        for c in range(2):
            piece[c] = velocity[c, 0, pl.ds(start, rows), :]


def rows_kernel(top, low, top_wall, low_wall, top_flow, low_flow, first, last):
    small, width = top.shape[2], top_flow.shape[3]
    first[...] = jnp.zeros(first.shape, F32)
    last[...] = jnp.zeros(last.shape, F32)
    for k, (start, rows) in STRIP.items():
        lanes = slice(0, width) if k == PARTS + 1 else slice(None)
        if k < PARTS:
            upper, lower = top[k, 0].astype(F32)[:HALO], low[k, 0].astype(F32)[small - HALO :]
        elif k == PARTS:
            upper, lower = 1.0 - top_wall[0].astype(F32), 1.0 - low_wall[0].astype(F32)
        else:
            upper, lower = top_flow[0, 0], low_flow[0, 0]
        first[start : start + rows, lanes] = upper[:rows]
        last[start : start + rows, lanes] = lower[HALO - rows :]


def strip(ref, k, upper, lanes=slice(None)):
    if k not in STRIP:
        return jnp.zeros((HALO, ref[0:1, lanes].shape[1]), F32)
    start, rows = STRIP[k]
    values = ref[start : start + rows, lanes]
    blank = jnp.zeros((HALO - rows, values.shape[1]), F32)
    return jnp.concatenate([blank, values] if upper else [values, blank], axis=0)


def columns_kernel(
    has, left, right, left_wall, right_wall, left_flow, right_flow, above, below, to_right, to_left
):
    parts = left.shape[0]
    wide, flow_wide = above.shape[1], above.shape[1] // 2
    gap = jnp.zeros((LANES - 2 * HALO, LANES), F32)

    def tall(k, inner, first, sides):
        lanes = slice(first, first + LANES)
        over, under = strip(above, k, True, lanes), strip(below, k, False, lanes)
        return jnp.concatenate([inner, under * sides[1], gap, over * sides[0]], axis=0).T

    for k in range(parts + 1):
        at = slice(k * HALO, (k + 1) * HALO)
        if k < parts:
            near, far = left[k, 0].astype(F32), right[k, 0].astype(F32)
        else:
            near, far = 1.0 - left_wall[0].astype(F32), 1.0 - right_wall[0].astype(F32)
        sides = (has[2], has[3])
        to_left[at, :] = tall(k, near, 0, sides)[:HALO]
        to_right[at, :] = tall(k, far, wide - LANES, sides)[LANES - HALO :]
    k = parts + 1
    at = slice(k * HALO, (k + 1) * HALO)
    size = left_flow.shape[2] + LANES
    blank = jnp.zeros((HALO, to_left.shape[1] - size), F32)
    to_left[at, :size] = tall(k, left_flow[0, 0], 0, (1.0, 1.0))[:HALO]
    to_right[at, :size] = tall(k, right_flow[0, 0], flow_wide - LANES, (1.0, 1.0))[LANES - HALO :]
    to_left[at, size:] = blank
    to_right[at, size:] = blank


def sides_kernel(has, place, velocity, above, below, from_left, from_right, sides, squares, mark):
    parts, tall, _ = sides.shape
    gap = jnp.zeros((LANES - 2 * HALO, tall), F32)
    for k in range(parts):
        at = slice(k * HALO, (k + 1) * HALO)
        tile = [from_right[at, :] * has[1], gap, from_left[at, :] * has[0]]
        sides[k] = jnp.concatenate(tile, axis=0).T
    at = slice(parts * HALO, (parts + 1) * HALO)
    rows, local = velocity.shape[2:]
    size = rows + LANES
    tile = [from_right[at, :size], gap[:, :size], from_left[at, :size]]
    tile = jnp.concatenate(tile, axis=0).T
    tile = tile * tile
    mark[0] = place[0]
    over, under = (strip(ref, parts, ref is above, slice(0, local)) for ref in (above, below))
    squares[:HALO, :local] = over * over
    squares[HALO : HALO + rows, :local] = velocity[0, 0] * velocity[0, 0]
    squares[HALO + rows :, :local] = under * under
    squares[:HALO, local:] = tile[size - HALO :]
    squares[HALO : HALO + rows, local:] = tile[:rows]
    squares[HALO + rows :, local:] = tile[rows : rows + HALO]


def forward_x_kernel(*refs):
    *pieces, tables, turns, out, total, lines, made, sent = refs
    count, _, rows, local = lines.shape
    place = lax.axis_index("gx")
    for mask, piece in enumerate(pieces):
        lines[place ^ mask] = piece[...]
    base = turns.shape[1]
    per = local // base
    u = [lines[t // per, 0, :, (t % per) * base : (t % per + 1) * base] for t in range(RADIX)]
    v = [lines[t // per, 1, :, (t % per) * base : (t % per + 1) * base] for t in range(RADIX)]
    energy = sum(b * b for b in v)
    energy = jnp.sum(energy.reshape(rows // 8, 8, base), axis=0)
    total[...] = sum(energy[:, k : k + LANES] for k in range(0, base, LANES))
    fields = ([a * a - b * b for a, b in zip(u, v)], [2.0 * a * b for a, b in zip(u, v)])
    zeros, mids, reals, imags = [], [], [[], [], []], [[], [], []]
    for a in fields:
        s04, s26, s15, s37 = a[0] + a[4], a[2] + a[6], a[1] + a[5], a[3] + a[7]
        d04, d26, d15, d37 = a[0] - a[4], a[2] - a[6], a[1] - a[5], a[3] - a[7]
        zeros.append((s04 + s26) + (s15 + s37))
        mids.append((s04 + s26) - (s15 + s37))
        minus, plus = ROOT * (d15 - d37), ROOT * (d15 + d37)
        turned = (
            (d04 + minus, -d26 - plus),
            (s04 - s26, s37 - s15),
            (d04 - minus, d26 - plus),
        )
        for index, (real, imag) in enumerate(turned):
            c, s = turns[index : index + 1, :], turns[index + 3 : index + 4, :]
            reals[index].append(real * c + imag * s)
            imags[index].append(imag * c - real * s)
    stacked = jnp.concatenate(
        [
            jnp.concatenate([jnp.concatenate(reals[i], axis=0) for i in range(3)], axis=0),
            jnp.concatenate([jnp.concatenate(imags[i], axis=0) for i in range(3)], axis=0),
        ],
        axis=1,
    )
    full, zero, middle = x_parts(tables, base)
    full = exact_dot(split(stacked), full)
    zero = exact_dot(split(jnp.concatenate(zeros, axis=0)), zero)
    middle = exact_dot(split(jnp.concatenate(mids, axis=0)), middle)
    low = lane_index((rows, LANES)) % 64 < 32
    target, copies = 0, []
    blocks = [full[2 * rows * i : 2 * rows * (i + 1)] for i in range(3)] + [zero, middle]
    for block in blocks:
        start = target
        for first in range(0, block.shape[1], LANES):
            a = block[:rows, first : first + LANES]
            c = block[rows:, first : first + LANES]
            made[target] = jnp.where(low, a, spin(c, 32))
            made[target + 1] = jnp.where(low, spin(a, -32), c)
            target += 2
        group = pl.ds(start, target - start)
        copies.append(pltpu.make_async_copy(made.at[group], out.at[group], sent.at[len(copies)]))
        copies[-1].start()
    for copy in copies:
        copy.wait()


def eighths(x, turn):
    s04, s26, s15, s37 = x[0] + x[4], x[2] + x[6], x[1] + x[5], x[3] + x[7]
    d04, d26, d15, d37 = x[0] - x[4], x[2] - x[6], x[1] - x[5], x[3] - x[7]
    quarter = turn(s15 - s37)
    spun_26, spun_37 = turn(d26), turn(d37)
    one, three = d15 + spun_37, d15 - spun_37
    spun_one, spun_three = turn(one), turn(three)
    one = ROOT * (one + spun_one)
    three = ROOT * (spun_three - three)
    return [
        (s04 + s26) + (s15 + s37),
        (d04 + spun_26) + one,
        (s04 - s26) + quarter,
        (d04 - spun_26) + three,
        (s04 + s26) - (s15 + s37),
        (d04 + spun_26) - one,
        (s04 - s26) - quarter,
        (d04 - spun_26) - three,
    ]


def solve_y_kernel(count_x, lines, total, wave, both, turns, out, held, spread, made, sent):
    count, rows, _ = lines.shape
    base = turns.shape[0]
    length = count * rows
    block = count_x * rows
    per = base // rows
    lanes = lane_index((base, LANES))
    sign = jnp.where(lanes < 64, 1.0, -1.0).astype(F32)

    def minus_i(z):
        return spin(z, 64) * sign

    def plus_i(z):
        return spin(z, 64) * -sign

    fields = [
        jnp.concatenate([lines[t * per + k] for k in range(per)], axis=0) for t in range(RADIX)
    ]
    mixed = eighths(fields, minus_i)
    terms, columns = turns.shape[1], 2 * RADIX
    picked = lax.broadcasted_iota(jnp.int32, (terms, columns * LANES), 0) % columns
    lane = lane_index(picked.shape)
    value = jnp.where((lane >= RADIX * LANES) & (lane % LANES >= 64), -1.0, 1.0)
    spread[...] = dot(turns[...], jnp.where(picked == lane // LANES, value, 0.0).astype(BF16))
    cosines = [spread[:, r * LANES : (r + 1) * LANES] for r in range(RADIX)]
    sines = [spread[:, (r + RADIX) * LANES : (r + RADIX + 1) * LANES] for r in range(RADIX)]
    mixed = [mixed[0]] + [
        mixed[r] * cosines[r] + spin(mixed[r], 64) * sines[r] for r in range(1, RADIX)
    ]
    tables = (both[: 2 * base], both[2 * base :])
    product = exact_dot(tables, split(jnp.concatenate(mixed, axis=1)))
    kx = wave[0:1, :]
    first = lanes % 64 < 32
    edge = jnp.float32(length // 2)
    square_kx = kx * kx
    alone = jnp.where(first, square_kx, 0.0)
    slope = jnp.where(first | (kx == -edge), 0.0, jnp.broadcast_to(kx, lanes.shape))
    q = lax.broadcasted_iota(jnp.int32, lanes.shape, 0)
    low_ky = RADIX * (q - jnp.where(q < base // 2, 0, base)).astype(F32)
    terms = []
    for r in range(RADIX):
        at = slice(r * LANES, (r + 1) * LANES)
        spectrum = product[:base, at] + minus_i(product[base:, at])
        ky = low_ky + float(r)
        symbol = alone + slope * ky
        if r == 0:
            corner = jnp.where((kx == -edge) & ~first, edge * edge, 0.0)
            symbol = jnp.where(ky == -edge, jnp.where(first, alone, corner), symbol)
        square = square_kx + ky * ky
        guess = pl.reciprocal(square, approx=True)
        terms.append(symbol * (guess * (2.0 - square * guess)) * spectrum)
    pairs = [
        jnp.where(first, low + spin(low, -32), high + spin(high, 32))
        for low, high in zip(terms[:4], terms[4:])
    ]
    product = exact_dot(tables, split(jnp.concatenate(pairs, axis=1)))
    mixed = []
    for r in range(RADIX // 2):
        at = slice(r * LANES, (r + 1) * LANES)
        value = product[:base, at] + plus_i(product[base:, at])
        cosine = jnp.where(first, cosines[r], cosines[r + 4])
        sine = jnp.where(first, sines[r], sines[r + 4])
        value = value * cosine - spin(value, 64) * sine
        value = jnp.where(first, value + spin(value, -32), spin(value, 32) - value)
        if r == 2:
            value = jnp.where(first, value, plus_i(value))
        elif r:
            turned = plus_i(value)
            odd = value + turned if r == 1 else turned - value
            value = jnp.where(first, value, ROOT * odd)
        mixed.append(value)
    even, odd = mixed[0] + mixed[2], mixed[0] - mixed[2]
    side, turned = mixed[1] + mixed[3], plus_i(mixed[1] - mixed[3])
    for t, values in enumerate((even + side, odd + turned, even - side, odd - turned)):
        start = MARGIN + 2 * t * base
        held[start : start + base, :] = values
        held[start + base : start + 2 * base, :] = spin(values, -32)
    held[0:MARGIN, :] = held[length : length + MARGIN, :]
    held[length + MARGIN : length + 2 * MARGIN, :] = held[MARGIN : 2 * MARGIN, :]
    spare = total[...] + spin(total[...], 32)
    kept = rows + 2 * MARGIN // count_x
    half = made.shape[1]
    rest = kept - half
    low = lane_index((8, LANES)) % 64 < 32
    copies = []
    for target in range(count):
        start = (target // count_x) * block + (target % count_x) * kept
        for row in range(0, half, 8):
            a = held[start + row : start + row + 8, :]
            if row < rest:
                b = spin(held[start + half + row : start + half + row + 8, :], 32)
            else:
                b = spare
            made[target, row : row + 8, :] = jnp.where(low, a, b)
        if (target + 1) % RADIX == 0:
            group = pl.ds(target + 1 - RADIX, RADIX)
            copies.append(pltpu.make_async_copy(made.at[group], out.at[group], sent.at[len(copies)]))
            copies[-1].start()
    for copy in copies:
        copy.wait()


def inverse_x_kernel(
    kept, scale, lines, tables, turns, *refs
):
    *outs, held = refs
    place = lax.axis_index("gx")
    count, half, _ = lines.shape
    base = turns.shape[1]
    length = RADIX * base
    rest = kept - half
    low = lane_index((half, LANES)) % 64 < 32
    groups, spare = [], None
    for first in range(0, count, 2):
        even, odd = lines[first], lines[first + 1]
        a = jnp.where(low, even, spin(odd, 32))
        b = jnp.where(low, spin(even, -32), odd)
        groups.append(jnp.concatenate([a, b[:rest]], axis=0))
        extra = b[rest : rest + 8]
        spare = extra if spare is None else spare + extra
    mean = jnp.sum(spare) * scale
    wide = 2 * base // LANES
    narrow = base // LANES
    stacked = jnp.concatenate(
        [jnp.concatenate(groups[i * wide : (i + 1) * wide], axis=1) for i in range(3)], axis=0
    )
    at = 3 * wide
    zeros = jnp.concatenate(groups[at : at + narrow], axis=1)
    mids = jnp.concatenate(groups[at + narrow : at + 2 * narrow], axis=1)
    full, zero, middle = x_parts(tables, base)
    full = exact_dot(split(stacked), full)
    zero = exact_dot(split(zeros), zero) * scale
    mid = exact_dot(split(mids), middle) * scale
    turned = []
    for i in range(3):
        real = full[i * kept : (i + 1) * kept, :base]
        imag = full[i * kept : (i + 1) * kept, base:]
        c = turns[i : i + 1, :] * (2.0 * scale)
        s = turns[i + 3 : i + 4, :] * (2.0 * scale)
        turned.append((real * c - imag * s, real * s + imag * c))
    for t in range(RADIX):
        value = zero + mid if t % 2 == 0 else zero - mid
        for i, (real, imag) in enumerate(turned):
            eighth = t * (i + 1) % RADIX
            c = (1.0, ROOT, 0.0, -ROOT, -1.0, -ROOT, 0.0, ROOT)[eighth]
            s = (0.0, ROOT, 1.0, ROOT, 0.0, -ROOT, -1.0, -ROOT)[eighth]
            if c:
                value = value + c * real
            if s:
                value = value - s * imag
        held[:, t * base : (t + 1) * base] = mean - value
    targets, local = len(outs), outs[0].shape[1] - LANES
    right = lane_index((kept, LANES)) < 64
    for mask, out in enumerate(outs):
        start = pl.multiple_of((place ^ mask) * local, LANES)
        after = pl.multiple_of(jnp.where(start + local == length, 0, start + local), LANES)
        before = pl.multiple_of(jnp.where(start == 0, length, start) - LANES, LANES)
        out[:, :local] = held[:, pl.ds(start, local)]
        out[:, local:] = jnp.where(
            right, held[:, pl.ds(after, LANES)], held[:, pl.ds(before, LANES)]
        )


def slopes_x(parts, band, with_edge):
    tiles = parts[0].shape[-1] // LANES
    pieces = []
    for first in list(range(0, tiles - 1, 2)) + ([tiles - 1] if with_edge else []):
        steps = (-1, 0, 1, 2) if first < tiles - 1 else (-1, 0, 1)
        table = band[...] if first < tiles - 1 else band[: 3 * LANES, :LANES]
        order = [(first + step) % tiles for step in steps]
        piece = None
        for part in parts:
            term = dot(jnp.concatenate([lane_tile(part, t) for t in order], axis=1), table)
            piece = term if piece is None else piece + term
        pieces.append(piece)
    return jnp.concatenate(pieces, axis=1)


def slope_y(read):
    value = read(3) - read(-3)
    for index in (0, 1):
        value = value + whole_weights[index] * (read(index + 1) - read(-index - 1))
    return value


def edged(k, side, center, up, down, above, below, sides, has, first=0):
    step = pl.program_id(0) + first
    tile, width = center.shape
    tall = sides.shape[1]
    last = (tall - LANES) // tile - 1
    base = pl.multiple_of(step * tile, 8)
    before = pl.multiple_of(jnp.where(step == 0, tall, base) - HALO, 8)
    over = jnp.where(step == 0, strip(above, k, True) * has[2], up)
    under = jnp.where(step == last, strip(below, k, False) * has[3], down)
    rows = (
        (over, sides[side, pl.ds(before, HALO), :]),
        (center, sides[side, pl.ds(base, tile), :]),
        (under, sides[side, pl.ds(pl.multiple_of(base + tile, 8), HALO), :]),
    )
    return jnp.concatenate([jnp.concatenate(pair, axis=1) for pair in rows], axis=0)


def edged_open(k, side, wall, wall_up, wall_down, above, below, sides, has, first=0):
    open_cells = [1.0 - ref[0].astype(F32) for ref in (wall, wall_up, wall_down)]
    return edged(k, side, *open_cells, above, below, sides, has, first)


def quiet_step_kernel(
    first, has, place, center, up, down, wall, wall_up, wall_down, above, below, sides, across, along, along_inner, calm, density, shown_open, mark
):
    parts, _, tile, width = center.shape
    high = tile + 2 * HALO
    opened = edged_open(parts, parts, wall, wall_up, wall_down, above, below, sides, has, first)
    values = []
    for k in range(parts):
        value = edged(
            k,
            k,
            center[k, 0].astype(F32),
            up[k, 0].astype(F32)[up.shape[2] - HALO :],
            down[k, 0].astype(F32)[:HALO],
            above,
            below,
            sides,
            has,
            first,
        )
        values.append(value)

    def drops(x, along_b, along_p):
        diverge = x[1] + along_b
        return (
            diverge + mean_flow * x[0],
            x[3] + mean_flow * x[1],
            along_p + mean_flow * x[2],
            diverge + mean_flow * x[3],
        )

    short = [value.astype(BF16) for value in values]
    x = slopes_x((jnp.concatenate(short, axis=0),), across, True)
    x = [x[k * high : (k + 1) * high] for k in range(parts)]
    table = along[...]
    dropped = drops(x, dot(table, short[2]), dot(table, short[3]))
    middle = [opened * (v - (time_step / 60.0) * d) for v, d in zip(values, dropped)]
    inner = slice(HALO, HALO + tile)
    x = slopes_x(split(jnp.concatenate([value[inner] for value in middle], axis=0)), across, False)
    x = [x[k * tile : (k + 1) * tile] for k in range(parts)]
    table = along_inner[...]
    y = [sum(dot(table, part) for part in split(middle[k][:, :width])) for k in (2, 3)]
    dropped = drops(x, *y)
    shown = opened[inner, :width]
    for k in range(parts):
        start = 0.5 * values[k][inner, :width] - (0.5 * time_step / 60.0) * dropped[k]
        value = shown * start + 0.5 * middle[k][inner, :width]
        if k == 0:
            density[0, 0] = value.astype(BF16)
        else:
            calm[k - 1] = value
    shown_open[0] = (time_step * opened).astype(BF16)
    mark[0] = place[0]


def tables_kernel(place, weights_x, weights_y, rise_x, rise_y, mark):
    mark[0] = place[0]
    _, tiles, reach_x, lanes = rise_x.shape
    wide, length_x = (tiles - 1) * lanes, weights_x.shape[1]
    first = place[0] * wide
    half = LANES // 2

    def weights(ref, start, size):
        length = ref.shape[1]
        start = jnp.where(start < 0, start + length, jnp.where(start >= length, start - length, start))
        return ref[:, pl.ds(pl.multiple_of(start, LANES), size)]

    cells = lax.broadcasted_iota(jnp.int32, (reach_x, lanes), 0)
    fine = lax.broadcasted_iota(jnp.int32, (reach_x, lanes), 1)
    right, left = weights(weights_x, first + wide, LANES), weights(weights_x, first - LANES, LANES)
    edge = jnp.where(lane_index(right.shape) < half, right, left)
    edge = jnp.concatenate([edge, edge], axis=1)
    for k in range(tiles):
        own = weights(weights_x, first + k * lanes, lanes) if k < tiles - 1 else edge
        target = fine // 2 - 1
        if k == tiles - 1:
            target = jnp.where(fine < half, target, target + half)
        value = jnp.zeros(fine.shape, F32)
        for t in range(4):
            value = jnp.where(cells == (target + t) % reach_x, own[t : t + 1, :], value)
        rise_x[0, k], rise_x[1, k] = split(value)
    steps, high, reach = rise_y.shape
    tall = steps * TILE
    first = place[1] * tall
    own = [weights(weights_y, first + k * LANES, LANES) for k in range(-1, tall // LANES + 1)]
    own = jnp.concatenate([jnp.concatenate(own, axis=1), jnp.zeros((4, tall + 2 * LANES), F32)], axis=0).T
    cells = lax.broadcasted_iota(jnp.int32, (high, reach), 1)
    last = cells >= reach // 3 * 2
    cells = cells % (reach // 3)
    target = lax.broadcasted_iota(jnp.int32, (high, reach), 0) // 2 + (HALO // 2 - 1)
    for k in range(steps):
        start = LANES - HALO + k * TILE
        value = jnp.zeros((high, reach), F32)
        for t in range(4):
            value = jnp.where(cells == target + t, own[start : start + high, t : t + 1], value)
        upper, lower = split(value)
        rise_y[k] = jnp.where(last, lower, upper)


def source_kernel(squares, opened, rise_x, rise_y, quiet, across, _, *refs):
    *lines, out, squared, cells_open, matrix, rows_matrix, calm, band, held, raised, forced, done, fetched, kept = refs
    steps = done.shape[0]
    tile, width = calm.shape[2:]
    high = tile + 2 * HALO
    rows = lines[0].shape[0]
    place = lax.axis_index("gx")

    def tile_copies(k):
        part = quiet.at[:, pl.ds(k * tile, tile), :]
        return (
            pltpu.make_async_copy(part, calm.at[k % 2], fetched.at[k % 2]),
            pltpu.make_async_copy(opened.at[k], cells_open.at[k % 2], fetched.at[2 + k % 2]),
        )

    def done_copy(k):
        part = out.at[1:, 0, pl.ds(k * tile, tile), :]
        return pltpu.make_async_copy(done.at[k], part, kept.at[k])

    arrays = ((squares, squared), (rise_x, matrix), (rise_y, rows_matrix), (across, band))
    copies = [
        pltpu.make_async_copy(source, target, fetched.at[4 + k])
        for k, (source, target) in enumerate(arrays)
    ]
    pieces = [
        pltpu.make_async_copy(
            piece,
            held.at[pl.ds(pl.multiple_of((place ^ mask) * rows, 8), rows), :],
            fetched.at[4 + len(arrays) + mask],
        )
        for mask, piece in enumerate(lines)
    ]
    for copy in (*pieces, *copies, *tile_copies(0)):
        copy.start()
    for copy in pieces + copies[:1]:
        copy.wait()

    level = held[MARGIN - HALO : MARGIN - HALO + squared.shape[0], :] - squared[...]
    count = level.shape[1] // LANES
    near = lane_index((level.shape[0], LANES)) < 64
    around = []
    for k in range(count):
        after, before = lane_tile(level, (k + 1) % count), lane_tile(level, (k - 1) % count)
        around.append(split(jnp.concatenate([lane_tile(level, k), jnp.where(near, after, before)], axis=1)))
    copies[1].wait()
    for k in range(count):
        lanes = 2 * LANES if k < count - 1 else LANES
        value = split(exact_dot(around[k], [matrix[part, k, :, :lanes] for part in range(2)]))
        for part in range(2):
            raised[part, :, 2 * k * LANES : 2 * k * LANES + lanes] = value[part]
    for copy in tile_copies(1):
        copy.start()
    for copy in copies[2:]:
        copy.wait()

    reach = rows_matrix.shape[2] // 3
    for k in range(steps):
        start = k * (tile // 2)
        window = [raised[part, start : start + reach, :] for part in (0, 1, 0)]
        calm_here, open_here = tile_copies(k)
        open_here.wait()
        free = cells_open[k % 2].astype(F32)
        value = free * dot(rows_matrix[k], jnp.concatenate(window, axis=0))
        forced[k % 2] = value
        inner = value[HALO : HALO + tile]
        shown = (0.5 / 60.0) * free[HALO : HALO + tile, :width]
        x = shown * slopes_x(split(inner), band, False)
        y = shown * slope_y(lambda d: forced[k % 2, HALO + d : HALO + d + tile, :width])
        calm_here.wait()
        still = calm.at[k % 2]
        done[k, 0] = (still[0] - x).astype(BF16)
        done[k, 1] = (still[1] - y).astype(BF16)
        done[k, 2] = (still[2] + inner[:, :width] - mean_flow * x).astype(BF16)
        done_copy(k).start()
        if k + 2 < steps:
            for copy in tile_copies(k + 2):
                copy.start()
    for k in range(steps):
        done_copy(k).wait()


def call(
    kernel, operands, outs, scratch=(), steps=0, specs=None, out_specs=None, after=(), aliases=None, megabytes=24, flops=0, moved=0, name=None
):
    count = len(operands)

    def body(*refs):
        kernel(*refs[:count], *refs[count + len(after) :])

    def whole(array):
        zeros = (0,) * len(array.shape)
        return pl.BlockSpec(array.shape, lambda *_: zeros)

    arguments = {}
    chosen = specs or {}
    if steps:
        arguments["grid"] = (steps,)
        in_specs = [chosen.get(i, whole(o)) for i, o in enumerate(operands)]
        arguments["out_specs"] = jax.tree.map(whole, outs) if out_specs is None else out_specs
    else:
        local = pl.BlockSpec(memory_space=pltpu.VMEM)
        in_specs = [chosen.get(i, local) for i in range(count)]
        if out_specs is not None:
            arguments["out_specs"] = out_specs
    return pl.pallas_call(
        body,
        out_shape=outs,
        in_specs=in_specs + [pl.BlockSpec(memory_space=pl.ANY)] * len(after),
        scratch_shapes=list(scratch),
        input_output_aliases=aliases or {},
        compiler_params=pltpu.CompilerParams(vmem_limit_bytes=megabytes << 20),
        cost_estimate=pl.CostEstimate(flops=flops, bytes_accessed=moved, transcendentals=0),
        name=name,
        **arguments,
    )(*operands, *after)


def ring(array, axis, step):
    size = lax.axis_size(axis)
    return lax.ppermute(array, axis, [(i, (i + step) % size) for i in range(size)])


def swap(array, axis, mask):
    return lax.ppermute(array, axis, [(i, i ^ mask) for i in range(lax.axis_size(axis))])


def shaped(*shape, kind=F32):
    return jax.ShapeDtypeStruct(shape, kind)


def pressure_lines(pieces, gathered, spread, stepped):
    _, rows, local_x = pieces[0].shape
    count_x, count_y = lax.axis_size("gx"), lax.axis_size("gy")
    count = count_x * count_y
    length_x, length_y = local_x * count_x, rows * count
    full, zero, middle, cos_turn, sin_turn = x_tables(length_x)
    turns = np.zeros((8, cos_turn.shape[1]), np.float32)
    turns[0:3], turns[3:6] = cos_turn, sin_turn
    spectra, total = call(
        forward_x_kernel,
        (*pieces, np.concatenate([beside(full), beside(zero, middle)]), turns),
        (shaped(count, rows, LANES), shaped(8, LANES)),
        (
            pltpu.VMEM((count_x, 2, rows, local_x), F32),
            pltpu.VMEM((count, rows, LANES), F32),
            pltpu.SemaphoreType.DMA((5,)),
        ),
        out_specs=(pl.BlockSpec(memory_space=pl.ANY), pl.BlockSpec(memory_space=pltpu.VMEM)),
        after=gathered,
        flops=10**9,
        moved=4 << 20,
        name="forward_x",
    )
    spectra = lax.all_to_all(spectra, ("gy", "gx"), 0, 0, tiled=True)
    place = lax.axis_index("gy") * count_x + spread[0]
    waves = jnp.asarray(wave_table(length_x, count))
    wave = lax.dynamic_slice(waves, (place, 0), (1, LANES))
    both, turns_y = y_tables(length_y)
    kept = rows + 2 * MARGIN // count_x
    half = (kept // 2 + 8) // 8 * 8
    solved = call(
        functools.partial(solve_y_kernel, count_x),
        (spectra, total, wave, beside(both), turns_y),
        shaped(count, half, LANES),
        (
            pltpu.VMEM((length_y + 2 * MARGIN, LANES), F32),
            pltpu.VMEM((length_y // RADIX, 2 * RADIX * LANES), F32),
            pltpu.VMEM((count, half, LANES), F32),
            pltpu.SemaphoreType.DMA((count // RADIX,)),
        ),
        out_specs=pl.BlockSpec(memory_space=pl.ANY),
        flops=4 * 10**9,
        moved=6 << 20,
        name="solve_y",
    )
    solved = lax.all_to_all(solved, ("gy", "gx"), 0, 0, tiled=True)
    back = 2.0 * zero.T
    back[LANES // 2] *= 0.5
    tables = np.concatenate(
        [beside(full.T), beside(back, 2.0 * middle.T)]
    )
    again = jnp.asarray(np.tile(turns, (count_x, 1, 1)))
    again = lax.dynamic_slice(again, (stepped[0], 0, 0), (1,) + turns.shape)
    pressed = call(
        functools.partial(inverse_x_kernel, kept, 1.0 / (length_x * length_y)),
        (solved, tables, again[0]),
        (shaped(kept, local_x + LANES),) * count_x,
        (pltpu.VMEM((kept, length_x), F32),),
        flops=10**9,
        moved=4 << 20,
        name="inverse_x",
    )
    return [piece if mask == 0 else swap(piece, "gx", mask) for mask, piece in enumerate(pressed)]


def fast_shards(velocity, weights_x, weights_y, acoustic, wall_mask):
    parts, _, tall, wide = acoustic.shape
    _, _, local_y, local_x = velocity.shape
    count_x, count_y = lax.axis_size("gx"), lax.axis_size("gy")
    place_x, place_y = lax.axis_index("gx"), lax.axis_index("gy")
    full, high, steps = wide + LANES, TILE + 2 * HALO, tall // TILE
    strips = (parts + 2) * HALO
    small = 2 * HALO
    has = jnp.stack([place_x > 0, place_x < count_x - 1, place_y > 0, place_y < count_y - 1])
    has = has.astype(F32)
    scalars = pl.BlockSpec(memory_space=pltpu.SMEM)

    def at(block, *index):
        return pl.BlockSpec(block, lambda i: index)

    own = place_x.astype(jnp.int32).reshape(1)
    sent = call(
        pieces_kernel,
        (velocity,),
        (shaped(2, local_y // count_x, local_x),) * count_x,
        moved=2 << 20,
        megabytes=8,
        name="pieces",
    )
    moved = [piece if mask == 0 else swap(piece, "gx", mask) for mask, piece in enumerate(sent)]
    first, last = call(
        rows_kernel,
        (acoustic, acoustic, wall_mask, wall_mask, velocity, velocity),
        (shaped(STRIP_ROWS, wide),) * 2,
        steps=1,
        specs={
            0: at((parts, 1, small, wide), 0, 0, 0, 0),
            1: at((parts, 1, small, wide), 0, 0, tall // small - 1, 0),
            2: at((1, HALO, wide), 0, 0, 0),
            3: at((1, HALO, wide), 0, tall // HALO - 1, 0),
            4: at((1, 1, HALO, local_x), 1, 0, 0, 0),
            5: at((1, 1, HALO, local_x), 1, 0, local_y // HALO - 1, 0),
        },
        after=moved[1:2],
        moved=2 << 20,
        megabytes=52,
        name="rows",
    )
    above, below = ring(last, "gy", 1), ring(first, "gy", -1)
    to_right, to_left = call(
        columns_kernel,
        (has, acoustic, acoustic, wall_mask, wall_mask, velocity, velocity, above, below),
        (shaped(strips, tall + LANES), shaped(strips, tall + LANES)),
        steps=1,
        specs={
            0: scalars,
            1: at((parts, 1, tall, LANES), 0, 0, 0, 0),
            2: at((parts, 1, tall, LANES), 0, 0, 0, wide // LANES - 1),
            3: at((1, tall, LANES), 0, 0, 0),
            4: at((1, tall, LANES), 0, 0, wide // LANES - 1),
            5: at((1, 1, local_y, LANES), 1, 0, 0, 0),
            6: at((1, 1, local_y, LANES), 1, 0, 0, local_x // LANES - 1),
        },
        moved=8 << 20,
        megabytes=54,
        name="columns",
    )
    from_left, from_right = ring(to_right, "gx", 1), ring(to_left, "gx", -1)
    local_memory = pl.BlockSpec(memory_space=pltpu.VMEM)
    tiles = wide // (2 * LANES) + 1
    rise_x, rise_y, listed = call(
        tables_kernel,
        (jnp.stack([place_x, place_y]).astype(jnp.int32), weights_x, weights_y),
        (
            shaped(2, tiles, 2 * LANES, 2 * LANES, kind=BF16),
            shaped(steps, high, 3 * (high // 2 + HALO), kind=BF16),
            shaped(1, kind=jnp.int32),
        ),
        specs={0: scalars},
        out_specs=(local_memory, local_memory, scalars),
        moved=4 << 20,
        megabytes=54,
        name="tables",
    )
    sides, squares, beside = call(
        sides_kernel,
        (has, listed, velocity, above, below, from_left, from_right),
        (
            shaped(parts + 1, tall + LANES, LANES),
            shaped(local_y + 2 * HALO, local_x + LANES),
            shaped(1, kind=jnp.int32),
        ),
        steps=1,
        specs={0: scalars, 1: scalars, 2: at((1, 1, local_y, local_x), 1, 0, 0, 0)},
        out_specs=(
            at((parts + 1, tall + LANES, LANES), 0, 0, 0),
            at((local_y + 2 * HALO, local_x + LANES), 0, 0),
            scalars,
        ),
        moved=8 << 20,
        megabytes=54,
        name="sides",
    )
    across, along = band_tables(high)
    along_inner = along[HALO : HALO + TILE]
    per, rows = TILE // small, TILE // HALO

    def tiled(first):
        walls = (
            pl.BlockSpec((1, TILE, wide), lambda i: (0, i + first, 0)),
            pl.BlockSpec((1, HALO, wide), lambda i: (0, jnp.maximum((i + first) * rows - 1, 0), 0)),
            pl.BlockSpec(
                (1, HALO, wide),
                lambda i: (0, jnp.minimum((i + first + 1) * rows, steps * rows - 1), 0),
            ),
        )
        cells = (
            pl.BlockSpec((parts, 1, TILE, wide), lambda i: (0, 0, i + first, 0)),
            pl.BlockSpec(
                (parts, 1, small, wide), lambda i: (0, 0, jnp.maximum((i + first) * per - 1, 0), 0)
            ),
            pl.BlockSpec(
                (parts, 1, small, wide),
                lambda i: (0, 0, jnp.minimum((i + first + 1) * per, steps * per - 1), 0),
            ),
        )
        return cells, walls

    def quiet_tiles(first, count, before):
        cells, walls = tiled(first)
        operands = (has, own, acoustic, acoustic, acoustic, wall_mask, wall_mask, wall_mask, above, below, sides)
        operands = operands + (across, along, along_inner)
        return call(
            functools.partial(quiet_step_kernel, first),
            operands,
            (
                shaped(parts - 1, tall, wide),
                shaped(*acoustic.shape, kind=BF16),
                shaped(steps, high, full, kind=BF16),
                shaped(1, kind=jnp.int32),
            ),
            steps=count,
            specs=dict(enumerate((scalars, scalars) + cells + walls)),
            out_specs=(
                pl.BlockSpec((parts - 1, TILE, wide), lambda i: (0, i + first, 0)),
                pl.BlockSpec((1, 1, TILE, wide), lambda i: (0, 0, i + first, 0)),
                pl.BlockSpec((1, high, full), lambda i: (i + first, 0, 0)),
                scalars,
            ),
            after=before,
            aliases={len(operands) + k: k for k in range(len(before))},
            megabytes=54,
            flops=3 * 10**9 * count,
            moved=(12 << 20) * count,
            name="quiet_step",
        )

    early = max(steps * 3 // 4, 1)
    *begun, stepped = quiet_tiles(0, early, ())
    if early < steps:
        *begun, _ = quiet_tiles(early, steps - early, begun)
    quiet, final, opened = begun
    lines = pressure_lines(moved, (above, below), beside, stepped)
    operands = (squares, opened, rise_x, rise_y, quiet, across, final, *lines)
    anywhere = pl.BlockSpec(memory_space=pl.ANY)
    specs = {k: anywhere for k in range(len(operands))}
    scratch = (
        pltpu.VMEM(squares.shape, F32),
        pltpu.VMEM((2,) + opened.shape[1:], BF16),
        pltpu.VMEM(rise_x.shape, BF16),
        pltpu.VMEM(rise_y.shape, BF16),
        pltpu.VMEM((2, parts - 1, TILE, wide), F32),
        pltpu.VMEM(across.shape, BF16),
        pltpu.VMEM((local_y + 2 * MARGIN, local_x + LANES), F32),
        pltpu.VMEM((2, local_y + 2 * HALO, full), BF16),
        pltpu.VMEM((2, high, full), F32),
        pltpu.VMEM((steps, parts - 1, TILE, wide), BF16),
        pltpu.SemaphoreType.DMA((8 + count_x,)),
        pltpu.SemaphoreType.DMA((steps,)),
    )
    return call(
        source_kernel,
        operands,
        shaped(*acoustic.shape, kind=BF16),
        scratch,
        specs=specs,
        out_specs=anywhere,
        aliases={6: 0},
        megabytes=56,
        flops=4 * 10**9,
        moved=16 << 20,
        name="source_step",
    )


def fits(count_x, count_y, velocity, acoustic):
    _, planes, local_y, local_x = velocity
    _, _, tall, wide = acoustic
    length_x, length_y = local_x * count_x, local_y * count_y
    rows = local_y // count_x
    base_x, base_y = length_x // RADIX, length_y // RADIX
    return (
        planes == 1
        and acoustic[0] == PARTS
        and length_x * 2 == count_x * count_y * LANES
        and base_x % (2 * LANES) == 0
        and local_x % base_x == 0
        and rows % 8 == 0
        and base_y % rows == 0
        and base_y % 8 == 0
        and count_x * count_y % RADIX == 0
        and MARGIN * 2 % (8 * count_x) == 0
        and tall == 2 * local_y
        and wide == 2 * local_x
        and tall % TILE == 0
        and tall % LANES == 0
        and tall >= 2 * TILE
        and count_x & (count_x - 1) == 0
        and wide % (2 * LANES) == 0
    )


def extended(array, sides, width):
    for axis, dim in sides:
        size, length = (lax.axis_size(axis), array.shape[dim])
        up = [(i, (i + 1) % size) for i in range(size - 1)]
        down = [(j, i) for i, j in up]
        last = lax.slice_in_dim(array, length - width, length, axis=dim)
        leading = lax.slice_in_dim(array, 0, width, axis=dim)
        before = lax.ppermute(last, axis, up)
        after = lax.ppermute(leading, axis, down)
        array = jnp.concatenate([before, array, after], axis=dim)
    return array


def gradients(padded):
    height = padded.shape[-2] - 6
    breadth = padded.shape[-1] - 6
    rows_mid = padded[..., 3 : 3 + height, :]
    cols_mid = padded[..., :, 3 : 3 + breadth]
    along_x = jnp.zeros_like(padded[..., 3 : 3 + height, 3 : 3 + breadth])
    along_y = jnp.zeros_like(along_x)
    for index, weight in enumerate(stencil_weights):
        distance = index + 1
        along_x = along_x + weight * (
            rows_mid[..., 3 + distance : 3 + distance + breadth]
            - rows_mid[..., 3 - distance : 3 - distance + breadth]
        )
        along_y = along_y + weight * (
            cols_mid[..., 3 + distance : 3 + distance + height, :]
            - cols_mid[..., 3 - distance : 3 - distance + height, :]
        )
    return (along_x, along_y)


def tendency(padded, source):
    along_x, along_y = gradients(padded)
    diverge = along_x[1] + along_y[2]
    forcing = jnp.stack([-diverge, -along_x[3], -along_y[3], source - diverge])
    return forcing - mean_flow * along_x


def spectral_index(flat, length):
    second = length // 16
    wave = flat // second + 16 * (flat % second)
    return jnp.where(wave < length // 2, wave, wave - length).astype(jnp.float32)


def twiddles(rows_count, cols_count, modulus, sign):
    products = jnp.arange(rows_count)[:, None] * jnp.arange(cols_count)[None, :] % modulus
    angles = 2.0 * math.pi / modulus * products.astype(jnp.float32)
    return (jnp.cos(angles), sign * jnp.sin(angles))


def mix_rows(real_part, imag_part, cosine, sine):
    exact = lax.Precision.HIGHEST
    cos_real = jnp.einsum("ka,...ab->...kb", cosine, real_part, precision=exact)
    cos_imag = jnp.einsum("ka,...ab->...kb", cosine, imag_part, precision=exact)
    sin_real = jnp.einsum("ka,...ab->...kb", sine, real_part, precision=exact)
    sin_imag = jnp.einsum("ka,...ab->...kb", sine, imag_part, precision=exact)
    return (cos_real - sin_imag, cos_imag + sin_real)


def mix_cols(real_part, imag_part, cosine, sine):
    exact = lax.Precision.HIGHEST
    cos_real = jnp.einsum("...kb,bc->...kc", real_part, cosine, precision=exact)
    cos_imag = jnp.einsum("...kb,bc->...kc", imag_part, cosine, precision=exact)
    sin_real = jnp.einsum("...kb,bc->...kc", real_part, sine, precision=exact)
    sin_imag = jnp.einsum("...kb,bc->...kc", imag_part, sine, precision=exact)
    return (cos_real - sin_imag, cos_imag + sin_real)


def rotate(real_part, imag_part, cosine, sine):
    return (real_part * cosine - imag_part * sine, real_part * sine + imag_part * cosine)


def discrete(real_part, imag_part, sign):
    length = real_part.shape[-1]
    second = length // 16
    initial = real_part.shape
    folded = initial[:-1] + (16, second)
    real_part = real_part.reshape(folded)
    imag_part = imag_part.reshape(folded)
    small_cos, small_sin = twiddles(16, 16, 16, sign)
    large_cos, large_sin = twiddles(second, second, second, sign)
    turn_cos, turn_sin = twiddles(16, second, length, sign)
    if sign < 0:
        real_part, imag_part = mix_rows(real_part, imag_part, small_cos, small_sin)
        real_part, imag_part = rotate(real_part, imag_part, turn_cos, turn_sin)
        real_part, imag_part = mix_cols(real_part, imag_part, large_cos, large_sin)
    else:
        real_part, imag_part = mix_cols(real_part, imag_part, large_cos, large_sin)
        real_part, imag_part = rotate(real_part, imag_part, turn_cos, turn_sin)
        real_part, imag_part = mix_rows(real_part, imag_part, small_cos, small_sin)
        real_part = real_part / length
        imag_part = imag_part / length
    return (real_part.reshape(initial), imag_part.reshape(initial))


def transform(stacked, sign, kind):
    if kind == "real_in":
        real_part = stacked
        imag_part = jnp.zeros_like(stacked)
    else:
        half = stacked.shape[0] // 2
        real_part = stacked[:half]
        imag_part = stacked[half:]
    real_out, imag_out = discrete(real_part, imag_part, sign)
    if kind == "real_out":
        return real_out
    return jnp.concatenate([real_out, imag_out], axis=0)


def project(stacked, wave_x, wave_y):
    coef_xx = wave_x * wave_x
    coef_xy = 2.0 * wave_x * wave_y
    coef_yy = wave_y * wave_y
    denominator = wave_x * wave_x + wave_y * wave_y
    positive = denominator > 0
    safe = jnp.where(positive, denominator, 1.0)

    def combine(parts):
        numerator = -(coef_xx * parts[0] + coef_xy * parts[1] + coef_yy * parts[2])
        return jnp.where(positive, numerator / safe, 0.0)

    return jnp.stack([combine(stacked[:3]), combine(stacked[3:])])


def refine(stacked, weights):
    result = jnp.zeros(stacked.shape[:-1] + (2 * stacked.shape[-1],), jnp.float32)
    for offset in range(4):
        result = (
            result
            + jnp.repeat(jnp.roll(stacked, 1 - offset, axis=-1), 2, axis=-1) * weights[offset]
        )
    return result


def lines_x(stacked, action):
    gathered = action(lax.all_to_all(stacked, "gx", split_axis=2, concat_axis=3, tiled=True))
    return lax.all_to_all(gathered, "gx", split_axis=3, concat_axis=2, tiled=True)


def lines_y(stacked, action):
    turned = jnp.swapaxes(stacked, 2, 3)
    gathered = action(lax.all_to_all(turned, "gy", split_axis=2, concat_axis=3, tiled=True))
    returned = lax.all_to_all(gathered, "gy", split_axis=3, concat_axis=2, tiled=True)
    return jnp.swapaxes(returned, 2, 3)


def expand(fields):
    return extended(fields, (("gx", 3), ("gy", 2)), 3)


def shards(velocity, weights_x, weights_y, acoustic, wall_mask):
    acoustic = acoustic.astype(jnp.float32)
    flow_x = velocity[0]
    flow_y = velocity[1]
    tensor = jnp.stack([flow_x * flow_x, flow_x * flow_y, flow_y * flow_y])
    count_gx = lax.axis_size("gx")
    count_gy = lax.axis_size("gy")
    place_x = lax.axis_index("gx")
    place_y = lax.axis_index("gy")
    local_y = tensor.shape[2]
    local_x = tensor.shape[3]
    length_x = local_x * count_gx
    length_y = local_y * count_gy

    def forward_real(portion):
        return transform(portion, -1, "real_in")

    def finish_x(portion):
        return refine(transform(portion, 1, "real_out"), weights_x)

    spectra = lines_x(tensor, forward_real)
    share_x = local_x // count_gy
    line_x = spectral_index(place_x * local_x + place_y * share_x + jnp.arange(share_x), length_x)[
        :, None
    ]
    line_y = spectral_index(jnp.arange(length_y), length_y)[None, :]

    def solve_y(portion):
        solved = project(transform(portion, -1, "complex"), line_x, line_y)
        return refine(transform(solved, 1, "complex"), weights_y)

    pressure = lines_y(spectra, solve_y)
    source = lines_x(pressure, finish_x)[0]
    open_cells = (1 - wall_mask).astype(jnp.float32)
    first_rate = tendency(expand(acoustic), source)
    middle = open_cells * (acoustic + time_step * first_rate)
    second_rate = tendency(expand(middle), source)
    return (open_cells * (acoustic + 0.5 * time_step * (first_rate + second_rate))).astype(
        jnp.bfloat16
    )


def solution(mesh):
    in_specs = (P(None, None, "gy", "gx"), P(), P(), P(None, None, "gy", "gx"), P(None, "gy", "gx"))
    out_specs = P(None, None, "gy", "gx")

    def chosen(velocity, weights_x, weights_y, acoustic, wall_mask):
        sizes = (mesh.shape["gx"], mesh.shape["gy"], velocity.shape, acoustic.shape)
        plan = fast_shards if fits(*sizes) else shards
        return plan(velocity, weights_x, weights_y, acoustic, wall_mask)

    return jax.shard_map(
        chosen, mesh=mesh, in_specs=in_specs, out_specs=out_specs, check_vma=False
    )
```

```python
import functools
import math

import jax
import jax.numpy as jnp
import ml_dtypes
import numpy as np
from jax import lax
from jax.experimental import pallas as pl
from jax.experimental.pallas import tpu as pltpu
from jax.sharding import PartitionSpec as P

stencil_weights = (0.75, -0.15, 1.0 / 60.0)
mean_flow = 0.3
time_step = 0.5
whole_weights = (45.0, -9.0, 1.0)

LANES = 128
RADIX = 8
HALO = 8
MARGIN = 16
TILE = 128
ROOT = math.sqrt(0.5)
STRIP = {2: (0, 6), 3: (6, 6), 1: (12, 3), 4: (15, 3), 5: (20, 4)}
STRIP_ROWS = 24
PARTS = 4
BF16 = jnp.bfloat16
F32 = jnp.float32


def halves(table):
    high = table.astype(np.float32).astype(ml_dtypes.bfloat16)
    low = (table - high.astype(np.float64)).astype(np.float32).astype(ml_dtypes.bfloat16)
    return high, low


def packed_columns(cosine, sine):
    half = LANES // 2
    parts = []
    for first in range(0, cosine.shape[1], half):
        parts += [cosine[:, first : first + half], sine[:, first : first + half]]
    return np.concatenate(parts, axis=1)


@functools.lru_cache(maxsize=None)
def x_tables(length):
    base = length // RADIX
    m = np.arange(base)[:, None]
    q = np.arange(base)[None, :]
    angle = 2.0 * np.pi * ((m * q) % base) / base
    cosine, sine = np.cos(angle), np.sin(angle)
    full = np.concatenate([packed_columns(cosine, -sine), packed_columns(sine, cosine)], axis=0)
    half = base // 2
    zero_cos, zero_sin = cosine[:, :half].copy(), -sine[:, :half]
    zero_cos[:, 0] = 0.0
    zero_sin = zero_sin.copy()
    zero_sin[:, 0] = (-1.0) ** np.arange(base)
    zero = packed_columns(zero_cos, zero_sin)
    shifted = 2.0 * np.pi * ((m * (RADIX * q[:, :half] + RADIX // 2)) % length) / length
    middle = packed_columns(np.cos(shifted), -np.sin(shifted))
    turns = 2.0 * np.pi * np.arange(1, RADIX // 2)[:, None] * np.arange(base)[None, :] / length
    return full, zero, middle, np.cos(turns), np.sin(turns)


@functools.lru_cache(maxsize=None)
def y_tables(length):
    base = length // RADIX
    index = np.arange(base)
    angle = 2.0 * np.pi * ((index[:, None] * index[None, :]) % base) / base
    both = np.concatenate([np.cos(angle), np.sin(angle)], axis=0)
    turns = 2.0 * np.pi * np.arange(RADIX)[:, None] * index[None, :] / length
    turns = np.concatenate([np.cos(turns), np.sin(turns)], axis=0).T
    high, rest = halves(turns)
    low = turns - high.astype(np.float64) - rest.astype(np.float64)
    return both, np.concatenate([high, rest, low.astype(ml_dtypes.bfloat16)], axis=1)


@functools.lru_cache(maxsize=None)
def wave_table(length, count):
    slots = LANES // 4
    base = length // RADIX
    waves = []
    for residue in (1, 2, 3):
        waves.append(RADIX * np.arange(base) + residue)
    waves.append(RADIX * np.arange(base // 2))
    waves.append(RADIX * np.arange(base // 2) + RADIX // 2)
    waves = np.concatenate(waves)
    waves = np.where(waves == 0, length // 2, waves)
    waves = np.where(waves < length // 2, waves, waves - length).reshape(count, slots)
    return np.tile(waves, (1, 4)).astype(np.float32)


@functools.lru_cache(maxsize=None)
def band_tables(rows):
    across = np.zeros((4 * LANES, 2 * LANES))
    column = np.arange(2 * LANES)
    down = np.zeros((rows, rows))
    for index, weight in enumerate(whole_weights):
        distance = index + 1
        across[column + LANES + distance, column] = weight
        across[column + LANES - distance, column] = -weight
        down += weight * (np.eye(rows, k=distance) - np.eye(rows, k=-distance))
    return across.astype(ml_dtypes.bfloat16), down.astype(ml_dtypes.bfloat16)


def beside(*tables):
    high, low = halves(np.concatenate(tables, axis=1))
    return np.concatenate([high, low], axis=0)


def split(values):
    high = values.astype(BF16)
    return high, (values - high.astype(F32)).astype(BF16)


def dot(left, right):
    return jnp.dot(left, right, preferred_element_type=F32)


def exact_dot(left, right):
    left_high, left_low = left
    right_high, right_low = right
    return dot(left_high, right_high) + (dot(left_low, right_high) + dot(left_high, right_low))


def lane_index(shape):
    return lax.broadcasted_iota(jnp.int32, shape, len(shape) - 1)


def spin(values, shift):
    return pltpu.roll(values, shift % values.shape[-1], values.ndim - 1)


def lane_tile(values, index):
    return values[:, index * LANES : (index + 1) * LANES]


def x_parts(tables, base):
    wide = 2 * base
    full = (tables[:wide], tables[wide : 2 * wide])
    at = 2 * wide
    high, low = tables[at : at + base], tables[at + base : at + 2 * base]
    return full, (high[:, :base], low[:, :base]), (high[:, base:], low[:, base:])


def pieces_kernel(velocity, *pieces):
    rows = pieces[0].shape[1]
    place = lax.axis_index("gx")
    for mask, piece in enumerate(pieces):
        start = pl.multiple_of((place ^ mask) * rows, 8)
        for c in range(2):
            piece[c] = velocity[c, 0, pl.ds(start, rows), :]


def rows_kernel(top, low, top_wall, low_wall, top_flow, low_flow, first, last):
    small, width = top.shape[2], top_flow.shape[3]
    first[...] = jnp.zeros(first.shape, F32)
    last[...] = jnp.zeros(last.shape, F32)
    for k, (start, rows) in STRIP.items():
        lanes = slice(0, width) if k == PARTS + 1 else slice(None)
        if k < PARTS:
            upper, lower = top[k, 0].astype(F32)[:HALO], low[k, 0].astype(F32)[small - HALO :]
        elif k == PARTS:
            upper, lower = 1.0 - top_wall[0].astype(F32), 1.0 - low_wall[0].astype(F32)
        else:
            upper, lower = top_flow[0, 0], low_flow[0, 0]
        first[start : start + rows, lanes] = upper[:rows]
        last[start : start + rows, lanes] = lower[HALO - rows :]


def strip(ref, k, upper, lanes=slice(None)):
    if k not in STRIP:
        return jnp.zeros((HALO, ref[0:1, lanes].shape[1]), F32)
    start, rows = STRIP[k]
    values = ref[start : start + rows, lanes]
    blank = jnp.zeros((HALO - rows, values.shape[1]), F32)
    return jnp.concatenate([blank, values] if upper else [values, blank], axis=0)


def columns_kernel(
    has, left, right, left_wall, right_wall, left_flow, right_flow, above, below, to_right, to_left
):
    parts = left.shape[0]
    wide, flow_wide = above.shape[1], above.shape[1] // 2
    gap = jnp.zeros((LANES - 2 * HALO, LANES), F32)

    def tall(k, inner, first, sides):
        lanes = slice(first, first + LANES)
        over, under = strip(above, k, True, lanes), strip(below, k, False, lanes)
        return jnp.concatenate([inner, under * sides[1], gap, over * sides[0]], axis=0).T

    for k in range(parts + 1):
        at = slice(k * HALO, (k + 1) * HALO)
        if k < parts:
            near, far = left[k, 0].astype(F32), right[k, 0].astype(F32)
        else:
            near, far = 1.0 - left_wall[0].astype(F32), 1.0 - right_wall[0].astype(F32)
        sides = (has[2], has[3])
        to_left[at, :] = tall(k, near, 0, sides)[:HALO]
        to_right[at, :] = tall(k, far, wide - LANES, sides)[LANES - HALO :]
    k = parts + 1
    at = slice(k * HALO, (k + 1) * HALO)
    size = left_flow.shape[2] + LANES
    blank = jnp.zeros((HALO, to_left.shape[1] - size), F32)
    to_left[at, :size] = tall(k, left_flow[0, 0], 0, (1.0, 1.0))[:HALO]
    to_right[at, :size] = tall(k, right_flow[0, 0], flow_wide - LANES, (1.0, 1.0))[LANES - HALO :]
    to_left[at, size:] = blank
    to_right[at, size:] = blank


def sides_kernel(has, place, velocity, above, below, from_left, from_right, sides, squares, mark):
    parts, tall, _ = sides.shape
    gap = jnp.zeros((LANES - 2 * HALO, tall), F32)
    for k in range(parts):
        at = slice(k * HALO, (k + 1) * HALO)
        tile = [from_right[at, :] * has[1], gap, from_left[at, :] * has[0]]
        sides[k] = jnp.concatenate(tile, axis=0).T
    at = slice(parts * HALO, (parts + 1) * HALO)
    rows, local = velocity.shape[2:]
    size = rows + LANES
    tile = [from_right[at, :size], gap[:, :size], from_left[at, :size]]
    tile = jnp.concatenate(tile, axis=0).T
    tile = tile * tile
    mark[0] = place[0]
    over, under = (strip(ref, parts, ref is above, slice(0, local)) for ref in (above, below))
    squares[:HALO, :local] = over * over
    squares[HALO : HALO + rows, :local] = velocity[0, 0] * velocity[0, 0]
    squares[HALO + rows :, :local] = under * under
    squares[:HALO, local:] = tile[size - HALO :]
    squares[HALO : HALO + rows, local:] = tile[:rows]
    squares[HALO + rows :, local:] = tile[rows : rows + HALO]


def forward_x_kernel(*refs):
    *pieces, tables, turns, out, total, lines, made, sent = refs
    count, _, rows, local = lines.shape
    place = lax.axis_index("gx")
    for mask, piece in enumerate(pieces):
        lines[place ^ mask] = piece[...]
    base = turns.shape[1]
    per = local // base
    u = [lines[t // per, 0, :, (t % per) * base : (t % per + 1) * base] for t in range(RADIX)]
    v = [lines[t // per, 1, :, (t % per) * base : (t % per + 1) * base] for t in range(RADIX)]
    energy = sum(b * b for b in v)
    energy = jnp.sum(energy.reshape(rows // 8, 8, base), axis=0)
    total[...] = sum(energy[:, k : k + LANES] for k in range(0, base, LANES))
    fields = ([a * a - b * b for a, b in zip(u, v)], [2.0 * a * b for a, b in zip(u, v)])
    zeros, mids, reals, imags = [], [], [[], [], []], [[], [], []]
    for a in fields:
        s04, s26, s15, s37 = a[0] + a[4], a[2] + a[6], a[1] + a[5], a[3] + a[7]
        d04, d26, d15, d37 = a[0] - a[4], a[2] - a[6], a[1] - a[5], a[3] - a[7]
        zeros.append((s04 + s26) + (s15 + s37))
        mids.append((s04 + s26) - (s15 + s37))
        minus, plus = ROOT * (d15 - d37), ROOT * (d15 + d37)
        turned = (
            (d04 + minus, -d26 - plus),
            (s04 - s26, s37 - s15),
            (d04 - minus, d26 - plus),
        )
        for index, (real, imag) in enumerate(turned):
            c, s = turns[index : index + 1, :], turns[index + 3 : index + 4, :]
            reals[index].append(real * c + imag * s)
            imags[index].append(imag * c - real * s)
    stacked = jnp.concatenate(
        [
            jnp.concatenate([jnp.concatenate(reals[i], axis=0) for i in range(3)], axis=0),
            jnp.concatenate([jnp.concatenate(imags[i], axis=0) for i in range(3)], axis=0),
        ],
        axis=1,
    )
    full, zero, middle = x_parts(tables, base)
    full = exact_dot(split(stacked), full)
    zero = exact_dot(split(jnp.concatenate(zeros, axis=0)), zero)
    middle = exact_dot(split(jnp.concatenate(mids, axis=0)), middle)
    low = lane_index((rows, LANES)) % 64 < 32
    target, copies = 0, []
    blocks = [full[2 * rows * i : 2 * rows * (i + 1)] for i in range(3)] + [zero, middle]
    for block in blocks:
        start = target
        for first in range(0, block.shape[1], LANES):
            a = block[:rows, first : first + LANES]
            c = block[rows:, first : first + LANES]
            made[target] = jnp.where(low, a, spin(c, 32))
            made[target + 1] = jnp.where(low, spin(a, -32), c)
            target += 2
        group = pl.ds(start, target - start)
        copies.append(pltpu.make_async_copy(made.at[group], out.at[group], sent.at[len(copies)]))
        copies[-1].start()
    for copy in copies:
        copy.wait()


def eighths(x, turn):
    s04, s26, s15, s37 = x[0] + x[4], x[2] + x[6], x[1] + x[5], x[3] + x[7]
    d04, d26, d15, d37 = x[0] - x[4], x[2] - x[6], x[1] - x[5], x[3] - x[7]
    quarter = turn(s15 - s37)
    spun_26, spun_37 = turn(d26), turn(d37)
    one, three = d15 + spun_37, d15 - spun_37
    spun_one, spun_three = turn(one), turn(three)
    one = ROOT * (one + spun_one)
    three = ROOT * (spun_three - three)
    return [
        (s04 + s26) + (s15 + s37),
        (d04 + spun_26) + one,
        (s04 - s26) + quarter,
        (d04 - spun_26) + three,
        (s04 + s26) - (s15 + s37),
        (d04 + spun_26) - one,
        (s04 - s26) - quarter,
        (d04 - spun_26) - three,
    ]


def solve_y_kernel(count_x, lines, total, wave, both, turns, out, held, spread, made, sent):
    count, rows, _ = lines.shape
    base = turns.shape[0]
    length = count * rows
    block = count_x * rows
    per = base // rows
    lanes = lane_index((base, LANES))
    sign = jnp.where(lanes < 64, 1.0, -1.0).astype(F32)

    def minus_i(z):
        return spin(z, 64) * sign

    def plus_i(z):
        return spin(z, 64) * -sign

    fields = [
        jnp.concatenate([lines[t * per + k] for k in range(per)], axis=0) for t in range(RADIX)
    ]
    mixed = eighths(fields, minus_i)
    terms, columns = turns.shape[1], 2 * RADIX
    picked = lax.broadcasted_iota(jnp.int32, (terms, columns * LANES), 0) % columns
    lane = lane_index(picked.shape)
    value = jnp.where((lane >= RADIX * LANES) & (lane % LANES >= 64), -1.0, 1.0)
    spread[...] = dot(turns[...], jnp.where(picked == lane // LANES, value, 0.0).astype(BF16))
    cosines = [spread[:, r * LANES : (r + 1) * LANES] for r in range(RADIX)]
    sines = [spread[:, (r + RADIX) * LANES : (r + RADIX + 1) * LANES] for r in range(RADIX)]
    mixed = [mixed[0]] + [
        mixed[r] * cosines[r] + spin(mixed[r], 64) * sines[r] for r in range(1, RADIX)
    ]
    tables = (both[: 2 * base], both[2 * base :])
    product = exact_dot(tables, split(jnp.concatenate(mixed, axis=1)))
    kx = wave[0:1, :]
    first = lanes % 64 < 32
    edge = jnp.float32(length // 2)
    square_kx = kx * kx
    alone = jnp.where(first, square_kx, 0.0)
    slope = jnp.where(first | (kx == -edge), 0.0, jnp.broadcast_to(kx, lanes.shape))
    q = lax.broadcasted_iota(jnp.int32, lanes.shape, 0)
    low_ky = RADIX * (q - jnp.where(q < base // 2, 0, base)).astype(F32)
    terms = []
    for r in range(RADIX):
        at = slice(r * LANES, (r + 1) * LANES)
        spectrum = product[:base, at] + minus_i(product[base:, at])
        ky = low_ky + float(r)
        symbol = alone + slope * ky
        if r == 0:
            corner = jnp.where((kx == -edge) & ~first, edge * edge, 0.0)
            symbol = jnp.where(ky == -edge, jnp.where(first, alone, corner), symbol)
        square = square_kx + ky * ky
        guess = pl.reciprocal(square, approx=True)
        terms.append(symbol * (guess * (2.0 - square * guess)) * spectrum)
    pairs = [
        jnp.where(first, low + spin(low, -32), high + spin(high, 32))
        for low, high in zip(terms[:4], terms[4:])
    ]
    product = exact_dot(tables, split(jnp.concatenate(pairs, axis=1)))
    mixed = []
    for r in range(RADIX // 2):
        at = slice(r * LANES, (r + 1) * LANES)
        value = product[:base, at] + plus_i(product[base:, at])
        cosine = jnp.where(first, cosines[r], cosines[r + 4])
        sine = jnp.where(first, sines[r], sines[r + 4])
        value = value * cosine - spin(value, 64) * sine
        value = jnp.where(first, value + spin(value, -32), spin(value, 32) - value)
        if r == 2:
            value = jnp.where(first, value, plus_i(value))
        elif r:
            turned = plus_i(value)
            odd = value + turned if r == 1 else turned - value
            value = jnp.where(first, value, ROOT * odd)
        mixed.append(value)
    even, odd = mixed[0] + mixed[2], mixed[0] - mixed[2]
    side, turned = mixed[1] + mixed[3], plus_i(mixed[1] - mixed[3])
    for t, values in enumerate((even + side, odd + turned, even - side, odd - turned)):
        start = MARGIN + 2 * t * base
        held[start : start + base, :] = values
        held[start + base : start + 2 * base, :] = spin(values, -32)
    held[0:MARGIN, :] = held[length : length + MARGIN, :]
    held[length + MARGIN : length + 2 * MARGIN, :] = held[MARGIN : 2 * MARGIN, :]
    spare = total[...] + spin(total[...], 32)
    kept = rows + 2 * MARGIN // count_x
    half = made.shape[1]
    rest = kept - half
    low = lane_index((8, LANES)) % 64 < 32
    copies = []
    for target in range(count):
        start = (target // count_x) * block + (target % count_x) * kept
        for row in range(0, half, 8):
            a = held[start + row : start + row + 8, :]
            if row < rest:
                b = spin(held[start + half + row : start + half + row + 8, :], 32)
            else:
                b = spare
            made[target, row : row + 8, :] = jnp.where(low, a, b)
        if (target + 1) % RADIX == 0:
            group = pl.ds(target + 1 - RADIX, RADIX)
            copies.append(pltpu.make_async_copy(made.at[group], out.at[group], sent.at[len(copies)]))
            copies[-1].start()
    for copy in copies:
        copy.wait()


def inverse_x_kernel(
    kept, scale, lines, tables, turns, *refs
):
    *outs, held = refs
    place = lax.axis_index("gx")
    count, half, _ = lines.shape
    base = turns.shape[1]
    length = RADIX * base
    rest = kept - half
    low = lane_index((half, LANES)) % 64 < 32
    groups, spare = [], None
    for first in range(0, count, 2):
        even, odd = lines[first], lines[first + 1]
        a = jnp.where(low, even, spin(odd, 32))
        b = jnp.where(low, spin(even, -32), odd)
        groups.append(jnp.concatenate([a, b[:rest]], axis=0))
        extra = b[rest : rest + 8]
        spare = extra if spare is None else spare + extra
    mean = jnp.sum(spare) * scale
    wide = 2 * base // LANES
    narrow = base // LANES
    stacked = jnp.concatenate(
        [jnp.concatenate(groups[i * wide : (i + 1) * wide], axis=1) for i in range(3)], axis=0
    )
    at = 3 * wide
    zeros = jnp.concatenate(groups[at : at + narrow], axis=1)
    mids = jnp.concatenate(groups[at + narrow : at + 2 * narrow], axis=1)
    full, zero, middle = x_parts(tables, base)
    full = exact_dot(split(stacked), full)
    zero = exact_dot(split(zeros), zero) * scale
    mid = exact_dot(split(mids), middle) * scale
    turned = []
    for i in range(3):
        real = full[i * kept : (i + 1) * kept, :base]
        imag = full[i * kept : (i + 1) * kept, base:]
        c = turns[i : i + 1, :] * (2.0 * scale)
        s = turns[i + 3 : i + 4, :] * (2.0 * scale)
        turned.append((real * c - imag * s, real * s + imag * c))
    for t in range(RADIX):
        value = zero + mid if t % 2 == 0 else zero - mid
        for i, (real, imag) in enumerate(turned):
            eighth = t * (i + 1) % RADIX
            c = (1.0, ROOT, 0.0, -ROOT, -1.0, -ROOT, 0.0, ROOT)[eighth]
            s = (0.0, ROOT, 1.0, ROOT, 0.0, -ROOT, -1.0, -ROOT)[eighth]
            if c:
                value = value + c * real
            if s:
                value = value - s * imag
        held[:, t * base : (t + 1) * base] = mean - value
    targets, local = len(outs), outs[0].shape[1] - LANES
    right = lane_index((kept, LANES)) < 64
    for mask, out in enumerate(outs):
        start = pl.multiple_of((place ^ mask) * local, LANES)
        after = pl.multiple_of(jnp.where(start + local == length, 0, start + local), LANES)
        before = pl.multiple_of(jnp.where(start == 0, length, start) - LANES, LANES)
        out[:, :local] = held[:, pl.ds(start, local)]
        out[:, local:] = jnp.where(
            right, held[:, pl.ds(after, LANES)], held[:, pl.ds(before, LANES)]
        )


def slopes_x(parts, band, with_edge):
    tiles = parts[0].shape[-1] // LANES
    pieces = []
    for first in list(range(0, tiles - 1, 2)) + ([tiles - 1] if with_edge else []):
        steps = (-1, 0, 1, 2) if first < tiles - 1 else (-1, 0, 1)
        table = band[...] if first < tiles - 1 else band[: 3 * LANES, :LANES]
        order = [(first + step) % tiles for step in steps]
        piece = None
        for part in parts:
            term = dot(jnp.concatenate([lane_tile(part, t) for t in order], axis=1), table)
            piece = term if piece is None else piece + term
        pieces.append(piece)
    return jnp.concatenate(pieces, axis=1)


def slope_y(read):
    value = read(3) - read(-3)
    for index in (0, 1):
        value = value + whole_weights[index] * (read(index + 1) - read(-index - 1))
    return value


def edged(k, side, center, up, down, above, below, sides, has, first=0):
    step = pl.program_id(0) + first
    tile, width = center.shape
    tall = sides.shape[1]
    last = (tall - LANES) // tile - 1
    base = pl.multiple_of(step * tile, 8)
    before = pl.multiple_of(jnp.where(step == 0, tall, base) - HALO, 8)
    over = jnp.where(step == 0, strip(above, k, True) * has[2], up)
    under = jnp.where(step == last, strip(below, k, False) * has[3], down)
    rows = (
        (over, sides[side, pl.ds(before, HALO), :]),
        (center, sides[side, pl.ds(base, tile), :]),
        (under, sides[side, pl.ds(pl.multiple_of(base + tile, 8), HALO), :]),
    )
    return jnp.concatenate([jnp.concatenate(pair, axis=1) for pair in rows], axis=0)


def edged_open(k, side, wall, wall_up, wall_down, above, below, sides, has, first=0):
    open_cells = [1.0 - ref[0].astype(F32) for ref in (wall, wall_up, wall_down)]
    return edged(k, side, *open_cells, above, below, sides, has, first)


def quiet_step_kernel(
    first, has, place, center, up, down, wall, wall_up, wall_down, above, below, sides, across, along, along_inner, calm, density, shown_open, mark
):
    parts, _, tile, width = center.shape
    high = tile + 2 * HALO
    opened = edged_open(parts, parts, wall, wall_up, wall_down, above, below, sides, has, first)
    values = []
    for k in range(parts):
        value = edged(
            k,
            k,
            center[k, 0].astype(F32),
            up[k, 0].astype(F32)[up.shape[2] - HALO :],
            down[k, 0].astype(F32)[:HALO],
            above,
            below,
            sides,
            has,
            first,
        )
        values.append(value)

    def drops(x, along_b, along_p):
        diverge = x[1] + along_b
        return (
            diverge + mean_flow * x[0],
            x[3] + mean_flow * x[1],
            along_p + mean_flow * x[2],
            diverge + mean_flow * x[3],
        )

    short = [value.astype(BF16) for value in values]
    x = slopes_x((jnp.concatenate(short, axis=0),), across, True)
    x = [x[k * high : (k + 1) * high] for k in range(parts)]
    table = along[...]
    dropped = drops(x, dot(table, short[2]), dot(table, short[3]))
    middle = [opened * (v - (time_step / 60.0) * d) for v, d in zip(values, dropped)]
    inner = slice(HALO, HALO + tile)
    x = slopes_x(split(jnp.concatenate([value[inner] for value in middle], axis=0)), across, False)
    x = [x[k * tile : (k + 1) * tile] for k in range(parts)]
    table = along_inner[...]
    y = [sum(dot(table, part) for part in split(middle[k][:, :width])) for k in (2, 3)]
    dropped = drops(x, *y)
    shown = opened[inner, :width]
    for k in range(parts):
        start = 0.5 * values[k][inner, :width] - (0.5 * time_step / 60.0) * dropped[k]
        value = shown * start + 0.5 * middle[k][inner, :width]
        if k == 0:
            density[0, 0] = value.astype(BF16)
        else:
            calm[k - 1] = value
    shown_open[0] = (time_step * opened).astype(BF16)
    mark[0] = place[0]


def tables_kernel(place, weights_x, weights_y, rise_x, rise_y, mark):
    mark[0] = place[0]
    _, tiles, reach_x, lanes = rise_x.shape
    wide, length_x = (tiles - 1) * lanes, weights_x.shape[1]
    first = place[0] * wide
    half = LANES // 2

    def weights(ref, start, size):
        length = ref.shape[1]
        start = jnp.where(start < 0, start + length, jnp.where(start >= length, start - length, start))
        return ref[:, pl.ds(pl.multiple_of(start, LANES), size)]

    cells = lax.broadcasted_iota(jnp.int32, (reach_x, lanes), 0)
    fine = lax.broadcasted_iota(jnp.int32, (reach_x, lanes), 1)
    right, left = weights(weights_x, first + wide, LANES), weights(weights_x, first - LANES, LANES)
    edge = jnp.where(lane_index(right.shape) < half, right, left)
    edge = jnp.concatenate([edge, edge], axis=1)
    for k in range(tiles):
        own = weights(weights_x, first + k * lanes, lanes) if k < tiles - 1 else edge
        target = fine // 2 - 1
        if k == tiles - 1:
            target = jnp.where(fine < half, target, target + half)
        value = jnp.zeros(fine.shape, F32)
        for t in range(4):
            value = jnp.where(cells == (target + t) % reach_x, own[t : t + 1, :], value)
        rise_x[0, k], rise_x[1, k] = split(value)
    steps, high, reach = rise_y.shape
    tall = steps * TILE
    first = place[1] * tall
    own = [weights(weights_y, first + k * LANES, LANES) for k in range(-1, tall // LANES + 1)]
    own = jnp.concatenate([jnp.concatenate(own, axis=1), jnp.zeros((4, tall + 2 * LANES), F32)], axis=0).T
    cells = lax.broadcasted_iota(jnp.int32, (high, reach), 1)
    last = cells >= reach // 3 * 2
    cells = cells % (reach // 3)
    target = lax.broadcasted_iota(jnp.int32, (high, reach), 0) // 2 + (HALO // 2 - 1)
    for k in range(steps):
        start = LANES - HALO + k * TILE
        value = jnp.zeros((high, reach), F32)
        for t in range(4):
            value = jnp.where(cells == target + t, own[start : start + high, t : t + 1], value)
        upper, lower = split(value)
        rise_y[k] = jnp.where(last, lower, upper)


def source_kernel(squares, opened, rise_x, rise_y, quiet, across, _, *refs):
    *lines, out, squared, cells_open, matrix, rows_matrix, calm, band, held, raised, forced, done, fetched, kept = refs
    steps = done.shape[0]
    tile, width = calm.shape[2:]
    high = tile + 2 * HALO
    rows = lines[0].shape[0]
    place = lax.axis_index("gx")

    def tile_copies(k):
        part = quiet.at[:, pl.ds(k * tile, tile), :]
        return (
            pltpu.make_async_copy(part, calm.at[k % 2], fetched.at[k % 2]),
            pltpu.make_async_copy(opened.at[k], cells_open.at[k % 2], fetched.at[2 + k % 2]),
        )

    def done_copy(k):
        part = out.at[1:, 0, pl.ds(k * tile, tile), :]
        return pltpu.make_async_copy(done.at[k], part, kept.at[k])

    arrays = ((squares, squared), (rise_x, matrix), (rise_y, rows_matrix), (across, band))
    copies = [
        pltpu.make_async_copy(source, target, fetched.at[4 + k])
        for k, (source, target) in enumerate(arrays)
    ]
    pieces = [
        pltpu.make_async_copy(
            piece,
            held.at[pl.ds(pl.multiple_of((place ^ mask) * rows, 8), rows), :],
            fetched.at[4 + len(arrays) + mask],
        )
        for mask, piece in enumerate(lines)
    ]
    for copy in (*pieces, *copies, *tile_copies(0), *tile_copies(1)):
        copy.start()
    for copy in pieces + copies[:1]:
        copy.wait()

    level = held[MARGIN - HALO : MARGIN - HALO + squared.shape[0], :] - squared[...]
    count = level.shape[1] // LANES
    near = lane_index((level.shape[0], LANES)) < 64
    around = []
    for k in range(count):
        after, before = lane_tile(level, (k + 1) % count), lane_tile(level, (k - 1) % count)
        around.append(split(jnp.concatenate([lane_tile(level, k), jnp.where(near, after, before)], axis=1)))
    copies[1].wait()
    for k in range(count):
        lanes = 2 * LANES if k < count - 1 else LANES
        value = split(exact_dot(around[k], [matrix[part, k, :, :lanes] for part in range(2)]))
        for part in range(2):
            raised[part, :, 2 * k * LANES : 2 * k * LANES + lanes] = value[part]
    for copy in copies[2:]:
        copy.wait()

    reach = rows_matrix.shape[2] // 3
    for k in range(steps):
        start = k * (tile // 2)
        window = [raised[part, start : start + reach, :] for part in (0, 1, 0)]
        calm_here, open_here = tile_copies(k)
        open_here.wait()
        free = cells_open[k % 2].astype(F32)
        value = free * dot(rows_matrix[k], jnp.concatenate(window, axis=0))
        forced[k % 2] = value
        inner = value[HALO : HALO + tile]
        shown = (0.5 / 60.0) * free[HALO : HALO + tile, :width]
        x = shown * slopes_x(split(inner), band, False)
        y = shown * slope_y(lambda d: forced[k % 2, HALO + d : HALO + d + tile, :width])
        calm_here.wait()
        still = calm.at[k % 2]
        done[k, 0] = (still[0] - x).astype(BF16)
        done[k, 1] = (still[1] - y).astype(BF16)
        done[k, 2] = (still[2] + inner[:, :width] - mean_flow * x).astype(BF16)
        done_copy(k).start()
        if k + 2 < steps:
            for copy in tile_copies(k + 2):
                copy.start()
    for k in range(steps):
        done_copy(k).wait()


def call(
    kernel, operands, outs, scratch=(), steps=0, specs=None, out_specs=None, after=(), aliases=None, megabytes=24, flops=0, moved=0, name=None
):
    count = len(operands)

    def body(*refs):
        kernel(*refs[:count], *refs[count + len(after) :])

    def whole(array):
        zeros = (0,) * len(array.shape)
        return pl.BlockSpec(array.shape, lambda *_: zeros)

    arguments = {}
    chosen = specs or {}
    if steps:
        arguments["grid"] = (steps,)
        in_specs = [chosen.get(i, whole(o)) for i, o in enumerate(operands)]
        arguments["out_specs"] = jax.tree.map(whole, outs) if out_specs is None else out_specs
    else:
        local = pl.BlockSpec(memory_space=pltpu.VMEM)
        in_specs = [chosen.get(i, local) for i in range(count)]
        if out_specs is not None:
            arguments["out_specs"] = out_specs
    return pl.pallas_call(
        body,
        out_shape=outs,
        in_specs=in_specs + [pl.BlockSpec(memory_space=pl.ANY)] * len(after),
        scratch_shapes=list(scratch),
        input_output_aliases=aliases or {},
        compiler_params=pltpu.CompilerParams(vmem_limit_bytes=megabytes << 20),
        cost_estimate=pl.CostEstimate(flops=flops, bytes_accessed=moved, transcendentals=0),
        name=name,
        **arguments,
    )(*operands, *after)


def ring(array, axis, step):
    size = lax.axis_size(axis)
    return lax.ppermute(array, axis, [(i, (i + step) % size) for i in range(size)])


def swap(array, axis, mask):
    return lax.ppermute(array, axis, [(i, i ^ mask) for i in range(lax.axis_size(axis))])


def shaped(*shape, kind=F32):
    return jax.ShapeDtypeStruct(shape, kind)


def pressure_lines(pieces, gathered, spread, stepped):
    _, rows, local_x = pieces[0].shape
    count_x, count_y = lax.axis_size("gx"), lax.axis_size("gy")
    count = count_x * count_y
    length_x, length_y = local_x * count_x, rows * count
    full, zero, middle, cos_turn, sin_turn = x_tables(length_x)
    turns = np.zeros((8, cos_turn.shape[1]), np.float32)
    turns[0:3], turns[3:6] = cos_turn, sin_turn
    spectra, total = call(
        forward_x_kernel,
        (*pieces, np.concatenate([beside(full), beside(zero, middle)]), turns),
        (shaped(count, rows, LANES), shaped(8, LANES)),
        (
            pltpu.VMEM((count_x, 2, rows, local_x), F32),
            pltpu.VMEM((count, rows, LANES), F32),
            pltpu.SemaphoreType.DMA((5,)),
        ),
        out_specs=(pl.BlockSpec(memory_space=pl.ANY), pl.BlockSpec(memory_space=pltpu.VMEM)),
        after=gathered,
        flops=10**9,
        moved=4 << 20,
        name="forward_x",
    )
    spectra = lax.all_to_all(spectra, ("gy", "gx"), 0, 0, tiled=True)
    place = lax.axis_index("gy") * count_x + spread[0]
    waves = jnp.asarray(wave_table(length_x, count))
    wave = lax.dynamic_slice(waves, (place, 0), (1, LANES))
    both, turns_y = y_tables(length_y)
    kept = rows + 2 * MARGIN // count_x
    half = (kept // 2 + 8) // 8 * 8
    solved = call(
        functools.partial(solve_y_kernel, count_x),
        (spectra, total, wave, beside(both), turns_y),
        shaped(count, half, LANES),
        (
            pltpu.VMEM((length_y + 2 * MARGIN, LANES), F32),
            pltpu.VMEM((length_y // RADIX, 2 * RADIX * LANES), F32),
            pltpu.VMEM((count, half, LANES), F32),
            pltpu.SemaphoreType.DMA((count // RADIX,)),
        ),
        out_specs=pl.BlockSpec(memory_space=pl.ANY),
        flops=4 * 10**9,
        moved=6 << 20,
        name="solve_y",
    )
    solved = lax.all_to_all(solved, ("gy", "gx"), 0, 0, tiled=True)
    back = 2.0 * zero.T
    back[LANES // 2] *= 0.5
    tables = np.concatenate(
        [beside(full.T), beside(back, 2.0 * middle.T)]
    )
    again = jnp.asarray(np.tile(turns, (count_x, 1, 1)))
    again = lax.dynamic_slice(again, (stepped[0], 0, 0), (1,) + turns.shape)
    pressed = call(
        functools.partial(inverse_x_kernel, kept, 1.0 / (length_x * length_y)),
        (solved, tables, again[0]),
        (shaped(kept, local_x + LANES),) * count_x,
        (pltpu.VMEM((kept, length_x), F32),),
        flops=10**9,
        moved=4 << 20,
        name="inverse_x",
    )
    return [piece if mask == 0 else swap(piece, "gx", mask) for mask, piece in enumerate(pressed)]


def fast_shards(velocity, weights_x, weights_y, acoustic, wall_mask):
    parts, _, tall, wide = acoustic.shape
    _, _, local_y, local_x = velocity.shape
    count_x, count_y = lax.axis_size("gx"), lax.axis_size("gy")
    place_x, place_y = lax.axis_index("gx"), lax.axis_index("gy")
    full, high, steps = wide + LANES, TILE + 2 * HALO, tall // TILE
    strips = (parts + 2) * HALO
    small = 2 * HALO
    has = jnp.stack([place_x > 0, place_x < count_x - 1, place_y > 0, place_y < count_y - 1])
    has = has.astype(F32)
    scalars = pl.BlockSpec(memory_space=pltpu.SMEM)

    def at(block, *index):
        return pl.BlockSpec(block, lambda i: index)

    own = place_x.astype(jnp.int32).reshape(1)
    sent = call(
        pieces_kernel,
        (velocity,),
        (shaped(2, local_y // count_x, local_x),) * count_x,
        moved=2 << 20,
        megabytes=8,
        name="pieces",
    )
    moved = [piece if mask == 0 else swap(piece, "gx", mask) for mask, piece in enumerate(sent)]
    first, last = call(
        rows_kernel,
        (acoustic, acoustic, wall_mask, wall_mask, velocity, velocity),
        (shaped(STRIP_ROWS, wide),) * 2,
        steps=1,
        specs={
            0: at((parts, 1, small, wide), 0, 0, 0, 0),
            1: at((parts, 1, small, wide), 0, 0, tall // small - 1, 0),
            2: at((1, HALO, wide), 0, 0, 0),
            3: at((1, HALO, wide), 0, tall // HALO - 1, 0),
            4: at((1, 1, HALO, local_x), 1, 0, 0, 0),
            5: at((1, 1, HALO, local_x), 1, 0, local_y // HALO - 1, 0),
        },
        after=moved[1:2],
        moved=2 << 20,
        megabytes=50,
        name="rows",
    )
    above, below = ring(last, "gy", 1), ring(first, "gy", -1)
    to_right, to_left = call(
        columns_kernel,
        (has, acoustic, acoustic, wall_mask, wall_mask, velocity, velocity, above, below),
        (shaped(strips, tall + LANES), shaped(strips, tall + LANES)),
        steps=1,
        specs={
            0: scalars,
            1: at((parts, 1, tall, LANES), 0, 0, 0, 0),
            2: at((parts, 1, tall, LANES), 0, 0, 0, wide // LANES - 1),
            3: at((1, tall, LANES), 0, 0, 0),
            4: at((1, tall, LANES), 0, 0, wide // LANES - 1),
            5: at((1, 1, local_y, LANES), 1, 0, 0, 0),
            6: at((1, 1, local_y, LANES), 1, 0, 0, local_x // LANES - 1),
        },
        moved=8 << 20,
        megabytes=54,
        name="columns",
    )
    from_left, from_right = ring(to_right, "gx", 1), ring(to_left, "gx", -1)
    local_memory = pl.BlockSpec(memory_space=pltpu.VMEM)
    tiles = wide // (2 * LANES) + 1
    rise_x, rise_y, listed = call(
        tables_kernel,
        (jnp.stack([place_x, place_y]).astype(jnp.int32), weights_x, weights_y),
        (
            shaped(2, tiles, 2 * LANES, 2 * LANES, kind=BF16),
            shaped(steps, high, 3 * (high // 2 + HALO), kind=BF16),
            shaped(1, kind=jnp.int32),
        ),
        specs={0: scalars},
        out_specs=(local_memory, local_memory, scalars),
        moved=4 << 20,
        megabytes=54,
        name="tables",
    )
    sides, squares, _ = call(
        sides_kernel,
        (has, listed, velocity, above, below, from_left, from_right),
        (
            shaped(parts + 1, tall + LANES, LANES),
            shaped(local_y + 2 * HALO, local_x + LANES),
            shaped(1, kind=jnp.int32),
        ),
        steps=1,
        specs={0: scalars, 1: scalars, 2: at((1, 1, local_y, local_x), 1, 0, 0, 0)},
        out_specs=(
            at((parts + 1, tall + LANES, LANES), 0, 0, 0),
            at((local_y + 2 * HALO, local_x + LANES), 0, 0),
            scalars,
        ),
        moved=8 << 20,
        megabytes=54,
        name="sides",
    )
    across, along = band_tables(high)
    along_inner = along[HALO : HALO + TILE]
    per, rows = TILE // small, TILE // HALO

    def tiled(first):
        walls = (
            pl.BlockSpec((1, TILE, wide), lambda i: (0, i + first, 0)),
            pl.BlockSpec((1, HALO, wide), lambda i: (0, jnp.maximum((i + first) * rows - 1, 0), 0)),
            pl.BlockSpec(
                (1, HALO, wide),
                lambda i: (0, jnp.minimum((i + first + 1) * rows, steps * rows - 1), 0),
            ),
        )
        cells = (
            pl.BlockSpec((parts, 1, TILE, wide), lambda i: (0, 0, i + first, 0)),
            pl.BlockSpec(
                (parts, 1, small, wide), lambda i: (0, 0, jnp.maximum((i + first) * per - 1, 0), 0)
            ),
            pl.BlockSpec(
                (parts, 1, small, wide),
                lambda i: (0, 0, jnp.minimum((i + first + 1) * per, steps * per - 1), 0),
            ),
        )
        return cells, walls

    def quiet_tiles(first, count, before):
        cells, walls = tiled(first)
        operands = (has, own, acoustic, acoustic, acoustic, wall_mask, wall_mask, wall_mask, above, below, sides)
        operands = operands + (across, along, along_inner)
        return call(
            functools.partial(quiet_step_kernel, first),
            operands,
            (
                shaped(parts - 1, tall, wide),
                shaped(*acoustic.shape, kind=BF16),
                shaped(steps, high, full, kind=BF16),
                shaped(1, kind=jnp.int32),
            ),
            steps=count,
            specs=dict(enumerate((scalars, scalars) + cells + walls)),
            out_specs=(
                pl.BlockSpec((parts - 1, TILE, wide), lambda i: (0, i + first, 0)),
                pl.BlockSpec((1, 1, TILE, wide), lambda i: (0, 0, i + first, 0)),
                pl.BlockSpec((1, high, full), lambda i: (i + first, 0, 0)),
                scalars,
            ),
            after=before,
            aliases={len(operands) + k: k for k in range(len(before))},
            megabytes=54,
            flops=3 * 10**9 * count,
            moved=(12 << 20) * count,
            name="quiet_step",
        )

    early = max(steps // 4, 1)
    *begun, spread = quiet_tiles(0, early, ())
    *begun, stepped = quiet_tiles(early, steps - early, begun)
    quiet, final, opened = begun
    lines = pressure_lines(moved, (above, below), spread, stepped)
    operands = (squares, opened, rise_x, rise_y, quiet, across, final, *lines)
    anywhere = pl.BlockSpec(memory_space=pl.ANY)
    specs = {k: anywhere for k in range(len(operands))}
    scratch = (
        pltpu.VMEM(squares.shape, F32),
        pltpu.VMEM((2,) + opened.shape[1:], BF16),
        pltpu.VMEM(rise_x.shape, BF16),
        pltpu.VMEM(rise_y.shape, BF16),
        pltpu.VMEM((2, parts - 1, TILE, wide), F32),
        pltpu.VMEM(across.shape, BF16),
        pltpu.VMEM((local_y + 2 * MARGIN, local_x + LANES), F32),
        pltpu.VMEM((2, local_y + 2 * HALO, full), BF16),
        pltpu.VMEM((2, high, full), F32),
        pltpu.VMEM((steps, parts - 1, TILE, wide), BF16),
        pltpu.SemaphoreType.DMA((8 + count_x,)),
        pltpu.SemaphoreType.DMA((steps,)),
    )
    return call(
        source_kernel,
        operands,
        shaped(*acoustic.shape, kind=BF16),
        scratch,
        specs=specs,
        out_specs=anywhere,
        aliases={6: 0},
        megabytes=56,
        flops=4 * 10**9,
        moved=16 << 20,
        name="source_step",
    )


def fits(count_x, count_y, velocity, acoustic):
    _, planes, local_y, local_x = velocity
    _, _, tall, wide = acoustic
    length_x, length_y = local_x * count_x, local_y * count_y
    rows = local_y // count_x
    base_x, base_y = length_x // RADIX, length_y // RADIX
    return (
        planes == 1
        and acoustic[0] == PARTS
        and length_x * 2 == count_x * count_y * LANES
        and base_x % (2 * LANES) == 0
        and local_x % base_x == 0
        and rows % 8 == 0
        and base_y % rows == 0
        and base_y % 8 == 0
        and count_x * count_y % RADIX == 0
        and MARGIN * 2 % (8 * count_x) == 0
        and tall == 2 * local_y
        and wide == 2 * local_x
        and tall % TILE == 0
        and tall % LANES == 0
        and tall >= 2 * TILE
        and count_x & (count_x - 1) == 0
        and wide % (2 * LANES) == 0
    )


def extended(array, sides, width):
    for axis, dim in sides:
        size, length = (lax.axis_size(axis), array.shape[dim])
        up = [(i, (i + 1) % size) for i in range(size - 1)]
        down = [(j, i) for i, j in up]
        last = lax.slice_in_dim(array, length - width, length, axis=dim)
        leading = lax.slice_in_dim(array, 0, width, axis=dim)
        before = lax.ppermute(last, axis, up)
        after = lax.ppermute(leading, axis, down)
        array = jnp.concatenate([before, array, after], axis=dim)
    return array


def gradients(padded):
    height = padded.shape[-2] - 6
    breadth = padded.shape[-1] - 6
    rows_mid = padded[..., 3 : 3 + height, :]
    cols_mid = padded[..., :, 3 : 3 + breadth]
    along_x = jnp.zeros_like(padded[..., 3 : 3 + height, 3 : 3 + breadth])
    along_y = jnp.zeros_like(along_x)
    for index, weight in enumerate(stencil_weights):
        distance = index + 1
        along_x = along_x + weight * (
            rows_mid[..., 3 + distance : 3 + distance + breadth]
            - rows_mid[..., 3 - distance : 3 - distance + breadth]
        )
        along_y = along_y + weight * (
            cols_mid[..., 3 + distance : 3 + distance + height, :]
            - cols_mid[..., 3 - distance : 3 - distance + height, :]
        )
    return (along_x, along_y)


def tendency(padded, source):
    along_x, along_y = gradients(padded)
    diverge = along_x[1] + along_y[2]
    forcing = jnp.stack([-diverge, -along_x[3], -along_y[3], source - diverge])
    return forcing - mean_flow * along_x


def spectral_index(flat, length):
    second = length // 16
    wave = flat // second + 16 * (flat % second)
    return jnp.where(wave < length // 2, wave, wave - length).astype(jnp.float32)


def twiddles(rows_count, cols_count, modulus, sign):
    products = jnp.arange(rows_count)[:, None] * jnp.arange(cols_count)[None, :] % modulus
    angles = 2.0 * math.pi / modulus * products.astype(jnp.float32)
    return (jnp.cos(angles), sign * jnp.sin(angles))


def mix_rows(real_part, imag_part, cosine, sine):
    exact = lax.Precision.HIGHEST
    cos_real = jnp.einsum("ka,...ab->...kb", cosine, real_part, precision=exact)
    cos_imag = jnp.einsum("ka,...ab->...kb", cosine, imag_part, precision=exact)
    sin_real = jnp.einsum("ka,...ab->...kb", sine, real_part, precision=exact)
    sin_imag = jnp.einsum("ka,...ab->...kb", sine, imag_part, precision=exact)
    return (cos_real - sin_imag, cos_imag + sin_real)


def mix_cols(real_part, imag_part, cosine, sine):
    exact = lax.Precision.HIGHEST
    cos_real = jnp.einsum("...kb,bc->...kc", real_part, cosine, precision=exact)
    cos_imag = jnp.einsum("...kb,bc->...kc", imag_part, cosine, precision=exact)
    sin_real = jnp.einsum("...kb,bc->...kc", real_part, sine, precision=exact)
    sin_imag = jnp.einsum("...kb,bc->...kc", imag_part, sine, precision=exact)
    return (cos_real - sin_imag, cos_imag + sin_real)


def rotate(real_part, imag_part, cosine, sine):
    return (real_part * cosine - imag_part * sine, real_part * sine + imag_part * cosine)


def discrete(real_part, imag_part, sign):
    length = real_part.shape[-1]
    second = length // 16
    initial = real_part.shape
    folded = initial[:-1] + (16, second)
    real_part = real_part.reshape(folded)
    imag_part = imag_part.reshape(folded)
    small_cos, small_sin = twiddles(16, 16, 16, sign)
    large_cos, large_sin = twiddles(second, second, second, sign)
    turn_cos, turn_sin = twiddles(16, second, length, sign)
    if sign < 0:
        real_part, imag_part = mix_rows(real_part, imag_part, small_cos, small_sin)
        real_part, imag_part = rotate(real_part, imag_part, turn_cos, turn_sin)
        real_part, imag_part = mix_cols(real_part, imag_part, large_cos, large_sin)
    else:
        real_part, imag_part = mix_cols(real_part, imag_part, large_cos, large_sin)
        real_part, imag_part = rotate(real_part, imag_part, turn_cos, turn_sin)
        real_part, imag_part = mix_rows(real_part, imag_part, small_cos, small_sin)
        real_part = real_part / length
        imag_part = imag_part / length
    return (real_part.reshape(initial), imag_part.reshape(initial))


def transform(stacked, sign, kind):
    if kind == "real_in":
        real_part = stacked
        imag_part = jnp.zeros_like(stacked)
    else:
        half = stacked.shape[0] // 2
        real_part = stacked[:half]
        imag_part = stacked[half:]
    real_out, imag_out = discrete(real_part, imag_part, sign)
    if kind == "real_out":
        return real_out
    return jnp.concatenate([real_out, imag_out], axis=0)


def project(stacked, wave_x, wave_y):
    coef_xx = wave_x * wave_x
    coef_xy = 2.0 * wave_x * wave_y
    coef_yy = wave_y * wave_y
    denominator = wave_x * wave_x + wave_y * wave_y
    positive = denominator > 0
    safe = jnp.where(positive, denominator, 1.0)

    def combine(parts):
        numerator = -(coef_xx * parts[0] + coef_xy * parts[1] + coef_yy * parts[2])
        return jnp.where(positive, numerator / safe, 0.0)

    return jnp.stack([combine(stacked[:3]), combine(stacked[3:])])


def refine(stacked, weights):
    result = jnp.zeros(stacked.shape[:-1] + (2 * stacked.shape[-1],), jnp.float32)
    for offset in range(4):
        result = (
            result
            + jnp.repeat(jnp.roll(stacked, 1 - offset, axis=-1), 2, axis=-1) * weights[offset]
        )
    return result


def lines_x(stacked, action):
    gathered = action(lax.all_to_all(stacked, "gx", split_axis=2, concat_axis=3, tiled=True))
    return lax.all_to_all(gathered, "gx", split_axis=3, concat_axis=2, tiled=True)


def lines_y(stacked, action):
    turned = jnp.swapaxes(stacked, 2, 3)
    gathered = action(lax.all_to_all(turned, "gy", split_axis=2, concat_axis=3, tiled=True))
    returned = lax.all_to_all(gathered, "gy", split_axis=3, concat_axis=2, tiled=True)
    return jnp.swapaxes(returned, 2, 3)


def expand(fields):
    return extended(fields, (("gx", 3), ("gy", 2)), 3)


def shards(velocity, weights_x, weights_y, acoustic, wall_mask):
    acoustic = acoustic.astype(jnp.float32)
    flow_x = velocity[0]
    flow_y = velocity[1]
    tensor = jnp.stack([flow_x * flow_x, flow_x * flow_y, flow_y * flow_y])
    count_gx = lax.axis_size("gx")
    count_gy = lax.axis_size("gy")
    place_x = lax.axis_index("gx")
    place_y = lax.axis_index("gy")
    local_y = tensor.shape[2]
    local_x = tensor.shape[3]
    length_x = local_x * count_gx
    length_y = local_y * count_gy

    def forward_real(portion):
        return transform(portion, -1, "real_in")

    def finish_x(portion):
        return refine(transform(portion, 1, "real_out"), weights_x)

    spectra = lines_x(tensor, forward_real)
    share_x = local_x // count_gy
    line_x = spectral_index(place_x * local_x + place_y * share_x + jnp.arange(share_x), length_x)[
        :, None
    ]
    line_y = spectral_index(jnp.arange(length_y), length_y)[None, :]

    def solve_y(portion):
        solved = project(transform(portion, -1, "complex"), line_x, line_y)
        return refine(transform(solved, 1, "complex"), weights_y)

    pressure = lines_y(spectra, solve_y)
    source = lines_x(pressure, finish_x)[0]
    open_cells = (1 - wall_mask).astype(jnp.float32)
    first_rate = tendency(expand(acoustic), source)
    middle = open_cells * (acoustic + time_step * first_rate)
    second_rate = tendency(expand(middle), source)
    return (open_cells * (acoustic + 0.5 * time_step * (first_rate + second_rate))).astype(
        jnp.bfloat16
    )


def solution(mesh):
    in_specs = (P(None, None, "gy", "gx"), P(), P(), P(None, None, "gy", "gx"), P(None, "gy", "gx"))
    out_specs = P(None, None, "gy", "gx")

    def chosen(velocity, weights_x, weights_y, acoustic, wall_mask):
        sizes = (mesh.shape["gx"], mesh.shape["gy"], velocity.shape, acoustic.shape)
        plan = fast_shards if fits(*sizes) else shards
        return plan(velocity, weights_x, weights_y, acoustic, wall_mask)

    return jax.shard_map(
        chosen, mesh=mesh, in_specs=in_specs, out_specs=out_specs, check_vma=False
    )
```
